128 devices in a mesh: section: 2 (over z_lo), batch: 64 (over y, x, z_hi, core).
Axes of the slice: x: 4, y: 4, z: 4 (z_hi: 2, z_lo: 2; z = z_hi * 2 + z_lo), core: 2. Of those that a mesh axis runs over, the one named last changes fastest.
Arguments:
- patch_io: bfloat16 [2, 2, 64, 64, 1024], P('section', None, 'batch'), may hold values from -6 to 6
- byte_states: bfloat16 [2, 64, 512, 1024], P(None, 'batch', 'section'), may hold values from -6 to 6
- patch_lengths: int32 [2, 64, 64], P(None, 'batch'), may hold values from 1 to 16, 512 in all within a row
- patch_live: int32 [2, 64, 64], P(None, 'batch'), may hold values 0 or 1
- attn_qkv: bfloat16 [2, 1024, 3072], P('section'), may hold values from -0.1875 to 0.1875
- attn_out: bfloat16 [2, 1024, 1024], P('section'), may hold values from -0.75 to 0.75
- gains: float32 [2, 2, 1024], P('section'), may hold values from 0.25 to 1.75
- ff_weights: bfloat16 [2816, 3, 1024], replicated, may hold values from -0.1875 to 0.1875
Outputs:
- patch_out: float32 [2, 2, 64, 64, 1024], P('section', None, 'batch')
- byte_grad: bfloat16 [2, 64, 512, 1024], P(None, 'batch', 'section')
- attn_qkv_grad: float32 [2, 1024, 3072], P('section')
- attn_out_grad: float32 [2, 1024, 1024], P('section')
- gains_grad: float32 [2, 2, 1024], P('section')
- ff_grad: float32 [2, 2816, 3, 1024], P('section', 'batch')
The draws below stay inside these ranges and needn't reach their ends.
Inputs may be any that keep to these rules, and one draw needn't show every extreme that they name: `patch_lengths`: each row of 64 patch lengths sums to 512; the largest in a row is 16.
All inputs are finite; a program needn't handle non-finite values. No bound on the sum of `patch_live` on one device may be relied on, other than what follows from the above.
Results may differ from the reference program's by a relative error of at most 0.017.
Values may be sent and summed in bfloat16 or wider, within the bound.
No kernel may reach another device: no remote copies, remote signals or barrier semaphores. Data moves between devices by JAX's collectives and lax.ppermute only.
A program may use at most 384 MiB of HBM per device.

```python
import math
import jax
import jax.numpy as jnp
import numpy as np
from jax import lax

D = 1024
HEADS = 16
HD = 64
FF = 2816
S = 64
MAXLEN = 16
MB = 2
BYTES = 512
NSEQ = 64


def place_ends(values, own_key, least, largest):
    longest = values.shape.index(max(values.shape))
    spots = []
    for shift in (0, 1):
        where = [jax.random.randint(jax.random.fold_in(own_key, axis), (), 0, length) for axis, length in enumerate(values.shape)]
        where[longest] = (where[longest] + shift) % values.shape[longest]
        spots.append(tuple(where))
    return values.at[spots[0]].set(least).at[spots[1]].set(largest)


def block_levels(own_key, shape, split, low, largest):
    loudness, own = 1.0, jax.random.fold_in(own_key, 6)
    for axis_at, shards_of in split:
        draws = jnp.exp(jax.random.uniform(jax.random.fold_in(own, axis_at), (shards_of,), jnp.float32, low / len(split), largest / len(split)))
        loudness = loudness * jnp.repeat(draws, shape[axis_at] // shards_of).reshape([-1 if axis == axis_at else 1 for axis in range(len(shape))])
    return loudness


def profile(amount, total, reach, slope):
    weights = [(1 << 20) // math.isqrt(standing ** slope) + 1 for standing in range(2, amount + 1)]
    rest, counts = total - reach - (amount - 1), [1] * (amount - 1)
    while rest > 0:
        candidates = [i for i in range(amount - 1) if counts[i] < reach]
        mass, budget = sum([weights[i] for i in candidates]), rest
        for i in candidates:
            extra = min(reach - counts[i], max(1, budget * weights[i] // mass), rest)
            counts[i] = counts[i] + extra
            rest = rest - extra
    return np.array([reach] + counts)


def uneven_parts(stream_key, count, total, bound, slope):
    if count == 2:
        one = jax.random.randint(stream_key, (), max(1, total - bound), min(bound, total - 1) + 1)
        return jnp.stack([one, total - one])
    sizes = jnp.asarray(profile(count, total, bound, slope), jnp.int32)
    pairs = (count - 1) // 2
    source_of, sink = sizes[1:1 + 2 * pairs:2], sizes[2:2 + 2 * pairs:2]
    slack = jnp.minimum(source_of - 1, bound - sink)
    moved = jax.random.randint(jax.random.fold_in(stream_key, 1), (pairs,), 0, 1 << 20) % (slack + 1)
    sizes = sizes.at[1:1 + 2 * pairs:2].set(source_of - moved).at[2:2 + 2 * pairs:2].set(sink + moved)
    return sizes[jax.random.permutation(jax.random.fold_in(stream_key, 2), count)]


def bell_draw(key, extent, scale, most, cuts=(), held_as=jnp.bfloat16):
    values = jax.random.normal(key, extent, jnp.float32) * scale
    if len(cuts) > 0:
        values = block_levels(key, extent, cuts, -0.22, 0.18) * values
    return jnp.clip(values, min=-most, max=most).astype(held_as)


def setup_inputs(seed: int = 0) -> dict:
    key_of = jax.random.split(jax.random.key(seed), 9)
    patch_io = bell_draw(key_of[0], (2, MB, NSEQ, S, D), 1.0, 6.0, ((0, 2), (2, 64)))
    byte_states = bell_draw(key_of[1], (MB, NSEQ, BYTES, D), 1.0, 6.0, ((1, 64), (2, 2)))
    patch_lengths = jax.vmap(lambda own: uneven_parts(own, S, BYTES, MAXLEN, 2))(jax.random.split(key_of[2], MB * NSEQ)).reshape((MB, NSEQ, S)).astype(jnp.int32)
    patch_live = place_ends((jax.random.randint(key_of[3], (MB, NSEQ, S), 0, 4) < 3).astype(jnp.int32), jax.random.fold_in(key_of[3], 1), 0, 1)
    attn_qkv = bell_draw(key_of[4], (2, D, 3 * D), D ** -0.5, 0.1875, ((0, 2),))
    attn_out = bell_draw(key_of[5], (2, D, D), (D // 16) ** -0.5, 0.75, ((0, 2),))
    gains = jnp.clip(1.0 + 0.15 * jax.random.normal(key_of[6], (2, 2, D), jnp.float32), 0.25, 1.75)
    ff_weights = bell_draw(key_of[7], (FF, 3, D), D ** -0.5, 0.1875)
    return dict(patch_io=patch_io, byte_states=byte_states, patch_lengths=patch_lengths, patch_live=patch_live, attn_qkv=attn_qkv, attn_out=attn_out, gains=gains, ff_weights=ff_weights)


epsilon = 1e-05
neg_big = -1e+30
highest = lax.Precision.HIGHEST

@jax.custom_vjp
def low(v):
    return lax.optimization_barrier(v.astype(jnp.bfloat16)).astype(jnp.float32)

@jax.custom_vjp
def low_back(v):
    return v

def low_keep(v):
    return (low(v), None)

def low_pass(kept, grad):
    return (grad,)

def back_keep(v):
    return (v, None)

def back_low(kept, grad):
    return (low(grad),)
low.defvjp(low_keep, low_pass)
low_back.defvjp(back_keep, back_low)

def product(form, left, right):
    return jnp.einsum(form, left, right, precision=highest)

def rms_norm(rows, gain):
    mean_square = lax.optimization_barrier(jnp.mean(rows * rows, axis=-1, keepdims=True))
    return rows * lax.rsqrt(mean_square + epsilon) * gain

def split_heads(rows):
    return rows.reshape(rows.shape[0], rows.shape[1], HEADS, HD)

def project(rows, matrix):
    return low(low_back(product('gsd,dc->gsc', rows, matrix)))

def attend(queries, keys, values, allowed):
    raw = product('gqhe,gkhe->ghqk', queries, keys)
    scores = low_back(raw * HD ** (-0.5))
    scores = jnp.where(allowed[:, None], scores, neg_big)
    highest_score = lax.optimization_barrier(jnp.max(scores, axis=-1, keepdims=True))
    exponent = jnp.exp(scores - highest_score)
    weights = low(exponent / lax.optimization_barrier(jnp.sum(exponent, axis=-1, keepdims=True)))
    mixed = product('ghqk,gkhe->gqhe', weights, values)
    mixed = low(low_back(mixed))
    return mixed.reshape(mixed.shape[0], mixed.shape[1], HEADS * HD)

def group_forward(params, patches, byte_rows, lengths, live):
    enc_qkv, enc_out, lat_qkv, lat_out, gain_patch, gain_byte, gain_attn, gain_ffn, ffn_weights = params
    width = patches.shape[2]
    seq = patches.shape[1]
    count = byte_rows.shape[1]
    spots = jnp.arange(count, dtype=jnp.int32)
    ends = jnp.cumsum(lengths, axis=-1).astype(jnp.int32)
    starts = ends - lengths
    allowed_bytes = (spots[None, None, :] >= starts[:, :, None]) & (spots[None, None, :] < ends[:, :, None])
    patch_norm = low(rms_norm(patches, gain_patch))
    byte_norm = low(rms_norm(byte_rows, gain_byte))
    queries = split_heads(project(patch_norm, enc_qkv[:, :width]))
    keys = split_heads(project(byte_norm, enc_qkv[:, width:2 * width]))
    values = split_heads(project(byte_norm, enc_qkv[:, 2 * width:]))
    mixed = attend(queries, keys, values, allowed_bytes)
    hidden = patches + product('gsd,dc->gsc', mixed, enc_out)
    sent = low(low_back(hidden))
    rows = jnp.arange(seq, dtype=jnp.int32)
    diagonal = rows[None, :] == rows[:, None]
    causal = rows[None, :] <= rows[:, None]
    allowed_causal = causal[None] & ((live[:, None, :] == 1) | diagonal[None])
    latent_norm = low(rms_norm(sent, gain_attn))
    queries2 = split_heads(project(latent_norm, lat_qkv[:, :width]))
    keys2 = split_heads(project(latent_norm, lat_qkv[:, width:2 * width]))
    values2 = split_heads(project(latent_norm, lat_qkv[:, 2 * width:]))
    mixed2 = attend(queries2, keys2, values2, allowed_causal)
    after = sent + low_back(product('gsd,dc->gsc', mixed2, lat_out))
    ffn_norm = low(rms_norm(after, gain_ffn))
    gate = low_back(product('gsd,fd->gsf', ffn_norm, ffn_weights[:, 0]))
    upward = low_back(product('gsd,fd->gsf', ffn_norm, ffn_weights[:, 1]))
    activated = low(gate * jax.nn.sigmoid(gate) * upward)
    return after + product('gsf,fd->gsd', activated, ffn_weights[:, 2])

def reference(patch_io, byte_states, patch_lengths, patch_live, attn_qkv, attn_out, gains, ff_weights):
    seq = patch_io.shape[3]
    width = patch_io.shape[4]
    count = byte_states.shape[2]
    patches = patch_io[0].astype(jnp.float32).reshape(-1, seq, width)
    cotangent = patch_io[1].astype(jnp.float32).reshape(-1, seq, width)
    byte_rows = byte_states.astype(jnp.float32).reshape(-1, count, width)
    lengths = patch_lengths.reshape(-1, seq).astype(jnp.int32)
    live = patch_live.reshape(-1, seq).astype(jnp.int32)
    total_seqs = patches.shape[0]
    group = math.gcd(total_seqs, max(1, 4096 // count))
    blocks = total_seqs // group
    qkv_f = attn_qkv.astype(jnp.float32)
    out_f = attn_out.astype(jnp.float32)
    gains_f = gains.astype(jnp.float32)
    params = (qkv_f[0], out_f[0], qkv_f[1], out_f[1], gains_f[0, 0], gains_f[0, 1], gains_f[1, 0], gains_f[1, 1], ff_weights.astype(jnp.float32))

    def split_blocks(array):
        return array.reshape((blocks, group) + array.shape[1:])

    def forward_all(params, patches, byte_rows):

        def run_block(items):
            return jax.checkpoint(group_forward)(params, items[0], items[1], items[2], items[3])
        result = lax.map(run_block, (split_blocks(patches), split_blocks(byte_rows), split_blocks(lengths), split_blocks(live)))
        return result.reshape(patches.shape)
    latents, pullback = jax.vjp(forward_all, params, patches, byte_rows)
    grad_params, grad_patches, grad_bytes = pullback(cotangent)
    patch_out = jnp.stack([grad_patches, latents]).reshape(patch_io.shape)
    byte_grad = grad_bytes.reshape(byte_states.shape).astype(jnp.bfloat16)
    attn_qkv_grad = jnp.stack([grad_params[0], grad_params[2]])
    attn_out_grad = jnp.stack([grad_params[1], grad_params[3]])
    gains_grad = jnp.stack([jnp.stack([grad_params[4], grad_params[5]]), jnp.stack([grad_params[6], grad_params[7]])])
    ff_grad = jnp.stack([jnp.zeros_like(grad_params[8]), grad_params[8]])
    return (patch_out, byte_grad, attn_qkv_grad, attn_out_grad, gains_grad, ff_grad)
```

```python
import jax
import jax.numpy as jnp
from jax import lax
from jax.sharding import Mesh
from jax.sharding import PartitionSpec as P

HEADS = 16
HD = 64
SCALE = HD**-0.5
EPS = 1e-05
NEG = -1e30
BATCH = ("y", "x", "zh", "core")
BF = jnp.bfloat16
F32 = jnp.float32


def dot(left, right):
    return jnp.dot(left, right, preferred_element_type=F32)


def dot_t(left, right):
    return jnp.einsum("sc,dc->sd", left, right, preferred_element_type=F32)


def t_dot(left, right):
    return jnp.einsum("sa,sb->ab", left, right, preferred_element_type=F32)


def rms_norm(rows, gain):
    mean_square = jnp.mean(rows * rows, axis=-1, keepdims=True)
    return rows * lax.rsqrt(mean_square + EPS) * gain


def norm_back(rows, gain, upstream):
    outputs, pullback = jax.vjp(rms_norm, rows, gain)
    return pullback(upstream)


def shift(value, axis, by):
    size = lax.axis_size(axis)
    return lax.ppermute(value, axis, [(i, (i + by) % size) for i in range(size)])


def along(value, by):
    return lax.ppermute(value, "s", [(0, 1)] if by > 0 else [(1, 0)])


def pick(stack, index):
    return lax.dynamic_index_in_dim(stack, index, 0, keepdims=False)


def ring_scatter(stack, axis):
    me = lax.axis_index(axis)
    half = stack.shape[-1] // 2
    far = pick(stack, (me + 2) % 4)
    from_left = shift(far[..., :half], axis, 1)
    from_right = shift(far[..., half:], axis, -1)
    right = pick(stack, (me + 1) % 4)
    left = pick(stack, (me + 3) % 4)
    right = jnp.concatenate(
        [(right[..., :half].astype(F32) + from_left.astype(F32)).astype(BF), right[..., half:]], -1
    )
    left = jnp.concatenate(
        [left[..., :half], (left[..., half:].astype(F32) + from_right.astype(F32)).astype(BF)], -1
    )
    got_left = shift(right, axis, 1)
    got_right = shift(left, axis, -1)
    own = pick(stack, me)
    return (own.astype(F32) + got_left.astype(F32) + got_right.astype(F32)).astype(BF)


def ring_gather(block, axis):
    me = lax.axis_index(axis)
    half = block.shape[-1] // 2
    before = shift(block, axis, 1)
    after = shift(block, axis, -1)
    far_a = shift(before[..., :half], axis, 1)
    far_b = shift(after[..., half:], axis, -1)
    out = jnp.zeros((4,) + block.shape, block.dtype)
    for offset, piece in ((0, block), (1, after), (2, jnp.concatenate([far_a, far_b], -1)), (3, before)):
        out = lax.dynamic_update_index_in_dim(out, piece, (me + offset) % 4, 0)
    return out


def plane_scatter(blocks):
    half = blocks.shape[-1] // 2
    rows = blocks.shape[2]
    one = blocks[..., :half]
    two = jnp.swapaxes(blocks[..., half:], 0, 1)
    one = ring_scatter(one.reshape(4, 4 * rows, half), "y").reshape(4, rows, half)
    two = ring_scatter(two.reshape(4, 4 * rows, half), "x").reshape(4, rows, half)
    one = ring_scatter(one, "x")
    two = ring_scatter(two, "y")
    return jnp.concatenate([one, two], -1)


def plane_gather(block):
    half = block.shape[-1] // 2
    rows = block.shape[0]
    one = ring_gather(block[:, :half], "x")
    two = ring_gather(block[:, half:], "y")
    one = ring_gather(one.reshape(4 * rows, half), "y").reshape(4, 4, rows, half)
    two = ring_gather(two.reshape(4 * rows, half), "x").reshape(4, 4, rows, half)
    return jnp.concatenate([one, jnp.swapaxes(two, 0, 1)], -1)


def pair_scatter(block):
    me = lax.axis_index("zh")
    got = shift(pick(block, 1 - me), "zh", 1)
    return (pick(block, me).astype(F32) + got.astype(F32)).astype(BF)


def pair_gather(block, axis, dim):
    me = lax.axis_index(axis)
    got = shift(block, axis, 1)
    first = jnp.where(me == 0, block, got)
    second = jnp.where(me == 0, got, block)
    return jnp.concatenate([first, second], dim)


def small_sum(value):
    value = value + shift(value, "core", 1)
    value = value + shift(value, "zh", 1)
    for axis in ("x", "y"):
        value = value + shift(value, axis, 1)
        value = value + shift(value, axis, 2)
    return value


def heads(rows, count):
    return rows.reshape(2, count, HEADS, HD)


def attend_forward(queries, keys, values, allowed):
    raw = jnp.einsum("bqhe,bkhe->bhqk", queries, keys, preferred_element_type=F32)
    scores = jnp.where(allowed[:, None], raw * SCALE, NEG)
    highest = jnp.max(scores, axis=-1, keepdims=True)
    exponent = jnp.exp(scores - highest)
    summed = jnp.sum(exponent, axis=-1, keepdims=True)
    weights = (exponent / summed).astype(BF)
    mixed = jnp.einsum("bhqk,bkhe->bqhe", weights, values, preferred_element_type=F32)
    return mixed.astype(BF), highest + jnp.log(summed)


def attend_backward(queries, keys, values, allowed, log_summed, grad_mixed):
    raw = jnp.einsum("bqhe,bkhe->bhqk", queries, keys, preferred_element_type=F32)
    scores = jnp.where(allowed[:, None], raw * SCALE, NEG)
    weights = jnp.exp(scores - log_summed)
    grad_v = jnp.einsum(
        "bhqk,bqhe->bkhe", weights.astype(BF), grad_mixed, preferred_element_type=F32
    ).astype(BF)
    grad_w = jnp.einsum("bqhe,bkhe->bhqk", grad_mixed, values, preferred_element_type=F32)
    inner = jnp.sum(grad_w * weights, axis=-1, keepdims=True)
    grad_s = (weights * (grad_w - inner)).astype(BF)
    grad_q = (
        jnp.einsum("bhqk,bkhe->bqhe", grad_s, keys, preferred_element_type=F32) * SCALE
    ).astype(BF)
    grad_k = (
        jnp.einsum("bhqk,bqhe->bkhe", grad_s, queries, preferred_element_type=F32) * SCALE
    ).astype(BF)
    return grad_q, grad_k, grad_v


def on_section(flag, compute):
    return lax.cond(flag, compute, lambda: jax.tree.map(jnp.zeros_like, jax.eval_shape(compute)))


def shards(patch_io, byte_states, patch_lengths, patch_live, attn_qkv, attn_out, gains, ff_weights):
    section = lax.axis_index("s")
    core = lax.axis_index("core")
    first = section == 0
    second = section == 1
    w_qkv = attn_qkv[0]
    w_out = attn_out[0]
    gain_pair = gains[0]
    micro, seq, width = patch_io.shape[1], patch_io.shape[3], patch_io.shape[4]
    half_bytes = byte_states.shape[2]
    count = 2 * half_bytes
    rows = micro * seq
    own_rows = patch_io[0, :, 0].reshape(rows, width)
    own_f = own_rows.astype(F32)
    lower = byte_states[:, 0]
    upper = along(lower, -1)
    byte_rows = jnp.concatenate([lower, upper], axis=1).reshape(micro * count, width)
    lengths = patch_lengths[:, 0]
    live = patch_live[:, 0]
    ends = jnp.cumsum(lengths, axis=1)
    starts = ends - lengths
    spots = lax.iota(jnp.int32, count)
    allowed_bytes = (spots >= starts[..., None]) & (spots < ends[..., None])
    places = lax.iota(jnp.int32, seq)
    allowed_causal = (places[None, :] <= places[:, None])[None] & (
        (live[:, None, :] == 1) | (places[None, :] == places[:, None])[None]
    )

    def zeros(shape, dtype=BF):
        return jnp.zeros(shape, dtype)

    def encoder_forward():
        patch_norm = rms_norm(own_f, gain_pair[0]).astype(BF)
        byte_norm = rms_norm(byte_rows.astype(F32), gain_pair[1]).astype(BF)
        queries = dot(patch_norm, w_qkv[:, :width]).astype(BF)
        key_value = dot(byte_norm, w_qkv[:, width:]).astype(BF)
        keys = key_value[:, :width]
        values = key_value[:, width:]
        mixed, log_summed = attend_forward(
            heads(queries, seq), heads(keys, count), heads(values, count), allowed_bytes
        )
        mixed = mixed.reshape(rows, width)
        hidden = own_f + dot(mixed, w_out)
        return hidden.astype(BF), (patch_norm, byte_norm, queries, keys, values, mixed, log_summed)

    def encoder_backward(grad_sent, kept):
        patch_norm, byte_norm, queries, keys, values, mixed, log_summed = kept
        grad_mixed = dot_t(grad_sent, w_out).astype(BF)
        grad_q, grad_k, grad_v = attend_backward(
            heads(queries, seq),
            heads(keys, count),
            heads(values, count),
            allowed_bytes,
            log_summed,
            heads(grad_mixed, seq),
        )
        grad_q = grad_q.reshape(rows, width)
        grad_k = grad_k.reshape(micro * count, width)
        grad_v = grad_v.reshape(micro * count, width)
        grad_patch_rows, gain_patch = norm_back(own_f, gain_pair[0], dot_t(grad_q, w_qkv[:, :width]))
        grad_byte_norm = dot_t(grad_k, w_qkv[:, width : 2 * width]) + dot_t(grad_v, w_qkv[:, 2 * width :])
        grad_byte_rows, gain_byte = norm_back(byte_rows.astype(F32), gain_pair[1], grad_byte_norm)
        patch_grad = grad_sent.astype(F32) + grad_patch_rows
        return (
            patch_grad,
            grad_byte_rows.astype(BF),
            jnp.stack([gain_patch, gain_byte]),
            (grad_q, grad_k, grad_v),
        )

    def latent_layer(input_rows):
        cotangent = own_rows
        input_f = input_rows.astype(F32)
        input_norm = rms_norm(input_f, gain_pair[0]).astype(BF)
        qkv = dot(input_norm, w_qkv).astype(BF)
        queries = heads(qkv[:, :width], seq)
        keys = heads(qkv[:, width : 2 * width], seq)
        values = heads(qkv[:, 2 * width :], seq)
        mixed, log_summed = attend_forward(queries, keys, values, allowed_causal)
        mixed = mixed.reshape(rows, width)
        after = input_f + dot(mixed, w_out)
        ffn_norm = rms_norm(after, gain_pair[1]).astype(BF)
        gate = dot_t(ffn_norm, ff_weights[:, 0])
        upward = dot_t(ffn_norm, ff_weights[:, 1])
        sig = jax.nn.sigmoid(gate)
        activated = gate * sig
        hidden = (activated * upward).astype(BF)
        latents = after + dot(hidden, ff_weights[:, 2])
        grad_hidden = dot_t(cotangent, ff_weights[:, 2])
        grad_gate = (grad_hidden * upward * (sig * (1.0 + gate * (1.0 - sig)))).astype(BF)
        grad_upward = (grad_hidden * activated).astype(BF)
        grad_ffn_norm = dot(grad_gate, ff_weights[:, 0]) + dot(grad_upward, ff_weights[:, 1])
        grad_after_norm, gain_ffn = norm_back(after, gain_pair[1], grad_ffn_norm)
        grad_after = cotangent.astype(F32) + grad_after_norm
        grad_branch = grad_after.astype(BF)
        grad_mixed = dot_t(grad_branch, w_out).astype(BF)
        grad_q, grad_k, grad_v = attend_backward(
            queries, keys, values, allowed_causal, log_summed, heads(grad_mixed, seq)
        )
        grad_q, grad_k, grad_v = (g.reshape(rows, width) for g in (grad_q, grad_k, grad_v))
        grad_input_norm = dot_t(jnp.concatenate([grad_q, grad_k, grad_v], 1), w_qkv)
        grad_input_rows, gain_attn = norm_back(input_f, gain_pair[0], grad_input_norm)
        grad_input = (grad_after + grad_input_rows).astype(BF)
        return (
            latents,
            grad_input,
            jnp.stack([gain_attn, gain_ffn]),
            (input_norm, mixed, grad_branch, grad_q, grad_k, grad_v),
            (jnp.concatenate([grad_gate, grad_upward, hidden], 1), ffn_norm),
        )

    sent, kept = on_section(first, encoder_forward)
    arrived = along(sent, 1)
    latents, grad_input, latent_gain, attn_parts, ffn_parts = on_section(
        second, lambda: latent_layer(arrived)
    )
    returned = along(grad_input, -1)

    half = width // 2

    def mine(value):
        return lax.dynamic_slice_in_dim(value, core * half, half, value.ndim - 1)

    def other(value):
        return shift(lax.dynamic_slice_in_dim(value, (1 - core) * half, half, value.ndim - 1), "core", 1)

    def both(value):
        return jnp.concatenate([value, shift(value, "core", 1)], 0)

    def both_half(value):
        return jnp.concatenate([mine(value), other(value)], 0)

    acts = both(ffn_parts[0])
    norm_half = both_half(ffn_parts[1])
    cot_half = both_half(own_rows)
    units = ff_weights.shape[0]

    def ffn_grads():
        up_grad = t_dot(acts[:, : 2 * units], norm_half).astype(BF)
        down_grad = t_dot(acts[:, 2 * units :], cot_half).astype(BF)
        whole = jnp.concatenate([up_grad, down_grad], 0).reshape(3, 16, units // 16, half)
        return jnp.swapaxes(whole, 0, 1).reshape(4, 4, 3 * (units // 16), half)

    ff_blocks = on_section(second, ffn_grads)
    ff_sum = plane_scatter(ff_blocks).reshape(3, 2, units // 32, half)
    ff_sum = pair_scatter(jnp.swapaxes(ff_sum, 0, 1).reshape(2, 3 * (units // 32), half))
    ff_sum = jnp.swapaxes(ff_sum.reshape(3, 2, units // 64, half), 0, 1)
    ff_sum = pair_gather(pick(ff_sum, core), "core", -1) if False else jnp.where(
        core == 0,
        jnp.concatenate([ff_sum[0], shift(pick(ff_sum, 1 - core), "core", 1)], -1),
        jnp.concatenate([shift(pick(ff_sum, 1 - core), "core", 1), ff_sum[1]], -1),
    )
    ff_grad = jnp.where(second, jnp.swapaxes(ff_sum, 0, 1).astype(F32), 0.0)

    patch_grad, byte_grad_rows, encoder_gain, byte_parts = on_section(
        first, lambda: encoder_backward(returned, kept)
    )
    byte_grad_rows = byte_grad_rows.reshape(micro, count, width)
    upper_grad = along(byte_grad_rows[:, half_bytes:], 1)
    byte_grad = jnp.where(first, byte_grad_rows[:, :half_bytes], upper_grad)
    patch_out = jnp.where(first, patch_grad, latents)

    left_q = both(jnp.where(first, kept[0], attn_parts[0]))
    left_o = both(jnp.where(first, kept[5], attn_parts[1]))
    right_o = both_half(jnp.where(first, returned, attn_parts[2]))
    right_q = both_half(jnp.where(first, byte_parts[0], attn_parts[3]))
    left_b = both(kept[1])
    right_bk = both_half(byte_parts[1])
    right_bv = both_half(byte_parts[2])
    right_k = both_half(attn_parts[4])
    right_v = both_half(attn_parts[5])

    def byte_grads():
        return t_dot(left_b, right_bk).astype(BF), t_dot(left_b, right_bv).astype(BF)

    def patch_grads():
        return t_dot(left_q, right_k).astype(BF), t_dot(left_q, right_v).astype(BF)

    grads_k, grads_v = lax.cond(first, byte_grads, patch_grads)
    grads_q = t_dot(left_q, right_q).astype(BF)
    grads_o = t_dot(left_o, right_o).astype(BF)
    share = width // 16
    blocks = jnp.stack([g.reshape(16, share, half) for g in (grads_q, grads_k, grads_v, grads_o)], 1)
    reduced = plane_scatter(blocks.reshape(4, 4, 4 * share, half))
    reduced = pair_scatter(reduced.reshape(2, 2 * share, half))
    gathered = pair_gather(reduced, "zh", 0)
    gathered = plane_gather(gathered).reshape(16, 4, share, half)
    gathered = pair_gather(gathered, "core", -1)
    gathered = jnp.swapaxes(gathered, 0, 1).reshape(4, width, width).astype(F32)
    total_qkv = jnp.swapaxes(gathered[:3], 0, 1).reshape(width, 3 * width)
    total_out = gathered[3]
    total_gain = small_sum(jnp.where(first, encoder_gain, latent_gain))
    patch_out = patch_out.reshape(1, micro, 1, seq, width)
    return (
        patch_out,
        byte_grad[:, None],
        total_qkv[None],
        total_out[None],
        total_gain[None],
        ff_grad[None],
    )


def solution(mesh):
    fine = Mesh(mesh.devices.reshape(2, 4, 4, 2, 2), ("s",) + BATCH)
    in_specs = (
        P("s", None, BATCH, None, None),
        P(None, BATCH, "s", None),
        P(None, BATCH, None),
        P(None, BATCH, None),
        P("s", None, None),
        P("s", None, None),
        P("s", None, None),
        P(),
    )
    out_specs = (
        P("s", None, BATCH, None, None),
        P(None, BATCH, "s", None),
        P("s", None, None),
        P("s", None, None),
        P("s", None, None),
        P("s", BATCH, None, None),
    )
    return jax.shard_map(shards, mesh=fine, in_specs=in_specs, out_specs=out_specs, check_vma=False)
```

```python
import functools

import jax
import jax.numpy as jnp
from jax import lax
from jax.experimental import pallas as pl
from jax.experimental.pallas import tpu as pltpu
from jax.sharding import Mesh
from jax.sharding import PartitionSpec as P

HD = 64
SCALE = HD**-0.5
EPS = 1e-05
NEG = -1e30
BATCH = ("y", "x", "zh", "core")
BF = jnp.bfloat16
F32 = jnp.float32
D = 1024
HALF = 512
GROUP = 256
VMEM_BYTES = 60 * 1024 * 1024


def nn(a, b):
    return lax.dot_general(a, b, (((1,), (0,)), ((), ())), preferred_element_type=F32)


def nt(a, b):
    return lax.dot_general(a, b, (((1,), (1,)), ((), ())), preferred_element_type=F32)


def tn(a, b):
    return lax.dot_general(a, b, (((0,), (0,)), ((), ())), preferred_element_type=F32)


def inverse_rms(x):
    return lax.rsqrt(jnp.mean(x * x, axis=-1, keepdims=True) + EPS)


def norm_back(x, gain, up):
    r = inverse_rms(x)
    scaled = up * gain
    inner = jnp.mean(scaled * x, axis=-1, keepdims=True)
    return r * (scaled - x * (r * r * inner)), up * (x * r)


def stack_heads(rows):
    head = lax.broadcasted_iota(jnp.int32, rows.shape, 1) // HD
    return jnp.concatenate([jnp.where(head == h, rows, jnp.zeros_like(rows)) for h in range(4)], 0)


def unstack_heads(stacked):
    head = lax.broadcasted_iota(jnp.int32, (HD, GROUP), 1) // HD
    out = stacked[0:HD]
    for h in range(1, 4):
        out = jnp.where(head == h, stacked[h * HD : (h + 1) * HD], out)
    return out


def softmax_columns(scores):
    top = functools.reduce(jnp.maximum, [jnp.max(s, axis=0, keepdims=True) for s in scores])
    parts = [jnp.exp(s - top) for s in scores]
    inverse = 1.0 / sum(jnp.sum(p, axis=0, keepdims=True) for p in parts)
    return [(p * inverse).astype(BF) for p in parts]


def encode_lower(patch, low, w_qkv, gains, pn, q, bn, k, v):
    x = patch[...].astype(F32)
    normed = (x * inverse_rms(x) * gains[0:1]).astype(BF)
    pn[...] = normed
    q[...] = nn(normed, w_qkv[:, 0:D]).astype(BF)
    for i in range(2):
        at = pl.ds(i * 256, 256)
        b = low[at, :].astype(F32)
        normed = (b * inverse_rms(b) * gains[1:2]).astype(BF)
        bn[at, :] = normed
        k[at, :] = nn(normed, w_qkv[:, D : 2 * D]).astype(BF)
        v[at, :] = nn(normed, w_qkv[:, 2 * D :]).astype(BF)


def encode_rest(patch, up, w_qkv, w_out, gains, bounds, q, k_lo, v_lo, hb, o1, weights, bn, k, v):
    for i in range(2):
        at = pl.ds(i * 256, 256)
        b = up[at, :].astype(F32)
        normed = (b * inverse_rms(b) * gains[1:2]).astype(BF)
        bn[at, :] = normed
        k[at, :] = nn(normed, w_qkv[:, D : 2 * D]).astype(BF)
        v[at, :] = nn(normed, w_qkv[:, 2 * D :]).astype(BF)
    spot = lax.broadcasted_iota(jnp.int32, (256, GROUP), 0)
    for m in range(2):
        start = bounds[m, 0:1, :]
        end = bounds[m, 1:2, :]
        inside = [(spot + h * 256 >= start) & (spot + h * 256 < end) for h in range(2)]
        keys_at = pl.ds(m * 256, 256)
        for g in range(4):
            lanes = slice(g * GROUP, (g + 1) * GROUP)
            stacked = stack_heads(q[m * HD : (m + 1) * HD, lanes] * BF(SCALE))
            scores = [
                jnp.where(inside[h], nt(ref[keys_at, lanes], stacked), NEG)
                for h, ref in enumerate((k_lo, k))
            ]
            w = softmax_columns(scores)
            weights[m * 8 + g * 2] = w[0]
            weights[m * 8 + g * 2 + 1] = w[1]
            mixed = tn(w[0], v_lo[keys_at, lanes]) + tn(w[1], v[keys_at, lanes])
            o1[m * HD : (m + 1) * HD, lanes] = unstack_heads(mixed).astype(BF)
    hb[...] = (patch[...].astype(F32) + nn(o1[...], w_out[...])).astype(BF)


def latent_layer(
    ids, hb, cot, allowed, w_qkv, w_out, gains, w_ff,
    latents, dhb, gain_grad, xn, o2, acts, norms, grads_mine, grads_other,
    qkv, weights, ff_buf, acc_out, acc_norm, dqkv, sems,
):
    core = ids[0]
    units = w_ff.shape[1]
    step = ff_buf.shape[2]
    steps = units // step

    def fetch(i, slot):
        return pltpu.make_async_copy(
            w_ff.at[:, pl.ds(pl.multiple_of(i * step, 128), step), :], ff_buf.at[slot], sems.at[slot]
        )

    fetch(0, 0).start()
    x = hb[...].astype(F32)
    normed = (x * inverse_rms(x) * gains[0:1]).astype(BF)
    xn[...] = normed
    qkv[...] = nn(normed, w_qkv[...]).astype(BF)
    for m in range(2):
        rows = slice(m * HD, (m + 1) * HD)
        for g in range(4):
            lanes = slice(g * GROUP, (g + 1) * GROUP)
            k_lanes = slice(D + g * GROUP, D + (g + 1) * GROUP)
            v_lanes = slice(2 * D + g * GROUP, 2 * D + (g + 1) * GROUP)
            stacked = stack_heads(qkv[rows, lanes] * BF(SCALE))
            scores = jnp.where(allowed[m] > 0.5, nt(qkv[rows, k_lanes], stacked), NEG)
            (w,) = softmax_columns([scores])
            weights[m * 4 + g] = w
            o2[rows, lanes] = unstack_heads(tn(w, qkv[rows, v_lanes])).astype(BF)
    after = x + nn(o2[...], w_out[...])
    yn = (after * inverse_rms(after) * gains[1:2]).astype(BF)
    c = cot[...]
    for h in range(2):
        lanes = slice(h * HALF, (h + 1) * HALF)
        norms[h, 0:128, :] = yn[:, lanes]
        norms[h, 128:256, :] = c[:, lanes]
    acc_out[...] = after
    acc_norm[...] = jnp.zeros_like(acc_norm)

    def ff_step(i, carry):
        slot = lax.rem(i, 2)

        @pl.when(i + 1 < steps)
        def _():
            fetch(i + 1, 1 - slot).start()

        fetch(i, slot).wait()
        w_gate, w_up, w_down = ff_buf.at[slot, 0], ff_buf.at[slot, 1], ff_buf.at[slot, 2]
        gate = nt(yn, w_gate[...])
        upward = nt(yn, w_up[...])
        du = nt(c, w_down[...])
        sig = 1.0 / (1.0 + jnp.exp(-gate))
        active = gate * sig
        hidden = (active * upward).astype(BF)
        d_gate = (du * upward * (sig * (1.0 + gate * (1.0 - sig)))).astype(BF)
        d_up = (du * active).astype(BF)
        at = pl.ds(pl.multiple_of(i * step, 128), step)
        acts[0, :, at] = d_gate
        acts[1, :, at] = d_up
        acts[2, :, at] = hidden
        acc_out[...] += nn(hidden, w_down[...])
        acc_norm[...] += nn(d_gate, w_gate[...]) + nn(d_up, w_up[...])
        return carry

    lax.fori_loop(0, steps, ff_step, 0)
    latents[...] = acc_out[...]
    back, gain_rows = norm_back(after, gains[1:2], acc_norm[...])
    gain_grad[1:2, :] = jnp.sum(gain_rows, axis=0, keepdims=True)
    d_after = c.astype(F32) + back
    da = d_after.astype(BF)
    d_mixed = nt(da, w_out[...]).astype(BF)
    for m in range(2):
        rows = slice(m * HD, (m + 1) * HD)
        for g in range(4):
            lanes = slice(g * GROUP, (g + 1) * GROUP)
            k_lanes = slice(D + g * GROUP, D + (g + 1) * GROUP)
            v_lanes = slice(2 * D + g * GROUP, 2 * D + (g + 1) * GROUP)
            q_stacked = stack_heads(qkv[rows, lanes] * BF(SCALE))
            o_stacked = stack_heads(d_mixed[rows, lanes])
            w_low = weights[m * 4 + g]
            w = w_low.astype(F32)
            dw = nt(qkv[rows, v_lanes], o_stacked)
            inner = jnp.sum(dw * w, axis=0, keepdims=True)
            ds = (w * (dw - inner)).astype(BF)
            dqkv[rows, lanes] = (unstack_heads(tn(ds, qkv[rows, k_lanes])) * SCALE).astype(BF)
            dqkv[rows, k_lanes] = nn(ds, q_stacked).astype(BF)
            dqkv[rows, v_lanes] = nn(w_low, o_stacked).astype(BF)
    d_normed = nt(dqkv[...], w_qkv[...])
    back, gain_rows = norm_back(x, gains[0:1], d_normed)
    gain_grad[0:1, :] = jnp.sum(gain_rows, axis=0, keepdims=True)
    dhb[...] = (d_after + back).astype(BF)
    for h in range(2):
        lanes = slice(h * HALF, (h + 1) * HALF)

        def put(target):
            target[0:128, :] = dqkv[:, h * HALF : (h + 1) * HALF]
            target[128:256, :] = da[:, lanes]
            target[256:384, :] = dqkv[:, D + h * HALF : D + (h + 1) * HALF]
            target[384:512, :] = dqkv[:, 2 * D + h * HALF : 2 * D + (h + 1) * HALF]

        @pl.when(core == h)
        def _():
            put(grads_mine)

        @pl.when(core != h)
        def _():
            put(grads_other)


def encoder_attention_back(
    ids, dhb, w_out, q, k_lo, k_up, v_lo, v_up, weights, grads_mine, grads_other
):
    core = ids[0]
    d_mixed = nt(dhb[...], w_out[...]).astype(BF)
    for g in range(4):
        lanes = slice(g * GROUP, (g + 1) * GROUP)
        out_lanes = slice((g % 2) * GROUP, (g % 2 + 1) * GROUP)

        def put(at, value, g=g, out_lanes=out_lanes):
            @pl.when(core == g // 2)
            def _():
                grads_mine[at, out_lanes] = value

            @pl.when(core != g // 2)
            def _():
                grads_other[at, out_lanes] = value

        put(slice(128, 256), dhb[:, lanes])
        for m in range(2):
            rows = slice(m * HD, (m + 1) * HD)
            keys_at = pl.ds(m * 256, 256)
            q_stacked = stack_heads(q[rows, lanes] * BF(SCALE))
            o_stacked = stack_heads(d_mixed[rows, lanes])
            low = [weights[m * 8 + g * 2 + h] for h in range(2)]
            w = [piece.astype(F32) for piece in low]
            dw = [nt(ref[keys_at, lanes], o_stacked) for ref in (v_lo, v_up)]
            inner = sum(jnp.sum(a * b, axis=0, keepdims=True) for a, b in zip(dw, w))
            ds = [(b * (a - inner)).astype(BF) for a, b in zip(dw, w)]
            dq = tn(ds[0], k_lo[keys_at, lanes]) + tn(ds[1], k_up[keys_at, lanes])
            put(rows, (unstack_heads(dq) * SCALE).astype(BF))
            for h in range(2):
                base = h * HALF + m * 256
                put(slice(256 + base, 512 + base), nn(ds[h], q_stacked).astype(BF))
                put(slice(1280 + base, 1536 + base), nn(low[h], o_stacked).astype(BF))


def encoder_input_back(
    ids, dhb, patch, low, up, w_qkv, gains, grads_mine, grads_other, patch_grad, low_grad, up_grad, gain_grad
):
    core = ids[0]
    parts = ((grads_mine, core), (grads_other, 1 - core))

    def columns(block, which):
        return pl.ds(pl.multiple_of(block * D + which * HALF, HALF), HALF)

    up_norm = sum(nt(ref[0:128, :], w_qkv[:, columns(0, which)]) for ref, which in parts)
    x = patch[...].astype(F32)
    back, gain_rows = norm_back(x, gains[0:1], up_norm)
    gain_grad[0:1, :] = jnp.sum(gain_rows, axis=0, keepdims=True)
    patch_grad[...] = dhb[...].astype(F32) + back
    total = jnp.zeros((1, D), F32)
    for h, (source, target) in enumerate(((low, low_grad), (up, up_grad))):
        for m in range(2):
            base = h * HALF + m * 256
            d_norm = sum(
                nt(ref[256 + base : 512 + base, :], w_qkv[:, columns(1, which)])
                + nt(ref[1280 + base : 1536 + base, :], w_qkv[:, columns(2, which)])
                for ref, which in parts
            )
            at = slice(m * 256, (m + 1) * 256)
            back, gain_rows = norm_back(source[at, :].astype(F32), gains[1:2], d_norm)
            total = total + jnp.sum(gain_rows, axis=0, keepdims=True)
            target[at, :] = back.astype(BF)
    gain_grad[1:2, :] = total


def turn_encoder(pn, o1, bn_lo, bn_up, left, left_bytes):
    left[0:D, :] = pn[...].T
    left[D : 2 * D, :] = o1[...].T
    left_bytes[:, 0:HALF] = bn_lo[...].T
    left_bytes[:, HALF : 2 * HALF] = bn_up[...].T


def turn_latent(xn, o2, left):
    left[0:D, :] = xn[...].T
    left[D : 2 * D, :] = o2[...].T


def turn_acts(acts, out):
    units = acts.shape[2]
    for j in range(3):
        out[j * units : (j + 1) * units, :] = acts[j].T


def encoder_weights(ids, left, left_far, bytes_near, bytes_far, near, far, *blocks):
    u = ids[1]
    for k in range(4):
        at = pl.ds(pl.multiple_of(lax.rem(u + k, 4) * 256, 256), 256)
        low_at = pl.ds(pl.multiple_of(lax.rem(u + k, 4) * 256 + D, 256), 256)
        blocks[k][0] = (nn(left[at, :], near[0:128, :]) + nn(left_far[at, :], far[0:128, :])).astype(BF)
        blocks[k][3] = (
            nn(left[low_at, :], near[128:256, :]) + nn(left_far[low_at, :], far[128:256, :])
        ).astype(BF)
        blocks[k][1] = (
            nn(bytes_near[at, :], near[256:1280, :]) + nn(bytes_far[at, :], far[256:1280, :])
        ).astype(BF)
        blocks[k][2] = (
            nn(bytes_near[at, :], near[1280:2304, :]) + nn(bytes_far[at, :], far[1280:2304, :])
        ).astype(BF)


def latent_weights(ids, left, left_far, near, far, *blocks):
    u = ids[1]
    for k in range(4):
        at = pl.ds(pl.multiple_of(lax.rem(u + k, 4) * 256, 256), 256)
        low_at = pl.ds(pl.multiple_of(lax.rem(u + k, 4) * 256 + D, 256), 256)
        for block, (source, first) in enumerate(((at, 0), (at, 256), (at, 384), (low_at, 128))):
            rows = slice(first, first + 128)
            blocks[k][block] = (
                nn(left[source, :], near[rows, :]) + nn(left_far[source, :], far[rows, :])
            ).astype(BF)


def ff_weights_grad(ids, acts, acts_far, near, far, *blocks):
    core, u = ids[0], ids[1]
    units = acts.shape[0] // 3
    share = units // 16
    for k in range(4):
        there = lax.rem(u + k, 4)
        for v in range(4):
            chunk = jnp.where(core == 0, there * 4 + v, v * 4 + there)
            for j in range(3):
                at = pl.ds(pl.multiple_of(j * units + chunk * share, 16), share)
                rows = slice(0, 128) if j < 2 else slice(128, 256)
                blocks[k][v, j * share : (j + 1) * share, :] = (
                    nn(acts[at, :], near[rows, :]) + nn(acts_far[at, :], far[rows, :])
                ).astype(BF)


def sum_four(own, a, b, c):
    return own.astype(F32) + a.astype(F32) + b.astype(F32) + c.astype(F32)


def attn_sum_first(ids, own, a, b, c, *outs):
    v = ids[2]
    for k in range(4):
        at = pl.ds(pl.multiple_of(lax.rem(v + k, 4) * HD, HD), HD)
        for block in range(4):
            outs[k][block] = sum_four(
                own[block, at, :], a[block, at, :], b[block, at, :], c[block, at, :]
            ).astype(BF)


def attn_sum_second(ids, own, a, b, c, mine, other):
    zh = ids[3]
    for target, which in ((mine, zh), (other, 1 - zh)):
        at = pl.ds(pl.multiple_of(which * 32, 32), 32)
        for block in range(4):
            target[block] = sum_four(
                own[block, at, :], a[block, at, :], b[block, at, :], c[block, at, :]
            ).astype(BF)


def ff_sum_first(ids, own, a, b, c, *outs):
    v = ids[2]
    for k in range(4):
        at = lax.rem(v + k, 4)
        outs[k][...] = sum_four(own[at], a[at], b[at], c[at]).astype(BF)


def ff_sum_second(own, a, b, c, out):
    out[...] = sum_four(own[...], a[...], b[...], c[...]).astype(BF)


def final_attn(ids, *refs):
    pieces, (qkv, out) = refs[:8], refs[8:]
    step = pl.program_id(0)
    for side in range(2):
        core = ids[0] if side == 0 else 1 - ids[0]
        u = ids[1] if side == 0 else ids[2]
        v = ids[2] if side == 0 else ids[1]
        zh = ids[3]
        for k in range(4):
            piece = pieces[side * 4 + k]

            @pl.when(lax.rem(u + k, 4) == step)
            def _(piece=piece, v=v, core=core, zh=zh):
                for j in range(4):
                    for z in range(2):
                        row = lax.rem(v + j, 4) * HD + jnp.where(zh == 0, z, 1 - z) * 32
                        at = pl.ds(pl.multiple_of(row, 32), 32)
                        for block in range(4):
                            value = piece[j, z, block].astype(F32)
                            first = core * HALF + (block * D if block < 3 else 0)
                            lanes = pl.ds(pl.multiple_of(first, HALF), HALF)
                            if block < 3:
                                qkv[at, lanes] = value
                            else:
                                out[at, lanes] = value


SMEM = pltpu.MemorySpace.SMEM
VMEM = pltpu.MemorySpace.VMEM


def call(kernel, args, outs, scratch=(), spaces=None, flops=0, moved=0):
    spaces = spaces or {}
    specs = [pl.BlockSpec(memory_space=spaces.get(i, VMEM)) for i in range(len(args))]
    return pl.pallas_call(
        kernel,
        out_shape=[jax.ShapeDtypeStruct(s, t) for s, t in outs],
        in_specs=specs,
        out_specs=[pl.BlockSpec(memory_space=VMEM) for _ in outs],
        scratch_shapes=list(scratch),
        compiler_params=pltpu.CompilerParams(vmem_limit_bytes=VMEM_BYTES),
        cost_estimate=pl.CostEstimate(flops=flops, bytes_accessed=moved, transcendentals=0),
    )(*args)


def nothing(outs):
    def kernel(*refs):
        pass

    return pl.pallas_call(
        kernel,
        out_shape=[jax.ShapeDtypeStruct(s, t) for s, t in outs],
        out_specs=[pl.BlockSpec(memory_space=pl.ANY) for _ in outs],
    )()


def on_section(flag, kernel, args, outs, **rest):
    return lax.cond(
        flag, lambda: call(kernel, args, outs, **rest), lambda: nothing(outs)
    )


def shift(value, axis, by):
    size = lax.axis_size(axis)
    return lax.ppermute(value, axis, [(i, (i + by) % size) for i in range(size)])


def along(value, by):
    return lax.ppermute(value, "s", [(0, 1)] if by > 0 else [(1, 0)])


def plane_shift(value, which, by, sections=(0, 1)):
    pairs = []
    for s in sections:
        for y in range(4):
            for x in range(4):
                for core in range(2):
                    ty, tx = ((y + by) % 4, x) if core == which else (y, (x + by) % 4)
                    pairs.append((((s * 4 + y) * 4 + x) * 2 + core, ((s * 4 + ty) * 4 + tx) * 2 + core))
    return lax.ppermute(value, ("s", "y", "x", "core"), pairs)


def exchange(blocks, which, sections=(0, 1)):
    return [plane_shift(blocks[k], which, k, sections) for k in (1, 2, 3)]


def collect(block, which):
    return [block] + [plane_shift(block, which, -k) for k in (1, 2, 3)]


def small_sum(value):
    value = value + shift(value, "core", 1)
    value = value + shift(value, "zh", 1)
    for axis in ("x", "y"):
        value = value + shift(value, axis, 1)
        value = value + shift(value, axis, 2)
    return value


def shards(patch_io, byte_states, patch_lengths, patch_live, attn_qkv, attn_out, gains, ff_weights):
    section = lax.axis_index("s")
    core = lax.axis_index("core")
    zh = lax.axis_index("zh")
    y, x = lax.axis_index("y"), lax.axis_index("x")
    first = section == 0
    second = section == 1
    ids = jnp.stack([core, jnp.where(core == 0, y, x), jnp.where(core == 0, x, y), zh]).astype(jnp.int32)
    w_qkv = attn_qkv[0]
    w_out = attn_out[0]
    gain_pair = gains[0]
    micro, seq = patch_io.shape[1], patch_io.shape[3]
    half_bytes = byte_states.shape[2]
    units = ff_weights.shape[0]
    rows = micro * seq
    own_rows = patch_io.reshape(rows, D)
    lower = byte_states.reshape(micro * half_bytes, D)
    upper = along(lower, -1)
    w_ff = jnp.swapaxes(ff_weights, 0, 1)
    lengths = patch_lengths[:, 0]
    live = patch_live[:, 0]
    ends = jnp.cumsum(lengths, axis=1)
    bounds = jnp.tile(jnp.stack([ends - lengths, ends], 1), (1, 1, 4))
    places = lax.iota(jnp.int32, seq)
    causal = places[:, None] <= places[None, :]
    diagonal = places[:, None] == places[None, :]
    allowed = causal[None] & ((live[:, :, None] == 1) | diagonal[None])
    allowed = jnp.tile(allowed.astype(F32), (1, 1, 4))

    wide = ((rows, D), BF)
    tall = ((micro * half_bytes, D), BF)
    pn, q, bn_lo, k_lo, v_lo = on_section(
        first, encode_lower, (own_rows, lower, w_qkv, gain_pair), [wide, wide, tall, tall, tall]
    )
    hb, o1, weights, bn_up, k_up, v_up = on_section(
        first,
        encode_rest,
        (own_rows, upper, w_qkv, w_out, gain_pair, bounds, q, k_lo, v_lo),
        [wide, wide, ((16, 256, GROUP), BF), tall, tall, tall],
    )
    arrived = along(hb, 1)
    grads_short = ((512, HALF), BF)
    step = 256
    latents, dhb, latent_gain, xn, o2, acts, norms, lat_mine, lat_other = on_section(
        second,
        latent_layer,
        (ids, arrived, own_rows, allowed, w_qkv, w_out, gain_pair, w_ff),
        [
            ((rows, D), F32), wide, ((2, D), F32), wide, wide,
            ((3, rows, units), BF), ((2, 256, HALF), BF), grads_short, grads_short,
        ],
        spaces={0: SMEM, 7: pl.ANY},
        scratch=[
            pltpu.VMEM((rows, 3 * D), BF),
            pltpu.VMEM((8, HD, GROUP), BF),
            pltpu.VMEM((2, 3, step, D), BF),
            pltpu.VMEM((rows, D), F32),
            pltpu.VMEM((rows, D), F32),
            pltpu.VMEM((rows, 3 * D), BF),
            pltpu.SemaphoreType.DMA((2,)),
        ],
    )
    returned = along(dhb, -1)

    left, left_bytes = lax.cond(
        first,
        lambda: call(turn_encoder, (pn, o1, bn_lo, bn_up), [((2 * D, rows), BF), ((D, 2 * HALF), BF)]),
        lambda: call(turn_latent, (xn, o2), [((2 * D, rows), BF)]) + nothing([((D, 2 * HALF), BF)]),
    )
    left_far = shift(left, "core", 1)
    bytes_far = shift(left_bytes, "core", 1)

    (acts_t,) = on_section(second, turn_acts, (acts,), [((3 * units, rows), BF)])
    acts_far = shift(acts_t, "core", 1)
    norms_near = lax.dynamic_index_in_dim(norms, core, 0, keepdims=False)
    norms_far = shift(lax.dynamic_index_in_dim(norms, 1 - core, 0, keepdims=False), "core", 1)
    share = units // 16
    ff_block = ((4, 3 * share, HALF), BF)
    ff_blocks = on_section(
        second, ff_weights_grad, (ids, acts_t, acts_far, norms_near, norms_far), [ff_block] * 4, spaces={0: SMEM}
    )
    ff_line = ((3 * share, HALF), BF)
    ff_got = exchange(ff_blocks, 0, (1,))
    ff_blocks = on_section(second, ff_sum_first, (ids, ff_blocks[0], *ff_got), [ff_line] * 4, spaces={0: SMEM})
    ff_got = exchange(ff_blocks, 1, (1,))
    (ff_sum,) = on_section(second, ff_sum_second, (ff_blocks[0], *ff_got), [ff_line])
    ff_sum = ff_sum.reshape(3, 2, share // 2, HALF)
    ff_own = lax.dynamic_index_in_dim(ff_sum, zh, 1, keepdims=False)
    ff_far = shift(lax.dynamic_index_in_dim(ff_sum, 1 - zh, 1, keepdims=False), "zh", 1)
    ff_sum = (ff_own.astype(F32) + ff_far.astype(F32)).astype(BF).reshape(3, 2, share // 4, HALF)
    ff_own = lax.dynamic_index_in_dim(ff_sum, core, 1, keepdims=False)
    ff_far = shift(lax.dynamic_index_in_dim(ff_sum, 1 - core, 1, keepdims=False), "core", 1)
    ff_pair = jnp.stack([jnp.where(core == 0, ff_own, ff_far), jnp.where(core == 0, ff_far, ff_own)], 2)
    ff_grad = jnp.swapaxes(ff_pair.reshape(3, share // 4, D), 0, 1).astype(F32)
    ff_grad = jnp.where(second, ff_grad, 0.0)

    grads_long = ((2304, HALF), BF)
    enc_mine, enc_other = on_section(
        first,
        encoder_attention_back,
        (ids, returned, w_out, q, k_lo, k_up, v_lo, v_up, weights),
        [grads_long, grads_long],
        spaces={0: SMEM},
    )
    enc_far = shift(enc_other, "core", 1)
    lat_far = shift(lat_other, "core", 1)
    attn_block = ((4, 256, HALF), BF)
    blocks = lax.cond(
        first,
        lambda: call(
            encoder_weights,
            (ids, left, left_far, left_bytes, bytes_far, enc_mine, enc_far),
            [attn_block] * 4,
            spaces={0: SMEM},
        ),
        lambda: call(
            latent_weights, (ids, left, left_far, lat_mine, lat_far), [attn_block] * 4, spaces={0: SMEM}
        ),
    )
    patch_grad, low_grad, up_grad, encoder_gain = on_section(
        first,
        encoder_input_back,
        (ids, returned, own_rows, lower, upper, w_qkv, gain_pair, enc_mine, enc_other),
        [((rows, D), F32), tall, tall, ((2, D), F32)],
        spaces={0: SMEM},
    )
    up_arrived = along(up_grad, 1)
    byte_grad = jnp.where(first, low_grad, up_arrived)
    patch_out = jnp.where(first, patch_grad, latents)

    got = exchange(blocks, 0)
    blocks = call(attn_sum_first, (ids, blocks[0], *got), [((4, HD, HALF), BF)] * 4, spaces={0: SMEM})
    got = exchange(blocks, 1)
    mine, other = call(attn_sum_second, (ids, blocks[0], *got), [((4, 32, HALF), BF)] * 2, spaces={0: SMEM})
    mine = (mine.astype(F32) + shift(other, "zh", 1).astype(F32)).astype(BF)
    piece = jnp.stack([mine, shift(mine, "zh", 1)])
    piece = jnp.stack(collect(piece, 1))
    pieces = collect(piece, 0)
    pieces = pieces + [shift(p, "core", 1) for p in pieces]
    whole = lambda p: pl.BlockSpec(p.shape, lambda i, n=p.ndim: (0,) * n)
    total_qkv, total_out = pl.pallas_call(
        final_attn,
        grid=(4,),
        out_shape=[jax.ShapeDtypeStruct((D, 3 * D), F32), jax.ShapeDtypeStruct((D, D), F32)],
        in_specs=[pl.BlockSpec(memory_space=SMEM)] + [whole(p) for p in pieces],
        out_specs=[pl.BlockSpec((256, 3 * D), lambda i: (i, 0)), pl.BlockSpec((256, D), lambda i: (i, 0))],
        compiler_params=pltpu.CompilerParams(vmem_limit_bytes=VMEM_BYTES),
    )(ids, *pieces)
    total_gain = small_sum(jnp.where(first, encoder_gain, latent_gain))
    return (
        patch_out.reshape(1, micro, 1, seq, D),
        byte_grad.reshape(micro, 1, half_bytes, D),
        total_qkv[None],
        total_out[None],
        total_gain[None],
        ff_grad[None],
    )


def solution(mesh):
    fine = Mesh(mesh.devices.reshape(2, 4, 4, 2, 2), ("s",) + BATCH)
    in_specs = (
        P("s", None, BATCH, None, None),
        P(None, BATCH, "s", None),
        P(None, BATCH, None),
        P(None, BATCH, None),
        P("s", None, None),
        P("s", None, None),
        P("s", None, None),
        P(),
    )
    out_specs = (
        P("s", None, BATCH, None, None),
        P(None, BATCH, "s", None),
        P("s", None, None),
        P("s", None, None),
        P("s", None, None),
        P("s", BATCH, None, None),
    )
    return jax.shard_map(shards, mesh=fine, in_specs=in_specs, out_specs=out_specs, check_vma=False)
```

```python
import functools

import jax
import jax.numpy as jnp
from jax import lax
from jax.experimental import pallas as pl
from jax.experimental.pallas import tpu as pltpu
from jax.sharding import Mesh
from jax.sharding import PartitionSpec as P

HD = 64
SCALE = HD**-0.5
EPS = 1e-05
NEG = -1e30
BATCH = ("y", "x", "zh", "core")
BF = jnp.bfloat16
F32 = jnp.float32
D = 1024
HALF = 512
GROUP = 256
VMEM_BYTES = 60 * 1024 * 1024


def nn(a, b):
    return lax.dot_general(a, b, (((1,), (0,)), ((), ())), preferred_element_type=F32)


def nt(a, b):
    return lax.dot_general(a, b, (((1,), (1,)), ((), ())), preferred_element_type=F32)


def tn(a, b):
    return lax.dot_general(a, b, (((0,), (0,)), ((), ())), preferred_element_type=F32)


def inverse_rms(x):
    return lax.rsqrt(jnp.mean(x * x, axis=-1, keepdims=True) + EPS)


def norm_back(x, gain, up):
    r = inverse_rms(x)
    scaled = up * gain
    inner = jnp.mean(scaled * x, axis=-1, keepdims=True)
    return r * (scaled - x * (r * r * inner)), up * (x * r)


def stack_heads(rows):
    head = lax.broadcasted_iota(jnp.int32, rows.shape, 1) // HD
    return jnp.concatenate([jnp.where(head == h, rows, jnp.zeros_like(rows)) for h in range(4)], 0)


def unstack_heads(stacked):
    head = lax.broadcasted_iota(jnp.int32, (HD, GROUP), 1) // HD
    out = stacked[0:HD]
    for h in range(1, 4):
        out = jnp.where(head == h, stacked[h * HD : (h + 1) * HD], out)
    return out


def softmax_columns(scores):
    top = functools.reduce(jnp.maximum, [jnp.max(s, axis=0, keepdims=True) for s in scores])
    parts = [jnp.exp(s - top) for s in scores]
    inverse = 1.0 / sum(jnp.sum(p, axis=0, keepdims=True) for p in parts)
    return [(p * inverse).astype(BF) for p in parts]


def encode_lower(patch, low, w_qkv, gains, pn, q, bn, k, v):
    x = patch[...].astype(F32)
    normed = (x * inverse_rms(x) * gains[0:1]).astype(BF)
    pn[...] = normed
    q[...] = nn(normed, w_qkv[:, 0:D]).astype(BF)
    for i in range(2):
        at = pl.ds(i * 256, 256)
        b = low[at, :].astype(F32)
        normed = (b * inverse_rms(b) * gains[1:2]).astype(BF)
        bn[at, :] = normed
        k[at, :] = nn(normed, w_qkv[:, D : 2 * D]).astype(BF)
        v[at, :] = nn(normed, w_qkv[:, 2 * D :]).astype(BF)


def encode_rest(m, patch, up, w_qkv, w_out, gains, bounds, q, k_lo, v_lo, hb, o1, weights, bn, k, v):
    b = up[...].astype(F32)
    normed = (b * inverse_rms(b) * gains[1:2]).astype(BF)
    bn[...] = normed
    k[...] = nn(normed, w_qkv[:, D : 2 * D]).astype(BF)
    v[...] = nn(normed, w_qkv[:, 2 * D :]).astype(BF)
    spot = lax.broadcasted_iota(jnp.int32, (256, GROUP), 0)
    start = bounds[m, 0:1, :]
    end = bounds[m, 1:2, :]
    inside = [(spot + h * 256 >= start) & (spot + h * 256 < end) for h in range(2)]
    low_at = slice(m * 256, (m + 1) * 256)
    rows = slice(m * HD, (m + 1) * HD)
    for g in range(4):
        lanes = slice(g * GROUP, (g + 1) * GROUP)
        stacked = stack_heads(q[rows, lanes] * BF(SCALE))
        scores = [
            jnp.where(inside[h], nt(keys, stacked), NEG)
            for h, keys in enumerate((k_lo[low_at, lanes], k[:, lanes]))
        ]
        w = softmax_columns(scores)
        weights[g * 2] = w[0]
        weights[g * 2 + 1] = w[1]
        mixed = tn(w[0], v_lo[low_at, lanes]) + tn(w[1], v[:, lanes])
        o1[:, lanes] = unstack_heads(mixed).astype(BF)
    hb[...] = (patch[rows, :].astype(F32) + nn(o1[...], w_out[...])).astype(BF)


def latent_layer(
    ids, hb_a, hb_b, cot, allowed, w_qkv, w_out, gains, w_ff, early_a, early_b,
    latents, dhb, gain_grad, xn, o2, acts, norms, vo_mine, vo_other, qk_mine, qk_other,
    qkv, weights, ff_buf, acc_out, acc_norm, dqkv, sems,
):
    core = ids[0]
    units = w_ff.shape[1]
    step = ff_buf.shape[2]
    steps = units // step

    def fetch(i, slot):
        return pltpu.make_async_copy(
            w_ff.at[:, pl.ds(pl.multiple_of(i * step, 128), step), :], ff_buf.at[slot], sems.at[slot]
        )

    fetch(0, 0).start()
    x = jnp.concatenate([hb_a[...], hb_b[...]], 0).astype(F32)
    normed = (x * inverse_rms(x) * gains[0:1]).astype(BF)
    xn[...] = normed
    qkv[...] = nn(normed, w_qkv[...]).astype(BF)
    for m in range(2):
        rows = slice(m * HD, (m + 1) * HD)
        for g in range(4):
            lanes = slice(g * GROUP, (g + 1) * GROUP)
            k_lanes = slice(D + g * GROUP, D + (g + 1) * GROUP)
            v_lanes = slice(2 * D + g * GROUP, 2 * D + (g + 1) * GROUP)
            stacked = stack_heads(qkv[rows, lanes] * BF(SCALE))
            scores = jnp.where(allowed[m] > 0.5, nt(qkv[rows, k_lanes], stacked), NEG)
            (w,) = softmax_columns([scores])
            weights[m * 4 + g] = w
            o2[rows, lanes] = unstack_heads(tn(w, qkv[rows, v_lanes])).astype(BF)
    after = x + nn(o2[...], w_out[...])
    yn = (after * inverse_rms(after) * gains[1:2]).astype(BF)
    c = cot[...]
    for h in range(2):
        lanes = slice(h * HALF, (h + 1) * HALF)
        norms[h, 0:128, :] = yn[:, lanes]
        norms[h, 128:256, :] = c[:, lanes]
    acc_out[...] = after
    acc_norm[...] = jnp.zeros_like(acc_norm)

    def ff_step(i, carry):
        slot = lax.rem(i, 2)

        @pl.when(i + 1 < steps)
        def _():
            fetch(i + 1, 1 - slot).start()

        fetch(i, slot).wait()
        w_gate, w_up, w_down = ff_buf.at[slot, 0], ff_buf.at[slot, 1], ff_buf.at[slot, 2]
        gate = nt(yn, w_gate[...])
        upward = nt(yn, w_up[...])
        du = nt(c, w_down[...])
        sig = 1.0 / (1.0 + jnp.exp(-gate))
        active = gate * sig
        hidden = (active * upward).astype(BF)
        d_gate = (du * upward * (sig * (1.0 + gate * (1.0 - sig)))).astype(BF)
        d_up = (du * active).astype(BF)
        at = pl.ds(pl.multiple_of(i * step, 128), step)
        acts[0, at, :] = d_gate.T
        acts[1, at, :] = d_up.T
        acts[2, at, :] = hidden.T
        acc_out[...] += nn(hidden, w_down[...])
        acc_norm[...] += nn(d_gate, w_gate[...]) + nn(d_up, w_up[...])
        return carry

    lax.fori_loop(0, steps, ff_step, 0)
    latents[...] = acc_out[...]
    back, gain_rows = norm_back(after, gains[1:2], acc_norm[...])
    gain_grad[1:2, :] = jnp.sum(gain_rows, axis=0, keepdims=True)
    d_after = c.astype(F32) + back
    da = d_after.astype(BF)
    d_mixed = nt(da, w_out[...]).astype(BF)
    for m in range(2):
        rows = slice(m * HD, (m + 1) * HD)
        for g in range(4):
            lanes = slice(g * GROUP, (g + 1) * GROUP)
            k_lanes = slice(D + g * GROUP, D + (g + 1) * GROUP)
            v_lanes = slice(2 * D + g * GROUP, 2 * D + (g + 1) * GROUP)
            q_stacked = stack_heads(qkv[rows, lanes] * BF(SCALE))
            o_stacked = stack_heads(d_mixed[rows, lanes])
            w_low = weights[m * 4 + g]
            w = w_low.astype(F32)
            dw = nt(qkv[rows, v_lanes], o_stacked)
            inner = jnp.sum(dw * w, axis=0, keepdims=True)
            ds = (w * (dw - inner)).astype(BF)
            dqkv[rows, lanes] = (unstack_heads(tn(ds, qkv[rows, k_lanes])) * SCALE).astype(BF)
            dqkv[rows, k_lanes] = nn(ds, q_stacked).astype(BF)
            dqkv[rows, v_lanes] = nn(w_low, o_stacked).astype(BF)
    d_normed = nt(dqkv[...], w_qkv[...])
    back, gain_rows = norm_back(x, gains[0:1], d_normed)
    gain_grad[0:1, :] = jnp.sum(gain_rows, axis=0, keepdims=True)
    dhb[...] = (d_after + back).astype(BF)
    for h in range(2):
        lanes = slice(h * HALF, (h + 1) * HALF)

        def put(vo, qk, h=h, lanes=lanes):
            vo[0:128, :] = da[:, lanes]
            vo[128:256, :] = dqkv[:, 2 * D + h * HALF : 2 * D + (h + 1) * HALF]
            qk[0:128, :] = dqkv[:, lanes]
            qk[128:256, :] = dqkv[:, D + h * HALF : D + (h + 1) * HALF]

        @pl.when(core == h)
        def _():
            put(vo_mine, qk_mine)

        @pl.when(core != h)
        def _():
            put(vo_other, qk_other)


def half_of(core, g, mine, other):
    lanes = slice((g % 2) * GROUP, (g % 2 + 1) * GROUP)

    def put(at, value):
        @pl.when(core == g // 2)
        def _():
            mine[at, lanes] = value

        @pl.when(core != g // 2)
        def _():
            other[at, lanes] = value

    return put


def encoder_values_back(ids, dhb, w_out, w_a, w_b, d_mixed, mine, other):
    d_mixed[...] = nt(dhb[...], w_out[...]).astype(BF)
    for g in range(4):
        lanes = slice(g * GROUP, (g + 1) * GROUP)
        put = half_of(ids[0], g, mine, other)
        put(slice(0, 128), dhb[:, lanes])
        for m, weights in enumerate((w_a, w_b)):
            o_stacked = stack_heads(d_mixed[m * HD : (m + 1) * HD, lanes])
            for h in range(2):
                base = 128 + h * HALF + m * 256
                put(slice(base, base + 256), nn(weights[g * 2 + h], o_stacked).astype(BF))


def encoder_scores_back(
    ids, d_mixed, q, k_lo, v_lo, k_a, k_b, v_a, v_b, w_a, w_b, mine, other
):
    for g in range(4):
        lanes = slice(g * GROUP, (g + 1) * GROUP)
        put = half_of(ids[0], g, mine, other)
        for m, (k_up, v_up, weights) in enumerate(((k_a, v_a, w_a), (k_b, v_b, w_b))):
            rows = slice(m * HD, (m + 1) * HD)
            low_at = slice(m * 256, (m + 1) * 256)
            q_stacked = stack_heads(q[rows, lanes] * BF(SCALE))
            o_stacked = stack_heads(d_mixed[rows, lanes])
            w = [weights[g * 2 + h].astype(F32) for h in range(2)]
            dw = [nt(values, o_stacked) for values in (v_lo[low_at, lanes], v_up[:, lanes])]
            inner = sum(jnp.sum(a * b, axis=0, keepdims=True) for a, b in zip(dw, w))
            ds = [(b * (a - inner)).astype(BF) for a, b in zip(dw, w)]
            dq = tn(ds[0], k_lo[low_at, lanes]) + tn(ds[1], k_up[:, lanes])
            put(rows, (unstack_heads(dq) * SCALE).astype(BF))
            for h in range(2):
                base = 128 + h * HALF + m * 256
                put(slice(base, base + 256), nn(ds[h], q_stacked).astype(BF))


def both_columns(core, block, w_qkv):
    return [
        w_qkv[:, pl.ds(pl.multiple_of(block * D + which * HALF, HALF), HALF)] for which in (core, 1 - core)
    ]


def bytes_back(core, h, m, source, w_qkv, gains, vo, qk):
    at = slice(128 + h * HALF + m * 256, 384 + h * HALF + m * 256)
    d_norm = sum(
        nt(ref[at, :], columns)
        for block, pair in ((1, qk), (2, vo))
        for ref, columns in zip(pair, both_columns(core, block, w_qkv))
    )
    back, gain_rows = norm_back(source.astype(F32), gains[1:2], d_norm)
    return back.astype(BF), jnp.sum(gain_rows, axis=0, keepdims=True)


def encoder_upper_back(
    ids, up_a, up_b, w_qkv, gains, vo_mine, vo_other, qk_mine, qk_other, after, up_grad, gain_grad
):
    total = jnp.zeros((1, D), F32)
    for m, source in enumerate((up_a, up_b)):
        back, rows = bytes_back(
            ids[0], 1, m, source[...], w_qkv, gains, (vo_mine, vo_other), (qk_mine, qk_other)
        )
        up_grad[m * 256 : (m + 1) * 256, :] = back
        total = total + rows
    gain_grad[...] = total


def encoder_lower_back(
    ids, dhb, patch, low, w_qkv, gains, vo_mine, vo_other, qk_mine, qk_other, after,
    patch_grad, low_grad, gain_grad,
):
    core = ids[0]
    up_norm = sum(
        nt(ref[0:128, :], columns)
        for ref, columns in zip((qk_mine, qk_other), both_columns(core, 0, w_qkv))
    )
    back, gain_rows = norm_back(patch[...].astype(F32), gains[0:1], up_norm)
    gain_grad[0:1, :] = jnp.sum(gain_rows, axis=0, keepdims=True)
    patch_grad[...] = dhb[...].astype(F32) + back
    total = jnp.zeros((1, D), F32)
    for m in range(2):
        at = slice(m * 256, (m + 1) * 256)
        back, rows = bytes_back(core, 0, m, low[at, :], w_qkv, gains, (vo_mine, vo_other), (qk_mine, qk_other))
        low_grad[at, :] = back
        total = total + rows
    gain_grad[1:2, :] = total


def turn_encoder(pn, o_a, o_b, bn_lo, bn_a, bn_b, left, left_bytes):
    left[0:D, :] = pn[...].T
    left[D : 2 * D, :] = jnp.concatenate([o_a[...], o_b[...]], 0).T
    left_bytes[:, 0:HALF] = bn_lo[...].T
    left_bytes[:, HALF : HALF + 256] = bn_a[...].T
    left_bytes[:, HALF + 256 : 2 * HALF] = bn_b[...].T


def turn_latent(xn, o2, left):
    left[0:D, :] = xn[...].T
    left[D : 2 * D, :] = o2[...].T


def rows_of_both(left, left_far, at):
    return jnp.concatenate([left[at, :], left_far[at, :]], 1)


def below(near, far, rows):
    return jnp.concatenate([near[rows, :], far[rows, :]], 0)


def encoder_weights(values, ids, left, left_far, bytes_near, bytes_far, near, far, *blocks):
    u = ids[1]
    short = below(near, far, slice(0, 128))
    short_block, long_block, base = (1, 0, D) if values else (0, 1, 0)
    for k in range(4):
        first = lax.rem(u + k, 4) * 256
        at = pl.ds(pl.multiple_of(first, 256), 256)
        short_at = pl.ds(pl.multiple_of(first + base, 256), 256)
        blocks[k][short_block] = nn(rows_of_both(left, left_far, short_at), short).astype(BF)
        blocks[k][long_block] = (
            nn(bytes_near[at, :], near[128:1152, :]) + nn(bytes_far[at, :], far[128:1152, :])
        ).astype(BF)


def latent_weights(values, ids, left, left_far, near, far, *blocks):
    u = ids[1]
    short = below(near, far, slice(0, 128))
    long = below(near, far, slice(128, 256))
    short_block, long_block, base = (1, 0, D) if values else (0, 1, 0)
    for k in range(4):
        first = lax.rem(u + k, 4) * 256
        at = pl.ds(pl.multiple_of(first, 256), 256)
        short_at = pl.ds(pl.multiple_of(first + base, 256), 256)
        blocks[k][short_block] = nn(rows_of_both(left, left_far, short_at), short).astype(BF)
        blocks[k][long_block] = nn(rows_of_both(left, left_far, at), long).astype(BF)


def ff_weights_grad(ids, acts_a, acts_b, acts_c, acts_d, norms_a, norms_b, norms_c, norms_d, *blocks):
    core, u = ids[0], ids[1]
    acts = (acts_a, acts_b, acts_c, acts_d)
    norms = (norms_a, norms_b, norms_c, norms_d)
    normed = jnp.concatenate([ref[0:128, :] for ref in norms], 0)
    cot = jnp.concatenate([ref[128:256, :] for ref in norms], 0)
    for k in range(4):
        there = lax.rem(u + k, 4)
        for v in range(4):
            chunk = jnp.where(core == 0, there * 4 + v, v * 4 + there)
            for j in range(3):
                rows = jnp.concatenate([ref[j, chunk] for ref in acts], 1)
                blocks[k][v, j] = nn(rows, normed if j < 2 else cot).astype(BF)


def sum_four(own, a, b, c):
    return own.astype(F32) + a.astype(F32) + b.astype(F32) + c.astype(F32)


def pack_gain(value):
    high = value.astype(BF)
    low = (value - high.astype(F32)).astype(BF)
    return jnp.concatenate(
        [high.astype(F32), low.astype(F32), jnp.zeros((8, HALF), F32)], 0
    ).astype(BF)


def unpack_gain(rows):
    rows = rows.astype(F32)
    return rows[0:4] + rows[4:8]


GAIN_AT = slice(128, 144)


def attn_sum_first(ids, own, a, b, c, *outs):
    v = ids[2]
    for k in range(4):
        at = pl.ds(pl.multiple_of(lax.rem(v + k, 4) * HD, HD), HD)
        for block in range(2):
            outs[k][block * HD : (block + 1) * HD, :] = sum_four(
                own[block, at, :], a[block, at, :], b[block, at, :], c[block, at, :]
            ).astype(BF)


def attn_sum_first_gain(ids, own, a, b, c, enc_gain, up_gain, lat_gain, *outs):
    attn_sum_first(ids, own, a, b, c, *outs)
    first = ids[4] == 0
    gain = jnp.where(
        first, jnp.concatenate([enc_gain[0:1, :], enc_gain[1:2, :] + up_gain[...]], 0), lat_gain[...]
    )
    halves = [gain[i : i + 1, h * HALF : (h + 1) * HALF] for i in range(2) for h in range(2)]
    packed = pack_gain(jnp.concatenate(halves, 0))
    for out in outs:
        out[GAIN_AT, :] = packed


def sum_all(*refs):
    refs, out = refs[:-1], refs[-1]
    out[0:128, :] = sum(ref[0:128, :].astype(F32) for ref in refs).astype(BF)
    if out.shape[0] > 128:
        out[GAIN_AT, :] = pack_gain(sum(unpack_gain(ref[GAIN_AT, :]) for ref in refs))


def stack_rows(*refs):
    refs, out = refs[:-1], refs[-1]
    for j, ref in enumerate(refs):
        out[j * 128 : (j + 1) * 128, :] = ref[0:128, :]
    if out.shape[0] > 512:
        out[512:528, :] = refs[0][GAIN_AT, :]


def ff_sum_first(ids, own, a, b, c, *outs):
    v = ids[2]
    for k in range(4):
        at = lax.rem(v + k, 4)
        outs[k][...] = sum_four(own[at], a[at], b[at], c[at]).astype(BF)


def ff_sum_second(own, a, b, c, out):
    out[...] = sum_four(own[...], a[...], b[...], c[...]).astype(BF)


def place(ids, pieces, targets):
    step = pl.program_id(0)
    for side in range(2):
        core = ids[0] if side == 0 else 1 - ids[0]
        u = ids[1] if side == 0 else ids[2]
        v = ids[2] if side == 0 else ids[1]
        for k in range(4):
            piece = pieces[side * 4 + k]

            @pl.when(lax.rem(u + k, 4) == step)
            def _(piece=piece, v=v, core=core):
                for j in range(4):
                    at = pl.ds(pl.multiple_of(lax.rem(v + j, 4) * HD, HD), HD)
                    for block, (target, column) in enumerate(targets):
                        lanes = pl.ds(pl.multiple_of(core * HALF + column, HALF), HALF)
                        first = j * 128 + block * HD
                        target[at, lanes] = piece[first : first + HD, :].astype(F32)


def final_values(ids, *refs):
    pieces, (qkv, out) = refs[:8], refs[8:]
    place(ids, pieces, ((qkv, 0), (out, 0)))


def final_queries(ids, *refs):
    pieces, (kept, qkv, gain) = refs[:8], refs[8:]
    place(ids, pieces, ((qkv, 0), (qkv, D)))
    total = sum(unpack_gain(piece[512:528, :]) for piece in pieces)
    for i in range(2):
        for h in range(2):
            gain[i : i + 1, h * HALF : (h + 1) * HALF] = total[2 * i + h : 2 * i + h + 1, :]


SMEM = pltpu.MemorySpace.SMEM
VMEM = pltpu.MemorySpace.VMEM


def call(kernel, args, outs, scratch=(), spaces=None, flops=0, moved=0):
    spaces = spaces or {}
    specs = [pl.BlockSpec(memory_space=spaces.get(i, VMEM)) for i in range(len(args))]
    return pl.pallas_call(
        kernel,
        out_shape=[jax.ShapeDtypeStruct(s, t) for s, t in outs],
        in_specs=specs,
        out_specs=[pl.BlockSpec(memory_space=VMEM) for _ in outs],
        scratch_shapes=list(scratch),
        compiler_params=pltpu.CompilerParams(vmem_limit_bytes=VMEM_BYTES),
        cost_estimate=pl.CostEstimate(flops=flops, bytes_accessed=moved, transcendentals=0),
    )(*args)


def nothing(outs):
    def kernel(*refs):
        pass

    return pl.pallas_call(
        kernel,
        out_shape=[jax.ShapeDtypeStruct(s, t) for s, t in outs],
        out_specs=[pl.BlockSpec(memory_space=pl.ANY) for _ in outs],
    )()


def on_section(flag, kernel, args, outs, **rest):
    return lax.cond(
        flag, lambda: call(kernel, args, outs, **rest), lambda: nothing(outs)
    )


def along(value, by):
    return lax.ppermute(value, "s", [(0, 1)] if by > 0 else [(1, 0)])


def swap(value, axis, sections=(0, 1)):
    pairs = [(s * 2 + i, s * 2 + 1 - i) for s in sections for i in range(2)]
    return lax.ppermute(value, ("s", axis), pairs)


def plane_shift(value, which, by, sections=(0, 1)):
    pairs = []
    for s in sections:
        for y in range(4):
            for x in range(4):
                for core in range(2):
                    ty, tx = ((y + by) % 4, x) if core == which else (y, (x + by) % 4)
                    pairs.append((((s * 4 + y) * 4 + x) * 2 + core, ((s * 4 + ty) * 4 + tx) * 2 + core))
    return lax.ppermute(value, ("s", "y", "x", "core"), pairs)


def exchange(blocks, which, sections=(0, 1)):
    return [plane_shift(blocks[k], which, k, sections) for k in (1, 2, 3)]


def collect(block, which):
    return [block] + [plane_shift(block, which, -k) for k in (1, 2, 3)]


def pick(stack, index, dim):
    return lax.dynamic_index_in_dim(stack, index, dim, keepdims=False)


def shards(patch_io, byte_states, patch_lengths, patch_live, attn_qkv, attn_out, gains, ff_weights):
    section = lax.axis_index("s")
    core = lax.axis_index("core")
    zh = lax.axis_index("zh")
    y, x = lax.axis_index("y"), lax.axis_index("x")
    first = section == 0
    second = section == 1
    ids = jnp.stack([core, jnp.where(core == 0, y, x), jnp.where(core == 0, x, y), zh, section])
    ids = ids.astype(jnp.int32)
    w_qkv = attn_qkv[0]
    w_out = attn_out[0]
    gain_pair = gains[0]
    micro, seq = patch_io.shape[1], patch_io.shape[3]
    half_bytes = byte_states.shape[2]
    units = ff_weights.shape[0]
    rows = micro * seq
    own_rows = patch_io.reshape(rows, D)
    up_a = along(byte_states[0, 0], -1)
    up_b = along(byte_states[1, 0], -1)
    lower = byte_states.reshape(micro * half_bytes, D)
    w_ff = jnp.swapaxes(ff_weights, 0, 1)
    lengths = patch_lengths[:, 0]
    live = patch_live[:, 0]
    ends = jnp.cumsum(lengths, axis=1)
    bounds = jnp.tile(jnp.stack([ends - lengths, ends], 1), (1, 1, 4))
    places = lax.iota(jnp.int32, seq)
    causal = places[:, None] <= places[None, :]
    diagonal = places[:, None] == places[None, :]
    allowed = causal[None] & ((live[:, :, None] == 1) | diagonal[None])
    allowed = jnp.tile(allowed.astype(F32), (1, 1, 4))

    wide = ((rows, D), BF)
    short = ((seq, D), BF)
    tall = ((micro * half_bytes, D), BF)
    piece = ((half_bytes, D), BF)
    pn, q, bn_lo, k_lo, v_lo = on_section(
        first, encode_lower, (own_rows, lower, w_qkv, gain_pair), [wide, wide, tall, tall, tall]
    )
    rest = []
    for m, up in enumerate((up_a, up_b)):
        rest.append(
            on_section(
                first,
                functools.partial(encode_rest, m),
                (own_rows, up, w_qkv, w_out, gain_pair, bounds, q, k_lo, v_lo),
                [short, short, ((8, 256, GROUP), BF), piece, piece, piece],
            )
        )
    (hb_a, o_a, w_a, bn_a, k_a, v_a), (hb_b, o_b, w_b, bn_b, k_b, v_b) = rest
    arrived = [along(hb_a, 1), along(hb_b, 1)]

    left_enc, left_bytes = on_section(
        first, turn_encoder, (pn, o_a, o_b, bn_lo, bn_a, bn_b), [((2 * D, rows), BF), ((D, 2 * HALF), BF)]
    )
    left_enc_far = swap(left_enc, "core", (0,))
    bytes_far = swap(left_bytes, "core", (0,))

    grads_short = ((256, HALF), BF)
    step = 256
    (
        latents, dhb, latent_gain, xn, o2, acts, norms,
        lat_vo, lat_vo_other, lat_qk, lat_qk_other,
    ) = on_section(
        second,
        latent_layer,
        (ids, *arrived, own_rows, allowed, w_qkv, w_out, gain_pair, w_ff, left_enc_far, bytes_far),
        [
            ((rows, D), F32), wide, ((2, D), F32), wide, wide,
            ((3, units, rows), BF), ((2, 256, HALF), BF), *[grads_short] * 4,
        ],
        spaces={0: SMEM, 8: pl.ANY, 9: pl.ANY, 10: pl.ANY},
        scratch=[
            pltpu.VMEM((rows, 3 * D), BF),
            pltpu.VMEM((8, HD, GROUP), BF),
            pltpu.VMEM((2, 3, step, D), BF),
            pltpu.VMEM((rows, D), F32),
            pltpu.VMEM((rows, D), F32),
            pltpu.VMEM((rows, 3 * D), BF),
            pltpu.SemaphoreType.DMA((2,)),
        ],
    )
    returned = along(dhb, -1)

    share = units // 32
    acts = acts.reshape(3, 16, 2, share, rows)
    acts_a = pick(acts, zh, 2)
    acts_b = swap(pick(acts, 1 - zh, 2), "zh", (1,))
    norms_zh = swap(norms, "zh", (1,))
    acts_c, acts_d = swap(acts_a, "core", (1,)), swap(acts_b, "core", (1,))
    norms_far = swap(jnp.stack([pick(norms, 1 - core, 0), pick(norms_zh, 1 - core, 0)]), "core", (1,))
    ff_block = ((4, 3, share, HALF), BF)
    ff_blocks = on_section(
        second,
        ff_weights_grad,
        (
            ids, acts_a, acts_b, acts_c, acts_d,
            pick(norms, core, 0), pick(norms_zh, core, 0), norms_far[0], norms_far[1],
        ),
        [ff_block] * 4,
        spaces={0: SMEM},
    )
    ff_line = ((3, share, HALF), BF)
    ff_got = exchange(ff_blocks, 0, (1,))
    ff_blocks = on_section(second, ff_sum_first, (ids, ff_blocks[0], *ff_got), [ff_line] * 4, spaces={0: SMEM})
    ff_got = exchange(ff_blocks, 1, (1,))
    (ff_sum,) = on_section(second, ff_sum_second, (ff_blocks[0], *ff_got), [ff_line])
    ff_sum = ff_sum.reshape(3, 2, share // 2, HALF)
    ff_own = pick(ff_sum, core, 1)
    ff_far = swap(pick(ff_sum, 1 - core, 1), "core", (1,))
    ff_pair = jnp.stack([jnp.where(core == 0, ff_own, ff_far), jnp.where(core == 0, ff_far, ff_own)], 2)
    ff_grad = jnp.swapaxes(ff_pair.reshape(3, share // 2, D), 0, 1).astype(F32)
    ff_grad = jnp.where(second, ff_grad, 0.0)

    (left_lat,) = on_section(second, turn_latent, (xn, o2), [((2 * D, rows), BF)])
    left_lat_far = swap(left_lat, "core", (1,))
    grads_long = ((1152, HALF), BF)
    d_mixed, enc_vo, enc_vo_other = on_section(
        first, encoder_values_back, (ids, returned, w_out, w_a, w_b), [wide, grads_long, grads_long],
        spaces={0: SMEM},
    )
    enc_vo_far = swap(enc_vo_other, "core", (0,))
    lat_vo_far = swap(lat_vo_other, "core", (1,))
    enc_qk, enc_qk_other = on_section(
        first,
        encoder_scores_back,
        (ids, d_mixed, q, k_lo, v_lo, k_a, k_b, v_a, v_b, w_a, w_b),
        [grads_long, grads_long],
        spaces={0: SMEM},
    )
    enc_qk_far = swap(enc_qk_other, "core", (0,))
    lat_qk_far = swap(lat_qk_other, "core", (1,))

    def attn_blocks(values, enc, enc_far, lat, lat_far):
        outs = [((2, 256, HALF), BF)] * 4
        return lax.cond(
            first,
            lambda: call(
                functools.partial(encoder_weights, values),
                (ids, left_enc, left_enc_far, left_bytes, bytes_far, enc, enc_far),
                outs,
                spaces={0: SMEM},
            ),
            lambda: call(
                functools.partial(latent_weights, values),
                (ids, left_lat, left_lat_far, lat, lat_far),
                outs,
                spaces={0: SMEM},
            ),
        )

    vo = attn_blocks(True, enc_vo, enc_vo_far, lat_vo, lat_vo_far)
    vo_got = exchange(vo, 0)
    qk = attn_blocks(False, enc_qk, enc_qk_far, lat_qk, lat_qk_far)
    qk_got = exchange(qk, 0)

    grads = (enc_vo, enc_vo_other, enc_qk, enc_qk_other)
    up_grad, up_gain = on_section(
        first,
        encoder_upper_back,
        (ids, up_a, up_b, w_qkv, gain_pair, *grads, qk[0]),
        [tall, ((1, D), F32)],
        spaces={0: SMEM, 9: pl.ANY},
    )
    up_arrived = along(up_grad, 1)
    patch_grad, low_grad, encoder_gain = on_section(
        first,
        encoder_lower_back,
        (ids, returned, own_rows, lower, w_qkv, gain_pair, *grads, up_gain),
        [((rows, D), F32), tall, ((2, D), F32)],
        spaces={0: SMEM, 10: pl.ANY},
    )
    byte_grad = jnp.where(first, low_grad, up_arrived)
    patch_out = jnp.where(first, patch_grad, latents)

    vo = call(attn_sum_first, (ids, vo[0], *vo_got), [((128, HALF), BF)] * 4, spaces={0: SMEM})
    qk = call(
        attn_sum_first_gain,
        (ids, qk[0], *qk_got, encoder_gain, up_gain, latent_gain),
        [((144, HALF), BF)] * 4,
        spaces={0: SMEM},
    )

    def rest_of_sum(blocks):
        count = blocks[0].shape[0]
        (block,) = call(sum_all, (blocks[0], *exchange(blocks, 1)), [((count, HALF), BF)])
        (block,) = call(sum_all, (block, swap(block, "zh")), [((count, HALF), BF)])
        (block,) = call(stack_rows, collect(block, 1), [((count + 384, HALF), BF)])
        pieces = collect(block, 0)
        return pieces + [swap(p, "core") for p in pieces]

    vo = rest_of_sum(vo)
    qk = rest_of_sum(qk)
    whole = lambda p: pl.BlockSpec(p.shape, lambda i, n=p.ndim: (0,) * n)
    params = pltpu.CompilerParams(vmem_limit_bytes=VMEM_BYTES)
    total_qkv, total_out = pl.pallas_call(
        final_values,
        grid=(4,),
        out_shape=[jax.ShapeDtypeStruct((D, 3 * D), F32), jax.ShapeDtypeStruct((D, D), F32)],
        in_specs=[pl.BlockSpec(memory_space=SMEM)] + [whole(p) for p in vo],
        out_specs=[pl.BlockSpec((256, D), lambda i: (i, 2)), pl.BlockSpec((256, D), lambda i: (i, 0))],
        compiler_params=params,
    )(ids, *vo)
    total_qkv, total_gain = pl.pallas_call(
        final_queries,
        grid=(4,),
        out_shape=[jax.ShapeDtypeStruct((D, 3 * D), F32), jax.ShapeDtypeStruct((2, D), F32)],
        in_specs=[pl.BlockSpec(memory_space=SMEM)]
        + [whole(p) for p in qk]
        + [pl.BlockSpec(memory_space=pl.ANY)],
        out_specs=[pl.BlockSpec((256, 2 * D), lambda i: (i, 0)), pl.BlockSpec((2, D), lambda i: (0, 0))],
        input_output_aliases={9: 0},
        compiler_params=params,
    )(ids, *qk, total_qkv)
    return (
        patch_out.reshape(1, micro, 1, seq, D),
        byte_grad.reshape(micro, 1, half_bytes, D),
        total_qkv[None],
        total_out[None],
        total_gain[None],
        ff_grad[None],
    )


def solution(mesh):
    fine = Mesh(mesh.devices.reshape(2, 4, 4, 2, 2), ("s",) + BATCH)
    in_specs = (
        P("s", None, BATCH, None, None),
        P(None, BATCH, "s", None),
        P(None, BATCH, None),
        P(None, BATCH, None),
        P("s", None, None),
        P("s", None, None),
        P("s", None, None),
        P(),
    )
    out_specs = (
        P("s", None, BATCH, None, None),
        P(None, BATCH, "s", None),
        P("s", None, None),
        P("s", None, None),
        P("s", None, None),
        P("s", BATCH, None, None),
    )
    return jax.shard_map(shards, mesh=fine, in_specs=in_specs, out_specs=out_specs, check_vma=False)
```

```python
import functools

import jax
import jax.numpy as jnp
from jax import lax
from jax.experimental import pallas as pl
from jax.experimental.pallas import tpu as pltpu
from jax.sharding import Mesh
from jax.sharding import PartitionSpec as P

HD = 64
SCALE = HD**-0.5
EPS = 1e-05
NEG = -1e30
BATCH = ("y", "x", "zh", "core")
BF = jnp.bfloat16
F32 = jnp.float32
D = 1024
HALF = 512
GROUP = 256
VMEM_BYTES = 60 * 1024 * 1024


UNITS = 2816
PACK_NORMS = 3 * UNITS
PACK_LEFT = PACK_NORMS + 4 * 256
PACK_GRADS = PACK_LEFT + 2 * D
PACK_ROWS = PACK_GRADS + 4 * 512


def nn(a, b):
    return lax.dot_general(a, b, (((1,), (0,)), ((), ())), preferred_element_type=F32)


def nt(a, b):
    return lax.dot_general(a, b, (((1,), (1,)), ((), ())), preferred_element_type=F32)


def tn(a, b):
    return lax.dot_general(a, b, (((0,), (0,)), ((), ())), preferred_element_type=F32)


def inverse_rms(x):
    return lax.rsqrt(jnp.mean(x * x, axis=-1, keepdims=True) + EPS)


def norm_back(x, gain, up):
    r = inverse_rms(x)
    scaled = up * gain
    inner = jnp.mean(scaled * x, axis=-1, keepdims=True)
    return r * (scaled - x * (r * r * inner)), up * (x * r)


def stack_heads(rows):
    head = lax.broadcasted_iota(jnp.int32, rows.shape, 1) // HD
    return jnp.concatenate([jnp.where(head == h, rows, jnp.zeros_like(rows)) for h in range(4)], 0)


def unstack_heads(stacked):
    head = lax.broadcasted_iota(jnp.int32, (HD, GROUP), 1) // HD
    out = stacked[0:HD]
    for h in range(1, 4):
        out = jnp.where(head == h, stacked[h * HD : (h + 1) * HD], out)
    return out


def softmax_columns(scores):
    top = functools.reduce(jnp.maximum, [jnp.max(s, axis=0, keepdims=True) for s in scores])
    parts = [jnp.exp(s - top) for s in scores]
    inverse = 1.0 / sum(jnp.sum(p, axis=0, keepdims=True) for p in parts)
    return [(p * inverse).astype(BF) for p in parts]


def encode_lower(patch, low, w_qkv, gains, pn, q, bn, k, v):
    x = patch[...].astype(F32)
    normed = (x * inverse_rms(x) * gains[0:1]).astype(BF)
    pn[...] = normed
    q[...] = nn(normed, w_qkv[:, 0:D]).astype(BF)
    for i in range(2):
        at = pl.ds(i * 256, 256)
        b = low[at, :].astype(F32)
        normed = (b * inverse_rms(b) * gains[1:2]).astype(BF)
        bn[at, :] = normed
        k[at, :] = nn(normed, w_qkv[:, D : 2 * D]).astype(BF)
        v[at, :] = nn(normed, w_qkv[:, 2 * D :]).astype(BF)


def encode_rest(m, patch, up, w_qkv, w_out, gains, bounds, q, k_lo, v_lo, hb, o1, weights, bn, k, v):
    b = up[...].astype(F32)
    normed = (b * inverse_rms(b) * gains[1:2]).astype(BF)
    bn[...] = normed
    k[...] = nn(normed, w_qkv[:, D : 2 * D]).astype(BF)
    v[...] = nn(normed, w_qkv[:, 2 * D :]).astype(BF)
    spot = lax.broadcasted_iota(jnp.int32, (256, GROUP), 0)
    start = bounds[m, 0:1, :]
    end = bounds[m, 1:2, :]
    inside = [(spot + h * 256 >= start) & (spot + h * 256 < end) for h in range(2)]
    low_at = slice(m * 256, (m + 1) * 256)
    rows = slice(m * HD, (m + 1) * HD)
    for g in range(4):
        lanes = slice(g * GROUP, (g + 1) * GROUP)
        stacked = stack_heads(q[rows, lanes] * BF(SCALE))
        scores = [
            jnp.where(inside[h], nt(keys, stacked), NEG)
            for h, keys in enumerate((k_lo[low_at, lanes], k[:, lanes]))
        ]
        w = softmax_columns(scores)
        weights[g * 2] = w[0]
        weights[g * 2 + 1] = w[1]
        mixed = tn(w[0], v_lo[low_at, lanes]) + tn(w[1], v[:, lanes])
        o1[:, lanes] = unstack_heads(mixed).astype(BF)
    hb[...] = (patch[rows, :].astype(F32) + nn(o1[...], w_out[...])).astype(BF)


def latent_layer(
    ids, hb_a, hb_b, cot, allowed, w_qkv, w_out, gains, w_ff,
    latents, dhb, gain_grad, packed, norms, grads,
    qkv, weights, o2, ff_buf, acc_out, acc_norm, dqkv, sems,
):
    core = ids[0]
    units = w_ff.shape[1]
    step = ff_buf.shape[2]
    steps = units // step

    def fetch(i, slot):
        return pltpu.make_async_copy(
            w_ff.at[:, pl.ds(pl.multiple_of(i * step, 128), step), :], ff_buf.at[slot], sems.at[slot]
        )

    fetch(0, 0).start()
    x = jnp.concatenate([hb_a[...], hb_b[...]], 0).astype(F32)
    normed = (x * inverse_rms(x) * gains[0:1]).astype(BF)
    packed[PACK_LEFT : PACK_LEFT + D, :] = normed.T
    qkv[...] = nn(normed, w_qkv[...]).astype(BF)
    for m in range(2):
        rows = slice(m * HD, (m + 1) * HD)
        for g in range(4):
            lanes = slice(g * GROUP, (g + 1) * GROUP)
            k_lanes = slice(D + g * GROUP, D + (g + 1) * GROUP)
            v_lanes = slice(2 * D + g * GROUP, 2 * D + (g + 1) * GROUP)
            stacked = stack_heads(qkv[rows, lanes] * BF(SCALE))
            scores = jnp.where(allowed[m] > 0.5, nt(qkv[rows, k_lanes], stacked), NEG)
            (w,) = softmax_columns([scores])
            weights[m * 4 + g] = w
            o2[rows, lanes] = unstack_heads(tn(w, qkv[rows, v_lanes])).astype(BF)
    packed[PACK_LEFT + D : PACK_LEFT + 2 * D, :] = o2[...].T
    after = x + nn(o2[...], w_out[...])
    yn = (after * inverse_rms(after) * gains[1:2]).astype(BF)
    c = cot[...]
    for h in range(2):

        @pl.when(core == h)
        def _(h=h):
            norms[0:128, :] = yn[:, h * HALF : (h + 1) * HALF]
            norms[128:256, :] = c[:, h * HALF : (h + 1) * HALF]

        @pl.when(core != h)
        def _(h=h):
            for b in range(4):
                lanes = slice(h * HALF + b * 128, h * HALF + (b + 1) * 128)
                packed[PACK_NORMS + b * 256 : PACK_NORMS + b * 256 + 128, :] = yn[:, lanes]
                packed[PACK_NORMS + b * 256 + 128 : PACK_NORMS + (b + 1) * 256, :] = c[:, lanes]

    acc_out[...] = after
    acc_norm[...] = jnp.zeros_like(acc_norm)

    def ff_step(i, carry):
        slot = lax.rem(i, 2)

        @pl.when(i + 1 < steps)
        def _():
            fetch(i + 1, 1 - slot).start()

        fetch(i, slot).wait()
        w_gate, w_up, w_down = ff_buf.at[slot, 0], ff_buf.at[slot, 1], ff_buf.at[slot, 2]
        gate = nt(yn, w_gate[...])
        upward = nt(yn, w_up[...])
        du = nt(c, w_down[...])
        sig = 1.0 / (1.0 + jnp.exp(-gate))
        active = gate * sig
        hidden = (active * upward).astype(BF)
        d_gate = (du * upward * (sig * (1.0 + gate * (1.0 - sig)))).astype(BF)
        d_up = (du * active).astype(BF)
        at = pl.ds(pl.multiple_of(i * step, 128), step)
        for j, value in enumerate((d_gate, d_up, hidden)):
            packed[pl.ds(pl.multiple_of(i * step + j * units, 128), step), :] = value.T
        acc_out[...] += nn(hidden, w_down[...])
        acc_norm[...] += nn(d_gate, w_gate[...]) + nn(d_up, w_up[...])
        return carry

    lax.fori_loop(0, steps, ff_step, 0)
    latents[...] = acc_out[...]
    back, gain_rows = norm_back(after, gains[1:2], acc_norm[...])
    gain_grad[1:2, :] = jnp.sum(gain_rows, axis=0, keepdims=True)
    d_after = c.astype(F32) + back
    da = d_after.astype(BF)
    d_mixed = nt(da, w_out[...]).astype(BF)
    for m in range(2):
        rows = slice(m * HD, (m + 1) * HD)
        for g in range(4):
            lanes = slice(g * GROUP, (g + 1) * GROUP)
            k_lanes = slice(D + g * GROUP, D + (g + 1) * GROUP)
            v_lanes = slice(2 * D + g * GROUP, 2 * D + (g + 1) * GROUP)
            q_stacked = stack_heads(qkv[rows, lanes] * BF(SCALE))
            o_stacked = stack_heads(d_mixed[rows, lanes])
            w_low = weights[m * 4 + g]
            w = w_low.astype(F32)
            dw = nt(qkv[rows, v_lanes], o_stacked)
            inner = jnp.sum(dw * w, axis=0, keepdims=True)
            ds = (w * (dw - inner)).astype(BF)
            dqkv[rows, lanes] = (unstack_heads(tn(ds, qkv[rows, k_lanes])) * SCALE).astype(BF)
            dqkv[rows, k_lanes] = nn(ds, q_stacked).astype(BF)
            dqkv[rows, v_lanes] = nn(w_low, o_stacked).astype(BF)
    d_normed = nt(dqkv[...], w_qkv[...])
    back, gain_rows = norm_back(x, gains[0:1], d_normed)
    gain_grad[0:1, :] = jnp.sum(gain_rows, axis=0, keepdims=True)
    dhb[...] = (d_after + back).astype(BF)
    for h in range(2):
        pieces = (
            dqkv[:, h * HALF : (h + 1) * HALF],
            da[:, h * HALF : (h + 1) * HALF],
            dqkv[:, D + h * HALF : D + (h + 1) * HALF],
            dqkv[:, 2 * D + h * HALF : 2 * D + (h + 1) * HALF],
        )

        @pl.when(core == h)
        def _(pieces=pieces):
            for i, value in enumerate(pieces):
                grads[i * 128 : (i + 1) * 128, :] = value

        @pl.when(core != h)
        def _(pieces=pieces):
            for i, value in enumerate(pieces):
                for b in range(4):
                    first = PACK_GRADS + b * 512 + i * 128
                    packed[first : first + 128, :] = value[:, b * 128 : (b + 1) * 128]


def half_of(core, g, mine, other):
    lanes = slice((g % 2) * GROUP, (g % 2 + 1) * GROUP)

    def put(at, value):
        @pl.when(core == g // 2)
        def _():
            mine[at, lanes] = value

        @pl.when(core != g // 2)
        def _():
            other[at, lanes] = value

    return put


def encoder_attention_back(
    ids, dhb, w_out, q, k_lo, v_lo, k_a, k_b, v_a, v_b, w_a, w_b, early, early_bytes, early_ff, mine, other
):
    d_mixed = nt(dhb[...], w_out[...]).astype(BF)
    for g in range(4):
        lanes = slice(g * GROUP, (g + 1) * GROUP)
        put = half_of(ids[0], g, mine, other)
        put(slice(128, 256), dhb[:, lanes])
        for m, (k_up, v_up, weights) in enumerate(((k_a, v_a, w_a), (k_b, v_b, w_b))):
            rows = slice(m * HD, (m + 1) * HD)
            low_at = slice(m * 256, (m + 1) * 256)
            q_stacked = stack_heads(q[rows, lanes] * BF(SCALE))
            o_stacked = stack_heads(d_mixed[rows, lanes])
            low = [weights[g * 2 + h] for h in range(2)]
            w = [piece.astype(F32) for piece in low]
            dw = [nt(values, o_stacked) for values in (v_lo[low_at, lanes], v_up[:, lanes])]
            inner = sum(jnp.sum(a * b, axis=0, keepdims=True) for a, b in zip(dw, w))
            ds = [(b * (a - inner)).astype(BF) for a, b in zip(dw, w)]
            dq = tn(ds[0], k_lo[low_at, lanes]) + tn(ds[1], k_up[:, lanes])
            put(rows, (unstack_heads(dq) * SCALE).astype(BF))
            for h in range(2):
                base = h * HALF + m * 256
                put(slice(256 + base, 512 + base), nn(ds[h], q_stacked).astype(BF))
                put(slice(1280 + base, 1536 + base), nn(low[h], o_stacked).astype(BF))


def both_columns(core, block, w_qkv):
    return [
        w_qkv[:, pl.ds(pl.multiple_of(block * D + which * HALF, HALF), HALF)] for which in (core, 1 - core)
    ]


def bytes_back(core, h, m, source, w_qkv, gains, grads):
    d_norm = sum(
        nt(ref[1024 * block - 768 + h * HALF + m * 256 : 1024 * block - 512 + h * HALF + m * 256, :], columns)
        for block in (1, 2)
        for ref, columns in zip(grads, both_columns(core, block, w_qkv))
    )
    back, gain_rows = norm_back(source.astype(F32), gains[1:2], d_norm)
    return back.astype(BF), jnp.sum(gain_rows, axis=0, keepdims=True)


def encoder_upper_back(ids, up_a, up_b, w_qkv, gains, mine, other, after, up_grad, gain_grad):
    total = jnp.zeros((1, D), F32)
    for m, source in enumerate((up_a, up_b)):
        back, rows = bytes_back(ids[0], 1, m, source[...], w_qkv, gains, (mine, other))
        up_grad[m * 256 : (m + 1) * 256, :] = back
        total = total + rows
    gain_grad[...] = total


def encoder_lower_back(
    ids, dhb, patch, low, w_qkv, gains, mine, other, after, patch_grad, low_grad, gain_grad
):
    core = ids[0]
    up_norm = sum(nt(ref[0:128, :], columns) for ref, columns in zip((mine, other), both_columns(core, 0, w_qkv)))
    back, gain_rows = norm_back(patch[...].astype(F32), gains[0:1], up_norm)
    gain_grad[0:1, :] = jnp.sum(gain_rows, axis=0, keepdims=True)
    patch_grad[...] = dhb[...].astype(F32) + back
    total = jnp.zeros((1, D), F32)
    for m in range(2):
        at = slice(m * 256, (m + 1) * 256)
        back, rows = bytes_back(core, 0, m, low[at, :], w_qkv, gains, (mine, other))
        low_grad[at, :] = back
        total = total + rows
    gain_grad[1:2, :] = total


def turn_encoder(pn, o_a, o_b, bn_lo, bn_a, bn_b, early, left, left_bytes):
    left[0:D, :] = pn[...].T
    left[D : 2 * D, :] = jnp.concatenate([o_a[...], o_b[...]], 0).T
    left_bytes[:, 0:HALF] = bn_lo[...].T
    left_bytes[:, HALF : HALF + 256] = bn_a[...].T
    left_bytes[:, HALF + 256 : 2 * HALF] = bn_b[...].T


def rows_of_both(left, left_far, at):
    return jnp.concatenate([left[at, :], left_far[at, :]], 1)


def below(near, far, rows):
    return jnp.concatenate([near[rows, :], far[rows, :]], 0)


def encoder_weights(ids, left, left_far, bytes_near, bytes_far, near, far, *blocks):
    u = ids[1]
    queries = below(near, far, slice(0, 128))
    outputs = below(near, far, slice(128, 256))
    for k in range(4):
        first = lax.rem(u + k, 4) * 256
        at = pl.ds(pl.multiple_of(first, 256), 256)
        low_at = pl.ds(pl.multiple_of(first + D, 256), 256)
        blocks[k][0] = nn(rows_of_both(left, left_far, at), queries).astype(BF)
        blocks[k][3] = nn(rows_of_both(left, left_far, low_at), outputs).astype(BF)
        for block in (1, 2):
            rows = slice(1024 * block - 768, 1024 * block + 256)
            blocks[k][block] = (nn(bytes_near[at, :], near[rows, :]) + nn(bytes_far[at, :], far[rows, :])).astype(BF)


def unpack(packed, first, rows):
    return jnp.concatenate([packed[first + b * rows : first + (b + 1) * rows, :] for b in range(4)], 1)


def latent_weights(ids, packed, packed_far, near, *blocks):
    u = ids[1]
    far = unpack(packed_far, PACK_GRADS, 512)
    rights = [jnp.concatenate([near[i * 128 : (i + 1) * 128, :], far[i * 128 : (i + 1) * 128, :]], 0) for i in range(4)]
    for k in range(4):
        first = PACK_LEFT + lax.rem(u + k, 4) * 256
        at = pl.ds(pl.multiple_of(first, 256), 256)
        low_at = pl.ds(pl.multiple_of(first + D, 256), 256)
        for block, (source, i) in enumerate(((at, 0), (at, 2), (at, 3), (low_at, 1))):
            blocks[k][block] = nn(rows_of_both(packed, packed_far, source), rights[i]).astype(BF)


def ff_weights_grad(ids, packed, packed_far, norms, early, early_bytes, own, right, left, far_a, far_b):
    core, u = ids[0], ids[1]
    share = UNITS // 16
    far = unpack(packed_far, PACK_NORMS, 256)
    normed = jnp.concatenate([norms[0:128, :], far[0:128, :]], 0)
    cot = jnp.concatenate([norms[128:256, :], far[128:256, :]], 0)
    for k in range(4):
        there = lax.rem(u + k, 4)
        for v in range(4):
            chunk = jnp.where(core == 0, there * 4 + v, v * 4 + there)
            for j in range(3):
                at = pl.ds(pl.multiple_of(j * UNITS + chunk * share, 16), share)
                value = nn(rows_of_both(packed, packed_far, at), normed if j < 2 else cot).astype(BF)
                rows = slice(j * share, (j + 1) * share)
                if k == 2:
                    far_a[v, rows, :] = value[:, :GROUP]
                    far_b[v, rows, :] = value[:, GROUP:]
                else:
                    (own, right, None, left)[k][v, rows, :] = value


def ff_add(right, left, from_left, from_right, new_right, new_left):
    new_right[:, :, 0:GROUP] = (right[:, :, 0:GROUP].astype(F32) + from_left[...].astype(F32)).astype(BF)
    new_right[:, :, GROUP:] = right[:, :, GROUP:]
    new_left[:, :, 0:GROUP] = left[:, :, 0:GROUP]
    new_left[:, :, GROUP:] = (left[:, :, GROUP:].astype(F32) + from_right[...].astype(F32)).astype(BF)


def sum_four(own, a, b, c):
    return own.astype(F32) + a.astype(F32) + b.astype(F32) + c.astype(F32)


def pack_gain(value):
    high = value.astype(BF)
    low = (value - high.astype(F32)).astype(BF)
    return jnp.concatenate(
        [high.astype(F32), low.astype(F32), jnp.zeros((8, HALF), F32)], 0
    ).astype(BF)


def unpack_gain(rows):
    rows = rows.astype(F32)
    return rows[0:4] + rows[4:8]


GAIN_AT = slice(256, 272)


def attn_sum_first(ids, own, a, b, c, *outs):
    v = ids[2]
    for k in range(4):
        at = pl.ds(pl.multiple_of(lax.rem(v + k, 4) * HD, HD), HD)
        for block in range(4):
            outs[k][block * HD : (block + 1) * HD, :] = sum_four(
                own[block, at, :], a[block, at, :], b[block, at, :], c[block, at, :]
            ).astype(BF)


def attn_sum_first_gain(ids, own, a, b, c, enc_gain, up_gain, lat_gain, *outs):
    attn_sum_first(ids, own, a, b, c, *outs)
    first = ids[4] == 0
    gain = jnp.where(
        first, jnp.concatenate([enc_gain[0:1, :], enc_gain[1:2, :] + up_gain[...]], 0), lat_gain[...]
    )
    halves = [gain[i : i + 1, h * HALF : (h + 1) * HALF] for i in range(2) for h in range(2)]
    packed = pack_gain(jnp.concatenate(halves, 0))
    for out in outs:
        out[GAIN_AT, :] = packed


def sum_all(*refs):
    refs, out = refs[:-1], refs[-1]
    out[0:256, :] = sum(ref[0:256, :].astype(F32) for ref in refs).astype(BF)
    out[GAIN_AT, :] = pack_gain(sum(unpack_gain(ref[GAIN_AT, :]) for ref in refs))


def stack_rows(*refs):
    refs, out = refs[:-1], refs[-1]
    for j, ref in enumerate(refs):
        out[j * 256 : (j + 1) * 256, :] = ref[0:256, :]
    out[1024:1040, :] = refs[0][GAIN_AT, :]


def ff_sum_first(ids, own, a, b, *outs):
    v = ids[2]
    for k in range(4):
        at = lax.rem(v + k, 4)
        outs[k][...] = (own[at].astype(F32) + a[at].astype(F32) + b[at].astype(F32)).astype(BF)


def ff_sum_second(own, a, b, c, out):
    out[...] = sum_four(own[...], a[...], b[...], c[...]).astype(BF)


def final_attn(ids, *refs):
    pieces, (qkv, out, gain) = refs[:8], refs[8:]
    step = pl.program_id(0)
    for side in range(2):
        core = ids[0] if side == 0 else 1 - ids[0]
        u = ids[1] if side == 0 else ids[2]
        v = ids[2] if side == 0 else ids[1]
        for k in range(4):
            piece = pieces[side * 4 + k]

            @pl.when(lax.rem(u + k, 4) == step)
            def _(piece=piece, v=v, core=core):
                for j in range(4):
                    at = pl.ds(pl.multiple_of(lax.rem(v + j, 4) * HD, HD), HD)
                    for block in range(4):
                        target, column = (qkv, block * D) if block < 3 else (out, 0)
                        lanes = pl.ds(pl.multiple_of(core * HALF + column, HALF), HALF)
                        first = j * 256 + block * HD
                        target[at, lanes] = piece[first : first + HD, :].astype(F32)

    mine = sum(unpack_gain(piece[1024:1040, :]) for piece in pieces[:4])
    other = sum(unpack_gain(piece[1024:1040, :]) for piece in pieces[4:])
    total = mine + other
    for i in range(2):
        for h in range(2):
            gain[i : i + 1, h * HALF : (h + 1) * HALF] = total[2 * i + h : 2 * i + h + 1, :]


SMEM = pltpu.MemorySpace.SMEM
VMEM = pltpu.MemorySpace.VMEM


def call(kernel, args, outs, scratch=(), spaces=None, flops=0, moved=0):
    spaces = spaces or {}
    specs = [pl.BlockSpec(memory_space=spaces.get(i, VMEM)) for i in range(len(args))]
    return pl.pallas_call(
        kernel,
        out_shape=[jax.ShapeDtypeStruct(s, t) for s, t in outs],
        in_specs=specs,
        out_specs=[pl.BlockSpec(memory_space=VMEM) for _ in outs],
        scratch_shapes=list(scratch),
        compiler_params=pltpu.CompilerParams(vmem_limit_bytes=VMEM_BYTES),
        cost_estimate=pl.CostEstimate(flops=flops, bytes_accessed=moved, transcendentals=0),
    )(*args)


def nothing(outs):
    def kernel(*refs):
        pass

    return pl.pallas_call(
        kernel,
        out_shape=[jax.ShapeDtypeStruct(s, t) for s, t in outs],
        out_specs=[pl.BlockSpec(memory_space=pl.ANY) for _ in outs],
    )()


def on_section(flag, kernel, args, outs, **rest):
    return lax.cond(
        flag, lambda: call(kernel, args, outs, **rest), lambda: nothing(outs)
    )


def along(value, by):
    return lax.ppermute(value, "s", [(0, 1)] if by > 0 else [(1, 0)])


def swap(value, axis, sections=(0, 1)):
    pairs = [(s * 2 + i, s * 2 + 1 - i) for s in sections for i in range(2)]
    return lax.ppermute(value, ("s", axis), pairs)


def plane_shift(value, which, by, sections=(0, 1)):
    pairs = []
    for s in sections:
        for y in range(4):
            for x in range(4):
                for core in range(2):
                    ty, tx = ((y + by) % 4, x) if core == which else (y, (x + by) % 4)
                    pairs.append((((s * 4 + y) * 4 + x) * 2 + core, ((s * 4 + ty) * 4 + tx) * 2 + core))
    return lax.ppermute(value, ("s", "y", "x", "core"), pairs)


def exchange(blocks, which, sections=(0, 1)):
    return [plane_shift(blocks[k], which, k, sections) for k in (1, 2, 3)]


def collect(block, which):
    return [block] + [plane_shift(block, which, -k) for k in (1, 2, 3)]


def pick(stack, index, dim):
    return lax.dynamic_index_in_dim(stack, index, dim, keepdims=False)


def shards(patch_io, byte_states, patch_lengths, patch_live, attn_qkv, attn_out, gains, ff_weights):
    section = lax.axis_index("s")
    core = lax.axis_index("core")
    zh = lax.axis_index("zh")
    y, x = lax.axis_index("y"), lax.axis_index("x")
    first = section == 0
    second = section == 1
    ids = jnp.stack([core, jnp.where(core == 0, y, x), jnp.where(core == 0, x, y), zh, section])
    ids = ids.astype(jnp.int32)
    w_qkv = attn_qkv[0]
    w_out = attn_out[0]
    gain_pair = gains[0]
    micro, seq = patch_io.shape[1], patch_io.shape[3]
    half_bytes = byte_states.shape[2]
    units = ff_weights.shape[0]
    rows = micro * seq
    own_rows = patch_io.reshape(rows, D)
    up_a = along(byte_states[0, 0], -1)
    up_b = along(byte_states[1, 0], -1)
    lower = byte_states.reshape(micro * half_bytes, D)
    w_ff = jnp.swapaxes(ff_weights, 0, 1)
    lengths = patch_lengths[:, 0]
    live = patch_live[:, 0]
    ends = jnp.cumsum(lengths, axis=1)
    bounds = jnp.tile(jnp.stack([ends - lengths, ends], 1), (1, 1, 4))
    places = lax.iota(jnp.int32, seq)
    causal = places[:, None] <= places[None, :]
    diagonal = places[:, None] == places[None, :]
    allowed = causal[None] & ((live[:, :, None] == 1) | diagonal[None])
    allowed = jnp.tile(allowed.astype(F32), (1, 1, 4))

    wide = ((rows, D), BF)
    short = ((seq, D), BF)
    tall = ((micro * half_bytes, D), BF)
    piece = ((half_bytes, D), BF)
    pn, q, bn_lo, k_lo, v_lo = on_section(
        first, encode_lower, (own_rows, lower, w_qkv, gain_pair), [wide, wide, tall, tall, tall]
    )
    rest = []
    for m, up in enumerate((up_a, up_b)):
        rest.append(
            on_section(
                first,
                functools.partial(encode_rest, m),
                (own_rows, up, w_qkv, w_out, gain_pair, bounds, q, k_lo, v_lo),
                [short, short, ((8, 256, GROUP), BF), piece, piece, piece],
            )
        )
    (hb_a, o_a, w_a, bn_a, k_a, v_a), (hb_b, o_b, w_b, bn_b, k_b, v_b) = rest
    arrived = [along(hb_a, 1), along(hb_b, 1)]

    left_enc, left_bytes = on_section(
        first,
        turn_encoder,
        (pn, o_a, o_b, bn_lo, bn_a, bn_b, arrived[1]),
        [((2 * D, rows), BF), ((D, 2 * HALF), BF)],
        spaces={6: pl.ANY},
    )
    left_far = swap(left_enc, "core", (0,))
    bytes_far = swap(left_bytes, "core", (0,))

    step = 256
    latents, dhb, latent_gain, packed, norms, lat_grads = on_section(
        second,
        latent_layer,
        (ids, *arrived, own_rows, allowed, w_qkv, w_out, gain_pair, w_ff),
        [
            ((rows, D), F32), wide, ((2, D), F32),
            ((PACK_ROWS, rows), BF), ((256, HALF), BF), ((512, HALF), BF),
        ],
        spaces={0: SMEM, 8: pl.ANY},
        scratch=[
            pltpu.VMEM((rows, 3 * D), BF),
            pltpu.VMEM((8, HD, GROUP), BF),
            pltpu.VMEM((rows, D), BF),
            pltpu.VMEM((2, 3, step, D), BF),
            pltpu.VMEM((rows, D), F32),
            pltpu.VMEM((rows, D), F32),
            pltpu.VMEM((rows, 3 * D), BF),
            pltpu.SemaphoreType.DMA((2,)),
        ],
    )
    returned = along(dhb, -1)

    packed_far = swap(packed, "core", (1,))
    share = units // 16
    ff_block = ((4, 3 * share, HALF), BF)
    ff_half = ((4, 3 * share, GROUP), BF)
    ff_own, ff_right, ff_left, ff_far_a, ff_far_b = on_section(
        second,
        ff_weights_grad,
        (ids, packed, packed_far, norms, left_far, bytes_far),
        [ff_block, ff_block, ff_block, ff_half, ff_half],
        spaces={0: SMEM, 4: pl.ANY, 5: pl.ANY},
    )
    from_left = plane_shift(ff_far_a, 0, 1, (1,))
    from_right = plane_shift(ff_far_b, 0, -1, (1,))
    ff_right, ff_left = on_section(
        second, ff_add, (ff_right, ff_left, from_left, from_right), [ff_block, ff_block]
    )
    from_left = plane_shift(ff_right, 0, 1, (1,))
    from_right = plane_shift(ff_left, 0, -1, (1,))
    ff_line = ((3 * share, HALF), BF)
    ff_blocks = on_section(
        second, ff_sum_first, (ids, ff_own, from_left, from_right), [ff_line] * 4, spaces={0: SMEM}
    )
    ff_got = exchange(ff_blocks, 1, (1,))
    (ff_sum,) = on_section(second, ff_sum_second, (ff_blocks[0], *ff_got), [ff_line])
    ff_sum = ff_sum.reshape(3, 2, share // 2, HALF)
    ff_far = swap(pick(ff_sum, 1 - zh, 1), "zh", (1,))
    ff_sum = (pick(ff_sum, zh, 1).astype(F32) + ff_far.astype(F32)).astype(BF).reshape(3, 2, share // 4, HALF)
    ff_mine = pick(ff_sum, core, 1)
    ff_far = swap(pick(ff_sum, 1 - core, 1), "core", (1,))
    ff_pair = jnp.stack([jnp.where(core == 0, ff_mine, ff_far), jnp.where(core == 0, ff_far, ff_mine)], 2)
    ff_grad = jnp.swapaxes(ff_pair.reshape(3, share // 4, D), 0, 1).astype(F32)
    ff_grad = jnp.where(second, ff_grad, 0.0)

    grads_long = ((2304, HALF), BF)
    enc_grads, enc_other = on_section(
        first,
        encoder_attention_back,
        (
            ids, returned, w_out, q, k_lo, v_lo, k_a, k_b, v_a, v_b, w_a, w_b,
            left_far, bytes_far, ff_far_a,
        ),
        [grads_long, grads_long],
        spaces={0: SMEM, 12: pl.ANY, 13: pl.ANY, 14: pl.ANY},
    )
    enc_far = swap(enc_other, "core", (0,))
    outs = [((4, 256, HALF), BF)] * 4
    blocks = lax.cond(
        first,
        lambda: call(
            encoder_weights,
            (ids, left_enc, left_far, left_bytes, bytes_far, enc_grads, enc_far),
            outs,
            spaces={0: SMEM},
        ),
        lambda: call(latent_weights, (ids, packed, packed_far, lat_grads), outs, spaces={0: SMEM}),
    )
    got = exchange(blocks, 0)
    up_grad, up_gain = on_section(
        first,
        encoder_upper_back,
        (ids, up_a, up_b, w_qkv, gain_pair, enc_grads, enc_other, blocks[0]),
        [tall, ((1, D), F32)],
        spaces={0: SMEM, 7: pl.ANY},
    )
    up_arrived = along(up_grad, 1)
    patch_grad, low_grad, encoder_gain = on_section(
        first,
        encoder_lower_back,
        (ids, returned, own_rows, lower, w_qkv, gain_pair, enc_grads, enc_other, up_gain),
        [((rows, D), F32), tall, ((2, D), F32)],
        spaces={0: SMEM, 8: pl.ANY},
    )
    byte_grad = jnp.where(first, low_grad, up_arrived)
    patch_out = jnp.where(first, patch_grad, latents)

    line = [((272, HALF), BF)]
    blocks = call(
        attn_sum_first_gain,
        (ids, blocks[0], *got, encoder_gain, up_gain, latent_gain),
        line * 4,
        spaces={0: SMEM},
    )
    (block,) = call(sum_all, (blocks[0], *exchange(blocks, 1)), line)
    (block,) = call(sum_all, (block, swap(block, "zh")), line)
    (block,) = call(stack_rows, collect(block, 1), [((1040, HALF), BF)])
    pieces = collect(block, 0)
    pieces = pieces + [swap(p, "core") for p in pieces]
    whole = lambda p: pl.BlockSpec(p.shape, lambda i, n=p.ndim: (0,) * n)
    total_qkv, total_out, total_gain = pl.pallas_call(
        final_attn,
        grid=(4,),
        out_shape=[
            jax.ShapeDtypeStruct((D, 3 * D), F32),
            jax.ShapeDtypeStruct((D, D), F32),
            jax.ShapeDtypeStruct((2, D), F32),
        ],
        in_specs=[pl.BlockSpec(memory_space=SMEM)] + [whole(p) for p in pieces],
        out_specs=[
            pl.BlockSpec((256, 3 * D), lambda i: (i, 0)),
            pl.BlockSpec((256, D), lambda i: (i, 0)),
            pl.BlockSpec((2, D), lambda i: (0, 0)),
        ],
        compiler_params=pltpu.CompilerParams(vmem_limit_bytes=VMEM_BYTES),
    )(ids, *pieces)
    return (
        patch_out.reshape(1, micro, 1, seq, D),
        byte_grad.reshape(micro, 1, half_bytes, D),
        total_qkv[None],
        total_out[None],
        total_gain[None],
        ff_grad[None],
    )


def solution(mesh):
    fine = Mesh(mesh.devices.reshape(2, 4, 4, 2, 2), ("s",) + BATCH)
    in_specs = (
        P("s", None, BATCH, None, None),
        P(None, BATCH, "s", None),
        P(None, BATCH, None),
        P(None, BATCH, None),
        P("s", None, None),
        P("s", None, None),
        P("s", None, None),
        P(),
    )
    out_specs = (
        P("s", None, BATCH, None, None),
        P(None, BATCH, "s", None),
        P("s", None, None),
        P("s", None, None),
        P("s", None, None),
        P("s", BATCH, None, None),
    )
    return jax.shard_map(shards, mesh=fine, in_specs=in_specs, out_specs=out_specs, check_vma=False)
```

```python
import functools
import math

import jax
import jax.numpy as jnp
from jax import lax
from jax.experimental import pallas as pl
from jax.experimental.pallas import tpu as pltpu
from jax.sharding import Mesh
from jax.sharding import PartitionSpec as P

HD = 64
SCALE = HD**-0.5
EPS = 1e-05
NEG = -1e30
BATCH = ("y", "x", "zh", "core")
BF = jnp.bfloat16
F32 = jnp.float32
D = 1024
HALF = 512
GROUP = 256
FINAL_VMEM = 32 * 1024 * 1024


UNITS = 2816
PACK_NORMS = 3 * UNITS
PACK_LEFT = PACK_NORMS + 4 * 256
PACK_GRADS = PACK_LEFT + 2 * D
PACK_ROWS = PACK_GRADS + 4 * 512


def nn(a, b):
    return lax.dot_general(a, b, (((1,), (0,)), ((), ())), preferred_element_type=F32)


def nt(a, b):
    return lax.dot_general(a, b, (((1,), (1,)), ((), ())), preferred_element_type=F32)


def tn(a, b):
    return lax.dot_general(a, b, (((0,), (0,)), ((), ())), preferred_element_type=F32)


def inverse_rms(x):
    return lax.rsqrt(jnp.mean(x * x, axis=-1, keepdims=True) + EPS)


def norm_back(x, gain, up):
    r = inverse_rms(x)
    scaled = up * gain
    inner = jnp.mean(scaled * x, axis=-1, keepdims=True)
    return r * (scaled - x * (r * r * inner)), up * (x * r)


def stack_heads(rows):
    head = lax.broadcasted_iota(jnp.int32, rows.shape, 1) // HD
    return jnp.concatenate([jnp.where(head == h, rows, jnp.zeros_like(rows)) for h in range(4)], 0)


def unstack_heads(stacked):
    head = lax.broadcasted_iota(jnp.int32, (HD, GROUP), 1) // HD
    out = stacked[0:HD]
    for h in range(1, 4):
        out = jnp.where(head == h, stacked[h * HD : (h + 1) * HD], out)
    return out


def softmax_columns(scores):
    top = functools.reduce(jnp.maximum, [jnp.max(s, axis=0, keepdims=True) for s in scores])
    parts = [jnp.exp(s - top) for s in scores]
    inverse = 1.0 / sum(jnp.sum(p, axis=0, keepdims=True) for p in parts)
    return [(p * inverse).astype(BF) for p in parts]


def encode_lower(patch, low, w_qkv, gains, pn, q, bn, k, v):
    x = patch[...].astype(F32)
    normed = (x * inverse_rms(x) * gains[0:1]).astype(BF)
    pn[...] = normed
    q[...] = nn(normed, w_qkv[:, 0:D]).astype(BF)
    for i in range(2):
        at = pl.ds(i * 256, 256)
        b = low[at, :].astype(F32)
        normed = (b * inverse_rms(b) * gains[1:2]).astype(BF)
        bn[at, :] = normed
        k[at, :] = nn(normed, w_qkv[:, D : 2 * D]).astype(BF)
        v[at, :] = nn(normed, w_qkv[:, 2 * D :]).astype(BF)


def encode_rest(m, patch, up, w_qkv, w_out, gains, bounds, q, k_lo, v_lo, hb, o1, weights, bn, k, v):
    b = up[...].astype(F32)
    normed = (b * inverse_rms(b) * gains[1:2]).astype(BF)
    bn[...] = normed
    k[...] = nn(normed, w_qkv[:, D : 2 * D]).astype(BF)
    v[...] = nn(normed, w_qkv[:, 2 * D :]).astype(BF)
    spot = lax.broadcasted_iota(jnp.int32, (256, GROUP), 0)
    start = bounds[m, 0:1, :]
    end = bounds[m, 1:2, :]
    inside = [(spot + h * 256 >= start) & (spot + h * 256 < end) for h in range(2)]
    low_at = slice(m * 256, (m + 1) * 256)
    rows = slice(m * HD, (m + 1) * HD)
    for g in range(4):
        lanes = slice(g * GROUP, (g + 1) * GROUP)
        stacked = stack_heads(q[rows, lanes] * BF(SCALE))
        scores = [
            jnp.where(inside[h], nt(keys, stacked), NEG)
            for h, keys in enumerate((k_lo[low_at, lanes], k[:, lanes]))
        ]
        w = softmax_columns(scores)
        weights[g * 2] = w[0]
        weights[g * 2 + 1] = w[1]
        mixed = tn(w[0], v_lo[low_at, lanes]) + tn(w[1], v[:, lanes])
        o1[:, lanes] = unstack_heads(mixed).astype(BF)
    hb[...] = (patch[rows, :].astype(F32) + nn(o1[...], w_out[...])).astype(BF)


def latent_layer(
    ids, hb_a, hb_b, cot, allowed, w_qkv, w_out, gains, w_ff,
    latents, dhb, gain_grad, packed, norms, grads,
    qkv, weights, o2, ff_buf, acc_out, acc_norm, dqkv, sems,
):
    core = ids[0]
    units = w_ff.shape[1]
    step = ff_buf.shape[2]
    steps = units // step

    def fetch(i, slot):
        return pltpu.make_async_copy(
            w_ff.at[:, pl.ds(pl.multiple_of(i * step, 128), step), :], ff_buf.at[slot], sems.at[slot]
        )

    fetch(0, 0).start()
    x = jnp.concatenate([hb_a[...], hb_b[...]], 0).astype(F32)
    normed = (x * inverse_rms(x) * gains[0:1]).astype(BF)
    packed[PACK_LEFT : PACK_LEFT + D, :] = normed.T
    qkv[...] = nn(normed, w_qkv[...]).astype(BF)
    for m in range(2):
        rows = slice(m * HD, (m + 1) * HD)
        for g in range(4):
            lanes = slice(g * GROUP, (g + 1) * GROUP)
            k_lanes = slice(D + g * GROUP, D + (g + 1) * GROUP)
            v_lanes = slice(2 * D + g * GROUP, 2 * D + (g + 1) * GROUP)
            stacked = stack_heads(qkv[rows, lanes] * BF(SCALE))
            scores = jnp.where(allowed[m] > 0.5, nt(qkv[rows, k_lanes], stacked), NEG)
            (w,) = softmax_columns([scores])
            weights[m * 4 + g] = w
            o2[rows, lanes] = unstack_heads(tn(w, qkv[rows, v_lanes])).astype(BF)
    packed[PACK_LEFT + D : PACK_LEFT + 2 * D, :] = o2[...].T
    after = x + nn(o2[...], w_out[...])
    yn = (after * inverse_rms(after) * gains[1:2]).astype(BF)
    c = cot[...]
    for h in range(2):

        @pl.when(core == h)
        def _(h=h):
            norms[0:128, :] = yn[:, h * HALF : (h + 1) * HALF]
            norms[128:256, :] = c[:, h * HALF : (h + 1) * HALF]

        @pl.when(core != h)
        def _(h=h):
            for b in range(4):
                lanes = slice(h * HALF + b * 128, h * HALF + (b + 1) * 128)
                packed[PACK_NORMS + b * 256 : PACK_NORMS + b * 256 + 128, :] = yn[:, lanes]
                packed[PACK_NORMS + b * 256 + 128 : PACK_NORMS + (b + 1) * 256, :] = c[:, lanes]

    acc_out[...] = after
    acc_norm[...] = jnp.zeros_like(acc_norm)

    def ff_step(i, carry):
        slot = lax.rem(i, 2)

        @pl.when(i + 1 < steps)
        def _():
            fetch(i + 1, 1 - slot).start()

        fetch(i, slot).wait()
        w_gate, w_up, w_down = ff_buf.at[slot, 0], ff_buf.at[slot, 1], ff_buf.at[slot, 2]
        gate = nt(yn, w_gate[...])
        upward = nt(yn, w_up[...])
        du = nt(c, w_down[...])
        sig = 1.0 / (1.0 + jnp.exp(-gate))
        active = gate * sig
        hidden = (active * upward).astype(BF)
        d_gate = (du * upward * (sig * (1.0 + gate * (1.0 - sig)))).astype(BF)
        d_up = (du * active).astype(BF)
        at = pl.ds(pl.multiple_of(i * step, 128), step)
        for j, value in enumerate((d_gate, d_up, hidden)):
            packed[pl.ds(pl.multiple_of(i * step + j * units, 128), step), :] = value.T
        acc_out[...] += nn(hidden, w_down[...])
        acc_norm[...] += nn(d_gate, w_gate[...]) + nn(d_up, w_up[...])
        return carry

    lax.fori_loop(0, steps, ff_step, 0)
    latents[...] = acc_out[...]
    back, gain_rows = norm_back(after, gains[1:2], acc_norm[...])
    gain_grad[1:2, :] = jnp.sum(gain_rows, axis=0, keepdims=True)
    d_after = c.astype(F32) + back
    da = d_after.astype(BF)
    d_mixed = nt(da, w_out[...]).astype(BF)
    for m in range(2):
        rows = slice(m * HD, (m + 1) * HD)
        for g in range(4):
            lanes = slice(g * GROUP, (g + 1) * GROUP)
            k_lanes = slice(D + g * GROUP, D + (g + 1) * GROUP)
            v_lanes = slice(2 * D + g * GROUP, 2 * D + (g + 1) * GROUP)
            q_stacked = stack_heads(qkv[rows, lanes] * BF(SCALE))
            o_stacked = stack_heads(d_mixed[rows, lanes])
            w_low = weights[m * 4 + g]
            w = w_low.astype(F32)
            dw = nt(qkv[rows, v_lanes], o_stacked)
            inner = jnp.sum(dw * w, axis=0, keepdims=True)
            ds = (w * (dw - inner)).astype(BF)
            dqkv[rows, lanes] = (unstack_heads(tn(ds, qkv[rows, k_lanes])) * SCALE).astype(BF)
            dqkv[rows, k_lanes] = nn(ds, q_stacked).astype(BF)
            dqkv[rows, v_lanes] = nn(w_low, o_stacked).astype(BF)
    d_normed = nt(dqkv[...], w_qkv[...])
    back, gain_rows = norm_back(x, gains[0:1], d_normed)
    gain_grad[0:1, :] = jnp.sum(gain_rows, axis=0, keepdims=True)
    dhb[...] = (d_after + back).astype(BF)
    for h in range(2):
        pieces = (
            dqkv[:, h * HALF : (h + 1) * HALF],
            da[:, h * HALF : (h + 1) * HALF],
            dqkv[:, D + h * HALF : D + (h + 1) * HALF],
            dqkv[:, 2 * D + h * HALF : 2 * D + (h + 1) * HALF],
        )

        @pl.when(core == h)
        def _(pieces=pieces):
            for i, value in enumerate(pieces):
                grads[i * 128 : (i + 1) * 128, :] = value

        @pl.when(core != h)
        def _(pieces=pieces):
            for i, value in enumerate(pieces):
                for b in range(4):
                    first = PACK_GRADS + b * 512 + i * 128
                    packed[first : first + 128, :] = value[:, b * 128 : (b + 1) * 128]


def half_of(core, g, mine, other):
    lanes = slice((g % 2) * GROUP, (g % 2 + 1) * GROUP)

    def put(at, value):
        @pl.when(core == g // 2)
        def _():
            mine[at, lanes] = value

        @pl.when(core != g // 2)
        def _():
            other[at, lanes] = value

    return put


def encoder_attention_back(
    ids, dhb, w_out, q, k_lo, v_lo, k_a, k_b, v_a, v_b, w_a, w_b, early, early_bytes, mine, other
):
    d_mixed = nt(dhb[...], w_out[...]).astype(BF)
    for g in range(4):
        lanes = slice(g * GROUP, (g + 1) * GROUP)
        put = half_of(ids[0], g, mine, other)
        put(slice(128, 256), dhb[:, lanes])
        for m, (k_up, v_up, weights) in enumerate(((k_a, v_a, w_a), (k_b, v_b, w_b))):
            rows = slice(m * HD, (m + 1) * HD)
            low_at = slice(m * 256, (m + 1) * 256)
            q_stacked = stack_heads(q[rows, lanes] * BF(SCALE))
            o_stacked = stack_heads(d_mixed[rows, lanes])
            low = [weights[g * 2 + h] for h in range(2)]
            w = [piece.astype(F32) for piece in low]
            dw = [nt(values, o_stacked) for values in (v_lo[low_at, lanes], v_up[:, lanes])]
            inner = sum(jnp.sum(a * b, axis=0, keepdims=True) for a, b in zip(dw, w))
            ds = [(b * (a - inner)).astype(BF) for a, b in zip(dw, w)]
            dq = tn(ds[0], k_lo[low_at, lanes]) + tn(ds[1], k_up[:, lanes])
            put(rows, (unstack_heads(dq) * SCALE).astype(BF))
            for h in range(2):
                base = h * HALF + m * 256
                put(slice(256 + base, 512 + base), nn(ds[h], q_stacked).astype(BF))
                put(slice(1280 + base, 1536 + base), nn(low[h], o_stacked).astype(BF))


def both_columns(core, block, w_qkv):
    return [
        w_qkv[:, pl.ds(pl.multiple_of(block * D + which * HALF, HALF), HALF)] for which in (core, 1 - core)
    ]


def bytes_back(core, h, m, source, w_qkv, gains, grads):
    d_norm = sum(
        nt(ref[1024 * block - 768 + h * HALF + m * 256 : 1024 * block - 512 + h * HALF + m * 256, :], columns)
        for block in (1, 2)
        for ref, columns in zip(grads, both_columns(core, block, w_qkv))
    )
    back, gain_rows = norm_back(source.astype(F32), gains[1:2], d_norm)
    return back.astype(BF), jnp.sum(gain_rows, axis=0, keepdims=True)


def encoder_upper_back(ids, up_a, up_b, w_qkv, gains, mine, other, after, up_grad, gain_grad):
    total = jnp.zeros((1, D), F32)
    for m, source in enumerate((up_a, up_b)):
        back, rows = bytes_back(ids[0], 1, m, source[...], w_qkv, gains, (mine, other))
        up_grad[m * 256 : (m + 1) * 256, :] = back
        total = total + rows
    gain_grad[...] = total


def encoder_lower_back(
    ids, dhb, patch, low, w_qkv, gains, mine, other, after, patch_grad, low_grad, gain_grad
):
    core = ids[0]
    up_norm = sum(nt(ref[0:128, :], columns) for ref, columns in zip((mine, other), both_columns(core, 0, w_qkv)))
    back, gain_rows = norm_back(patch[...].astype(F32), gains[0:1], up_norm)
    gain_grad[0:1, :] = jnp.sum(gain_rows, axis=0, keepdims=True)
    patch_grad[...] = dhb[...].astype(F32) + back
    total = jnp.zeros((1, D), F32)
    for m in range(2):
        at = slice(m * 256, (m + 1) * 256)
        back, rows = bytes_back(core, 0, m, low[at, :], w_qkv, gains, (mine, other))
        low_grad[at, :] = back
        total = total + rows
    gain_grad[1:2, :] = total


def turn_encoder(pn, o_a, o_b, bn_lo, bn_a, bn_b, early, left, left_bytes):
    left[0:D, :] = pn[...].T
    left[D : 2 * D, :] = jnp.concatenate([o_a[...], o_b[...]], 0).T
    left_bytes[:, 0:HALF] = bn_lo[...].T
    left_bytes[:, HALF : HALF + 256] = bn_a[...].T
    left_bytes[:, HALF + 256 : 2 * HALF] = bn_b[...].T


def rows_of_both(left, left_far, at):
    return jnp.concatenate([left[at, :], left_far[at, :]], 1)


def below(near, far, rows):
    return jnp.concatenate([near[rows, :], far[rows, :]], 0)


def encoder_weights(ids, left, left_far, bytes_near, bytes_far, near, far, *blocks):
    u = ids[1]
    queries = below(near, far, slice(0, 128))
    outputs = below(near, far, slice(128, 256))
    for k in range(4):
        first = lax.rem(u + k, 4) * 256
        at = pl.ds(pl.multiple_of(first, 256), 256)
        low_at = pl.ds(pl.multiple_of(first + D, 256), 256)
        blocks[k][0] = nn(rows_of_both(left, left_far, at), queries).astype(BF)
        blocks[k][3] = nn(rows_of_both(left, left_far, low_at), outputs).astype(BF)
        for block in (1, 2):
            rows = slice(1024 * block - 768, 1024 * block + 256)
            blocks[k][block] = (nn(bytes_near[at, :], near[rows, :]) + nn(bytes_far[at, :], far[rows, :])).astype(BF)


def unpack(packed, first, rows):
    return jnp.concatenate([packed[first + b * rows : first + (b + 1) * rows, :] for b in range(4)], 1)


def latent_weights(ids, packed, packed_far, near, *blocks):
    u = ids[1]
    far = unpack(packed_far, PACK_GRADS, 512)
    rights = [jnp.concatenate([near[i * 128 : (i + 1) * 128, :], far[i * 128 : (i + 1) * 128, :]], 0) for i in range(4)]
    for k in range(4):
        first = PACK_LEFT + lax.rem(u + k, 4) * 256
        at = pl.ds(pl.multiple_of(first, 256), 256)
        low_at = pl.ds(pl.multiple_of(first + D, 256), 256)
        for block, (source, i) in enumerate(((at, 0), (at, 2), (at, 3), (low_at, 1))):
            blocks[k][block] = nn(rows_of_both(packed, packed_far, source), rights[i]).astype(BF)


def ff_weights_grad(ids, packed, packed_far, norms, early, own, right, left, far_a, far_b):
    core, u = ids[0], ids[1]
    share = UNITS // 16
    far = unpack(packed_far, PACK_NORMS, 256)
    normed = jnp.concatenate([norms[0:128, :], far[0:128, :]], 0)
    cot = jnp.concatenate([norms[128:256, :], far[128:256, :]], 0)
    for k in range(4):
        there = lax.rem(u + k, 4)
        for v in range(4):
            chunk = jnp.where(core == 0, there * 4 + v, v * 4 + there)
            for j in range(3):
                at = pl.ds(pl.multiple_of(j * UNITS + chunk * share, 16), share)
                value = nn(rows_of_both(packed, packed_far, at), normed if j < 2 else cot).astype(BF)
                rows = slice(j * share, (j + 1) * share)
                if k == 2:
                    far_a[v, rows, :] = value[:, :GROUP]
                    far_b[v, rows, :] = value[:, GROUP:]
                else:
                    (own, right, None, left)[k][v, rows, :] = value


def ff_add(right, left, from_left, from_right, new_right, new_left):
    new_right[:, :, 0:GROUP] = (right[:, :, 0:GROUP].astype(F32) + from_left[...].astype(F32)).astype(BF)
    new_right[:, :, GROUP:] = right[:, :, GROUP:]
    new_left[:, :, 0:GROUP] = left[:, :, 0:GROUP]
    new_left[:, :, GROUP:] = (left[:, :, GROUP:].astype(F32) + from_right[...].astype(F32)).astype(BF)


def sum_four(own, a, b, c):
    return own.astype(F32) + a.astype(F32) + b.astype(F32) + c.astype(F32)


def pack_gain(value):
    high = value.astype(BF)
    low = (value - high.astype(F32)).astype(BF)
    return jnp.concatenate(
        [high.astype(F32), low.astype(F32), jnp.zeros((8, HALF), F32)], 0
    ).astype(BF)


def unpack_gain(rows):
    rows = rows.astype(F32)
    return rows[0:4] + rows[4:8]


GAIN_AT = slice(256, 272)


def attn_sum_first(ids, own, a, b, c, *outs):
    v = ids[2]
    for k in range(4):
        at = pl.ds(pl.multiple_of(lax.rem(v + k, 4) * HD, HD), HD)
        for block in range(4):
            outs[k][block * HD : (block + 1) * HD, :] = sum_four(
                own[block, at, :], a[block, at, :], b[block, at, :], c[block, at, :]
            ).astype(BF)


def attn_sum_first_gain(ids, own, a, b, c, enc_gain, up_gain, lat_gain, *outs):
    attn_sum_first(ids, own, a, b, c, *outs)
    first = ids[4] == 0
    gain = jnp.where(
        first, jnp.concatenate([enc_gain[0:1, :], enc_gain[1:2, :] + up_gain[...]], 0), lat_gain[...]
    )
    halves = [gain[i : i + 1, h * HALF : (h + 1) * HALF] for i in range(2) for h in range(2)]
    packed = pack_gain(jnp.concatenate(halves, 0))
    for out in outs:
        out[GAIN_AT, :] = packed


def sum_all(*refs):
    refs, out = refs[:-1], refs[-1]
    out[0:256, :] = sum(ref[0:256, :].astype(F32) for ref in refs).astype(BF)
    out[GAIN_AT, :] = pack_gain(sum(unpack_gain(ref[GAIN_AT, :]) for ref in refs))


def stack_rows(*refs):
    refs, out = refs[:-1], refs[-1]
    for j, ref in enumerate(refs):
        out[j * 256 : (j + 1) * 256, :] = ref[0:256, :]
    out[1024:1040, :] = refs[0][GAIN_AT, :]


def ff_sum_first(ids, own, a, b, *outs):
    v = ids[2]
    for k in range(4):
        at = lax.rem(v + k, 4)
        outs[k][...] = (own[at].astype(F32) + a[at].astype(F32) + b[at].astype(F32)).astype(BF)


def ff_sum_second(own, a, b, c, out):
    out[...] = sum_four(own[...], a[...], b[...], c[...]).astype(BF)


def final_attn(ids, *refs):
    pieces, (qkv, out, gain) = refs[:8], refs[8:]
    step = pl.program_id(0)
    for side in range(2):
        core = ids[0] if side == 0 else 1 - ids[0]
        u = ids[1] if side == 0 else ids[2]
        v = ids[2] if side == 0 else ids[1]
        for k in range(4):
            piece = pieces[side * 4 + k]

            @pl.when(lax.rem(u + k, 4) == step)
            def _(piece=piece, v=v, core=core):
                for j in range(4):
                    at = pl.ds(pl.multiple_of(lax.rem(v + j, 4) * HD, HD), HD)
                    for block in range(4):
                        target, column = (qkv, block * D) if block < 3 else (out, 0)
                        lanes = pl.ds(pl.multiple_of(core * HALF + column, HALF), HALF)
                        first = j * 256 + block * HD
                        target[at, lanes] = piece[first : first + HD, :].astype(F32)

    mine = sum(unpack_gain(piece[1024:1040, :]) for piece in pieces[:4])
    other = sum(unpack_gain(piece[1024:1040, :]) for piece in pieces[4:])
    total = mine + other
    for i in range(2):
        for h in range(2):
            gain[i : i + 1, h * HALF : (h + 1) * HALF] = total[2 * i + h : 2 * i + h + 1, :]


SMEM = pltpu.MemorySpace.SMEM
VMEM = pltpu.MemorySpace.VMEM


def size(shape, dtype):
    return math.prod(shape) * jnp.dtype(dtype).itemsize


def call(kernel, args, outs, scratch=(), spaces=None, spare=6):
    spaces = spaces or {}
    vmem = sum(size(a.shape, a.dtype) for i, a in enumerate(args) if i not in spaces)
    vmem += sum(size(*o) for o in outs)
    vmem += sum(size(s.shape, s.dtype) for s in scratch if hasattr(s, "shape") and s.memory_space == VMEM)
    specs = [pl.BlockSpec(memory_space=spaces.get(i, VMEM)) for i in range(len(args))]
    return pl.pallas_call(
        kernel,
        out_shape=[jax.ShapeDtypeStruct(s, t) for s, t in outs],
        in_specs=specs,
        out_specs=[pl.BlockSpec(memory_space=VMEM) for _ in outs],
        scratch_shapes=list(scratch),
        compiler_params=pltpu.CompilerParams(vmem_limit_bytes=vmem + spare * 1024 * 1024),
    )(*args)


def nothing(outs):
    def kernel(*refs):
        pass

    return pl.pallas_call(
        kernel,
        out_shape=[jax.ShapeDtypeStruct(s, t) for s, t in outs],
        out_specs=[pl.BlockSpec(memory_space=pl.ANY) for _ in outs],
    )()


def on_section(flag, kernel, args, outs, **rest):
    return lax.cond(
        flag, lambda: call(kernel, args, outs, **rest), lambda: nothing(outs)
    )


def along(value, by):
    return lax.ppermute(value, "s", [(0, 1)] if by > 0 else [(1, 0)])


def swap(value, axis, sections=(0, 1)):
    pairs = [(s * 2 + i, s * 2 + 1 - i) for s in sections for i in range(2)]
    return lax.ppermute(value, ("s", axis), pairs)


def plane_shift(value, which, by, sections=(0, 1)):
    pairs = []
    for s in sections:
        for y in range(4):
            for x in range(4):
                for core in range(2):
                    ty, tx = ((y + by) % 4, x) if core == which else (y, (x + by) % 4)
                    pairs.append((((s * 4 + y) * 4 + x) * 2 + core, ((s * 4 + ty) * 4 + tx) * 2 + core))
    return lax.ppermute(value, ("s", "y", "x", "core"), pairs)


def exchange(blocks, which, sections=(0, 1)):
    return [plane_shift(blocks[k], which, k, sections) for k in (1, 2, 3)]


def collect(block, which):
    return [block] + [plane_shift(block, which, -k) for k in (1, 2, 3)]


def pick(stack, index, dim):
    return lax.dynamic_index_in_dim(stack, index, dim, keepdims=False)


def shards(patch_io, byte_states, patch_lengths, patch_live, attn_qkv, attn_out, gains, ff_weights):
    section = lax.axis_index("s")
    core = lax.axis_index("core")
    zh = lax.axis_index("zh")
    y, x = lax.axis_index("y"), lax.axis_index("x")
    first = section == 0
    second = section == 1
    ids = jnp.stack([core, jnp.where(core == 0, y, x), jnp.where(core == 0, x, y), zh, section])
    ids = ids.astype(jnp.int32)
    w_qkv = attn_qkv[0]
    w_out = attn_out[0]
    gain_pair = gains[0]
    micro, seq = patch_io.shape[1], patch_io.shape[3]
    half_bytes = byte_states.shape[2]
    units = ff_weights.shape[0]
    rows = micro * seq
    own_rows = patch_io.reshape(rows, D)
    up_a = along(byte_states[0, 0], -1)
    up_b = along(byte_states[1, 0], -1)
    lower = byte_states.reshape(micro * half_bytes, D)
    w_ff = jnp.swapaxes(ff_weights, 0, 1)
    lengths = patch_lengths[:, 0]
    live = patch_live[:, 0]
    ends = jnp.cumsum(lengths, axis=1)
    bounds = jnp.tile(jnp.stack([ends - lengths, ends], 1), (1, 1, 4))
    places = lax.iota(jnp.int32, seq)
    causal = places[:, None] <= places[None, :]
    diagonal = places[:, None] == places[None, :]
    allowed = causal[None] & ((live[:, :, None] == 1) | diagonal[None])
    allowed = lax.optimization_barrier(jnp.tile(allowed.astype(F32), (1, 1, 4)))

    wide = ((rows, D), BF)
    short = ((seq, D), BF)
    tall = ((micro * half_bytes, D), BF)
    piece = ((half_bytes, D), BF)
    pn, q, bn_lo, k_lo, v_lo = on_section(
        first, encode_lower, (own_rows, lower, w_qkv, gain_pair), [wide, wide, tall, tall, tall]
    )
    rest = []
    for m, up in enumerate((up_a, up_b)):
        rest.append(
            on_section(
                first,
                functools.partial(encode_rest, m),
                (own_rows, up, w_qkv, w_out, gain_pair, bounds, q, k_lo, v_lo),
                [short, short, ((8, 256, GROUP), BF), piece, piece, piece],
            )
        )
    (hb_a, o_a, w_a, bn_a, k_a, v_a), (hb_b, o_b, w_b, bn_b, k_b, v_b) = rest
    arrived = [along(hb_a, 1), along(hb_b, 1)]

    left_enc, left_bytes = on_section(
        first,
        turn_encoder,
        (pn, o_a, o_b, bn_lo, bn_a, bn_b, arrived[1]),
        [((2 * D, rows), BF), ((D, 2 * HALF), BF)],
        spaces={6: pl.ANY},
    )
    left_far = swap(left_enc, "core", (0,))
    bytes_far = swap(left_bytes, "core", (0,))

    step = 256
    latents, dhb, latent_gain, packed, norms, lat_grads = on_section(
        second,
        latent_layer,
        (ids, *arrived, own_rows, allowed, w_qkv, w_out, gain_pair, w_ff),
        [
            ((rows, D), F32), wide, ((2, D), F32),
            ((PACK_ROWS, rows), BF), ((256, HALF), BF), ((512, HALF), BF),
        ],
        spaces={0: SMEM, 8: pl.ANY},
        scratch=[
            pltpu.VMEM((rows, 3 * D), BF),
            pltpu.VMEM((8, HD, GROUP), BF),
            pltpu.VMEM((rows, D), BF),
            pltpu.VMEM((2, 3, step, D), BF),
            pltpu.VMEM((rows, D), F32),
            pltpu.VMEM((rows, D), F32),
            pltpu.VMEM((rows, 3 * D), BF),
            pltpu.SemaphoreType.DMA((2,)),
        ],
    )
    returned = along(dhb, -1)

    packed, returned = lax.optimization_barrier((packed, returned))
    packed_far = swap(packed, "core", (1,))
    grads_long = ((2304, HALF), BF)
    enc_grads, enc_other = on_section(
        first,
        encoder_attention_back,
        (
            ids, returned, w_out, q, k_lo, v_lo, k_a, k_b, v_a, v_b, w_a, w_b,
            left_far, bytes_far,
        ),
        [grads_long, grads_long],
        spaces={0: SMEM, 12: pl.ANY, 13: pl.ANY},
    )
    enc_far = swap(enc_other, "core", (0,))
    outs = [((4, 256, HALF), BF)] * 4
    blocks = lax.cond(
        first,
        lambda: call(
            encoder_weights,
            (ids, left_enc, left_far, left_bytes, bytes_far, enc_grads, enc_far),
            outs,
            spaces={0: SMEM},
        ),
        lambda: call(latent_weights, (ids, packed, packed_far, lat_grads), outs, spaces={0: SMEM}),
    )
    got = exchange(blocks, 0)
    share = units // 16
    ff_block = ((4, 3 * share, HALF), BF)
    ff_half = ((4, 3 * share, GROUP), BF)
    byte_outs = [tall, ((1, D), F32)], [((rows, D), F32), tall, ((2, D), F32)]
    ff_outs = [ff_block, ff_block, ff_block, ff_half, ff_half]

    def input_grads():
        upper_part = call(
            encoder_upper_back,
            (ids, up_a, up_b, w_qkv, gain_pair, enc_grads, enc_other, blocks[0]),
            byte_outs[0],
            spaces={0: SMEM, 7: pl.ANY},
        )
        lower_part = call(
            encoder_lower_back,
            (ids, returned, own_rows, lower, w_qkv, gain_pair, enc_grads, enc_other, upper_part[1]),
            byte_outs[1],
            spaces={0: SMEM, 8: pl.ANY},
        )
        return (*upper_part, *lower_part, *nothing(ff_outs))

    def ff_grads():
        parts = call(
            ff_weights_grad, (ids, packed, packed_far, norms, blocks[0]), ff_outs, spaces={0: SMEM, 4: pl.ANY}
        )
        return (*nothing(byte_outs[0] + byte_outs[1]), *parts)

    (
        up_grad, up_gain, patch_grad, low_grad, encoder_gain,
        ff_own, ff_right, ff_left, ff_far_a, ff_far_b,
    ) = lax.cond(first, input_grads, ff_grads)
    up_arrived = along(up_grad, 1)
    byte_grad = jnp.where(first, low_grad, up_arrived)
    patch_out = jnp.where(first, patch_grad, latents)

    line = [((272, HALF), BF)]
    blocks = call(
        attn_sum_first_gain,
        (ids, blocks[0], *got, encoder_gain, up_gain, latent_gain),
        line * 4,
        spaces={0: SMEM},
    )
    met = exchange(blocks, 1)
    ff_far_a, ff_far_b, _ = lax.optimization_barrier((ff_far_a, ff_far_b, blocks))
    from_left = plane_shift(ff_far_a, 0, 1, (1,))
    from_right = plane_shift(ff_far_b, 0, -1, (1,))
    from_left, from_right, met = lax.optimization_barrier((from_left, from_right, met))
    (block,) = call(sum_all, (blocks[0], *met), line)
    ff_right, ff_left = on_section(
        second, ff_add, (ff_right, ff_left, from_left, from_right), [ff_block, ff_block]
    )
    from_left = plane_shift(ff_right, 0, 1, (1,))
    from_right = plane_shift(ff_left, 0, -1, (1,))
    (block,) = call(sum_all, (block, swap(block, "zh")), line)
    (block,) = call(stack_rows, collect(block, 1), [((1040, HALF), BF)])
    from_left, from_right, block = lax.optimization_barrier((from_left, from_right, block))
    ff_line = ((3 * share, HALF), BF)
    ff_blocks = on_section(
        second, ff_sum_first, (ids, ff_own, from_left, from_right), [ff_line] * 4, spaces={0: SMEM}
    )
    ff_got = exchange(ff_blocks, 1, (1,))
    (ff_sum,) = on_section(second, ff_sum_second, (ff_blocks[0], *ff_got), [ff_line])
    ff_sum = ff_sum.reshape(3, 2, share // 2, HALF)
    ff_far = swap(pick(ff_sum, 1 - zh, 1), "zh", (1,))
    ff_sum = (pick(ff_sum, zh, 1).astype(F32) + ff_far.astype(F32)).astype(BF).reshape(3, 2, share // 4, HALF)
    ff_mine = pick(ff_sum, core, 1)
    ff_far = swap(pick(ff_sum, 1 - core, 1), "core", (1,))
    ff_pair = jnp.stack([jnp.where(core == 0, ff_mine, ff_far), jnp.where(core == 0, ff_far, ff_mine)], 2)
    ff_grad = jnp.swapaxes(ff_pair.reshape(3, share // 4, D), 0, 1).astype(F32)
    ff_grad = jnp.where(second, ff_grad, 0.0)

    pieces = collect(block, 0)
    pieces = pieces + [swap(p, "core") for p in pieces]
    whole = lambda p: pl.BlockSpec(p.shape, lambda i, n=p.ndim: (0,) * n)
    total_qkv, total_out, total_gain = pl.pallas_call(
        final_attn,
        grid=(4,),
        out_shape=[
            jax.ShapeDtypeStruct((D, 3 * D), F32),
            jax.ShapeDtypeStruct((D, D), F32),
            jax.ShapeDtypeStruct((2, D), F32),
        ],
        in_specs=[pl.BlockSpec(memory_space=SMEM)] + [whole(p) for p in pieces],
        out_specs=[
            pl.BlockSpec((256, 3 * D), lambda i: (i, 0)),
            pl.BlockSpec((256, D), lambda i: (i, 0)),
            pl.BlockSpec((2, D), lambda i: (0, 0)),
        ],
        compiler_params=pltpu.CompilerParams(vmem_limit_bytes=FINAL_VMEM),
    )(ids, *pieces)
    return (
        patch_out.reshape(1, micro, 1, seq, D),
        byte_grad.reshape(micro, 1, half_bytes, D),
        total_qkv[None],
        total_out[None],
        total_gain[None],
        ff_grad[None],
    )


def solution(mesh):
    fine = Mesh(mesh.devices.reshape(2, 4, 4, 2, 2), ("s",) + BATCH)
    in_specs = (
        P("s", None, BATCH, None, None),
        P(None, BATCH, "s", None),
        P(None, BATCH, None),
        P(None, BATCH, None),
        P("s", None, None),
        P("s", None, None),
        P("s", None, None),
        P(),
    )
    out_specs = (
        P("s", None, BATCH, None, None),
        P(None, BATCH, "s", None),
        P("s", None, None),
        P("s", None, None),
        P("s", None, None),
        P("s", BATCH, None, None),
    )
    return jax.shard_map(shards, mesh=fine, in_specs=in_specs, out_specs=out_specs, check_vma=False)
```

```python
import functools
import math

import jax
import jax.numpy as jnp
from jax import lax
from jax.experimental import pallas as pl
from jax.experimental.pallas import tpu as pltpu
from jax.sharding import Mesh
from jax.sharding import PartitionSpec as P

HD = 64
SCALE = HD**-0.5
EPS = 1e-05
NEG = -1e30
BATCH = ("y", "x", "zh", "core")
BF = jnp.bfloat16
F32 = jnp.float32
D = 1024
HALF = 512
GROUP = 256
FINAL_VMEM = 32 * 1024 * 1024


UNITS = 2816
PACK_NORMS = 3 * UNITS
PACK_LEFT = PACK_NORMS + 4 * 256
PACK_GRADS = PACK_LEFT + 2 * D
PACK_ROWS = PACK_GRADS + 4 * 512


def nn(a, b):
    return lax.dot_general(a, b, (((1,), (0,)), ((), ())), preferred_element_type=F32)


def nt(a, b):
    return lax.dot_general(a, b, (((1,), (1,)), ((), ())), preferred_element_type=F32)


def tn(a, b):
    return lax.dot_general(a, b, (((0,), (0,)), ((), ())), preferred_element_type=F32)


def inverse_rms(x):
    return lax.rsqrt(jnp.mean(x * x, axis=-1, keepdims=True) + EPS)


def norm_back(x, gain, up):
    r = inverse_rms(x)
    scaled = up * gain
    inner = jnp.mean(scaled * x, axis=-1, keepdims=True)
    return r * (scaled - x * (r * r * inner)), up * (x * r)


def stack_heads(rows):
    head = lax.broadcasted_iota(jnp.int32, rows.shape, 1) // HD
    return jnp.concatenate([jnp.where(head == h, rows, jnp.zeros_like(rows)) for h in range(4)], 0)


def unstack_heads(stacked):
    head = lax.broadcasted_iota(jnp.int32, (HD, GROUP), 1) // HD
    out = stacked[0:HD]
    for h in range(1, 4):
        out = jnp.where(head == h, stacked[h * HD : (h + 1) * HD], out)
    return out


def softmax_columns(scores):
    top = functools.reduce(jnp.maximum, [jnp.max(s, axis=0, keepdims=True) for s in scores])
    parts = [jnp.exp(s - top) for s in scores]
    inverse = 1.0 / sum(jnp.sum(p, axis=0, keepdims=True) for p in parts)
    return [(p * inverse).astype(BF) for p in parts]


def encode_lower(patch, low, w_qkv, gains, pn, q, bn, k, v):
    x = patch[...].astype(F32)
    normed = (x * inverse_rms(x) * gains[0:1]).astype(BF)
    pn[...] = normed
    q[...] = nn(normed, w_qkv[:, 0:D]).astype(BF)
    for i in range(2):
        at = pl.ds(i * 256, 256)
        b = low[at, :].astype(F32)
        normed = (b * inverse_rms(b) * gains[1:2]).astype(BF)
        bn[at, :] = normed
        k[at, :] = nn(normed, w_qkv[:, D : 2 * D]).astype(BF)
        v[at, :] = nn(normed, w_qkv[:, 2 * D :]).astype(BF)


def encode_rest(m, patch, up, w_qkv, w_out, gains, bounds, q, k_lo, v_lo, hb, o1, weights, bn, k, v):
    b = up[...].astype(F32)
    normed = (b * inverse_rms(b) * gains[1:2]).astype(BF)
    bn[...] = normed
    k[...] = nn(normed, w_qkv[:, D : 2 * D]).astype(BF)
    v[...] = nn(normed, w_qkv[:, 2 * D :]).astype(BF)
    spot = lax.broadcasted_iota(jnp.int32, (256, GROUP), 0)
    start = bounds[m, 0:1, :]
    end = bounds[m, 1:2, :]
    inside = [(spot + h * 256 >= start) & (spot + h * 256 < end) for h in range(2)]
    low_at = slice(m * 256, (m + 1) * 256)
    rows = slice(m * HD, (m + 1) * HD)
    for g in range(4):
        lanes = slice(g * GROUP, (g + 1) * GROUP)
        stacked = stack_heads(q[rows, lanes] * BF(SCALE))
        scores = [
            jnp.where(inside[h], nt(keys, stacked), NEG)
            for h, keys in enumerate((k_lo[low_at, lanes], k[:, lanes]))
        ]
        w = softmax_columns(scores)
        weights[g * 2] = w[0]
        weights[g * 2 + 1] = w[1]
        mixed = tn(w[0], v_lo[low_at, lanes]) + tn(w[1], v[:, lanes])
        o1[:, lanes] = unstack_heads(mixed).astype(BF)
    hb[...] = (patch[rows, :].astype(F32) + nn(o1[...], w_out[...])).astype(BF)


def latent_layer(
    ids, hb_a, hb_b, cot, allowed, w_qkv, w_out, gains, w_ff,
    latents, dhb, gain_grad, norms, grads, packed,
    qkv, weights, o2, ff_buf, acc_out, acc_norm, dqkv, sems,
):
    core = ids[0]
    units = w_ff.shape[1]
    step = ff_buf.shape[2]
    steps = units // step

    def fetch(i, slot):
        return pltpu.make_async_copy(
            w_ff.at[:, pl.ds(pl.multiple_of(i * step, 128), step), :], ff_buf.at[slot], sems.at[slot]
        )

    fetch(0, 0).start()
    x = jnp.concatenate([hb_a[...], hb_b[...]], 0).astype(F32)
    normed = (x * inverse_rms(x) * gains[0:1]).astype(BF)
    packed[PACK_LEFT : PACK_LEFT + D, :] = normed.T
    qkv[...] = nn(normed, w_qkv[...]).astype(BF)
    for m in range(2):
        rows = slice(m * HD, (m + 1) * HD)
        for g in range(4):
            lanes = slice(g * GROUP, (g + 1) * GROUP)
            k_lanes = slice(D + g * GROUP, D + (g + 1) * GROUP)
            v_lanes = slice(2 * D + g * GROUP, 2 * D + (g + 1) * GROUP)
            stacked = stack_heads(qkv[rows, lanes] * BF(SCALE))
            scores = jnp.where(allowed[m] > 0.5, nt(qkv[rows, k_lanes], stacked), NEG)
            (w,) = softmax_columns([scores])
            weights[m * 4 + g] = w
            o2[rows, lanes] = unstack_heads(tn(w, qkv[rows, v_lanes])).astype(BF)
    packed[PACK_LEFT + D : PACK_LEFT + 2 * D, :] = o2[...].T
    after = x + nn(o2[...], w_out[...])
    yn = (after * inverse_rms(after) * gains[1:2]).astype(BF)
    c = cot[...]
    for h in range(2):

        @pl.when(core == h)
        def _(h=h):
            norms[0:128, :] = yn[:, h * HALF : (h + 1) * HALF]
            norms[128:256, :] = c[:, h * HALF : (h + 1) * HALF]

        @pl.when(core != h)
        def _(h=h):
            for b in range(4):
                lanes = slice(h * HALF + b * 128, h * HALF + (b + 1) * 128)
                packed[PACK_NORMS + b * 256 : PACK_NORMS + b * 256 + 128, :] = yn[:, lanes]
                packed[PACK_NORMS + b * 256 + 128 : PACK_NORMS + (b + 1) * 256, :] = c[:, lanes]

    acc_out[...] = after
    acc_norm[...] = jnp.zeros_like(acc_norm)

    def ff_step(i, carry):
        slot = lax.rem(i, 2)

        @pl.when(i + 1 < steps)
        def _():
            fetch(i + 1, 1 - slot).start()

        fetch(i, slot).wait()
        w_gate, w_up, w_down = ff_buf.at[slot, 0], ff_buf.at[slot, 1], ff_buf.at[slot, 2]
        gate = nt(yn, w_gate[...])
        upward = nt(yn, w_up[...])
        du = nt(c, w_down[...])
        sig = 1.0 / (1.0 + jnp.exp(-gate))
        active = gate * sig
        hidden = (active * upward).astype(BF)
        d_gate = (du * upward * (sig * (1.0 + gate * (1.0 - sig)))).astype(BF)
        d_up = (du * active).astype(BF)
        at = pl.ds(pl.multiple_of(i * step, 128), step)
        for j, value in enumerate((d_gate, d_up, hidden)):
            packed[pl.ds(pl.multiple_of(i * step + j * units, 128), step), :] = value.T
        acc_out[...] += nn(hidden, w_down[...])
        acc_norm[...] += nn(d_gate, w_gate[...]) + nn(d_up, w_up[...])
        return carry

    lax.fori_loop(0, steps, ff_step, 0)
    latents[...] = acc_out[...]
    back, gain_rows = norm_back(after, gains[1:2], acc_norm[...])
    gain_grad[1:2, :] = jnp.sum(gain_rows, axis=0, keepdims=True)
    d_after = c.astype(F32) + back
    da = d_after.astype(BF)
    d_mixed = nt(da, w_out[...]).astype(BF)
    for m in range(2):
        rows = slice(m * HD, (m + 1) * HD)
        for g in range(4):
            lanes = slice(g * GROUP, (g + 1) * GROUP)
            k_lanes = slice(D + g * GROUP, D + (g + 1) * GROUP)
            v_lanes = slice(2 * D + g * GROUP, 2 * D + (g + 1) * GROUP)
            q_stacked = stack_heads(qkv[rows, lanes] * BF(SCALE))
            o_stacked = stack_heads(d_mixed[rows, lanes])
            w_low = weights[m * 4 + g]
            w = w_low.astype(F32)
            dw = nt(qkv[rows, v_lanes], o_stacked)
            inner = jnp.sum(dw * w, axis=0, keepdims=True)
            ds = (w * (dw - inner)).astype(BF)
            dqkv[rows, lanes] = (unstack_heads(tn(ds, qkv[rows, k_lanes])) * SCALE).astype(BF)
            dqkv[rows, k_lanes] = nn(ds, q_stacked).astype(BF)
            dqkv[rows, v_lanes] = nn(w_low, o_stacked).astype(BF)
    d_normed = nt(dqkv[...], w_qkv[...])
    back, gain_rows = norm_back(x, gains[0:1], d_normed)
    gain_grad[0:1, :] = jnp.sum(gain_rows, axis=0, keepdims=True)
    dhb[...] = (d_after + back).astype(BF)
    for h in range(2):
        pieces = (
            dqkv[:, h * HALF : (h + 1) * HALF],
            da[:, h * HALF : (h + 1) * HALF],
            dqkv[:, D + h * HALF : D + (h + 1) * HALF],
            dqkv[:, 2 * D + h * HALF : 2 * D + (h + 1) * HALF],
        )

        @pl.when(core == h)
        def _(pieces=pieces):
            for i, value in enumerate(pieces):
                grads[i * 128 : (i + 1) * 128, :] = value

        @pl.when(core != h)
        def _(pieces=pieces):
            for i, value in enumerate(pieces):
                for b in range(4):
                    first = PACK_GRADS + b * 512 + i * 128
                    packed[first : first + 128, :] = value[:, b * 128 : (b + 1) * 128]


def half_of(core, g, mine, other):
    lanes = slice((g % 2) * GROUP, (g % 2 + 1) * GROUP)

    def put(at, value):
        @pl.when(core == g // 2)
        def _():
            mine[at, lanes] = value

        @pl.when(core != g // 2)
        def _():
            other[at, lanes] = value

    return put


def encoder_attention_back(
    ids, dhb, w_out, q, k_lo, v_lo, k_a, k_b, v_a, v_b, w_a, w_b, mine, other
):
    d_mixed = nt(dhb[...], w_out[...]).astype(BF)
    for g in range(4):
        lanes = slice(g * GROUP, (g + 1) * GROUP)
        put = half_of(ids[0], g, mine, other)
        put(slice(128, 256), dhb[:, lanes])
        for m, (k_up, v_up, weights) in enumerate(((k_a, v_a, w_a), (k_b, v_b, w_b))):
            rows = slice(m * HD, (m + 1) * HD)
            low_at = slice(m * 256, (m + 1) * 256)
            q_stacked = stack_heads(q[rows, lanes] * BF(SCALE))
            o_stacked = stack_heads(d_mixed[rows, lanes])
            low = [weights[g * 2 + h] for h in range(2)]
            w = [piece.astype(F32) for piece in low]
            dw = [nt(values, o_stacked) for values in (v_lo[low_at, lanes], v_up[:, lanes])]
            inner = sum(jnp.sum(a * b, axis=0, keepdims=True) for a, b in zip(dw, w))
            ds = [(b * (a - inner)).astype(BF) for a, b in zip(dw, w)]
            dq = tn(ds[0], k_lo[low_at, lanes]) + tn(ds[1], k_up[:, lanes])
            put(rows, (unstack_heads(dq) * SCALE).astype(BF))
            for h in range(2):
                base = h * HALF + m * 256
                put(slice(256 + base, 512 + base), nn(ds[h], q_stacked).astype(BF))
                put(slice(1280 + base, 1536 + base), nn(low[h], o_stacked).astype(BF))


def both_columns(core, block, w_qkv):
    return [
        w_qkv[:, pl.ds(pl.multiple_of(block * D + which * HALF, HALF), HALF)] for which in (core, 1 - core)
    ]


def bytes_back(core, h, m, source, w_qkv, gains, grads):
    d_norm = sum(
        nt(ref[1024 * block - 768 + h * HALF + m * 256 : 1024 * block - 512 + h * HALF + m * 256, :], columns)
        for block in (1, 2)
        for ref, columns in zip(grads, both_columns(core, block, w_qkv))
    )
    back, gain_rows = norm_back(source.astype(F32), gains[1:2], d_norm)
    return back.astype(BF), jnp.sum(gain_rows, axis=0, keepdims=True)


def encoder_upper_back(ids, up_a, up_b, w_qkv, gains, mine, other, after, up_grad, gain_grad):
    total = jnp.zeros((1, D), F32)
    for m, source in enumerate((up_a, up_b)):
        back, rows = bytes_back(ids[0], 1, m, source[...], w_qkv, gains, (mine, other))
        up_grad[m * 256 : (m + 1) * 256, :] = back
        total = total + rows
    gain_grad[...] = total


def encoder_lower_back(
    ids, dhb, patch, low, w_qkv, gains, mine, other, after, patch_grad, low_grad, gain_grad
):
    core = ids[0]
    up_norm = sum(nt(ref[0:128, :], columns) for ref, columns in zip((mine, other), both_columns(core, 0, w_qkv)))
    back, gain_rows = norm_back(patch[...].astype(F32), gains[0:1], up_norm)
    gain_grad[0:1, :] = jnp.sum(gain_rows, axis=0, keepdims=True)
    patch_grad[...] = dhb[...].astype(F32) + back
    total = jnp.zeros((1, D), F32)
    for m in range(2):
        at = slice(m * 256, (m + 1) * 256)
        back, rows = bytes_back(core, 0, m, low[at, :], w_qkv, gains, (mine, other))
        low_grad[at, :] = back
        total = total + rows
    gain_grad[1:2, :] = total


def turn_encoder(pn, o_a, o_b, bn_lo, bn_a, bn_b, packed):
    for b, rows in enumerate([bn_lo[i * 128 : (i + 1) * 128, :] for i in range(4)]
                             + [ref[i * 128 : (i + 1) * 128, :] for ref in (bn_a, bn_b) for i in range(2)]):
        packed[b * D : (b + 1) * D, :] = rows.T
    packed[PACK_LEFT : PACK_LEFT + D, :] = pn[...].T
    packed[PACK_LEFT + D : PACK_LEFT + 2 * D, :] = jnp.concatenate([o_a[...], o_b[...]], 0).T


def rows_of_both(left, left_far, at):
    return jnp.concatenate([left[at, :], left_far[at, :]], 1)


def below(near, far, rows):
    return jnp.concatenate([near[rows, :], far[rows, :]], 0)


def encoder_weights(ids, packed, packed_far, near, far, *blocks):
    u = ids[1]
    queries = below(near, far, slice(0, 128))
    outputs = below(near, far, slice(128, 256))
    for k in range(4):
        first = lax.rem(u + k, 4) * 256

        def at(base, first=first):
            return pl.ds(pl.multiple_of(first + base, 256), 256)

        blocks[k][0] = nn(rows_of_both(packed, packed_far, at(PACK_LEFT)), queries).astype(BF)
        blocks[k][3] = nn(rows_of_both(packed, packed_far, at(PACK_LEFT + D)), outputs).astype(BF)
        lefts = [jnp.concatenate([ref[at(b * D), :] for b in range(8)], 1) for ref in (packed, packed_far)]
        for block in (1, 2):
            rows = slice(1024 * block - 768, 1024 * block + 256)
            blocks[k][block] = (nn(lefts[0], near[rows, :]) + nn(lefts[1], far[rows, :])).astype(BF)


def unpack(packed, first, rows):
    return jnp.concatenate([packed[first + b * rows : first + (b + 1) * rows, :] for b in range(4)], 1)


def latent_weights(ids, packed, packed_far, near, *blocks):
    u = ids[1]
    far = unpack(packed_far, PACK_GRADS, 512)
    rights = [jnp.concatenate([near[i * 128 : (i + 1) * 128, :], far[i * 128 : (i + 1) * 128, :]], 0) for i in range(4)]
    for k in range(4):
        first = PACK_LEFT + lax.rem(u + k, 4) * 256
        at = pl.ds(pl.multiple_of(first, 256), 256)
        low_at = pl.ds(pl.multiple_of(first + D, 256), 256)
        for block, (source, i) in enumerate(((at, 0), (at, 2), (at, 3), (low_at, 1))):
            blocks[k][block] = nn(rows_of_both(packed, packed_far, source), rights[i]).astype(BF)


def ff_weights_grad(ids, packed, packed_far, norms, out):
    share = UNITS // 16
    far = unpack(packed_far, PACK_NORMS, 256)
    normed = jnp.concatenate([norms[0:128, :], far[0:128, :]], 0)
    cot = jnp.concatenate([norms[128:256, :], far[128:256, :]], 0)
    for chunk in range(16):
        for j in range(3):
            at = slice(j * UNITS + chunk * share, j * UNITS + (chunk + 1) * share)
            out[chunk, j * share : (j + 1) * share, :] = nn(
                rows_of_both(packed, packed_far, at), normed if j < 2 else cot
            ).astype(BF)


def sum_four(own, a, b, c):
    return own.astype(F32) + a.astype(F32) + b.astype(F32) + c.astype(F32)


def pack_gain(value):
    high = value.astype(BF)
    low = (value - high.astype(F32)).astype(BF)
    return jnp.concatenate(
        [high.astype(F32), low.astype(F32), jnp.zeros((8, HALF), F32)], 0
    ).astype(BF)


def unpack_gain(rows):
    rows = rows.astype(F32)
    return rows[0:4] + rows[4:8]


GAIN_AT = slice(256, 272)


def attn_sum_first(ids, own, a, b, c, *outs):
    v = ids[2]
    for k in range(4):
        at = pl.ds(pl.multiple_of(lax.rem(v + k, 4) * HD, HD), HD)
        for block in range(4):
            outs[k][block * HD : (block + 1) * HD, :] = sum_four(
                own[block, at, :], a[block, at, :], b[block, at, :], c[block, at, :]
            ).astype(BF)


def attn_sum_first_gain(ids, own, a, b, c, enc_gain, up_gain, lat_gain, *outs):
    attn_sum_first(ids, own, a, b, c, *outs)
    first = ids[4] == 0
    gain = jnp.where(
        first, jnp.concatenate([enc_gain[0:1, :], enc_gain[1:2, :] + up_gain[...]], 0), lat_gain[...]
    )
    halves = [gain[i : i + 1, h * HALF : (h + 1) * HALF] for i in range(2) for h in range(2)]
    packed = pack_gain(jnp.concatenate(halves, 0))
    for out in outs:
        out[GAIN_AT, :] = packed


def sum_all(*refs):
    refs, out = refs[:-1], refs[-1]
    out[0:256, :] = sum(ref[0:256, :].astype(F32) for ref in refs).astype(BF)
    out[GAIN_AT, :] = pack_gain(sum(unpack_gain(ref[GAIN_AT, :]) for ref in refs))


def stack_rows(*refs):
    refs, out = refs[:-1], refs[-1]
    for j, ref in enumerate(refs):
        out[j * 256 : (j + 1) * 256, :] = ref[0:256, :]
    out[1024:1040, :] = refs[0][GAIN_AT, :]


def final_attn(ids, *refs):
    pieces, (qkv, out, gain) = refs[:8], refs[8:]
    step = pl.program_id(0)
    for side in range(2):
        core = ids[0] if side == 0 else 1 - ids[0]
        u = ids[1] if side == 0 else ids[2]
        v = ids[2] if side == 0 else ids[1]
        for k in range(4):
            piece = pieces[side * 4 + k]

            @pl.when(lax.rem(u + k, 4) == step)
            def _(piece=piece, v=v, core=core):
                for j in range(4):
                    at = pl.ds(pl.multiple_of(lax.rem(v + j, 4) * HD, HD), HD)
                    for block in range(4):
                        target, column = (qkv, block * D) if block < 3 else (out, 0)
                        lanes = pl.ds(pl.multiple_of(core * HALF + column, HALF), HALF)
                        first = j * 256 + block * HD
                        target[at, lanes] = piece[first : first + HD, :].astype(F32)

    mine = sum(unpack_gain(piece[1024:1040, :]) for piece in pieces[:4])
    other = sum(unpack_gain(piece[1024:1040, :]) for piece in pieces[4:])
    total = mine + other
    for i in range(2):
        for h in range(2):
            gain[i : i + 1, h * HALF : (h + 1) * HALF] = total[2 * i + h : 2 * i + h + 1, :]


SMEM = pltpu.MemorySpace.SMEM
VMEM = pltpu.MemorySpace.VMEM


def size(shape, dtype):
    return math.prod(shape) * jnp.dtype(dtype).itemsize


def call(kernel, args, outs, scratch=(), spaces=None, spare=6):
    spaces = spaces or {}
    vmem = sum(size(a.shape, a.dtype) for i, a in enumerate(args) if i not in spaces)
    vmem += sum(size(*o) for o in outs)
    vmem += sum(size(s.shape, s.dtype) for s in scratch if hasattr(s, "shape") and s.memory_space == VMEM)
    specs = [pl.BlockSpec(memory_space=spaces.get(i, VMEM)) for i in range(len(args))]
    return pl.pallas_call(
        kernel,
        out_shape=[jax.ShapeDtypeStruct(s, t) for s, t in outs],
        in_specs=specs,
        out_specs=[pl.BlockSpec(memory_space=VMEM) for _ in outs],
        scratch_shapes=list(scratch),
        compiler_params=pltpu.CompilerParams(vmem_limit_bytes=vmem + spare * 1024 * 1024),
    )(*args)


def nothing(outs):
    def kernel(*refs):
        pass

    return pl.pallas_call(
        kernel,
        out_shape=[jax.ShapeDtypeStruct(s, t) for s, t in outs],
        out_specs=[pl.BlockSpec(memory_space=pl.ANY) for _ in outs],
    )()


def on_section(flag, kernel, args, outs, **rest):
    return lax.cond(
        flag, lambda: call(kernel, args, outs, **rest), lambda: nothing(outs)
    )


def along(value, by):
    return lax.ppermute(value, "s", [(0, 1)] if by > 0 else [(1, 0)])


def swap(value, axis, sections=(0, 1)):
    pairs = [(s * 2 + i, s * 2 + 1 - i) for s in sections for i in range(2)]
    return lax.ppermute(value, ("s", axis), pairs)


def plane_shift(value, which, by, sections=(0, 1)):
    pairs = []
    for s in sections:
        for y in range(4):
            for x in range(4):
                for core in range(2):
                    ty, tx = ((y + by) % 4, x) if core == which else (y, (x + by) % 4)
                    pairs.append((((s * 4 + y) * 4 + x) * 2 + core, ((s * 4 + ty) * 4 + tx) * 2 + core))
    return lax.ppermute(value, ("s", "y", "x", "core"), pairs)


def exchange(blocks, which, sections=(0, 1)):
    return [plane_shift(blocks[k], which, k, sections) for k in (1, 2, 3)]


def collect(block, which):
    return [block] + [plane_shift(block, which, -k) for k in (1, 2, 3)]


def pick(stack, index, dim):
    return lax.dynamic_index_in_dim(stack, index, dim, keepdims=False)


def shards(patch_io, byte_states, patch_lengths, patch_live, attn_qkv, attn_out, gains, ff_weights):
    section = lax.axis_index("s")
    core = lax.axis_index("core")
    zh = lax.axis_index("zh")
    y, x = lax.axis_index("y"), lax.axis_index("x")
    first = section == 0
    second = section == 1
    ids = jnp.stack([core, jnp.where(core == 0, y, x), jnp.where(core == 0, x, y), zh, section])
    ids = ids.astype(jnp.int32)
    w_qkv = attn_qkv[0]
    w_out = attn_out[0]
    gain_pair = gains[0]
    micro, seq = patch_io.shape[1], patch_io.shape[3]
    half_bytes = byte_states.shape[2]
    units = ff_weights.shape[0]
    rows = micro * seq
    own_rows = patch_io.reshape(rows, D)
    up_a = along(byte_states[0, 0], -1)
    up_b = along(byte_states[1, 0], -1)
    lower = byte_states.reshape(micro * half_bytes, D)
    w_ff = jnp.swapaxes(ff_weights, 0, 1)
    lengths = patch_lengths[:, 0]
    live = patch_live[:, 0]
    ends = jnp.cumsum(lengths, axis=1)
    bounds = jnp.tile(jnp.stack([ends - lengths, ends], 1), (1, 1, 4))
    places = lax.iota(jnp.int32, seq)
    causal = places[:, None] <= places[None, :]
    diagonal = places[:, None] == places[None, :]
    allowed = causal[None] & ((live[:, :, None] == 1) | diagonal[None])
    allowed = lax.optimization_barrier(jnp.tile(allowed.astype(F32), (1, 1, 4)))

    wide = ((rows, D), BF)
    short = ((seq, D), BF)
    tall = ((micro * half_bytes, D), BF)
    piece = ((half_bytes, D), BF)
    pn, q, bn_lo, k_lo, v_lo = on_section(
        first, encode_lower, (own_rows, lower, w_qkv, gain_pair), [wide, wide, tall, tall, tall]
    )
    rest = []
    for m, up in enumerate((up_a, up_b)):
        rest.append(
            on_section(
                first,
                functools.partial(encode_rest, m),
                (own_rows, up, w_qkv, w_out, gain_pair, bounds, q, k_lo, v_lo),
                [short, short, ((8, 256, GROUP), BF), piece, piece, piece],
            )
        )
    (hb_a, o_a, w_a, bn_a, k_a, v_a), (hb_b, o_b, w_b, bn_b, k_b, v_b) = rest
    arrived = [along(hb_a, 1), along(hb_b, 1)]

    step = 256
    latent_outs = [
        ((rows, D), F32), wide, ((2, D), F32), ((256, HALF), BF), ((512, HALF), BF), ((PACK_ROWS, rows), BF),
    ]

    def latent():
        return call(
            latent_layer,
            (ids, *arrived, own_rows, allowed, w_qkv, w_out, gain_pair, w_ff),
            latent_outs,
            spaces={0: SMEM, 8: pl.ANY},
            scratch=[
                pltpu.VMEM((rows, 3 * D), BF),
                pltpu.VMEM((8, HD, GROUP), BF),
                pltpu.VMEM((rows, D), BF),
                pltpu.VMEM((2, 3, step, D), BF),
                pltpu.VMEM((rows, D), F32),
                pltpu.VMEM((rows, D), F32),
                pltpu.VMEM((rows, 3 * D), BF),
                pltpu.SemaphoreType.DMA((2,)),
            ],
        )

    def turn():
        return nothing(latent_outs[:5]) + call(
            turn_encoder, (pn, o_a, o_b, bn_lo, bn_a, bn_b), latent_outs[5:]
        )

    latents, dhb, latent_gain, norms, lat_grads, packed = lax.cond(second, latent, turn)
    returned = along(dhb, -1)

    packed, returned = lax.optimization_barrier((packed, returned))
    packed_far = swap(packed, "core")

    share = units // 16
    (ff_blocks,) = on_section(
        second, ff_weights_grad, (ids, packed, packed_far, norms), [((16, 3 * share, HALF), BF)], spaces={0: SMEM}
    )
    ff_sum = lax.psum_scatter(ff_blocks, ("y", "x"), scatter_dimension=0, tiled=False)
    ff_sum = ff_sum.reshape(3, 2, share // 2, HALF)
    ff_far = swap(pick(ff_sum, 1 - zh, 1), "zh", (1,))
    ff_sum = (pick(ff_sum, zh, 1).astype(F32) + ff_far.astype(F32)).astype(BF).reshape(3, 2, share // 4, HALF)
    ff_mine = pick(ff_sum, core, 1)
    ff_far = swap(pick(ff_sum, 1 - core, 1), "core", (1,))
    ff_pair = jnp.stack([jnp.where(core == 0, ff_mine, ff_far), jnp.where(core == 0, ff_far, ff_mine)], 2)
    ff_grad = jnp.swapaxes(ff_pair.reshape(3, share // 4, D), 0, 1).astype(F32)
    ff_grad = jnp.where(second, ff_grad, 0.0)

    grads_long = ((2304, HALF), BF)
    enc_grads, enc_other = on_section(
        first,
        encoder_attention_back,
        (ids, returned, w_out, q, k_lo, v_lo, k_a, k_b, v_a, v_b, w_a, w_b),
        [grads_long, grads_long],
        spaces={0: SMEM},
    )
    enc_far = swap(enc_other, "core", (0,))
    outs = [((4, 256, HALF), BF)] * 4
    blocks = lax.cond(
        first,
        lambda: call(encoder_weights, (ids, packed, packed_far, enc_grads, enc_far), outs, spaces={0: SMEM}),
        lambda: call(latent_weights, (ids, packed, packed_far, lat_grads), outs, spaces={0: SMEM}),
    )
    got = exchange(blocks, 0)
    up_grad, up_gain = on_section(
        first,
        encoder_upper_back,
        (ids, up_a, up_b, w_qkv, gain_pair, enc_grads, enc_other, blocks[0]),
        [tall, ((1, D), F32)],
        spaces={0: SMEM, 7: pl.ANY},
    )
    up_arrived = along(up_grad, 1)
    patch_grad, low_grad, encoder_gain = on_section(
        first,
        encoder_lower_back,
        (ids, returned, own_rows, lower, w_qkv, gain_pair, enc_grads, enc_other, up_gain),
        [((rows, D), F32), tall, ((2, D), F32)],
        spaces={0: SMEM, 8: pl.ANY},
    )
    line = [((272, HALF), BF)]
    blocks = call(
        attn_sum_first_gain,
        (ids, blocks[0], *got, encoder_gain, up_gain, latent_gain),
        line * 4,
        spaces={0: SMEM},
    )
    met, up_arrived = lax.optimization_barrier((exchange(blocks, 1), up_arrived))
    (block,) = call(sum_all, (blocks[0], *met), line)
    (block,) = call(sum_all, (block, swap(block, "zh")), line)
    (block,) = call(stack_rows, collect(block, 1), [((1040, HALF), BF)])
    pieces = collect(block, 0)
    byte_grad = jnp.where(first, low_grad, up_arrived)
    patch_out = jnp.where(first, patch_grad, latents)
    pieces = pieces + [swap(p, "core") for p in pieces]
    whole = lambda p: pl.BlockSpec(p.shape, lambda i, n=p.ndim: (0,) * n)
    total_qkv, total_out, total_gain = pl.pallas_call(
        final_attn,
        grid=(4,),
        out_shape=[
            jax.ShapeDtypeStruct((D, 3 * D), F32),
            jax.ShapeDtypeStruct((D, D), F32),
            jax.ShapeDtypeStruct((2, D), F32),
        ],
        in_specs=[pl.BlockSpec(memory_space=SMEM)] + [whole(p) for p in pieces],
        out_specs=[
            pl.BlockSpec((256, 3 * D), lambda i: (i, 0)),
            pl.BlockSpec((256, D), lambda i: (i, 0)),
            pl.BlockSpec((2, D), lambda i: (0, 0)),
        ],
        compiler_params=pltpu.CompilerParams(vmem_limit_bytes=FINAL_VMEM),
    )(ids, *pieces)
    return (
        patch_out.reshape(1, micro, 1, seq, D),
        byte_grad.reshape(micro, 1, half_bytes, D),
        total_qkv[None],
        total_out[None],
        total_gain[None],
        ff_grad[None],
    )


def solution(mesh):
    fine = Mesh(mesh.devices.reshape(2, 4, 4, 2, 2), ("s",) + BATCH)
    in_specs = (
        P("s", None, BATCH, None, None),
        P(None, BATCH, "s", None),
        P(None, BATCH, None),
        P(None, BATCH, None),
        P("s", None, None),
        P("s", None, None),
        P("s", None, None),
        P(),
    )
    out_specs = (
        P("s", None, BATCH, None, None),
        P(None, BATCH, "s", None),
        P("s", None, None),
        P("s", None, None),
        P("s", None, None),
        P("s", BATCH, None, None),
    )
    return jax.shard_map(shards, mesh=fine, in_specs=in_specs, out_specs=out_specs, check_vma=False)
```

```python
import functools
import math

import jax
import jax.numpy as jnp
from jax import lax
from jax.experimental import pallas as pl
from jax.experimental.pallas import tpu as pltpu
from jax.sharding import Mesh
from jax.sharding import PartitionSpec as P

HD = 64
SCALE = HD**-0.5
EPS = 1e-05
NEG = -1e30
BATCH = ("y", "x", "zh", "core")
BF = jnp.bfloat16
F32 = jnp.float32
D = 1024
HALF = 512
GROUP = 256
FINAL_VMEM = 32 * 1024 * 1024


UNITS = 2816
PACK_NORMS = 3 * UNITS
PACK_LEFT = PACK_NORMS + 4 * 256
PACK_GRADS = PACK_LEFT + 2 * D
PACK_ROWS = PACK_GRADS + 4 * 512


def nn(a, b):
    return lax.dot_general(a, b, (((1,), (0,)), ((), ())), preferred_element_type=F32)


def nt(a, b):
    return lax.dot_general(a, b, (((1,), (1,)), ((), ())), preferred_element_type=F32)


def tn(a, b):
    return lax.dot_general(a, b, (((0,), (0,)), ((), ())), preferred_element_type=F32)


def inverse_rms(x):
    return lax.rsqrt(jnp.mean(x * x, axis=-1, keepdims=True) + EPS)


def norm_back(x, gain, up):
    r = inverse_rms(x)
    scaled = up * gain
    inner = jnp.mean(scaled * x, axis=-1, keepdims=True)
    return r * (scaled - x * (r * r * inner)), up * (x * r)


def stack_heads(rows):
    head = lax.broadcasted_iota(jnp.int32, rows.shape, 1) // HD
    return jnp.concatenate([jnp.where(head == h, rows, jnp.zeros_like(rows)) for h in range(4)], 0)


def unstack_heads(stacked):
    head = lax.broadcasted_iota(jnp.int32, (HD, GROUP), 1) // HD
    out = stacked[0:HD]
    for h in range(1, 4):
        out = jnp.where(head == h, stacked[h * HD : (h + 1) * HD], out)
    return out


def softmax_columns(scores):
    top = functools.reduce(jnp.maximum, [jnp.max(s, axis=0, keepdims=True) for s in scores])
    parts = [jnp.exp(s - top) for s in scores]
    inverse = 1.0 / sum(jnp.sum(p, axis=0, keepdims=True) for p in parts)
    return [(p * inverse).astype(BF) for p in parts]


def encode_lower(patch, low, w_qkv, gains, pn, q, bn, k, v):
    x = patch[...].astype(F32)
    normed = (x * inverse_rms(x) * gains[0:1]).astype(BF)
    pn[...] = normed
    q[...] = nn(normed, w_qkv[:, 0:D]).astype(BF)
    for i in range(2):
        at = pl.ds(i * 256, 256)
        b = low[at, :].astype(F32)
        normed = (b * inverse_rms(b) * gains[1:2]).astype(BF)
        bn[at, :] = normed
        k[at, :] = nn(normed, w_qkv[:, D : 2 * D]).astype(BF)
        v[at, :] = nn(normed, w_qkv[:, 2 * D :]).astype(BF)


def encode_rest(m, patch, up, w_qkv, w_out, gains, bounds, q, k_lo, v_lo, hb, o1, weights, bn, k, v):
    b = up[...].astype(F32)
    normed = (b * inverse_rms(b) * gains[1:2]).astype(BF)
    bn[...] = normed
    k[...] = nn(normed, w_qkv[:, D : 2 * D]).astype(BF)
    v[...] = nn(normed, w_qkv[:, 2 * D :]).astype(BF)
    spot = lax.broadcasted_iota(jnp.int32, (256, GROUP), 0)
    start = bounds[m, 0:1, :]
    end = bounds[m, 1:2, :]
    inside = [(spot + h * 256 >= start) & (spot + h * 256 < end) for h in range(2)]
    low_at = slice(m * 256, (m + 1) * 256)
    rows = slice(m * HD, (m + 1) * HD)
    for g in range(4):
        lanes = slice(g * GROUP, (g + 1) * GROUP)
        stacked = stack_heads(q[rows, lanes] * BF(SCALE))
        scores = [
            jnp.where(inside[h], nt(keys, stacked), NEG)
            for h, keys in enumerate((k_lo[low_at, lanes], k[:, lanes]))
        ]
        w = softmax_columns(scores)
        weights[g * 2] = w[0]
        weights[g * 2 + 1] = w[1]
        mixed = tn(w[0], v_lo[low_at, lanes]) + tn(w[1], v[:, lanes])
        o1[:, lanes] = unstack_heads(mixed).astype(BF)
    hb[...] = (patch[rows, :].astype(F32) + nn(o1[...], w_out[...])).astype(BF)


def latent_layer(
    ids, hb_a, hb_b, cot, allowed, w_qkv, w_out, gains, w_ff,
    latents, dhb, gain_grad, norms, grads, packed,
    qkv, weights, o2, ff_buf, acc_out, acc_norm, dqkv, sems,
):
    core = ids[0]
    units = w_ff.shape[1]
    step = ff_buf.shape[2]
    steps = units // step

    def fetch(i, slot):
        return pltpu.make_async_copy(
            w_ff.at[:, pl.ds(pl.multiple_of(i * step, 128), step), :], ff_buf.at[slot], sems.at[slot]
        )

    fetch(0, 0).start()
    x = jnp.concatenate([hb_a[...], hb_b[...]], 0).astype(F32)
    normed = (x * inverse_rms(x) * gains[0:1]).astype(BF)
    packed[PACK_LEFT : PACK_LEFT + D, :] = normed.T
    qkv[...] = nn(normed, w_qkv[...]).astype(BF)
    for m in range(2):
        rows = slice(m * HD, (m + 1) * HD)
        for g in range(4):
            lanes = slice(g * GROUP, (g + 1) * GROUP)
            k_lanes = slice(D + g * GROUP, D + (g + 1) * GROUP)
            v_lanes = slice(2 * D + g * GROUP, 2 * D + (g + 1) * GROUP)
            stacked = stack_heads(qkv[rows, lanes] * BF(SCALE))
            scores = jnp.where(allowed[m] > 0.5, nt(qkv[rows, k_lanes], stacked), NEG)
            (w,) = softmax_columns([scores])
            weights[m * 4 + g] = w
            o2[rows, lanes] = unstack_heads(tn(w, qkv[rows, v_lanes])).astype(BF)
    packed[PACK_LEFT + D : PACK_LEFT + 2 * D, :] = o2[...].T
    after = x + nn(o2[...], w_out[...])
    yn = (after * inverse_rms(after) * gains[1:2]).astype(BF)
    c = cot[...]
    for h in range(2):

        @pl.when(core == h)
        def _(h=h):
            norms[0:128, :] = yn[:, h * HALF : (h + 1) * HALF]
            norms[128:256, :] = c[:, h * HALF : (h + 1) * HALF]

        @pl.when(core != h)
        def _(h=h):
            for b in range(4):
                lanes = slice(h * HALF + b * 128, h * HALF + (b + 1) * 128)
                packed[PACK_NORMS + b * 256 : PACK_NORMS + b * 256 + 128, :] = yn[:, lanes]
                packed[PACK_NORMS + b * 256 + 128 : PACK_NORMS + (b + 1) * 256, :] = c[:, lanes]

    acc_out[...] = after
    acc_norm[...] = jnp.zeros_like(acc_norm)

    def ff_step(i, carry):
        slot = lax.rem(i, 2)

        @pl.when(i + 1 < steps)
        def _():
            fetch(i + 1, 1 - slot).start()

        fetch(i, slot).wait()
        w_gate, w_up, w_down = ff_buf.at[slot, 0], ff_buf.at[slot, 1], ff_buf.at[slot, 2]
        gate = nt(yn, w_gate[...])
        upward = nt(yn, w_up[...])
        du = nt(c, w_down[...])
        sig = 1.0 / (1.0 + jnp.exp(-gate))
        active = gate * sig
        hidden = (active * upward).astype(BF)
        d_gate = (du * upward * (sig * (1.0 + gate * (1.0 - sig)))).astype(BF)
        d_up = (du * active).astype(BF)
        at = pl.ds(pl.multiple_of(i * step, 128), step)
        for j, value in enumerate((d_gate, d_up, hidden)):
            packed[pl.ds(pl.multiple_of(i * step + j * units, 128), step), :] = value.T
        acc_out[...] += nn(hidden, w_down[...])
        acc_norm[...] += nn(d_gate, w_gate[...]) + nn(d_up, w_up[...])
        return carry

    lax.fori_loop(0, steps, ff_step, 0)
    latents[...] = acc_out[...]
    back, gain_rows = norm_back(after, gains[1:2], acc_norm[...])
    gain_grad[1:2, :] = jnp.sum(gain_rows, axis=0, keepdims=True)
    d_after = c.astype(F32) + back
    da = d_after.astype(BF)
    d_mixed = nt(da, w_out[...]).astype(BF)
    for m in range(2):
        rows = slice(m * HD, (m + 1) * HD)
        for g in range(4):
            lanes = slice(g * GROUP, (g + 1) * GROUP)
            k_lanes = slice(D + g * GROUP, D + (g + 1) * GROUP)
            v_lanes = slice(2 * D + g * GROUP, 2 * D + (g + 1) * GROUP)
            q_stacked = stack_heads(qkv[rows, lanes] * BF(SCALE))
            o_stacked = stack_heads(d_mixed[rows, lanes])
            w_low = weights[m * 4 + g]
            w = w_low.astype(F32)
            dw = nt(qkv[rows, v_lanes], o_stacked)
            inner = jnp.sum(dw * w, axis=0, keepdims=True)
            ds = (w * (dw - inner)).astype(BF)
            dqkv[rows, lanes] = (unstack_heads(tn(ds, qkv[rows, k_lanes])) * SCALE).astype(BF)
            dqkv[rows, k_lanes] = nn(ds, q_stacked).astype(BF)
            dqkv[rows, v_lanes] = nn(w_low, o_stacked).astype(BF)
    d_normed = nt(dqkv[...], w_qkv[...])
    back, gain_rows = norm_back(x, gains[0:1], d_normed)
    gain_grad[0:1, :] = jnp.sum(gain_rows, axis=0, keepdims=True)
    dhb[...] = (d_after + back).astype(BF)
    for h in range(2):
        pieces = (
            dqkv[:, h * HALF : (h + 1) * HALF],
            da[:, h * HALF : (h + 1) * HALF],
            dqkv[:, D + h * HALF : D + (h + 1) * HALF],
            dqkv[:, 2 * D + h * HALF : 2 * D + (h + 1) * HALF],
        )

        @pl.when(core == h)
        def _(pieces=pieces):
            for i, value in enumerate(pieces):
                grads[i * 128 : (i + 1) * 128, :] = value

        @pl.when(core != h)
        def _(pieces=pieces):
            for i, value in enumerate(pieces):
                for b in range(4):
                    first = PACK_GRADS + b * 512 + i * 128
                    packed[first : first + 128, :] = value[:, b * 128 : (b + 1) * 128]


def half_of(core, g, mine, other):
    lanes = slice((g % 2) * GROUP, (g % 2 + 1) * GROUP)

    def put(at, value):
        @pl.when(core == g // 2)
        def _():
            mine[at, lanes] = value

        @pl.when(core != g // 2)
        def _():
            other[at, lanes] = value

    return put


def encoder_attention_back(
    ids, dhb, w_out, q, k_lo, v_lo, k_a, k_b, v_a, v_b, w_a, w_b, mine, other
):
    d_mixed = nt(dhb[...], w_out[...]).astype(BF)
    for g in range(4):
        lanes = slice(g * GROUP, (g + 1) * GROUP)
        put = half_of(ids[0], g, mine, other)
        put(slice(128, 256), dhb[:, lanes])
        for m, (k_up, v_up, weights) in enumerate(((k_a, v_a, w_a), (k_b, v_b, w_b))):
            rows = slice(m * HD, (m + 1) * HD)
            low_at = slice(m * 256, (m + 1) * 256)
            q_stacked = stack_heads(q[rows, lanes] * BF(SCALE))
            o_stacked = stack_heads(d_mixed[rows, lanes])
            low = [weights[g * 2 + h] for h in range(2)]
            w = [piece.astype(F32) for piece in low]
            dw = [nt(values, o_stacked) for values in (v_lo[low_at, lanes], v_up[:, lanes])]
            inner = sum(jnp.sum(a * b, axis=0, keepdims=True) for a, b in zip(dw, w))
            ds = [(b * (a - inner)).astype(BF) for a, b in zip(dw, w)]
            dq = tn(ds[0], k_lo[low_at, lanes]) + tn(ds[1], k_up[:, lanes])
            put(rows, (unstack_heads(dq) * SCALE).astype(BF))
            for h in range(2):
                base = h * HALF + m * 256
                put(slice(256 + base, 512 + base), nn(ds[h], q_stacked).astype(BF))
                put(slice(1280 + base, 1536 + base), nn(low[h], o_stacked).astype(BF))


def both_columns(core, block, w_qkv):
    return [
        w_qkv[:, pl.ds(pl.multiple_of(block * D + which * HALF, HALF), HALF)] for which in (core, 1 - core)
    ]


def bytes_back(core, h, m, source, w_qkv, gains, grads):
    d_norm = sum(
        nt(ref[1024 * block - 768 + h * HALF + m * 256 : 1024 * block - 512 + h * HALF + m * 256, :], columns)
        for block in (1, 2)
        for ref, columns in zip(grads, both_columns(core, block, w_qkv))
    )
    back, gain_rows = norm_back(source.astype(F32), gains[1:2], d_norm)
    return back.astype(BF), jnp.sum(gain_rows, axis=0, keepdims=True)


def encoder_upper_back(ids, up_a, up_b, w_qkv, gains, mine, other, after, up_grad, gain_grad):
    total = jnp.zeros((1, D), F32)
    for m, source in enumerate((up_a, up_b)):
        back, rows = bytes_back(ids[0], 1, m, source[...], w_qkv, gains, (mine, other))
        up_grad[m * 256 : (m + 1) * 256, :] = back
        total = total + rows
    gain_grad[...] = total


def encoder_lower_back(
    ids, dhb, patch, low, w_qkv, gains, mine, other, after, patch_grad, low_grad, gain_grad
):
    core = ids[0]
    up_norm = sum(nt(ref[0:128, :], columns) for ref, columns in zip((mine, other), both_columns(core, 0, w_qkv)))
    back, gain_rows = norm_back(patch[...].astype(F32), gains[0:1], up_norm)
    gain_grad[0:1, :] = jnp.sum(gain_rows, axis=0, keepdims=True)
    patch_grad[...] = dhb[...].astype(F32) + back
    total = jnp.zeros((1, D), F32)
    for m in range(2):
        at = slice(m * 256, (m + 1) * 256)
        back, rows = bytes_back(core, 0, m, low[at, :], w_qkv, gains, (mine, other))
        low_grad[at, :] = back
        total = total + rows
    gain_grad[1:2, :] = total


def turn_encoder(pn, o_a, o_b, bn_lo, bn_a, bn_b, packed):
    for b, rows in enumerate([bn_lo[i * 128 : (i + 1) * 128, :] for i in range(4)]
                             + [ref[i * 128 : (i + 1) * 128, :] for ref in (bn_a, bn_b) for i in range(2)]):
        packed[b * D : (b + 1) * D, :] = rows.T
    packed[PACK_LEFT : PACK_LEFT + D, :] = pn[...].T
    packed[PACK_LEFT + D : PACK_LEFT + 2 * D, :] = jnp.concatenate([o_a[...], o_b[...]], 0).T


def rows_of_both(left, left_far, at):
    return jnp.concatenate([left[at, :], left_far[at, :]], 1)


def below(near, far, rows):
    return jnp.concatenate([near[rows, :], far[rows, :]], 0)


def encoder_weights(ids, packed, packed_far, near, far, *blocks):
    u = ids[1]
    queries = below(near, far, slice(0, 128))
    outputs = below(near, far, slice(128, 256))
    for k in range(4):
        first = lax.rem(u + k, 4) * 256

        def at(base, first=first):
            return pl.ds(pl.multiple_of(first + base, 256), 256)

        blocks[k][0] = nn(rows_of_both(packed, packed_far, at(PACK_LEFT)), queries).astype(BF)
        blocks[k][3] = nn(rows_of_both(packed, packed_far, at(PACK_LEFT + D)), outputs).astype(BF)
        lefts = [jnp.concatenate([ref[at(b * D), :] for b in range(8)], 1) for ref in (packed, packed_far)]
        for block in (1, 2):
            rows = slice(1024 * block - 768, 1024 * block + 256)
            blocks[k][block] = (nn(lefts[0], near[rows, :]) + nn(lefts[1], far[rows, :])).astype(BF)


def unpack(packed, first, rows):
    return jnp.concatenate([packed[first + b * rows : first + (b + 1) * rows, :] for b in range(4)], 1)


def latent_weights(ids, packed, packed_far, near, *blocks):
    u = ids[1]
    far = unpack(packed_far, PACK_GRADS, 512)
    rights = [jnp.concatenate([near[i * 128 : (i + 1) * 128, :], far[i * 128 : (i + 1) * 128, :]], 0) for i in range(4)]
    for k in range(4):
        first = PACK_LEFT + lax.rem(u + k, 4) * 256
        at = pl.ds(pl.multiple_of(first, 256), 256)
        low_at = pl.ds(pl.multiple_of(first + D, 256), 256)
        for block, (source, i) in enumerate(((at, 0), (at, 2), (at, 3), (low_at, 1))):
            blocks[k][block] = nn(rows_of_both(packed, packed_far, source), rights[i]).astype(BF)


def ff_weights_grad(ids, packed, packed_far, norms, own, right, left, far_a, far_b):
    core, u = ids[0], ids[1]
    share = UNITS // 16
    far = unpack(packed_far, PACK_NORMS, 256)
    normed = jnp.concatenate([norms[0:128, :], far[0:128, :]], 0)
    cot = jnp.concatenate([norms[128:256, :], far[128:256, :]], 0)
    for k in range(4):
        there = lax.rem(u + k, 4)
        for v in range(4):
            chunk = jnp.where(core == 0, there * 4 + v, v * 4 + there)
            for j in range(3):
                at = pl.ds(pl.multiple_of(j * UNITS + chunk * share, 16), share)
                value = nn(rows_of_both(packed, packed_far, at), normed if j < 2 else cot).astype(BF)
                rows = slice(j * share, (j + 1) * share)
                if k == 2:
                    far_a[v, rows, :] = value[:, :GROUP]
                    far_b[v, rows, :] = value[:, GROUP:]
                else:
                    (own, right, None, left)[k][v, rows, :] = value


def ff_add(right, left, from_left, from_right, after, new_right, new_left):
    new_right[:, :, 0:GROUP] = (right[:, :, 0:GROUP].astype(F32) + from_left[...].astype(F32)).astype(BF)
    new_right[:, :, GROUP:] = right[:, :, GROUP:]
    new_left[:, :, 0:GROUP] = left[:, :, 0:GROUP]
    new_left[:, :, GROUP:] = (left[:, :, GROUP:].astype(F32) + from_right[...].astype(F32)).astype(BF)


def sum_four(own, a, b, c):
    return own.astype(F32) + a.astype(F32) + b.astype(F32) + c.astype(F32)


def pack_gain(value):
    high = value.astype(BF)
    low = (value - high.astype(F32)).astype(BF)
    return jnp.concatenate(
        [high.astype(F32), low.astype(F32), jnp.zeros((8, HALF), F32)], 0
    ).astype(BF)


def unpack_gain(rows):
    rows = rows.astype(F32)
    return rows[0:4] + rows[4:8]


GAIN_AT = slice(256, 272)


def attn_sum_first(ids, own, a, b, c, *outs):
    v = ids[2]
    for k in range(4):
        at = pl.ds(pl.multiple_of(lax.rem(v + k, 4) * HD, HD), HD)
        for block in range(4):
            outs[k][block * HD : (block + 1) * HD, :] = sum_four(
                own[block, at, :], a[block, at, :], b[block, at, :], c[block, at, :]
            ).astype(BF)


def attn_sum_first_gain(ids, own, a, b, c, enc_gain, up_gain, lat_gain, *outs):
    attn_sum_first(ids, own, a, b, c, *outs)
    first = ids[4] == 0
    gain = jnp.where(
        first, jnp.concatenate([enc_gain[0:1, :], enc_gain[1:2, :] + up_gain[...]], 0), lat_gain[...]
    )
    halves = [gain[i : i + 1, h * HALF : (h + 1) * HALF] for i in range(2) for h in range(2)]
    packed = pack_gain(jnp.concatenate(halves, 0))
    for out in outs:
        out[GAIN_AT, :] = packed


def sum_all(*refs):
    refs, out = refs[:-1], refs[-1]
    out[0:256, :] = sum(ref[0:256, :].astype(F32) for ref in refs).astype(BF)
    out[GAIN_AT, :] = pack_gain(sum(unpack_gain(ref[GAIN_AT, :]) for ref in refs))


def stack_rows(*refs):
    refs, out = refs[:-1], refs[-1]
    for j, ref in enumerate(refs):
        out[j * 256 : (j + 1) * 256, :] = ref[0:256, :]
    out[1024:1040, :] = refs[0][GAIN_AT, :]


def ff_sum_first(ids, own, a, b, *outs):
    v = ids[2]
    for k in range(4):
        at = lax.rem(v + k, 4)
        outs[k][...] = (own[at].astype(F32) + a[at].astype(F32) + b[at].astype(F32)).astype(BF)


def ff_sum_second(own, a, b, c, out):
    out[...] = sum_four(own[...], a[...], b[...], c[...]).astype(BF)


def final_attn(ids, *refs):
    pieces, (qkv, out, gain) = refs[:8], refs[8:]
    step = pl.program_id(0)
    for side in range(2):
        core = ids[0] if side == 0 else 1 - ids[0]
        u = ids[1] if side == 0 else ids[2]
        v = ids[2] if side == 0 else ids[1]
        for k in range(4):
            piece = pieces[side * 4 + k]

            @pl.when(lax.rem(u + k, 4) == step)
            def _(piece=piece, v=v, core=core):
                for j in range(4):
                    at = pl.ds(pl.multiple_of(lax.rem(v + j, 4) * HD, HD), HD)
                    for block in range(4):
                        target, column = (qkv, block * D) if block < 3 else (out, 0)
                        lanes = pl.ds(pl.multiple_of(core * HALF + column, HALF), HALF)
                        first = j * 256 + block * HD
                        target[at, lanes] = piece[first : first + HD, :].astype(F32)

    mine = sum(unpack_gain(piece[1024:1040, :]) for piece in pieces[:4])
    other = sum(unpack_gain(piece[1024:1040, :]) for piece in pieces[4:])
    total = mine + other
    for i in range(2):
        for h in range(2):
            gain[i : i + 1, h * HALF : (h + 1) * HALF] = total[2 * i + h : 2 * i + h + 1, :]


SMEM = pltpu.MemorySpace.SMEM
VMEM = pltpu.MemorySpace.VMEM


def size(shape, dtype):
    return math.prod(shape) * jnp.dtype(dtype).itemsize


def call(kernel, args, outs, scratch=(), spaces=None, spare=6):
    spaces = spaces or {}
    vmem = sum(size(a.shape, a.dtype) for i, a in enumerate(args) if i not in spaces)
    vmem += sum(size(*o) for o in outs)
    vmem += sum(size(s.shape, s.dtype) for s in scratch if hasattr(s, "shape") and s.memory_space == VMEM)
    specs = [pl.BlockSpec(memory_space=spaces.get(i, VMEM)) for i in range(len(args))]
    return pl.pallas_call(
        kernel,
        out_shape=[jax.ShapeDtypeStruct(s, t) for s, t in outs],
        in_specs=specs,
        out_specs=[pl.BlockSpec(memory_space=VMEM) for _ in outs],
        scratch_shapes=list(scratch),
        compiler_params=pltpu.CompilerParams(vmem_limit_bytes=vmem + spare * 1024 * 1024),
    )(*args)


def nothing(outs):
    def kernel(*refs):
        pass

    return pl.pallas_call(
        kernel,
        out_shape=[jax.ShapeDtypeStruct(s, t) for s, t in outs],
        out_specs=[pl.BlockSpec(memory_space=pl.ANY) for _ in outs],
    )()


def on_section(flag, kernel, args, outs, **rest):
    return lax.cond(
        flag, lambda: call(kernel, args, outs, **rest), lambda: nothing(outs)
    )


def along(value, by):
    return lax.ppermute(value, "s", [(0, 1)] if by > 0 else [(1, 0)])


def swap(value, axis, sections=(0, 1)):
    pairs = [(s * 2 + i, s * 2 + 1 - i) for s in sections for i in range(2)]
    return lax.ppermute(value, ("s", axis), pairs)


def plane_shift(value, which, by, sections=(0, 1)):
    pairs = []
    for s in sections:
        for y in range(4):
            for x in range(4):
                for core in range(2):
                    ty, tx = ((y + by) % 4, x) if core == which else (y, (x + by) % 4)
                    pairs.append((((s * 4 + y) * 4 + x) * 2 + core, ((s * 4 + ty) * 4 + tx) * 2 + core))
    return lax.ppermute(value, ("s", "y", "x", "core"), pairs)


def exchange(blocks, which, sections=(0, 1)):
    return [plane_shift(blocks[k], which, k, sections) for k in (1, 2, 3)]


def collect(block, which):
    return [block] + [plane_shift(block, which, -k) for k in (1, 2, 3)]


def pick(stack, index, dim):
    return lax.dynamic_index_in_dim(stack, index, dim, keepdims=False)


def shards(patch_io, byte_states, patch_lengths, patch_live, attn_qkv, attn_out, gains, ff_weights):
    section = lax.axis_index("s")
    core = lax.axis_index("core")
    zh = lax.axis_index("zh")
    y, x = lax.axis_index("y"), lax.axis_index("x")
    first = section == 0
    second = section == 1
    ids = jnp.stack([core, jnp.where(core == 0, y, x), jnp.where(core == 0, x, y), zh, section])
    ids = ids.astype(jnp.int32)
    w_qkv = attn_qkv[0]
    w_out = attn_out[0]
    gain_pair = gains[0]
    micro, seq = patch_io.shape[1], patch_io.shape[3]
    half_bytes = byte_states.shape[2]
    units = ff_weights.shape[0]
    rows = micro * seq
    own_rows = patch_io.reshape(rows, D)
    up_a = along(byte_states[0, 0], -1)
    up_b = along(byte_states[1, 0], -1)
    lower = byte_states.reshape(micro * half_bytes, D)
    w_ff = jnp.swapaxes(ff_weights, 0, 1)
    lengths = patch_lengths[:, 0]
    live = patch_live[:, 0]
    ends = jnp.cumsum(lengths, axis=1)
    bounds = jnp.tile(jnp.stack([ends - lengths, ends], 1), (1, 1, 4))
    places = lax.iota(jnp.int32, seq)
    causal = places[:, None] <= places[None, :]
    diagonal = places[:, None] == places[None, :]
    allowed = causal[None] & ((live[:, :, None] == 1) | diagonal[None])
    allowed = lax.optimization_barrier(jnp.tile(allowed.astype(F32), (1, 1, 4)))

    wide = ((rows, D), BF)
    short = ((seq, D), BF)
    tall = ((micro * half_bytes, D), BF)
    piece = ((half_bytes, D), BF)
    pn, q, bn_lo, k_lo, v_lo = on_section(
        first, encode_lower, (own_rows, lower, w_qkv, gain_pair), [wide, wide, tall, tall, tall]
    )
    rest = []
    for m, up in enumerate((up_a, up_b)):
        rest.append(
            on_section(
                first,
                functools.partial(encode_rest, m),
                (own_rows, up, w_qkv, w_out, gain_pair, bounds, q, k_lo, v_lo),
                [short, short, ((8, 256, GROUP), BF), piece, piece, piece],
            )
        )
    (hb_a, o_a, w_a, bn_a, k_a, v_a), (hb_b, o_b, w_b, bn_b, k_b, v_b) = rest
    arrived = [along(hb_a, 1), along(hb_b, 1)]

    step = 256
    latent_outs = [
        ((rows, D), F32), wide, ((2, D), F32), ((256, HALF), BF), ((512, HALF), BF), ((PACK_ROWS, rows), BF),
    ]

    def latent():
        return call(
            latent_layer,
            (ids, *arrived, own_rows, allowed, w_qkv, w_out, gain_pair, w_ff),
            latent_outs,
            spaces={0: SMEM, 8: pl.ANY},
            scratch=[
                pltpu.VMEM((rows, 3 * D), BF),
                pltpu.VMEM((8, HD, GROUP), BF),
                pltpu.VMEM((rows, D), BF),
                pltpu.VMEM((2, 3, step, D), BF),
                pltpu.VMEM((rows, D), F32),
                pltpu.VMEM((rows, D), F32),
                pltpu.VMEM((rows, 3 * D), BF),
                pltpu.SemaphoreType.DMA((2,)),
            ],
        )

    def turn():
        return nothing(latent_outs[:5]) + call(
            turn_encoder, (pn, o_a, o_b, bn_lo, bn_a, bn_b), latent_outs[5:]
        )

    latents, dhb, latent_gain, norms, lat_grads, packed = lax.cond(second, latent, turn)
    returned = along(dhb, -1)

    packed_far = swap(packed, "core")

    share = units // 16
    ff_block = ((4, 3 * share, HALF), BF)
    ff_half = ((4, 3 * share, GROUP), BF)
    ff_own, ff_right, ff_left, ff_far_a, ff_far_b = on_section(
        second,
        ff_weights_grad,
        (ids, packed, packed_far, norms),
        [ff_block, ff_block, ff_block, ff_half, ff_half],
        spaces={0: SMEM},
    )
    from_left = plane_shift(ff_far_a, 0, 1, (1,))
    from_right = plane_shift(ff_far_b, 0, -1, (1,))

    grads_long = ((2304, HALF), BF)
    enc_grads, enc_other = on_section(
        first,
        encoder_attention_back,
        (ids, returned, w_out, q, k_lo, v_lo, k_a, k_b, v_a, v_b, w_a, w_b),
        [grads_long, grads_long],
        spaces={0: SMEM},
    )
    enc_far = swap(enc_other, "core", (0,))
    outs = [((4, 256, HALF), BF)] * 4
    blocks = lax.cond(
        first,
        lambda: call(encoder_weights, (ids, packed, packed_far, enc_grads, enc_far), outs, spaces={0: SMEM}),
        lambda: call(latent_weights, (ids, packed, packed_far, lat_grads), outs, spaces={0: SMEM}),
    )
    got = exchange(blocks, 0)
    byte_outs = [tall, ((1, D), F32)], [((rows, D), F32), tall, ((2, D), F32)]

    def input_grads():
        upper_part = call(
            encoder_upper_back,
            (ids, up_a, up_b, w_qkv, gain_pair, enc_grads, enc_other, blocks[0]),
            byte_outs[0],
            spaces={0: SMEM, 7: pl.ANY},
        )
        lower_part = call(
            encoder_lower_back,
            (ids, returned, own_rows, lower, w_qkv, gain_pair, enc_grads, enc_other, upper_part[1]),
            byte_outs[1],
            spaces={0: SMEM, 8: pl.ANY},
        )
        return (*upper_part, *lower_part, *nothing([ff_block, ff_block]))

    def ff_middle():
        added = call(
            ff_add, (ff_right, ff_left, from_left, from_right, blocks[0]), [ff_block, ff_block], spaces={4: pl.ANY}
        )
        return (*nothing(byte_outs[0] + byte_outs[1]), *added)

    up_grad, up_gain, patch_grad, low_grad, encoder_gain, ff_right_sum, ff_left_sum = lax.cond(
        first, input_grads, ff_middle
    )
    line = [((272, HALF), BF)]
    blocks = call(
        attn_sum_first_gain,
        (ids, blocks[0], *got, encoder_gain, up_gain, latent_gain),
        line * 4,
        spaces={0: SMEM},
    )
    ff_right_sum, ff_left_sum, up_grad, _ = lax.optimization_barrier((ff_right_sum, ff_left_sum, up_grad, blocks))
    from_left = plane_shift(ff_right_sum, 0, 1, (1,))
    from_right = plane_shift(ff_left_sum, 0, -1, (1,))
    up_arrived = along(up_grad, 1)
    (block,) = call(sum_all, (blocks[0], *exchange(blocks, 1)), line)
    (block,) = call(sum_all, (block, swap(block, "zh")), line)
    (block,) = call(stack_rows, collect(block, 1), [((1040, HALF), BF)])
    from_left, from_right, up_arrived, block = lax.optimization_barrier((from_left, from_right, up_arrived, block))
    ff_line = ((3 * share, HALF), BF)
    ff_blocks = on_section(
        second, ff_sum_first, (ids, ff_own, from_left, from_right), [ff_line] * 4, spaces={0: SMEM}
    )
    ff_got = exchange(ff_blocks, 1, (1,))
    pieces = collect(block, 0)
    (ff_sum,) = on_section(second, ff_sum_second, (ff_blocks[0], *ff_got), [ff_line])
    ff_sum = ff_sum.reshape(3, 2, share // 2, HALF)
    ff_far = swap(pick(ff_sum, 1 - zh, 1), "zh", (1,))
    ff_sum = (pick(ff_sum, zh, 1).astype(F32) + ff_far.astype(F32)).astype(BF).reshape(3, 2, share // 4, HALF)
    ff_mine = pick(ff_sum, core, 1)
    ff_far = swap(pick(ff_sum, 1 - core, 1), "core", (1,))

    def ff_result():
        low, high = jnp.where(core == 0, ff_mine, ff_far), jnp.where(core == 0, ff_far, ff_mine)
        return jnp.swapaxes(jnp.concatenate([low, high], 2), 0, 1).astype(F32)

    ff_grad = lax.cond(second, ff_result, lambda: jnp.zeros((share // 4, 3, D), F32))
    byte_grad = jnp.where(first, low_grad, up_arrived)
    patch_out = jnp.where(first, patch_grad, latents)
    byte_grad, patch_out, ff_grad, *pieces = lax.optimization_barrier((byte_grad, patch_out, ff_grad, *pieces))
    pieces = pieces + [swap(p, "core") for p in pieces]
    whole = lambda p: pl.BlockSpec(p.shape, lambda i, n=p.ndim: (0,) * n)
    total_qkv, total_out, total_gain = pl.pallas_call(
        final_attn,
        grid=(4,),
        out_shape=[
            jax.ShapeDtypeStruct((D, 3 * D), F32),
            jax.ShapeDtypeStruct((D, D), F32),
            jax.ShapeDtypeStruct((2, D), F32),
        ],
        in_specs=[pl.BlockSpec(memory_space=SMEM)] + [whole(p) for p in pieces],
        out_specs=[
            pl.BlockSpec((256, 3 * D), lambda i: (i, 0)),
            pl.BlockSpec((256, D), lambda i: (i, 0)),
            pl.BlockSpec((2, D), lambda i: (0, 0)),
        ],
        compiler_params=pltpu.CompilerParams(vmem_limit_bytes=FINAL_VMEM),
    )(ids, *pieces)
    return (
        patch_out.reshape(1, micro, 1, seq, D),
        byte_grad.reshape(micro, 1, half_bytes, D),
        total_qkv[None],
        total_out[None],
        total_gain[None],
        ff_grad[None],
    )


def solution(mesh):
    fine = Mesh(mesh.devices.reshape(2, 4, 4, 2, 2), ("s",) + BATCH)
    in_specs = (
        P("s", None, BATCH, None, None),
        P(None, BATCH, "s", None),
        P(None, BATCH, None),
        P(None, BATCH, None),
        P("s", None, None),
        P("s", None, None),
        P("s", None, None),
        P(),
    )
    out_specs = (
        P("s", None, BATCH, None, None),
        P(None, BATCH, "s", None),
        P("s", None, None),
        P("s", None, None),
        P("s", None, None),
        P("s", BATCH, None, None),
    )
    return jax.shard_map(shards, mesh=fine, in_specs=in_specs, out_specs=out_specs, check_vma=False)
```

```python
import functools
import math

import jax
import jax.numpy as jnp
from jax import lax
from jax.experimental import pallas as pl
from jax.experimental.pallas import tpu as pltpu
from jax.sharding import Mesh
from jax.sharding import PartitionSpec as P

HD = 64
SCALE = HD**-0.5
EPS = 1e-05
NEG = -1e30
BATCH = ("y", "x", "zh", "core")
BF = jnp.bfloat16
F32 = jnp.float32
D = 1024
HALF = 512
GROUP = 256
FINAL_VMEM = 32 * 1024 * 1024


UNITS = 2816
PACK_NORMS = 3 * UNITS
PACK_LEFT = PACK_NORMS + 4 * 256
PACK_GRADS = PACK_LEFT + 2 * D
PACK_ROWS = PACK_GRADS + 4 * 512


def nn(a, b):
    return lax.dot_general(a, b, (((1,), (0,)), ((), ())), preferred_element_type=F32)


def nt(a, b):
    return lax.dot_general(a, b, (((1,), (1,)), ((), ())), preferred_element_type=F32)


def tn(a, b):
    return lax.dot_general(a, b, (((0,), (0,)), ((), ())), preferred_element_type=F32)


def inverse_rms(x):
    return lax.rsqrt(jnp.mean(x * x, axis=-1, keepdims=True) + EPS)


def norm_back(x, gain, up):
    r = inverse_rms(x)
    scaled = up * gain
    inner = jnp.mean(scaled * x, axis=-1, keepdims=True)
    return r * (scaled - x * (r * r * inner)), up * (x * r)


def stack_heads(rows):
    head = lax.broadcasted_iota(jnp.int32, rows.shape, 1) // HD
    return jnp.concatenate([jnp.where(head == h, rows, jnp.zeros_like(rows)) for h in range(4)], 0)


def unstack_heads(stacked):
    head = lax.broadcasted_iota(jnp.int32, (HD, GROUP), 1) // HD
    out = stacked[0:HD]
    for h in range(1, 4):
        out = jnp.where(head == h, stacked[h * HD : (h + 1) * HD], out)
    return out


def softmax_columns(scores):
    top = functools.reduce(jnp.maximum, [jnp.max(s, axis=0, keepdims=True) for s in scores])
    parts = [jnp.exp(s - top) for s in scores]
    inverse = 1.0 / sum(jnp.sum(p, axis=0, keepdims=True) for p in parts)
    return [(p * inverse).astype(BF) for p in parts]


def encode_lower(patch, low, w_qkv, gains, pn, q, bn, k, v):
    x = patch[...].astype(F32)
    normed = (x * inverse_rms(x) * gains[0:1]).astype(BF)
    pn[...] = normed
    q[...] = nn(normed, w_qkv[:, 0:D]).astype(BF)
    for i in range(2):
        at = pl.ds(i * 256, 256)
        b = low[at, :].astype(F32)
        normed = (b * inverse_rms(b) * gains[1:2]).astype(BF)
        bn[at, :] = normed
        k[at, :] = nn(normed, w_qkv[:, D : 2 * D]).astype(BF)
        v[at, :] = nn(normed, w_qkv[:, 2 * D :]).astype(BF)


def encode_rest(m, patch, up, w_qkv, w_out, gains, bounds, q, k_lo, v_lo, hb, o1, weights, bn, k, v):
    b = up[...].astype(F32)
    normed = (b * inverse_rms(b) * gains[1:2]).astype(BF)
    bn[...] = normed
    k[...] = nn(normed, w_qkv[:, D : 2 * D]).astype(BF)
    v[...] = nn(normed, w_qkv[:, 2 * D :]).astype(BF)
    spot = lax.broadcasted_iota(jnp.int32, (256, GROUP), 0)
    start = bounds[m, 0:1, :]
    end = bounds[m, 1:2, :]
    inside = [(spot + h * 256 >= start) & (spot + h * 256 < end) for h in range(2)]
    low_at = slice(m * 256, (m + 1) * 256)
    rows = slice(m * HD, (m + 1) * HD)
    for g in range(4):
        lanes = slice(g * GROUP, (g + 1) * GROUP)
        stacked = stack_heads(q[rows, lanes] * BF(SCALE))
        scores = [
            jnp.where(inside[h], nt(keys, stacked), NEG)
            for h, keys in enumerate((k_lo[low_at, lanes], k[:, lanes]))
        ]
        w = softmax_columns(scores)
        weights[g * 2] = w[0]
        weights[g * 2 + 1] = w[1]
        mixed = tn(w[0], v_lo[low_at, lanes]) + tn(w[1], v[:, lanes])
        o1[:, lanes] = unstack_heads(mixed).astype(BF)
    hb[...] = (patch[rows, :].astype(F32) + nn(o1[...], w_out[...])).astype(BF)


def latent_layer(
    ids, hb_a, hb_b, cot, allowed, w_qkv, w_out, gains, w_ff,
    latents, dhb, gain_grad, norms, grads, packed,
    qkv, weights, o2, ff_buf, acc_out, acc_norm, dqkv, sems,
):
    core = ids[0]
    units = w_ff.shape[1]
    step = ff_buf.shape[2]
    steps = units // step

    def fetch(i, slot):
        return pltpu.make_async_copy(
            w_ff.at[:, pl.ds(pl.multiple_of(i * step, 128), step), :], ff_buf.at[slot], sems.at[slot]
        )

    fetch(0, 0).start()
    x = jnp.concatenate([hb_a[...], hb_b[...]], 0).astype(F32)
    normed = (x * inverse_rms(x) * gains[0:1]).astype(BF)
    packed[PACK_LEFT : PACK_LEFT + D, :] = normed.T
    qkv[...] = nn(normed, w_qkv[...]).astype(BF)
    for m in range(2):
        rows = slice(m * HD, (m + 1) * HD)
        for g in range(4):
            lanes = slice(g * GROUP, (g + 1) * GROUP)
            k_lanes = slice(D + g * GROUP, D + (g + 1) * GROUP)
            v_lanes = slice(2 * D + g * GROUP, 2 * D + (g + 1) * GROUP)
            stacked = stack_heads(qkv[rows, lanes] * BF(SCALE))
            scores = jnp.where(allowed[m] > 0.5, nt(qkv[rows, k_lanes], stacked), NEG)
            (w,) = softmax_columns([scores])
            weights[m * 4 + g] = w
            o2[rows, lanes] = unstack_heads(tn(w, qkv[rows, v_lanes])).astype(BF)
    packed[PACK_LEFT + D : PACK_LEFT + 2 * D, :] = o2[...].T
    after = x + nn(o2[...], w_out[...])
    yn = (after * inverse_rms(after) * gains[1:2]).astype(BF)
    c = cot[...]
    for h in range(2):

        @pl.when(core == h)
        def _(h=h):
            norms[0:128, :] = yn[:, h * HALF : (h + 1) * HALF]
            norms[128:256, :] = c[:, h * HALF : (h + 1) * HALF]

        @pl.when(core != h)
        def _(h=h):
            for b in range(4):
                lanes = slice(h * HALF + b * 128, h * HALF + (b + 1) * 128)
                packed[PACK_NORMS + b * 256 : PACK_NORMS + b * 256 + 128, :] = yn[:, lanes]
                packed[PACK_NORMS + b * 256 + 128 : PACK_NORMS + (b + 1) * 256, :] = c[:, lanes]

    acc_out[...] = after
    acc_norm[...] = jnp.zeros_like(acc_norm)

    def ff_step(i, carry):
        slot = lax.rem(i, 2)

        @pl.when(i + 1 < steps)
        def _():
            fetch(i + 1, 1 - slot).start()

        fetch(i, slot).wait()
        w_gate, w_up, w_down = ff_buf.at[slot, 0], ff_buf.at[slot, 1], ff_buf.at[slot, 2]
        gate = nt(yn, w_gate[...])
        upward = nt(yn, w_up[...])
        du = nt(c, w_down[...])
        sig = 1.0 / (1.0 + jnp.exp(-gate))
        active = gate * sig
        hidden = (active * upward).astype(BF)
        d_gate = (du * upward * (sig * (1.0 + gate * (1.0 - sig)))).astype(BF)
        d_up = (du * active).astype(BF)
        at = pl.ds(pl.multiple_of(i * step, 128), step)
        for j, value in enumerate((d_gate, d_up, hidden)):
            packed[pl.ds(pl.multiple_of(i * step + j * units, 128), step), :] = value.T
        acc_out[...] += nn(hidden, w_down[...])
        acc_norm[...] += nn(d_gate, w_gate[...]) + nn(d_up, w_up[...])
        return carry

    lax.fori_loop(0, steps, ff_step, 0)
    latents[...] = acc_out[...]
    back, gain_rows = norm_back(after, gains[1:2], acc_norm[...])
    gain_grad[1:2, :] = jnp.sum(gain_rows, axis=0, keepdims=True)
    d_after = c.astype(F32) + back
    da = d_after.astype(BF)
    d_mixed = nt(da, w_out[...]).astype(BF)
    for m in range(2):
        rows = slice(m * HD, (m + 1) * HD)
        for g in range(4):
            lanes = slice(g * GROUP, (g + 1) * GROUP)
            k_lanes = slice(D + g * GROUP, D + (g + 1) * GROUP)
            v_lanes = slice(2 * D + g * GROUP, 2 * D + (g + 1) * GROUP)
            q_stacked = stack_heads(qkv[rows, lanes] * BF(SCALE))
            o_stacked = stack_heads(d_mixed[rows, lanes])
            w_low = weights[m * 4 + g]
            w = w_low.astype(F32)
            dw = nt(qkv[rows, v_lanes], o_stacked)
            inner = jnp.sum(dw * w, axis=0, keepdims=True)
            ds = (w * (dw - inner)).astype(BF)
            dqkv[rows, lanes] = (unstack_heads(tn(ds, qkv[rows, k_lanes])) * SCALE).astype(BF)
            dqkv[rows, k_lanes] = nn(ds, q_stacked).astype(BF)
            dqkv[rows, v_lanes] = nn(w_low, o_stacked).astype(BF)
    d_normed = nt(dqkv[...], w_qkv[...])
    back, gain_rows = norm_back(x, gains[0:1], d_normed)
    gain_grad[0:1, :] = jnp.sum(gain_rows, axis=0, keepdims=True)
    dhb[...] = (d_after + back).astype(BF)
    for h in range(2):
        pieces = (
            dqkv[:, h * HALF : (h + 1) * HALF],
            da[:, h * HALF : (h + 1) * HALF],
            dqkv[:, D + h * HALF : D + (h + 1) * HALF],
            dqkv[:, 2 * D + h * HALF : 2 * D + (h + 1) * HALF],
        )

        @pl.when(core == h)
        def _(pieces=pieces):
            for i, value in enumerate(pieces):
                grads[i * 128 : (i + 1) * 128, :] = value

        @pl.when(core != h)
        def _(pieces=pieces):
            for i, value in enumerate(pieces):
                for b in range(4):
                    first = PACK_GRADS + b * 512 + i * 128
                    packed[first : first + 128, :] = value[:, b * 128 : (b + 1) * 128]


def half_of(core, g, mine, other):
    lanes = slice((g % 2) * GROUP, (g % 2 + 1) * GROUP)

    def put(at, value):
        @pl.when(core == g // 2)
        def _():
            mine[at, lanes] = value

        @pl.when(core != g // 2)
        def _():
            other[at, lanes] = value

    return put


def encoder_attention_back(
    ids, dhb, w_out, q, k_lo, v_lo, k_a, k_b, v_a, v_b, w_a, w_b, mine, other
):
    d_mixed = nt(dhb[...], w_out[...]).astype(BF)
    for g in range(4):
        lanes = slice(g * GROUP, (g + 1) * GROUP)
        put = half_of(ids[0], g, mine, other)
        put(slice(128, 256), dhb[:, lanes])
        for m, (k_up, v_up, weights) in enumerate(((k_a, v_a, w_a), (k_b, v_b, w_b))):
            rows = slice(m * HD, (m + 1) * HD)
            low_at = slice(m * 256, (m + 1) * 256)
            q_stacked = stack_heads(q[rows, lanes] * BF(SCALE))
            o_stacked = stack_heads(d_mixed[rows, lanes])
            low = [weights[g * 2 + h] for h in range(2)]
            w = [piece.astype(F32) for piece in low]
            dw = [nt(values, o_stacked) for values in (v_lo[low_at, lanes], v_up[:, lanes])]
            inner = sum(jnp.sum(a * b, axis=0, keepdims=True) for a, b in zip(dw, w))
            ds = [(b * (a - inner)).astype(BF) for a, b in zip(dw, w)]
            dq = tn(ds[0], k_lo[low_at, lanes]) + tn(ds[1], k_up[:, lanes])
            put(rows, (unstack_heads(dq) * SCALE).astype(BF))
            for h in range(2):
                base = h * HALF + m * 256
                put(slice(256 + base, 512 + base), nn(ds[h], q_stacked).astype(BF))
                put(slice(1280 + base, 1536 + base), nn(low[h], o_stacked).astype(BF))


def both_columns(core, block, w_qkv):
    return [
        w_qkv[:, pl.ds(pl.multiple_of(block * D + which * HALF, HALF), HALF)] for which in (core, 1 - core)
    ]


def bytes_back(core, h, m, source, w_qkv, gains, grads):
    d_norm = sum(
        nt(ref[1024 * block - 768 + h * HALF + m * 256 : 1024 * block - 512 + h * HALF + m * 256, :], columns)
        for block in (1, 2)
        for ref, columns in zip(grads, both_columns(core, block, w_qkv))
    )
    back, gain_rows = norm_back(source.astype(F32), gains[1:2], d_norm)
    return back.astype(BF), jnp.sum(gain_rows, axis=0, keepdims=True)


def encoder_upper_back(ids, up_a, up_b, w_qkv, gains, mine, other, after, up_grad, gain_grad):
    total = jnp.zeros((1, D), F32)
    for m, source in enumerate((up_a, up_b)):
        back, rows = bytes_back(ids[0], 1, m, source[...], w_qkv, gains, (mine, other))
        up_grad[m * 256 : (m + 1) * 256, :] = back
        total = total + rows
    gain_grad[...] = total


def encoder_lower_back(
    ids, dhb, patch, low, w_qkv, gains, mine, other, after, patch_grad, low_grad, gain_grad
):
    core = ids[0]
    up_norm = sum(nt(ref[0:128, :], columns) for ref, columns in zip((mine, other), both_columns(core, 0, w_qkv)))
    back, gain_rows = norm_back(patch[...].astype(F32), gains[0:1], up_norm)
    gain_grad[0:1, :] = jnp.sum(gain_rows, axis=0, keepdims=True)
    patch_grad[...] = dhb[...].astype(F32) + back
    total = jnp.zeros((1, D), F32)
    for m in range(2):
        at = slice(m * 256, (m + 1) * 256)
        back, rows = bytes_back(core, 0, m, low[at, :], w_qkv, gains, (mine, other))
        low_grad[at, :] = back
        total = total + rows
    gain_grad[1:2, :] = total


def turn_encoder(pn, o_a, o_b, bn_lo, bn_a, bn_b, packed):
    for b, rows in enumerate([bn_lo[i * 128 : (i + 1) * 128, :] for i in range(4)]
                             + [ref[i * 128 : (i + 1) * 128, :] for ref in (bn_a, bn_b) for i in range(2)]):
        packed[b * D : (b + 1) * D, :] = rows.T
    packed[PACK_LEFT : PACK_LEFT + D, :] = pn[...].T
    packed[PACK_LEFT + D : PACK_LEFT + 2 * D, :] = jnp.concatenate([o_a[...], o_b[...]], 0).T


def rows_of_both(left, left_far, at):
    return jnp.concatenate([left[at, :], left_far[at, :]], 1)


def below(near, far, rows):
    return jnp.concatenate([near[rows, :], far[rows, :]], 0)


def encoder_weights(ids, packed, packed_far, near, far, *blocks):
    u = ids[1]
    queries = below(near, far, slice(0, 128))
    outputs = below(near, far, slice(128, 256))
    for k in range(4):
        first = lax.rem(u + k, 4) * 256

        def at(base, first=first):
            return pl.ds(pl.multiple_of(first + base, 256), 256)

        blocks[k][0] = nn(rows_of_both(packed, packed_far, at(PACK_LEFT)), queries).astype(BF)
        blocks[k][3] = nn(rows_of_both(packed, packed_far, at(PACK_LEFT + D)), outputs).astype(BF)
        lefts = [jnp.concatenate([ref[at(b * D), :] for b in range(8)], 1) for ref in (packed, packed_far)]
        for block in (1, 2):
            rows = slice(1024 * block - 768, 1024 * block + 256)
            blocks[k][block] = (nn(lefts[0], near[rows, :]) + nn(lefts[1], far[rows, :])).astype(BF)


def unpack(packed, first, rows):
    return jnp.concatenate([packed[first + b * rows : first + (b + 1) * rows, :] for b in range(4)], 1)


def latent_weights(ids, packed, packed_far, near, *blocks):
    u = ids[1]
    far = unpack(packed_far, PACK_GRADS, 512)
    rights = [jnp.concatenate([near[i * 128 : (i + 1) * 128, :], far[i * 128 : (i + 1) * 128, :]], 0) for i in range(4)]
    for k in range(4):
        first = PACK_LEFT + lax.rem(u + k, 4) * 256
        at = pl.ds(pl.multiple_of(first, 256), 256)
        low_at = pl.ds(pl.multiple_of(first + D, 256), 256)
        for block, (source, i) in enumerate(((at, 0), (at, 2), (at, 3), (low_at, 1))):
            blocks[k][block] = nn(rows_of_both(packed, packed_far, source), rights[i]).astype(BF)


def ff_weights_grad(ids, packed, packed_far, norms, own, right, left, far_a, far_b):
    core, u = ids[0], ids[1]
    share = UNITS // 16
    far = unpack(packed_far, PACK_NORMS, 256)
    normed = jnp.concatenate([norms[0:128, :], far[0:128, :]], 0)
    cot = jnp.concatenate([norms[128:256, :], far[128:256, :]], 0)
    for k in range(4):
        there = lax.rem(u + k, 4)
        for v in range(4):
            chunk = jnp.where(core == 0, there * 4 + v, v * 4 + there)
            for j in range(3):
                at = pl.ds(pl.multiple_of(j * UNITS + chunk * share, 16), share)
                value = nn(rows_of_both(packed, packed_far, at), normed if j < 2 else cot).astype(BF)
                rows = slice(j * share, (j + 1) * share)
                if k == 2:
                    far_a[v, rows, :] = value[:, :GROUP]
                    far_b[v, rows, :] = value[:, GROUP:]
                else:
                    (own, right, None, left)[k][v, rows, :] = value


def ff_add(right, left, from_left, from_right, after, new_right, new_left):
    new_right[:, :, 0:GROUP] = (right[:, :, 0:GROUP].astype(F32) + from_left[...].astype(F32)).astype(BF)
    new_right[:, :, GROUP:] = right[:, :, GROUP:]
    new_left[:, :, 0:GROUP] = left[:, :, 0:GROUP]
    new_left[:, :, GROUP:] = (left[:, :, GROUP:].astype(F32) + from_right[...].astype(F32)).astype(BF)


def sum_four(own, a, b, c):
    return own.astype(F32) + a.astype(F32) + b.astype(F32) + c.astype(F32)


def pack_gain(value):
    high = value.astype(BF)
    low = (value - high.astype(F32)).astype(BF)
    return jnp.concatenate(
        [high.astype(F32), low.astype(F32), jnp.zeros((8, HALF), F32)], 0
    ).astype(BF)


def unpack_gain(rows):
    rows = rows.astype(F32)
    return rows[0:4] + rows[4:8]


GAIN_AT = slice(256, 272)


def attn_sum_first(ids, own, a, b, c, *outs):
    v = ids[2]
    for k in range(4):
        at = pl.ds(pl.multiple_of(lax.rem(v + k, 4) * HD, HD), HD)
        for block in range(4):
            outs[k][block * HD : (block + 1) * HD, :] = sum_four(
                own[block, at, :], a[block, at, :], b[block, at, :], c[block, at, :]
            ).astype(BF)


def attn_sum_first_gain(ids, own, a, b, c, enc_gain, up_gain, lat_gain, *outs):
    attn_sum_first(ids, own, a, b, c, *outs)
    first = ids[4] == 0
    gain = jnp.where(
        first, jnp.concatenate([enc_gain[0:1, :], enc_gain[1:2, :] + up_gain[...]], 0), lat_gain[...]
    )
    halves = [gain[i : i + 1, h * HALF : (h + 1) * HALF] for i in range(2) for h in range(2)]
    packed = pack_gain(jnp.concatenate(halves, 0))
    for out in outs:
        out[GAIN_AT, :] = packed


def sum_all(*refs):
    refs, out = refs[:-1], refs[-1]
    out[0:256, :] = sum(ref[0:256, :].astype(F32) for ref in refs).astype(BF)
    out[GAIN_AT, :] = pack_gain(sum(unpack_gain(ref[GAIN_AT, :]) for ref in refs))


def stack_rows(*refs):
    refs, out = refs[:-1], refs[-1]
    for j, ref in enumerate(refs):
        out[j * 256 : (j + 1) * 256, :] = ref[0:256, :]
    out[1024:1040, :] = refs[0][GAIN_AT, :]


def ff_sum_first(ids, own, a, b, *outs):
    v = ids[2]
    for k in range(4):
        at = lax.rem(v + k, 4)
        outs[k][...] = (own[at].astype(F32) + a[at].astype(F32) + b[at].astype(F32)).astype(BF)


def ff_sum_second(own, a, b, c, out):
    out[...] = sum_four(own[...], a[...], b[...], c[...]).astype(BF)


def final_attn(ids, *refs):
    pieces, (qkv, out, gain) = refs[:8], refs[8:]
    step = pl.program_id(0)
    for side in range(2):
        core = ids[0] if side == 0 else 1 - ids[0]
        u = ids[1] if side == 0 else ids[2]
        v = ids[2] if side == 0 else ids[1]
        for k in range(4):
            piece = pieces[side * 4 + k]

            @pl.when(lax.rem(u + k, 4) == step)
            def _(piece=piece, v=v, core=core):
                for j in range(4):
                    at = pl.ds(pl.multiple_of(lax.rem(v + j, 4) * HD, HD), HD)
                    for block in range(4):
                        target, column = (qkv, block * D) if block < 3 else (out, 0)
                        lanes = pl.ds(pl.multiple_of(core * HALF + column, HALF), HALF)
                        first = j * 256 + block * HD
                        target[at, lanes] = piece[first : first + HD, :].astype(F32)

    mine = sum(unpack_gain(piece[1024:1040, :]) for piece in pieces[:4])
    other = sum(unpack_gain(piece[1024:1040, :]) for piece in pieces[4:])
    total = mine + other
    for i in range(2):
        for h in range(2):
            gain[i : i + 1, h * HALF : (h + 1) * HALF] = total[2 * i + h : 2 * i + h + 1, :]


SMEM = pltpu.MemorySpace.SMEM
VMEM = pltpu.MemorySpace.VMEM


def size(shape, dtype):
    return math.prod(shape) * jnp.dtype(dtype).itemsize


def call(kernel, args, outs, scratch=(), spaces=None, spare=6):
    spaces = spaces or {}
    vmem = sum(size(a.shape, a.dtype) for i, a in enumerate(args) if i not in spaces)
    vmem += sum(size(*o) for o in outs)
    vmem += sum(size(s.shape, s.dtype) for s in scratch if hasattr(s, "shape") and s.memory_space == VMEM)
    specs = [pl.BlockSpec(memory_space=spaces.get(i, VMEM)) for i in range(len(args))]
    return pl.pallas_call(
        kernel,
        out_shape=[jax.ShapeDtypeStruct(s, t) for s, t in outs],
        in_specs=specs,
        out_specs=[pl.BlockSpec(memory_space=VMEM) for _ in outs],
        scratch_shapes=list(scratch),
        compiler_params=pltpu.CompilerParams(vmem_limit_bytes=vmem + spare * 1024 * 1024),
    )(*args)


def nothing(outs):
    def kernel(*refs):
        pass

    return pl.pallas_call(
        kernel,
        out_shape=[jax.ShapeDtypeStruct(s, t) for s, t in outs],
        out_specs=[pl.BlockSpec(memory_space=pl.ANY) for _ in outs],
    )()


def on_section(flag, kernel, args, outs, **rest):
    return lax.cond(
        flag, lambda: call(kernel, args, outs, **rest), lambda: nothing(outs)
    )


def along(value, by):
    return lax.ppermute(value, "s", [(0, 1)] if by > 0 else [(1, 0)])


def swap(value, axis, sections=(0, 1)):
    pairs = [(s * 2 + i, s * 2 + 1 - i) for s in sections for i in range(2)]
    return lax.ppermute(value, ("s", axis), pairs)


def plane_shift(value, which, by, sections=(0, 1)):
    pairs = []
    for s in sections:
        for y in range(4):
            for x in range(4):
                for core in range(2):
                    ty, tx = ((y + by) % 4, x) if core == which else (y, (x + by) % 4)
                    pairs.append((((s * 4 + y) * 4 + x) * 2 + core, ((s * 4 + ty) * 4 + tx) * 2 + core))
    return lax.ppermute(value, ("s", "y", "x", "core"), pairs)


def exchange(blocks, which, sections=(0, 1)):
    return [plane_shift(blocks[k], which, k, sections) for k in (1, 2, 3)]


def collect(block, which):
    return [block] + [plane_shift(block, which, -k) for k in (1, 2, 3)]


def pick(stack, index, dim):
    return lax.dynamic_index_in_dim(stack, index, dim, keepdims=False)


def shards(patch_io, byte_states, patch_lengths, patch_live, attn_qkv, attn_out, gains, ff_weights):
    section = lax.axis_index("s")
    core = lax.axis_index("core")
    zh = lax.axis_index("zh")
    y, x = lax.axis_index("y"), lax.axis_index("x")
    first = section == 0
    second = section == 1
    ids = jnp.stack([core, jnp.where(core == 0, y, x), jnp.where(core == 0, x, y), zh, section])
    ids = ids.astype(jnp.int32)
    w_qkv = attn_qkv[0]
    w_out = attn_out[0]
    gain_pair = gains[0]
    micro, seq = patch_io.shape[1], patch_io.shape[3]
    half_bytes = byte_states.shape[2]
    units = ff_weights.shape[0]
    rows = micro * seq
    own_rows = patch_io.reshape(rows, D)
    up_a = along(byte_states[0, 0], -1)
    up_b = along(byte_states[1, 0], -1)
    lower = byte_states.reshape(micro * half_bytes, D)
    w_ff = jnp.swapaxes(ff_weights, 0, 1)
    lengths = patch_lengths[:, 0]
    live = patch_live[:, 0]
    ends = jnp.cumsum(lengths, axis=1)
    bounds = jnp.tile(jnp.stack([ends - lengths, ends], 1), (1, 1, 4))
    places = lax.iota(jnp.int32, seq)
    causal = places[:, None] <= places[None, :]
    diagonal = places[:, None] == places[None, :]
    allowed = causal[None] & ((live[:, :, None] == 1) | diagonal[None])
    allowed = lax.optimization_barrier(jnp.tile(allowed.astype(F32), (1, 1, 4)))

    wide = ((rows, D), BF)
    short = ((seq, D), BF)
    tall = ((micro * half_bytes, D), BF)
    piece = ((half_bytes, D), BF)
    pn, q, bn_lo, k_lo, v_lo = on_section(
        first, encode_lower, (own_rows, lower, w_qkv, gain_pair), [wide, wide, tall, tall, tall]
    )
    rest = []
    for m, up in enumerate((up_a, up_b)):
        rest.append(
            on_section(
                first,
                functools.partial(encode_rest, m),
                (own_rows, up, w_qkv, w_out, gain_pair, bounds, q, k_lo, v_lo),
                [short, short, ((8, 256, GROUP), BF), piece, piece, piece],
            )
        )
    (hb_a, o_a, w_a, bn_a, k_a, v_a), (hb_b, o_b, w_b, bn_b, k_b, v_b) = rest
    arrived = [along(hb_a, 1), along(hb_b, 1)]

    step = 256
    latent_outs = [
        ((rows, D), F32), wide, ((2, D), F32), ((256, HALF), BF), ((512, HALF), BF), ((PACK_ROWS, rows), BF),
    ]

    def latent():
        return call(
            latent_layer,
            (ids, *arrived, own_rows, allowed, w_qkv, w_out, gain_pair, w_ff),
            latent_outs,
            spaces={0: SMEM, 8: pl.ANY},
            scratch=[
                pltpu.VMEM((rows, 3 * D), BF),
                pltpu.VMEM((8, HD, GROUP), BF),
                pltpu.VMEM((rows, D), BF),
                pltpu.VMEM((2, 3, step, D), BF),
                pltpu.VMEM((rows, D), F32),
                pltpu.VMEM((rows, D), F32),
                pltpu.VMEM((rows, 3 * D), BF),
                pltpu.SemaphoreType.DMA((2,)),
            ],
        )

    def turn():
        return nothing(latent_outs[:5]) + call(
            turn_encoder, (pn, o_a, o_b, bn_lo, bn_a, bn_b), latent_outs[5:]
        )

    latents, dhb, latent_gain, norms, lat_grads, packed = lax.cond(second, latent, turn)
    returned = along(dhb, -1)

    packed_far = swap(packed, "core")

    share = units // 16
    ff_block = ((4, 3 * share, HALF), BF)
    ff_half = ((4, 3 * share, GROUP), BF)
    ff_own, ff_right, ff_left, ff_far_a, ff_far_b = on_section(
        second,
        ff_weights_grad,
        (ids, packed, packed_far, norms),
        [ff_block, ff_block, ff_block, ff_half, ff_half],
        spaces={0: SMEM},
    )
    from_left = plane_shift(ff_far_a, 0, 1, (1,))
    from_right = plane_shift(ff_far_b, 0, -1, (1,))

    grads_long = ((2304, HALF), BF)
    enc_grads, enc_other = on_section(
        first,
        encoder_attention_back,
        (ids, returned, w_out, q, k_lo, v_lo, k_a, k_b, v_a, v_b, w_a, w_b),
        [grads_long, grads_long],
        spaces={0: SMEM},
    )
    enc_far = swap(enc_other, "core", (0,))
    outs = [((4, 256, HALF), BF)] * 4
    blocks = lax.cond(
        first,
        lambda: call(encoder_weights, (ids, packed, packed_far, enc_grads, enc_far), outs, spaces={0: SMEM}),
        lambda: call(latent_weights, (ids, packed, packed_far, lat_grads), outs, spaces={0: SMEM}),
    )
    got = exchange(blocks, 0)
    byte_outs = [tall, ((1, D), F32)], [((rows, D), F32), tall, ((2, D), F32)]

    def input_grads():
        upper_part = call(
            encoder_upper_back,
            (ids, up_a, up_b, w_qkv, gain_pair, enc_grads, enc_other, blocks[0]),
            byte_outs[0],
            spaces={0: SMEM, 7: pl.ANY},
        )
        lower_part = call(
            encoder_lower_back,
            (ids, returned, own_rows, lower, w_qkv, gain_pair, enc_grads, enc_other, upper_part[1]),
            byte_outs[1],
            spaces={0: SMEM, 8: pl.ANY},
        )
        return (*upper_part, *lower_part, *nothing([ff_block, ff_block]))

    def ff_middle():
        added = call(
            ff_add, (ff_right, ff_left, from_left, from_right, blocks[0]), [ff_block, ff_block], spaces={4: pl.ANY}
        )
        return (*nothing(byte_outs[0] + byte_outs[1]), *added)

    up_grad, up_gain, patch_grad, low_grad, encoder_gain, ff_right_sum, ff_left_sum = lax.cond(
        first, input_grads, ff_middle
    )
    line = [((272, HALF), BF)]
    blocks = call(
        attn_sum_first_gain,
        (ids, blocks[0], *got, encoder_gain, up_gain, latent_gain),
        line * 4,
        spaces={0: SMEM},
    )
    ff_right_sum, ff_left_sum, _ = lax.optimization_barrier((ff_right_sum, ff_left_sum, blocks))
    from_left = plane_shift(ff_right_sum, 0, 1, (1,))
    from_right = plane_shift(ff_left_sum, 0, -1, (1,))
    (block,) = call(sum_all, (blocks[0], *exchange(blocks, 1)), line)
    from_left, from_right, block = lax.optimization_barrier((from_left, from_right, block))
    ff_line = ((3 * share, HALF), BF)
    ff_blocks = on_section(
        second, ff_sum_first, (ids, ff_own, from_left, from_right), [ff_line] * 4, spaces={0: SMEM}
    )
    ff_got = exchange(ff_blocks, 1, (1,))
    across, ff_got = lax.optimization_barrier((swap(block, "zh"), ff_got))
    (block,) = call(sum_all, (block, across), line)
    up_grad, block = lax.optimization_barrier((up_grad, block))
    up_arrived = along(up_grad, 1)
    (block,) = call(stack_rows, collect(block, 1), [((1040, HALF), BF)])
    pieces = collect(block, 0)
    (ff_sum,) = on_section(second, ff_sum_second, (ff_blocks[0], *ff_got), [ff_line])
    ff_sum = ff_sum.reshape(3, 2, share // 2, HALF)
    ff_far = swap(pick(ff_sum, 1 - zh, 1), "zh", (1,))
    ff_sum = (pick(ff_sum, zh, 1).astype(F32) + ff_far.astype(F32)).astype(BF).reshape(3, 2, share // 4, HALF)
    ff_mine = pick(ff_sum, core, 1)
    ff_far = swap(pick(ff_sum, 1 - core, 1), "core", (1,))

    def ff_result():
        low, high = jnp.where(core == 0, ff_mine, ff_far), jnp.where(core == 0, ff_far, ff_mine)
        return jnp.swapaxes(jnp.concatenate([low, high], 2), 0, 1).astype(F32)

    ff_grad = lax.cond(second, ff_result, lambda: jnp.zeros((share // 4, 3, D), F32))
    byte_grad = jnp.where(first, low_grad, up_arrived)
    patch_out = jnp.where(first, patch_grad, latents)
    own_far = swap(pieces[0], "core")
    patch_out, ff_grad, *pieces = lax.optimization_barrier((patch_out, ff_grad, *pieces))
    pieces = pieces + [own_far] + [swap(p, "core") for p in pieces[1:]]
    whole = lambda p: pl.BlockSpec(p.shape, lambda i, n=p.ndim: (0,) * n)
    total_qkv, total_out, total_gain = pl.pallas_call(
        final_attn,
        grid=(4,),
        out_shape=[
            jax.ShapeDtypeStruct((D, 3 * D), F32),
            jax.ShapeDtypeStruct((D, D), F32),
            jax.ShapeDtypeStruct((2, D), F32),
        ],
        in_specs=[pl.BlockSpec(memory_space=SMEM)] + [whole(p) for p in pieces],
        out_specs=[
            pl.BlockSpec((256, 3 * D), lambda i: (i, 0)),
            pl.BlockSpec((256, D), lambda i: (i, 0)),
            pl.BlockSpec((2, D), lambda i: (0, 0)),
        ],
        compiler_params=pltpu.CompilerParams(vmem_limit_bytes=FINAL_VMEM),
    )(ids, *pieces)
    return (
        patch_out.reshape(1, micro, 1, seq, D),
        byte_grad.reshape(micro, 1, half_bytes, D),
        total_qkv[None],
        total_out[None],
        total_gain[None],
        ff_grad[None],
    )


def solution(mesh):
    fine = Mesh(mesh.devices.reshape(2, 4, 4, 2, 2), ("s",) + BATCH)
    in_specs = (
        P("s", None, BATCH, None, None),
        P(None, BATCH, "s", None),
        P(None, BATCH, None),
        P(None, BATCH, None),
        P("s", None, None),
        P("s", None, None),
        P("s", None, None),
        P(),
    )
    out_specs = (
        P("s", None, BATCH, None, None),
        P(None, BATCH, "s", None),
        P("s", None, None),
        P("s", None, None),
        P("s", None, None),
        P("s", BATCH, None, None),
    )
    return jax.shard_map(shards, mesh=fine, in_specs=in_specs, out_specs=out_specs, check_vma=False)
```

```python
import functools
import math

import jax
import jax.numpy as jnp
from jax import lax
from jax.experimental import pallas as pl
from jax.experimental.pallas import tpu as pltpu
from jax.sharding import Mesh
from jax.sharding import PartitionSpec as P

HD = 64
SCALE = HD**-0.5
EPS = 1e-05
NEG = -1e30
BATCH = ("y", "x", "zh", "core")
BF = jnp.bfloat16
F32 = jnp.float32
D = 1024
HALF = 512
GROUP = 256
FINAL_VMEM = 32 * 1024 * 1024


UNITS = 2816
PACK_NORMS = 3 * UNITS
PACK_LEFT = PACK_NORMS + 4 * 256
PACK_GRADS = PACK_LEFT + 2 * D
PACK_ROWS = PACK_GRADS + 4 * 512
WINDOW = 96
WINDOW_STEP = 80
ACROSS_NORMS = 48 * WINDOW
ACROSS_ROWS = ACROSS_NORMS + 8 * 256


def nn(a, b):
    return lax.dot_general(a, b, (((1,), (0,)), ((), ())), preferred_element_type=F32)


def nt(a, b):
    return lax.dot_general(a, b, (((1,), (1,)), ((), ())), preferred_element_type=F32)


def tn(a, b):
    return lax.dot_general(a, b, (((0,), (0,)), ((), ())), preferred_element_type=F32)


def inverse_rms(x):
    return lax.rsqrt(jnp.mean(x * x, axis=-1, keepdims=True) + EPS)


def norm_back(x, gain, up):
    r = inverse_rms(x)
    scaled = up * gain
    inner = jnp.mean(scaled * x, axis=-1, keepdims=True)
    return r * (scaled - x * (r * r * inner)), up * (x * r)


def stack_heads(rows):
    head = lax.broadcasted_iota(jnp.int32, rows.shape, 1) // HD
    return jnp.concatenate([jnp.where(head == h, rows, jnp.zeros_like(rows)) for h in range(4)], 0)


def unstack_heads(stacked):
    head = lax.broadcasted_iota(jnp.int32, (HD, GROUP), 1) // HD
    out = stacked[0:HD]
    for h in range(1, 4):
        out = jnp.where(head == h, stacked[h * HD : (h + 1) * HD], out)
    return out


def softmax_columns(scores):
    top = functools.reduce(jnp.maximum, [jnp.max(s, axis=0, keepdims=True) for s in scores])
    parts = [jnp.exp(s - top) for s in scores]
    inverse = 1.0 / sum(jnp.sum(p, axis=0, keepdims=True) for p in parts)
    return [(p * inverse).astype(BF) for p in parts]


def encode_lower(patch, low, w_qkv, gains, pn, q, bn, k, v):
    x = patch[...].astype(F32)
    normed = (x * inverse_rms(x) * gains[0:1]).astype(BF)
    pn[...] = normed
    q[...] = nn(normed, w_qkv[:, 0:D]).astype(BF)
    for i in range(2):
        at = pl.ds(i * 256, 256)
        b = low[at, :].astype(F32)
        normed = (b * inverse_rms(b) * gains[1:2]).astype(BF)
        bn[at, :] = normed
        k[at, :] = nn(normed, w_qkv[:, D : 2 * D]).astype(BF)
        v[at, :] = nn(normed, w_qkv[:, 2 * D :]).astype(BF)


def encode_rest(m, patch, up, w_qkv, w_out, gains, bounds, q, k_lo, v_lo, hb, o1, weights, bn, k, v):
    b = up[...].astype(F32)
    normed = (b * inverse_rms(b) * gains[1:2]).astype(BF)
    bn[...] = normed
    k[...] = nn(normed, w_qkv[:, D : 2 * D]).astype(BF)
    v[...] = nn(normed, w_qkv[:, 2 * D :]).astype(BF)
    spot = lax.broadcasted_iota(jnp.int32, (256, GROUP), 0)
    start = bounds[m, 0:1, :]
    end = bounds[m, 1:2, :]
    inside = [(spot + h * 256 >= start) & (spot + h * 256 < end) for h in range(2)]
    low_at = slice(m * 256, (m + 1) * 256)
    rows = slice(m * HD, (m + 1) * HD)
    for g in range(4):
        lanes = slice(g * GROUP, (g + 1) * GROUP)
        stacked = stack_heads(q[rows, lanes] * BF(SCALE))
        scores = [
            jnp.where(inside[h], nt(keys, stacked), NEG)
            for h, keys in enumerate((k_lo[low_at, lanes], k[:, lanes]))
        ]
        w = softmax_columns(scores)
        weights[g * 2] = w[0]
        weights[g * 2 + 1] = w[1]
        mixed = tn(w[0], v_lo[low_at, lanes]) + tn(w[1], v[:, lanes])
        o1[:, lanes] = unstack_heads(mixed).astype(BF)
    hb[...] = (patch[rows, :].astype(F32) + nn(o1[...], w_out[...])).astype(BF)


def latent_layer(
    ids, hb_a, hb_b, cot, allowed, w_qkv, w_out, gains, w_ff,
    latents, dhb, gain_grad, norms, grads, packed,
    qkv, weights, o2, ff_buf, acc_out, acc_norm, dqkv, sems,
):
    core = ids[0]
    units = w_ff.shape[1]
    step = ff_buf.shape[2]
    steps = units // step

    def fetch(i, slot):
        return pltpu.make_async_copy(
            w_ff.at[:, pl.ds(pl.multiple_of(i * step, 128), step), :], ff_buf.at[slot], sems.at[slot]
        )

    fetch(0, 0).start()
    x = jnp.concatenate([hb_a[...], hb_b[...]], 0).astype(F32)
    normed = (x * inverse_rms(x) * gains[0:1]).astype(BF)
    packed[PACK_LEFT : PACK_LEFT + D, :] = normed.T
    qkv[...] = nn(normed, w_qkv[...]).astype(BF)
    for m in range(2):
        rows = slice(m * HD, (m + 1) * HD)
        for g in range(4):
            lanes = slice(g * GROUP, (g + 1) * GROUP)
            k_lanes = slice(D + g * GROUP, D + (g + 1) * GROUP)
            v_lanes = slice(2 * D + g * GROUP, 2 * D + (g + 1) * GROUP)
            stacked = stack_heads(qkv[rows, lanes] * BF(SCALE))
            scores = jnp.where(allowed[m] > 0.5, nt(qkv[rows, k_lanes], stacked), NEG)
            (w,) = softmax_columns([scores])
            weights[m * 4 + g] = w
            o2[rows, lanes] = unstack_heads(tn(w, qkv[rows, v_lanes])).astype(BF)
    packed[PACK_LEFT + D : PACK_LEFT + 2 * D, :] = o2[...].T
    after = x + nn(o2[...], w_out[...])
    yn = (after * inverse_rms(after) * gains[1:2]).astype(BF)
    c = cot[...]
    for h in range(2):

        @pl.when(core == h)
        def _(h=h):
            norms[0:128, :] = yn[:, h * HALF : (h + 1) * HALF]
            norms[128:256, :] = c[:, h * HALF : (h + 1) * HALF]

        @pl.when(core != h)
        def _(h=h):
            for b in range(4):
                lanes = slice(h * HALF + b * 128, h * HALF + (b + 1) * 128)
                packed[PACK_NORMS + b * 256 : PACK_NORMS + b * 256 + 128, :] = yn[:, lanes]
                packed[PACK_NORMS + b * 256 + 128 : PACK_NORMS + (b + 1) * 256, :] = c[:, lanes]

    acc_out[...] = after
    acc_norm[...] = jnp.zeros_like(acc_norm)

    def ff_step(i, carry):
        slot = lax.rem(i, 2)

        @pl.when(i + 1 < steps)
        def _():
            fetch(i + 1, 1 - slot).start()

        fetch(i, slot).wait()
        w_gate, w_up, w_down = ff_buf.at[slot, 0], ff_buf.at[slot, 1], ff_buf.at[slot, 2]
        gate = nt(yn, w_gate[...])
        upward = nt(yn, w_up[...])
        du = nt(c, w_down[...])
        sig = 1.0 / (1.0 + jnp.exp(-gate))
        active = gate * sig
        hidden = (active * upward).astype(BF)
        d_gate = (du * upward * (sig * (1.0 + gate * (1.0 - sig)))).astype(BF)
        d_up = (du * active).astype(BF)
        at = pl.ds(pl.multiple_of(i * step, 128), step)
        for j, value in enumerate((d_gate, d_up, hidden)):
            packed[pl.ds(pl.multiple_of(i * step + j * units, 128), step), :] = value.T
        acc_out[...] += nn(hidden, w_down[...])
        acc_norm[...] += nn(d_gate, w_gate[...]) + nn(d_up, w_up[...])
        return carry

    lax.fori_loop(0, steps, ff_step, 0)
    latents[...] = acc_out[...]
    back, gain_rows = norm_back(after, gains[1:2], acc_norm[...])
    gain_grad[1:2, :] = jnp.sum(gain_rows, axis=0, keepdims=True)
    d_after = c.astype(F32) + back
    da = d_after.astype(BF)
    d_mixed = nt(da, w_out[...]).astype(BF)
    for m in range(2):
        rows = slice(m * HD, (m + 1) * HD)
        for g in range(4):
            lanes = slice(g * GROUP, (g + 1) * GROUP)
            k_lanes = slice(D + g * GROUP, D + (g + 1) * GROUP)
            v_lanes = slice(2 * D + g * GROUP, 2 * D + (g + 1) * GROUP)
            q_stacked = stack_heads(qkv[rows, lanes] * BF(SCALE))
            o_stacked = stack_heads(d_mixed[rows, lanes])
            w_low = weights[m * 4 + g]
            w = w_low.astype(F32)
            dw = nt(qkv[rows, v_lanes], o_stacked)
            inner = jnp.sum(dw * w, axis=0, keepdims=True)
            ds = (w * (dw - inner)).astype(BF)
            dqkv[rows, lanes] = (unstack_heads(tn(ds, qkv[rows, k_lanes])) * SCALE).astype(BF)
            dqkv[rows, k_lanes] = nn(ds, q_stacked).astype(BF)
            dqkv[rows, v_lanes] = nn(w_low, o_stacked).astype(BF)
    d_normed = nt(dqkv[...], w_qkv[...])
    back, gain_rows = norm_back(x, gains[0:1], d_normed)
    gain_grad[0:1, :] = jnp.sum(gain_rows, axis=0, keepdims=True)
    dhb[...] = (d_after + back).astype(BF)
    for h in range(2):
        pieces = (
            dqkv[:, h * HALF : (h + 1) * HALF],
            da[:, h * HALF : (h + 1) * HALF],
            dqkv[:, D + h * HALF : D + (h + 1) * HALF],
            dqkv[:, 2 * D + h * HALF : 2 * D + (h + 1) * HALF],
        )

        @pl.when(core == h)
        def _(pieces=pieces):
            for i, value in enumerate(pieces):
                grads[i * 128 : (i + 1) * 128, :] = value

        @pl.when(core != h)
        def _(pieces=pieces):
            for i, value in enumerate(pieces):
                for b in range(4):
                    first = PACK_GRADS + b * 512 + i * 128
                    packed[first : first + 128, :] = value[:, b * 128 : (b + 1) * 128]


def half_of(core, g, mine, other):
    lanes = slice((g % 2) * GROUP, (g % 2 + 1) * GROUP)

    def put(at, value):
        @pl.when(core == g // 2)
        def _():
            mine[at, lanes] = value

        @pl.when(core != g // 2)
        def _():
            other[at, lanes] = value

    return put


def encoder_attention_back(
    ids, dhb, w_out, q, k_lo, v_lo, k_a, k_b, v_a, v_b, w_a, w_b, mine, other
):
    d_mixed = nt(dhb[...], w_out[...]).astype(BF)
    for g in range(4):
        lanes = slice(g * GROUP, (g + 1) * GROUP)
        put = half_of(ids[0], g, mine, other)
        put(slice(128, 256), dhb[:, lanes])
        for m, (k_up, v_up, weights) in enumerate(((k_a, v_a, w_a), (k_b, v_b, w_b))):
            rows = slice(m * HD, (m + 1) * HD)
            low_at = slice(m * 256, (m + 1) * 256)
            q_stacked = stack_heads(q[rows, lanes] * BF(SCALE))
            o_stacked = stack_heads(d_mixed[rows, lanes])
            low = [weights[g * 2 + h] for h in range(2)]
            w = [piece.astype(F32) for piece in low]
            dw = [nt(values, o_stacked) for values in (v_lo[low_at, lanes], v_up[:, lanes])]
            inner = sum(jnp.sum(a * b, axis=0, keepdims=True) for a, b in zip(dw, w))
            ds = [(b * (a - inner)).astype(BF) for a, b in zip(dw, w)]
            dq = tn(ds[0], k_lo[low_at, lanes]) + tn(ds[1], k_up[:, lanes])
            put(rows, (unstack_heads(dq) * SCALE).astype(BF))
            for h in range(2):
                base = h * HALF + m * 256
                put(slice(256 + base, 512 + base), nn(ds[h], q_stacked).astype(BF))
                put(slice(1280 + base, 1536 + base), nn(low[h], o_stacked).astype(BF))


def both_columns(core, block, w_qkv):
    return [
        w_qkv[:, pl.ds(pl.multiple_of(block * D + which * HALF, HALF), HALF)] for which in (core, 1 - core)
    ]


def bytes_back(core, h, m, source, w_qkv, gains, grads):
    d_norm = sum(
        nt(ref[1024 * block - 768 + h * HALF + m * 256 : 1024 * block - 512 + h * HALF + m * 256, :], columns)
        for block in (1, 2)
        for ref, columns in zip(grads, both_columns(core, block, w_qkv))
    )
    back, gain_rows = norm_back(source.astype(F32), gains[1:2], d_norm)
    return back.astype(BF), jnp.sum(gain_rows, axis=0, keepdims=True)


def encoder_upper_back(ids, up_a, up_b, w_qkv, gains, mine, other, after, up_grad, gain_grad):
    total = jnp.zeros((1, D), F32)
    for m, source in enumerate((up_a, up_b)):
        back, rows = bytes_back(ids[0], 1, m, source[...], w_qkv, gains, (mine, other))
        up_grad[m * 256 : (m + 1) * 256, :] = back
        total = total + rows
    gain_grad[...] = total


def encoder_lower_back(
    ids, dhb, patch, low, w_qkv, gains, mine, other, after, patch_grad, low_grad, gain_grad
):
    core = ids[0]
    up_norm = sum(nt(ref[0:128, :], columns) for ref, columns in zip((mine, other), both_columns(core, 0, w_qkv)))
    back, gain_rows = norm_back(patch[...].astype(F32), gains[0:1], up_norm)
    gain_grad[0:1, :] = jnp.sum(gain_rows, axis=0, keepdims=True)
    patch_grad[...] = dhb[...].astype(F32) + back
    total = jnp.zeros((1, D), F32)
    for m in range(2):
        at = slice(m * 256, (m + 1) * 256)
        back, rows = bytes_back(core, 0, m, low[at, :], w_qkv, gains, (mine, other))
        low_grad[at, :] = back
        total = total + rows
    gain_grad[1:2, :] = total


def turn_encoder(pn, o_a, o_b, bn_lo, bn_a, bn_b, packed):
    for b, rows in enumerate([bn_lo[i * 128 : (i + 1) * 128, :] for i in range(4)]
                             + [ref[i * 128 : (i + 1) * 128, :] for ref in (bn_a, bn_b) for i in range(2)]):
        packed[b * D : (b + 1) * D, :] = rows.T
    packed[PACK_LEFT : PACK_LEFT + D, :] = pn[...].T
    packed[PACK_LEFT + D : PACK_LEFT + 2 * D, :] = jnp.concatenate([o_a[...], o_b[...]], 0).T


def rows_of_both(left, left_far, at):
    return jnp.concatenate([left[at, :], left_far[at, :]], 1)


def below(near, far, rows):
    return jnp.concatenate([near[rows, :], far[rows, :]], 0)


def encoder_weights(ids, packed, packed_far, near, far, *blocks):
    u = ids[1]
    queries = below(near, far, slice(0, 128))
    outputs = below(near, far, slice(128, 256))
    for k in range(4):
        first = lax.rem(u + k, 4) * 256

        def at(base, first=first):
            return pl.ds(pl.multiple_of(first + base, 256), 256)

        blocks[k][0] = nn(rows_of_both(packed, packed_far, at(PACK_LEFT)), queries).astype(BF)
        blocks[k][3] = nn(rows_of_both(packed, packed_far, at(PACK_LEFT + D)), outputs).astype(BF)
        lefts = [jnp.concatenate([ref[at(b * D), :] for b in range(8)], 1) for ref in (packed, packed_far)]
        for block in (1, 2):
            rows = slice(1024 * block - 768, 1024 * block + 256)
            blocks[k][block] = (nn(lefts[0], near[rows, :]) + nn(lefts[1], far[rows, :])).astype(BF)


def unpack(packed, first, rows):
    return jnp.concatenate([packed[first + b * rows : first + (b + 1) * rows, :] for b in range(4)], 1)


def latent_weights(ids, packed, packed_far, near, *blocks):
    u = ids[1]
    far = unpack(packed_far, PACK_GRADS, 512)
    rights = [jnp.concatenate([near[i * 128 : (i + 1) * 128, :], far[i * 128 : (i + 1) * 128, :]], 0) for i in range(4)]
    for k in range(4):
        first = PACK_LEFT + lax.rem(u + k, 4) * 256
        at = pl.ds(pl.multiple_of(first, 256), 256)
        low_at = pl.ds(pl.multiple_of(first + D, 256), 256)
        for block, (source, i) in enumerate(((at, 0), (at, 2), (at, 3), (low_at, 1))):
            blocks[k][block] = nn(rows_of_both(packed, packed_far, source), rights[i]).astype(BF)


def pack_across(ids, packed, norms, out):
    core, zh = ids[0], ids[3]
    for j in range(3):
        for chunk in range(16):
            first = j * UNITS + chunk * (UNITS // 16) + (1 - zh) * WINDOW_STEP
            to = (j * 16 + chunk) * WINDOW
            out[to : to + WINDOW, :] = packed[pl.ds(pl.multiple_of(first, 16), WINDOW), :]
    for b in range(4):
        near = pl.ds(pl.multiple_of(ACROSS_NORMS + (core * 4 + b) * 256, 256), 256)
        far = pl.ds(pl.multiple_of(ACROSS_NORMS + ((1 - core) * 4 + b) * 256, 256), 256)
        out[near, :] = norms[:, b * 128 : (b + 1) * 128]
        out[far, :] = packed[PACK_NORMS + b * 256 : PACK_NORMS + (b + 1) * 256, :]


def ff_weights_grad(ids, packed, packed_far, across, across_far, norms, own, right, left, far_a, far_b):
    core, u, zh = ids[0], ids[1], ids[3]
    both = [norms[...], unpack(packed_far, PACK_NORMS, 256)]
    for ref in (across, across_far):
        blocks = [
            ref[pl.ds(pl.multiple_of(ACROSS_NORMS + (core * 4 + b) * 256, 256), 256), :] for b in range(4)
        ]
        both.append(jnp.concatenate(blocks, 1))
    normed = jnp.concatenate([value[0:128, :] for value in both], 0)
    cot = jnp.concatenate([value[128:256, :] for value in both], 0)
    for k in range(4):
        there = lax.rem(u + k, 4)
        for v in range(4):
            chunk = jnp.where(core == 0, there * 4 + v, v * 4 + there)
            for j in range(3):
                at = pl.ds(
                    pl.multiple_of(j * UNITS + chunk * (UNITS // 16) + zh * WINDOW_STEP, 16), WINDOW
                )
                across_at = pl.ds(pl.multiple_of((j * 16 + chunk) * WINDOW, 16), WINDOW)
                lefts = [packed[at, :], packed_far[at, :], across[across_at, :], across_far[across_at, :]]
                value = nn(jnp.concatenate(lefts, 1), normed if j < 2 else cot).astype(BF)
                rows = slice(j * WINDOW, (j + 1) * WINDOW)
                if k == 2:
                    far_a[v, rows, :] = value[:, :GROUP]
                    far_b[v, rows, :] = value[:, GROUP:]
                else:
                    (own, right, None, left)[k][v, rows, :] = value


def ff_add(right, left, from_left, from_right, new_right, new_left):
    new_right[:, :, 0:GROUP] = (right[:, :, 0:GROUP].astype(F32) + from_left[...].astype(F32)).astype(BF)
    new_right[:, :, GROUP:] = right[:, :, GROUP:]
    new_left[:, :, 0:GROUP] = left[:, :, 0:GROUP]
    new_left[:, :, GROUP:] = (left[:, :, GROUP:].astype(F32) + from_right[...].astype(F32)).astype(BF)


def sum_four(own, a, b, c):
    return own.astype(F32) + a.astype(F32) + b.astype(F32) + c.astype(F32)


def pack_gain(value):
    high = value.astype(BF)
    low = (value - high.astype(F32)).astype(BF)
    return jnp.concatenate(
        [high.astype(F32), low.astype(F32), jnp.zeros((8, HALF), F32)], 0
    ).astype(BF)


def unpack_gain(rows):
    rows = rows.astype(F32)
    return rows[0:4] + rows[4:8]


GAIN_AT = slice(256, 272)


def attn_sum_first(ids, own, a, b, c, *outs):
    v = ids[2]
    for k in range(4):
        at = pl.ds(pl.multiple_of(lax.rem(v + k, 4) * HD, HD), HD)
        for block in range(4):
            outs[k][block * HD : (block + 1) * HD, :] = sum_four(
                own[block, at, :], a[block, at, :], b[block, at, :], c[block, at, :]
            ).astype(BF)


def attn_sum_first_gain(ids, own, a, b, c, enc_gain, up_gain, lat_gain, *outs):
    attn_sum_first(ids, own, a, b, c, *outs)
    first = ids[4] == 0
    gain = jnp.where(
        first, jnp.concatenate([enc_gain[0:1, :], enc_gain[1:2, :] + up_gain[...]], 0), lat_gain[...]
    )
    halves = [gain[i : i + 1, h * HALF : (h + 1) * HALF] for i in range(2) for h in range(2)]
    packed = pack_gain(jnp.concatenate(halves, 0))
    for out in outs:
        out[GAIN_AT, :] = packed


def sum_all(*refs):
    refs, out = refs[:-1], refs[-1]
    out[0:256, :] = sum(ref[0:256, :].astype(F32) for ref in refs).astype(BF)
    out[GAIN_AT, :] = pack_gain(sum(unpack_gain(ref[GAIN_AT, :]) for ref in refs))


def stack_rows(*refs):
    refs, out = refs[:-1], refs[-1]
    for j, ref in enumerate(refs):
        out[j * 256 : (j + 1) * 256, :] = ref[0:256, :]
    out[1024:1040, :] = refs[0][GAIN_AT, :]


def ff_sum_first(ids, own, a, b, *outs):
    v = ids[2]
    for k in range(4):
        at = lax.rem(v + k, 4)
        outs[k][...] = (own[at].astype(F32) + a[at].astype(F32) + b[at].astype(F32)).astype(BF)


def ff_sum_second(own, a, b, c, out):
    out[...] = sum_four(own[...], a[...], b[...], c[...]).astype(BF)


def final_attn(ids, *refs):
    pieces, (qkv, out, gain) = refs[:8], refs[8:]
    step = pl.program_id(0)
    for side in range(2):
        core = ids[0] if side == 0 else 1 - ids[0]
        u = ids[1] if side == 0 else ids[2]
        v = ids[2] if side == 0 else ids[1]
        for k in range(4):
            piece = pieces[side * 4 + k]

            @pl.when(lax.rem(u + k, 4) == step)
            def _(piece=piece, v=v, core=core):
                for j in range(4):
                    at = pl.ds(pl.multiple_of(lax.rem(v + j, 4) * HD, HD), HD)
                    for block in range(4):
                        target, column = (qkv, block * D) if block < 3 else (out, 0)
                        lanes = pl.ds(pl.multiple_of(core * HALF + column, HALF), HALF)
                        first = j * 256 + block * HD
                        target[at, lanes] = piece[first : first + HD, :].astype(F32)

    mine = sum(unpack_gain(piece[1024:1040, :]) for piece in pieces[:4])
    other = sum(unpack_gain(piece[1024:1040, :]) for piece in pieces[4:])
    total = mine + other
    for i in range(2):
        for h in range(2):
            gain[i : i + 1, h * HALF : (h + 1) * HALF] = total[2 * i + h : 2 * i + h + 1, :]


SMEM = pltpu.MemorySpace.SMEM
VMEM = pltpu.MemorySpace.VMEM


def size(shape, dtype):
    return math.prod(shape) * jnp.dtype(dtype).itemsize


def call(kernel, args, outs, scratch=(), spaces=None, spare=6):
    spaces = spaces or {}
    vmem = sum(size(a.shape, a.dtype) for i, a in enumerate(args) if i not in spaces)
    vmem += sum(size(*o) for o in outs)
    vmem += sum(size(s.shape, s.dtype) for s in scratch if hasattr(s, "shape") and s.memory_space == VMEM)
    specs = [pl.BlockSpec(memory_space=spaces.get(i, VMEM)) for i in range(len(args))]
    return pl.pallas_call(
        kernel,
        out_shape=[jax.ShapeDtypeStruct(s, t) for s, t in outs],
        in_specs=specs,
        out_specs=[pl.BlockSpec(memory_space=VMEM) for _ in outs],
        scratch_shapes=list(scratch),
        compiler_params=pltpu.CompilerParams(vmem_limit_bytes=vmem + spare * 1024 * 1024),
    )(*args)


def nothing(outs):
    def kernel(*refs):
        pass

    return pl.pallas_call(
        kernel,
        out_shape=[jax.ShapeDtypeStruct(s, t) for s, t in outs],
        out_specs=[pl.BlockSpec(memory_space=pl.ANY) for _ in outs],
    )()


def on_section(flag, kernel, args, outs, **rest):
    return lax.cond(
        flag, lambda: call(kernel, args, outs, **rest), lambda: nothing(outs)
    )


def along(value, by):
    return lax.ppermute(value, "s", [(0, 1)] if by > 0 else [(1, 0)])


def swap(value, axis, sections=(0, 1)):
    pairs = [(s * 2 + i, s * 2 + 1 - i) for s in sections for i in range(2)]
    return lax.ppermute(value, ("s", axis), pairs)


def plane_shift(value, which, by, sections=(0, 1)):
    pairs = []
    for s in sections:
        for y in range(4):
            for x in range(4):
                for core in range(2):
                    ty, tx = ((y + by) % 4, x) if core == which else (y, (x + by) % 4)
                    pairs.append((((s * 4 + y) * 4 + x) * 2 + core, ((s * 4 + ty) * 4 + tx) * 2 + core))
    return lax.ppermute(value, ("s", "y", "x", "core"), pairs)


def exchange(blocks, which, sections=(0, 1)):
    return [plane_shift(blocks[k], which, k, sections) for k in (1, 2, 3)]


def collect(block, which):
    return [block] + [plane_shift(block, which, -k) for k in (1, 2, 3)]


def pick(stack, index, dim):
    return lax.dynamic_index_in_dim(stack, index, dim, keepdims=False)


def shards(patch_io, byte_states, patch_lengths, patch_live, attn_qkv, attn_out, gains, ff_weights):
    section = lax.axis_index("s")
    core = lax.axis_index("core")
    zh = lax.axis_index("zh")
    y, x = lax.axis_index("y"), lax.axis_index("x")
    first = section == 0
    second = section == 1
    ids = jnp.stack([core, jnp.where(core == 0, y, x), jnp.where(core == 0, x, y), zh, section])
    ids = ids.astype(jnp.int32)
    w_qkv = attn_qkv[0]
    w_out = attn_out[0]
    gain_pair = gains[0]
    micro, seq = patch_io.shape[1], patch_io.shape[3]
    half_bytes = byte_states.shape[2]
    units = ff_weights.shape[0]
    rows = micro * seq
    own_rows = patch_io.reshape(rows, D)
    up_a = along(byte_states[0, 0], -1)
    up_b = along(byte_states[1, 0], -1)
    lower = byte_states.reshape(micro * half_bytes, D)
    w_ff = jnp.swapaxes(ff_weights, 0, 1)
    lengths = patch_lengths[:, 0]
    live = patch_live[:, 0]
    ends = jnp.cumsum(lengths, axis=1)
    bounds = jnp.tile(jnp.stack([ends - lengths, ends], 1), (1, 1, 4))
    places = lax.iota(jnp.int32, seq)
    causal = places[:, None] <= places[None, :]
    diagonal = places[:, None] == places[None, :]
    allowed = causal[None] & ((live[:, :, None] == 1) | diagonal[None])
    allowed = lax.optimization_barrier(jnp.tile(allowed.astype(F32), (1, 1, 4)))

    wide = ((rows, D), BF)
    short = ((seq, D), BF)
    tall = ((micro * half_bytes, D), BF)
    piece = ((half_bytes, D), BF)
    pn, q, bn_lo, k_lo, v_lo = on_section(
        first, encode_lower, (own_rows, lower, w_qkv, gain_pair), [wide, wide, tall, tall, tall]
    )
    rest = []
    for m, up in enumerate((up_a, up_b)):
        rest.append(
            on_section(
                first,
                functools.partial(encode_rest, m),
                (own_rows, up, w_qkv, w_out, gain_pair, bounds, q, k_lo, v_lo),
                [short, short, ((8, 256, GROUP), BF), piece, piece, piece],
            )
        )
    (hb_a, o_a, w_a, bn_a, k_a, v_a), (hb_b, o_b, w_b, bn_b, k_b, v_b) = rest
    arrived = [along(hb_a, 1), along(hb_b, 1)]

    step = 256
    latent_outs = [
        ((rows, D), F32), wide, ((2, D), F32), ((256, HALF), BF), ((512, HALF), BF), ((PACK_ROWS, rows), BF),
    ]

    def latent():
        return call(
            latent_layer,
            (ids, *arrived, own_rows, allowed, w_qkv, w_out, gain_pair, w_ff),
            latent_outs,
            spaces={0: SMEM, 8: pl.ANY},
            scratch=[
                pltpu.VMEM((rows, 3 * D), BF),
                pltpu.VMEM((8, HD, GROUP), BF),
                pltpu.VMEM((rows, D), BF),
                pltpu.VMEM((2, 3, step, D), BF),
                pltpu.VMEM((rows, D), F32),
                pltpu.VMEM((rows, D), F32),
                pltpu.VMEM((rows, 3 * D), BF),
                pltpu.SemaphoreType.DMA((2,)),
            ],
        )

    def turn():
        return nothing(latent_outs[:5]) + call(
            turn_encoder, (pn, o_a, o_b, bn_lo, bn_a, bn_b), latent_outs[5:]
        )

    latents, dhb, latent_gain, norms, lat_grads, packed = lax.cond(second, latent, turn)
    returned = along(dhb, -1)

    packed_far = swap(packed, "core")

    share = units // 16
    ff_block = ((4, 3 * WINDOW, HALF), BF)
    ff_half = ((4, 3 * WINDOW, GROUP), BF)
    (across,) = on_section(
        second, pack_across, (ids, packed, norms), [((ACROSS_ROWS, rows), BF)], spaces={0: SMEM}
    )
    across = swap(across, "zh", (1,))

    grads_long = ((2304, HALF), BF)
    enc_grads, enc_other = on_section(
        first,
        encoder_attention_back,
        (ids, returned, w_out, q, k_lo, v_lo, k_a, k_b, v_a, v_b, w_a, w_b),
        [grads_long, grads_long],
        spaces={0: SMEM},
    )
    enc_far = swap(enc_other, "core", (0,))
    outs = [((4, 256, HALF), BF)] * 4
    blocks = lax.cond(
        first,
        lambda: call(encoder_weights, (ids, packed, packed_far, enc_grads, enc_far), outs, spaces={0: SMEM}),
        lambda: call(latent_weights, (ids, packed, packed_far, lat_grads), outs, spaces={0: SMEM}),
    )
    got = exchange(blocks, 0)
    across, _ = lax.optimization_barrier((across, blocks))
    across_far = swap(across, "core", (1,))
    ff_outs = [ff_block, ff_block, ff_block, ff_half, ff_half]
    byte_outs = [tall, ((1, D), F32)], [((rows, D), F32), tall, ((2, D), F32)]

    def input_grads():
        upper_part = call(
            encoder_upper_back,
            (ids, up_a, up_b, w_qkv, gain_pair, enc_grads, enc_other, blocks[0]),
            byte_outs[0],
            spaces={0: SMEM, 7: pl.ANY},
        )
        lower_part = call(
            encoder_lower_back,
            (ids, returned, own_rows, lower, w_qkv, gain_pair, enc_grads, enc_other, upper_part[1]),
            byte_outs[1],
            spaces={0: SMEM, 8: pl.ANY},
        )
        return (*upper_part, *lower_part, *nothing(ff_outs))

    def ff_grads():
        parts = call(
            ff_weights_grad,
            (ids, packed, packed_far, across, across_far, norms),
            ff_outs,
            spaces={0: SMEM},
        )
        return (*nothing(byte_outs[0] + byte_outs[1]), *parts)

    (
        up_grad, up_gain, patch_grad, low_grad, encoder_gain,
        ff_own, ff_right, ff_left, ff_far_a, ff_far_b,
    ) = lax.cond(first, input_grads, ff_grads)
    line = [((272, HALF), BF)]
    blocks = call(
        attn_sum_first_gain,
        (ids, blocks[0], *got, encoder_gain, up_gain, latent_gain),
        line * 4,
        spaces={0: SMEM},
    )
    ff_far_a, ff_far_b, _ = lax.optimization_barrier((ff_far_a, ff_far_b, blocks))
    from_left = plane_shift(ff_far_a, 0, 1, (1,))
    from_right = plane_shift(ff_far_b, 0, -1, (1,))
    from_left, from_right, met = lax.optimization_barrier((from_left, from_right, exchange(blocks, 1)))
    ff_right, ff_left = on_section(
        second, ff_add, (ff_right, ff_left, from_left, from_right), [ff_block, ff_block]
    )
    from_left = plane_shift(ff_right, 0, 1, (1,))
    from_right = plane_shift(ff_left, 0, -1, (1,))
    (block,) = call(sum_all, (blocks[0], *met), line)
    across_block, _ = lax.optimization_barrier((swap(block, "zh"), ff_right))
    (block,) = call(sum_all, (block, across_block), line)
    up_grad, block = lax.optimization_barrier((up_grad, block))
    up_arrived = along(up_grad, 1)
    (block,) = call(stack_rows, collect(block, 1), [((1040, HALF), BF)])
    from_left, from_right, block = lax.optimization_barrier((from_left, from_right, block))
    pieces = collect(block, 0)
    ff_line = ((3 * WINDOW, HALF), BF)
    ff_blocks = on_section(
        second, ff_sum_first, (ids, ff_own, from_left, from_right), [ff_line] * 4, spaces={0: SMEM}
    )
    ff_got = exchange(ff_blocks, 1, (1,))
    (ff_sum,) = on_section(second, ff_sum_second, (ff_blocks[0], *ff_got), [ff_line])
    ff_sum = ff_sum.reshape(3, WINDOW, HALF)
    start = zh * (share // 2 - WINDOW_STEP)
    ff_mine = lax.dynamic_slice_in_dim(ff_sum, start + core * (share // 4), share // 4, 1)
    ff_far = lax.dynamic_slice_in_dim(ff_sum, start + (1 - core) * (share // 4), share // 4, 1)
    ff_far = swap(ff_far, "core", (1,))

    def ff_result():
        low, high = jnp.where(core == 0, ff_mine, ff_far), jnp.where(core == 0, ff_far, ff_mine)
        return jnp.swapaxes(jnp.concatenate([low, high], 2), 0, 1).astype(F32)

    ff_grad = lax.cond(second, ff_result, lambda: jnp.zeros((share // 4, 3, D), F32))
    byte_grad = jnp.where(first, low_grad, up_arrived)
    patch_out = jnp.where(first, patch_grad, latents)
    own_far = swap(pieces[0], "core")
    patch_out, ff_grad, *pieces = lax.optimization_barrier((patch_out, ff_grad, *pieces))
    pieces = pieces + [own_far] + [swap(p, "core") for p in pieces[1:]]
    whole = lambda p: pl.BlockSpec(p.shape, lambda i, n=p.ndim: (0,) * n)
    total_qkv, total_out, total_gain = pl.pallas_call(
        final_attn,
        grid=(4,),
        out_shape=[
            jax.ShapeDtypeStruct((D, 3 * D), F32),
            jax.ShapeDtypeStruct((D, D), F32),
            jax.ShapeDtypeStruct((2, D), F32),
        ],
        in_specs=[pl.BlockSpec(memory_space=SMEM)] + [whole(p) for p in pieces],
        out_specs=[
            pl.BlockSpec((256, 3 * D), lambda i: (i, 0)),
            pl.BlockSpec((256, D), lambda i: (i, 0)),
            pl.BlockSpec((2, D), lambda i: (0, 0)),
        ],
        compiler_params=pltpu.CompilerParams(vmem_limit_bytes=FINAL_VMEM),
    )(ids, *pieces)
    return (
        patch_out.reshape(1, micro, 1, seq, D),
        byte_grad.reshape(micro, 1, half_bytes, D),
        total_qkv[None],
        total_out[None],
        total_gain[None],
        ff_grad[None],
    )


def solution(mesh):
    fine = Mesh(mesh.devices.reshape(2, 4, 4, 2, 2), ("s",) + BATCH)
    in_specs = (
        P("s", None, BATCH, None, None),
        P(None, BATCH, "s", None),
        P(None, BATCH, None),
        P(None, BATCH, None),
        P("s", None, None),
        P("s", None, None),
        P("s", None, None),
        P(),
    )
    out_specs = (
        P("s", None, BATCH, None, None),
        P(None, BATCH, "s", None),
        P("s", None, None),
        P("s", None, None),
        P("s", None, None),
        P("s", BATCH, None, None),
    )
    return jax.shard_map(shards, mesh=fine, in_specs=in_specs, out_specs=out_specs, check_vma=False)
```

```python
import functools
import math

import jax
import jax.numpy as jnp
from jax import lax
from jax.experimental import pallas as pl
from jax.experimental.pallas import tpu as pltpu
from jax.sharding import Mesh
from jax.sharding import PartitionSpec as P

HD = 64
SCALE = HD**-0.5
EPS = 1e-05
NEG = -1e30
BATCH = ("y", "x", "zh", "core")
BF = jnp.bfloat16
F32 = jnp.float32
D = 1024
HALF = 512
GROUP = 256
FINAL_VMEM = 32 * 1024 * 1024


UNITS = 2816
PACK_NORMS = 3 * UNITS
PACK_LEFT = PACK_NORMS + 4 * 256
PACK_GRADS = PACK_LEFT + 2 * D
PACK_ROWS = PACK_GRADS + 4 * 512


def nn(a, b):
    return lax.dot_general(a, b, (((1,), (0,)), ((), ())), preferred_element_type=F32)


def nt(a, b):
    return lax.dot_general(a, b, (((1,), (1,)), ((), ())), preferred_element_type=F32)


def tn(a, b):
    return lax.dot_general(a, b, (((0,), (0,)), ((), ())), preferred_element_type=F32)


def inverse_rms(x):
    return lax.rsqrt(jnp.mean(x * x, axis=-1, keepdims=True) + EPS)


def norm_back(x, gain, up):
    r = inverse_rms(x)
    scaled = up * gain
    inner = jnp.mean(scaled * x, axis=-1, keepdims=True)
    return r * (scaled - x * (r * r * inner)), up * (x * r)


def stack_heads(rows):
    head = lax.broadcasted_iota(jnp.int32, rows.shape, 1) // HD
    return jnp.concatenate([jnp.where(head == h, rows, jnp.zeros_like(rows)) for h in range(4)], 0)


def unstack_heads(stacked):
    head = lax.broadcasted_iota(jnp.int32, (HD, GROUP), 1) // HD
    out = stacked[0:HD]
    for h in range(1, 4):
        out = jnp.where(head == h, stacked[h * HD : (h + 1) * HD], out)
    return out


def softmax_columns(scores):
    top = functools.reduce(jnp.maximum, [jnp.max(s, axis=0, keepdims=True) for s in scores])
    parts = [jnp.exp(s - top) for s in scores]
    inverse = 1.0 / sum(jnp.sum(p, axis=0, keepdims=True) for p in parts)
    return [(p * inverse).astype(BF) for p in parts]


def encode_lower(patch, low, w_qkv, gains, pn, q, bn, k, v):
    x = patch[...].astype(F32)
    normed = (x * inverse_rms(x) * gains[0:1]).astype(BF)
    pn[...] = normed
    q[...] = nn(normed, w_qkv[:, 0:D]).astype(BF)
    for i in range(2):
        at = pl.ds(i * 256, 256)
        b = low[at, :].astype(F32)
        normed = (b * inverse_rms(b) * gains[1:2]).astype(BF)
        bn[at, :] = normed
        k[at, :] = nn(normed, w_qkv[:, D : 2 * D]).astype(BF)
        v[at, :] = nn(normed, w_qkv[:, 2 * D :]).astype(BF)


def encode_rest(m, patch, up, w_qkv, w_out, gains, bounds, q, k_lo, v_lo, hb, o1, weights, bn, k, v):
    b = up[...].astype(F32)
    normed = (b * inverse_rms(b) * gains[1:2]).astype(BF)
    bn[...] = normed
    k[...] = nn(normed, w_qkv[:, D : 2 * D]).astype(BF)
    v[...] = nn(normed, w_qkv[:, 2 * D :]).astype(BF)
    spot = lax.broadcasted_iota(jnp.int32, (256, GROUP), 0)
    start = bounds[m, 0:1, :]
    end = bounds[m, 1:2, :]
    inside = [(spot + h * 256 >= start) & (spot + h * 256 < end) for h in range(2)]
    low_at = slice(m * 256, (m + 1) * 256)
    rows = slice(m * HD, (m + 1) * HD)
    for g in range(4):
        lanes = slice(g * GROUP, (g + 1) * GROUP)
        stacked = stack_heads(q[rows, lanes] * BF(SCALE))
        scores = [
            jnp.where(inside[h], nt(keys, stacked), NEG)
            for h, keys in enumerate((k_lo[low_at, lanes], k[:, lanes]))
        ]
        w = softmax_columns(scores)
        weights[g * 2] = w[0]
        weights[g * 2 + 1] = w[1]
        mixed = tn(w[0], v_lo[low_at, lanes]) + tn(w[1], v[:, lanes])
        o1[:, lanes] = unstack_heads(mixed).astype(BF)
    hb[...] = (patch[rows, :].astype(F32) + nn(o1[...], w_out[...])).astype(BF)


def latent_layer(
    ids, hb_a, hb_b, cot, allowed, w_qkv, w_out, gains, w_ff,
    latents, dhb, gain_grad, norms, grads, packed,
    qkv, weights, o2, ff_buf, acc_out, acc_norm, dqkv, sems,
):
    core = ids[0]
    units = w_ff.shape[1]
    step = ff_buf.shape[2]
    steps = units // step

    def fetch(i, slot):
        return pltpu.make_async_copy(
            w_ff.at[:, pl.ds(pl.multiple_of(i * step, 128), step), :], ff_buf.at[slot], sems.at[slot]
        )

    fetch(0, 0).start()
    x = jnp.concatenate([hb_a[...], hb_b[...]], 0).astype(F32)
    normed = (x * inverse_rms(x) * gains[0:1]).astype(BF)
    packed[PACK_LEFT : PACK_LEFT + D, :] = normed.T
    qkv[...] = nn(normed, w_qkv[...]).astype(BF)
    for m in range(2):
        rows = slice(m * HD, (m + 1) * HD)
        for g in range(4):
            lanes = slice(g * GROUP, (g + 1) * GROUP)
            k_lanes = slice(D + g * GROUP, D + (g + 1) * GROUP)
            v_lanes = slice(2 * D + g * GROUP, 2 * D + (g + 1) * GROUP)
            stacked = stack_heads(qkv[rows, lanes] * BF(SCALE))
            scores = jnp.where(allowed[m] > 0.5, nt(qkv[rows, k_lanes], stacked), NEG)
            (w,) = softmax_columns([scores])
            weights[m * 4 + g] = w
            o2[rows, lanes] = unstack_heads(tn(w, qkv[rows, v_lanes])).astype(BF)
    packed[PACK_LEFT + D : PACK_LEFT + 2 * D, :] = o2[...].T
    after = x + nn(o2[...], w_out[...])
    yn = (after * inverse_rms(after) * gains[1:2]).astype(BF)
    c = cot[...]
    for h in range(2):

        @pl.when(core == h)
        def _(h=h):
            norms[0:128, :] = yn[:, h * HALF : (h + 1) * HALF]
            norms[128:256, :] = c[:, h * HALF : (h + 1) * HALF]

        @pl.when(core != h)
        def _(h=h):
            for b in range(4):
                lanes = slice(h * HALF + b * 128, h * HALF + (b + 1) * 128)
                packed[PACK_NORMS + b * 256 : PACK_NORMS + b * 256 + 128, :] = yn[:, lanes]
                packed[PACK_NORMS + b * 256 + 128 : PACK_NORMS + (b + 1) * 256, :] = c[:, lanes]

    acc_out[...] = after
    acc_norm[...] = jnp.zeros_like(acc_norm)

    def ff_step(i, carry):
        slot = lax.rem(i, 2)

        @pl.when(i + 1 < steps)
        def _():
            fetch(i + 1, 1 - slot).start()

        fetch(i, slot).wait()
        w_gate, w_up, w_down = ff_buf.at[slot, 0], ff_buf.at[slot, 1], ff_buf.at[slot, 2]
        gate = nt(yn, w_gate[...])
        upward = nt(yn, w_up[...])
        du = nt(c, w_down[...])
        sig = 1.0 / (1.0 + jnp.exp(-gate))
        active = gate * sig
        hidden = (active * upward).astype(BF)
        d_gate = (du * upward * (sig * (1.0 + gate * (1.0 - sig)))).astype(BF)
        d_up = (du * active).astype(BF)
        at = pl.ds(pl.multiple_of(i * step, 128), step)
        for j, value in enumerate((d_gate, d_up, hidden)):
            packed[pl.ds(pl.multiple_of(i * step + j * units, 128), step), :] = value.T
        acc_out[...] += nn(hidden, w_down[...])
        acc_norm[...] += nn(d_gate, w_gate[...]) + nn(d_up, w_up[...])
        return carry

    lax.fori_loop(0, steps, ff_step, 0)
    latents[...] = acc_out[...]
    back, gain_rows = norm_back(after, gains[1:2], acc_norm[...])
    gain_grad[1:2, :] = jnp.sum(gain_rows, axis=0, keepdims=True)
    d_after = c.astype(F32) + back
    da = d_after.astype(BF)
    d_mixed = nt(da, w_out[...]).astype(BF)
    for m in range(2):
        rows = slice(m * HD, (m + 1) * HD)
        for g in range(4):
            lanes = slice(g * GROUP, (g + 1) * GROUP)
            k_lanes = slice(D + g * GROUP, D + (g + 1) * GROUP)
            v_lanes = slice(2 * D + g * GROUP, 2 * D + (g + 1) * GROUP)
            q_stacked = stack_heads(qkv[rows, lanes] * BF(SCALE))
            o_stacked = stack_heads(d_mixed[rows, lanes])
            w_low = weights[m * 4 + g]
            w = w_low.astype(F32)
            dw = nt(qkv[rows, v_lanes], o_stacked)
            inner = jnp.sum(dw * w, axis=0, keepdims=True)
            ds = (w * (dw - inner)).astype(BF)
            dqkv[rows, lanes] = (unstack_heads(tn(ds, qkv[rows, k_lanes])) * SCALE).astype(BF)
            dqkv[rows, k_lanes] = nn(ds, q_stacked).astype(BF)
            dqkv[rows, v_lanes] = nn(w_low, o_stacked).astype(BF)
    d_normed = nt(dqkv[...], w_qkv[...])
    back, gain_rows = norm_back(x, gains[0:1], d_normed)
    gain_grad[0:1, :] = jnp.sum(gain_rows, axis=0, keepdims=True)
    dhb[...] = (d_after + back).astype(BF)
    for h in range(2):
        pieces = (
            dqkv[:, h * HALF : (h + 1) * HALF],
            da[:, h * HALF : (h + 1) * HALF],
            dqkv[:, D + h * HALF : D + (h + 1) * HALF],
            dqkv[:, 2 * D + h * HALF : 2 * D + (h + 1) * HALF],
        )

        @pl.when(core == h)
        def _(pieces=pieces):
            for i, value in enumerate(pieces):
                grads[i * 128 : (i + 1) * 128, :] = value

        @pl.when(core != h)
        def _(pieces=pieces):
            for i, value in enumerate(pieces):
                for b in range(4):
                    first = PACK_GRADS + b * 512 + i * 128
                    packed[first : first + 128, :] = value[:, b * 128 : (b + 1) * 128]


def half_of(core, g, mine, other):
    lanes = slice((g % 2) * GROUP, (g % 2 + 1) * GROUP)

    def put(at, value):
        @pl.when(core == g // 2)
        def _():
            mine[at, lanes] = value

        @pl.when(core != g // 2)
        def _():
            other[at, lanes] = value

    return put


def encoder_attention_back(
    ids, dhb, w_out, q, k_lo, v_lo, k_a, k_b, v_a, v_b, w_a, w_b, mine, other
):
    d_mixed = nt(dhb[...], w_out[...]).astype(BF)
    for g in range(4):
        lanes = slice(g * GROUP, (g + 1) * GROUP)
        put = half_of(ids[0], g, mine, other)
        put(slice(128, 256), dhb[:, lanes])
        for m, (k_up, v_up, weights) in enumerate(((k_a, v_a, w_a), (k_b, v_b, w_b))):
            rows = slice(m * HD, (m + 1) * HD)
            low_at = slice(m * 256, (m + 1) * 256)
            q_stacked = stack_heads(q[rows, lanes] * BF(SCALE))
            o_stacked = stack_heads(d_mixed[rows, lanes])
            low = [weights[g * 2 + h] for h in range(2)]
            w = [piece.astype(F32) for piece in low]
            dw = [nt(values, o_stacked) for values in (v_lo[low_at, lanes], v_up[:, lanes])]
            inner = sum(jnp.sum(a * b, axis=0, keepdims=True) for a, b in zip(dw, w))
            ds = [(b * (a - inner)).astype(BF) for a, b in zip(dw, w)]
            dq = tn(ds[0], k_lo[low_at, lanes]) + tn(ds[1], k_up[:, lanes])
            put(rows, (unstack_heads(dq) * SCALE).astype(BF))
            for h in range(2):
                base = h * HALF + m * 256
                put(slice(256 + base, 512 + base), nn(ds[h], q_stacked).astype(BF))
                put(slice(1280 + base, 1536 + base), nn(low[h], o_stacked).astype(BF))


def both_columns(core, block, w_qkv):
    return [
        w_qkv[:, pl.ds(pl.multiple_of(block * D + which * HALF, HALF), HALF)] for which in (core, 1 - core)
    ]


def bytes_back(core, h, m, source, w_qkv, gains, grads):
    d_norm = sum(
        nt(ref[1024 * block - 768 + h * HALF + m * 256 : 1024 * block - 512 + h * HALF + m * 256, :], columns)
        for block in (1, 2)
        for ref, columns in zip(grads, both_columns(core, block, w_qkv))
    )
    back, gain_rows = norm_back(source.astype(F32), gains[1:2], d_norm)
    return back.astype(BF), jnp.sum(gain_rows, axis=0, keepdims=True)


def encoder_upper_back(ids, up_a, up_b, w_qkv, gains, mine, other, after, up_grad, gain_grad):
    total = jnp.zeros((1, D), F32)
    for m, source in enumerate((up_a, up_b)):
        back, rows = bytes_back(ids[0], 1, m, source[...], w_qkv, gains, (mine, other))
        up_grad[m * 256 : (m + 1) * 256, :] = back
        total = total + rows
    gain_grad[...] = total


def encoder_lower_back(
    ids, dhb, patch, low, w_qkv, gains, mine, other, after, patch_grad, low_grad, gain_grad
):
    core = ids[0]
    up_norm = sum(nt(ref[0:128, :], columns) for ref, columns in zip((mine, other), both_columns(core, 0, w_qkv)))
    back, gain_rows = norm_back(patch[...].astype(F32), gains[0:1], up_norm)
    gain_grad[0:1, :] = jnp.sum(gain_rows, axis=0, keepdims=True)
    patch_grad[...] = dhb[...].astype(F32) + back
    total = jnp.zeros((1, D), F32)
    for m in range(2):
        at = slice(m * 256, (m + 1) * 256)
        back, rows = bytes_back(core, 0, m, low[at, :], w_qkv, gains, (mine, other))
        low_grad[at, :] = back
        total = total + rows
    gain_grad[1:2, :] = total


def turn_encoder(pn, o_a, o_b, bn_lo, bn_a, bn_b, packed):
    for b, rows in enumerate([bn_lo[i * 128 : (i + 1) * 128, :] for i in range(4)]
                             + [ref[i * 128 : (i + 1) * 128, :] for ref in (bn_a, bn_b) for i in range(2)]):
        packed[b * D : (b + 1) * D, :] = rows.T
    packed[PACK_LEFT : PACK_LEFT + D, :] = pn[...].T
    packed[PACK_LEFT + D : PACK_LEFT + 2 * D, :] = jnp.concatenate([o_a[...], o_b[...]], 0).T


def rows_of_both(left, left_far, at):
    return jnp.concatenate([left[at, :], left_far[at, :]], 1)


def below(near, far, rows):
    return jnp.concatenate([near[rows, :], far[rows, :]], 0)


def encoder_weights(ids, packed, packed_far, near, far, *blocks):
    u = ids[1]
    queries = below(near, far, slice(0, 128))
    outputs = below(near, far, slice(128, 256))
    for k in range(4):
        first = lax.rem(u + k, 4) * 256

        def at(base, first=first):
            return pl.ds(pl.multiple_of(first + base, 256), 256)

        blocks[k][0] = nn(rows_of_both(packed, packed_far, at(PACK_LEFT)), queries).astype(BF)
        blocks[k][3] = nn(rows_of_both(packed, packed_far, at(PACK_LEFT + D)), outputs).astype(BF)
        lefts = [jnp.concatenate([ref[at(b * D), :] for b in range(8)], 1) for ref in (packed, packed_far)]
        for block in (1, 2):
            rows = slice(1024 * block - 768, 1024 * block + 256)
            blocks[k][block] = (nn(lefts[0], near[rows, :]) + nn(lefts[1], far[rows, :])).astype(BF)


def unpack(packed, first, rows):
    return jnp.concatenate([packed[first + b * rows : first + (b + 1) * rows, :] for b in range(4)], 1)


def latent_weights(ids, packed, packed_far, near, *blocks):
    u = ids[1]
    far = unpack(packed_far, PACK_GRADS, 512)
    rights = [jnp.concatenate([near[i * 128 : (i + 1) * 128, :], far[i * 128 : (i + 1) * 128, :]], 0) for i in range(4)]
    for k in range(4):
        first = PACK_LEFT + lax.rem(u + k, 4) * 256
        at = pl.ds(pl.multiple_of(first, 256), 256)
        low_at = pl.ds(pl.multiple_of(first + D, 256), 256)
        for block, (source, i) in enumerate(((at, 0), (at, 2), (at, 3), (low_at, 1))):
            blocks[k][block] = nn(rows_of_both(packed, packed_far, source), rights[i]).astype(BF)


def ff_weights_grad(ids, packed, packed_far, norms, own, right, left, far_a, far_b):
    core, u = ids[0], ids[1]
    share = UNITS // 16
    far = unpack(packed_far, PACK_NORMS, 256)
    normed = jnp.concatenate([norms[0:128, :], far[0:128, :]], 0)
    cot = jnp.concatenate([norms[128:256, :], far[128:256, :]], 0)
    for k in range(4):
        there = lax.rem(u + k, 4)
        for v in range(4):
            chunk = jnp.where(core == 0, there * 4 + v, v * 4 + there)
            for j in range(3):
                at = pl.ds(pl.multiple_of(j * UNITS + chunk * share, 16), share)
                value = nn(rows_of_both(packed, packed_far, at), normed if j < 2 else cot).astype(BF)
                rows = slice(j * share, (j + 1) * share)
                if k == 2:
                    far_a[v, rows, :] = value[:, :GROUP]
                    far_b[v, rows, :] = value[:, GROUP:]
                else:
                    (own, right, None, left)[k][v, rows, :] = value


def ff_add(right, left, from_left, from_right, after, new_right, new_left):
    new_right[:, :, 0:GROUP] = (right[:, :, 0:GROUP].astype(F32) + from_left[...].astype(F32)).astype(BF)
    new_right[:, :, GROUP:] = right[:, :, GROUP:]
    new_left[:, :, 0:GROUP] = left[:, :, 0:GROUP]
    new_left[:, :, GROUP:] = (left[:, :, GROUP:].astype(F32) + from_right[...].astype(F32)).astype(BF)


def sum_four(own, a, b, c):
    return own.astype(F32) + a.astype(F32) + b.astype(F32) + c.astype(F32)


def pack_gain(value):
    high = value.astype(BF)
    low = (value - high.astype(F32)).astype(BF)
    return jnp.concatenate(
        [high.astype(F32), low.astype(F32), jnp.zeros((8, HALF), F32)], 0
    ).astype(BF)


def unpack_gain(rows):
    rows = rows.astype(F32)
    return rows[0:4] + rows[4:8]


GAIN_AT = slice(256, 272)


def attn_sum_first(ids, own, a, b, c, *outs):
    v = ids[2]
    for k in range(4):
        at = pl.ds(pl.multiple_of(lax.rem(v + k, 4) * HD, HD), HD)
        for block in range(4):
            outs[k][block * HD : (block + 1) * HD, :] = sum_four(
                own[block, at, :], a[block, at, :], b[block, at, :], c[block, at, :]
            ).astype(BF)


def attn_sum_first_gain(ids, own, a, b, c, enc_gain, up_gain, lat_gain, *outs):
    attn_sum_first(ids, own, a, b, c, *outs)
    first = ids[4] == 0
    gain = jnp.where(
        first, jnp.concatenate([enc_gain[0:1, :], enc_gain[1:2, :] + up_gain[...]], 0), lat_gain[...]
    )
    halves = [gain[i : i + 1, h * HALF : (h + 1) * HALF] for i in range(2) for h in range(2)]
    packed = pack_gain(jnp.concatenate(halves, 0))
    for out in outs:
        out[GAIN_AT, :] = packed


def sum_all(*refs):
    refs, out = refs[:-1], refs[-1]
    out[0:256, :] = sum(ref[0:256, :].astype(F32) for ref in refs).astype(BF)
    out[GAIN_AT, :] = pack_gain(sum(unpack_gain(ref[GAIN_AT, :]) for ref in refs))


def stack_rows(*refs):
    refs, out = refs[:-1], refs[-1]
    for j, ref in enumerate(refs):
        out[j * 256 : (j + 1) * 256, :] = ref[0:256, :]
    out[1024:1040, :] = refs[0][GAIN_AT, :]


def ff_sum_first(ids, own, a, b, *outs):
    v = ids[2]
    for k in range(4):
        at = lax.rem(v + k, 4)
        outs[k][...] = (own[at].astype(F32) + a[at].astype(F32) + b[at].astype(F32)).astype(BF)


def ff_sum_second(own, a, b, c, out):
    out[...] = sum_four(own[...], a[...], b[...], c[...]).astype(BF)


def final_attn(ids, *refs):
    pieces, (qkv, out, gain) = refs[:8], refs[8:]
    step = pl.program_id(0)
    for side in range(2):
        core = ids[0] if side == 0 else 1 - ids[0]
        u = ids[1] if side == 0 else ids[2]
        v = ids[2] if side == 0 else ids[1]
        for k in range(4):
            piece = pieces[side * 4 + k]

            @pl.when(lax.rem(u + k, 4) == step)
            def _(piece=piece, v=v, core=core):
                for j in range(4):
                    at = pl.ds(pl.multiple_of(lax.rem(v + j, 4) * HD, HD), HD)
                    for block in range(4):
                        target, column = (qkv, block * D) if block < 3 else (out, 0)
                        lanes = pl.ds(pl.multiple_of(core * HALF + column, HALF), HALF)
                        first = j * 256 + block * HD
                        target[at, lanes] = piece[first : first + HD, :].astype(F32)

    mine = sum(unpack_gain(piece[1024:1040, :]) for piece in pieces[:4])
    other = sum(unpack_gain(piece[1024:1040, :]) for piece in pieces[4:])
    total = mine + other
    for i in range(2):
        for h in range(2):
            gain[i : i + 1, h * HALF : (h + 1) * HALF] = total[2 * i + h : 2 * i + h + 1, :]


SMEM = pltpu.MemorySpace.SMEM
VMEM = pltpu.MemorySpace.VMEM


def size(shape, dtype):
    return math.prod(shape) * jnp.dtype(dtype).itemsize


def call(kernel, args, outs, scratch=(), spaces=None, spare=6):
    spaces = spaces or {}
    vmem = sum(size(a.shape, a.dtype) for i, a in enumerate(args) if i not in spaces)
    vmem += sum(size(*o) for o in outs)
    vmem += sum(size(s.shape, s.dtype) for s in scratch if hasattr(s, "shape") and s.memory_space == VMEM)
    specs = [pl.BlockSpec(memory_space=spaces.get(i, VMEM)) for i in range(len(args))]
    return pl.pallas_call(
        kernel,
        out_shape=[jax.ShapeDtypeStruct(s, t) for s, t in outs],
        in_specs=specs,
        out_specs=[pl.BlockSpec(memory_space=VMEM) for _ in outs],
        scratch_shapes=list(scratch),
        compiler_params=pltpu.CompilerParams(vmem_limit_bytes=vmem + spare * 1024 * 1024),
    )(*args)


def nothing(outs):
    def kernel(*refs):
        pass

    return pl.pallas_call(
        kernel,
        out_shape=[jax.ShapeDtypeStruct(s, t) for s, t in outs],
        out_specs=[pl.BlockSpec(memory_space=pl.ANY) for _ in outs],
    )()


def on_section(flag, kernel, args, outs, **rest):
    return lax.cond(
        flag, lambda: call(kernel, args, outs, **rest), lambda: nothing(outs)
    )


def along(value, by):
    return lax.ppermute(value, "s", [(0, 1)] if by > 0 else [(1, 0)])


def swap(value, axis, sections=(0, 1)):
    pairs = [(s * 2 + i, s * 2 + 1 - i) for s in sections for i in range(2)]
    return lax.ppermute(value, ("s", axis), pairs)


def plane_shift(value, which, by, sections=(0, 1)):
    pairs = []
    for s in sections:
        for y in range(4):
            for x in range(4):
                for core in range(2):
                    ty, tx = ((y + by) % 4, x) if core == which else (y, (x + by) % 4)
                    pairs.append((((s * 4 + y) * 4 + x) * 2 + core, ((s * 4 + ty) * 4 + tx) * 2 + core))
    return lax.ppermute(value, ("s", "y", "x", "core"), pairs)


def exchange(blocks, which, sections=(0, 1)):
    return [plane_shift(blocks[k], which, k, sections) for k in (1, 2, 3)]


def collect(block, which):
    return [block] + [plane_shift(block, which, -k) for k in (1, 2, 3)]


def pick(stack, index, dim):
    return lax.dynamic_index_in_dim(stack, index, dim, keepdims=False)


def shards(patch_io, byte_states, patch_lengths, patch_live, attn_qkv, attn_out, gains, ff_weights):
    section = lax.axis_index("s")
    core = lax.axis_index("core")
    zh = lax.axis_index("zh")
    y, x = lax.axis_index("y"), lax.axis_index("x")
    first = section == 0
    second = section == 1
    ids = jnp.stack([core, jnp.where(core == 0, y, x), jnp.where(core == 0, x, y), zh, section])
    ids = ids.astype(jnp.int32)
    w_qkv = attn_qkv[0]
    w_out = attn_out[0]
    gain_pair = gains[0]
    micro, seq = patch_io.shape[1], patch_io.shape[3]
    half_bytes = byte_states.shape[2]
    units = ff_weights.shape[0]
    rows = micro * seq
    own_rows = patch_io.reshape(rows, D)
    up_a = along(byte_states[0, 0], -1)
    up_b = along(byte_states[1, 0], -1)
    lower = byte_states.reshape(micro * half_bytes, D)
    w_ff = jnp.swapaxes(ff_weights, 0, 1)
    lengths = patch_lengths[:, 0]
    live = patch_live[:, 0]
    ends = jnp.cumsum(lengths, axis=1)
    bounds = jnp.tile(jnp.stack([ends - lengths, ends], 1), (1, 1, 4))
    places = lax.iota(jnp.int32, seq)
    causal = places[:, None] <= places[None, :]
    diagonal = places[:, None] == places[None, :]
    allowed = causal[None] & ((live[:, :, None] == 1) | diagonal[None])
    allowed = lax.optimization_barrier(jnp.tile(allowed.astype(F32), (1, 1, 4)))

    wide = ((rows, D), BF)
    short = ((seq, D), BF)
    tall = ((micro * half_bytes, D), BF)
    piece = ((half_bytes, D), BF)
    pn, q, bn_lo, k_lo, v_lo = on_section(
        first, encode_lower, (own_rows, lower, w_qkv, gain_pair), [wide, wide, tall, tall, tall]
    )
    rest = []
    for m, up in enumerate((up_a, up_b)):
        rest.append(
            on_section(
                first,
                functools.partial(encode_rest, m),
                (own_rows, up, w_qkv, w_out, gain_pair, bounds, q, k_lo, v_lo),
                [short, short, ((8, 256, GROUP), BF), piece, piece, piece],
            )
        )
    (hb_a, o_a, w_a, bn_a, k_a, v_a), (hb_b, o_b, w_b, bn_b, k_b, v_b) = rest
    arrived = [along(hb_a, 1), along(hb_b, 1)]

    step = 256
    latent_outs = [
        ((rows, D), F32), wide, ((2, D), F32), ((256, HALF), BF), ((512, HALF), BF), ((PACK_ROWS, rows), BF),
    ]

    def latent():
        return call(
            latent_layer,
            (ids, *arrived, own_rows, allowed, w_qkv, w_out, gain_pair, w_ff),
            latent_outs,
            spaces={0: SMEM, 8: pl.ANY},
            scratch=[
                pltpu.VMEM((rows, 3 * D), BF),
                pltpu.VMEM((8, HD, GROUP), BF),
                pltpu.VMEM((rows, D), BF),
                pltpu.VMEM((2, 3, step, D), BF),
                pltpu.VMEM((rows, D), F32),
                pltpu.VMEM((rows, D), F32),
                pltpu.VMEM((rows, 3 * D), BF),
                pltpu.SemaphoreType.DMA((2,)),
            ],
        )

    def turn():
        return nothing(latent_outs[:5]) + call(
            turn_encoder, (pn, o_a, o_b, bn_lo, bn_a, bn_b), latent_outs[5:]
        )

    latents, dhb, latent_gain, norms, lat_grads, packed = lax.cond(second, latent, turn)
    returned = along(dhb, -1)

    packed_far = swap(packed, "core")

    share = units // 16
    ff_block = ((4, 3 * share, HALF), BF)
    ff_half = ((4, 3 * share, GROUP), BF)
    ff_own, ff_right, ff_left, ff_far_a, ff_far_b = on_section(
        second,
        ff_weights_grad,
        (ids, packed, packed_far, norms),
        [ff_block, ff_block, ff_block, ff_half, ff_half],
        spaces={0: SMEM},
    )
    from_left = plane_shift(ff_far_a, 0, 1, (1,))
    from_right = plane_shift(ff_far_b, 0, -1, (1,))

    grads_long = ((2304, HALF), BF)
    enc_grads, enc_other = on_section(
        first,
        encoder_attention_back,
        (ids, returned, w_out, q, k_lo, v_lo, k_a, k_b, v_a, v_b, w_a, w_b),
        [grads_long, grads_long],
        spaces={0: SMEM},
    )
    enc_far = swap(enc_other, "core", (0,))
    outs = [((4, 256, HALF), BF)] * 4
    blocks = lax.cond(
        first,
        lambda: call(encoder_weights, (ids, packed, packed_far, enc_grads, enc_far), outs, spaces={0: SMEM}),
        lambda: call(latent_weights, (ids, packed, packed_far, lat_grads), outs, spaces={0: SMEM}),
    )
    got = exchange(blocks, 0)
    up_grad, up_gain = on_section(
        first,
        encoder_upper_back,
        (ids, up_a, up_b, w_qkv, gain_pair, enc_grads, enc_other, blocks[0]),
        [tall, ((1, D), F32)],
        spaces={0: SMEM, 7: pl.ANY},
    )
    up_arrived = along(up_grad, 1)
    low_outs = [((rows, D), F32), tall, ((2, D), F32)]

    def lower_grads():
        parts = call(
            encoder_lower_back,
            (ids, returned, own_rows, lower, w_qkv, gain_pair, enc_grads, enc_other, up_gain),
            low_outs,
            spaces={0: SMEM, 8: pl.ANY},
        )
        return (*parts, *nothing([ff_block, ff_block]))

    def ff_middle():
        added = call(
            ff_add, (ff_right, ff_left, from_left, from_right, up_gain), [ff_block, ff_block], spaces={4: pl.ANY}
        )
        return (*nothing(low_outs), *added)

    patch_grad, low_grad, encoder_gain, ff_right_sum, ff_left_sum = lax.cond(first, lower_grads, ff_middle)
    line = [((272, HALF), BF)]
    blocks = call(
        attn_sum_first_gain,
        (ids, blocks[0], *got, encoder_gain, up_gain, latent_gain),
        line * 4,
        spaces={0: SMEM},
    )
    ff_right_sum, ff_left_sum, _ = lax.optimization_barrier((ff_right_sum, ff_left_sum, blocks))
    from_left = plane_shift(ff_right_sum, 0, 1, (1,))
    from_right = plane_shift(ff_left_sum, 0, -1, (1,))
    met, up_arrived = lax.optimization_barrier((exchange(blocks, 1), up_arrived))
    (block,) = call(sum_all, (blocks[0], *met), line)
    (block,) = call(sum_all, (block, swap(block, "zh")), line)
    (block,) = call(stack_rows, collect(block, 1), [((1040, HALF), BF)])
    pieces = collect(block, 0)
    own_far = swap(block, "core")
    from_left, from_right, first_piece = lax.optimization_barrier((from_left, from_right, pieces[1]))
    pieces[1] = first_piece
    ff_line = ((3 * share, HALF), BF)
    ff_blocks = on_section(
        second, ff_sum_first, (ids, ff_own, from_left, from_right), [ff_line] * 4, spaces={0: SMEM}
    )
    ff_got = exchange(ff_blocks, 1, (1,))
    (ff_sum,) = on_section(second, ff_sum_second, (ff_blocks[0], *ff_got), [ff_line])
    ff_sum = ff_sum.reshape(3, 2, share // 2, HALF)
    ff_far = swap(pick(ff_sum, 1 - zh, 1), "zh", (1,))
    ff_sum = (pick(ff_sum, zh, 1).astype(F32) + ff_far.astype(F32)).astype(BF).reshape(3, 2, share // 4, HALF)
    ff_mine = pick(ff_sum, core, 1)
    ff_far = swap(pick(ff_sum, 1 - core, 1), "core", (1,))

    def ff_result():
        low, high = jnp.where(core == 0, ff_mine, ff_far), jnp.where(core == 0, ff_far, ff_mine)
        return jnp.swapaxes(jnp.concatenate([low, high], 2), 0, 1).astype(F32)

    ff_grad = lax.cond(second, ff_result, lambda: jnp.zeros((share // 4, 3, D), F32))
    byte_grad = jnp.where(first, low_grad, up_arrived)
    patch_out = jnp.where(first, patch_grad, latents)
    pieces = pieces + [own_far] + [swap(p, "core") for p in pieces[1:]]
    whole = lambda p: pl.BlockSpec(p.shape, lambda i, n=p.ndim: (0,) * n)
    total_qkv, total_out, total_gain = pl.pallas_call(
        final_attn,
        grid=(4,),
        out_shape=[
            jax.ShapeDtypeStruct((D, 3 * D), F32),
            jax.ShapeDtypeStruct((D, D), F32),
            jax.ShapeDtypeStruct((2, D), F32),
        ],
        in_specs=[pl.BlockSpec(memory_space=SMEM)] + [whole(p) for p in pieces],
        out_specs=[
            pl.BlockSpec((256, 3 * D), lambda i: (i, 0)),
            pl.BlockSpec((256, D), lambda i: (i, 0)),
            pl.BlockSpec((2, D), lambda i: (0, 0)),
        ],
        compiler_params=pltpu.CompilerParams(vmem_limit_bytes=FINAL_VMEM),
    )(ids, *pieces)
    return (
        patch_out.reshape(1, micro, 1, seq, D),
        byte_grad.reshape(micro, 1, half_bytes, D),
        total_qkv[None],
        total_out[None],
        total_gain[None],
        ff_grad[None],
    )


def solution(mesh):
    fine = Mesh(mesh.devices.reshape(2, 4, 4, 2, 2), ("s",) + BATCH)
    in_specs = (
        P("s", None, BATCH, None, None),
        P(None, BATCH, "s", None),
        P(None, BATCH, None),
        P(None, BATCH, None),
        P("s", None, None),
        P("s", None, None),
        P("s", None, None),
        P(),
    )
    out_specs = (
        P("s", None, BATCH, None, None),
        P(None, BATCH, "s", None),
        P("s", None, None),
        P("s", None, None),
        P("s", None, None),
        P("s", BATCH, None, None),
    )
    return jax.shard_map(shards, mesh=fine, in_specs=in_specs, out_specs=out_specs, check_vma=False)
```

```python
import functools
import math

import jax
import jax.numpy as jnp
from jax import lax
from jax.experimental import pallas as pl
from jax.experimental.pallas import tpu as pltpu
from jax.sharding import Mesh
from jax.sharding import PartitionSpec as P

HD = 64
SCALE = HD**-0.5
EPS = 1e-05
NEG = -1e30
BATCH = ("y", "x", "zh", "core")
BF = jnp.bfloat16
F32 = jnp.float32
D = 1024
HALF = 512
GROUP = 256
FINAL_VMEM = 32 * 1024 * 1024


UNITS = 2816
PACK_NORMS = 3 * UNITS
PACK_LEFT = PACK_NORMS + 4 * 256
PACK_GRADS = PACK_LEFT + 2 * D
PACK_ROWS = PACK_GRADS + 4 * 512


def nn(a, b):
    return lax.dot_general(a, b, (((1,), (0,)), ((), ())), preferred_element_type=F32)


def nt(a, b):
    return lax.dot_general(a, b, (((1,), (1,)), ((), ())), preferred_element_type=F32)


def tn(a, b):
    return lax.dot_general(a, b, (((0,), (0,)), ((), ())), preferred_element_type=F32)


def inverse_rms(x):
    return lax.rsqrt(jnp.mean(x * x, axis=-1, keepdims=True) + EPS)


def norm_back(x, gain, up):
    r = inverse_rms(x)
    scaled = up * gain
    inner = jnp.mean(scaled * x, axis=-1, keepdims=True)
    return r * (scaled - x * (r * r * inner)), up * (x * r)


def stack_heads(rows):
    head = lax.broadcasted_iota(jnp.int32, rows.shape, 1) // HD
    return jnp.concatenate([jnp.where(head == h, rows, jnp.zeros_like(rows)) for h in range(4)], 0)


def unstack_heads(stacked):
    head = lax.broadcasted_iota(jnp.int32, (HD, GROUP), 1) // HD
    out = stacked[0:HD]
    for h in range(1, 4):
        out = jnp.where(head == h, stacked[h * HD : (h + 1) * HD], out)
    return out


def softmax_columns(scores):
    top = functools.reduce(jnp.maximum, [jnp.max(s, axis=0, keepdims=True) for s in scores])
    parts = [jnp.exp(s - top) for s in scores]
    inverse = 1.0 / sum(jnp.sum(p, axis=0, keepdims=True) for p in parts)
    return [(p * inverse).astype(BF) for p in parts]


def encode_lower(patch, low, w_qkv, gains, pn, q, bn, k, v):
    x = patch[...].astype(F32)
    normed = (x * inverse_rms(x) * gains[0:1]).astype(BF)
    pn[...] = normed
    q[...] = nn(normed, w_qkv[:, 0:D]).astype(BF)
    for i in range(2):
        at = pl.ds(i * 256, 256)
        b = low[at, :].astype(F32)
        normed = (b * inverse_rms(b) * gains[1:2]).astype(BF)
        bn[at, :] = normed
        k[at, :] = nn(normed, w_qkv[:, D : 2 * D]).astype(BF)
        v[at, :] = nn(normed, w_qkv[:, 2 * D :]).astype(BF)


def encode_rest(m, patch, up, w_qkv, w_out, gains, bounds, q, k_lo, v_lo, hb, o1, weights, bn, k, v):
    b = up[...].astype(F32)
    normed = (b * inverse_rms(b) * gains[1:2]).astype(BF)
    bn[...] = normed
    k[...] = nn(normed, w_qkv[:, D : 2 * D]).astype(BF)
    v[...] = nn(normed, w_qkv[:, 2 * D :]).astype(BF)
    spot = lax.broadcasted_iota(jnp.int32, (256, GROUP), 0)
    start = bounds[m, 0:1, :]
    end = bounds[m, 1:2, :]
    inside = [(spot + h * 256 >= start) & (spot + h * 256 < end) for h in range(2)]
    low_at = slice(m * 256, (m + 1) * 256)
    rows = slice(m * HD, (m + 1) * HD)
    for g in range(4):
        lanes = slice(g * GROUP, (g + 1) * GROUP)
        stacked = stack_heads(q[rows, lanes] * BF(SCALE))
        scores = [
            jnp.where(inside[h], nt(keys, stacked), NEG)
            for h, keys in enumerate((k_lo[low_at, lanes], k[:, lanes]))
        ]
        w = softmax_columns(scores)
        weights[g * 2] = w[0]
        weights[g * 2 + 1] = w[1]
        mixed = tn(w[0], v_lo[low_at, lanes]) + tn(w[1], v[:, lanes])
        o1[:, lanes] = unstack_heads(mixed).astype(BF)
    hb[...] = (patch[rows, :].astype(F32) + nn(o1[...], w_out[...])).astype(BF)


def latent_layer(
    ids, hb_a, hb_b, cot, allowed, w_qkv, w_out, gains, w_ff,
    latents, dhb, gain_grad, norms, grads, packed,
    qkv, weights, o2, ff_buf, acc_out, acc_norm, dqkv, sems,
):
    core = ids[0]
    units = w_ff.shape[1]
    step = ff_buf.shape[2]
    steps = units // step

    def fetch(i, slot):
        return pltpu.make_async_copy(
            w_ff.at[:, pl.ds(pl.multiple_of(i * step, 128), step), :], ff_buf.at[slot], sems.at[slot]
        )

    fetch(0, 0).start()
    x = jnp.concatenate([hb_a[...], hb_b[...]], 0).astype(F32)
    normed = (x * inverse_rms(x) * gains[0:1]).astype(BF)
    packed[PACK_LEFT : PACK_LEFT + D, :] = normed.T
    qkv[...] = nn(normed, w_qkv[...]).astype(BF)
    for m in range(2):
        rows = slice(m * HD, (m + 1) * HD)
        for g in range(4):
            lanes = slice(g * GROUP, (g + 1) * GROUP)
            k_lanes = slice(D + g * GROUP, D + (g + 1) * GROUP)
            v_lanes = slice(2 * D + g * GROUP, 2 * D + (g + 1) * GROUP)
            stacked = stack_heads(qkv[rows, lanes] * BF(SCALE))
            scores = jnp.where(allowed[m] > 0.5, nt(qkv[rows, k_lanes], stacked), NEG)
            (w,) = softmax_columns([scores])
            weights[m * 4 + g] = w
            o2[rows, lanes] = unstack_heads(tn(w, qkv[rows, v_lanes])).astype(BF)
    packed[PACK_LEFT + D : PACK_LEFT + 2 * D, :] = o2[...].T
    after = x + nn(o2[...], w_out[...])
    yn = (after * inverse_rms(after) * gains[1:2]).astype(BF)
    c = cot[...]
    for h in range(2):

        @pl.when(core == h)
        def _(h=h):
            norms[0:128, :] = yn[:, h * HALF : (h + 1) * HALF]
            norms[128:256, :] = c[:, h * HALF : (h + 1) * HALF]

        @pl.when(core != h)
        def _(h=h):
            for b in range(4):
                lanes = slice(h * HALF + b * 128, h * HALF + (b + 1) * 128)
                packed[PACK_NORMS + b * 256 : PACK_NORMS + b * 256 + 128, :] = yn[:, lanes]
                packed[PACK_NORMS + b * 256 + 128 : PACK_NORMS + (b + 1) * 256, :] = c[:, lanes]

    acc_out[...] = after
    acc_norm[...] = jnp.zeros_like(acc_norm)

    def ff_step(i, carry):
        slot = lax.rem(i, 2)

        @pl.when(i + 1 < steps)
        def _():
            fetch(i + 1, 1 - slot).start()

        fetch(i, slot).wait()
        w_gate, w_up, w_down = ff_buf.at[slot, 0], ff_buf.at[slot, 1], ff_buf.at[slot, 2]
        gate = nt(yn, w_gate[...])
        upward = nt(yn, w_up[...])
        du = nt(c, w_down[...])
        sig = 1.0 / (1.0 + jnp.exp(-gate))
        active = gate * sig
        hidden = (active * upward).astype(BF)
        d_gate = (du * upward * (sig * (1.0 + gate * (1.0 - sig)))).astype(BF)
        d_up = (du * active).astype(BF)
        at = pl.ds(pl.multiple_of(i * step, 128), step)
        for j, value in enumerate((d_gate, d_up, hidden)):
            packed[pl.ds(pl.multiple_of(i * step + j * units, 128), step), :] = value.T
        acc_out[...] += nn(hidden, w_down[...])
        acc_norm[...] += nn(d_gate, w_gate[...]) + nn(d_up, w_up[...])
        return carry

    lax.fori_loop(0, steps, ff_step, 0)
    latents[...] = acc_out[...]
    back, gain_rows = norm_back(after, gains[1:2], acc_norm[...])
    gain_grad[1:2, :] = jnp.sum(gain_rows, axis=0, keepdims=True)
    d_after = c.astype(F32) + back
    da = d_after.astype(BF)
    d_mixed = nt(da, w_out[...]).astype(BF)
    for m in range(2):
        rows = slice(m * HD, (m + 1) * HD)
        for g in range(4):
            lanes = slice(g * GROUP, (g + 1) * GROUP)
            k_lanes = slice(D + g * GROUP, D + (g + 1) * GROUP)
            v_lanes = slice(2 * D + g * GROUP, 2 * D + (g + 1) * GROUP)
            q_stacked = stack_heads(qkv[rows, lanes] * BF(SCALE))
            o_stacked = stack_heads(d_mixed[rows, lanes])
            w_low = weights[m * 4 + g]
            w = w_low.astype(F32)
            dw = nt(qkv[rows, v_lanes], o_stacked)
            inner = jnp.sum(dw * w, axis=0, keepdims=True)
            ds = (w * (dw - inner)).astype(BF)
            dqkv[rows, lanes] = (unstack_heads(tn(ds, qkv[rows, k_lanes])) * SCALE).astype(BF)
            dqkv[rows, k_lanes] = nn(ds, q_stacked).astype(BF)
            dqkv[rows, v_lanes] = nn(w_low, o_stacked).astype(BF)
    d_normed = nt(dqkv[...], w_qkv[...])
    back, gain_rows = norm_back(x, gains[0:1], d_normed)
    gain_grad[0:1, :] = jnp.sum(gain_rows, axis=0, keepdims=True)
    dhb[...] = (d_after + back).astype(BF)
    for h in range(2):
        pieces = (
            dqkv[:, h * HALF : (h + 1) * HALF],
            da[:, h * HALF : (h + 1) * HALF],
            dqkv[:, D + h * HALF : D + (h + 1) * HALF],
            dqkv[:, 2 * D + h * HALF : 2 * D + (h + 1) * HALF],
        )

        @pl.when(core == h)
        def _(pieces=pieces):
            for i, value in enumerate(pieces):
                grads[i * 128 : (i + 1) * 128, :] = value

        @pl.when(core != h)
        def _(pieces=pieces):
            for i, value in enumerate(pieces):
                for b in range(4):
                    first = PACK_GRADS + b * 512 + i * 128
                    packed[first : first + 128, :] = value[:, b * 128 : (b + 1) * 128]


def half_of(core, g, mine, other):
    lanes = slice((g % 2) * GROUP, (g % 2 + 1) * GROUP)

    def put(at, value):
        @pl.when(core == g // 2)
        def _():
            mine[at, lanes] = value

        @pl.when(core != g // 2)
        def _():
            other[at, lanes] = value

    return put


def encoder_attention_back(
    ids, dhb, w_out, q, k_lo, v_lo, k_a, k_b, v_a, v_b, w_a, w_b, mine, other
):
    d_mixed = nt(dhb[...], w_out[...]).astype(BF)
    for g in range(4):
        lanes = slice(g * GROUP, (g + 1) * GROUP)
        put = half_of(ids[0], g, mine, other)
        put(slice(128, 256), dhb[:, lanes])
        for m, (k_up, v_up, weights) in enumerate(((k_a, v_a, w_a), (k_b, v_b, w_b))):
            rows = slice(m * HD, (m + 1) * HD)
            low_at = slice(m * 256, (m + 1) * 256)
            q_stacked = stack_heads(q[rows, lanes] * BF(SCALE))
            o_stacked = stack_heads(d_mixed[rows, lanes])
            low = [weights[g * 2 + h] for h in range(2)]
            w = [piece.astype(F32) for piece in low]
            dw = [nt(values, o_stacked) for values in (v_lo[low_at, lanes], v_up[:, lanes])]
            inner = sum(jnp.sum(a * b, axis=0, keepdims=True) for a, b in zip(dw, w))
            ds = [(b * (a - inner)).astype(BF) for a, b in zip(dw, w)]
            dq = tn(ds[0], k_lo[low_at, lanes]) + tn(ds[1], k_up[:, lanes])
            put(rows, (unstack_heads(dq) * SCALE).astype(BF))
            for h in range(2):
                base = h * HALF + m * 256
                put(slice(256 + base, 512 + base), nn(ds[h], q_stacked).astype(BF))
                put(slice(1280 + base, 1536 + base), nn(low[h], o_stacked).astype(BF))


def both_columns(core, block, w_qkv):
    return [
        w_qkv[:, pl.ds(pl.multiple_of(block * D + which * HALF, HALF), HALF)] for which in (core, 1 - core)
    ]


def bytes_back(core, h, m, source, w_qkv, gains, grads):
    d_norm = sum(
        nt(ref[1024 * block - 768 + h * HALF + m * 256 : 1024 * block - 512 + h * HALF + m * 256, :], columns)
        for block in (1, 2)
        for ref, columns in zip(grads, both_columns(core, block, w_qkv))
    )
    back, gain_rows = norm_back(source.astype(F32), gains[1:2], d_norm)
    return back.astype(BF), jnp.sum(gain_rows, axis=0, keepdims=True)


def encoder_upper_back(ids, up_a, up_b, w_qkv, gains, mine, other, up_grad, gain_grad):
    total = jnp.zeros((1, D), F32)
    for m, source in enumerate((up_a, up_b)):
        back, rows = bytes_back(ids[0], 1, m, source[...], w_qkv, gains, (mine, other))
        up_grad[m * 256 : (m + 1) * 256, :] = back
        total = total + rows
    gain_grad[...] = total


def encoder_lower_back(
    ids, dhb, patch, low, w_qkv, gains, mine, other, after, patch_grad, low_grad, gain_grad
):
    core = ids[0]
    up_norm = sum(nt(ref[0:128, :], columns) for ref, columns in zip((mine, other), both_columns(core, 0, w_qkv)))
    back, gain_rows = norm_back(patch[...].astype(F32), gains[0:1], up_norm)
    gain_grad[0:1, :] = jnp.sum(gain_rows, axis=0, keepdims=True)
    patch_grad[...] = dhb[...].astype(F32) + back
    total = jnp.zeros((1, D), F32)
    for m in range(2):
        at = slice(m * 256, (m + 1) * 256)
        back, rows = bytes_back(core, 0, m, low[at, :], w_qkv, gains, (mine, other))
        low_grad[at, :] = back
        total = total + rows
    gain_grad[1:2, :] = total


def turn_encoder(pn, o_a, o_b, bn_lo, bn_a, bn_b, packed):
    for b, rows in enumerate([bn_lo[i * 128 : (i + 1) * 128, :] for i in range(4)]
                             + [ref[i * 128 : (i + 1) * 128, :] for ref in (bn_a, bn_b) for i in range(2)]):
        packed[b * D : (b + 1) * D, :] = rows.T
    packed[PACK_LEFT : PACK_LEFT + D, :] = pn[...].T
    packed[PACK_LEFT + D : PACK_LEFT + 2 * D, :] = jnp.concatenate([o_a[...], o_b[...]], 0).T


def rows_of_both(left, left_far, at):
    return jnp.concatenate([left[at, :], left_far[at, :]], 1)


def below(near, far, rows):
    return jnp.concatenate([near[rows, :], far[rows, :]], 0)


def encoder_weights(ids, packed, packed_far, near, far, *blocks):
    u = ids[1]
    queries = below(near, far, slice(0, 128))
    outputs = below(near, far, slice(128, 256))
    for k in range(4):
        first = lax.rem(u + k, 4) * 256

        def at(base, first=first):
            return pl.ds(pl.multiple_of(first + base, 256), 256)

        blocks[k][0] = nn(rows_of_both(packed, packed_far, at(PACK_LEFT)), queries).astype(BF)
        blocks[k][3] = nn(rows_of_both(packed, packed_far, at(PACK_LEFT + D)), outputs).astype(BF)
        lefts = [jnp.concatenate([ref[at(b * D), :] for b in range(8)], 1) for ref in (packed, packed_far)]
        for block in (1, 2):
            rows = slice(1024 * block - 768, 1024 * block + 256)
            blocks[k][block] = (nn(lefts[0], near[rows, :]) + nn(lefts[1], far[rows, :])).astype(BF)


def unpack(packed, first, rows):
    return jnp.concatenate([packed[first + b * rows : first + (b + 1) * rows, :] for b in range(4)], 1)


def latent_weights(ids, packed, packed_far, near, *blocks):
    u = ids[1]
    far = unpack(packed_far, PACK_GRADS, 512)
    rights = [jnp.concatenate([near[i * 128 : (i + 1) * 128, :], far[i * 128 : (i + 1) * 128, :]], 0) for i in range(4)]
    for k in range(4):
        first = PACK_LEFT + lax.rem(u + k, 4) * 256
        at = pl.ds(pl.multiple_of(first, 256), 256)
        low_at = pl.ds(pl.multiple_of(first + D, 256), 256)
        for block, (source, i) in enumerate(((at, 0), (at, 2), (at, 3), (low_at, 1))):
            blocks[k][block] = nn(rows_of_both(packed, packed_far, source), rights[i]).astype(BF)


def attn_weights(ids, packed, packed_far, near, far, lat_near, after, *blocks):
    @pl.when(ids[4] == 0)
    def _():
        encoder_weights(ids, packed, packed_far, near, far, *blocks)

    @pl.when(ids[4] == 1)
    def _():
        latent_weights(ids, packed, packed_far, lat_near, *blocks)


def ff_weights_grad(ids, packed, packed_far, norms, own, right, left, far_a, far_b):
    core, u = ids[0], ids[1]
    share = UNITS // 16
    far = unpack(packed_far, PACK_NORMS, 256)
    normed = jnp.concatenate([norms[0:128, :], far[0:128, :]], 0)
    cot = jnp.concatenate([norms[128:256, :], far[128:256, :]], 0)
    for k in range(4):
        there = lax.rem(u + k, 4)
        for v in range(4):
            chunk = jnp.where(core == 0, there * 4 + v, v * 4 + there)
            for j in range(3):
                at = pl.ds(pl.multiple_of(j * UNITS + chunk * share, 16), share)
                value = nn(rows_of_both(packed, packed_far, at), normed if j < 2 else cot).astype(BF)
                rows = slice(j * share, (j + 1) * share)
                if k == 2:
                    far_a[v, rows, :] = value[:, :GROUP]
                    far_b[v, rows, :] = value[:, GROUP:]
                else:
                    (own, right, None, left)[k][v, rows, :] = value


def ff_add(ids, right, left, from_left, from_right, after, new_right, new_left):
    new_right[:, :, 0:GROUP] = (right[:, :, 0:GROUP].astype(F32) + from_left[...].astype(F32)).astype(BF)
    new_right[:, :, GROUP:] = right[:, :, GROUP:]
    new_left[:, :, 0:GROUP] = left[:, :, 0:GROUP]
    new_left[:, :, GROUP:] = (left[:, :, GROUP:].astype(F32) + from_right[...].astype(F32)).astype(BF)


def sum_four(own, a, b, c):
    return own.astype(F32) + a.astype(F32) + b.astype(F32) + c.astype(F32)


def pack_gain(value):
    high = value.astype(BF)
    low = (value - high.astype(F32)).astype(BF)
    return jnp.concatenate(
        [high.astype(F32), low.astype(F32), jnp.zeros((8, HALF), F32)], 0
    ).astype(BF)


def unpack_gain(rows):
    rows = rows.astype(F32)
    return rows[0:4] + rows[4:8]


GAIN_AT = slice(256, 272)


def attn_sum_first(ids, own, a, b, c, *outs):
    v = ids[2]
    for k in range(4):
        at = pl.ds(pl.multiple_of(lax.rem(v + k, 4) * HD, HD), HD)
        for block in range(4):
            outs[k][block * HD : (block + 1) * HD, :] = sum_four(
                own[block, at, :], a[block, at, :], b[block, at, :], c[block, at, :]
            ).astype(BF)


def attn_sum_first_gain(ids, own, a, b, c, enc_gain, up_gain, lat_gain, *outs):
    attn_sum_first(ids, own, a, b, c, *outs)
    first = ids[4] == 0
    gain = jnp.where(
        first, jnp.concatenate([enc_gain[0:1, :], enc_gain[1:2, :] + up_gain[...]], 0), lat_gain[...]
    )
    halves = [gain[i : i + 1, h * HALF : (h + 1) * HALF] for i in range(2) for h in range(2)]
    packed = pack_gain(jnp.concatenate(halves, 0))
    for out in outs:
        out[GAIN_AT, :] = packed


def sum_all(*refs):
    refs, out = refs[:-1], refs[-1]
    out[0:256, :] = sum(ref[0:256, :].astype(F32) for ref in refs).astype(BF)
    out[GAIN_AT, :] = pack_gain(sum(unpack_gain(ref[GAIN_AT, :]) for ref in refs))


def stack_rows(*refs):
    refs, out = refs[:-1], refs[-1]
    for j, ref in enumerate(refs):
        out[j * 256 : (j + 1) * 256, :] = ref[0:256, :]
    out[1024:1040, :] = refs[0][GAIN_AT, :]


def ff_sum_first(ids, own, a, b, *outs):
    v = ids[2]
    for k in range(4):
        at = lax.rem(v + k, 4)
        outs[k][...] = (own[at].astype(F32) + a[at].astype(F32) + b[at].astype(F32)).astype(BF)


def ff_sum_second(ids, own, a, b, c, out):
    out[...] = sum_four(own[...], a[...], b[...], c[...]).astype(BF)


def final_attn(ids, *refs):
    pieces, (qkv, out, gain) = refs[:8], refs[8:]
    step = pl.program_id(0)
    for side in range(2):
        core = ids[0] if side == 0 else 1 - ids[0]
        u = ids[1] if side == 0 else ids[2]
        v = ids[2] if side == 0 else ids[1]
        for k in range(4):
            piece = pieces[side * 4 + k]

            @pl.when(lax.rem(u + k, 4) == step)
            def _(piece=piece, v=v, core=core):
                for j in range(4):
                    at = pl.ds(pl.multiple_of(lax.rem(v + j, 4) * HD, HD), HD)
                    for block in range(4):
                        target, column = (qkv, block * D) if block < 3 else (out, 0)
                        lanes = pl.ds(pl.multiple_of(core * HALF + column, HALF), HALF)
                        first = j * 256 + block * HD
                        target[at, lanes] = piece[first : first + HD, :].astype(F32)

    mine = sum(unpack_gain(piece[1024:1040, :]) for piece in pieces[:4])
    other = sum(unpack_gain(piece[1024:1040, :]) for piece in pieces[4:])
    total = mine + other
    for i in range(2):
        for h in range(2):
            gain[i : i + 1, h * HALF : (h + 1) * HALF] = total[2 * i + h : 2 * i + h + 1, :]


SMEM = pltpu.MemorySpace.SMEM
VMEM = pltpu.MemorySpace.VMEM


def size(shape, dtype):
    return math.prod(shape) * jnp.dtype(dtype).itemsize


def call(kernel, args, outs, scratch=(), spaces=None, spare=6):
    spaces = spaces or {}
    vmem = sum(size(a.shape, a.dtype) for i, a in enumerate(args) if i not in spaces)
    vmem += sum(size(*o) for o in outs)
    vmem += sum(size(s.shape, s.dtype) for s in scratch if hasattr(s, "shape") and s.memory_space == VMEM)
    specs = [pl.BlockSpec(memory_space=spaces.get(i, VMEM)) for i in range(len(args))]
    return pl.pallas_call(
        kernel,
        out_shape=[jax.ShapeDtypeStruct(s, t) for s, t in outs],
        in_specs=specs,
        out_specs=[pl.BlockSpec(memory_space=VMEM) for _ in outs],
        scratch_shapes=list(scratch),
        compiler_params=pltpu.CompilerParams(vmem_limit_bytes=vmem + spare * 1024 * 1024),
    )(*args)


def nothing(outs):
    def kernel(*refs):
        pass

    return pl.pallas_call(
        kernel,
        out_shape=[jax.ShapeDtypeStruct(s, t) for s, t in outs],
        out_specs=[pl.BlockSpec(memory_space=pl.ANY) for _ in outs],
    )()


def in_section(section, kernel):
    def guarded(ids, *refs):
        @pl.when(ids[4] == section)
        def _():
            kernel(ids, *refs)

    return guarded


def on_section(flag, kernel, args, outs, **rest):
    return lax.cond(
        flag, lambda: call(kernel, args, outs, **rest), lambda: nothing(outs)
    )


def along(value, by):
    return lax.ppermute(value, "s", [(0, 1)] if by > 0 else [(1, 0)])


def swap(value, axis, sections=(0, 1)):
    pairs = [(s * 2 + i, s * 2 + 1 - i) for s in sections for i in range(2)]
    return lax.ppermute(value, ("s", axis), pairs)


def plane_shift(value, which, by, sections=(0, 1)):
    pairs = []
    for s in sections:
        for y in range(4):
            for x in range(4):
                for core in range(2):
                    ty, tx = ((y + by) % 4, x) if core == which else (y, (x + by) % 4)
                    pairs.append((((s * 4 + y) * 4 + x) * 2 + core, ((s * 4 + ty) * 4 + tx) * 2 + core))
    return lax.ppermute(value, ("s", "y", "x", "core"), pairs)


def exchange(blocks, which, sections=(0, 1)):
    return [plane_shift(blocks[k], which, k, sections) for k in (1, 2, 3)]


def collect(block, which):
    return [block] + [plane_shift(block, which, -k) for k in (1, 2, 3)]


def pick(stack, index, dim):
    return lax.dynamic_index_in_dim(stack, index, dim, keepdims=False)


def shards(patch_io, byte_states, patch_lengths, patch_live, attn_qkv, attn_out, gains, ff_weights):
    section = lax.axis_index("s")
    core = lax.axis_index("core")
    zh = lax.axis_index("zh")
    y, x = lax.axis_index("y"), lax.axis_index("x")
    first = section == 0
    second = section == 1
    ids = jnp.stack([core, jnp.where(core == 0, y, x), jnp.where(core == 0, x, y), zh, section])
    ids = ids.astype(jnp.int32)
    w_qkv = attn_qkv[0]
    w_out = attn_out[0]
    gain_pair = gains[0]
    micro, seq = patch_io.shape[1], patch_io.shape[3]
    half_bytes = byte_states.shape[2]
    units = ff_weights.shape[0]
    rows = micro * seq
    own_rows = patch_io.reshape(rows, D)
    up_a = along(byte_states[0, 0], -1)
    up_b = along(byte_states[1, 0], -1)
    lower = byte_states.reshape(micro * half_bytes, D)
    w_ff = jnp.swapaxes(ff_weights, 0, 1)
    lengths = patch_lengths[:, 0]
    live = patch_live[:, 0]
    ends = jnp.cumsum(lengths, axis=1)
    bounds = jnp.tile(jnp.stack([ends - lengths, ends], 1), (1, 1, 4))
    places = lax.iota(jnp.int32, seq)
    causal = places[:, None] <= places[None, :]
    diagonal = places[:, None] == places[None, :]
    allowed = causal[None] & ((live[:, :, None] == 1) | diagonal[None])
    allowed = lax.optimization_barrier(jnp.tile(allowed.astype(F32), (1, 1, 4)))

    wide = ((rows, D), BF)
    short = ((seq, D), BF)
    tall = ((micro * half_bytes, D), BF)
    piece = ((half_bytes, D), BF)
    pn, q, bn_lo, k_lo, v_lo = on_section(
        first, encode_lower, (own_rows, lower, w_qkv, gain_pair), [wide, wide, tall, tall, tall]
    )
    rest = []
    for m, up in enumerate((up_a, up_b)):
        rest.append(
            on_section(
                first,
                functools.partial(encode_rest, m),
                (own_rows, up, w_qkv, w_out, gain_pair, bounds, q, k_lo, v_lo),
                [short, short, ((8, 256, GROUP), BF), piece, piece, piece],
            )
        )
    (hb_a, o_a, w_a, bn_a, k_a, v_a), (hb_b, o_b, w_b, bn_b, k_b, v_b) = rest
    arrived = [along(hb_a, 1), along(hb_b, 1)]

    step = 256
    latent_outs = [
        ((rows, D), F32), wide, ((2, D), F32), ((256, HALF), BF), ((512, HALF), BF), ((PACK_ROWS, rows), BF),
    ]

    def latent():
        return call(
            latent_layer,
            (ids, *arrived, own_rows, allowed, w_qkv, w_out, gain_pair, w_ff),
            latent_outs,
            spaces={0: SMEM, 8: pl.ANY},
            scratch=[
                pltpu.VMEM((rows, 3 * D), BF),
                pltpu.VMEM((8, HD, GROUP), BF),
                pltpu.VMEM((rows, D), BF),
                pltpu.VMEM((2, 3, step, D), BF),
                pltpu.VMEM((rows, D), F32),
                pltpu.VMEM((rows, D), F32),
                pltpu.VMEM((rows, 3 * D), BF),
                pltpu.SemaphoreType.DMA((2,)),
            ],
        )

    def turn():
        return nothing(latent_outs[:5]) + call(
            turn_encoder, (pn, o_a, o_b, bn_lo, bn_a, bn_b), latent_outs[5:]
        )

    latents, dhb, latent_gain, norms, lat_grads, packed = lax.cond(second, latent, turn)
    returned = along(dhb, -1)

    packed_far = swap(packed, "core")

    share = units // 16
    ff_block = ((4, 3 * share, HALF), BF)
    ff_half = ((4, 3 * share, GROUP), BF)
    ff_own, ff_right, ff_left, ff_far_a, ff_far_b = call(
        in_section(1, ff_weights_grad),
        (ids, packed, packed_far, norms),
        [ff_block, ff_block, ff_block, ff_half, ff_half],
        spaces={0: SMEM},
    )
    from_left = plane_shift(ff_far_a, 0, 1, (1,))
    from_right = plane_shift(ff_far_b, 0, -1, (1,))

    grads_long = ((2304, HALF), BF)
    enc_grads, enc_other = on_section(
        first,
        encoder_attention_back,
        (ids, returned, w_out, q, k_lo, v_lo, k_a, k_b, v_a, v_b, w_a, w_b),
        [grads_long, grads_long],
        spaces={0: SMEM},
    )
    enc_far = swap(enc_other, "core", (0,))
    up_grad, up_gain = on_section(
        first,
        encoder_upper_back,
        (ids, up_a, up_b, w_qkv, gain_pair, enc_grads, enc_other),
        [tall, ((1, D), F32)],
        spaces={0: SMEM},
    )
    up_arrived = along(up_grad, 1)
    outs = [((4, 256, HALF), BF)] * 4
    blocks = call(
        attn_weights,
        (ids, packed, packed_far, enc_grads, enc_far, lat_grads, up_gain),
        outs,
        spaces={0: SMEM, 6: pl.ANY},
    )
    blocks, from_left, from_right = lax.optimization_barrier((blocks, from_left, from_right))
    got, up_arrived = lax.optimization_barrier((exchange(blocks, 0), up_arrived))
    ff_right_sum, ff_left_sum = call(
        in_section(1, ff_add),
        (ids, ff_right, ff_left, from_left, from_right, blocks[0]),
        [ff_block, ff_block],
        spaces={0: SMEM, 5: pl.ANY},
    )
    patch_grad, low_grad, encoder_gain = on_section(
        first,
        encoder_lower_back,
        (ids, returned, own_rows, lower, w_qkv, gain_pair, enc_grads, enc_other, blocks[0]),
        [((rows, D), F32), tall, ((2, D), F32)],
        spaces={0: SMEM, 8: pl.ANY},
    )
    line = [((272, HALF), BF)]
    blocks = call(
        attn_sum_first_gain,
        (ids, blocks[0], *got, encoder_gain, up_gain, latent_gain),
        line * 4,
        spaces={0: SMEM},
    )
    ff_right_sum, ff_left_sum, _ = lax.optimization_barrier((ff_right_sum, ff_left_sum, blocks))
    from_left = plane_shift(ff_right_sum, 0, 1, (1,))
    from_right = plane_shift(ff_left_sum, 0, -1, (1,))
    (block,) = call(sum_all, (blocks[0], *exchange(blocks, 1)), line)
    (block,) = call(sum_all, (block, swap(block, "zh")), line)
    (block,) = call(stack_rows, collect(block, 1), [((1040, HALF), BF)])
    from_left, from_right, block = lax.optimization_barrier((from_left, from_right, block))
    pieces = collect(block, 0)
    own_far = swap(block, "core")
    ff_line = ((3 * share, HALF), BF)
    ff_blocks = call(
        in_section(1, ff_sum_first), (ids, ff_own, from_left, from_right), [ff_line] * 4, spaces={0: SMEM}
    )
    ff_got = exchange(ff_blocks, 1, (1,))
    (ff_sum,) = call(in_section(1, ff_sum_second), (ids, ff_blocks[0], *ff_got), [ff_line], spaces={0: SMEM})
    ff_sum = ff_sum.reshape(3, 2, share // 2, HALF)
    ff_far = swap(pick(ff_sum, 1 - zh, 1), "zh", (1,))
    ff_sum = (pick(ff_sum, zh, 1).astype(F32) + ff_far.astype(F32)).astype(BF).reshape(3, 2, share // 4, HALF)
    ff_mine = pick(ff_sum, core, 1)
    ff_far = swap(pick(ff_sum, 1 - core, 1), "core", (1,))

    def ff_result():
        low, high = jnp.where(core == 0, ff_mine, ff_far), jnp.where(core == 0, ff_far, ff_mine)
        return jnp.swapaxes(jnp.concatenate([low, high], 2), 0, 1).astype(F32)

    ff_grad = lax.cond(second, ff_result, lambda: jnp.zeros((share // 4, 3, D), F32))
    byte_grad = jnp.where(first, low_grad, up_arrived)
    patch_out = jnp.where(first, patch_grad, latents)
    patch_out, ff_grad, *pieces = lax.optimization_barrier((patch_out, ff_grad, *pieces))
    pieces = pieces + [own_far] + [swap(p, "core") for p in pieces[1:]]
    whole = lambda p: pl.BlockSpec(p.shape, lambda i, n=p.ndim: (0,) * n)
    total_qkv, total_out, total_gain = pl.pallas_call(
        final_attn,
        grid=(4,),
        out_shape=[
            jax.ShapeDtypeStruct((D, 3 * D), F32),
            jax.ShapeDtypeStruct((D, D), F32),
            jax.ShapeDtypeStruct((2, D), F32),
        ],
        in_specs=[pl.BlockSpec(memory_space=SMEM)] + [whole(p) for p in pieces],
        out_specs=[
            pl.BlockSpec((256, 3 * D), lambda i: (i, 0)),
            pl.BlockSpec((256, D), lambda i: (i, 0)),
            pl.BlockSpec((2, D), lambda i: (0, 0)),
        ],
        compiler_params=pltpu.CompilerParams(vmem_limit_bytes=FINAL_VMEM),
    )(ids, *pieces)
    return (
        patch_out.reshape(1, micro, 1, seq, D),
        byte_grad.reshape(micro, 1, half_bytes, D),
        total_qkv[None],
        total_out[None],
        total_gain[None],
        ff_grad[None],
    )


def solution(mesh):
    fine = Mesh(mesh.devices.reshape(2, 4, 4, 2, 2), ("s",) + BATCH)
    in_specs = (
        P("s", None, BATCH, None, None),
        P(None, BATCH, "s", None),
        P(None, BATCH, None),
        P(None, BATCH, None),
        P("s", None, None),
        P("s", None, None),
        P("s", None, None),
        P(),
    )
    out_specs = (
        P("s", None, BATCH, None, None),
        P(None, BATCH, "s", None),
        P("s", None, None),
        P("s", None, None),
        P("s", None, None),
        P("s", BATCH, None, None),
    )
    return jax.shard_map(shards, mesh=fine, in_specs=in_specs, out_specs=out_specs, check_vma=False)
```

```python
import functools
import math

import jax
import jax.numpy as jnp
from jax import lax
from jax.experimental import pallas as pl
from jax.experimental.pallas import tpu as pltpu
from jax.sharding import Mesh
from jax.sharding import PartitionSpec as P

HD = 64
SCALE = HD**-0.5
EPS = 1e-05
NEG = -1e30
BATCH = ("y", "x", "zh", "core")
BF = jnp.bfloat16
F32 = jnp.float32
D = 1024
HALF = 512
GROUP = 256
FINAL_VMEM = 32 * 1024 * 1024


UNITS = 2816
PACK_NORMS = 3 * UNITS
PACK_LEFT = PACK_NORMS + 4 * 256
PACK_GRADS = PACK_LEFT + 2 * D
PACK_ROWS = PACK_GRADS + 4 * 512


def nn(a, b):
    return lax.dot_general(a, b, (((1,), (0,)), ((), ())), preferred_element_type=F32)


def nt(a, b):
    return lax.dot_general(a, b, (((1,), (1,)), ((), ())), preferred_element_type=F32)


def tn(a, b):
    return lax.dot_general(a, b, (((0,), (0,)), ((), ())), preferred_element_type=F32)


def inverse_rms(x):
    return lax.rsqrt(jnp.mean(x * x, axis=-1, keepdims=True) + EPS)


def norm_back(x, gain, up):
    r = inverse_rms(x)
    scaled = up * gain
    inner = jnp.mean(scaled * x, axis=-1, keepdims=True)
    return r * (scaled - x * (r * r * inner)), up * (x * r)


def stack_heads(rows):
    head = lax.broadcasted_iota(jnp.int32, rows.shape, 1) // HD
    return jnp.concatenate([jnp.where(head == h, rows, jnp.zeros_like(rows)) for h in range(4)], 0)


def unstack_heads(stacked):
    head = lax.broadcasted_iota(jnp.int32, (HD, GROUP), 1) // HD
    out = stacked[0:HD]
    for h in range(1, 4):
        out = jnp.where(head == h, stacked[h * HD : (h + 1) * HD], out)
    return out


def softmax_columns(scores):
    top = functools.reduce(jnp.maximum, [jnp.max(s, axis=0, keepdims=True) for s in scores])
    parts = [jnp.exp(s - top) for s in scores]
    inverse = 1.0 / sum(jnp.sum(p, axis=0, keepdims=True) for p in parts)
    return [(p * inverse).astype(BF) for p in parts]


def encode_lower(patch, low, w_qkv, gains, pn, q, bn, k, v):
    x = patch[...].astype(F32)
    normed = (x * inverse_rms(x) * gains[0:1]).astype(BF)
    pn[...] = normed
    q[...] = nn(normed, w_qkv[:, 0:D]).astype(BF)
    for i in range(2):
        at = pl.ds(i * 256, 256)
        b = low[at, :].astype(F32)
        normed = (b * inverse_rms(b) * gains[1:2]).astype(BF)
        bn[at, :] = normed
        k[at, :] = nn(normed, w_qkv[:, D : 2 * D]).astype(BF)
        v[at, :] = nn(normed, w_qkv[:, 2 * D :]).astype(BF)


def encode_rest(m, patch, up, w_qkv, w_out, gains, bounds, q, k_lo, v_lo, hb, o1, weights, bn, k, v):
    b = up[...].astype(F32)
    normed = (b * inverse_rms(b) * gains[1:2]).astype(BF)
    bn[...] = normed
    k[...] = nn(normed, w_qkv[:, D : 2 * D]).astype(BF)
    v[...] = nn(normed, w_qkv[:, 2 * D :]).astype(BF)
    spot = lax.broadcasted_iota(jnp.int32, (256, GROUP), 0)
    start = bounds[m, 0:1, :]
    end = bounds[m, 1:2, :]
    inside = [(spot + h * 256 >= start) & (spot + h * 256 < end) for h in range(2)]
    low_at = slice(m * 256, (m + 1) * 256)
    rows = slice(m * HD, (m + 1) * HD)
    for g in range(4):
        lanes = slice(g * GROUP, (g + 1) * GROUP)
        stacked = stack_heads(q[rows, lanes] * BF(SCALE))
        scores = [
            jnp.where(inside[h], nt(keys, stacked), NEG)
            for h, keys in enumerate((k_lo[low_at, lanes], k[:, lanes]))
        ]
        w = softmax_columns(scores)
        weights[g * 2] = w[0]
        weights[g * 2 + 1] = w[1]
        mixed = tn(w[0], v_lo[low_at, lanes]) + tn(w[1], v[:, lanes])
        o1[:, lanes] = unstack_heads(mixed).astype(BF)
    hb[...] = (patch[rows, :].astype(F32) + nn(o1[...], w_out[...])).astype(BF)


def latent_layer(
    ids, hb_a, hb_b, cot, allowed, w_qkv, w_out, gains, w_ff,
    latents, dhb, gain_grad, norms, grads, packed,
    qkv, weights, o2, ff_buf, acc_out, acc_norm, dqkv, sems,
):
    core = ids[0]
    units = w_ff.shape[1]
    step = ff_buf.shape[2]
    steps = units // step

    def fetch(i, slot):
        return pltpu.make_async_copy(
            w_ff.at[:, pl.ds(pl.multiple_of(i * step, 128), step), :], ff_buf.at[slot], sems.at[slot]
        )

    fetch(0, 0).start()
    x = jnp.concatenate([hb_a[...], hb_b[...]], 0).astype(F32)
    normed = (x * inverse_rms(x) * gains[0:1]).astype(BF)
    packed[PACK_LEFT : PACK_LEFT + D, :] = normed.T
    qkv[...] = nn(normed, w_qkv[...]).astype(BF)
    for m in range(2):
        rows = slice(m * HD, (m + 1) * HD)
        for g in range(4):
            lanes = slice(g * GROUP, (g + 1) * GROUP)
            k_lanes = slice(D + g * GROUP, D + (g + 1) * GROUP)
            v_lanes = slice(2 * D + g * GROUP, 2 * D + (g + 1) * GROUP)
            stacked = stack_heads(qkv[rows, lanes] * BF(SCALE))
            scores = jnp.where(allowed[m] > 0.5, nt(qkv[rows, k_lanes], stacked), NEG)
            (w,) = softmax_columns([scores])
            weights[m * 4 + g] = w
            o2[rows, lanes] = unstack_heads(tn(w, qkv[rows, v_lanes])).astype(BF)
    packed[PACK_LEFT + D : PACK_LEFT + 2 * D, :] = o2[...].T
    after = x + nn(o2[...], w_out[...])
    yn = (after * inverse_rms(after) * gains[1:2]).astype(BF)
    c = cot[...]
    for h in range(2):

        @pl.when(core == h)
        def _(h=h):
            norms[0:128, :] = yn[:, h * HALF : (h + 1) * HALF]
            norms[128:256, :] = c[:, h * HALF : (h + 1) * HALF]

        @pl.when(core != h)
        def _(h=h):
            for b in range(4):
                lanes = slice(h * HALF + b * 128, h * HALF + (b + 1) * 128)
                packed[PACK_NORMS + b * 256 : PACK_NORMS + b * 256 + 128, :] = yn[:, lanes]
                packed[PACK_NORMS + b * 256 + 128 : PACK_NORMS + (b + 1) * 256, :] = c[:, lanes]

    acc_out[...] = after
    acc_norm[...] = jnp.zeros_like(acc_norm)

    def ff_step(i, carry):
        slot = lax.rem(i, 2)

        @pl.when(i + 1 < steps)
        def _():
            fetch(i + 1, 1 - slot).start()

        fetch(i, slot).wait()
        w_gate, w_up, w_down = ff_buf.at[slot, 0], ff_buf.at[slot, 1], ff_buf.at[slot, 2]
        gate = nt(yn, w_gate[...])
        upward = nt(yn, w_up[...])
        du = nt(c, w_down[...])
        sig = 1.0 / (1.0 + jnp.exp(-gate))
        active = gate * sig
        hidden = (active * upward).astype(BF)
        d_gate = (du * upward * (sig * (1.0 + gate * (1.0 - sig)))).astype(BF)
        d_up = (du * active).astype(BF)
        at = pl.ds(pl.multiple_of(i * step, 128), step)
        for j, value in enumerate((d_gate, d_up, hidden)):
            packed[pl.ds(pl.multiple_of(i * step + j * units, 128), step), :] = value.T
        acc_out[...] += nn(hidden, w_down[...])
        acc_norm[...] += nn(d_gate, w_gate[...]) + nn(d_up, w_up[...])
        return carry

    lax.fori_loop(0, steps, ff_step, 0)
    latents[...] = acc_out[...]
    back, gain_rows = norm_back(after, gains[1:2], acc_norm[...])
    gain_grad[1:2, :] = jnp.sum(gain_rows, axis=0, keepdims=True)
    d_after = c.astype(F32) + back
    da = d_after.astype(BF)
    d_mixed = nt(da, w_out[...]).astype(BF)
    for m in range(2):
        rows = slice(m * HD, (m + 1) * HD)
        for g in range(4):
            lanes = slice(g * GROUP, (g + 1) * GROUP)
            k_lanes = slice(D + g * GROUP, D + (g + 1) * GROUP)
            v_lanes = slice(2 * D + g * GROUP, 2 * D + (g + 1) * GROUP)
            q_stacked = stack_heads(qkv[rows, lanes] * BF(SCALE))
            o_stacked = stack_heads(d_mixed[rows, lanes])
            w_low = weights[m * 4 + g]
            w = w_low.astype(F32)
            dw = nt(qkv[rows, v_lanes], o_stacked)
            inner = jnp.sum(dw * w, axis=0, keepdims=True)
            ds = (w * (dw - inner)).astype(BF)
            dqkv[rows, lanes] = (unstack_heads(tn(ds, qkv[rows, k_lanes])) * SCALE).astype(BF)
            dqkv[rows, k_lanes] = nn(ds, q_stacked).astype(BF)
            dqkv[rows, v_lanes] = nn(w_low, o_stacked).astype(BF)
    d_normed = nt(dqkv[...], w_qkv[...])
    back, gain_rows = norm_back(x, gains[0:1], d_normed)
    gain_grad[0:1, :] = jnp.sum(gain_rows, axis=0, keepdims=True)
    dhb[...] = (d_after + back).astype(BF)
    for h in range(2):
        pieces = (
            dqkv[:, h * HALF : (h + 1) * HALF],
            da[:, h * HALF : (h + 1) * HALF],
            dqkv[:, D + h * HALF : D + (h + 1) * HALF],
            dqkv[:, 2 * D + h * HALF : 2 * D + (h + 1) * HALF],
        )

        @pl.when(core == h)
        def _(pieces=pieces):
            for i, value in enumerate(pieces):
                grads[i * 128 : (i + 1) * 128, :] = value

        @pl.when(core != h)
        def _(pieces=pieces):
            for i, value in enumerate(pieces):
                for b in range(4):
                    first = PACK_GRADS + b * 512 + i * 128
                    packed[first : first + 128, :] = value[:, b * 128 : (b + 1) * 128]


def half_of(core, g, mine, other):
    lanes = slice((g % 2) * GROUP, (g % 2 + 1) * GROUP)

    def put(at, value):
        @pl.when(core == g // 2)
        def _():
            mine[at, lanes] = value

        @pl.when(core != g // 2)
        def _():
            other[at, lanes] = value

    return put


def encoder_attention_back(
    ids, dhb, w_out, q, k_lo, v_lo, k_a, k_b, v_a, v_b, w_a, w_b, mine, other
):
    d_mixed = nt(dhb[...], w_out[...]).astype(BF)
    for g in range(4):
        lanes = slice(g * GROUP, (g + 1) * GROUP)
        put = half_of(ids[0], g, mine, other)
        put(slice(128, 256), dhb[:, lanes])
        for m, (k_up, v_up, weights) in enumerate(((k_a, v_a, w_a), (k_b, v_b, w_b))):
            rows = slice(m * HD, (m + 1) * HD)
            low_at = slice(m * 256, (m + 1) * 256)
            q_stacked = stack_heads(q[rows, lanes] * BF(SCALE))
            o_stacked = stack_heads(d_mixed[rows, lanes])
            low = [weights[g * 2 + h] for h in range(2)]
            w = [piece.astype(F32) for piece in low]
            dw = [nt(values, o_stacked) for values in (v_lo[low_at, lanes], v_up[:, lanes])]
            inner = sum(jnp.sum(a * b, axis=0, keepdims=True) for a, b in zip(dw, w))
            ds = [(b * (a - inner)).astype(BF) for a, b in zip(dw, w)]
            dq = tn(ds[0], k_lo[low_at, lanes]) + tn(ds[1], k_up[:, lanes])
            put(rows, (unstack_heads(dq) * SCALE).astype(BF))
            for h in range(2):
                base = h * HALF + m * 256
                put(slice(256 + base, 512 + base), nn(ds[h], q_stacked).astype(BF))
                put(slice(1280 + base, 1536 + base), nn(low[h], o_stacked).astype(BF))


def both_columns(core, block, w_qkv):
    return [
        w_qkv[:, pl.ds(pl.multiple_of(block * D + which * HALF, HALF), HALF)] for which in (core, 1 - core)
    ]


def bytes_back(core, h, m, source, w_qkv, gains, grads):
    d_norm = sum(
        nt(ref[1024 * block - 768 + h * HALF + m * 256 : 1024 * block - 512 + h * HALF + m * 256, :], columns)
        for block in (1, 2)
        for ref, columns in zip(grads, both_columns(core, block, w_qkv))
    )
    back, gain_rows = norm_back(source.astype(F32), gains[1:2], d_norm)
    return back.astype(BF), jnp.sum(gain_rows, axis=0, keepdims=True)


def encoder_upper_back(ids, up_a, up_b, w_qkv, gains, mine, other, up_grad, gain_grad):
    total = jnp.zeros((1, D), F32)
    for m, source in enumerate((up_a, up_b)):
        back, rows = bytes_back(ids[0], 1, m, source[...], w_qkv, gains, (mine, other))
        up_grad[m * 256 : (m + 1) * 256, :] = back
        total = total + rows
    gain_grad[...] = total


def encoder_lower_back(
    ids, dhb, patch, low, w_qkv, gains, mine, other, after, patch_grad, low_grad, gain_grad
):
    core = ids[0]
    up_norm = sum(nt(ref[0:128, :], columns) for ref, columns in zip((mine, other), both_columns(core, 0, w_qkv)))
    back, gain_rows = norm_back(patch[...].astype(F32), gains[0:1], up_norm)
    gain_grad[0:1, :] = jnp.sum(gain_rows, axis=0, keepdims=True)
    patch_grad[...] = dhb[...].astype(F32) + back
    total = jnp.zeros((1, D), F32)
    for m in range(2):
        at = slice(m * 256, (m + 1) * 256)
        back, rows = bytes_back(core, 0, m, low[at, :], w_qkv, gains, (mine, other))
        low_grad[at, :] = back
        total = total + rows
    gain_grad[1:2, :] = total


def turn_encoder(pn, o_a, o_b, bn_lo, bn_a, bn_b, packed):
    for b, rows in enumerate([bn_lo[i * 128 : (i + 1) * 128, :] for i in range(4)]
                             + [ref[i * 128 : (i + 1) * 128, :] for ref in (bn_a, bn_b) for i in range(2)]):
        packed[b * D : (b + 1) * D, :] = rows.T
    packed[PACK_LEFT : PACK_LEFT + D, :] = pn[...].T
    packed[PACK_LEFT + D : PACK_LEFT + 2 * D, :] = jnp.concatenate([o_a[...], o_b[...]], 0).T


def rows_of_both(left, left_far, at):
    return jnp.concatenate([left[at, :], left_far[at, :]], 1)


def below(near, far, rows):
    return jnp.concatenate([near[rows, :], far[rows, :]], 0)


def encoder_weights(ids, packed, packed_far, near, far, after, *blocks):
    u = ids[1]
    queries = below(near, far, slice(0, 128))
    outputs = below(near, far, slice(128, 256))
    for k in range(4):
        first = lax.rem(u + k, 4) * 256

        def at(base, first=first):
            return pl.ds(pl.multiple_of(first + base, 256), 256)

        blocks[k][0] = nn(rows_of_both(packed, packed_far, at(PACK_LEFT)), queries).astype(BF)
        blocks[k][3] = nn(rows_of_both(packed, packed_far, at(PACK_LEFT + D)), outputs).astype(BF)
        lefts = [jnp.concatenate([ref[at(b * D), :] for b in range(8)], 1) for ref in (packed, packed_far)]
        for block in (1, 2):
            rows = slice(1024 * block - 768, 1024 * block + 256)
            blocks[k][block] = (nn(lefts[0], near[rows, :]) + nn(lefts[1], far[rows, :])).astype(BF)


def unpack(packed, first, rows):
    return jnp.concatenate([packed[first + b * rows : first + (b + 1) * rows, :] for b in range(4)], 1)


def latent_weights(ids, packed, packed_far, near, *blocks):
    u = ids[1]
    far = unpack(packed_far, PACK_GRADS, 512)
    rights = [jnp.concatenate([near[i * 128 : (i + 1) * 128, :], far[i * 128 : (i + 1) * 128, :]], 0) for i in range(4)]
    for k in range(4):
        first = PACK_LEFT + lax.rem(u + k, 4) * 256
        at = pl.ds(pl.multiple_of(first, 256), 256)
        low_at = pl.ds(pl.multiple_of(first + D, 256), 256)
        for block, (source, i) in enumerate(((at, 0), (at, 2), (at, 3), (low_at, 1))):
            blocks[k][block] = nn(rows_of_both(packed, packed_far, source), rights[i]).astype(BF)


def ff_weights_grad(ids, packed, packed_far, norms, own, right, left, far_a, far_b):
    core, u = ids[0], ids[1]
    share = UNITS // 16
    far = unpack(packed_far, PACK_NORMS, 256)
    normed = jnp.concatenate([norms[0:128, :], far[0:128, :]], 0)
    cot = jnp.concatenate([norms[128:256, :], far[128:256, :]], 0)
    for k in range(4):
        there = lax.rem(u + k, 4)
        for v in range(4):
            chunk = jnp.where(core == 0, there * 4 + v, v * 4 + there)
            for j in range(3):
                at = pl.ds(pl.multiple_of(j * UNITS + chunk * share, 16), share)
                value = nn(rows_of_both(packed, packed_far, at), normed if j < 2 else cot).astype(BF)
                rows = slice(j * share, (j + 1) * share)
                if k == 2:
                    far_a[v, rows, :] = value[:, :GROUP]
                    far_b[v, rows, :] = value[:, GROUP:]
                else:
                    (own, right, None, left)[k][v, rows, :] = value


def ff_add(right, left, from_left, from_right, after, new_right, new_left):
    new_right[:, :, 0:GROUP] = (right[:, :, 0:GROUP].astype(F32) + from_left[...].astype(F32)).astype(BF)
    new_right[:, :, GROUP:] = right[:, :, GROUP:]
    new_left[:, :, 0:GROUP] = left[:, :, 0:GROUP]
    new_left[:, :, GROUP:] = (left[:, :, GROUP:].astype(F32) + from_right[...].astype(F32)).astype(BF)


def sum_four(own, a, b, c):
    return own.astype(F32) + a.astype(F32) + b.astype(F32) + c.astype(F32)


def pack_gain(value):
    high = value.astype(BF)
    low = (value - high.astype(F32)).astype(BF)
    return jnp.concatenate(
        [high.astype(F32), low.astype(F32), jnp.zeros((8, HALF), F32)], 0
    ).astype(BF)


def unpack_gain(rows):
    rows = rows.astype(F32)
    return rows[0:4] + rows[4:8]


GAIN_AT = slice(256, 272)


def attn_sum_first(ids, own, a, b, c, *outs):
    v = ids[2]
    for k in range(4):
        at = pl.ds(pl.multiple_of(lax.rem(v + k, 4) * HD, HD), HD)
        for block in range(4):
            outs[k][block * HD : (block + 1) * HD, :] = sum_four(
                own[block, at, :], a[block, at, :], b[block, at, :], c[block, at, :]
            ).astype(BF)


def attn_sum_first_gain(ids, own, a, b, c, enc_gain, up_gain, lat_gain, *outs):
    attn_sum_first(ids, own, a, b, c, *outs)
    first = ids[4] == 0
    gain = jnp.where(
        first, jnp.concatenate([enc_gain[0:1, :], enc_gain[1:2, :] + up_gain[...]], 0), lat_gain[...]
    )
    halves = [gain[i : i + 1, h * HALF : (h + 1) * HALF] for i in range(2) for h in range(2)]
    packed = pack_gain(jnp.concatenate(halves, 0))
    for out in outs:
        out[GAIN_AT, :] = packed


def sum_all(*refs):
    refs, out = refs[:-1], refs[-1]
    out[0:256, :] = sum(ref[0:256, :].astype(F32) for ref in refs).astype(BF)
    out[GAIN_AT, :] = pack_gain(sum(unpack_gain(ref[GAIN_AT, :]) for ref in refs))


def stack_rows(*refs):
    refs, out = refs[:-1], refs[-1]
    for j, ref in enumerate(refs):
        out[j * 256 : (j + 1) * 256, :] = ref[0:256, :]
    out[1024:1040, :] = refs[0][GAIN_AT, :]


def ff_sum_first(ids, own, a, b, *outs):
    v = ids[2]
    for k in range(4):
        at = lax.rem(v + k, 4)
        outs[k][...] = (own[at].astype(F32) + a[at].astype(F32) + b[at].astype(F32)).astype(BF)


def ff_sum_second(ids, own, a, b, c, out):
    out[...] = sum_four(own[...], a[...], b[...], c[...]).astype(BF)


def final_attn(ids, *refs):
    pieces, (qkv, out, gain) = refs[:8], refs[8:]
    step = pl.program_id(0)
    for side in range(2):
        core = ids[0] if side == 0 else 1 - ids[0]
        u = ids[1] if side == 0 else ids[2]
        v = ids[2] if side == 0 else ids[1]
        for k in range(4):
            piece = pieces[side * 4 + k]

            @pl.when(lax.rem(u + k, 4) == step)
            def _(piece=piece, v=v, core=core):
                for j in range(4):
                    at = pl.ds(pl.multiple_of(lax.rem(v + j, 4) * HD, HD), HD)
                    for block in range(4):
                        target, column = (qkv, block * D) if block < 3 else (out, 0)
                        lanes = pl.ds(pl.multiple_of(core * HALF + column, HALF), HALF)
                        first = j * 256 + block * HD
                        target[at, lanes] = piece[first : first + HD, :].astype(F32)

    mine = sum(unpack_gain(piece[1024:1040, :]) for piece in pieces[:4])
    other = sum(unpack_gain(piece[1024:1040, :]) for piece in pieces[4:])
    total = mine + other
    for i in range(2):
        for h in range(2):
            gain[i : i + 1, h * HALF : (h + 1) * HALF] = total[2 * i + h : 2 * i + h + 1, :]


SMEM = pltpu.MemorySpace.SMEM
VMEM = pltpu.MemorySpace.VMEM


def size(shape, dtype):
    return math.prod(shape) * jnp.dtype(dtype).itemsize


def call(kernel, args, outs, scratch=(), spaces=None, spare=6):
    spaces = spaces or {}
    vmem = sum(size(a.shape, a.dtype) for i, a in enumerate(args) if i not in spaces)
    vmem += sum(size(*o) for o in outs)
    vmem += sum(size(s.shape, s.dtype) for s in scratch if hasattr(s, "shape") and s.memory_space == VMEM)
    specs = [pl.BlockSpec(memory_space=spaces.get(i, VMEM)) for i in range(len(args))]
    return pl.pallas_call(
        kernel,
        out_shape=[jax.ShapeDtypeStruct(s, t) for s, t in outs],
        in_specs=specs,
        out_specs=[pl.BlockSpec(memory_space=VMEM) for _ in outs],
        scratch_shapes=list(scratch),
        compiler_params=pltpu.CompilerParams(vmem_limit_bytes=vmem + spare * 1024 * 1024),
    )(*args)


def nothing(outs):
    def kernel(*refs):
        pass

    return pl.pallas_call(
        kernel,
        out_shape=[jax.ShapeDtypeStruct(s, t) for s, t in outs],
        out_specs=[pl.BlockSpec(memory_space=pl.ANY) for _ in outs],
    )()


def in_section(section, kernel):
    def guarded(ids, *refs):
        @pl.when(ids[4] == section)
        def _():
            kernel(ids, *refs)

    return guarded


def on_section(flag, kernel, args, outs, **rest):
    return lax.cond(
        flag, lambda: call(kernel, args, outs, **rest), lambda: nothing(outs)
    )


def along(value, by):
    return lax.ppermute(value, "s", [(0, 1)] if by > 0 else [(1, 0)])


def swap(value, axis, sections=(0, 1)):
    pairs = [(s * 2 + i, s * 2 + 1 - i) for s in sections for i in range(2)]
    return lax.ppermute(value, ("s", axis), pairs)


def plane_shift(value, which, by, sections=(0, 1)):
    pairs = []
    for s in sections:
        for y in range(4):
            for x in range(4):
                for core in range(2):
                    ty, tx = ((y + by) % 4, x) if core == which else (y, (x + by) % 4)
                    pairs.append((((s * 4 + y) * 4 + x) * 2 + core, ((s * 4 + ty) * 4 + tx) * 2 + core))
    return lax.ppermute(value, ("s", "y", "x", "core"), pairs)


def exchange(blocks, which, sections=(0, 1)):
    return [plane_shift(blocks[k], which, k, sections) for k in (1, 2, 3)]


def collect(block, which):
    return [block] + [plane_shift(block, which, -k) for k in (1, 2, 3)]


def pick(stack, index, dim):
    return lax.dynamic_index_in_dim(stack, index, dim, keepdims=False)


def shards(patch_io, byte_states, patch_lengths, patch_live, attn_qkv, attn_out, gains, ff_weights):
    section = lax.axis_index("s")
    core = lax.axis_index("core")
    zh = lax.axis_index("zh")
    y, x = lax.axis_index("y"), lax.axis_index("x")
    first = section == 0
    second = section == 1
    ids = jnp.stack([core, jnp.where(core == 0, y, x), jnp.where(core == 0, x, y), zh, section])
    ids = ids.astype(jnp.int32)
    w_qkv = attn_qkv[0]
    w_out = attn_out[0]
    gain_pair = gains[0]
    micro, seq = patch_io.shape[1], patch_io.shape[3]
    half_bytes = byte_states.shape[2]
    units = ff_weights.shape[0]
    rows = micro * seq
    own_rows = patch_io.reshape(rows, D)
    up_a = along(byte_states[0, 0], -1)
    up_b = along(byte_states[1, 0], -1)
    lower = byte_states.reshape(micro * half_bytes, D)
    w_ff = jnp.swapaxes(ff_weights, 0, 1)
    lengths = patch_lengths[:, 0]
    live = patch_live[:, 0]
    ends = jnp.cumsum(lengths, axis=1)
    bounds = jnp.tile(jnp.stack([ends - lengths, ends], 1), (1, 1, 4))
    places = lax.iota(jnp.int32, seq)
    causal = places[:, None] <= places[None, :]
    diagonal = places[:, None] == places[None, :]
    allowed = causal[None] & ((live[:, :, None] == 1) | diagonal[None])
    allowed = lax.optimization_barrier(jnp.tile(allowed.astype(F32), (1, 1, 4)))

    wide = ((rows, D), BF)
    short = ((seq, D), BF)
    tall = ((micro * half_bytes, D), BF)
    piece = ((half_bytes, D), BF)
    pn, q, bn_lo, k_lo, v_lo = on_section(
        first, encode_lower, (own_rows, lower, w_qkv, gain_pair), [wide, wide, tall, tall, tall]
    )
    rest = []
    for m, up in enumerate((up_a, up_b)):
        rest.append(
            on_section(
                first,
                functools.partial(encode_rest, m),
                (own_rows, up, w_qkv, w_out, gain_pair, bounds, q, k_lo, v_lo),
                [short, short, ((8, 256, GROUP), BF), piece, piece, piece],
            )
        )
    (hb_a, o_a, w_a, bn_a, k_a, v_a), (hb_b, o_b, w_b, bn_b, k_b, v_b) = rest
    arrived = [along(hb_a, 1), along(hb_b, 1)]

    step = 256
    latent_outs = [
        ((rows, D), F32), wide, ((2, D), F32), ((256, HALF), BF), ((512, HALF), BF), ((PACK_ROWS, rows), BF),
    ]

    def latent():
        return call(
            latent_layer,
            (ids, *arrived, own_rows, allowed, w_qkv, w_out, gain_pair, w_ff),
            latent_outs,
            spaces={0: SMEM, 8: pl.ANY},
            scratch=[
                pltpu.VMEM((rows, 3 * D), BF),
                pltpu.VMEM((8, HD, GROUP), BF),
                pltpu.VMEM((rows, D), BF),
                pltpu.VMEM((2, 3, step, D), BF),
                pltpu.VMEM((rows, D), F32),
                pltpu.VMEM((rows, D), F32),
                pltpu.VMEM((rows, 3 * D), BF),
                pltpu.SemaphoreType.DMA((2,)),
            ],
        )

    def turn():
        return nothing(latent_outs[:5]) + call(
            turn_encoder, (pn, o_a, o_b, bn_lo, bn_a, bn_b), latent_outs[5:]
        )

    latents, dhb, latent_gain, norms, lat_grads, packed = lax.cond(second, latent, turn)
    returned = along(dhb, -1)

    packed_far = swap(packed, "core")

    share = units // 16
    ff_block = ((4, 3 * share, HALF), BF)
    ff_half = ((4, 3 * share, GROUP), BF)
    ff_own, ff_right, ff_left, ff_far_a, ff_far_b = on_section(
        second,
        ff_weights_grad,
        (ids, packed, packed_far, norms),
        [ff_block, ff_block, ff_block, ff_half, ff_half],
        spaces={0: SMEM},
    )
    from_left = plane_shift(ff_far_a, 0, 1, (1,))
    from_right = plane_shift(ff_far_b, 0, -1, (1,))

    grads_long = ((2304, HALF), BF)
    enc_grads, enc_other = on_section(
        first,
        encoder_attention_back,
        (ids, returned, w_out, q, k_lo, v_lo, k_a, k_b, v_a, v_b, w_a, w_b),
        [grads_long, grads_long],
        spaces={0: SMEM},
    )
    enc_far = swap(enc_other, "core", (0,))
    up_grad, up_gain = on_section(
        first,
        encoder_upper_back,
        (ids, up_a, up_b, w_qkv, gain_pair, enc_grads, enc_other),
        [tall, ((1, D), F32)],
        spaces={0: SMEM},
    )
    up_arrived = along(up_grad, 1)
    outs = [((4, 256, HALF), BF)] * 4
    blocks = lax.cond(
        first,
        lambda: call(
            encoder_weights,
            (ids, packed, packed_far, enc_grads, enc_far, up_gain),
            outs,
            spaces={0: SMEM, 5: pl.ANY},
        ),
        lambda: call(latent_weights, (ids, packed, packed_far, lat_grads), outs, spaces={0: SMEM}),
    )
    last, from_left, from_right = lax.optimization_barrier((blocks[3], from_left, from_right))
    blocks = [*blocks[:3], last]
    got, up_arrived = lax.optimization_barrier((exchange(blocks, 0), up_arrived))
    low_outs = [((rows, D), F32), tall, ((2, D), F32)]

    def lower_grads():
        parts = call(
            encoder_lower_back,
            (ids, returned, own_rows, lower, w_qkv, gain_pair, enc_grads, enc_other, blocks[0]),
            low_outs,
            spaces={0: SMEM, 8: pl.ANY},
        )
        return (*parts, *nothing([ff_block, ff_block]))

    def ff_middle():
        added = call(
            ff_add, (ff_right, ff_left, from_left, from_right, blocks[0]), [ff_block, ff_block], spaces={4: pl.ANY}
        )
        return (*nothing(low_outs), *added)

    patch_grad, low_grad, encoder_gain, ff_right_sum, ff_left_sum = lax.cond(first, lower_grads, ff_middle)
    line = [((272, HALF), BF)]
    blocks = call(
        attn_sum_first_gain,
        (ids, blocks[0], *got, encoder_gain, up_gain, latent_gain),
        line * 4,
        spaces={0: SMEM},
    )
    ff_right_sum, ff_left_sum, _ = lax.optimization_barrier((ff_right_sum, ff_left_sum, blocks))
    from_left = plane_shift(ff_right_sum, 0, 1, (1,))
    from_right = plane_shift(ff_left_sum, 0, -1, (1,))
    (block,) = call(sum_all, (blocks[0], *exchange(blocks, 1)), line)
    from_left, from_right, block = lax.optimization_barrier((from_left, from_right, block))
    ff_line = ((3 * share, HALF), BF)
    ff_blocks = call(
        in_section(1, ff_sum_first), (ids, ff_own, from_left, from_right), [ff_line] * 4, spaces={0: SMEM}
    )
    ff_got = exchange(ff_blocks, 1, (1,))
    across, ff_got = lax.optimization_barrier((swap(block, "zh"), ff_got))
    (block,) = call(sum_all, (block, across), line)
    (block,) = call(stack_rows, collect(block, 1), [((1040, HALF), BF)])
    pieces = collect(block, 0)
    own_far = swap(block, "core")
    (ff_sum,) = call(in_section(1, ff_sum_second), (ids, ff_blocks[0], *ff_got), [ff_line], spaces={0: SMEM})
    ff_sum = ff_sum.reshape(3, 2, share // 2, HALF)
    ff_far = swap(pick(ff_sum, 1 - zh, 1), "zh", (1,))
    ff_sum = (pick(ff_sum, zh, 1).astype(F32) + ff_far.astype(F32)).astype(BF).reshape(3, 2, share // 4, HALF)
    ff_mine = pick(ff_sum, core, 1)
    ff_far = swap(pick(ff_sum, 1 - core, 1), "core", (1,))

    def ff_result():
        low, high = jnp.where(core == 0, ff_mine, ff_far), jnp.where(core == 0, ff_far, ff_mine)
        return jnp.swapaxes(jnp.concatenate([low, high], 2), 0, 1).astype(F32)

    ff_grad = lax.cond(second, ff_result, lambda: jnp.zeros((share // 4, 3, D), F32))
    byte_grad = jnp.where(first, low_grad, up_arrived)
    patch_out = jnp.where(first, patch_grad, latents)
    patch_out, ff_grad, *pieces = lax.optimization_barrier((patch_out, ff_grad, *pieces))
    pieces = pieces + [own_far] + [swap(p, "core") for p in pieces[1:]]
    whole = lambda p: pl.BlockSpec(p.shape, lambda i, n=p.ndim: (0,) * n)
    total_qkv, total_out, total_gain = pl.pallas_call(
        final_attn,
        grid=(4,),
        out_shape=[
            jax.ShapeDtypeStruct((D, 3 * D), F32),
            jax.ShapeDtypeStruct((D, D), F32),
            jax.ShapeDtypeStruct((2, D), F32),
        ],
        in_specs=[pl.BlockSpec(memory_space=SMEM)] + [whole(p) for p in pieces],
        out_specs=[
            pl.BlockSpec((256, 3 * D), lambda i: (i, 0)),
            pl.BlockSpec((256, D), lambda i: (i, 0)),
            pl.BlockSpec((2, D), lambda i: (0, 0)),
        ],
        compiler_params=pltpu.CompilerParams(vmem_limit_bytes=FINAL_VMEM),
    )(ids, *pieces)
    return (
        patch_out.reshape(1, micro, 1, seq, D),
        byte_grad.reshape(micro, 1, half_bytes, D),
        total_qkv[None],
        total_out[None],
        total_gain[None],
        ff_grad[None],
    )


def solution(mesh):
    fine = Mesh(mesh.devices.reshape(2, 4, 4, 2, 2), ("s",) + BATCH)
    in_specs = (
        P("s", None, BATCH, None, None),
        P(None, BATCH, "s", None),
        P(None, BATCH, None),
        P(None, BATCH, None),
        P("s", None, None),
        P("s", None, None),
        P("s", None, None),
        P(),
    )
    out_specs = (
        P("s", None, BATCH, None, None),
        P(None, BATCH, "s", None),
        P("s", None, None),
        P("s", None, None),
        P("s", None, None),
        P("s", BATCH, None, None),
    )
    return jax.shard_map(shards, mesh=fine, in_specs=in_specs, out_specs=out_specs, check_vma=False)
```

```python
import functools
import math

import jax
import jax.numpy as jnp
from jax import lax
from jax.experimental import pallas as pl
from jax.experimental.pallas import tpu as pltpu
from jax.sharding import Mesh
from jax.sharding import PartitionSpec as P

HD = 64
SCALE = HD**-0.5
EPS = 1e-05
NEG = -1e30
BATCH = ("y", "x", "zh", "core")
BF = jnp.bfloat16
F32 = jnp.float32
D = 1024
HALF = 512
GROUP = 256
FINAL_VMEM = 32 * 1024 * 1024


UNITS = 2816
PACK_NORMS = 3 * UNITS
PACK_LEFT = PACK_NORMS + 4 * 256
PACK_GRADS = PACK_LEFT + 2 * D
PACK_ROWS = PACK_GRADS + 4 * 512


def nn(a, b):
    return lax.dot_general(a, b, (((1,), (0,)), ((), ())), preferred_element_type=F32)


def nt(a, b):
    return lax.dot_general(a, b, (((1,), (1,)), ((), ())), preferred_element_type=F32)


def tn(a, b):
    return lax.dot_general(a, b, (((0,), (0,)), ((), ())), preferred_element_type=F32)


def inverse_rms(x):
    return lax.rsqrt(jnp.mean(x * x, axis=-1, keepdims=True) + EPS)


def norm_back(x, gain, up):
    r = inverse_rms(x)
    scaled = up * gain
    inner = jnp.mean(scaled * x, axis=-1, keepdims=True)
    return r * (scaled - x * (r * r * inner)), up * (x * r)


def stack_heads(rows):
    head = lax.broadcasted_iota(jnp.int32, rows.shape, 1) // HD
    return jnp.concatenate([jnp.where(head == h, rows, jnp.zeros_like(rows)) for h in range(4)], 0)


def unstack_heads(stacked):
    head = lax.broadcasted_iota(jnp.int32, (HD, GROUP), 1) // HD
    out = stacked[0:HD]
    for h in range(1, 4):
        out = jnp.where(head == h, stacked[h * HD : (h + 1) * HD], out)
    return out


def softmax_columns(scores):
    top = functools.reduce(jnp.maximum, [jnp.max(s, axis=0, keepdims=True) for s in scores])
    parts = [jnp.exp(s - top) for s in scores]
    inverse = 1.0 / sum(jnp.sum(p, axis=0, keepdims=True) for p in parts)
    return [(p * inverse).astype(BF) for p in parts]


def encode_lower(patch, low, w_qkv, gains, pn, q, bn, k, v):
    x = patch[...].astype(F32)
    normed = (x * inverse_rms(x) * gains[0:1]).astype(BF)
    pn[...] = normed
    q[...] = nn(normed, w_qkv.block(0)[...]).astype(BF)
    for i in range(2):
        at = pl.ds(i * 256, 256)
        b = low[at, :].astype(F32)
        normed = (b * inverse_rms(b) * gains[1:2]).astype(BF)
        bn[at, :] = normed
        k[at, :] = nn(normed, w_qkv.block(1)[...]).astype(BF)
        v[at, :] = nn(normed, w_qkv.block(2)[...]).astype(BF)


def encode_rest(m, patch, up, w_qkv, w_out, gains, bounds, q, k_lo, v_lo, hb, o1, weights, bn, k, v):
    b = up[...].astype(F32)
    normed = (b * inverse_rms(b) * gains[1:2]).astype(BF)
    bn[...] = normed
    k[...] = nn(normed, w_qkv.block(1)[...]).astype(BF)
    v[...] = nn(normed, w_qkv.block(2)[...]).astype(BF)
    spot = lax.broadcasted_iota(jnp.int32, (256, GROUP), 0)
    start = bounds[m, 0:1, :]
    end = bounds[m, 1:2, :]
    inside = [(spot + h * 256 >= start) & (spot + h * 256 < end) for h in range(2)]
    low_at = slice(m * 256, (m + 1) * 256)
    rows = slice(m * HD, (m + 1) * HD)
    for g in range(4):
        lanes = slice(g * GROUP, (g + 1) * GROUP)
        stacked = stack_heads(q[rows, lanes] * BF(SCALE))
        scores = [
            jnp.where(inside[h], nt(keys, stacked), NEG)
            for h, keys in enumerate((k_lo[low_at, lanes], k[:, lanes]))
        ]
        w = softmax_columns(scores)
        weights[g * 2] = w[0]
        weights[g * 2 + 1] = w[1]
        mixed = tn(w[0], v_lo[low_at, lanes]) + tn(w[1], v[:, lanes])
        o1[:, lanes] = unstack_heads(mixed).astype(BF)
    hb[...] = (patch[rows, :].astype(F32) + nn(o1[...], w_out[...])).astype(BF)


def latent_layer(
    ids, hb_a, hb_b, cot, allowed, w_qkv, w_out, gains, w_ff,
    latents, dhb, gain_grad, norms, grads, packed,
    qkv, weights, o2, ff_buf, acc_out, acc_norm, dqkv, sems,
):
    core = ids[0]
    units = w_ff.shape[1]
    step = ff_buf.shape[2]
    steps = units // step

    def fetch(i, slot):
        return pltpu.make_async_copy(
            w_ff.at[:, pl.ds(pl.multiple_of(i * step, 128), step), :], ff_buf.at[slot], sems.at[slot]
        )

    fetch(0, 0).start()
    x = jnp.concatenate([hb_a[...], hb_b[...]], 0).astype(F32)
    normed = (x * inverse_rms(x) * gains[0:1]).astype(BF)
    packed[PACK_LEFT : PACK_LEFT + D, :] = normed.T
    for j in range(3):
        qkv[:, j * D : (j + 1) * D] = nn(normed, w_qkv.block(j)[...]).astype(BF)
    for m in range(2):
        rows = slice(m * HD, (m + 1) * HD)
        for g in range(4):
            lanes = slice(g * GROUP, (g + 1) * GROUP)
            k_lanes = slice(D + g * GROUP, D + (g + 1) * GROUP)
            v_lanes = slice(2 * D + g * GROUP, 2 * D + (g + 1) * GROUP)
            stacked = stack_heads(qkv[rows, lanes] * BF(SCALE))
            scores = jnp.where(allowed[m] > 0.5, nt(qkv[rows, k_lanes], stacked), NEG)
            (w,) = softmax_columns([scores])
            weights[m * 4 + g] = w
            o2[rows, lanes] = unstack_heads(tn(w, qkv[rows, v_lanes])).astype(BF)
    packed[PACK_LEFT + D : PACK_LEFT + 2 * D, :] = o2[...].T
    after = x + nn(o2[...], w_out[...])
    yn = (after * inverse_rms(after) * gains[1:2]).astype(BF)
    c = cot[...]
    for h in range(2):

        @pl.when(core == h)
        def _(h=h):
            norms[0:128, :] = yn[:, h * HALF : (h + 1) * HALF]
            norms[128:256, :] = c[:, h * HALF : (h + 1) * HALF]

        @pl.when(core != h)
        def _(h=h):
            for b in range(4):
                lanes = slice(h * HALF + b * 128, h * HALF + (b + 1) * 128)
                packed[PACK_NORMS + b * 256 : PACK_NORMS + b * 256 + 128, :] = yn[:, lanes]
                packed[PACK_NORMS + b * 256 + 128 : PACK_NORMS + (b + 1) * 256, :] = c[:, lanes]

    acc_out[...] = after
    acc_norm[...] = jnp.zeros_like(acc_norm)

    def ff_step(i, carry):
        slot = lax.rem(i, 2)

        @pl.when(i + 1 < steps)
        def _():
            fetch(i + 1, 1 - slot).start()

        fetch(i, slot).wait()
        w_gate, w_up, w_down = ff_buf.at[slot, 0], ff_buf.at[slot, 1], ff_buf.at[slot, 2]
        gate = nt(yn, w_gate[...])
        upward = nt(yn, w_up[...])
        du = nt(c, w_down[...])
        sig = 1.0 / (1.0 + jnp.exp(-gate))
        active = gate * sig
        hidden = (active * upward).astype(BF)
        d_gate = (du * upward * (sig * (1.0 + gate * (1.0 - sig)))).astype(BF)
        d_up = (du * active).astype(BF)
        at = pl.ds(pl.multiple_of(i * step, 128), step)
        for j, value in enumerate((d_gate, d_up, hidden)):
            packed[pl.ds(pl.multiple_of(i * step + j * units, 128), step), :] = value.T
        acc_out[...] += nn(hidden, w_down[...])
        acc_norm[...] += nn(d_gate, w_gate[...]) + nn(d_up, w_up[...])
        return carry

    lax.fori_loop(0, steps, ff_step, 0)
    latents[...] = acc_out[...]
    back, gain_rows = norm_back(after, gains[1:2], acc_norm[...])
    gain_grad[1:2, :] = jnp.sum(gain_rows, axis=0, keepdims=True)
    d_after = c.astype(F32) + back
    da = d_after.astype(BF)
    d_mixed = nt(da, w_out[...]).astype(BF)
    for m in range(2):
        rows = slice(m * HD, (m + 1) * HD)
        for g in range(4):
            lanes = slice(g * GROUP, (g + 1) * GROUP)
            k_lanes = slice(D + g * GROUP, D + (g + 1) * GROUP)
            v_lanes = slice(2 * D + g * GROUP, 2 * D + (g + 1) * GROUP)
            q_stacked = stack_heads(qkv[rows, lanes] * BF(SCALE))
            o_stacked = stack_heads(d_mixed[rows, lanes])
            w_low = weights[m * 4 + g]
            w = w_low.astype(F32)
            dw = nt(qkv[rows, v_lanes], o_stacked)
            inner = jnp.sum(dw * w, axis=0, keepdims=True)
            ds = (w * (dw - inner)).astype(BF)
            dqkv[rows, lanes] = (unstack_heads(tn(ds, qkv[rows, k_lanes])) * SCALE).astype(BF)
            dqkv[rows, k_lanes] = nn(ds, q_stacked).astype(BF)
            dqkv[rows, v_lanes] = nn(w_low, o_stacked).astype(BF)
    d_normed = sum(nt(dqkv[:, j * D : (j + 1) * D], w_qkv.block(j)[...]) for j in range(3))
    back, gain_rows = norm_back(x, gains[0:1], d_normed)
    gain_grad[0:1, :] = jnp.sum(gain_rows, axis=0, keepdims=True)
    dhb[...] = (d_after + back).astype(BF)
    for h in range(2):
        pieces = (
            dqkv[:, h * HALF : (h + 1) * HALF],
            da[:, h * HALF : (h + 1) * HALF],
            dqkv[:, D + h * HALF : D + (h + 1) * HALF],
            dqkv[:, 2 * D + h * HALF : 2 * D + (h + 1) * HALF],
        )

        @pl.when(core == h)
        def _(pieces=pieces):
            for i, value in enumerate(pieces):
                grads[i * 128 : (i + 1) * 128, :] = value

        @pl.when(core != h)
        def _(pieces=pieces):
            for i, value in enumerate(pieces):
                for b in range(4):
                    first = PACK_GRADS + b * 512 + i * 128
                    packed[first : first + 128, :] = value[:, b * 128 : (b + 1) * 128]


def half_of(core, g, mine, other):
    lanes = slice((g % 2) * GROUP, (g % 2 + 1) * GROUP)

    def put(at, value):
        @pl.when(core == g // 2)
        def _():
            mine[at, lanes] = value

        @pl.when(core != g // 2)
        def _():
            other[at, lanes] = value

    return put


def encoder_attention_back(
    ids, dhb, w_out, q, k_lo, v_lo, k_a, k_b, v_a, v_b, w_a, w_b, mine, other
):
    d_mixed = nt(dhb[...], w_out[...]).astype(BF)
    for g in range(4):
        lanes = slice(g * GROUP, (g + 1) * GROUP)
        put = half_of(ids[0], g, mine, other)
        put(slice(128, 256), dhb[:, lanes])
        for m, (k_up, v_up, weights) in enumerate(((k_a, v_a, w_a), (k_b, v_b, w_b))):
            rows = slice(m * HD, (m + 1) * HD)
            low_at = slice(m * 256, (m + 1) * 256)
            q_stacked = stack_heads(q[rows, lanes] * BF(SCALE))
            o_stacked = stack_heads(d_mixed[rows, lanes])
            low = [weights[g * 2 + h] for h in range(2)]
            w = [piece.astype(F32) for piece in low]
            dw = [nt(values, o_stacked) for values in (v_lo[low_at, lanes], v_up[:, lanes])]
            inner = sum(jnp.sum(a * b, axis=0, keepdims=True) for a, b in zip(dw, w))
            ds = [(b * (a - inner)).astype(BF) for a, b in zip(dw, w)]
            dq = tn(ds[0], k_lo[low_at, lanes]) + tn(ds[1], k_up[:, lanes])
            put(rows, (unstack_heads(dq) * SCALE).astype(BF))
            for h in range(2):
                base = h * HALF + m * 256
                put(slice(256 + base, 512 + base), nn(ds[h], q_stacked).astype(BF))
                put(slice(1280 + base, 1536 + base), nn(low[h], o_stacked).astype(BF))


def both_columns(core, block, w_qkv):
    return [
        w_qkv.block(block)[:, pl.ds(pl.multiple_of(which * HALF, HALF), HALF)] for which in (core, 1 - core)
    ]


def bytes_back(core, h, m, source, w_qkv, gains, grads):
    d_norm = sum(
        nt(ref[1024 * block - 768 + h * HALF + m * 256 : 1024 * block - 512 + h * HALF + m * 256, :], columns)
        for block in (1, 2)
        for ref, columns in zip(grads, both_columns(core, block, w_qkv))
    )
    back, gain_rows = norm_back(source.astype(F32), gains[1:2], d_norm)
    return back.astype(BF), jnp.sum(gain_rows, axis=0, keepdims=True)


def encoder_upper_back(ids, up_a, up_b, w_qkv, gains, mine, other, up_grad, gain_grad):
    total = jnp.zeros((1, D), F32)
    for m, source in enumerate((up_a, up_b)):
        back, rows = bytes_back(ids[0], 1, m, source[...], w_qkv, gains, (mine, other))
        up_grad[m * 256 : (m + 1) * 256, :] = back
        total = total + rows
    gain_grad[...] = total


def encoder_lower_back(
    ids, dhb, patch, low, w_qkv, gains, mine, other, after, patch_grad, low_grad, gain_grad
):
    core = ids[0]
    up_norm = sum(nt(ref[0:128, :], columns) for ref, columns in zip((mine, other), both_columns(core, 0, w_qkv)))
    back, gain_rows = norm_back(patch[...].astype(F32), gains[0:1], up_norm)
    gain_grad[0:1, :] = jnp.sum(gain_rows, axis=0, keepdims=True)
    patch_grad[...] = dhb[...].astype(F32) + back
    total = jnp.zeros((1, D), F32)
    for m in range(2):
        at = slice(m * 256, (m + 1) * 256)
        back, rows = bytes_back(core, 0, m, low[at, :], w_qkv, gains, (mine, other))
        low_grad[at, :] = back
        total = total + rows
    gain_grad[1:2, :] = total


def turn_encoder(pn, o_a, o_b, bn_lo, bn_a, bn_b, packed):
    for b, rows in enumerate([bn_lo[i * 128 : (i + 1) * 128, :] for i in range(4)]
                             + [ref[i * 128 : (i + 1) * 128, :] for ref in (bn_a, bn_b) for i in range(2)]):
        packed[b * D : (b + 1) * D, :] = rows.T
    packed[PACK_LEFT : PACK_LEFT + D, :] = pn[...].T
    packed[PACK_LEFT + D : PACK_LEFT + 2 * D, :] = jnp.concatenate([o_a[...], o_b[...]], 0).T


def rows_of_both(left, left_far, at):
    return jnp.concatenate([left[at, :], left_far[at, :]], 1)


def below(near, far, rows):
    return jnp.concatenate([near[rows, :], far[rows, :]], 0)


def encoder_weights(ids, packed, packed_far, near, far, after, *blocks):
    u = ids[1]
    queries = below(near, far, slice(0, 128))
    outputs = below(near, far, slice(128, 256))
    for k in range(4):
        first = lax.rem(u + k, 4) * 256

        def at(base, first=first):
            return pl.ds(pl.multiple_of(first + base, 256), 256)

        blocks[k][0] = nn(rows_of_both(packed, packed_far, at(PACK_LEFT)), queries).astype(BF)
        blocks[k][3] = nn(rows_of_both(packed, packed_far, at(PACK_LEFT + D)), outputs).astype(BF)
        lefts = [jnp.concatenate([ref[at(b * D), :] for b in range(8)], 1) for ref in (packed, packed_far)]
        for block in (1, 2):
            rows = slice(1024 * block - 768, 1024 * block + 256)
            blocks[k][block] = (nn(lefts[0], near[rows, :]) + nn(lefts[1], far[rows, :])).astype(BF)


def unpack(packed, first, rows):
    return jnp.concatenate([packed[first + b * rows : first + (b + 1) * rows, :] for b in range(4)], 1)


def latent_weights(ids, packed, packed_far, near, *blocks):
    u = ids[1]
    far = unpack(packed_far, PACK_GRADS, 512)
    rights = [jnp.concatenate([near[i * 128 : (i + 1) * 128, :], far[i * 128 : (i + 1) * 128, :]], 0) for i in range(4)]
    for k in range(4):
        first = PACK_LEFT + lax.rem(u + k, 4) * 256
        at = pl.ds(pl.multiple_of(first, 256), 256)
        low_at = pl.ds(pl.multiple_of(first + D, 256), 256)
        for block, (source, i) in enumerate(((at, 0), (at, 2), (at, 3), (low_at, 1))):
            blocks[k][block] = nn(rows_of_both(packed, packed_far, source), rights[i]).astype(BF)


def ff_weights_grad(ids, packed, packed_far, norms, own, right, left, far_a, far_b):
    core, u = ids[0], ids[1]
    share = UNITS // 16
    far = unpack(packed_far, PACK_NORMS, 256)
    normed = jnp.concatenate([norms[0:128, :], far[0:128, :]], 0)
    cot = jnp.concatenate([norms[128:256, :], far[128:256, :]], 0)
    for k in range(4):
        there = lax.rem(u + k, 4)
        for v in range(4):
            chunk = jnp.where(core == 0, there * 4 + v, v * 4 + there)
            for j in range(3):
                at = pl.ds(pl.multiple_of(j * UNITS + chunk * share, 16), share)
                value = nn(rows_of_both(packed, packed_far, at), normed if j < 2 else cot).astype(BF)
                rows = slice(j * share, (j + 1) * share)
                if k == 2:
                    far_a[v, rows, :] = value[:, :GROUP]
                    far_b[v, rows, :] = value[:, GROUP:]
                else:
                    (own, right, None, left)[k][v, rows, :] = value


def ff_add(right, left, from_left, from_right, after, new_right, new_left):
    new_right[:, :, 0:GROUP] = (right[:, :, 0:GROUP].astype(F32) + from_left[...].astype(F32)).astype(BF)
    new_right[:, :, GROUP:] = right[:, :, GROUP:]
    new_left[:, :, 0:GROUP] = left[:, :, 0:GROUP]
    new_left[:, :, GROUP:] = (left[:, :, GROUP:].astype(F32) + from_right[...].astype(F32)).astype(BF)


def sum_four(own, a, b, c):
    return own.astype(F32) + a.astype(F32) + b.astype(F32) + c.astype(F32)


def pack_gain(value):
    high = value.astype(BF)
    low = (value - high.astype(F32)).astype(BF)
    return jnp.concatenate(
        [high.astype(F32), low.astype(F32), jnp.zeros((8, HALF), F32)], 0
    ).astype(BF)


def unpack_gain(rows):
    rows = rows.astype(F32)
    return rows[0:4] + rows[4:8]


GAIN_AT = slice(256, 272)


def attn_sum_first(ids, own, a, b, c, *outs):
    v = ids[2]
    for k in range(4):
        at = pl.ds(pl.multiple_of(lax.rem(v + k, 4) * HD, HD), HD)
        for block in range(4):
            outs[k][block * HD : (block + 1) * HD, :] = sum_four(
                own[block, at, :], a[block, at, :], b[block, at, :], c[block, at, :]
            ).astype(BF)


def attn_sum_first_gain(ids, own, a, b, c, enc_gain, up_gain, lat_gain, *outs):
    attn_sum_first(ids, own, a, b, c, *outs)
    first = ids[4] == 0
    gain = jnp.where(
        first, jnp.concatenate([enc_gain[0:1, :], enc_gain[1:2, :] + up_gain[...]], 0), lat_gain[...]
    )
    halves = [gain[i : i + 1, h * HALF : (h + 1) * HALF] for i in range(2) for h in range(2)]
    packed = pack_gain(jnp.concatenate(halves, 0))
    for out in outs:
        out[GAIN_AT, :] = packed


def sum_all(*refs):
    refs, out = refs[:-1], refs[-1]
    out[0:256, :] = sum(ref[0:256, :].astype(F32) for ref in refs).astype(BF)
    out[GAIN_AT, :] = pack_gain(sum(unpack_gain(ref[GAIN_AT, :]) for ref in refs))


def stack_rows(*refs):
    refs, out = refs[:-1], refs[-1]
    for j, ref in enumerate(refs):
        out[j * 256 : (j + 1) * 256, :] = ref[0:256, :]
    out[1024:1040, :] = refs[0][GAIN_AT, :]


def ff_sum_first(ids, own, a, b, *outs):
    v = ids[2]
    for k in range(4):
        at = lax.rem(v + k, 4)
        outs[k][...] = (own[at].astype(F32) + a[at].astype(F32) + b[at].astype(F32)).astype(BF)


def ff_sum_second(own, a, b, c, out):
    out[...] = sum_four(own[...], a[...], b[...], c[...]).astype(BF)


def final_attn(ids, *refs):
    pieces, (qkv, out, gain) = refs[:8], refs[8:]
    step = pl.program_id(0)
    for side in range(2):
        core = ids[0] if side == 0 else 1 - ids[0]
        u = ids[1] if side == 0 else ids[2]
        v = ids[2] if side == 0 else ids[1]
        for k in range(4):
            piece = pieces[side * 4 + k]

            @pl.when(lax.rem(u + k, 4) == step)
            def _(piece=piece, v=v, core=core):
                for j in range(4):
                    at = pl.ds(pl.multiple_of(lax.rem(v + j, 4) * HD, HD), HD)
                    for block in range(4):
                        target, column = (qkv, block * D) if block < 3 else (out, 0)
                        lanes = pl.ds(pl.multiple_of(core * HALF + column, HALF), HALF)
                        first = j * 256 + block * HD
                        target[at, lanes] = piece[first : first + HD, :].astype(F32)

    mine = sum(unpack_gain(piece[1024:1040, :]) for piece in pieces[:4])
    other = sum(unpack_gain(piece[1024:1040, :]) for piece in pieces[4:])
    total = mine + other
    for i in range(2):
        for h in range(2):
            gain[i : i + 1, h * HALF : (h + 1) * HALF] = total[2 * i + h : 2 * i + h + 1, :]


SMEM = pltpu.MemorySpace.SMEM
VMEM = pltpu.MemorySpace.VMEM


def size(shape, dtype):
    return math.prod(shape) * jnp.dtype(dtype).itemsize


class Arriving:
    def __init__(self, copy, buffer):
        self.copy, self.buffer, self.here = copy, buffer, False

    def ready(self):
        if not self.here:
            self.copy.wait()
            self.here = True
        return self.buffer

    def __getitem__(self, index):
        return self.ready()[index]


class ArrivingBlocks:
    def __init__(self, blocks):
        self.blocks = blocks

    def block(self, j):
        return self.blocks[j]


def fetching(kernel, n_args, n_outs, plan):
    def wrapped(*refs):
        args, outs, rest = list(refs[:n_args]), refs[n_args : n_args + n_outs], refs[n_args + n_outs :]
        scratch, buffers, sems = rest[: len(rest) - len(plan) - 1], rest[len(rest) - len(plan) - 1 : -1], rest[-1]
        arriving = []
        blocks = {}
        for i, (a, j) in enumerate(plan):
            source = refs[a] if j is None else refs[a].at[:, j * D : (j + 1) * D]
            copy = pltpu.make_async_copy(source, buffers[i], sems.at[i])
            copy.start()
            arriving.append(Arriving(copy, buffers[i]))
            if j is None:
                args[a] = arriving[-1]
            else:
                blocks.setdefault(a, {})[j] = arriving[-1]
        for a, found in blocks.items():
            args[a] = ArrivingBlocks(found)
        kernel(*args, *outs, *scratch)
        for value in arriving:
            value.ready()

    return wrapped


def call(kernel, args, outs, scratch=(), spaces=None, spare=6, fetch=()):
    spaces = dict(spaces or {})
    scratch = list(scratch)
    plan = [f if isinstance(f, tuple) else (f, None) for f in fetch]
    if plan:
        for a, j in plan:
            spaces[a] = pl.ANY
            shape = args[a].shape if j is None else (args[a].shape[0], D)
            scratch.append(pltpu.VMEM(shape, args[a].dtype))
        scratch.append(pltpu.SemaphoreType.DMA((len(plan),)))
        kernel = fetching(kernel, len(args), len(outs), plan)
    vmem = sum(size(a.shape, a.dtype) for i, a in enumerate(args) if i not in spaces)
    vmem += sum(size(*o) for o in outs)
    vmem += sum(size(s.shape, s.dtype) for s in scratch if hasattr(s, "shape") and s.memory_space == VMEM)
    specs = [pl.BlockSpec(memory_space=spaces.get(i, VMEM)) for i in range(len(args))]
    return pl.pallas_call(
        kernel,
        out_shape=[jax.ShapeDtypeStruct(s, t) for s, t in outs],
        in_specs=specs,
        out_specs=[pl.BlockSpec(memory_space=VMEM) for _ in outs],
        scratch_shapes=scratch,
        compiler_params=pltpu.CompilerParams(vmem_limit_bytes=vmem + spare * 1024 * 1024),
    )(*args)


def nothing(outs):
    def kernel(*refs):
        pass

    return pl.pallas_call(
        kernel,
        out_shape=[jax.ShapeDtypeStruct(s, t) for s, t in outs],
        out_specs=[pl.BlockSpec(memory_space=pl.ANY) for _ in outs],
    )()


def on_section(flag, kernel, args, outs, **rest):
    return lax.cond(
        flag, lambda: call(kernel, args, outs, **rest), lambda: nothing(outs)
    )


def along(value, by):
    return lax.ppermute(value, "s", [(0, 1)] if by > 0 else [(1, 0)])


def swap(value, axis, sections=(0, 1)):
    pairs = [(s * 2 + i, s * 2 + 1 - i) for s in sections for i in range(2)]
    return lax.ppermute(value, ("s", axis), pairs)


def plane_shift(value, which, by, sections=(0, 1)):
    pairs = []
    for s in sections:
        for y in range(4):
            for x in range(4):
                for core in range(2):
                    ty, tx = ((y + by) % 4, x) if core == which else (y, (x + by) % 4)
                    pairs.append((((s * 4 + y) * 4 + x) * 2 + core, ((s * 4 + ty) * 4 + tx) * 2 + core))
    return lax.ppermute(value, ("s", "y", "x", "core"), pairs)


def exchange(blocks, which, sections=(0, 1)):
    return [plane_shift(blocks[k], which, k, sections) for k in (1, 2, 3)]


def collect(block, which):
    return [block] + [plane_shift(block, which, -k) for k in (1, 2, 3)]


def pick(stack, index, dim):
    return lax.dynamic_index_in_dim(stack, index, dim, keepdims=False)


def shards(patch_io, byte_states, patch_lengths, patch_live, attn_qkv, attn_out, gains, ff_weights):
    section = lax.axis_index("s")
    core = lax.axis_index("core")
    zh = lax.axis_index("zh")
    y, x = lax.axis_index("y"), lax.axis_index("x")
    first = section == 0
    second = section == 1
    ids = jnp.stack([core, jnp.where(core == 0, y, x), jnp.where(core == 0, x, y), zh, section])
    ids = ids.astype(jnp.int32)
    w_qkv = attn_qkv[0]
    w_out = attn_out[0]
    gain_pair = gains[0]
    micro, seq = patch_io.shape[1], patch_io.shape[3]
    half_bytes = byte_states.shape[2]
    units = ff_weights.shape[0]
    rows = micro * seq
    own_rows = patch_io.reshape(rows, D)
    up_a = along(byte_states[0, 0], -1)
    up_b = along(byte_states[1, 0], -1)
    lower = byte_states.reshape(micro * half_bytes, D)
    w_ff = jnp.swapaxes(ff_weights, 0, 1)
    lengths = patch_lengths[:, 0]
    live = patch_live[:, 0]
    ends = jnp.cumsum(lengths, axis=1)
    bounds = jnp.tile(jnp.stack([ends - lengths, ends], 1), (1, 1, 4))
    places = lax.iota(jnp.int32, seq)
    causal = places[:, None] <= places[None, :]
    diagonal = places[:, None] == places[None, :]
    allowed = causal[None] & ((live[:, :, None] == 1) | diagonal[None])
    allowed = lax.optimization_barrier(jnp.tile(allowed.astype(F32), (1, 1, 4)))

    wide = ((rows, D), BF)
    short = ((seq, D), BF)
    tall = ((micro * half_bytes, D), BF)
    piece = ((half_bytes, D), BF)
    pn, q, bn_lo, k_lo, v_lo = on_section(
        first,
        encode_lower,
        (own_rows, lower, w_qkv, gain_pair),
        [wide, wide, tall, tall, tall],
        fetch=((2, 0), 1, (2, 1), (2, 2)),
    )
    rest = []
    for m, up in enumerate((up_a, up_b)):
        rest.append(
            on_section(
                first,
                functools.partial(encode_rest, m),
                (own_rows, up, w_qkv, w_out, gain_pair, bounds, q, k_lo, v_lo),
                [short, short, ((8, 256, GROUP), BF), piece, piece, piece],
                fetch=((2, 1), (2, 2), 7, 8, 3),
            )
        )
    (hb_a, o_a, w_a, bn_a, k_a, v_a), (hb_b, o_b, w_b, bn_b, k_b, v_b) = rest
    arrived = [along(hb_a, 1), along(hb_b, 1)]

    step = 256
    latent_outs = [
        ((rows, D), F32), wide, ((2, D), F32), ((256, HALF), BF), ((512, HALF), BF), ((PACK_ROWS, rows), BF),
    ]

    def latent():
        return call(
            latent_layer,
            (ids, *arrived, own_rows, allowed, w_qkv, w_out, gain_pair, w_ff),
            latent_outs,
            spaces={0: SMEM, 8: pl.ANY},
            fetch=((5, 0), (5, 1), (5, 2), 6),
            scratch=[
                pltpu.VMEM((rows, 3 * D), BF),
                pltpu.VMEM((8, HD, GROUP), BF),
                pltpu.VMEM((rows, D), BF),
                pltpu.VMEM((2, 3, step, D), BF),
                pltpu.VMEM((rows, D), F32),
                pltpu.VMEM((rows, D), F32),
                pltpu.VMEM((rows, 3 * D), BF),
                pltpu.SemaphoreType.DMA((2,)),
            ],
        )

    def turn():
        return nothing(latent_outs[:5]) + call(
            turn_encoder, (pn, o_a, o_b, bn_lo, bn_a, bn_b), latent_outs[5:]
        )

    latents, dhb, latent_gain, norms, lat_grads, packed = lax.cond(second, latent, turn)
    returned = along(dhb, -1)

    packed_far = swap(packed, "core")

    share = units // 16
    ff_block = ((4, 3 * share, HALF), BF)
    ff_half = ((4, 3 * share, GROUP), BF)
    ff_own, ff_right, ff_left, ff_far_a, ff_far_b = on_section(
        second,
        ff_weights_grad,
        (ids, packed, packed_far, norms),
        [ff_block, ff_block, ff_block, ff_half, ff_half],
        spaces={0: SMEM},
    )
    from_left = plane_shift(ff_far_a, 0, 1, (1,))
    from_right = plane_shift(ff_far_b, 0, -1, (1,))

    grads_long = ((2304, HALF), BF)
    enc_grads, enc_other = on_section(
        first,
        encoder_attention_back,
        (ids, returned, w_out, q, k_lo, v_lo, k_a, k_b, v_a, v_b, w_a, w_b),
        [grads_long, grads_long],
        spaces={0: SMEM},
        fetch=(2, 5, 8, 10, 4, 6, 9, 11, 7),
    )
    enc_far = swap(enc_other, "core", (0,))
    up_grad, up_gain = on_section(
        first,
        encoder_upper_back,
        (ids, up_a, up_b, w_qkv, gain_pair, enc_grads, enc_other),
        [tall, ((1, D), F32)],
        spaces={0: SMEM},
        fetch=(5, (3, 1), 6, (3, 2), 1, 2),
    )
    up_arrived = along(up_grad, 1)
    outs = [((4, 256, HALF), BF)] * 4
    blocks = lax.cond(
        first,
        lambda: call(
            encoder_weights,
            (ids, packed, packed_far, enc_grads, enc_far, up_gain),
            outs,
            spaces={0: SMEM, 5: pl.ANY},
            fetch=(3, 4, 1, 2),
        ),
        lambda: call(latent_weights, (ids, packed, packed_far, lat_grads), outs, spaces={0: SMEM}),
    )
    last, from_left, from_right = lax.optimization_barrier((blocks[3], from_left, from_right))
    blocks = [*blocks[:3], last]
    got, up_arrived = lax.optimization_barrier((exchange(blocks, 0), up_arrived))
    low_outs = [((rows, D), F32), tall, ((2, D), F32)]

    def lower_grads():
        parts = call(
            encoder_lower_back,
            (ids, returned, own_rows, lower, w_qkv, gain_pair, enc_grads, enc_other, blocks[0]),
            low_outs,
            spaces={0: SMEM, 8: pl.ANY},
            fetch=(6, 7, (4, 0), (4, 1), (4, 2), 3),
        )
        return (*parts, *nothing([ff_block, ff_block]))

    def ff_middle():
        added = call(
            ff_add, (ff_right, ff_left, from_left, from_right, blocks[0]), [ff_block, ff_block], spaces={4: pl.ANY}
        )
        return (*nothing(low_outs), *added)

    patch_grad, low_grad, encoder_gain, ff_right_sum, ff_left_sum = lax.cond(first, lower_grads, ff_middle)
    line = [((272, HALF), BF)]
    blocks = call(
        attn_sum_first_gain,
        (ids, blocks[0], *got, encoder_gain, up_gain, latent_gain),
        line * 4,
        spaces={0: SMEM},
    )
    ff_right_sum, ff_left_sum, _ = lax.optimization_barrier((ff_right_sum, ff_left_sum, blocks))
    from_left = plane_shift(ff_right_sum, 0, 1, (1,))
    from_right = plane_shift(ff_left_sum, 0, -1, (1,))
    (block,) = call(sum_all, (blocks[0], *exchange(blocks, 1)), line)
    from_left, from_right, block = lax.optimization_barrier((from_left, from_right, block))
    ff_line = ((3 * share, HALF), BF)
    ff_blocks = on_section(
        second, ff_sum_first, (ids, ff_own, from_left, from_right), [ff_line] * 4, spaces={0: SMEM}
    )
    ff_got = exchange(ff_blocks, 1, (1,))
    across, ff_got = lax.optimization_barrier((swap(block, "zh"), ff_got))
    (block,) = call(sum_all, (block, across), line)
    (block,) = call(stack_rows, collect(block, 1), [((1040, HALF), BF)])
    pieces = collect(block, 0)
    own_far = swap(block, "core")
    (ff_sum,) = on_section(second, ff_sum_second, (ff_blocks[0], *ff_got), [ff_line])
    ff_sum = ff_sum.reshape(3, 2, share // 2, HALF)
    ff_far = swap(pick(ff_sum, 1 - zh, 1), "zh", (1,))
    ff_sum = (pick(ff_sum, zh, 1).astype(F32) + ff_far.astype(F32)).astype(BF).reshape(3, 2, share // 4, HALF)
    ff_mine = pick(ff_sum, core, 1)
    ff_far = swap(pick(ff_sum, 1 - core, 1), "core", (1,))

    def ff_result():
        low, high = jnp.where(core == 0, ff_mine, ff_far), jnp.where(core == 0, ff_far, ff_mine)
        return jnp.swapaxes(jnp.concatenate([low, high], 2), 0, 1).astype(F32)

    ff_grad = lax.cond(second, ff_result, lambda: jnp.zeros((share // 4, 3, D), F32))
    byte_grad = jnp.where(first, low_grad, up_arrived)
    patch_out = jnp.where(first, patch_grad, latents)
    patch_out, ff_grad, *pieces = lax.optimization_barrier((patch_out, ff_grad, *pieces))
    pieces = pieces + [own_far] + [swap(p, "core") for p in pieces[1:]]
    whole = lambda p: pl.BlockSpec(p.shape, lambda i, n=p.ndim: (0,) * n)
    total_qkv, total_out, total_gain = pl.pallas_call(
        final_attn,
        grid=(4,),
        out_shape=[
            jax.ShapeDtypeStruct((D, 3 * D), F32),
            jax.ShapeDtypeStruct((D, D), F32),
            jax.ShapeDtypeStruct((2, D), F32),
        ],
        in_specs=[pl.BlockSpec(memory_space=SMEM)] + [whole(p) for p in pieces],
        out_specs=[
            pl.BlockSpec((256, 3 * D), lambda i: (i, 0)),
            pl.BlockSpec((256, D), lambda i: (i, 0)),
            pl.BlockSpec((2, D), lambda i: (0, 0)),
        ],
        compiler_params=pltpu.CompilerParams(vmem_limit_bytes=FINAL_VMEM),
    )(ids, *pieces)
    return (
        patch_out.reshape(1, micro, 1, seq, D),
        byte_grad.reshape(micro, 1, half_bytes, D),
        total_qkv[None],
        total_out[None],
        total_gain[None],
        ff_grad[None],
    )


def solution(mesh):
    fine = Mesh(mesh.devices.reshape(2, 4, 4, 2, 2), ("s",) + BATCH)
    in_specs = (
        P("s", None, BATCH, None, None),
        P(None, BATCH, "s", None),
        P(None, BATCH, None),
        P(None, BATCH, None),
        P("s", None, None),
        P("s", None, None),
        P("s", None, None),
        P(),
    )
    out_specs = (
        P("s", None, BATCH, None, None),
        P(None, BATCH, "s", None),
        P("s", None, None),
        P("s", None, None),
        P("s", None, None),
        P("s", BATCH, None, None),
    )
    return jax.shard_map(shards, mesh=fine, in_specs=in_specs, out_specs=out_specs, check_vma=False)
```

```python
import functools
import math

import jax
import jax.numpy as jnp
from jax import lax
from jax.experimental import pallas as pl
from jax.experimental.pallas import tpu as pltpu
from jax.sharding import Mesh
from jax.sharding import PartitionSpec as P

HD = 64
SCALE = HD**-0.5
EPS = 1e-05
NEG = -1e30
BATCH = ("y", "x", "zh", "core")
BF = jnp.bfloat16
F32 = jnp.float32
D = 1024
HALF = 512
GROUP = 256
FINAL_VMEM = 32 * 1024 * 1024


UNITS = 2816
PACK_NORMS = 3 * UNITS
PACK_LEFT = PACK_NORMS + 4 * 256
PACK_GRADS = PACK_LEFT + 2 * D
PACK_ROWS = PACK_GRADS + 4 * 512


def nn(a, b):
    return lax.dot_general(a, b, (((1,), (0,)), ((), ())), preferred_element_type=F32)


def nt(a, b):
    return lax.dot_general(a, b, (((1,), (1,)), ((), ())), preferred_element_type=F32)


def tn(a, b):
    return lax.dot_general(a, b, (((0,), (0,)), ((), ())), preferred_element_type=F32)


def inverse_rms(x):
    return lax.rsqrt(jnp.mean(x * x, axis=-1, keepdims=True) + EPS)


def norm_back(x, gain, up):
    r = inverse_rms(x)
    scaled = up * gain
    inner = jnp.mean(scaled * x, axis=-1, keepdims=True)
    return r * (scaled - x * (r * r * inner)), up * (x * r)


def stack_heads(rows):
    head = lax.broadcasted_iota(jnp.int32, rows.shape, 1) // HD
    return jnp.concatenate([jnp.where(head == h, rows, jnp.zeros_like(rows)) for h in range(4)], 0)


def unstack_heads(stacked):
    head = lax.broadcasted_iota(jnp.int32, (HD, GROUP), 1) // HD
    out = stacked[0:HD]
    for h in range(1, 4):
        out = jnp.where(head == h, stacked[h * HD : (h + 1) * HD], out)
    return out


def softmax_columns(scores):
    top = functools.reduce(jnp.maximum, [jnp.max(s, axis=0, keepdims=True) for s in scores])
    parts = [jnp.exp(s - top) for s in scores]
    inverse = 1.0 / sum(jnp.sum(p, axis=0, keepdims=True) for p in parts)
    return [(p * inverse).astype(BF) for p in parts]


def encode_lower(patch, low, w_qkv, gains, pn, q, bn, k, v):
    x = patch[...].astype(F32)
    normed = (x * inverse_rms(x) * gains[0:1]).astype(BF)
    pn[...] = normed
    q[...] = nn(normed, w_qkv.block(0)[...]).astype(BF)
    for i in range(2):
        at = pl.ds(i * 256, 256)
        b = low[at, :].astype(F32)
        normed = (b * inverse_rms(b) * gains[1:2]).astype(BF)
        bn[at, :] = normed
        k[at, :] = nn(normed, w_qkv.block(1)[...]).astype(BF)
        v[at, :] = nn(normed, w_qkv.block(2)[...]).astype(BF)


def encode_rest(m, patch, up, w_qkv, w_out, gains, bounds, q, k_lo, v_lo, hb, o1, weights, bn, k, v):
    b = up[...].astype(F32)
    normed = (b * inverse_rms(b) * gains[1:2]).astype(BF)
    bn[...] = normed
    k[...] = nn(normed, w_qkv.block(1)[...]).astype(BF)
    v[...] = nn(normed, w_qkv.block(2)[...]).astype(BF)
    spot = lax.broadcasted_iota(jnp.int32, (256, GROUP), 0)
    start = bounds[m, 0:1, :]
    end = bounds[m, 1:2, :]
    inside = [(spot + h * 256 >= start) & (spot + h * 256 < end) for h in range(2)]
    low_at = slice(m * 256, (m + 1) * 256)
    rows = slice(m * HD, (m + 1) * HD)
    for g in range(4):
        lanes = slice(g * GROUP, (g + 1) * GROUP)
        stacked = stack_heads(q[rows, lanes] * BF(SCALE))
        scores = [
            jnp.where(inside[h], nt(keys, stacked), NEG)
            for h, keys in enumerate((k_lo[low_at, lanes], k[:, lanes]))
        ]
        w = softmax_columns(scores)
        weights[g * 2] = w[0]
        weights[g * 2 + 1] = w[1]
        mixed = tn(w[0], v_lo[low_at, lanes]) + tn(w[1], v[:, lanes])
        o1[:, lanes] = unstack_heads(mixed).astype(BF)
    hb[...] = (patch[rows, :].astype(F32) + nn(o1[...], w_out[...])).astype(BF)


def latent_layer(
    ids, hb_a, hb_b, cot, allowed, w_qkv, w_out, gains, w_ff, d_hidden,
    latents, dhb, gain_grad, norms, grads, packed,
    qkv, weights, o2, ff_buf, acc_out, acc_norm, dqkv, sems,
):
    core = ids[0]
    units = w_ff.shape[1]
    step = 256
    parts = 4
    part = units // parts

    fetches = []
    for i in range(parts):
        at = slice(i * part, (i + 1) * part)
        fetches.append(pltpu.make_async_copy(w_ff.at[:, at, :], ff_buf.at[:, at, :], sems.at[i]))
        fetches[-1].start()
    x = jnp.concatenate([hb_a[...], hb_b[...]], 0).astype(F32)
    normed = (x * inverse_rms(x) * gains[0:1]).astype(BF)
    packed[PACK_LEFT : PACK_LEFT + D, :] = normed.T
    for j in range(3):
        qkv[:, j * D : (j + 1) * D] = nn(normed, w_qkv.block(j)[...]).astype(BF)
    for m in range(2):
        rows = slice(m * HD, (m + 1) * HD)
        for g in range(4):
            lanes = slice(g * GROUP, (g + 1) * GROUP)
            k_lanes = slice(D + g * GROUP, D + (g + 1) * GROUP)
            v_lanes = slice(2 * D + g * GROUP, 2 * D + (g + 1) * GROUP)
            stacked = stack_heads(qkv[rows, lanes] * BF(SCALE))
            scores = jnp.where(allowed[m] > 0.5, nt(qkv[rows, k_lanes], stacked), NEG)
            (w,) = softmax_columns([scores])
            weights[m * 4 + g] = w
            o2[rows, lanes] = unstack_heads(tn(w, qkv[rows, v_lanes])).astype(BF)
    packed[PACK_LEFT + D : PACK_LEFT + 2 * D, :] = o2[...].T
    after = x + nn(o2[...], w_out[...])
    yn = (after * inverse_rms(after) * gains[1:2]).astype(BF)
    c = cot[...]
    for h in range(2):

        @pl.when(core == h)
        def _(h=h):
            norms[0:128, :] = yn[:, h * HALF : (h + 1) * HALF]
            norms[128:256, :] = c[:, h * HALF : (h + 1) * HALF]

        @pl.when(core != h)
        def _(h=h):
            for b in range(4):
                lanes = slice(h * HALF + b * 128, h * HALF + (b + 1) * 128)
                packed[PACK_NORMS + b * 256 : PACK_NORMS + b * 256 + 128, :] = yn[:, lanes]
                packed[PACK_NORMS + b * 256 + 128 : PACK_NORMS + (b + 1) * 256, :] = c[:, lanes]

    for copy in fetches:
        copy.wait()
    acc_out[...] = after
    for i in range(units // step):
        at = slice(i * step, (i + 1) * step)
        gate = nt(yn, ff_buf[0, at, :])
        upward = nt(yn, ff_buf[1, at, :])
        du = d_hidden[:, at]
        sig = 1.0 / (1.0 + jnp.exp(-gate))
        active = gate * sig
        hidden = (active * upward).astype(BF)
        d_gate = (du * upward * (sig * (1.0 + gate * (1.0 - sig)))).astype(BF)
        d_up = (du * active).astype(BF)
        for j, value in enumerate((d_gate, d_up, hidden)):
            packed[i * step + j * units : (i + 1) * step + j * units, :] = value.T
        acc_out[...] += nn(hidden, ff_buf[2, at, :])
        back = nn(d_gate, ff_buf[0, at, :]) + nn(d_up, ff_buf[1, at, :])
        if i == 0:
            acc_norm[...] = back
        else:
            acc_norm[...] += back
    latents[...] = acc_out[...]
    back, gain_rows = norm_back(after, gains[1:2], acc_norm[...])
    gain_grad[1:2, :] = jnp.sum(gain_rows, axis=0, keepdims=True)
    d_after = c.astype(F32) + back
    da = d_after.astype(BF)
    d_mixed = nt(da, w_out[...]).astype(BF)
    for m in range(2):
        rows = slice(m * HD, (m + 1) * HD)
        for g in range(4):
            lanes = slice(g * GROUP, (g + 1) * GROUP)
            k_lanes = slice(D + g * GROUP, D + (g + 1) * GROUP)
            v_lanes = slice(2 * D + g * GROUP, 2 * D + (g + 1) * GROUP)
            q_stacked = stack_heads(qkv[rows, lanes] * BF(SCALE))
            o_stacked = stack_heads(d_mixed[rows, lanes])
            w_low = weights[m * 4 + g]
            w = w_low.astype(F32)
            dw = nt(qkv[rows, v_lanes], o_stacked)
            inner = jnp.sum(dw * w, axis=0, keepdims=True)
            ds = (w * (dw - inner)).astype(BF)
            dqkv[rows, lanes] = (unstack_heads(tn(ds, qkv[rows, k_lanes])) * SCALE).astype(BF)
            dqkv[rows, k_lanes] = nn(ds, q_stacked).astype(BF)
            dqkv[rows, v_lanes] = nn(w_low, o_stacked).astype(BF)
    d_normed = sum(nt(dqkv[:, j * D : (j + 1) * D], w_qkv.block(j)[...]) for j in range(3))
    back, gain_rows = norm_back(x, gains[0:1], d_normed)
    gain_grad[0:1, :] = jnp.sum(gain_rows, axis=0, keepdims=True)
    dhb[...] = (d_after + back).astype(BF)
    for h in range(2):
        pieces = (
            dqkv[:, h * HALF : (h + 1) * HALF],
            da[:, h * HALF : (h + 1) * HALF],
            dqkv[:, D + h * HALF : D + (h + 1) * HALF],
            dqkv[:, 2 * D + h * HALF : 2 * D + (h + 1) * HALF],
        )

        @pl.when(core == h)
        def _(pieces=pieces):
            for i, value in enumerate(pieces):
                grads[i * 128 : (i + 1) * 128, :] = value

        @pl.when(core != h)
        def _(pieces=pieces):
            for i, value in enumerate(pieces):
                for b in range(4):
                    first = PACK_GRADS + b * 512 + i * 128
                    packed[first : first + 128, :] = value[:, b * 128 : (b + 1) * 128]


def hidden_back(cot, w_ff, d_hidden, buffer, sems):
    parts = 4
    part = w_ff.shape[1] // parts
    copies = []
    for i in range(parts):
        at = slice(i * part, (i + 1) * part)
        copies.append(pltpu.make_async_copy(w_ff.at[2, at, :], buffer.at[at, :], sems.at[i]))
        copies[-1].start()
    for copy in copies:
        copy.wait()
    for i in range(w_ff.shape[1] // 256):
        at = slice(i * 256, (i + 1) * 256)
        d_hidden[:, at] = nt(cot[...], buffer[at, :])


def half_of(core, g, mine, other):
    lanes = slice((g % 2) * GROUP, (g % 2 + 1) * GROUP)

    def put(at, value):
        @pl.when(core == g // 2)
        def _():
            mine[at, lanes] = value

        @pl.when(core != g // 2)
        def _():
            other[at, lanes] = value

    return put


def encoder_attention_back(
    ids, dhb, w_out, q, k_lo, v_lo, k_a, k_b, v_a, v_b, w_a, w_b, mine, other
):
    d_mixed = nt(dhb[...], w_out[...]).astype(BF)
    for g in range(4):
        lanes = slice(g * GROUP, (g + 1) * GROUP)
        put = half_of(ids[0], g, mine, other)
        put(slice(128, 256), dhb[:, lanes])
        for m, (k_up, v_up, weights) in enumerate(((k_a, v_a, w_a), (k_b, v_b, w_b))):
            rows = slice(m * HD, (m + 1) * HD)
            low_at = slice(m * 256, (m + 1) * 256)
            q_stacked = stack_heads(q[rows, lanes] * BF(SCALE))
            o_stacked = stack_heads(d_mixed[rows, lanes])
            low = [weights[g * 2 + h] for h in range(2)]
            w = [piece.astype(F32) for piece in low]
            dw = [nt(values, o_stacked) for values in (v_lo[low_at, lanes], v_up[:, lanes])]
            inner = sum(jnp.sum(a * b, axis=0, keepdims=True) for a, b in zip(dw, w))
            ds = [(b * (a - inner)).astype(BF) for a, b in zip(dw, w)]
            dq = tn(ds[0], k_lo[low_at, lanes]) + tn(ds[1], k_up[:, lanes])
            put(rows, (unstack_heads(dq) * SCALE).astype(BF))
            for h in range(2):
                base = h * HALF + m * 256
                put(slice(256 + base, 512 + base), nn(ds[h], q_stacked).astype(BF))
                put(slice(1280 + base, 1536 + base), nn(low[h], o_stacked).astype(BF))


def both_columns(core, block, w_qkv):
    return [
        w_qkv.block(block)[:, pl.ds(pl.multiple_of(which * HALF, HALF), HALF)] for which in (core, 1 - core)
    ]


def bytes_back(core, h, m, source, w_qkv, gains, grads):
    d_norm = sum(
        nt(ref[1024 * block - 768 + h * HALF + m * 256 : 1024 * block - 512 + h * HALF + m * 256, :], columns)
        for block in (1, 2)
        for ref, columns in zip(grads, both_columns(core, block, w_qkv))
    )
    back, gain_rows = norm_back(source.astype(F32), gains[1:2], d_norm)
    return back.astype(BF), jnp.sum(gain_rows, axis=0, keepdims=True)


def encoder_upper_back(ids, up_a, up_b, w_qkv, gains, mine, other, up_grad, gain_grad):
    total = jnp.zeros((1, D), F32)
    for m, source in enumerate((up_a, up_b)):
        back, rows = bytes_back(ids[0], 1, m, source[...], w_qkv, gains, (mine, other))
        up_grad[m * 256 : (m + 1) * 256, :] = back
        total = total + rows
    gain_grad[...] = total


def encoder_lower_back(
    ids, dhb, patch, low, w_qkv, gains, mine, other, after, patch_grad, low_grad, gain_grad
):
    core = ids[0]
    up_norm = sum(nt(ref[0:128, :], columns) for ref, columns in zip((mine, other), both_columns(core, 0, w_qkv)))
    back, gain_rows = norm_back(patch[...].astype(F32), gains[0:1], up_norm)
    gain_grad[0:1, :] = jnp.sum(gain_rows, axis=0, keepdims=True)
    patch_grad[...] = dhb[...].astype(F32) + back
    total = jnp.zeros((1, D), F32)
    for m in range(2):
        at = slice(m * 256, (m + 1) * 256)
        back, rows = bytes_back(core, 0, m, low[at, :], w_qkv, gains, (mine, other))
        low_grad[at, :] = back
        total = total + rows
    gain_grad[1:2, :] = total


def turn_encoder(pn, o_a, o_b, bn_lo, bn_a, bn_b, packed):
    for b, rows in enumerate([bn_lo[i * 128 : (i + 1) * 128, :] for i in range(4)]
                             + [ref[i * 128 : (i + 1) * 128, :] for ref in (bn_a, bn_b) for i in range(2)]):
        packed[b * D : (b + 1) * D, :] = rows.T
    packed[PACK_LEFT : PACK_LEFT + D, :] = pn[...].T
    packed[PACK_LEFT + D : PACK_LEFT + 2 * D, :] = jnp.concatenate([o_a[...], o_b[...]], 0).T


def rows_of_both(left, left_far, at):
    return jnp.concatenate([left[at, :], left_far[at, :]], 1)


def below(near, far, rows):
    return jnp.concatenate([near[rows, :], far[rows, :]], 0)


def encoder_weights(ids, packed, packed_far, near, far, after, *blocks):
    u = ids[1]
    queries = below(near, far, slice(0, 128))
    outputs = below(near, far, slice(128, 256))
    for k in range(4):
        first = lax.rem(u + k, 4) * 256

        def at(base, first=first):
            return pl.ds(pl.multiple_of(first + base, 256), 256)

        blocks[k][0] = nn(rows_of_both(packed, packed_far, at(PACK_LEFT)), queries).astype(BF)
        blocks[k][3] = nn(rows_of_both(packed, packed_far, at(PACK_LEFT + D)), outputs).astype(BF)
        lefts = [jnp.concatenate([ref[at(b * D), :] for b in range(8)], 1) for ref in (packed, packed_far)]
        for block in (1, 2):
            rows = slice(1024 * block - 768, 1024 * block + 256)
            blocks[k][block] = (nn(lefts[0], near[rows, :]) + nn(lefts[1], far[rows, :])).astype(BF)


def unpack(packed, first, rows):
    return jnp.concatenate([packed[first + b * rows : first + (b + 1) * rows, :] for b in range(4)], 1)


def latent_weights(ids, packed, packed_far, near, *blocks):
    u = ids[1]
    far = unpack(packed_far, PACK_GRADS, 512)
    rights = [jnp.concatenate([near[i * 128 : (i + 1) * 128, :], far[i * 128 : (i + 1) * 128, :]], 0) for i in range(4)]
    for k in range(4):
        first = PACK_LEFT + lax.rem(u + k, 4) * 256
        at = pl.ds(pl.multiple_of(first, 256), 256)
        low_at = pl.ds(pl.multiple_of(first + D, 256), 256)
        for block, (source, i) in enumerate(((at, 0), (at, 2), (at, 3), (low_at, 1))):
            blocks[k][block] = nn(rows_of_both(packed, packed_far, source), rights[i]).astype(BF)


def ff_weights_grad(ids, packed, packed_far, norms, own, right, left, far_a, far_b):
    core, u = ids[0], ids[1]
    share = UNITS // 16
    far = unpack(packed_far, PACK_NORMS, 256)
    normed = jnp.concatenate([norms[0:128, :], far[0:128, :]], 0)
    cot = jnp.concatenate([norms[128:256, :], far[128:256, :]], 0)
    for k in range(4):
        there = lax.rem(u + k, 4)
        for v in range(4):
            chunk = jnp.where(core == 0, there * 4 + v, v * 4 + there)
            for j in range(3):
                at = pl.ds(pl.multiple_of(j * UNITS + chunk * share, 16), share)
                value = nn(rows_of_both(packed, packed_far, at), normed if j < 2 else cot).astype(BF)
                rows = slice(j * share, (j + 1) * share)
                if k == 2:
                    far_a[v, rows, :] = value[:, :GROUP]
                    far_b[v, rows, :] = value[:, GROUP:]
                else:
                    (own, right, None, left)[k][v, rows, :] = value


def ff_add(right, left, from_left, from_right, after, new_right, new_left):
    new_right[:, :, 0:GROUP] = (right[:, :, 0:GROUP].astype(F32) + from_left[...].astype(F32)).astype(BF)
    new_right[:, :, GROUP:] = right[:, :, GROUP:]
    new_left[:, :, 0:GROUP] = left[:, :, 0:GROUP]
    new_left[:, :, GROUP:] = (left[:, :, GROUP:].astype(F32) + from_right[...].astype(F32)).astype(BF)


def sum_four(own, a, b, c):
    return own.astype(F32) + a.astype(F32) + b.astype(F32) + c.astype(F32)


def pack_gain(value):
    high = value.astype(BF)
    low = (value - high.astype(F32)).astype(BF)
    return jnp.concatenate(
        [high.astype(F32), low.astype(F32), jnp.zeros((8, HALF), F32)], 0
    ).astype(BF)


def unpack_gain(rows):
    rows = rows.astype(F32)
    return rows[0:4] + rows[4:8]


GAIN_AT = slice(256, 272)


def attn_sum_first(ids, own, a, b, c, *outs):
    v = ids[2]
    for k in range(4):
        at = pl.ds(pl.multiple_of(lax.rem(v + k, 4) * HD, HD), HD)
        for block in range(4):
            outs[k][block * HD : (block + 1) * HD, :] = sum_four(
                own[block, at, :], a[block, at, :], b[block, at, :], c[block, at, :]
            ).astype(BF)


def attn_sum_first_gain(ids, own, a, b, c, enc_gain, up_gain, lat_gain, *outs):
    attn_sum_first(ids, own, a, b, c, *outs)
    first = ids[4] == 0
    gain = jnp.where(
        first, jnp.concatenate([enc_gain[0:1, :], enc_gain[1:2, :] + up_gain[...]], 0), lat_gain[...]
    )
    halves = [gain[i : i + 1, h * HALF : (h + 1) * HALF] for i in range(2) for h in range(2)]
    packed = pack_gain(jnp.concatenate(halves, 0))
    for out in outs:
        out[GAIN_AT, :] = packed


def sum_all(*refs):
    refs, out = refs[:-1], refs[-1]
    out[0:256, :] = sum(ref[0:256, :].astype(F32) for ref in refs).astype(BF)
    out[GAIN_AT, :] = pack_gain(sum(unpack_gain(ref[GAIN_AT, :]) for ref in refs))


def stack_rows(*refs):
    refs, out = refs[:-1], refs[-1]
    for j, ref in enumerate(refs):
        out[j * 256 : (j + 1) * 256, :] = ref[0:256, :]
    out[1024:1040, :] = refs[0][GAIN_AT, :]


def ff_sum_first(ids, own, a, b, *outs):
    v = ids[2]
    for k in range(4):
        at = lax.rem(v + k, 4)
        outs[k][...] = (own[at].astype(F32) + a[at].astype(F32) + b[at].astype(F32)).astype(BF)


def ff_sum_second(own, a, b, c, out):
    out[...] = sum_four(own[...], a[...], b[...], c[...]).astype(BF)


def final_attn(ids, *refs):
    pieces, (qkv, out, gain) = refs[:8], refs[8:]
    step = pl.program_id(0)
    for side in range(2):
        core = ids[0] if side == 0 else 1 - ids[0]
        u = ids[1] if side == 0 else ids[2]
        v = ids[2] if side == 0 else ids[1]
        for k in range(4):
            piece = pieces[side * 4 + k]

            @pl.when(lax.rem(u + k, 4) == step)
            def _(piece=piece, v=v, core=core):
                for j in range(4):
                    at = pl.ds(pl.multiple_of(lax.rem(v + j, 4) * HD, HD), HD)
                    for block in range(4):
                        target, column = (qkv, block * D) if block < 3 else (out, 0)
                        lanes = pl.ds(pl.multiple_of(core * HALF + column, HALF), HALF)
                        first = j * 256 + block * HD
                        target[at, lanes] = piece[first : first + HD, :].astype(F32)

    mine = sum(unpack_gain(piece[1024:1040, :]) for piece in pieces[:4])
    other = sum(unpack_gain(piece[1024:1040, :]) for piece in pieces[4:])
    total = mine + other
    for i in range(2):
        for h in range(2):
            gain[i : i + 1, h * HALF : (h + 1) * HALF] = total[2 * i + h : 2 * i + h + 1, :]


SMEM = pltpu.MemorySpace.SMEM
VMEM = pltpu.MemorySpace.VMEM


def size(shape, dtype):
    return math.prod(shape) * jnp.dtype(dtype).itemsize


class Arriving:
    def __init__(self, copy, buffer):
        self.copy, self.buffer, self.here = copy, buffer, False

    def ready(self):
        if not self.here:
            self.copy.wait()
            self.here = True
        return self.buffer

    def __getitem__(self, index):
        return self.ready()[index]


class ArrivingBlocks:
    def __init__(self, blocks):
        self.blocks = blocks

    def block(self, j):
        return self.blocks[j]


def fetching(kernel, n_args, n_outs, plan):
    def wrapped(*refs):
        args, outs, rest = list(refs[:n_args]), refs[n_args : n_args + n_outs], refs[n_args + n_outs :]
        scratch, buffers, sems = rest[: len(rest) - len(plan) - 1], rest[len(rest) - len(plan) - 1 : -1], rest[-1]
        arriving = []
        blocks = {}
        for i, (a, j) in enumerate(plan):
            source = refs[a] if j is None else refs[a].at[:, j * D : (j + 1) * D]
            copy = pltpu.make_async_copy(source, buffers[i], sems.at[i])
            copy.start()
            arriving.append(Arriving(copy, buffers[i]))
            if j is None:
                args[a] = arriving[-1]
            else:
                blocks.setdefault(a, {})[j] = arriving[-1]
        for a, found in blocks.items():
            args[a] = ArrivingBlocks(found)
        kernel(*args, *outs, *scratch)
        for value in arriving:
            value.ready()

    return wrapped


def call(kernel, args, outs, scratch=(), spaces=None, spare=6, fetch=()):
    spaces = dict(spaces or {})
    scratch = list(scratch)
    plan = [f if isinstance(f, tuple) else (f, None) for f in fetch]
    if plan:
        for a, j in plan:
            spaces[a] = pl.ANY
            shape = args[a].shape if j is None else (args[a].shape[0], D)
            scratch.append(pltpu.VMEM(shape, args[a].dtype))
        scratch.append(pltpu.SemaphoreType.DMA((len(plan),)))
        kernel = fetching(kernel, len(args), len(outs), plan)
    vmem = sum(size(a.shape, a.dtype) for i, a in enumerate(args) if i not in spaces)
    vmem += sum(size(*o) for o in outs)
    vmem += sum(size(s.shape, s.dtype) for s in scratch if hasattr(s, "shape") and s.memory_space == VMEM)
    specs = [pl.BlockSpec(memory_space=spaces.get(i, VMEM)) for i in range(len(args))]
    return pl.pallas_call(
        kernel,
        out_shape=[jax.ShapeDtypeStruct(s, t) for s, t in outs],
        in_specs=specs,
        out_specs=[pl.BlockSpec(memory_space=VMEM) for _ in outs],
        scratch_shapes=scratch,
        compiler_params=pltpu.CompilerParams(vmem_limit_bytes=vmem + spare * 1024 * 1024),
    )(*args)


def nothing(outs):
    def kernel(*refs):
        pass

    return pl.pallas_call(
        kernel,
        out_shape=[jax.ShapeDtypeStruct(s, t) for s, t in outs],
        out_specs=[pl.BlockSpec(memory_space=pl.ANY) for _ in outs],
    )()


def on_section(flag, kernel, args, outs, **rest):
    return lax.cond(
        flag, lambda: call(kernel, args, outs, **rest), lambda: nothing(outs)
    )


def along(value, by):
    return lax.ppermute(value, "s", [(0, 1)] if by > 0 else [(1, 0)])


def swap(value, axis, sections=(0, 1)):
    pairs = [(s * 2 + i, s * 2 + 1 - i) for s in sections for i in range(2)]
    return lax.ppermute(value, ("s", axis), pairs)


def plane_shift(value, which, by, sections=(0, 1)):
    pairs = []
    for s in sections:
        for y in range(4):
            for x in range(4):
                for core in range(2):
                    ty, tx = ((y + by) % 4, x) if core == which else (y, (x + by) % 4)
                    pairs.append((((s * 4 + y) * 4 + x) * 2 + core, ((s * 4 + ty) * 4 + tx) * 2 + core))
    return lax.ppermute(value, ("s", "y", "x", "core"), pairs)


def exchange(blocks, which, sections=(0, 1)):
    return [plane_shift(blocks[k], which, k, sections) for k in (1, 2, 3)]


def collect(block, which):
    return [block] + [plane_shift(block, which, -k) for k in (1, 2, 3)]


def pick(stack, index, dim):
    return lax.dynamic_index_in_dim(stack, index, dim, keepdims=False)


def shards(patch_io, byte_states, patch_lengths, patch_live, attn_qkv, attn_out, gains, ff_weights):
    section = lax.axis_index("s")
    core = lax.axis_index("core")
    zh = lax.axis_index("zh")
    y, x = lax.axis_index("y"), lax.axis_index("x")
    first = section == 0
    second = section == 1
    ids = jnp.stack([core, jnp.where(core == 0, y, x), jnp.where(core == 0, x, y), zh, section])
    ids = ids.astype(jnp.int32)
    w_qkv = attn_qkv[0]
    w_out = attn_out[0]
    gain_pair = gains[0]
    micro, seq = patch_io.shape[1], patch_io.shape[3]
    half_bytes = byte_states.shape[2]
    units = ff_weights.shape[0]
    rows = micro * seq
    own_rows = patch_io.reshape(rows, D)
    up_a = along(byte_states[0, 0], -1)
    up_b = along(byte_states[1, 0], -1)
    lower = byte_states.reshape(micro * half_bytes, D)
    w_ff = jnp.swapaxes(ff_weights, 0, 1)
    lengths = patch_lengths[:, 0]
    live = patch_live[:, 0]
    ends = jnp.cumsum(lengths, axis=1)
    bounds = jnp.tile(jnp.stack([ends - lengths, ends], 1), (1, 1, 4))
    places = lax.iota(jnp.int32, seq)
    causal = places[:, None] <= places[None, :]
    diagonal = places[:, None] == places[None, :]
    allowed = causal[None] & ((live[:, :, None] == 1) | diagonal[None])
    allowed = lax.optimization_barrier(jnp.tile(allowed.astype(F32), (1, 1, 4)))

    wide = ((rows, D), BF)
    short = ((seq, D), BF)
    tall = ((micro * half_bytes, D), BF)
    piece = ((half_bytes, D), BF)
    (d_hidden,) = on_section(
        second,
        hidden_back,
        (own_rows, w_ff),
        [((rows, units), F32)],
        spaces={1: pl.ANY},
        scratch=[pltpu.VMEM((units, D), BF), pltpu.SemaphoreType.DMA((4,))],
    )
    pn, q, bn_lo, k_lo, v_lo = on_section(
        first,
        encode_lower,
        (own_rows, lower, w_qkv, gain_pair),
        [wide, wide, tall, tall, tall],
        fetch=((2, 0), 1, (2, 1), (2, 2)),
    )
    rest = []
    for m, up in enumerate((up_a, up_b)):
        rest.append(
            on_section(
                first,
                functools.partial(encode_rest, m),
                (own_rows, up, w_qkv, w_out, gain_pair, bounds, q, k_lo, v_lo),
                [short, short, ((8, 256, GROUP), BF), piece, piece, piece],
                fetch=((2, 1), (2, 2), 7, 8, 3),
            )
        )
    (hb_a, o_a, w_a, bn_a, k_a, v_a), (hb_b, o_b, w_b, bn_b, k_b, v_b) = rest
    arrived = [along(hb_a, 1), along(hb_b, 1)]

    latent_outs = [
        ((rows, D), F32), wide, ((2, D), F32), ((256, HALF), BF), ((512, HALF), BF), ((PACK_ROWS, rows), BF),
    ]

    def latent():
        return call(
            latent_layer,
            (ids, *arrived, own_rows, allowed, w_qkv, w_out, gain_pair, w_ff, d_hidden),
            latent_outs,
            spaces={0: SMEM, 8: pl.ANY},
            fetch=((5, 0), (5, 1), (5, 2), 6),
            scratch=[
                pltpu.VMEM((rows, 3 * D), BF),
                pltpu.VMEM((8, HD, GROUP), BF),
                pltpu.VMEM((rows, D), BF),
                pltpu.VMEM((3, units, D), BF),
                pltpu.VMEM((rows, D), F32),
                pltpu.VMEM((rows, D), F32),
                pltpu.VMEM((rows, 3 * D), BF),
                pltpu.SemaphoreType.DMA((4,)),
            ],
        )

    def turn():
        return nothing(latent_outs[:5]) + call(
            turn_encoder, (pn, o_a, o_b, bn_lo, bn_a, bn_b), latent_outs[5:]
        )

    latents, dhb, latent_gain, norms, lat_grads, packed = lax.cond(second, latent, turn)
    returned = along(dhb, -1)

    packed_far = swap(packed, "core")

    share = units // 16
    ff_block = ((4, 3 * share, HALF), BF)
    ff_half = ((4, 3 * share, GROUP), BF)
    ff_own, ff_right, ff_left, ff_far_a, ff_far_b = on_section(
        second,
        ff_weights_grad,
        (ids, packed, packed_far, norms),
        [ff_block, ff_block, ff_block, ff_half, ff_half],
        spaces={0: SMEM},
    )

    grads_long = ((2304, HALF), BF)
    enc_grads, enc_other = on_section(
        first,
        encoder_attention_back,
        (ids, returned, w_out, q, k_lo, v_lo, k_a, k_b, v_a, v_b, w_a, w_b),
        [grads_long, grads_long],
        spaces={0: SMEM},
        fetch=(2, 5, 8, 10, 4, 6, 9, 11, 7),
    )
    enc_far = swap(enc_other, "core", (0,))
    up_grad, up_gain = on_section(
        first,
        encoder_upper_back,
        (ids, up_a, up_b, w_qkv, gain_pair, enc_grads, enc_other),
        [tall, ((1, D), F32)],
        spaces={0: SMEM},
        fetch=(5, (3, 1), 6, (3, 2), 1, 2),
    )
    up_arrived = along(up_grad, 1)
    ff_far_a, ff_far_b, up_gain = lax.optimization_barrier((ff_far_a, ff_far_b, up_gain))
    from_left = plane_shift(ff_far_a, 0, 1, (1,))
    from_right = plane_shift(ff_far_b, 0, -1, (1,))
    outs = [((4, 256, HALF), BF)] * 4
    blocks = lax.cond(
        first,
        lambda: call(
            encoder_weights,
            (ids, packed, packed_far, enc_grads, enc_far, up_gain),
            outs,
            spaces={0: SMEM, 5: pl.ANY},
            fetch=(3, 4, 1, 2),
        ),
        lambda: call(latent_weights, (ids, packed, packed_far, lat_grads), outs, spaces={0: SMEM}),
    )
    last, from_left, from_right = lax.optimization_barrier((blocks[3], from_left, from_right))
    blocks = [*blocks[:3], last]
    got, up_arrived = lax.optimization_barrier((exchange(blocks, 0), up_arrived))
    low_outs = [((rows, D), F32), tall, ((2, D), F32)]

    def lower_grads():
        parts = call(
            encoder_lower_back,
            (ids, returned, own_rows, lower, w_qkv, gain_pair, enc_grads, enc_other, blocks[0]),
            low_outs,
            spaces={0: SMEM, 8: pl.ANY},
            fetch=(6, 7, (4, 0), (4, 1), (4, 2), 3),
        )
        return (*parts, *nothing([ff_block, ff_block]))

    def ff_middle():
        added = call(
            ff_add, (ff_right, ff_left, from_left, from_right, blocks[0]), [ff_block, ff_block], spaces={4: pl.ANY}
        )
        return (*nothing(low_outs), *added)

    patch_grad, low_grad, encoder_gain, ff_right_sum, ff_left_sum = lax.cond(first, lower_grads, ff_middle)
    line = [((272, HALF), BF)]
    blocks = call(
        attn_sum_first_gain,
        (ids, blocks[0], *got, encoder_gain, up_gain, latent_gain),
        line * 4,
        spaces={0: SMEM},
    )
    ff_right_sum, ff_left_sum, _ = lax.optimization_barrier((ff_right_sum, ff_left_sum, blocks))
    from_left = plane_shift(ff_right_sum, 0, 1, (1,))
    from_right = plane_shift(ff_left_sum, 0, -1, (1,))
    (block,) = call(sum_all, (blocks[0], *exchange(blocks, 1)), line)
    byte_grad = jnp.where(first, low_grad, up_arrived)
    patch_out = jnp.where(first, patch_grad, latents)
    from_left, from_right, block, byte_grad, patch_out = lax.optimization_barrier(
        (from_left, from_right, block, byte_grad, patch_out)
    )
    ff_line = ((3 * share, HALF), BF)
    ff_blocks = on_section(
        second, ff_sum_first, (ids, ff_own, from_left, from_right), [ff_line] * 4, spaces={0: SMEM}
    )
    ff_got = exchange(ff_blocks, 1, (1,))
    across, ff_got = lax.optimization_barrier((swap(block, "zh"), ff_got))
    (block,) = call(sum_all, (block, across), line)
    (block,) = call(stack_rows, collect(block, 1), [((1040, HALF), BF)])
    pieces = collect(block, 0)
    own_far = swap(block, "core")
    (ff_sum,) = on_section(second, ff_sum_second, (ff_blocks[0], *ff_got), [ff_line])
    ff_sum = ff_sum.reshape(3, 2, share // 2, HALF)
    ff_far = swap(pick(ff_sum, 1 - zh, 1), "zh", (1,))
    ff_sum = (pick(ff_sum, zh, 1).astype(F32) + ff_far.astype(F32)).astype(BF).reshape(3, 2, share // 4, HALF)
    ff_mine = pick(ff_sum, core, 1)
    ff_far = swap(pick(ff_sum, 1 - core, 1), "core", (1,))

    def ff_result():
        low, high = jnp.where(core == 0, ff_mine, ff_far), jnp.where(core == 0, ff_far, ff_mine)
        return jnp.swapaxes(jnp.concatenate([low, high], 2), 0, 1).astype(F32)

    ff_grad = lax.cond(second, ff_result, lambda: jnp.zeros((share // 4, 3, D), F32))
    ff_grad, *pieces = lax.optimization_barrier((ff_grad, *pieces))
    pieces = pieces + [own_far] + [swap(p, "core") for p in pieces[1:]]
    whole = lambda p: pl.BlockSpec(p.shape, lambda i, n=p.ndim: (0,) * n)
    total_qkv, total_out, total_gain = pl.pallas_call(
        final_attn,
        grid=(4,),
        out_shape=[
            jax.ShapeDtypeStruct((D, 3 * D), F32),
            jax.ShapeDtypeStruct((D, D), F32),
            jax.ShapeDtypeStruct((2, D), F32),
        ],
        in_specs=[pl.BlockSpec(memory_space=SMEM)] + [whole(p) for p in pieces],
        out_specs=[
            pl.BlockSpec((256, 3 * D), lambda i: (i, 0)),
            pl.BlockSpec((256, D), lambda i: (i, 0)),
            pl.BlockSpec((2, D), lambda i: (0, 0)),
        ],
        compiler_params=pltpu.CompilerParams(vmem_limit_bytes=FINAL_VMEM),
    )(ids, *pieces)
    return (
        patch_out.reshape(1, micro, 1, seq, D),
        byte_grad.reshape(micro, 1, half_bytes, D),
        total_qkv[None],
        total_out[None],
        total_gain[None],
        ff_grad[None],
    )


def solution(mesh):
    fine = Mesh(mesh.devices.reshape(2, 4, 4, 2, 2), ("s",) + BATCH)
    in_specs = (
        P("s", None, BATCH, None, None),
        P(None, BATCH, "s", None),
        P(None, BATCH, None),
        P(None, BATCH, None),
        P("s", None, None),
        P("s", None, None),
        P("s", None, None),
        P(),
    )
    out_specs = (
        P("s", None, BATCH, None, None),
        P(None, BATCH, "s", None),
        P("s", None, None),
        P("s", None, None),
        P("s", None, None),
        P("s", BATCH, None, None),
    )
    return jax.shard_map(shards, mesh=fine, in_specs=in_specs, out_specs=out_specs, check_vma=False)
```

```python
import functools
import math

import jax
import jax.numpy as jnp
from jax import lax
from jax.experimental import pallas as pl
from jax.experimental.pallas import tpu as pltpu
from jax.sharding import Mesh
from jax.sharding import PartitionSpec as P

HD = 64
SCALE = HD**-0.5
EPS = 1e-05
NEG = -1e30
BATCH = ("y", "x", "zh", "core")
BF = jnp.bfloat16
F32 = jnp.float32
D = 1024
HALF = 512
GROUP = 256
FINAL_VMEM = 32 * 1024 * 1024


UNITS = 2816
PACK_NORMS = 3 * UNITS
PACK_LEFT = PACK_NORMS + 4 * 256
PACK_GRADS = PACK_LEFT + 2 * D
PACK_ROWS = PACK_GRADS + 4 * 512


def nn(a, b):
    return lax.dot_general(a, b, (((1,), (0,)), ((), ())), preferred_element_type=F32)


def nt(a, b):
    return lax.dot_general(a, b, (((1,), (1,)), ((), ())), preferred_element_type=F32)


def tn(a, b):
    return lax.dot_general(a, b, (((0,), (0,)), ((), ())), preferred_element_type=F32)


def inverse_rms(x):
    return lax.rsqrt(jnp.mean(x * x, axis=-1, keepdims=True) + EPS)


def norm_back(x, gain, up):
    r = inverse_rms(x)
    scaled = up * gain
    inner = jnp.mean(scaled * x, axis=-1, keepdims=True)
    return r * (scaled - x * (r * r * inner)), up * (x * r)


def stack_heads(rows):
    head = lax.broadcasted_iota(jnp.int32, rows.shape, 1) // HD
    return jnp.concatenate([jnp.where(head == h, rows, jnp.zeros_like(rows)) for h in range(4)], 0)


def unstack_heads(stacked):
    head = lax.broadcasted_iota(jnp.int32, (HD, GROUP), 1) // HD
    out = stacked[0:HD]
    for h in range(1, 4):
        out = jnp.where(head == h, stacked[h * HD : (h + 1) * HD], out)
    return out


def softmax_columns(scores):
    top = functools.reduce(jnp.maximum, [jnp.max(s, axis=0, keepdims=True) for s in scores])
    parts = [jnp.exp(s - top) for s in scores]
    inverse = 1.0 / sum(jnp.sum(p, axis=0, keepdims=True) for p in parts)
    return [(p * inverse).astype(BF) for p in parts]


def encode_lower(patch, low, w_qkv, gains, pn, q, bn, k, v):
    x = patch[...].astype(F32)
    normed = (x * inverse_rms(x) * gains[0:1]).astype(BF)
    pn[...] = normed
    q[...] = nn(normed, w_qkv.block(0)[...]).astype(BF)
    for i in range(2):
        at = pl.ds(i * 256, 256)
        b = low[at, :].astype(F32)
        normed = (b * inverse_rms(b) * gains[1:2]).astype(BF)
        bn[at, :] = normed
        k[at, :] = nn(normed, w_qkv.block(1)[...]).astype(BF)
        v[at, :] = nn(normed, w_qkv.block(2)[...]).astype(BF)


def encode_rest(m, patch, up, w_qkv, w_out, gains, bounds, q, k_lo, v_lo, hb, o1, weights, bn, k, v):
    b = up[...].astype(F32)
    normed = (b * inverse_rms(b) * gains[1:2]).astype(BF)
    bn[...] = normed
    k[...] = nn(normed, w_qkv.block(1)[...]).astype(BF)
    v[...] = nn(normed, w_qkv.block(2)[...]).astype(BF)
    spot = lax.broadcasted_iota(jnp.int32, (256, GROUP), 0)
    start = bounds[m, 0:1, :]
    end = bounds[m, 1:2, :]
    inside = [(spot + h * 256 >= start) & (spot + h * 256 < end) for h in range(2)]
    low_at = slice(m * 256, (m + 1) * 256)
    rows = slice(m * HD, (m + 1) * HD)
    for g in range(4):
        lanes = slice(g * GROUP, (g + 1) * GROUP)
        stacked = stack_heads(q[rows, lanes] * BF(SCALE))
        scores = [
            jnp.where(inside[h], nt(keys, stacked), NEG)
            for h, keys in enumerate((k_lo[low_at, lanes], k[:, lanes]))
        ]
        w = softmax_columns(scores)
        weights[g * 2] = w[0]
        weights[g * 2 + 1] = w[1]
        mixed = tn(w[0], v_lo[low_at, lanes]) + tn(w[1], v[:, lanes])
        o1[:, lanes] = unstack_heads(mixed).astype(BF)
    hb[...] = (patch[rows, :].astype(F32) + nn(o1[...], w_out[...])).astype(BF)


def latent_layer(
    ids, hb_a, hb_b, cot, allowed, w_qkv, w_out, gains, w_ff, d_hidden,
    latents, dhb, gain_grad, norms, grads, packed,
    qkv, weights, o2, ff_buf, acc_out, acc_norm, dqkv, sems,
):
    core = ids[0]
    units = w_ff.shape[1]
    step = 256
    parts = 4
    part = units // parts

    fetches = []
    for i in range(parts):
        at = slice(i * part, (i + 1) * part)
        fetches.append(pltpu.make_async_copy(w_ff.at[:, at, :], ff_buf.at[:, at, :], sems.at[i]))
        fetches[-1].start()
    x = jnp.concatenate([hb_a[...], hb_b[...]], 0).astype(F32)
    normed = (x * inverse_rms(x) * gains[0:1]).astype(BF)
    packed[PACK_LEFT : PACK_LEFT + D, :] = normed.T
    for j in range(3):
        qkv[:, j * D : (j + 1) * D] = nn(normed, w_qkv.block(j)[...]).astype(BF)
    for m in range(2):
        rows = slice(m * HD, (m + 1) * HD)
        for g in range(4):
            lanes = slice(g * GROUP, (g + 1) * GROUP)
            k_lanes = slice(D + g * GROUP, D + (g + 1) * GROUP)
            v_lanes = slice(2 * D + g * GROUP, 2 * D + (g + 1) * GROUP)
            stacked = stack_heads(qkv[rows, lanes] * BF(SCALE))
            scores = jnp.where(allowed[m] > 0.5, nt(qkv[rows, k_lanes], stacked), NEG)
            (w,) = softmax_columns([scores])
            weights[m * 4 + g] = w
            o2[rows, lanes] = unstack_heads(tn(w, qkv[rows, v_lanes])).astype(BF)
    packed[PACK_LEFT + D : PACK_LEFT + 2 * D, :] = o2[...].T
    after = x + nn(o2[...], w_out[...])
    yn = (after * inverse_rms(after) * gains[1:2]).astype(BF)
    c = cot[...]
    for h in range(2):

        @pl.when(core == h)
        def _(h=h):
            norms[0:128, :] = yn[:, h * HALF : (h + 1) * HALF]
            norms[128:256, :] = c[:, h * HALF : (h + 1) * HALF]

        @pl.when(core != h)
        def _(h=h):
            for b in range(4):
                lanes = slice(h * HALF + b * 128, h * HALF + (b + 1) * 128)
                packed[PACK_NORMS + b * 256 : PACK_NORMS + b * 256 + 128, :] = yn[:, lanes]
                packed[PACK_NORMS + b * 256 + 128 : PACK_NORMS + (b + 1) * 256, :] = c[:, lanes]

    for copy in fetches:
        copy.wait()
    acc_out[...] = after
    for i in range(units // step):
        at = slice(i * step, (i + 1) * step)
        gate = nt(yn, ff_buf[0, at, :])
        upward = nt(yn, ff_buf[1, at, :])
        du = d_hidden[:, at]
        sig = 1.0 / (1.0 + jnp.exp(-gate))
        active = gate * sig
        hidden = (active * upward).astype(BF)
        d_gate = (du * upward * (sig * (1.0 + gate * (1.0 - sig)))).astype(BF)
        d_up = (du * active).astype(BF)
        for j, value in enumerate((d_gate, d_up, hidden)):
            packed[i * step + j * units : (i + 1) * step + j * units, :] = value.T
        acc_out[...] += nn(hidden, ff_buf[2, at, :])
        back = nn(d_gate, ff_buf[0, at, :]) + nn(d_up, ff_buf[1, at, :])
        if i == 0:
            acc_norm[...] = back
        else:
            acc_norm[...] += back
    latents[...] = acc_out[...]
    back, gain_rows = norm_back(after, gains[1:2], acc_norm[...])
    gain_grad[1:2, :] = jnp.sum(gain_rows, axis=0, keepdims=True)
    d_after = c.astype(F32) + back
    da = d_after.astype(BF)
    d_mixed = nt(da, w_out[...]).astype(BF)
    for m in range(2):
        rows = slice(m * HD, (m + 1) * HD)
        for g in range(4):
            lanes = slice(g * GROUP, (g + 1) * GROUP)
            k_lanes = slice(D + g * GROUP, D + (g + 1) * GROUP)
            v_lanes = slice(2 * D + g * GROUP, 2 * D + (g + 1) * GROUP)
            q_stacked = stack_heads(qkv[rows, lanes] * BF(SCALE))
            o_stacked = stack_heads(d_mixed[rows, lanes])
            w_low = weights[m * 4 + g]
            w = w_low.astype(F32)
            dw = nt(qkv[rows, v_lanes], o_stacked)
            inner = jnp.sum(dw * w, axis=0, keepdims=True)
            ds = (w * (dw - inner)).astype(BF)
            dqkv[rows, lanes] = (unstack_heads(tn(ds, qkv[rows, k_lanes])) * SCALE).astype(BF)
            dqkv[rows, k_lanes] = nn(ds, q_stacked).astype(BF)
            dqkv[rows, v_lanes] = nn(w_low, o_stacked).astype(BF)
    d_normed = sum(nt(dqkv[:, j * D : (j + 1) * D], w_qkv.block(j)[...]) for j in range(3))
    back, gain_rows = norm_back(x, gains[0:1], d_normed)
    gain_grad[0:1, :] = jnp.sum(gain_rows, axis=0, keepdims=True)
    dhb[...] = (d_after + back).astype(BF)
    for h in range(2):
        pieces = (
            dqkv[:, h * HALF : (h + 1) * HALF],
            da[:, h * HALF : (h + 1) * HALF],
            dqkv[:, D + h * HALF : D + (h + 1) * HALF],
            dqkv[:, 2 * D + h * HALF : 2 * D + (h + 1) * HALF],
        )

        @pl.when(core == h)
        def _(pieces=pieces):
            for i, value in enumerate(pieces):
                grads[i * 128 : (i + 1) * 128, :] = value

        @pl.when(core != h)
        def _(pieces=pieces):
            for i, value in enumerate(pieces):
                for b in range(4):
                    first = PACK_GRADS + b * 512 + i * 128
                    packed[first : first + 128, :] = value[:, b * 128 : (b + 1) * 128]


def hidden_back(cot, w_ff, d_hidden, buffer, sems):
    parts = 4
    part = w_ff.shape[1] // parts
    copies = []
    for i in range(parts):
        at = slice(i * part, (i + 1) * part)
        copies.append(pltpu.make_async_copy(w_ff.at[2, at, :], buffer.at[at, :], sems.at[i]))
        copies[-1].start()
    for copy in copies:
        copy.wait()
    for i in range(w_ff.shape[1] // 256):
        at = slice(i * 256, (i + 1) * 256)
        d_hidden[:, at] = nt(cot[...], buffer[at, :])


def half_of(core, g, mine, other):
    lanes = slice((g % 2) * GROUP, (g % 2 + 1) * GROUP)

    def put(at, value):
        @pl.when(core == g // 2)
        def _():
            mine[at, lanes] = value

        @pl.when(core != g // 2)
        def _():
            other[at, lanes] = value

    return put


def encoder_attention_back(
    ids, dhb, w_out, q, k_lo, v_lo, k_a, k_b, v_a, v_b, w_a, w_b, mine, other
):
    d_mixed = nt(dhb[...], w_out[...]).astype(BF)
    for g in range(4):
        lanes = slice(g * GROUP, (g + 1) * GROUP)
        put = half_of(ids[0], g, mine, other)
        put(slice(128, 256), dhb[:, lanes])
        for m, (k_up, v_up, weights) in enumerate(((k_a, v_a, w_a), (k_b, v_b, w_b))):
            rows = slice(m * HD, (m + 1) * HD)
            low_at = slice(m * 256, (m + 1) * 256)
            q_stacked = stack_heads(q[rows, lanes] * BF(SCALE))
            o_stacked = stack_heads(d_mixed[rows, lanes])
            low = [weights[g * 2 + h] for h in range(2)]
            w = [piece.astype(F32) for piece in low]
            dw = [nt(values, o_stacked) for values in (v_lo[low_at, lanes], v_up[:, lanes])]
            inner = sum(jnp.sum(a * b, axis=0, keepdims=True) for a, b in zip(dw, w))
            ds = [(b * (a - inner)).astype(BF) for a, b in zip(dw, w)]
            dq = tn(ds[0], k_lo[low_at, lanes]) + tn(ds[1], k_up[:, lanes])
            put(rows, (unstack_heads(dq) * SCALE).astype(BF))
            for h in range(2):
                base = h * HALF + m * 256
                put(slice(256 + base, 512 + base), nn(ds[h], q_stacked).astype(BF))
                put(slice(1280 + base, 1536 + base), nn(low[h], o_stacked).astype(BF))


def both_columns(core, block, w_qkv):
    return [
        w_qkv.block(block)[:, pl.ds(pl.multiple_of(which * HALF, HALF), HALF)] for which in (core, 1 - core)
    ]


def bytes_back(core, h, m, source, w_qkv, gains, grads):
    d_norm = sum(
        nt(ref[1024 * block - 768 + h * HALF + m * 256 : 1024 * block - 512 + h * HALF + m * 256, :], columns)
        for block in (1, 2)
        for ref, columns in zip(grads, both_columns(core, block, w_qkv))
    )
    back, gain_rows = norm_back(source.astype(F32), gains[1:2], d_norm)
    return back.astype(BF), jnp.sum(gain_rows, axis=0, keepdims=True)


def encoder_upper_back(ids, up_a, up_b, w_qkv, gains, mine, other, up_grad, gain_grad):
    total = jnp.zeros((1, D), F32)
    for m, source in enumerate((up_a, up_b)):
        back, rows = bytes_back(ids[0], 1, m, source[...], w_qkv, gains, (mine, other))
        up_grad[m * 256 : (m + 1) * 256, :] = back
        total = total + rows
    gain_grad[...] = total


def encoder_lower_back(
    ids, dhb, patch, low, w_qkv, gains, mine, other, after, patch_grad, low_grad, gain_grad
):
    core = ids[0]
    up_norm = sum(nt(ref[0:128, :], columns) for ref, columns in zip((mine, other), both_columns(core, 0, w_qkv)))
    back, gain_rows = norm_back(patch[...].astype(F32), gains[0:1], up_norm)
    gain_grad[0:1, :] = jnp.sum(gain_rows, axis=0, keepdims=True)
    patch_grad[...] = dhb[...].astype(F32) + back
    total = jnp.zeros((1, D), F32)
    for m in range(2):
        at = slice(m * 256, (m + 1) * 256)
        back, rows = bytes_back(core, 0, m, low[at, :], w_qkv, gains, (mine, other))
        low_grad[at, :] = back
        total = total + rows
    gain_grad[1:2, :] = total


def turn_encoder(pn, o_a, o_b, bn_lo, bn_a, bn_b, packed):
    for b, rows in enumerate([bn_lo[i * 128 : (i + 1) * 128, :] for i in range(4)]
                             + [ref[i * 128 : (i + 1) * 128, :] for ref in (bn_a, bn_b) for i in range(2)]):
        packed[b * D : (b + 1) * D, :] = rows.T
    packed[PACK_LEFT : PACK_LEFT + D, :] = pn[...].T
    packed[PACK_LEFT + D : PACK_LEFT + 2 * D, :] = jnp.concatenate([o_a[...], o_b[...]], 0).T


def rows_of_both(left, left_far, at):
    return jnp.concatenate([left[at, :], left_far[at, :]], 1)


def below(near, far, rows):
    return jnp.concatenate([near[rows, :], far[rows, :]], 0)


def deliver(blocks, k, block, value):
    own, right, left, far_a, far_b = blocks
    value = value.astype(BF)
    if k == 2:
        far_a[block] = value[:, :GROUP]
        far_b[block] = value[:, GROUP:]
    else:
        (own, right, None, left)[k][block] = value


def encoder_weights(ids, packed, packed_far, near, far, after, *blocks):
    u = ids[1]
    queries = below(near, far, slice(0, 128))
    outputs = below(near, far, slice(128, 256))
    for k in range(4):
        first = lax.rem(u + k, 4) * 256

        def at(base, first=first):
            return pl.ds(pl.multiple_of(first + base, 256), 256)

        deliver(blocks, k, 0, nn(rows_of_both(packed, packed_far, at(PACK_LEFT)), queries))
        deliver(blocks, k, 3, nn(rows_of_both(packed, packed_far, at(PACK_LEFT + D)), outputs))
        lefts = [jnp.concatenate([ref[at(b * D), :] for b in range(8)], 1) for ref in (packed, packed_far)]
        for block in (1, 2):
            rows = slice(1024 * block - 768, 1024 * block + 256)
            deliver(blocks, k, block, nn(lefts[0], near[rows, :]) + nn(lefts[1], far[rows, :]))


def unpack(packed, first, rows):
    return jnp.concatenate([packed[first + b * rows : first + (b + 1) * rows, :] for b in range(4)], 1)


def latent_weights(ids, packed, packed_far, near, *blocks):
    u = ids[1]
    far = unpack(packed_far, PACK_GRADS, 512)
    rights = [jnp.concatenate([near[i * 128 : (i + 1) * 128, :], far[i * 128 : (i + 1) * 128, :]], 0) for i in range(4)]
    for k in range(4):
        first = PACK_LEFT + lax.rem(u + k, 4) * 256
        at = pl.ds(pl.multiple_of(first, 256), 256)
        low_at = pl.ds(pl.multiple_of(first + D, 256), 256)
        for block, (source, i) in enumerate(((at, 0), (at, 2), (at, 3), (low_at, 1))):
            deliver(blocks, k, block, nn(rows_of_both(packed, packed_far, source), rights[i]))


def ff_weights_grad(ids, packed, packed_far, norms, own, right, left, far_a, far_b):
    core, u = ids[0], ids[1]
    share = UNITS // 16
    far = unpack(packed_far, PACK_NORMS, 256)
    normed = jnp.concatenate([norms[0:128, :], far[0:128, :]], 0)
    cot = jnp.concatenate([norms[128:256, :], far[128:256, :]], 0)
    for k in range(4):
        there = lax.rem(u + k, 4)
        for v in range(4):
            chunk = jnp.where(core == 0, there * 4 + v, v * 4 + there)
            for j in range(3):
                at = pl.ds(pl.multiple_of(j * UNITS + chunk * share, 16), share)
                value = nn(rows_of_both(packed, packed_far, at), normed if j < 2 else cot).astype(BF)
                rows = slice(j * share, (j + 1) * share)
                if k == 2:
                    far_a[v, rows, :] = value[:, :GROUP]
                    far_b[v, rows, :] = value[:, GROUP:]
                else:
                    (own, right, None, left)[k][v, rows, :] = value


def ring_add(right, left, from_left, from_right, after, new_right, new_left):
    new_right[:, :, 0:GROUP] = (right[:, :, 0:GROUP].astype(F32) + from_left[...].astype(F32)).astype(BF)
    new_right[:, :, GROUP:] = right[:, :, GROUP:]
    new_left[:, :, 0:GROUP] = left[:, :, 0:GROUP]
    new_left[:, :, GROUP:] = (left[:, :, GROUP:].astype(F32) + from_right[...].astype(F32)).astype(BF)


def sum_four(own, a, b, c):
    return own.astype(F32) + a.astype(F32) + b.astype(F32) + c.astype(F32)


def pack_gain(value):
    high = value.astype(BF)
    low = (value - high.astype(F32)).astype(BF)
    return jnp.concatenate(
        [high.astype(F32), low.astype(F32), jnp.zeros((8, HALF), F32)], 0
    ).astype(BF)


def unpack_gain(rows):
    rows = rows.astype(F32)
    return rows[0:4] + rows[4:8]


GAIN_AT = slice(256, 272)


def attn_sum_first(ids, own, a, b, enc_gain, up_gain, lat_gain, *outs):
    v = ids[2]
    first = ids[4] == 0
    gain = jnp.where(
        first, jnp.concatenate([enc_gain[0:1, :], enc_gain[1:2, :] + up_gain[...]], 0), lat_gain[...]
    )
    halves = [gain[i : i + 1, h * HALF : (h + 1) * HALF] for i in range(2) for h in range(2)]
    packed = pack_gain(jnp.concatenate(halves, 0))
    for k in range(4):
        at = pl.ds(pl.multiple_of(lax.rem(v + k, 4) * HD, HD), HD)
        for block in range(4):
            total = sum(ref[block, at, :].astype(F32) for ref in (own, a, b))
            outs[k][block * HD : (block + 1) * HD, :] = total.astype(BF)
        outs[k][GAIN_AT, :] = packed


def sum_all(*refs):
    refs, out = refs[:-1], refs[-1]
    out[0:256, :] = sum(ref[0:256, :].astype(F32) for ref in refs).astype(BF)
    out[GAIN_AT, :] = pack_gain(sum(unpack_gain(ref[GAIN_AT, :]) for ref in refs))


def stack_rows(*refs):
    refs, out = refs[:-1], refs[-1]
    for j, ref in enumerate(refs):
        out[j * 256 : (j + 1) * 256, :] = ref[0:256, :]
    out[1024:1040, :] = refs[0][GAIN_AT, :]


def ff_sum_first(ids, own, a, b, *outs):
    v = ids[2]
    for k in range(4):
        at = lax.rem(v + k, 4)
        outs[k][...] = (own[at].astype(F32) + a[at].astype(F32) + b[at].astype(F32)).astype(BF)


def ff_sum_second(own, a, b, c, out):
    out[...] = sum_four(own[...], a[...], b[...], c[...]).astype(BF)


def final_attn(ids, *refs):
    pieces, (qkv, out, gain) = refs[:8], refs[8:]
    step = pl.program_id(0)
    for side in range(2):
        core = ids[0] if side == 0 else 1 - ids[0]
        u = ids[1] if side == 0 else ids[2]
        v = ids[2] if side == 0 else ids[1]
        for k in range(4):
            piece = pieces[side * 4 + k]

            @pl.when(lax.rem(u + k, 4) == step)
            def _(piece=piece, v=v, core=core):
                for j in range(4):
                    at = pl.ds(pl.multiple_of(lax.rem(v + j, 4) * HD, HD), HD)
                    for block in range(4):
                        target, column = (qkv, block * D) if block < 3 else (out, 0)
                        lanes = pl.ds(pl.multiple_of(core * HALF + column, HALF), HALF)
                        first = j * 256 + block * HD
                        target[at, lanes] = piece[first : first + HD, :].astype(F32)

    mine = sum(unpack_gain(piece[1024:1040, :]) for piece in pieces[:4])
    other = sum(unpack_gain(piece[1024:1040, :]) for piece in pieces[4:])
    total = mine + other
    for i in range(2):
        for h in range(2):
            gain[i : i + 1, h * HALF : (h + 1) * HALF] = total[2 * i + h : 2 * i + h + 1, :]


SMEM = pltpu.MemorySpace.SMEM
VMEM = pltpu.MemorySpace.VMEM


def size(shape, dtype):
    return math.prod(shape) * jnp.dtype(dtype).itemsize


class Arriving:
    def __init__(self, copy, buffer):
        self.copy, self.buffer, self.here = copy, buffer, False

    def ready(self):
        if not self.here:
            self.copy.wait()
            self.here = True
        return self.buffer

    def __getitem__(self, index):
        return self.ready()[index]


class ArrivingBlocks:
    def __init__(self, blocks):
        self.blocks = blocks

    def block(self, j):
        return self.blocks[j]


def fetching(kernel, n_args, n_outs, plan):
    def wrapped(*refs):
        args, outs, rest = list(refs[:n_args]), refs[n_args : n_args + n_outs], refs[n_args + n_outs :]
        scratch, buffers, sems = rest[: len(rest) - len(plan) - 1], rest[len(rest) - len(plan) - 1 : -1], rest[-1]
        arriving = []
        blocks = {}
        for i, (a, j) in enumerate(plan):
            source = refs[a] if j is None else refs[a].at[:, j * D : (j + 1) * D]
            copy = pltpu.make_async_copy(source, buffers[i], sems.at[i])
            copy.start()
            arriving.append(Arriving(copy, buffers[i]))
            if j is None:
                args[a] = arriving[-1]
            else:
                blocks.setdefault(a, {})[j] = arriving[-1]
        for a, found in blocks.items():
            args[a] = ArrivingBlocks(found)
        kernel(*args, *outs, *scratch)
        for value in arriving:
            value.ready()

    return wrapped


def call(kernel, args, outs, scratch=(), spaces=None, spare=6, fetch=()):
    spaces = dict(spaces or {})
    scratch = list(scratch)
    plan = [f if isinstance(f, tuple) else (f, None) for f in fetch]
    if plan:
        for a, j in plan:
            spaces[a] = pl.ANY
            shape = args[a].shape if j is None else (args[a].shape[0], D)
            scratch.append(pltpu.VMEM(shape, args[a].dtype))
        scratch.append(pltpu.SemaphoreType.DMA((len(plan),)))
        kernel = fetching(kernel, len(args), len(outs), plan)
    vmem = sum(size(a.shape, a.dtype) for i, a in enumerate(args) if i not in spaces)
    vmem += sum(size(*o) for o in outs)
    vmem += sum(size(s.shape, s.dtype) for s in scratch if hasattr(s, "shape") and s.memory_space == VMEM)
    specs = [pl.BlockSpec(memory_space=spaces.get(i, VMEM)) for i in range(len(args))]
    return pl.pallas_call(
        kernel,
        out_shape=[jax.ShapeDtypeStruct(s, t) for s, t in outs],
        in_specs=specs,
        out_specs=[pl.BlockSpec(memory_space=VMEM) for _ in outs],
        scratch_shapes=scratch,
        compiler_params=pltpu.CompilerParams(vmem_limit_bytes=vmem + spare * 1024 * 1024),
    )(*args)


def nothing(outs):
    def kernel(*refs):
        pass

    return pl.pallas_call(
        kernel,
        out_shape=[jax.ShapeDtypeStruct(s, t) for s, t in outs],
        out_specs=[pl.BlockSpec(memory_space=pl.ANY) for _ in outs],
    )()


def on_section(flag, kernel, args, outs, **rest):
    return lax.cond(
        flag, lambda: call(kernel, args, outs, **rest), lambda: nothing(outs)
    )


def along(value, by):
    return lax.ppermute(value, "s", [(0, 1)] if by > 0 else [(1, 0)])


def swap(value, axis, sections=(0, 1)):
    pairs = [(s * 2 + i, s * 2 + 1 - i) for s in sections for i in range(2)]
    return lax.ppermute(value, ("s", axis), pairs)


def plane_shift(value, which, by, sections=(0, 1)):
    pairs = []
    for s in sections:
        for y in range(4):
            for x in range(4):
                for core in range(2):
                    ty, tx = ((y + by) % 4, x) if core == which else (y, (x + by) % 4)
                    pairs.append((((s * 4 + y) * 4 + x) * 2 + core, ((s * 4 + ty) * 4 + tx) * 2 + core))
    return lax.ppermute(value, ("s", "y", "x", "core"), pairs)


def exchange(blocks, which, sections=(0, 1)):
    return [plane_shift(blocks[k], which, k, sections) for k in (1, 2, 3)]


def collect(block, which):
    return [block] + [plane_shift(block, which, -k) for k in (1, 2, 3)]


def pick(stack, index, dim):
    return lax.dynamic_index_in_dim(stack, index, dim, keepdims=False)


def shards(patch_io, byte_states, patch_lengths, patch_live, attn_qkv, attn_out, gains, ff_weights):
    section = lax.axis_index("s")
    core = lax.axis_index("core")
    zh = lax.axis_index("zh")
    y, x = lax.axis_index("y"), lax.axis_index("x")
    first = section == 0
    second = section == 1
    ids = jnp.stack([core, jnp.where(core == 0, y, x), jnp.where(core == 0, x, y), zh, section])
    ids = ids.astype(jnp.int32)
    w_qkv = attn_qkv[0]
    w_out = attn_out[0]
    gain_pair = gains[0]
    micro, seq = patch_io.shape[1], patch_io.shape[3]
    half_bytes = byte_states.shape[2]
    units = ff_weights.shape[0]
    rows = micro * seq
    own_rows = patch_io.reshape(rows, D)
    up_a = along(byte_states[0, 0], -1)
    up_b = along(byte_states[1, 0], -1)
    lower = byte_states.reshape(micro * half_bytes, D)
    w_ff = jnp.swapaxes(ff_weights, 0, 1)
    lengths = patch_lengths[:, 0]
    live = patch_live[:, 0]
    ends = jnp.cumsum(lengths, axis=1)
    bounds = jnp.tile(jnp.stack([ends - lengths, ends], 1), (1, 1, 4))
    places = lax.iota(jnp.int32, seq)
    causal = places[:, None] <= places[None, :]
    diagonal = places[:, None] == places[None, :]
    allowed = causal[None] & ((live[:, :, None] == 1) | diagonal[None])
    allowed = lax.optimization_barrier(jnp.tile(allowed.astype(F32), (1, 1, 4)))

    wide = ((rows, D), BF)
    short = ((seq, D), BF)
    tall = ((micro * half_bytes, D), BF)
    piece = ((half_bytes, D), BF)
    (d_hidden,) = on_section(
        second,
        hidden_back,
        (own_rows, w_ff),
        [((rows, units), F32)],
        spaces={1: pl.ANY},
        scratch=[pltpu.VMEM((units, D), BF), pltpu.SemaphoreType.DMA((4,))],
    )
    pn, q, bn_lo, k_lo, v_lo = on_section(
        first,
        encode_lower,
        (own_rows, lower, w_qkv, gain_pair),
        [wide, wide, tall, tall, tall],
        fetch=((2, 0), 1, (2, 1), (2, 2)),
    )
    rest = []
    for m, up in enumerate((up_a, up_b)):
        rest.append(
            on_section(
                first,
                functools.partial(encode_rest, m),
                (own_rows, up, w_qkv, w_out, gain_pair, bounds, q, k_lo, v_lo),
                [short, short, ((8, 256, GROUP), BF), piece, piece, piece],
                fetch=((2, 1), (2, 2), 7, 8, 3),
            )
        )
    (hb_a, o_a, w_a, bn_a, k_a, v_a), (hb_b, o_b, w_b, bn_b, k_b, v_b) = rest
    arrived = [along(hb_a, 1), along(hb_b, 1)]

    latent_outs = [
        ((rows, D), F32), wide, ((2, D), F32), ((256, HALF), BF), ((512, HALF), BF), ((PACK_ROWS, rows), BF),
    ]

    def latent():
        return call(
            latent_layer,
            (ids, *arrived, own_rows, allowed, w_qkv, w_out, gain_pair, w_ff, d_hidden),
            latent_outs,
            spaces={0: SMEM, 8: pl.ANY},
            fetch=((5, 0), (5, 1), (5, 2), 6),
            scratch=[
                pltpu.VMEM((rows, 3 * D), BF),
                pltpu.VMEM((8, HD, GROUP), BF),
                pltpu.VMEM((rows, D), BF),
                pltpu.VMEM((3, units, D), BF),
                pltpu.VMEM((rows, D), F32),
                pltpu.VMEM((rows, D), F32),
                pltpu.VMEM((rows, 3 * D), BF),
                pltpu.SemaphoreType.DMA((4,)),
            ],
        )

    def turn():
        return nothing(latent_outs[:5]) + call(
            turn_encoder, (pn, o_a, o_b, bn_lo, bn_a, bn_b), latent_outs[5:]
        )

    latents, dhb, latent_gain, norms, lat_grads, packed = lax.cond(second, latent, turn)
    returned = along(dhb, -1)

    packed_far = swap(packed, "core")

    share = units // 16
    ff_block = ((4, 3 * share, HALF), BF)
    ff_half = ((4, 3 * share, GROUP), BF)
    ff_own, ff_right, ff_left, ff_far_a, ff_far_b = on_section(
        second,
        ff_weights_grad,
        (ids, packed, packed_far, norms),
        [ff_block, ff_block, ff_block, ff_half, ff_half],
        spaces={0: SMEM},
    )

    grads_long = ((2304, HALF), BF)
    enc_grads, enc_other = on_section(
        first,
        encoder_attention_back,
        (ids, returned, w_out, q, k_lo, v_lo, k_a, k_b, v_a, v_b, w_a, w_b),
        [grads_long, grads_long],
        spaces={0: SMEM},
        fetch=(2, 5, 8, 10, 4, 6, 9, 11, 7),
    )
    enc_far = swap(enc_other, "core", (0,))
    up_grad, up_gain = on_section(
        first,
        encoder_upper_back,
        (ids, up_a, up_b, w_qkv, gain_pair, enc_grads, enc_other),
        [tall, ((1, D), F32)],
        spaces={0: SMEM},
        fetch=(5, (3, 1), 6, (3, 2), 1, 2),
    )
    up_arrived = along(up_grad, 1)
    ff_far_a, ff_far_b, up_gain = lax.optimization_barrier((ff_far_a, ff_far_b, up_gain))
    from_left = plane_shift(ff_far_a, 0, 1, (1,))
    from_right = plane_shift(ff_far_b, 0, -1, (1,))
    attn_block = ((4, 256, HALF), BF)
    outs = [attn_block] * 3 + [((4, 256, GROUP), BF)] * 2
    blocks = lax.cond(
        first,
        lambda: call(
            encoder_weights,
            (ids, packed, packed_far, enc_grads, enc_far, up_gain),
            outs,
            spaces={0: SMEM, 5: pl.ANY},
            fetch=(3, 4, 1, 2),
        ),
        lambda: call(latent_weights, (ids, packed, packed_far, lat_grads), outs, spaces={0: SMEM}),
    )
    attn_own, attn_right, attn_left, attn_far_a, attn_far_b = blocks
    by_left = plane_shift(attn_far_a, 0, 1)
    by_right = plane_shift(attn_far_b, 0, -1)
    ff_right, ff_left = on_section(
        second,
        ring_add,
        (ff_right, ff_left, from_left, from_right, attn_own),
        [ff_block, ff_block],
        spaces={4: pl.ANY},
    )
    from_left = plane_shift(ff_right, 0, 1, (1,))
    from_right = plane_shift(ff_left, 0, -1, (1,))
    attn_right, attn_left = call(
        ring_add,
        (attn_right, attn_left, by_left, by_right, attn_own),
        [attn_block] * 2,
        spaces={4: pl.ANY},
    )
    by_left = plane_shift(attn_right, 0, 1)
    by_right = plane_shift(attn_left, 0, -1)
    patch_grad, low_grad, encoder_gain = on_section(
        first,
        encoder_lower_back,
        (ids, returned, own_rows, lower, w_qkv, gain_pair, enc_grads, enc_other, attn_right),
        [((rows, D), F32), tall, ((2, D), F32)],
        spaces={0: SMEM, 8: pl.ANY},
        fetch=(6, 7, (4, 0), (4, 1), (4, 2), 3),
    )
    by_left, by_right, up_arrived = lax.optimization_barrier((by_left, by_right, up_arrived))
    line = [((272, HALF), BF)]
    blocks = call(
        attn_sum_first,
        (ids, attn_own, by_left, by_right, encoder_gain, up_gain, latent_gain),
        line * 4,
        spaces={0: SMEM},
    )
    (block,) = call(sum_all, (blocks[0], *exchange(blocks, 1)), line)
    byte_grad = jnp.where(first, low_grad, up_arrived)
    patch_out = jnp.where(first, patch_grad, latents)
    from_left, from_right, block, byte_grad, patch_out = lax.optimization_barrier(
        (from_left, from_right, block, byte_grad, patch_out)
    )
    ff_line = ((3 * share, HALF), BF)
    ff_blocks = on_section(
        second, ff_sum_first, (ids, ff_own, from_left, from_right), [ff_line] * 4, spaces={0: SMEM}
    )
    ff_got = exchange(ff_blocks, 1, (1,))
    across, ff_got = lax.optimization_barrier((swap(block, "zh"), ff_got))
    (block,) = call(sum_all, (block, across), line)
    (block,) = call(stack_rows, collect(block, 1), [((1040, HALF), BF)])
    pieces = collect(block, 0)
    own_far = swap(block, "core")
    (ff_sum,) = on_section(second, ff_sum_second, (ff_blocks[0], *ff_got), [ff_line])
    ff_sum = ff_sum.reshape(3, 2, share // 2, HALF)
    ff_far = swap(pick(ff_sum, 1 - zh, 1), "zh", (1,))
    ff_sum = (pick(ff_sum, zh, 1).astype(F32) + ff_far.astype(F32)).astype(BF).reshape(3, 2, share // 4, HALF)
    ff_mine = pick(ff_sum, core, 1)
    ff_far = swap(pick(ff_sum, 1 - core, 1), "core", (1,))

    def ff_result():
        low, high = jnp.where(core == 0, ff_mine, ff_far), jnp.where(core == 0, ff_far, ff_mine)
        return jnp.swapaxes(jnp.concatenate([low, high], 2), 0, 1).astype(F32)

    ff_grad = lax.cond(second, ff_result, lambda: jnp.zeros((share // 4, 3, D), F32))
    ff_grad, *pieces = lax.optimization_barrier((ff_grad, *pieces))
    pieces = pieces + [own_far] + [swap(p, "core") for p in pieces[1:]]
    whole = lambda p: pl.BlockSpec(p.shape, lambda i, n=p.ndim: (0,) * n)
    total_qkv, total_out, total_gain = pl.pallas_call(
        final_attn,
        grid=(4,),
        out_shape=[
            jax.ShapeDtypeStruct((D, 3 * D), F32),
            jax.ShapeDtypeStruct((D, D), F32),
            jax.ShapeDtypeStruct((2, D), F32),
        ],
        in_specs=[pl.BlockSpec(memory_space=SMEM)] + [whole(p) for p in pieces],
        out_specs=[
            pl.BlockSpec((256, 3 * D), lambda i: (i, 0)),
            pl.BlockSpec((256, D), lambda i: (i, 0)),
            pl.BlockSpec((2, D), lambda i: (0, 0)),
        ],
        compiler_params=pltpu.CompilerParams(vmem_limit_bytes=FINAL_VMEM),
    )(ids, *pieces)
    return (
        patch_out.reshape(1, micro, 1, seq, D),
        byte_grad.reshape(micro, 1, half_bytes, D),
        total_qkv[None],
        total_out[None],
        total_gain[None],
        ff_grad[None],
    )


def solution(mesh):
    fine = Mesh(mesh.devices.reshape(2, 4, 4, 2, 2), ("s",) + BATCH)
    in_specs = (
        P("s", None, BATCH, None, None),
        P(None, BATCH, "s", None),
        P(None, BATCH, None),
        P(None, BATCH, None),
        P("s", None, None),
        P("s", None, None),
        P("s", None, None),
        P(),
    )
    out_specs = (
        P("s", None, BATCH, None, None),
        P(None, BATCH, "s", None),
        P("s", None, None),
        P("s", None, None),
        P("s", None, None),
        P("s", BATCH, None, None),
    )
    return jax.shard_map(shards, mesh=fine, in_specs=in_specs, out_specs=out_specs, check_vma=False)
```

```python
import functools
import math

import jax
import jax.numpy as jnp
from jax import lax
from jax.experimental import pallas as pl
from jax.experimental.pallas import tpu as pltpu
from jax.sharding import Mesh
from jax.sharding import PartitionSpec as P

HD = 64
SCALE = HD**-0.5
EPS = 1e-05
NEG = -1e30
BATCH = ("y", "x", "zh", "core")
BF = jnp.bfloat16
F32 = jnp.float32
D = 1024
HALF = 512
GROUP = 256
FINAL_VMEM = 32 * 1024 * 1024


UNITS = 2816
PACK_NORMS = 3 * UNITS
PACK_LEFT = PACK_NORMS + 4 * 256
PACK_GRADS = PACK_LEFT + 2 * D
PACK_ROWS = PACK_GRADS + 4 * 512


def nn(a, b):
    return lax.dot_general(a, b, (((1,), (0,)), ((), ())), preferred_element_type=F32)


def nt(a, b):
    return lax.dot_general(a, b, (((1,), (1,)), ((), ())), preferred_element_type=F32)


def tn(a, b):
    return lax.dot_general(a, b, (((0,), (0,)), ((), ())), preferred_element_type=F32)


def inverse_rms(x):
    return lax.rsqrt(jnp.mean(x * x, axis=-1, keepdims=True) + EPS)


def norm_back(x, gain, up):
    r = inverse_rms(x)
    scaled = up * gain
    inner = jnp.mean(scaled * x, axis=-1, keepdims=True)
    return r * (scaled - x * (r * r * inner)), up * (x * r)


def stack_heads(rows):
    head = lax.broadcasted_iota(jnp.int32, rows.shape, 1) // HD
    return jnp.concatenate([jnp.where(head == h, rows, jnp.zeros_like(rows)) for h in range(4)], 0)


def unstack_heads(stacked):
    head = lax.broadcasted_iota(jnp.int32, (HD, GROUP), 1) // HD
    out = stacked[0:HD]
    for h in range(1, 4):
        out = jnp.where(head == h, stacked[h * HD : (h + 1) * HD], out)
    return out


def softmax_columns(scores):
    top = functools.reduce(jnp.maximum, [jnp.max(s, axis=0, keepdims=True) for s in scores])
    parts = [jnp.exp(s - top) for s in scores]
    inverse = 1.0 / sum(jnp.sum(p, axis=0, keepdims=True) for p in parts)
    return [(p * inverse).astype(BF) for p in parts]


def encode_lower(patch, low, w_qkv, gains, pn, q, bn, k, v):
    x = patch[...].astype(F32)
    normed = (x * inverse_rms(x) * gains[0:1]).astype(BF)
    pn[...] = normed
    q[...] = nn(normed, w_qkv.block(0)[...]).astype(BF)
    for i in range(2):
        at = pl.ds(i * 256, 256)
        b = low[at, :].astype(F32)
        normed = (b * inverse_rms(b) * gains[1:2]).astype(BF)
        bn[at, :] = normed
        k[at, :] = nn(normed, w_qkv.block(1)[...]).astype(BF)
        v[at, :] = nn(normed, w_qkv.block(2)[...]).astype(BF)


def encode_rest(m, patch, up, w_qkv, w_out, gains, bounds, q, k_lo, v_lo, hb, o1, weights, bn, k, v):
    b = up[...].astype(F32)
    normed = (b * inverse_rms(b) * gains[1:2]).astype(BF)
    bn[...] = normed
    k[...] = nn(normed, w_qkv.block(1)[...]).astype(BF)
    v[...] = nn(normed, w_qkv.block(2)[...]).astype(BF)
    spot = lax.broadcasted_iota(jnp.int32, (256, GROUP), 0)
    start = bounds[m, 0:1, :]
    end = bounds[m, 1:2, :]
    inside = [(spot + h * 256 >= start) & (spot + h * 256 < end) for h in range(2)]
    low_at = slice(m * 256, (m + 1) * 256)
    rows = slice(m * HD, (m + 1) * HD)
    for g in range(4):
        lanes = slice(g * GROUP, (g + 1) * GROUP)
        stacked = stack_heads(q[rows, lanes] * BF(SCALE))
        scores = [
            jnp.where(inside[h], nt(keys, stacked), NEG)
            for h, keys in enumerate((k_lo[low_at, lanes], k[:, lanes]))
        ]
        w = softmax_columns(scores)
        weights[g * 2] = w[0]
        weights[g * 2 + 1] = w[1]
        mixed = tn(w[0], v_lo[low_at, lanes]) + tn(w[1], v[:, lanes])
        o1[:, lanes] = unstack_heads(mixed).astype(BF)
    hb[...] = (patch[rows, :].astype(F32) + nn(o1[...], w_out[...])).astype(BF)


def latent_layer(
    ids, hb_a, hb_b, cot, allowed, w_qkv, w_out, gains, w_ff, d_hidden,
    latents, dhb, gain_grad, norms, grads, packed,
    qkv, weights, o2, ff_buf, acc_out, acc_norm, dqkv, sems,
):
    core = ids[0]
    units = w_ff.shape[1]
    step = 256
    parts = 4
    part = units // parts

    fetches = []
    for i in range(parts):
        at = slice(i * part, (i + 1) * part)
        fetches.append(pltpu.make_async_copy(w_ff.at[:, at, :], ff_buf.at[:, at, :], sems.at[i]))
        fetches[-1].start()
    x = jnp.concatenate([hb_a[...], hb_b[...]], 0).astype(F32)
    normed = (x * inverse_rms(x) * gains[0:1]).astype(BF)
    packed[PACK_LEFT : PACK_LEFT + D, :] = normed.T
    for j in range(3):
        qkv[:, j * D : (j + 1) * D] = nn(normed, w_qkv.block(j)[...]).astype(BF)
    for m in range(2):
        rows = slice(m * HD, (m + 1) * HD)
        for g in range(4):
            lanes = slice(g * GROUP, (g + 1) * GROUP)
            k_lanes = slice(D + g * GROUP, D + (g + 1) * GROUP)
            v_lanes = slice(2 * D + g * GROUP, 2 * D + (g + 1) * GROUP)
            stacked = stack_heads(qkv[rows, lanes] * BF(SCALE))
            scores = jnp.where(allowed[m] > 0.5, nt(qkv[rows, k_lanes], stacked), NEG)
            (w,) = softmax_columns([scores])
            weights[m * 4 + g] = w
            o2[rows, lanes] = unstack_heads(tn(w, qkv[rows, v_lanes])).astype(BF)
    packed[PACK_LEFT + D : PACK_LEFT + 2 * D, :] = o2[...].T
    after = x + nn(o2[...], w_out[...])
    yn = (after * inverse_rms(after) * gains[1:2]).astype(BF)
    c = cot[...]
    for h in range(2):

        @pl.when(core == h)
        def _(h=h):
            norms[0:128, :] = yn[:, h * HALF : (h + 1) * HALF]
            norms[128:256, :] = c[:, h * HALF : (h + 1) * HALF]

        @pl.when(core != h)
        def _(h=h):
            for b in range(4):
                lanes = slice(h * HALF + b * 128, h * HALF + (b + 1) * 128)
                packed[PACK_NORMS + b * 256 : PACK_NORMS + b * 256 + 128, :] = yn[:, lanes]
                packed[PACK_NORMS + b * 256 + 128 : PACK_NORMS + (b + 1) * 256, :] = c[:, lanes]

    for copy in fetches:
        copy.wait()
    acc_out[...] = after
    for i in range(units // step):
        at = slice(i * step, (i + 1) * step)
        gate = nt(yn, ff_buf[0, at, :])
        upward = nt(yn, ff_buf[1, at, :])
        du = d_hidden[:, at]
        sig = 1.0 / (1.0 + jnp.exp(-gate))
        active = gate * sig
        hidden = (active * upward).astype(BF)
        d_gate = (du * upward * (sig * (1.0 + gate * (1.0 - sig)))).astype(BF)
        d_up = (du * active).astype(BF)
        for j, value in enumerate((d_gate, d_up, hidden)):
            packed[i * step + j * units : (i + 1) * step + j * units, :] = value.T
        acc_out[...] += nn(hidden, ff_buf[2, at, :])
        back = nn(d_gate, ff_buf[0, at, :]) + nn(d_up, ff_buf[1, at, :])
        if i == 0:
            acc_norm[...] = back
        else:
            acc_norm[...] += back
    latents[...] = acc_out[...]
    back, gain_rows = norm_back(after, gains[1:2], acc_norm[...])
    gain_grad[1:2, :] = jnp.sum(gain_rows, axis=0, keepdims=True)
    d_after = c.astype(F32) + back
    da = d_after.astype(BF)
    d_mixed = nt(da, w_out[...]).astype(BF)
    for m in range(2):
        rows = slice(m * HD, (m + 1) * HD)
        for g in range(4):
            lanes = slice(g * GROUP, (g + 1) * GROUP)
            k_lanes = slice(D + g * GROUP, D + (g + 1) * GROUP)
            v_lanes = slice(2 * D + g * GROUP, 2 * D + (g + 1) * GROUP)
            q_stacked = stack_heads(qkv[rows, lanes] * BF(SCALE))
            o_stacked = stack_heads(d_mixed[rows, lanes])
            w_low = weights[m * 4 + g]
            w = w_low.astype(F32)
            dw = nt(qkv[rows, v_lanes], o_stacked)
            inner = jnp.sum(dw * w, axis=0, keepdims=True)
            ds = (w * (dw - inner)).astype(BF)
            dqkv[rows, lanes] = (unstack_heads(tn(ds, qkv[rows, k_lanes])) * SCALE).astype(BF)
            dqkv[rows, k_lanes] = nn(ds, q_stacked).astype(BF)
            dqkv[rows, v_lanes] = nn(w_low, o_stacked).astype(BF)
    d_normed = sum(nt(dqkv[:, j * D : (j + 1) * D], w_qkv.block(j)[...]) for j in range(3))
    back, gain_rows = norm_back(x, gains[0:1], d_normed)
    gain_grad[0:1, :] = jnp.sum(gain_rows, axis=0, keepdims=True)
    dhb[...] = (d_after + back).astype(BF)
    for h in range(2):
        pieces = (
            dqkv[:, h * HALF : (h + 1) * HALF],
            da[:, h * HALF : (h + 1) * HALF],
            dqkv[:, D + h * HALF : D + (h + 1) * HALF],
            dqkv[:, 2 * D + h * HALF : 2 * D + (h + 1) * HALF],
        )

        @pl.when(core == h)
        def _(pieces=pieces):
            for i, value in enumerate(pieces):
                grads[i * 128 : (i + 1) * 128, :] = value

        @pl.when(core != h)
        def _(pieces=pieces):
            for i, value in enumerate(pieces):
                for b in range(4):
                    first = PACK_GRADS + b * 512 + i * 128
                    packed[first : first + 128, :] = value[:, b * 128 : (b + 1) * 128]


def hidden_back(cot, w_ff, d_hidden, buffer, sems):
    parts = 4
    part = w_ff.shape[1] // parts
    copies = []
    for i in range(parts):
        at = slice(i * part, (i + 1) * part)
        copies.append(pltpu.make_async_copy(w_ff.at[2, at, :], buffer.at[at, :], sems.at[i]))
        copies[-1].start()
    for copy in copies:
        copy.wait()
    for i in range(w_ff.shape[1] // 256):
        at = slice(i * 256, (i + 1) * 256)
        d_hidden[:, at] = nt(cot[...], buffer[at, :])


def half_of(core, g, mine, other):
    lanes = slice((g % 2) * GROUP, (g % 2 + 1) * GROUP)

    def put(at, value):
        @pl.when(core == g // 2)
        def _():
            mine[at, lanes] = value

        @pl.when(core != g // 2)
        def _():
            other[at, lanes] = value

    return put


def encoder_attention_back(
    ids, dhb, w_out, q, k_lo, v_lo, k_a, k_b, v_a, v_b, w_a, w_b, mine, other
):
    d_mixed = nt(dhb[...], w_out[...]).astype(BF)
    for g in range(4):
        lanes = slice(g * GROUP, (g + 1) * GROUP)
        put = half_of(ids[0], g, mine, other)
        put(slice(128, 256), dhb[:, lanes])
        for m, (k_up, v_up, weights) in enumerate(((k_a, v_a, w_a), (k_b, v_b, w_b))):
            rows = slice(m * HD, (m + 1) * HD)
            low_at = slice(m * 256, (m + 1) * 256)
            q_stacked = stack_heads(q[rows, lanes] * BF(SCALE))
            o_stacked = stack_heads(d_mixed[rows, lanes])
            low = [weights[g * 2 + h] for h in range(2)]
            w = [piece.astype(F32) for piece in low]
            dw = [nt(values, o_stacked) for values in (v_lo[low_at, lanes], v_up[:, lanes])]
            inner = sum(jnp.sum(a * b, axis=0, keepdims=True) for a, b in zip(dw, w))
            ds = [(b * (a - inner)).astype(BF) for a, b in zip(dw, w)]
            dq = tn(ds[0], k_lo[low_at, lanes]) + tn(ds[1], k_up[:, lanes])
            put(rows, (unstack_heads(dq) * SCALE).astype(BF))
            for h in range(2):
                base = h * HALF + m * 256
                put(slice(256 + base, 512 + base), nn(ds[h], q_stacked).astype(BF))
                put(slice(1280 + base, 1536 + base), nn(low[h], o_stacked).astype(BF))


def both_columns(core, block, w_qkv):
    return [
        w_qkv.block(block)[:, pl.ds(pl.multiple_of(which * HALF, HALF), HALF)] for which in (core, 1 - core)
    ]


def bytes_back(core, h, m, source, w_qkv, gains, grads):
    d_norm = sum(
        nt(ref[1024 * block - 768 + h * HALF + m * 256 : 1024 * block - 512 + h * HALF + m * 256, :], columns)
        for block in (1, 2)
        for ref, columns in zip(grads, both_columns(core, block, w_qkv))
    )
    back, gain_rows = norm_back(source.astype(F32), gains[1:2], d_norm)
    return back.astype(BF), jnp.sum(gain_rows, axis=0, keepdims=True)


def encoder_upper_back(ids, up_a, up_b, w_qkv, gains, mine, other, up_grad, gain_grad):
    total = jnp.zeros((1, D), F32)
    for m, source in enumerate((up_a, up_b)):
        back, rows = bytes_back(ids[0], 1, m, source[...], w_qkv, gains, (mine, other))
        up_grad[m * 256 : (m + 1) * 256, :] = back
        total = total + rows
    gain_grad[...] = total


def encoder_lower_back(
    ids, dhb, patch, low, w_qkv, gains, mine, other, after, patch_grad, low_grad, gain_grad
):
    core = ids[0]
    up_norm = sum(nt(ref[0:128, :], columns) for ref, columns in zip((mine, other), both_columns(core, 0, w_qkv)))
    back, gain_rows = norm_back(patch[...].astype(F32), gains[0:1], up_norm)
    gain_grad[0:1, :] = jnp.sum(gain_rows, axis=0, keepdims=True)
    patch_grad[...] = dhb[...].astype(F32) + back
    total = jnp.zeros((1, D), F32)
    for m in range(2):
        at = slice(m * 256, (m + 1) * 256)
        back, rows = bytes_back(core, 0, m, low[at, :], w_qkv, gains, (mine, other))
        low_grad[at, :] = back
        total = total + rows
    gain_grad[1:2, :] = total


def turn_encoder(pn, o_a, o_b, bn_lo, bn_a, bn_b, packed):
    for b, rows in enumerate([bn_lo[i * 128 : (i + 1) * 128, :] for i in range(4)]
                             + [ref[i * 128 : (i + 1) * 128, :] for ref in (bn_a, bn_b) for i in range(2)]):
        packed[b * D : (b + 1) * D, :] = rows.T
    packed[PACK_LEFT : PACK_LEFT + D, :] = pn[...].T
    packed[PACK_LEFT + D : PACK_LEFT + 2 * D, :] = jnp.concatenate([o_a[...], o_b[...]], 0).T


def rows_of_both(left, left_far, at):
    return jnp.concatenate([left[at, :], left_far[at, :]], 1)


def below(near, far, rows):
    return jnp.concatenate([near[rows, :], far[rows, :]], 0)


def encoder_weights(ids, packed, packed_far, near, far, after, *blocks):
    u = ids[1]
    queries = below(near, far, slice(0, 128))
    outputs = below(near, far, slice(128, 256))
    for k in range(4):
        first = lax.rem(u + k, 4) * 256

        def at(base, first=first):
            return pl.ds(pl.multiple_of(first + base, 256), 256)

        blocks[k][0] = nn(rows_of_both(packed, packed_far, at(PACK_LEFT)), queries).astype(BF)
        blocks[k][3] = nn(rows_of_both(packed, packed_far, at(PACK_LEFT + D)), outputs).astype(BF)
        lefts = [jnp.concatenate([ref[at(b * D), :] for b in range(8)], 1) for ref in (packed, packed_far)]
        for block in (1, 2):
            rows = slice(1024 * block - 768, 1024 * block + 256)
            blocks[k][block] = (nn(lefts[0], near[rows, :]) + nn(lefts[1], far[rows, :])).astype(BF)


def unpack(packed, first, rows):
    return jnp.concatenate([packed[first + b * rows : first + (b + 1) * rows, :] for b in range(4)], 1)


def latent_weights(ids, packed, packed_far, near, *blocks):
    u = ids[1]
    far = unpack(packed_far, PACK_GRADS, 512)
    rights = [jnp.concatenate([near[i * 128 : (i + 1) * 128, :], far[i * 128 : (i + 1) * 128, :]], 0) for i in range(4)]
    for k in range(4):
        first = PACK_LEFT + lax.rem(u + k, 4) * 256
        at = pl.ds(pl.multiple_of(first, 256), 256)
        low_at = pl.ds(pl.multiple_of(first + D, 256), 256)
        for block, (source, i) in enumerate(((at, 0), (at, 2), (at, 3), (low_at, 1))):
            blocks[k][block] = nn(rows_of_both(packed, packed_far, source), rights[i]).astype(BF)


def ff_weights_grad(ids, packed, packed_far, norms, own, right, left, far_a, far_b):
    core, u = ids[0], ids[1]
    share = UNITS // 16
    far = unpack(packed_far, PACK_NORMS, 256)
    normed = jnp.concatenate([norms[0:128, :], far[0:128, :]], 0)
    cot = jnp.concatenate([norms[128:256, :], far[128:256, :]], 0)
    for k in range(4):
        there = lax.rem(u + k, 4)
        for v in range(4):
            chunk = jnp.where(core == 0, there * 4 + v, v * 4 + there)
            for j in range(3):
                at = pl.ds(pl.multiple_of(j * UNITS + chunk * share, 16), share)
                value = nn(rows_of_both(packed, packed_far, at), normed if j < 2 else cot).astype(BF)
                rows = slice(j * share, (j + 1) * share)
                if k == 2:
                    far_a[v, rows, :] = value[:, :GROUP]
                    far_b[v, rows, :] = value[:, GROUP:]
                else:
                    (own, right, None, left)[k][v, rows, :] = value


def ff_add(right, left, from_left, from_right, after, new_right, new_left):
    new_right[:, :, 0:GROUP] = (right[:, :, 0:GROUP].astype(F32) + from_left[...].astype(F32)).astype(BF)
    new_right[:, :, GROUP:] = right[:, :, GROUP:]
    new_left[:, :, 0:GROUP] = left[:, :, 0:GROUP]
    new_left[:, :, GROUP:] = (left[:, :, GROUP:].astype(F32) + from_right[...].astype(F32)).astype(BF)


def sum_four(own, a, b, c):
    return own.astype(F32) + a.astype(F32) + b.astype(F32) + c.astype(F32)


def pack_gain(value):
    high = value.astype(BF)
    low = (value - high.astype(F32)).astype(BF)
    return jnp.concatenate(
        [high.astype(F32), low.astype(F32), jnp.zeros((8, HALF), F32)], 0
    ).astype(BF)


def unpack_gain(rows):
    rows = rows.astype(F32)
    return rows[0:4] + rows[4:8]


GAIN_AT = slice(256, 272)


def attn_sum_first(ids, own, a, b, c, *outs):
    v = ids[2]
    for k in range(4):
        at = pl.ds(pl.multiple_of(lax.rem(v + k, 4) * HD, HD), HD)
        for block in range(4):
            outs[k][block * HD : (block + 1) * HD, :] = sum_four(
                own[block, at, :], a[block, at, :], b[block, at, :], c[block, at, :]
            ).astype(BF)


def attn_sum_first_gain(ids, own, a, b, c, enc_gain, up_gain, lat_gain, *outs):
    attn_sum_first(ids, own, a, b, c, *outs)
    first = ids[4] == 0
    gain = jnp.where(
        first, jnp.concatenate([enc_gain[0:1, :], enc_gain[1:2, :] + up_gain[...]], 0), lat_gain[...]
    )
    halves = [gain[i : i + 1, h * HALF : (h + 1) * HALF] for i in range(2) for h in range(2)]
    packed = pack_gain(jnp.concatenate(halves, 0))
    for out in outs:
        out[GAIN_AT, :] = packed


def sum_all(*refs):
    refs, out = refs[:-1], refs[-1]
    out[0:256, :] = sum(ref[0:256, :].astype(F32) for ref in refs).astype(BF)
    out[GAIN_AT, :] = pack_gain(sum(unpack_gain(ref[GAIN_AT, :]) for ref in refs))


def stack_rows(*refs):
    refs, out = refs[:-1], refs[-1]
    for j, ref in enumerate(refs):
        out[j * 256 : (j + 1) * 256, :] = ref[0:256, :]
    out[1024:1040, :] = refs[0][GAIN_AT, :]


def ff_sum_first(ids, own, a, b, *outs):
    v = ids[2]
    for k in range(4):
        at = lax.rem(v + k, 4)
        outs[k][...] = (own[at].astype(F32) + a[at].astype(F32) + b[at].astype(F32)).astype(BF)


def ff_sum_second(own, a, b, c, out):
    out[...] = sum_four(own[...], a[...], b[...], c[...]).astype(BF)


def final_attn(ids, *refs):
    pieces, (qkv, out, gain) = refs[:8], refs[8:]
    step = pl.program_id(0)
    for side in range(2):
        core = ids[0] if side == 0 else 1 - ids[0]
        u = ids[1] if side == 0 else ids[2]
        v = ids[2] if side == 0 else ids[1]
        for k in range(4):
            piece = pieces[side * 4 + k]

            @pl.when(lax.rem(u + k, 4) == step)
            def _(piece=piece, v=v, core=core):
                for j in range(4):
                    at = pl.ds(pl.multiple_of(lax.rem(v + j, 4) * HD, HD), HD)
                    for block in range(4):
                        target, column = (qkv, block * D) if block < 3 else (out, 0)
                        lanes = pl.ds(pl.multiple_of(core * HALF + column, HALF), HALF)
                        first = j * 256 + block * HD
                        target[at, lanes] = piece[first : first + HD, :].astype(F32)

    mine = sum(unpack_gain(piece[1024:1040, :]) for piece in pieces[:4])
    other = sum(unpack_gain(piece[1024:1040, :]) for piece in pieces[4:])
    total = mine + other
    for i in range(2):
        for h in range(2):
            gain[i : i + 1, h * HALF : (h + 1) * HALF] = total[2 * i + h : 2 * i + h + 1, :]


SMEM = pltpu.MemorySpace.SMEM
VMEM = pltpu.MemorySpace.VMEM


def size(shape, dtype):
    return math.prod(shape) * jnp.dtype(dtype).itemsize


class Arriving:
    def __init__(self, copy, buffer):
        self.copy, self.buffer, self.here = copy, buffer, False

    def ready(self):
        if not self.here:
            self.copy.wait()
            self.here = True
        return self.buffer

    def __getitem__(self, index):
        return self.ready()[index]


class ArrivingBlocks:
    def __init__(self, blocks):
        self.blocks = blocks

    def block(self, j):
        return self.blocks[j]


def fetching(kernel, n_args, n_outs, plan):
    def wrapped(*refs):
        args, outs, rest = list(refs[:n_args]), refs[n_args : n_args + n_outs], refs[n_args + n_outs :]
        scratch, buffers, sems = rest[: len(rest) - len(plan) - 1], rest[len(rest) - len(plan) - 1 : -1], rest[-1]
        arriving = []
        blocks = {}
        for i, (a, j) in enumerate(plan):
            source = refs[a] if j is None else refs[a].at[:, j * D : (j + 1) * D]
            copy = pltpu.make_async_copy(source, buffers[i], sems.at[i])
            copy.start()
            arriving.append(Arriving(copy, buffers[i]))
            if j is None:
                args[a] = arriving[-1]
            else:
                blocks.setdefault(a, {})[j] = arriving[-1]
        for a, found in blocks.items():
            args[a] = ArrivingBlocks(found)
        kernel(*args, *outs, *scratch)
        for value in arriving:
            value.ready()

    return wrapped


def call(kernel, args, outs, scratch=(), spaces=None, spare=6, fetch=()):
    spaces = dict(spaces or {})
    scratch = list(scratch)
    plan = [f if isinstance(f, tuple) else (f, None) for f in fetch]
    if plan:
        for a, j in plan:
            spaces[a] = pl.ANY
            shape = args[a].shape if j is None else (args[a].shape[0], D)
            scratch.append(pltpu.VMEM(shape, args[a].dtype))
        scratch.append(pltpu.SemaphoreType.DMA((len(plan),)))
        kernel = fetching(kernel, len(args), len(outs), plan)
    vmem = sum(size(a.shape, a.dtype) for i, a in enumerate(args) if i not in spaces)
    vmem += sum(size(*o) for o in outs)
    vmem += sum(size(s.shape, s.dtype) for s in scratch if hasattr(s, "shape") and s.memory_space == VMEM)
    specs = [pl.BlockSpec(memory_space=spaces.get(i, VMEM)) for i in range(len(args))]
    return pl.pallas_call(
        kernel,
        out_shape=[jax.ShapeDtypeStruct(s, t) for s, t in outs],
        in_specs=specs,
        out_specs=[pl.BlockSpec(memory_space=VMEM) for _ in outs],
        scratch_shapes=scratch,
        compiler_params=pltpu.CompilerParams(vmem_limit_bytes=vmem + spare * 1024 * 1024),
    )(*args)


def nothing(outs):
    def kernel(*refs):
        pass

    return pl.pallas_call(
        kernel,
        out_shape=[jax.ShapeDtypeStruct(s, t) for s, t in outs],
        out_specs=[pl.BlockSpec(memory_space=pl.ANY) for _ in outs],
    )()


def on_section(flag, kernel, args, outs, **rest):
    return lax.cond(
        flag, lambda: call(kernel, args, outs, **rest), lambda: nothing(outs)
    )


def along(value, by):
    return lax.ppermute(value, "s", [(0, 1)] if by > 0 else [(1, 0)])


def swap(value, axis, sections=(0, 1)):
    pairs = [(s * 2 + i, s * 2 + 1 - i) for s in sections for i in range(2)]
    return lax.ppermute(value, ("s", axis), pairs)


def plane_shift(value, which, by, sections=(0, 1)):
    pairs = []
    for s in sections:
        for y in range(4):
            for x in range(4):
                for core in range(2):
                    ty, tx = ((y + by) % 4, x) if core == which else (y, (x + by) % 4)
                    pairs.append((((s * 4 + y) * 4 + x) * 2 + core, ((s * 4 + ty) * 4 + tx) * 2 + core))
    return lax.ppermute(value, ("s", "y", "x", "core"), pairs)


def exchange(blocks, which, sections=(0, 1)):
    return [plane_shift(blocks[k], which, k, sections) for k in (1, 2, 3)]


def collect(block, which):
    return [block] + [plane_shift(block, which, -k) for k in (1, 2, 3)]


def pick(stack, index, dim):
    return lax.dynamic_index_in_dim(stack, index, dim, keepdims=False)


def shards(patch_io, byte_states, patch_lengths, patch_live, attn_qkv, attn_out, gains, ff_weights):
    section = lax.axis_index("s")
    core = lax.axis_index("core")
    zh = lax.axis_index("zh")
    y, x = lax.axis_index("y"), lax.axis_index("x")
    first = section == 0
    second = section == 1
    ids = jnp.stack([core, jnp.where(core == 0, y, x), jnp.where(core == 0, x, y), zh, section])
    ids = ids.astype(jnp.int32)
    w_qkv = attn_qkv[0]
    w_out = attn_out[0]
    gain_pair = gains[0]
    micro, seq = patch_io.shape[1], patch_io.shape[3]
    half_bytes = byte_states.shape[2]
    units = ff_weights.shape[0]
    rows = micro * seq
    own_rows = patch_io.reshape(rows, D)
    up_a = along(byte_states[0, 0], -1)
    up_b = along(byte_states[1, 0], -1)
    lower = byte_states.reshape(micro * half_bytes, D)
    w_ff = jnp.swapaxes(ff_weights, 0, 1)
    lengths = patch_lengths[:, 0]
    live = patch_live[:, 0]
    ends = jnp.cumsum(lengths, axis=1)
    bounds = jnp.tile(jnp.stack([ends - lengths, ends], 1), (1, 1, 4))
    places = lax.iota(jnp.int32, seq)
    causal = places[:, None] <= places[None, :]
    diagonal = places[:, None] == places[None, :]
    allowed = causal[None] & ((live[:, :, None] == 1) | diagonal[None])
    allowed = lax.optimization_barrier(jnp.tile(allowed.astype(F32), (1, 1, 4)))

    wide = ((rows, D), BF)
    short = ((seq, D), BF)
    tall = ((micro * half_bytes, D), BF)
    piece = ((half_bytes, D), BF)
    (d_hidden,) = on_section(
        second,
        hidden_back,
        (own_rows, w_ff),
        [((rows, units), F32)],
        spaces={1: pl.ANY},
        scratch=[pltpu.VMEM((units, D), BF), pltpu.SemaphoreType.DMA((4,))],
    )
    pn, q, bn_lo, k_lo, v_lo = on_section(
        first,
        encode_lower,
        (own_rows, lower, w_qkv, gain_pair),
        [wide, wide, tall, tall, tall],
        fetch=((2, 0), 1, (2, 1), (2, 2)),
    )
    rest = []
    for m, up in enumerate((up_a, up_b)):
        rest.append(
            on_section(
                first,
                functools.partial(encode_rest, m),
                (own_rows, up, w_qkv, w_out, gain_pair, bounds, q, k_lo, v_lo),
                [short, short, ((8, 256, GROUP), BF), piece, piece, piece],
                fetch=((2, 1), (2, 2), 7, 8, 3),
            )
        )
    (hb_a, o_a, w_a, bn_a, k_a, v_a), (hb_b, o_b, w_b, bn_b, k_b, v_b) = rest
    arrived = [along(hb_a, 1), along(hb_b, 1)]

    latent_outs = [
        ((rows, D), F32), wide, ((2, D), F32), ((256, HALF), BF), ((512, HALF), BF), ((PACK_ROWS, rows), BF),
    ]

    def latent():
        return call(
            latent_layer,
            (ids, *arrived, own_rows, allowed, w_qkv, w_out, gain_pair, w_ff, d_hidden),
            latent_outs,
            spaces={0: SMEM, 8: pl.ANY},
            fetch=((5, 0), (5, 1), (5, 2), 6),
            scratch=[
                pltpu.VMEM((rows, 3 * D), BF),
                pltpu.VMEM((8, HD, GROUP), BF),
                pltpu.VMEM((rows, D), BF),
                pltpu.VMEM((3, units, D), BF),
                pltpu.VMEM((rows, D), F32),
                pltpu.VMEM((rows, D), F32),
                pltpu.VMEM((rows, 3 * D), BF),
                pltpu.SemaphoreType.DMA((4,)),
            ],
        )

    def turn():
        return nothing(latent_outs[:5]) + call(
            turn_encoder, (pn, o_a, o_b, bn_lo, bn_a, bn_b), latent_outs[5:]
        )

    latents, dhb, latent_gain, norms, lat_grads, packed = lax.cond(second, latent, turn)
    returned = along(dhb, -1)

    packed_far = swap(packed, "core")

    share = units // 16
    ff_block = ((4, 3 * share, HALF), BF)
    ff_half = ((4, 3 * share, GROUP), BF)
    ff_own, ff_right, ff_left, ff_far_a, ff_far_b = on_section(
        second,
        ff_weights_grad,
        (ids, packed, packed_far, norms),
        [ff_block, ff_block, ff_block, ff_half, ff_half],
        spaces={0: SMEM},
    )

    grads_long = ((2304, HALF), BF)
    enc_grads, enc_other = on_section(
        first,
        encoder_attention_back,
        (ids, returned, w_out, q, k_lo, v_lo, k_a, k_b, v_a, v_b, w_a, w_b),
        [grads_long, grads_long],
        spaces={0: SMEM},
        fetch=(2, 5, 8, 10, 4, 6, 9, 11, 7),
    )
    enc_far = swap(enc_other, "core", (0,))
    up_grad, up_gain = on_section(
        first,
        encoder_upper_back,
        (ids, up_a, up_b, w_qkv, gain_pair, enc_grads, enc_other),
        [tall, ((1, D), F32)],
        spaces={0: SMEM},
        fetch=(5, (3, 1), 6, (3, 2), 1, 2),
    )
    up_arrived = along(up_grad, 1)
    ff_far_a, ff_far_b, up_gain = lax.optimization_barrier((ff_far_a, ff_far_b, up_gain))
    from_left = plane_shift(ff_far_a, 0, 1)
    from_right = plane_shift(ff_far_b, 0, -1)
    outs = [((4, 256, HALF), BF)] * 4
    blocks = lax.cond(
        first,
        lambda: call(
            encoder_weights,
            (ids, packed, packed_far, enc_grads, enc_far, up_gain),
            outs,
            spaces={0: SMEM, 5: pl.ANY},
            fetch=(3, 4, 1, 2),
        ),
        lambda: call(latent_weights, (ids, packed, packed_far, lat_grads), outs, spaces={0: SMEM}),
    )
    last, from_left, from_right = lax.optimization_barrier((blocks[3], from_left, from_right))
    blocks = [*blocks[:3], last]
    got, up_arrived = lax.optimization_barrier((exchange(blocks, 0), up_arrived))
    low_outs = [((rows, D), F32), tall, ((2, D), F32)]

    def lower_grads():
        parts = call(
            encoder_lower_back,
            (ids, returned, own_rows, lower, w_qkv, gain_pair, enc_grads, enc_other, blocks[0]),
            low_outs,
            spaces={0: SMEM, 8: pl.ANY},
            fetch=(6, 7, (4, 0), (4, 1), (4, 2), 3),
        )
        return (*parts, *nothing([ff_block, ff_block]))

    def ff_middle():
        added = call(
            ff_add, (ff_right, ff_left, from_left, from_right, blocks[0]), [ff_block, ff_block], spaces={4: pl.ANY}
        )
        return (*nothing(low_outs), *added)

    patch_grad, low_grad, encoder_gain, ff_right_sum, ff_left_sum = lax.cond(first, lower_grads, ff_middle)
    line = [((272, HALF), BF)]
    blocks = call(
        attn_sum_first_gain,
        (ids, blocks[0], *got, encoder_gain, up_gain, latent_gain),
        line * 4,
        spaces={0: SMEM},
    )
    ff_right_sum, ff_left_sum, _ = lax.optimization_barrier((ff_right_sum, ff_left_sum, blocks))
    from_left = plane_shift(ff_right_sum, 0, 1)
    from_right = plane_shift(ff_left_sum, 0, -1)
    (block,) = call(sum_all, (blocks[0], *exchange(blocks, 1)), line)
    byte_grad = jnp.where(first, low_grad, up_arrived)
    patch_out = jnp.where(first, patch_grad, latents)
    from_left, from_right, block, byte_grad, patch_out = lax.optimization_barrier(
        (from_left, from_right, block, byte_grad, patch_out)
    )
    ff_line = ((3 * share, HALF), BF)
    ff_blocks = on_section(
        second, ff_sum_first, (ids, ff_own, from_left, from_right), [ff_line] * 4, spaces={0: SMEM}
    )
    ff_got = exchange(ff_blocks, 1)
    across, ff_got = lax.optimization_barrier((swap(block, "zh"), ff_got))
    (block,) = call(sum_all, (block, across), line)
    (block,) = call(stack_rows, collect(block, 1), [((1040, HALF), BF)])
    pieces = collect(block, 0)
    own_far = swap(block, "core")
    (ff_sum,) = on_section(second, ff_sum_second, (ff_blocks[0], *ff_got), [ff_line])
    ff_sum = ff_sum.reshape(3, 2, share // 2, HALF)
    ff_far = swap(pick(ff_sum, 1 - zh, 1), "zh")
    ff_sum = (pick(ff_sum, zh, 1).astype(F32) + ff_far.astype(F32)).astype(BF).reshape(3, 2, share // 4, HALF)
    ff_mine = pick(ff_sum, core, 1)
    ff_far = swap(pick(ff_sum, 1 - core, 1), "core")

    def ff_result():
        low, high = jnp.where(core == 0, ff_mine, ff_far), jnp.where(core == 0, ff_far, ff_mine)
        return jnp.swapaxes(jnp.concatenate([low, high], 2), 0, 1).astype(F32)

    ff_grad = lax.cond(second, ff_result, lambda: jnp.zeros((share // 4, 3, D), F32))
    ff_grad, *pieces = lax.optimization_barrier((ff_grad, *pieces))
    pieces = pieces + [own_far] + [swap(p, "core") for p in pieces[1:]]
    whole = lambda p: pl.BlockSpec(p.shape, lambda i, n=p.ndim: (0,) * n)
    total_qkv, total_out, total_gain = pl.pallas_call(
        final_attn,
        grid=(4,),
        out_shape=[
            jax.ShapeDtypeStruct((D, 3 * D), F32),
            jax.ShapeDtypeStruct((D, D), F32),
            jax.ShapeDtypeStruct((2, D), F32),
        ],
        in_specs=[pl.BlockSpec(memory_space=SMEM)] + [whole(p) for p in pieces],
        out_specs=[
            pl.BlockSpec((256, 3 * D), lambda i: (i, 0)),
            pl.BlockSpec((256, D), lambda i: (i, 0)),
            pl.BlockSpec((2, D), lambda i: (0, 0)),
        ],
        compiler_params=pltpu.CompilerParams(vmem_limit_bytes=FINAL_VMEM),
    )(ids, *pieces)
    return (
        patch_out.reshape(1, micro, 1, seq, D),
        byte_grad.reshape(micro, 1, half_bytes, D),
        total_qkv[None],
        total_out[None],
        total_gain[None],
        ff_grad[None],
    )


def solution(mesh):
    fine = Mesh(mesh.devices.reshape(2, 4, 4, 2, 2), ("s",) + BATCH)
    in_specs = (
        P("s", None, BATCH, None, None),
        P(None, BATCH, "s", None),
        P(None, BATCH, None),
        P(None, BATCH, None),
        P("s", None, None),
        P("s", None, None),
        P("s", None, None),
        P(),
    )
    out_specs = (
        P("s", None, BATCH, None, None),
        P(None, BATCH, "s", None),
        P("s", None, None),
        P("s", None, None),
        P("s", None, None),
        P("s", BATCH, None, None),
    )
    return jax.shard_map(shards, mesh=fine, in_specs=in_specs, out_specs=out_specs, check_vma=False)
```

```python
import functools
import math

import jax
import jax.numpy as jnp
from jax import lax
from jax.experimental import pallas as pl
from jax.experimental.pallas import tpu as pltpu
from jax.sharding import Mesh
from jax.sharding import PartitionSpec as P

HD = 64
SCALE = HD**-0.5
EPS = 1e-05
NEG = -1e30
BATCH = ("y", "x", "zh", "core")
BF = jnp.bfloat16
F32 = jnp.float32
D = 1024
HALF = 512
GROUP = 256
FINAL_VMEM = 32 * 1024 * 1024


UNITS = 2816
PACK_NORMS = 3 * UNITS
PACK_LEFT = PACK_NORMS + 4 * 256
PACK_GRADS = PACK_LEFT + 2 * D
PACK_ROWS = PACK_GRADS + 4 * 512


def nn(a, b):
    return lax.dot_general(a, b, (((1,), (0,)), ((), ())), preferred_element_type=F32)


def nt(a, b):
    return lax.dot_general(a, b, (((1,), (1,)), ((), ())), preferred_element_type=F32)


def tn(a, b):
    return lax.dot_general(a, b, (((0,), (0,)), ((), ())), preferred_element_type=F32)


def inverse_rms(x):
    return lax.rsqrt(jnp.mean(x * x, axis=-1, keepdims=True) + EPS)


def norm_back(x, gain, up):
    r = inverse_rms(x)
    scaled = up * gain
    inner = jnp.mean(scaled * x, axis=-1, keepdims=True)
    return r * (scaled - x * (r * r * inner)), up * (x * r)


def stack_heads(rows):
    head = lax.broadcasted_iota(jnp.int32, rows.shape, 1) // HD
    return jnp.concatenate([jnp.where(head == h, rows, jnp.zeros_like(rows)) for h in range(4)], 0)


def unstack_heads(stacked):
    head = lax.broadcasted_iota(jnp.int32, (HD, GROUP), 1) // HD
    out = stacked[0:HD]
    for h in range(1, 4):
        out = jnp.where(head == h, stacked[h * HD : (h + 1) * HD], out)
    return out


def softmax_columns(scores):
    top = functools.reduce(jnp.maximum, [jnp.max(s, axis=0, keepdims=True) for s in scores])
    parts = [jnp.exp(s - top) for s in scores]
    inverse = 1.0 / sum(jnp.sum(p, axis=0, keepdims=True) for p in parts)
    return [(p * inverse).astype(BF) for p in parts]


def encode_lower(patch, low, w_qkv, gains, pn, q, bn, k, v):
    x = patch[...].astype(F32)
    normed = (x * inverse_rms(x) * gains[0:1]).astype(BF)
    pn[...] = normed
    q[...] = nn(normed, w_qkv.block(0)[...]).astype(BF)
    for i in range(2):
        at = pl.ds(i * 256, 256)
        b = low[at, :].astype(F32)
        normed = (b * inverse_rms(b) * gains[1:2]).astype(BF)
        bn[at, :] = normed
        k[at, :] = nn(normed, w_qkv.block(1)[...]).astype(BF)
        v[at, :] = nn(normed, w_qkv.block(2)[...]).astype(BF)


def encode_rest(m, patch, up, w_qkv, w_out, gains, bounds, q, k_lo, v_lo, hb, o1, weights, bn, k, v):
    b = up[...].astype(F32)
    normed = (b * inverse_rms(b) * gains[1:2]).astype(BF)
    bn[...] = normed
    k[...] = nn(normed, w_qkv.block(1)[...]).astype(BF)
    v[...] = nn(normed, w_qkv.block(2)[...]).astype(BF)
    spot = lax.broadcasted_iota(jnp.int32, (256, GROUP), 0)
    start = bounds[m, 0:1, :]
    end = bounds[m, 1:2, :]
    inside = [(spot + h * 256 >= start) & (spot + h * 256 < end) for h in range(2)]
    low_at = slice(m * 256, (m + 1) * 256)
    rows = slice(m * HD, (m + 1) * HD)
    for g in range(4):
        lanes = slice(g * GROUP, (g + 1) * GROUP)
        stacked = stack_heads(q[rows, lanes] * BF(SCALE))
        scores = [
            jnp.where(inside[h], nt(keys, stacked), NEG)
            for h, keys in enumerate((k_lo[low_at, lanes], k[:, lanes]))
        ]
        w = softmax_columns(scores)
        weights[g * 2] = w[0]
        weights[g * 2 + 1] = w[1]
        mixed = tn(w[0], v_lo[low_at, lanes]) + tn(w[1], v[:, lanes])
        o1[:, lanes] = unstack_heads(mixed).astype(BF)
    hb[...] = (patch[rows, :].astype(F32) + nn(o1[...], w_out[...])).astype(BF)


def latent_layer(
    ids, hb_a, hb_b, cot, allowed, w_qkv, w_out, gains, w_ff, d_hidden,
    latents, dhb, gain_grad, norms, grads, packed,
    qkv, weights, o2, ff_buf, acc_out, acc_norm, dqkv, sems,
):
    core = ids[0]
    units = w_ff.shape[1]
    step = 256
    parts = 4
    part = units // parts

    fetches = []
    for i in range(parts):
        at = slice(i * part, (i + 1) * part)
        fetches.append(pltpu.make_async_copy(w_ff.at[:, at, :], ff_buf.at[:, at, :], sems.at[i]))
        fetches[-1].start()
    x = jnp.concatenate([hb_a[...], hb_b[...]], 0).astype(F32)
    normed = (x * inverse_rms(x) * gains[0:1]).astype(BF)
    packed[PACK_LEFT : PACK_LEFT + D, :] = normed.T
    for j in range(3):
        qkv[:, j * D : (j + 1) * D] = nn(normed, w_qkv.block(j)[...]).astype(BF)
    for m in range(2):
        rows = slice(m * HD, (m + 1) * HD)
        for g in range(4):
            lanes = slice(g * GROUP, (g + 1) * GROUP)
            k_lanes = slice(D + g * GROUP, D + (g + 1) * GROUP)
            v_lanes = slice(2 * D + g * GROUP, 2 * D + (g + 1) * GROUP)
            stacked = stack_heads(qkv[rows, lanes] * BF(SCALE))
            scores = jnp.where(allowed[m] > 0.5, nt(qkv[rows, k_lanes], stacked), NEG)
            (w,) = softmax_columns([scores])
            weights[m * 4 + g] = w
            o2[rows, lanes] = unstack_heads(tn(w, qkv[rows, v_lanes])).astype(BF)
    packed[PACK_LEFT + D : PACK_LEFT + 2 * D, :] = o2[...].T
    after = x + nn(o2[...], w_out[...])
    yn = (after * inverse_rms(after) * gains[1:2]).astype(BF)
    c = cot[...]
    for h in range(2):

        @pl.when(core == h)
        def _(h=h):
            norms[0:128, :] = yn[:, h * HALF : (h + 1) * HALF]
            norms[128:256, :] = c[:, h * HALF : (h + 1) * HALF]

        @pl.when(core != h)
        def _(h=h):
            for b in range(4):
                lanes = slice(h * HALF + b * 128, h * HALF + (b + 1) * 128)
                packed[PACK_NORMS + b * 256 : PACK_NORMS + b * 256 + 128, :] = yn[:, lanes]
                packed[PACK_NORMS + b * 256 + 128 : PACK_NORMS + (b + 1) * 256, :] = c[:, lanes]

    for copy in fetches:
        copy.wait()
    acc_out[...] = after
    for i in range(units // step):
        at = slice(i * step, (i + 1) * step)
        gate = nt(yn, ff_buf[0, at, :])
        upward = nt(yn, ff_buf[1, at, :])
        du = d_hidden[:, at]
        sig = 1.0 / (1.0 + jnp.exp(-gate))
        active = gate * sig
        hidden = (active * upward).astype(BF)
        d_gate = (du * upward * (sig * (1.0 + gate * (1.0 - sig)))).astype(BF)
        d_up = (du * active).astype(BF)
        for j, value in enumerate((d_gate, d_up, hidden)):
            packed[i * step + j * units : (i + 1) * step + j * units, :] = value.T
        acc_out[...] += nn(hidden, ff_buf[2, at, :])
        back = nn(d_gate, ff_buf[0, at, :]) + nn(d_up, ff_buf[1, at, :])
        if i == 0:
            acc_norm[...] = back
        else:
            acc_norm[...] += back
    latents[...] = acc_out[...]
    back, gain_rows = norm_back(after, gains[1:2], acc_norm[...])
    gain_grad[1:2, :] = jnp.sum(gain_rows, axis=0, keepdims=True)
    d_after = c.astype(F32) + back
    da = d_after.astype(BF)
    d_mixed = nt(da, w_out[...]).astype(BF)
    for m in range(2):
        rows = slice(m * HD, (m + 1) * HD)
        for g in range(4):
            lanes = slice(g * GROUP, (g + 1) * GROUP)
            k_lanes = slice(D + g * GROUP, D + (g + 1) * GROUP)
            v_lanes = slice(2 * D + g * GROUP, 2 * D + (g + 1) * GROUP)
            q_stacked = stack_heads(qkv[rows, lanes] * BF(SCALE))
            o_stacked = stack_heads(d_mixed[rows, lanes])
            w_low = weights[m * 4 + g]
            w = w_low.astype(F32)
            dw = nt(qkv[rows, v_lanes], o_stacked)
            inner = jnp.sum(dw * w, axis=0, keepdims=True)
            ds = (w * (dw - inner)).astype(BF)
            dqkv[rows, lanes] = (unstack_heads(tn(ds, qkv[rows, k_lanes])) * SCALE).astype(BF)
            dqkv[rows, k_lanes] = nn(ds, q_stacked).astype(BF)
            dqkv[rows, v_lanes] = nn(w_low, o_stacked).astype(BF)
    d_normed = sum(nt(dqkv[:, j * D : (j + 1) * D], w_qkv.block(j)[...]) for j in range(3))
    back, gain_rows = norm_back(x, gains[0:1], d_normed)
    gain_grad[0:1, :] = jnp.sum(gain_rows, axis=0, keepdims=True)
    dhb[...] = (d_after + back).astype(BF)
    for h in range(2):
        pieces = (
            dqkv[:, h * HALF : (h + 1) * HALF],
            da[:, h * HALF : (h + 1) * HALF],
            dqkv[:, D + h * HALF : D + (h + 1) * HALF],
            dqkv[:, 2 * D + h * HALF : 2 * D + (h + 1) * HALF],
        )

        @pl.when(core == h)
        def _(pieces=pieces):
            for i, value in enumerate(pieces):
                grads[i * 128 : (i + 1) * 128, :] = value

        @pl.when(core != h)
        def _(pieces=pieces):
            for i, value in enumerate(pieces):
                for b in range(4):
                    first = PACK_GRADS + b * 512 + i * 128
                    packed[first : first + 128, :] = value[:, b * 128 : (b + 1) * 128]


def hidden_back(cot, w_ff, d_hidden, buffer, sems):
    parts = 4
    part = w_ff.shape[1] // parts
    copies = []
    for i in range(parts):
        at = slice(i * part, (i + 1) * part)
        copies.append(pltpu.make_async_copy(w_ff.at[2, at, :], buffer.at[at, :], sems.at[i]))
        copies[-1].start()
    for copy in copies:
        copy.wait()
    for i in range(w_ff.shape[1] // 256):
        at = slice(i * 256, (i + 1) * 256)
        d_hidden[:, at] = nt(cot[...], buffer[at, :])


def half_of(core, g, mine, other):
    lanes = slice((g % 2) * GROUP, (g % 2 + 1) * GROUP)

    def put(at, value):
        @pl.when(core == g // 2)
        def _():
            mine[at, lanes] = value

        @pl.when(core != g // 2)
        def _():
            other[at, lanes] = value

    return put


def encoder_attention_back(
    ids, dhb, w_out, q, k_lo, v_lo, k_a, k_b, v_a, v_b, w_a, w_b, mine, other
):
    d_mixed = nt(dhb[...], w_out[...]).astype(BF)
    for g in range(4):
        lanes = slice(g * GROUP, (g + 1) * GROUP)
        put = half_of(ids[0], g, mine, other)
        put(slice(128, 256), dhb[:, lanes])
        for m, (k_up, v_up, weights) in enumerate(((k_a, v_a, w_a), (k_b, v_b, w_b))):
            rows = slice(m * HD, (m + 1) * HD)
            low_at = slice(m * 256, (m + 1) * 256)
            q_stacked = stack_heads(q[rows, lanes] * BF(SCALE))
            o_stacked = stack_heads(d_mixed[rows, lanes])
            low = [weights[g * 2 + h] for h in range(2)]
            w = [piece.astype(F32) for piece in low]
            dw = [nt(values, o_stacked) for values in (v_lo[low_at, lanes], v_up[:, lanes])]
            inner = sum(jnp.sum(a * b, axis=0, keepdims=True) for a, b in zip(dw, w))
            ds = [(b * (a - inner)).astype(BF) for a, b in zip(dw, w)]
            dq = tn(ds[0], k_lo[low_at, lanes]) + tn(ds[1], k_up[:, lanes])
            put(rows, (unstack_heads(dq) * SCALE).astype(BF))
            for h in range(2):
                base = h * HALF + m * 256
                put(slice(256 + base, 512 + base), nn(ds[h], q_stacked).astype(BF))
                put(slice(1280 + base, 1536 + base), nn(low[h], o_stacked).astype(BF))


def both_columns(core, block, w_qkv):
    return [
        w_qkv.block(block)[:, pl.ds(pl.multiple_of(which * HALF, HALF), HALF)] for which in (core, 1 - core)
    ]


def bytes_back(core, h, m, source, w_qkv, gains, grads):
    d_norm = sum(
        nt(ref[1024 * block - 768 + h * HALF + m * 256 : 1024 * block - 512 + h * HALF + m * 256, :], columns)
        for block in (1, 2)
        for ref, columns in zip(grads, both_columns(core, block, w_qkv))
    )
    back, gain_rows = norm_back(source.astype(F32), gains[1:2], d_norm)
    return back.astype(BF), jnp.sum(gain_rows, axis=0, keepdims=True)


def encoder_upper_back(ids, up_a, up_b, w_qkv, gains, mine, other, up_grad, gain_grad):
    total = jnp.zeros((1, D), F32)
    for m, source in enumerate((up_a, up_b)):
        back, rows = bytes_back(ids[0], 1, m, source[...], w_qkv, gains, (mine, other))
        up_grad[m * 256 : (m + 1) * 256, :] = back
        total = total + rows
    gain_grad[...] = total


def encoder_lower_back(
    ids, dhb, patch, low, w_qkv, gains, mine, other, after, patch_grad, low_grad, gain_grad
):
    core = ids[0]
    up_norm = sum(nt(ref[0:128, :], columns) for ref, columns in zip((mine, other), both_columns(core, 0, w_qkv)))
    back, gain_rows = norm_back(patch[...].astype(F32), gains[0:1], up_norm)
    gain_grad[0:1, :] = jnp.sum(gain_rows, axis=0, keepdims=True)
    patch_grad[...] = dhb[...].astype(F32) + back
    total = jnp.zeros((1, D), F32)
    for m in range(2):
        at = slice(m * 256, (m + 1) * 256)
        back, rows = bytes_back(core, 0, m, low[at, :], w_qkv, gains, (mine, other))
        low_grad[at, :] = back
        total = total + rows
    gain_grad[1:2, :] = total


def turn_encoder(pn, o_a, o_b, bn_lo, bn_a, bn_b, packed):
    for b, rows in enumerate([bn_lo[i * 128 : (i + 1) * 128, :] for i in range(4)]
                             + [ref[i * 128 : (i + 1) * 128, :] for ref in (bn_a, bn_b) for i in range(2)]):
        packed[b * D : (b + 1) * D, :] = rows.T
    packed[PACK_LEFT : PACK_LEFT + D, :] = pn[...].T
    packed[PACK_LEFT + D : PACK_LEFT + 2 * D, :] = jnp.concatenate([o_a[...], o_b[...]], 0).T


def rows_of_both(left, left_far, at):
    return jnp.concatenate([left[at, :], left_far[at, :]], 1)


def below(near, far, rows):
    return jnp.concatenate([near[rows, :], far[rows, :]], 0)


def encoder_weights(ids, packed, packed_far, near, far, after, *blocks):
    u = ids[1]
    queries = below(near, far, slice(0, 128))
    outputs = below(near, far, slice(128, 256))
    for k in range(4):
        first = lax.rem(u + k, 4) * 256

        def at(base, first=first):
            return pl.ds(pl.multiple_of(first + base, 256), 256)

        blocks[k][0] = nn(rows_of_both(packed, packed_far, at(PACK_LEFT)), queries).astype(BF)
        blocks[k][3] = nn(rows_of_both(packed, packed_far, at(PACK_LEFT + D)), outputs).astype(BF)
        lefts = [jnp.concatenate([ref[at(b * D), :] for b in range(8)], 1) for ref in (packed, packed_far)]
        for block in (1, 2):
            rows = slice(1024 * block - 768, 1024 * block + 256)
            blocks[k][block] = (nn(lefts[0], near[rows, :]) + nn(lefts[1], far[rows, :])).astype(BF)


def unpack(packed, first, rows):
    return jnp.concatenate([packed[first + b * rows : first + (b + 1) * rows, :] for b in range(4)], 1)


def latent_weights(ids, packed, packed_far, near, *blocks):
    u = ids[1]
    far = unpack(packed_far, PACK_GRADS, 512)
    rights = [jnp.concatenate([near[i * 128 : (i + 1) * 128, :], far[i * 128 : (i + 1) * 128, :]], 0) for i in range(4)]
    for k in range(4):
        first = PACK_LEFT + lax.rem(u + k, 4) * 256
        at = pl.ds(pl.multiple_of(first, 256), 256)
        low_at = pl.ds(pl.multiple_of(first + D, 256), 256)
        for block, (source, i) in enumerate(((at, 0), (at, 2), (at, 3), (low_at, 1))):
            blocks[k][block] = nn(rows_of_both(packed, packed_far, source), rights[i]).astype(BF)


def ff_weights_grad(ids, packed, packed_far, norms, own, right, left, far_a, far_b):
    core, u = ids[0], ids[1]
    share = UNITS // 16
    far = unpack(packed_far, PACK_NORMS, 256)
    normed = jnp.concatenate([norms[0:128, :], far[0:128, :]], 0)
    cot = jnp.concatenate([norms[128:256, :], far[128:256, :]], 0)
    for k in range(4):
        there = lax.rem(u + k, 4)
        for v in range(4):
            chunk = jnp.where(core == 0, there * 4 + v, v * 4 + there)
            for j in range(3):
                at = pl.ds(pl.multiple_of(j * UNITS + chunk * share, 16), share)
                value = nn(rows_of_both(packed, packed_far, at), normed if j < 2 else cot).astype(BF)
                rows = slice(j * share, (j + 1) * share)
                if k == 2:
                    far_a[v, rows, :] = value[:, :GROUP]
                    far_b[v, rows, :] = value[:, GROUP:]
                else:
                    (own, right, None, left)[k][v, rows, :] = value


def ff_add(right, left, from_left, from_right, after, new_right, new_left):
    new_right[:, :, 0:GROUP] = (right[:, :, 0:GROUP].astype(F32) + from_left[...].astype(F32)).astype(BF)
    new_right[:, :, GROUP:] = right[:, :, GROUP:]
    new_left[:, :, 0:GROUP] = left[:, :, 0:GROUP]
    new_left[:, :, GROUP:] = (left[:, :, GROUP:].astype(F32) + from_right[...].astype(F32)).astype(BF)


def sum_four(own, a, b, c):
    return own.astype(F32) + a.astype(F32) + b.astype(F32) + c.astype(F32)


def pack_gain(value):
    high = value.astype(BF)
    low = (value - high.astype(F32)).astype(BF)
    return jnp.concatenate(
        [high.astype(F32), low.astype(F32), jnp.zeros((8, HALF), F32)], 0
    ).astype(BF)


def unpack_gain(rows):
    rows = rows.astype(F32)
    return rows[0:4] + rows[4:8]


GAIN_AT = slice(256, 272)


def attn_sum_first(ids, own, a, b, c, *outs):
    v = ids[2]
    for k in range(4):
        at = pl.ds(pl.multiple_of(lax.rem(v + k, 4) * HD, HD), HD)
        for block in range(4):
            outs[k][block * HD : (block + 1) * HD, :] = sum_four(
                own[block, at, :], a[block, at, :], b[block, at, :], c[block, at, :]
            ).astype(BF)


def attn_sum_first_gain(ids, own, a, b, c, enc_gain, up_gain, lat_gain, *outs):
    attn_sum_first(ids, own, a, b, c, *outs)
    first = ids[4] == 0
    gain = jnp.where(
        first, jnp.concatenate([enc_gain[0:1, :], enc_gain[1:2, :] + up_gain[...]], 0), lat_gain[...]
    )
    halves = [gain[i : i + 1, h * HALF : (h + 1) * HALF] for i in range(2) for h in range(2)]
    packed = pack_gain(jnp.concatenate(halves, 0))
    for out in outs:
        out[GAIN_AT, :] = packed


def sum_all(*refs):
    refs, out = refs[:-1], refs[-1]
    out[0:256, :] = sum(ref[0:256, :].astype(F32) for ref in refs).astype(BF)
    out[GAIN_AT, :] = pack_gain(sum(unpack_gain(ref[GAIN_AT, :]) for ref in refs))


def stack_rows(*refs):
    refs, out = refs[:-1], refs[-1]
    for j, ref in enumerate(refs):
        out[j * 256 : (j + 1) * 256, :] = ref[0:256, :]
    out[1024:1040, :] = refs[0][GAIN_AT, :]


def ff_sum_first(ids, own, a, b, *outs):
    v = ids[2]
    for k in range(4):
        at = lax.rem(v + k, 4)
        outs[k][...] = (own[at].astype(F32) + a[at].astype(F32) + b[at].astype(F32)).astype(BF)


def ff_sum_second(own, a, b, c, out):
    out[...] = sum_four(own[...], a[...], b[...], c[...]).astype(BF)


def final_attn(ids, *refs):
    pieces, (qkv, out, gain) = refs[:8], refs[8:]
    step = pl.program_id(0)
    for side in range(2):
        core = ids[0] if side == 0 else 1 - ids[0]
        u = ids[1] if side == 0 else ids[2]
        v = ids[2] if side == 0 else ids[1]
        for k in range(4):
            piece = pieces[side * 4 + k]

            @pl.when(lax.rem(u + k, 4) == step)
            def _(piece=piece, v=v, core=core):
                for j in range(4):
                    at = pl.ds(pl.multiple_of(lax.rem(v + j, 4) * HD, HD), HD)
                    for block in range(4):
                        target, column = (qkv, block * D) if block < 3 else (out, 0)
                        lanes = pl.ds(pl.multiple_of(core * HALF + column, HALF), HALF)
                        first = j * 256 + block * HD
                        target[at, lanes] = piece[first : first + HD, :].astype(F32)

    mine = sum(unpack_gain(piece[1024:1040, :]) for piece in pieces[:4])
    other = sum(unpack_gain(piece[1024:1040, :]) for piece in pieces[4:])
    total = mine + other
    for i in range(2):
        for h in range(2):
            gain[i : i + 1, h * HALF : (h + 1) * HALF] = total[2 * i + h : 2 * i + h + 1, :]


SMEM = pltpu.MemorySpace.SMEM
VMEM = pltpu.MemorySpace.VMEM


def size(shape, dtype):
    return math.prod(shape) * jnp.dtype(dtype).itemsize


class Arriving:
    def __init__(self, copy, buffer):
        self.copy, self.buffer, self.here = copy, buffer, False

    def ready(self):
        if not self.here:
            self.copy.wait()
            self.here = True
        return self.buffer

    def __getitem__(self, index):
        return self.ready()[index]


class ArrivingBlocks:
    def __init__(self, blocks):
        self.blocks = blocks

    def block(self, j):
        return self.blocks[j]


def fetching(kernel, n_args, n_outs, plan):
    def wrapped(*refs):
        args, outs, rest = list(refs[:n_args]), refs[n_args : n_args + n_outs], refs[n_args + n_outs :]
        scratch, buffers, sems = rest[: len(rest) - len(plan) - 1], rest[len(rest) - len(plan) - 1 : -1], rest[-1]
        arriving = []
        blocks = {}
        for i, (a, j) in enumerate(plan):
            source = refs[a] if j is None else refs[a].at[:, j * D : (j + 1) * D]
            copy = pltpu.make_async_copy(source, buffers[i], sems.at[i])
            copy.start()
            arriving.append(Arriving(copy, buffers[i]))
            if j is None:
                args[a] = arriving[-1]
            else:
                blocks.setdefault(a, {})[j] = arriving[-1]
        for a, found in blocks.items():
            args[a] = ArrivingBlocks(found)
        kernel(*args, *outs, *scratch)
        for value in arriving:
            value.ready()

    return wrapped


def call(kernel, args, outs, scratch=(), spaces=None, spare=6, fetch=()):
    spaces = dict(spaces or {})
    scratch = list(scratch)
    plan = [f if isinstance(f, tuple) else (f, None) for f in fetch]
    if plan:
        for a, j in plan:
            spaces[a] = pl.ANY
            shape = args[a].shape if j is None else (args[a].shape[0], D)
            scratch.append(pltpu.VMEM(shape, args[a].dtype))
        scratch.append(pltpu.SemaphoreType.DMA((len(plan),)))
        kernel = fetching(kernel, len(args), len(outs), plan)
    vmem = sum(size(a.shape, a.dtype) for i, a in enumerate(args) if i not in spaces)
    vmem += sum(size(*o) for o in outs)
    vmem += sum(size(s.shape, s.dtype) for s in scratch if hasattr(s, "shape") and s.memory_space == VMEM)
    specs = [pl.BlockSpec(memory_space=spaces.get(i, VMEM)) for i in range(len(args))]
    return pl.pallas_call(
        kernel,
        out_shape=[jax.ShapeDtypeStruct(s, t) for s, t in outs],
        in_specs=specs,
        out_specs=[pl.BlockSpec(memory_space=VMEM) for _ in outs],
        scratch_shapes=scratch,
        compiler_params=pltpu.CompilerParams(vmem_limit_bytes=vmem + spare * 1024 * 1024),
    )(*args)


def nothing(outs):
    def kernel(*refs):
        pass

    return pl.pallas_call(
        kernel,
        out_shape=[jax.ShapeDtypeStruct(s, t) for s, t in outs],
        out_specs=[pl.BlockSpec(memory_space=pl.ANY) for _ in outs],
    )()


def on_section(flag, kernel, args, outs, **rest):
    return lax.cond(
        flag, lambda: call(kernel, args, outs, **rest), lambda: nothing(outs)
    )


def along(value, by):
    return lax.ppermute(value, "s", [(0, 1)] if by > 0 else [(1, 0)])


def swap(value, axis, sections=(0, 1)):
    pairs = [(s * 2 + i, s * 2 + 1 - i) for s in sections for i in range(2)]
    return lax.ppermute(value, ("s", axis), pairs)


def plane_shift(value, which, by, sections=(0, 1)):
    pairs = []
    for s in sections:
        for y in range(4):
            for x in range(4):
                for core in range(2):
                    ty, tx = ((y + by) % 4, x) if core == which else (y, (x + by) % 4)
                    pairs.append((((s * 4 + y) * 4 + x) * 2 + core, ((s * 4 + ty) * 4 + tx) * 2 + core))
    return lax.ppermute(value, ("s", "y", "x", "core"), pairs)


def exchange(blocks, which, sections=(0, 1)):
    return [plane_shift(blocks[k], which, k, sections) for k in (1, 2, 3)]


def collect(block, which):
    return [block] + [plane_shift(block, which, -k) for k in (1, 2, 3)]


def pick(stack, index, dim):
    return lax.dynamic_index_in_dim(stack, index, dim, keepdims=False)


def shards(patch_io, byte_states, patch_lengths, patch_live, attn_qkv, attn_out, gains, ff_weights):
    section = lax.axis_index("s")
    core = lax.axis_index("core")
    zh = lax.axis_index("zh")
    y, x = lax.axis_index("y"), lax.axis_index("x")
    first = section == 0
    second = section == 1
    ids = jnp.stack([core, jnp.where(core == 0, y, x), jnp.where(core == 0, x, y), zh, section])
    ids = ids.astype(jnp.int32)
    w_qkv = attn_qkv[0]
    w_out = attn_out[0]
    gain_pair = gains[0]
    micro, seq = patch_io.shape[1], patch_io.shape[3]
    half_bytes = byte_states.shape[2]
    units = ff_weights.shape[0]
    rows = micro * seq
    own_rows = patch_io.reshape(rows, D)
    up_a = along(byte_states[0, 0], -1)
    up_b = along(byte_states[1, 0], -1)
    lower = byte_states.reshape(micro * half_bytes, D)
    w_ff = jnp.swapaxes(ff_weights, 0, 1)
    lengths = patch_lengths[:, 0]
    live = patch_live[:, 0]
    ends = jnp.cumsum(lengths, axis=1)
    bounds = jnp.tile(jnp.stack([ends - lengths, ends], 1), (1, 1, 4))
    places = lax.iota(jnp.int32, seq)
    causal = places[:, None] <= places[None, :]
    diagonal = places[:, None] == places[None, :]
    allowed = causal[None] & ((live[:, :, None] == 1) | diagonal[None])
    allowed = lax.optimization_barrier(jnp.tile(allowed.astype(F32), (1, 1, 4)))

    wide = ((rows, D), BF)
    short = ((seq, D), BF)
    tall = ((micro * half_bytes, D), BF)
    piece = ((half_bytes, D), BF)
    (d_hidden,) = on_section(
        second,
        hidden_back,
        (own_rows, w_ff),
        [((rows, units), F32)],
        spaces={1: pl.ANY},
        scratch=[pltpu.VMEM((units, D), BF), pltpu.SemaphoreType.DMA((4,))],
    )
    pn, q, bn_lo, k_lo, v_lo = on_section(
        first,
        encode_lower,
        (own_rows, lower, w_qkv, gain_pair),
        [wide, wide, tall, tall, tall],
        fetch=((2, 0), 1, (2, 1), (2, 2)),
    )
    rest = []
    for m, up in enumerate((up_a, up_b)):
        rest.append(
            on_section(
                first,
                functools.partial(encode_rest, m),
                (own_rows, up, w_qkv, w_out, gain_pair, bounds, q, k_lo, v_lo),
                [short, short, ((8, 256, GROUP), BF), piece, piece, piece],
                fetch=((2, 1), (2, 2), 7, 8, 3),
            )
        )
    (hb_a, o_a, w_a, bn_a, k_a, v_a), (hb_b, o_b, w_b, bn_b, k_b, v_b) = rest
    arrived = [along(hb_a, 1), along(hb_b, 1)]

    latent_outs = [
        ((rows, D), F32), wide, ((2, D), F32), ((256, HALF), BF), ((512, HALF), BF), ((PACK_ROWS, rows), BF),
    ]

    def latent():
        return call(
            latent_layer,
            (ids, *arrived, own_rows, allowed, w_qkv, w_out, gain_pair, w_ff, d_hidden),
            latent_outs,
            spaces={0: SMEM, 8: pl.ANY},
            fetch=((5, 0), (5, 1), (5, 2), 6),
            scratch=[
                pltpu.VMEM((rows, 3 * D), BF),
                pltpu.VMEM((8, HD, GROUP), BF),
                pltpu.VMEM((rows, D), BF),
                pltpu.VMEM((3, units, D), BF),
                pltpu.VMEM((rows, D), F32),
                pltpu.VMEM((rows, D), F32),
                pltpu.VMEM((rows, 3 * D), BF),
                pltpu.SemaphoreType.DMA((4,)),
            ],
        )

    def turn():
        return nothing(latent_outs[:5]) + call(
            turn_encoder, (pn, o_a, o_b, bn_lo, bn_a, bn_b), latent_outs[5:]
        )

    latents, dhb, latent_gain, norms, lat_grads, packed = lax.cond(second, latent, turn)
    returned = along(dhb, -1)

    packed_far = swap(packed, "core")

    share = units // 16
    ff_block = ((4, 3 * share, HALF), BF)
    ff_half = ((4, 3 * share, GROUP), BF)
    ff_own, ff_right, ff_left, ff_far_a, ff_far_b = on_section(
        second,
        ff_weights_grad,
        (ids, packed, packed_far, norms),
        [ff_block, ff_block, ff_block, ff_half, ff_half],
        spaces={0: SMEM},
    )

    grads_long = ((2304, HALF), BF)
    enc_grads, enc_other = on_section(
        first,
        encoder_attention_back,
        (ids, returned, w_out, q, k_lo, v_lo, k_a, k_b, v_a, v_b, w_a, w_b),
        [grads_long, grads_long],
        spaces={0: SMEM},
        fetch=(2, 5, 8, 10, 4, 6, 9, 11, 7),
    )
    enc_far = swap(enc_other, "core", (0,))
    up_grad, up_gain = on_section(
        first,
        encoder_upper_back,
        (ids, up_a, up_b, w_qkv, gain_pair, enc_grads, enc_other),
        [tall, ((1, D), F32)],
        spaces={0: SMEM},
        fetch=(5, (3, 1), 6, (3, 2), 1, 2),
    )
    up_arrived = along(up_grad, 1)
    ff_far_a, ff_far_b, up_gain = lax.optimization_barrier((ff_far_a, ff_far_b, up_gain))
    from_left = plane_shift(ff_far_a, 0, 1)
    from_right = plane_shift(ff_far_b, 0, -1)
    outs = [((4, 256, HALF), BF)] * 4
    blocks = lax.cond(
        first,
        lambda: call(
            encoder_weights,
            (ids, packed, packed_far, enc_grads, enc_far, up_gain),
            outs,
            spaces={0: SMEM, 5: pl.ANY},
            fetch=(3, 4, 1, 2),
        ),
        lambda: call(latent_weights, (ids, packed, packed_far, lat_grads), outs, spaces={0: SMEM}),
    )
    last, from_left, from_right = lax.optimization_barrier((blocks[3], from_left, from_right))
    blocks = [*blocks[:3], last]
    got, up_arrived = lax.optimization_barrier((exchange(blocks, 0), up_arrived))
    low_outs = [((rows, D), F32), tall, ((2, D), F32)]

    def lower_grads():
        parts = call(
            encoder_lower_back,
            (ids, returned, own_rows, lower, w_qkv, gain_pair, enc_grads, enc_other, blocks[0]),
            low_outs,
            spaces={0: SMEM, 8: pl.ANY},
            fetch=(6, 7, (4, 0), (4, 1), (4, 2), 3),
        )
        return (*parts, *nothing([ff_block, ff_block]))

    def ff_middle():
        added = call(
            ff_add, (ff_right, ff_left, from_left, from_right, blocks[0]), [ff_block, ff_block], spaces={4: pl.ANY}
        )
        return (*nothing(low_outs), *added)

    patch_grad, low_grad, encoder_gain, ff_right_sum, ff_left_sum = lax.cond(first, lower_grads, ff_middle)
    line = [((272, HALF), BF)]
    blocks = call(
        attn_sum_first_gain,
        (ids, blocks[0], *got, encoder_gain, up_gain, latent_gain),
        line * 4,
        spaces={0: SMEM},
    )
    ff_right_sum, ff_left_sum, _ = lax.optimization_barrier((ff_right_sum, ff_left_sum, blocks))
    from_left = plane_shift(ff_right_sum, 0, 1, (1,))
    from_right = plane_shift(ff_left_sum, 0, -1, (1,))
    (block,) = call(sum_all, (blocks[0], *exchange(blocks, 1)), line)
    byte_grad = jnp.where(first, low_grad, up_arrived)
    patch_out = jnp.where(first, patch_grad, latents)
    from_left, from_right, block, byte_grad, patch_out = lax.optimization_barrier(
        (from_left, from_right, block, byte_grad, patch_out)
    )
    ff_line = ((3 * share, HALF), BF)
    ff_blocks = on_section(
        second, ff_sum_first, (ids, ff_own, from_left, from_right), [ff_line] * 4, spaces={0: SMEM}
    )
    ff_got = exchange(ff_blocks, 1)
    across, ff_got = lax.optimization_barrier((swap(block, "zh"), ff_got))
    (block,) = call(sum_all, (block, across), line)
    (block,) = call(stack_rows, collect(block, 1), [((1040, HALF), BF)])
    pieces = collect(block, 0)
    own_far = swap(block, "core")
    (ff_sum,) = on_section(second, ff_sum_second, (ff_blocks[0], *ff_got), [ff_line])
    ff_sum = ff_sum.reshape(3, 2, share // 2, HALF)
    ff_far = swap(pick(ff_sum, 1 - zh, 1), "zh")
    ff_sum = (pick(ff_sum, zh, 1).astype(F32) + ff_far.astype(F32)).astype(BF).reshape(3, 2, share // 4, HALF)
    ff_mine = pick(ff_sum, core, 1)
    ff_far = swap(pick(ff_sum, 1 - core, 1), "core")

    def ff_result():
        low, high = jnp.where(core == 0, ff_mine, ff_far), jnp.where(core == 0, ff_far, ff_mine)
        return jnp.swapaxes(jnp.concatenate([low, high], 2), 0, 1).astype(F32)

    ff_grad = lax.cond(second, ff_result, lambda: jnp.zeros((share // 4, 3, D), F32))
    ff_grad, *pieces = lax.optimization_barrier((ff_grad, *pieces))
    pieces = pieces + [own_far] + [swap(p, "core") for p in pieces[1:]]
    whole = lambda p: pl.BlockSpec(p.shape, lambda i, n=p.ndim: (0,) * n)
    total_qkv, total_out, total_gain = pl.pallas_call(
        final_attn,
        grid=(4,),
        out_shape=[
            jax.ShapeDtypeStruct((D, 3 * D), F32),
            jax.ShapeDtypeStruct((D, D), F32),
            jax.ShapeDtypeStruct((2, D), F32),
        ],
        in_specs=[pl.BlockSpec(memory_space=SMEM)] + [whole(p) for p in pieces],
        out_specs=[
            pl.BlockSpec((256, 3 * D), lambda i: (i, 0)),
            pl.BlockSpec((256, D), lambda i: (i, 0)),
            pl.BlockSpec((2, D), lambda i: (0, 0)),
        ],
        compiler_params=pltpu.CompilerParams(vmem_limit_bytes=FINAL_VMEM),
    )(ids, *pieces)
    return (
        patch_out.reshape(1, micro, 1, seq, D),
        byte_grad.reshape(micro, 1, half_bytes, D),
        total_qkv[None],
        total_out[None],
        total_gain[None],
        ff_grad[None],
    )


def solution(mesh):
    fine = Mesh(mesh.devices.reshape(2, 4, 4, 2, 2), ("s",) + BATCH)
    in_specs = (
        P("s", None, BATCH, None, None),
        P(None, BATCH, "s", None),
        P(None, BATCH, None),
        P(None, BATCH, None),
        P("s", None, None),
        P("s", None, None),
        P("s", None, None),
        P(),
    )
    out_specs = (
        P("s", None, BATCH, None, None),
        P(None, BATCH, "s", None),
        P("s", None, None),
        P("s", None, None),
        P("s", None, None),
        P("s", BATCH, None, None),
    )
    return jax.shard_map(shards, mesh=fine, in_specs=in_specs, out_specs=out_specs, check_vma=False)
```

```python
import functools
import math

import jax
import jax.numpy as jnp
from jax import lax
from jax.experimental import pallas as pl
from jax.experimental.pallas import tpu as pltpu
from jax.sharding import Mesh
from jax.sharding import PartitionSpec as P

HD = 64
SCALE = HD**-0.5
EPS = 1e-05
NEG = -1e30
BATCH = ("y", "x", "zh", "core")
BF = jnp.bfloat16
F32 = jnp.float32
D = 1024
HALF = 512
GROUP = 256
FINAL_VMEM = 32 * 1024 * 1024


UNITS = 2816
PACK_NORMS = 3 * UNITS
PACK_LEFT = PACK_NORMS + 4 * 256
PACK_GRADS = PACK_LEFT + 2 * D
PACK_ROWS = PACK_GRADS + 4 * 512


def nn(a, b):
    return lax.dot_general(a, b, (((1,), (0,)), ((), ())), preferred_element_type=F32)


def nt(a, b):
    return lax.dot_general(a, b, (((1,), (1,)), ((), ())), preferred_element_type=F32)


def tn(a, b):
    return lax.dot_general(a, b, (((0,), (0,)), ((), ())), preferred_element_type=F32)


def inverse_rms(x):
    return lax.rsqrt(jnp.mean(x * x, axis=-1, keepdims=True) + EPS)


def norm_back(x, gain, up):
    r = inverse_rms(x)
    scaled = up * gain
    inner = jnp.mean(scaled * x, axis=-1, keepdims=True)
    return r * (scaled - x * (r * r * inner)), up * (x * r)


def stack_heads(rows):
    head = lax.broadcasted_iota(jnp.int32, rows.shape, 1) // HD
    return jnp.concatenate([jnp.where(head == h, rows, jnp.zeros_like(rows)) for h in range(4)], 0)


def unstack_heads(stacked):
    head = lax.broadcasted_iota(jnp.int32, (HD, GROUP), 1) // HD
    out = stacked[0:HD]
    for h in range(1, 4):
        out = jnp.where(head == h, stacked[h * HD : (h + 1) * HD], out)
    return out


def softmax_columns(scores):
    top = functools.reduce(jnp.maximum, [jnp.max(s, axis=0, keepdims=True) for s in scores])
    parts = [jnp.exp(s - top) for s in scores]
    inverse = 1.0 / sum(jnp.sum(p, axis=0, keepdims=True) for p in parts)
    return [(p * inverse).astype(BF) for p in parts]


def encode_lower(patch, low, w_qkv, gains, pn, q, bn, k, v):
    x = patch[...].astype(F32)
    normed = (x * inverse_rms(x) * gains[0:1]).astype(BF)
    pn[...] = normed
    q[...] = nn(normed, w_qkv.block(0)[...]).astype(BF)
    for i in range(2):
        at = pl.ds(i * 256, 256)
        b = low[at, :].astype(F32)
        normed = (b * inverse_rms(b) * gains[1:2]).astype(BF)
        bn[at, :] = normed
        k[at, :] = nn(normed, w_qkv.block(1)[...]).astype(BF)
        v[at, :] = nn(normed, w_qkv.block(2)[...]).astype(BF)


def encode_rest(m, patch, up, w_qkv, w_out, gains, bounds, q, k_lo, v_lo, hb, o1, weights, bn, k, v):
    b = up[...].astype(F32)
    normed = (b * inverse_rms(b) * gains[1:2]).astype(BF)
    bn[...] = normed
    k[...] = nn(normed, w_qkv.block(1)[...]).astype(BF)
    v[...] = nn(normed, w_qkv.block(2)[...]).astype(BF)
    spot = lax.broadcasted_iota(jnp.int32, (256, GROUP), 0)
    start = bounds[m, 0:1, :]
    end = bounds[m, 1:2, :]
    inside = [(spot + h * 256 >= start) & (spot + h * 256 < end) for h in range(2)]
    low_at = slice(m * 256, (m + 1) * 256)
    rows = slice(m * HD, (m + 1) * HD)
    for g in range(4):
        lanes = slice(g * GROUP, (g + 1) * GROUP)
        stacked = stack_heads(q[rows, lanes] * BF(SCALE))
        scores = [
            jnp.where(inside[h], nt(keys, stacked), NEG)
            for h, keys in enumerate((k_lo[low_at, lanes], k[:, lanes]))
        ]
        w = softmax_columns(scores)
        weights[g * 2] = w[0]
        weights[g * 2 + 1] = w[1]
        mixed = tn(w[0], v_lo[low_at, lanes]) + tn(w[1], v[:, lanes])
        o1[:, lanes] = unstack_heads(mixed).astype(BF)
    hb[...] = (patch[rows, :].astype(F32) + nn(o1[...], w_out[...])).astype(BF)


def latent_layer(
    ids, hb_a, hb_b, cot, allowed, w_qkv, w_out, gains, w_ff, d_hidden,
    latents, dhb, gain_grad, norms, grads, packed,
    qkv, weights, o2, ff_buf, acc_out, acc_norm, dqkv, sems,
):
    core = ids[0]
    units = w_ff.shape[1]
    step = 256
    parts = 4
    part = units // parts

    fetches = []
    for i in range(parts):
        at = slice(i * part, (i + 1) * part)
        fetches.append(pltpu.make_async_copy(w_ff.at[:, at, :], ff_buf.at[:, at, :], sems.at[i]))
        fetches[-1].start()
    x = jnp.concatenate([hb_a[...], hb_b[...]], 0).astype(F32)
    normed = (x * inverse_rms(x) * gains[0:1]).astype(BF)
    packed[PACK_LEFT : PACK_LEFT + D, :] = normed.T
    for j in range(3):
        qkv[:, j * D : (j + 1) * D] = nn(normed, w_qkv.block(j)[...]).astype(BF)
    for m in range(2):
        rows = slice(m * HD, (m + 1) * HD)
        for g in range(4):
            lanes = slice(g * GROUP, (g + 1) * GROUP)
            k_lanes = slice(D + g * GROUP, D + (g + 1) * GROUP)
            v_lanes = slice(2 * D + g * GROUP, 2 * D + (g + 1) * GROUP)
            stacked = stack_heads(qkv[rows, lanes] * BF(SCALE))
            scores = jnp.where(allowed[m] > 0.5, nt(qkv[rows, k_lanes], stacked), NEG)
            (w,) = softmax_columns([scores])
            weights[m * 4 + g] = w
            o2[rows, lanes] = unstack_heads(tn(w, qkv[rows, v_lanes])).astype(BF)
    packed[PACK_LEFT + D : PACK_LEFT + 2 * D, :] = o2[...].T
    after = x + nn(o2[...], w_out[...])
    yn = (after * inverse_rms(after) * gains[1:2]).astype(BF)
    c = cot[...]
    for h in range(2):

        @pl.when(core == h)
        def _(h=h):
            norms[0:128, :] = yn[:, h * HALF : (h + 1) * HALF]
            norms[128:256, :] = c[:, h * HALF : (h + 1) * HALF]

        @pl.when(core != h)
        def _(h=h):
            for b in range(4):
                lanes = slice(h * HALF + b * 128, h * HALF + (b + 1) * 128)
                packed[PACK_NORMS + b * 256 : PACK_NORMS + b * 256 + 128, :] = yn[:, lanes]
                packed[PACK_NORMS + b * 256 + 128 : PACK_NORMS + (b + 1) * 256, :] = c[:, lanes]

    for copy in fetches:
        copy.wait()
    acc_out[...] = after
    for i in range(units // step):
        at = slice(i * step, (i + 1) * step)
        gate = nt(yn, ff_buf[0, at, :])
        upward = nt(yn, ff_buf[1, at, :])
        du = d_hidden[:, at]
        sig = 1.0 / (1.0 + jnp.exp(-gate))
        active = gate * sig
        hidden = (active * upward).astype(BF)
        d_gate = (du * upward * (sig * (1.0 + gate * (1.0 - sig)))).astype(BF)
        d_up = (du * active).astype(BF)
        for j, value in enumerate((d_gate, d_up, hidden)):
            packed[i * step + j * units : (i + 1) * step + j * units, :] = value.T
        acc_out[...] += nn(hidden, ff_buf[2, at, :])
        back = nn(d_gate, ff_buf[0, at, :]) + nn(d_up, ff_buf[1, at, :])
        if i == 0:
            acc_norm[...] = back
        else:
            acc_norm[...] += back
    latents[...] = acc_out[...]
    back, gain_rows = norm_back(after, gains[1:2], acc_norm[...])
    gain_grad[1:2, :] = jnp.sum(gain_rows, axis=0, keepdims=True)
    d_after = c.astype(F32) + back
    da = d_after.astype(BF)
    d_mixed = nt(da, w_out[...]).astype(BF)
    for m in range(2):
        rows = slice(m * HD, (m + 1) * HD)
        for g in range(4):
            lanes = slice(g * GROUP, (g + 1) * GROUP)
            k_lanes = slice(D + g * GROUP, D + (g + 1) * GROUP)
            v_lanes = slice(2 * D + g * GROUP, 2 * D + (g + 1) * GROUP)
            q_stacked = stack_heads(qkv[rows, lanes] * BF(SCALE))
            o_stacked = stack_heads(d_mixed[rows, lanes])
            w_low = weights[m * 4 + g]
            w = w_low.astype(F32)
            dw = nt(qkv[rows, v_lanes], o_stacked)
            inner = jnp.sum(dw * w, axis=0, keepdims=True)
            ds = (w * (dw - inner)).astype(BF)
            dqkv[rows, lanes] = (unstack_heads(tn(ds, qkv[rows, k_lanes])) * SCALE).astype(BF)
            dqkv[rows, k_lanes] = nn(ds, q_stacked).astype(BF)
            dqkv[rows, v_lanes] = nn(w_low, o_stacked).astype(BF)
    d_normed = sum(nt(dqkv[:, j * D : (j + 1) * D], w_qkv.block(j)[...]) for j in range(3))
    back, gain_rows = norm_back(x, gains[0:1], d_normed)
    gain_grad[0:1, :] = jnp.sum(gain_rows, axis=0, keepdims=True)
    dhb[...] = (d_after + back).astype(BF)
    for h in range(2):
        pieces = (
            dqkv[:, h * HALF : (h + 1) * HALF],
            da[:, h * HALF : (h + 1) * HALF],
            dqkv[:, D + h * HALF : D + (h + 1) * HALF],
            dqkv[:, 2 * D + h * HALF : 2 * D + (h + 1) * HALF],
        )

        @pl.when(core == h)
        def _(pieces=pieces):
            for i, value in enumerate(pieces):
                grads[i * 128 : (i + 1) * 128, :] = value

        @pl.when(core != h)
        def _(pieces=pieces):
            for i, value in enumerate(pieces):
                for b in range(4):
                    first = PACK_GRADS + b * 512 + i * 128
                    packed[first : first + 128, :] = value[:, b * 128 : (b + 1) * 128]


def hidden_back(cot, w_ff, d_hidden, buffer, sems):
    parts = 4
    part = w_ff.shape[1] // parts
    copies = []
    for i in range(parts):
        at = slice(i * part, (i + 1) * part)
        copies.append(pltpu.make_async_copy(w_ff.at[2, at, :], buffer.at[at, :], sems.at[i]))
        copies[-1].start()
    for copy in copies:
        copy.wait()
    for i in range(w_ff.shape[1] // 256):
        at = slice(i * 256, (i + 1) * 256)
        d_hidden[:, at] = nt(cot[...], buffer[at, :])


def encoder_attention_back(
    ids, dhb, w_out, q, k_lo, v_lo, k_a, k_b, v_a, v_b, w_a, w_b, mine, other, both, sems
):
    d_mixed = nt(dhb[...], w_out[...]).astype(BF)
    for g in range(4):
        lanes = slice(g * GROUP, (g + 1) * GROUP)
        out_lanes = slice((g % 2) * GROUP, (g % 2 + 1) * GROUP)
        half = jnp.where(ids[0] == g // 2, 0, 1)

        def put(at, value, half=half, out_lanes=out_lanes):
            both[half, at, out_lanes] = value

        put(slice(128, 256), dhb[:, lanes])
        for m, (k_up, v_up, weights) in enumerate(((k_a, v_a, w_a), (k_b, v_b, w_b))):
            rows = slice(m * HD, (m + 1) * HD)
            low_at = slice(m * 256, (m + 1) * 256)
            q_stacked = stack_heads(q[rows, lanes] * BF(SCALE))
            o_stacked = stack_heads(d_mixed[rows, lanes])
            low = [weights[g * 2 + h] for h in range(2)]
            w = [piece.astype(F32) for piece in low]
            dw = [nt(values, o_stacked) for values in (v_lo[low_at, lanes], v_up[:, lanes])]
            inner = sum(jnp.sum(a * b, axis=0, keepdims=True) for a, b in zip(dw, w))
            ds = [(b * (a - inner)).astype(BF) for a, b in zip(dw, w)]
            dq = tn(ds[0], k_lo[low_at, lanes]) + tn(ds[1], k_up[:, lanes])
            put(rows, (unstack_heads(dq) * SCALE).astype(BF))
            for h in range(2):
                base = h * HALF + m * 256
                put(slice(256 + base, 512 + base), nn(ds[h], q_stacked).astype(BF))
                put(slice(1280 + base, 1536 + base), nn(low[h], o_stacked).astype(BF))
    copies = [pltpu.make_async_copy(both.at[i], out, sems.at[i]) for i, out in enumerate((mine, other))]
    for copy in copies:
        copy.start()
    for copy in copies:
        copy.wait()


def both_columns(core, block, w_qkv):
    return [
        w_qkv.block(block)[:, pl.ds(pl.multiple_of(which * HALF, HALF), HALF)] for which in (core, 1 - core)
    ]


def bytes_back(core, h, source, w_qkv, gains, grads):
    d_norm = sum(
        nt(ref[1024 * block - 768 + h * HALF : 1024 * block - 256 + h * HALF, :], columns)
        for block in (1, 2)
        for ref, columns in zip(grads, both_columns(core, block, w_qkv))
    )
    back, gain_rows = norm_back(source.astype(F32), gains[1:2], d_norm)
    return back.astype(BF), jnp.sum(gain_rows, axis=0, keepdims=True)


def encoder_upper_back(ids, up_a, up_b, w_qkv, gains, mine, other, up_grad, gain_grad):
    source = jnp.concatenate([up_a[...], up_b[...]], 0)
    back, rows = bytes_back(ids[0], 1, source, w_qkv, gains, (mine, other))
    up_grad[...] = back
    gain_grad[...] = rows


def encoder_lower_back(
    ids, dhb, patch, low, w_qkv, gains, mine, other, after, patch_grad, low_grad, gain_grad
):
    core = ids[0]
    up_norm = sum(nt(ref[0:128, :], columns) for ref, columns in zip((mine, other), both_columns(core, 0, w_qkv)))
    back, gain_rows = norm_back(patch[...].astype(F32), gains[0:1], up_norm)
    gain_grad[0:1, :] = jnp.sum(gain_rows, axis=0, keepdims=True)
    patch_grad[...] = dhb[...].astype(F32) + back
    back, rows = bytes_back(core, 0, low[...], w_qkv, gains, (mine, other))
    low_grad[...] = back
    gain_grad[1:2, :] = rows


def turn_encoder(pn, o_a, o_b, bn_lo, bn_a, bn_b, packed):
    for b, rows in enumerate([bn_lo[i * 128 : (i + 1) * 128, :] for i in range(4)]
                             + [ref[i * 128 : (i + 1) * 128, :] for ref in (bn_a, bn_b) for i in range(2)]):
        packed[b * D : (b + 1) * D, :] = rows.T
    packed[PACK_LEFT : PACK_LEFT + D, :] = pn[...].T
    packed[PACK_LEFT + D : PACK_LEFT + 2 * D, :] = jnp.concatenate([o_a[...], o_b[...]], 0).T


def rows_of_both(left, left_far, at):
    return jnp.concatenate([left[at, :], left_far[at, :]], 1)


def below(near, far, rows):
    return jnp.concatenate([near[rows, :], far[rows, :]], 0)


def encoder_weights(ids, packed, packed_far, near, far, after, *blocks):
    u = ids[1]
    queries = below(near, far, slice(0, 128))
    outputs = below(near, far, slice(128, 256))
    for k in range(4):
        first = lax.rem(u + k, 4) * 256

        def at(base, first=first):
            return pl.ds(pl.multiple_of(first + base, 256), 256)

        blocks[k][0] = nn(rows_of_both(packed, packed_far, at(PACK_LEFT)), queries).astype(BF)
        blocks[k][3] = nn(rows_of_both(packed, packed_far, at(PACK_LEFT + D)), outputs).astype(BF)
        lefts = [jnp.concatenate([ref[at(b * D), :] for b in range(8)], 1) for ref in (packed, packed_far)]
        for block in (1, 2):
            rows = slice(1024 * block - 768, 1024 * block + 256)
            blocks[k][block] = (nn(lefts[0], near[rows, :]) + nn(lefts[1], far[rows, :])).astype(BF)


def unpack(packed, first, rows):
    return jnp.concatenate([packed[first + b * rows : first + (b + 1) * rows, :] for b in range(4)], 1)


def latent_weights(ids, packed, packed_far, near, *blocks):
    u = ids[1]
    far = unpack(packed_far, PACK_GRADS, 512)
    rights = [jnp.concatenate([near[i * 128 : (i + 1) * 128, :], far[i * 128 : (i + 1) * 128, :]], 0) for i in range(4)]
    for k in range(4):
        first = PACK_LEFT + lax.rem(u + k, 4) * 256
        at = pl.ds(pl.multiple_of(first, 256), 256)
        low_at = pl.ds(pl.multiple_of(first + D, 256), 256)
        for block, (source, i) in enumerate(((at, 0), (at, 2), (at, 3), (low_at, 1))):
            blocks[k][block] = nn(rows_of_both(packed, packed_far, source), rights[i]).astype(BF)


def ff_weights_grad(ids, packed, packed_far, norms, own, right, left, far_a, far_b):
    core, u = ids[0], ids[1]
    share = UNITS // 16
    far = unpack(packed_far, PACK_NORMS, 256)
    normed = jnp.concatenate([norms[0:128, :], far[0:128, :]], 0)
    cot = jnp.concatenate([norms[128:256, :], far[128:256, :]], 0)
    for k in range(4):
        there = lax.rem(u + k, 4)
        for j in range(3):
            parts = []
            for v in range(4):
                chunk = jnp.where(core == 0, there * 4 + v, v * 4 + there)
                at = pl.ds(pl.multiple_of(j * UNITS + chunk * share, 16), share)
                parts.append(rows_of_both(packed, packed_far, at))
            value = nn(jnp.concatenate(parts, 0), normed if j < 2 else cot).astype(BF)
            rows = slice(j * share, (j + 1) * share)
            for v in range(4):
                piece = value[v * share : (v + 1) * share, :]
                if k == 2:
                    far_a[v, rows, :] = piece[:, :GROUP]
                    far_b[v, rows, :] = piece[:, GROUP:]
                else:
                    (own, right, None, left)[k][v, rows, :] = piece


def ff_add(right, left, from_left, from_right, after, new_right, new_left):
    new_right[:, :, 0:GROUP] = (right[:, :, 0:GROUP].astype(F32) + from_left[...].astype(F32)).astype(BF)
    new_right[:, :, GROUP:] = right[:, :, GROUP:]
    new_left[:, :, 0:GROUP] = left[:, :, 0:GROUP]
    new_left[:, :, GROUP:] = (left[:, :, GROUP:].astype(F32) + from_right[...].astype(F32)).astype(BF)


def sum_four(own, a, b, c):
    return own.astype(F32) + a.astype(F32) + b.astype(F32) + c.astype(F32)


def pack_gain(value):
    high = value.astype(BF)
    low = (value - high.astype(F32)).astype(BF)
    return jnp.concatenate(
        [high.astype(F32), low.astype(F32), jnp.zeros((8, HALF), F32)], 0
    ).astype(BF)


def unpack_gain(rows):
    rows = rows.astype(F32)
    return rows[0:4] + rows[4:8]


GAIN_AT = slice(256, 272)


def attn_sum_first(ids, own, a, b, c, *outs):
    v = ids[2]
    for k in range(4):
        at = pl.ds(pl.multiple_of(lax.rem(v + k, 4) * HD, HD), HD)
        for block in range(4):
            outs[k][block * HD : (block + 1) * HD, :] = sum_four(
                own[block, at, :], a[block, at, :], b[block, at, :], c[block, at, :]
            ).astype(BF)


def attn_sum_first_gain(ids, own, a, b, c, enc_gain, up_gain, lat_gain, *outs):
    attn_sum_first(ids, own, a, b, c, *outs)
    first = ids[4] == 0
    gain = jnp.where(
        first, jnp.concatenate([enc_gain[0:1, :], enc_gain[1:2, :] + up_gain[...]], 0), lat_gain[...]
    )
    halves = [gain[i : i + 1, h * HALF : (h + 1) * HALF] for i in range(2) for h in range(2)]
    packed = pack_gain(jnp.concatenate(halves, 0))
    for out in outs:
        out[GAIN_AT, :] = packed


def sum_all(*refs):
    refs, out = refs[:-1], refs[-1]
    out[0:256, :] = sum(ref[0:256, :].astype(F32) for ref in refs).astype(BF)
    out[GAIN_AT, :] = pack_gain(sum(unpack_gain(ref[GAIN_AT, :]) for ref in refs))


def stack_rows(*refs):
    refs, out = refs[:-1], refs[-1]
    for j, ref in enumerate(refs):
        out[j * 256 : (j + 1) * 256, :] = ref[0:256, :]
    out[1024:1040, :] = refs[0][GAIN_AT, :]


def ff_sum_first(ids, own, a, b, *outs):
    v = ids[2]
    for k in range(4):
        at = lax.rem(v + k, 4)
        outs[k][...] = (own[at].astype(F32) + a[at].astype(F32) + b[at].astype(F32)).astype(BF)


def ff_sum_second(own, a, b, c, out):
    out[...] = sum_four(own[...], a[...], b[...], c[...]).astype(BF)


def final_attn(ids, *refs):
    pieces, (qkv, out, gain) = refs[:8], refs[8:]
    step = pl.program_id(0)
    for side in range(2):
        core = ids[0] if side == 0 else 1 - ids[0]
        u = ids[1] if side == 0 else ids[2]
        v = ids[2] if side == 0 else ids[1]
        for k in range(4):
            piece = pieces[side * 4 + k]

            @pl.when(lax.rem(u + k, 4) == step)
            def _(piece=piece, v=v, core=core):
                for j in range(4):
                    at = pl.ds(pl.multiple_of(lax.rem(v + j, 4) * HD, HD), HD)
                    for block in range(4):
                        target, column = (qkv, block * D) if block < 3 else (out, 0)
                        lanes = pl.ds(pl.multiple_of(core * HALF + column, HALF), HALF)
                        first = j * 256 + block * HD
                        target[at, lanes] = piece[first : first + HD, :].astype(F32)

    mine = sum(unpack_gain(piece[1024:1040, :]) for piece in pieces[:4])
    other = sum(unpack_gain(piece[1024:1040, :]) for piece in pieces[4:])
    total = mine + other
    for i in range(2):
        for h in range(2):
            gain[i : i + 1, h * HALF : (h + 1) * HALF] = total[2 * i + h : 2 * i + h + 1, :]


SMEM = pltpu.MemorySpace.SMEM
VMEM = pltpu.MemorySpace.VMEM


def size(shape, dtype):
    return math.prod(shape) * jnp.dtype(dtype).itemsize


class Arriving:
    def __init__(self, copy, buffer):
        self.copy, self.buffer, self.here = copy, buffer, False

    def ready(self):
        if not self.here:
            self.copy.wait()
            self.here = True
        return self.buffer

    def __getitem__(self, index):
        return self.ready()[index]


class ArrivingBlocks:
    def __init__(self, blocks):
        self.blocks = blocks

    def block(self, j):
        return self.blocks[j]


def fetching(kernel, n_args, n_outs, plan):
    def wrapped(*refs):
        args, outs, rest = list(refs[:n_args]), refs[n_args : n_args + n_outs], refs[n_args + n_outs :]
        scratch, buffers, sems = rest[: len(rest) - len(plan) - 1], rest[len(rest) - len(plan) - 1 : -1], rest[-1]
        arriving = []
        blocks = {}
        for i, (a, j) in enumerate(plan):
            source = refs[a] if j is None else refs[a].at[:, j * D : (j + 1) * D]
            copy = pltpu.make_async_copy(source, buffers[i], sems.at[i])
            copy.start()
            arriving.append(Arriving(copy, buffers[i]))
            if j is None:
                args[a] = arriving[-1]
            else:
                blocks.setdefault(a, {})[j] = arriving[-1]
        for a, found in blocks.items():
            args[a] = ArrivingBlocks(found)
        kernel(*args, *outs, *scratch)
        for value in arriving:
            value.ready()

    return wrapped


def call(kernel, args, outs, scratch=(), spaces=None, spare=6, fetch=(), far_outs=False):
    spaces = dict(spaces or {})
    scratch = list(scratch)
    plan = [f if isinstance(f, tuple) else (f, None) for f in fetch]
    if plan:
        for a, j in plan:
            spaces[a] = pl.ANY
            shape = args[a].shape if j is None else (args[a].shape[0], D)
            scratch.append(pltpu.VMEM(shape, args[a].dtype))
        scratch.append(pltpu.SemaphoreType.DMA((len(plan),)))
        kernel = fetching(kernel, len(args), len(outs), plan)
    vmem = sum(size(a.shape, a.dtype) for i, a in enumerate(args) if i not in spaces)
    vmem += 0 if far_outs else sum(size(*o) for o in outs)
    vmem += sum(size(s.shape, s.dtype) for s in scratch if hasattr(s, "shape") and s.memory_space == VMEM)
    specs = [pl.BlockSpec(memory_space=spaces.get(i, VMEM)) for i in range(len(args))]
    return pl.pallas_call(
        kernel,
        out_shape=[jax.ShapeDtypeStruct(s, t) for s, t in outs],
        in_specs=specs,
        out_specs=[pl.BlockSpec(memory_space=pl.ANY if far_outs else VMEM) for _ in outs],
        scratch_shapes=scratch,
        compiler_params=pltpu.CompilerParams(vmem_limit_bytes=vmem + spare * 1024 * 1024),
    )(*args)


def nothing(outs):
    def kernel(*refs):
        pass

    return pl.pallas_call(
        kernel,
        out_shape=[jax.ShapeDtypeStruct(s, t) for s, t in outs],
        out_specs=[pl.BlockSpec(memory_space=pl.ANY) for _ in outs],
    )()


def on_section(flag, kernel, args, outs, **rest):
    return lax.cond(
        flag, lambda: call(kernel, args, outs, **rest), lambda: nothing(outs)
    )


def along(value, by):
    return lax.ppermute(value, "s", [(0, 1)] if by > 0 else [(1, 0)])


def swap(value, axis, sections=(0, 1)):
    pairs = [(s * 2 + i, s * 2 + 1 - i) for s in sections for i in range(2)]
    return lax.ppermute(value, ("s", axis), pairs)


def plane_shift(value, which, by, sections=(0, 1)):
    pairs = []
    for s in sections:
        for y in range(4):
            for x in range(4):
                for core in range(2):
                    ty, tx = ((y + by) % 4, x) if core == which else (y, (x + by) % 4)
                    pairs.append((((s * 4 + y) * 4 + x) * 2 + core, ((s * 4 + ty) * 4 + tx) * 2 + core))
    return lax.ppermute(value, ("s", "y", "x", "core"), pairs)


def exchange(blocks, which, sections=(0, 1)):
    return [plane_shift(blocks[k], which, k, sections) for k in (1, 2, 3)]


def collect(block, which):
    return [block] + [plane_shift(block, which, -k) for k in (1, 2, 3)]


def pick(stack, index, dim):
    return lax.dynamic_index_in_dim(stack, index, dim, keepdims=False)


def shards(patch_io, byte_states, patch_lengths, patch_live, attn_qkv, attn_out, gains, ff_weights):
    section = lax.axis_index("s")
    core = lax.axis_index("core")
    zh = lax.axis_index("zh")
    y, x = lax.axis_index("y"), lax.axis_index("x")
    first = section == 0
    second = section == 1
    ids = jnp.stack([core, jnp.where(core == 0, y, x), jnp.where(core == 0, x, y), zh, section])
    ids = ids.astype(jnp.int32)
    w_qkv = attn_qkv[0]
    w_out = attn_out[0]
    gain_pair = gains[0]
    micro, seq = patch_io.shape[1], patch_io.shape[3]
    half_bytes = byte_states.shape[2]
    units = ff_weights.shape[0]
    rows = micro * seq
    own_rows = patch_io.reshape(rows, D)
    up_a = along(byte_states[0, 0], -1)
    up_b = along(byte_states[1, 0], -1)
    lower = byte_states.reshape(micro * half_bytes, D)
    w_ff = jnp.swapaxes(ff_weights, 0, 1)
    lengths = patch_lengths[:, 0]
    live = patch_live[:, 0]
    ends = jnp.cumsum(lengths, axis=1)
    bounds = jnp.tile(jnp.stack([ends - lengths, ends], 1), (1, 1, 4))
    places = lax.iota(jnp.int32, seq)
    causal = places[:, None] <= places[None, :]
    diagonal = places[:, None] == places[None, :]
    allowed = causal[None] & ((live[:, :, None] == 1) | diagonal[None])
    allowed = lax.optimization_barrier(jnp.tile(allowed.astype(F32), (1, 1, 4)))

    wide = ((rows, D), BF)
    short = ((seq, D), BF)
    tall = ((micro * half_bytes, D), BF)
    piece = ((half_bytes, D), BF)
    (d_hidden,) = on_section(
        second,
        hidden_back,
        (own_rows, w_ff),
        [((rows, units), F32)],
        spaces={1: pl.ANY},
        scratch=[pltpu.VMEM((units, D), BF), pltpu.SemaphoreType.DMA((4,))],
    )
    pn, q, bn_lo, k_lo, v_lo = on_section(
        first,
        encode_lower,
        (own_rows, lower, w_qkv, gain_pair),
        [wide, wide, tall, tall, tall],
        fetch=((2, 0), 1, (2, 1), (2, 2)),
    )
    rest = []
    for m, up in enumerate((up_a, up_b)):
        rest.append(
            on_section(
                first,
                functools.partial(encode_rest, m),
                (own_rows, up, w_qkv, w_out, gain_pair, bounds, q, k_lo, v_lo),
                [short, short, ((8, 256, GROUP), BF), piece, piece, piece],
                fetch=((2, 1), (2, 2), 7, 8, 3),
            )
        )
    (hb_a, o_a, w_a, bn_a, k_a, v_a), (hb_b, o_b, w_b, bn_b, k_b, v_b) = rest
    arrived = [along(hb_a, 1), along(hb_b, 1)]

    latent_outs = [
        ((rows, D), F32), wide, ((2, D), F32), ((256, HALF), BF), ((512, HALF), BF), ((PACK_ROWS, rows), BF),
    ]

    def latent():
        return call(
            latent_layer,
            (ids, *arrived, own_rows, allowed, w_qkv, w_out, gain_pair, w_ff, d_hidden),
            latent_outs,
            spaces={0: SMEM, 8: pl.ANY},
            fetch=((5, 0), (5, 1), (5, 2), 6),
            scratch=[
                pltpu.VMEM((rows, 3 * D), BF),
                pltpu.VMEM((8, HD, GROUP), BF),
                pltpu.VMEM((rows, D), BF),
                pltpu.VMEM((3, units, D), BF),
                pltpu.VMEM((rows, D), F32),
                pltpu.VMEM((rows, D), F32),
                pltpu.VMEM((rows, 3 * D), BF),
                pltpu.SemaphoreType.DMA((4,)),
            ],
        )

    def turn():
        return nothing(latent_outs[:5]) + call(
            turn_encoder, (pn, o_a, o_b, bn_lo, bn_a, bn_b), latent_outs[5:]
        )

    latents, dhb, latent_gain, norms, lat_grads, packed = lax.cond(second, latent, turn)
    returned = along(dhb, -1)

    packed_far = swap(packed, "core")

    share = units // 16
    ff_block = ((4, 3 * share, HALF), BF)
    ff_half = ((4, 3 * share, GROUP), BF)
    ff_own, ff_right, ff_left, ff_far_a, ff_far_b = on_section(
        second,
        ff_weights_grad,
        (ids, packed, packed_far, norms),
        [ff_block, ff_block, ff_block, ff_half, ff_half],
        spaces={0: SMEM},
    )

    grads_long = ((2304, HALF), BF)
    enc_grads, enc_other = on_section(
        first,
        encoder_attention_back,
        (ids, returned, w_out, q, k_lo, v_lo, k_a, k_b, v_a, v_b, w_a, w_b),
        [grads_long, grads_long],
        spaces={0: SMEM},
        scratch=[pltpu.VMEM((2, 2304, HALF), BF), pltpu.SemaphoreType.DMA((2,))],
        fetch=(2, 5, 8, 10, 4, 6, 9, 11, 7),
        far_outs=True,
    )
    enc_far = swap(enc_other, "core", (0,))
    up_grad, up_gain = on_section(
        first,
        encoder_upper_back,
        (ids, up_a, up_b, w_qkv, gain_pair, enc_grads, enc_other),
        [tall, ((1, D), F32)],
        spaces={0: SMEM},
        fetch=(5, (3, 1), 6, (3, 2), 1, 2),
    )
    up_arrived = along(up_grad, 1)
    ff_far_a, ff_far_b, up_gain = lax.optimization_barrier((ff_far_a, ff_far_b, up_gain))
    from_left = plane_shift(ff_far_a, 0, 1)
    from_right = plane_shift(ff_far_b, 0, -1)
    outs = [((4, 256, HALF), BF)] * 4
    blocks = lax.cond(
        first,
        lambda: call(
            encoder_weights,
            (ids, packed, packed_far, enc_grads, enc_far, up_gain),
            outs,
            spaces={0: SMEM, 5: pl.ANY},
            fetch=(3, 4, 1, 2),
        ),
        lambda: call(latent_weights, (ids, packed, packed_far, lat_grads), outs, spaces={0: SMEM}),
    )
    last, from_left, from_right = lax.optimization_barrier((blocks[3], from_left, from_right))
    blocks = [*blocks[:3], last]
    got, up_arrived = lax.optimization_barrier((exchange(blocks, 0), up_arrived))
    low_outs = [((rows, D), F32), tall, ((2, D), F32)]

    def lower_grads():
        parts = call(
            encoder_lower_back,
            (ids, returned, own_rows, lower, w_qkv, gain_pair, enc_grads, enc_other, blocks[0]),
            low_outs,
            spaces={0: SMEM, 8: pl.ANY},
            fetch=(6, 7, (4, 0), (4, 1), (4, 2), 3),
        )
        return (*parts, *nothing([ff_block, ff_block]))

    def ff_middle():
        added = call(
            ff_add, (ff_right, ff_left, from_left, from_right, blocks[0]), [ff_block, ff_block], spaces={4: pl.ANY}
        )
        return (*nothing(low_outs), *added)

    patch_grad, low_grad, encoder_gain, ff_right_sum, ff_left_sum = lax.cond(first, lower_grads, ff_middle)
    line = [((272, HALF), BF)]
    blocks = call(
        attn_sum_first_gain,
        (ids, blocks[0], *got, encoder_gain, up_gain, latent_gain),
        line * 4,
        spaces={0: SMEM},
    )
    ff_right_sum, ff_left_sum, _ = lax.optimization_barrier((ff_right_sum, ff_left_sum, blocks))
    from_left = plane_shift(ff_right_sum, 0, 1, (1,))
    from_right = plane_shift(ff_left_sum, 0, -1, (1,))
    (block,) = call(sum_all, (blocks[0], *exchange(blocks, 1)), line)
    byte_grad = jnp.where(first, low_grad, up_arrived)
    patch_out = jnp.where(first, patch_grad, latents)
    from_left, from_right, block, byte_grad, patch_out = lax.optimization_barrier(
        (from_left, from_right, block, byte_grad, patch_out)
    )
    ff_line = ((3 * share, HALF), BF)
    ff_blocks = on_section(
        second, ff_sum_first, (ids, ff_own, from_left, from_right), [ff_line] * 4, spaces={0: SMEM}
    )
    ff_got = exchange(ff_blocks, 1)
    across, ff_got = lax.optimization_barrier((swap(block, "zh"), ff_got))
    (block,) = call(sum_all, (block, across), line)
    (block,) = call(stack_rows, collect(block, 1), [((1040, HALF), BF)])
    pieces = collect(block, 0)
    own_far = swap(block, "core")
    (ff_sum,) = on_section(second, ff_sum_second, (ff_blocks[0], *ff_got), [ff_line])
    ff_sum = ff_sum.reshape(3, 2, share // 2, HALF)
    ff_far = swap(pick(ff_sum, 1 - zh, 1), "zh")
    ff_sum = (pick(ff_sum, zh, 1).astype(F32) + ff_far.astype(F32)).astype(BF).reshape(3, 2, share // 4, HALF)
    ff_mine = pick(ff_sum, core, 1)
    ff_far = swap(pick(ff_sum, 1 - core, 1), "core")

    def ff_result():
        low, high = jnp.where(core == 0, ff_mine, ff_far), jnp.where(core == 0, ff_far, ff_mine)
        return jnp.swapaxes(jnp.concatenate([low, high], 2), 0, 1).astype(F32)

    ff_grad = lax.cond(second, ff_result, lambda: jnp.zeros((share // 4, 3, D), F32))
    ff_grad, *pieces = lax.optimization_barrier((ff_grad, *pieces))
    pieces = pieces + [own_far] + [swap(p, "core") for p in pieces[1:]]
    whole = lambda p: pl.BlockSpec(p.shape, lambda i, n=p.ndim: (0,) * n)
    total_qkv, total_out, total_gain = pl.pallas_call(
        final_attn,
        grid=(4,),
        out_shape=[
            jax.ShapeDtypeStruct((D, 3 * D), F32),
            jax.ShapeDtypeStruct((D, D), F32),
            jax.ShapeDtypeStruct((2, D), F32),
        ],
        in_specs=[pl.BlockSpec(memory_space=SMEM)] + [whole(p) for p in pieces],
        out_specs=[
            pl.BlockSpec((256, 3 * D), lambda i: (i, 0)),
            pl.BlockSpec((256, D), lambda i: (i, 0)),
            pl.BlockSpec((2, D), lambda i: (0, 0)),
        ],
        compiler_params=pltpu.CompilerParams(vmem_limit_bytes=FINAL_VMEM),
    )(ids, *pieces)
    return (
        patch_out.reshape(1, micro, 1, seq, D),
        byte_grad.reshape(micro, 1, half_bytes, D),
        total_qkv[None],
        total_out[None],
        total_gain[None],
        ff_grad[None],
    )


def solution(mesh):
    fine = Mesh(mesh.devices.reshape(2, 4, 4, 2, 2), ("s",) + BATCH)
    in_specs = (
        P("s", None, BATCH, None, None),
        P(None, BATCH, "s", None),
        P(None, BATCH, None),
        P(None, BATCH, None),
        P("s", None, None),
        P("s", None, None),
        P("s", None, None),
        P(),
    )
    out_specs = (
        P("s", None, BATCH, None, None),
        P(None, BATCH, "s", None),
        P("s", None, None),
        P("s", None, None),
        P("s", None, None),
        P("s", BATCH, None, None),
    )
    return jax.shard_map(shards, mesh=fine, in_specs=in_specs, out_specs=out_specs, check_vma=False)
```

```python
import functools
import math

import jax
import jax.numpy as jnp
from jax import lax
from jax.experimental import pallas as pl
from jax.experimental.pallas import tpu as pltpu
from jax.sharding import Mesh
from jax.sharding import PartitionSpec as P

HD = 64
SCALE = HD**-0.5
EPS = 1e-05
NEG = -1e30
BATCH = ("y", "x", "zh", "core")
BF = jnp.bfloat16
F32 = jnp.float32
D = 1024
HALF = 512
GROUP = 256
FINAL_VMEM = 32 * 1024 * 1024


UNITS = 2816
PACK_NORMS = 3 * UNITS
PACK_LEFT = PACK_NORMS + 4 * 256
PACK_GRADS = PACK_LEFT + 2 * D
PACK_ROWS = PACK_GRADS + 4 * 512


def nn(a, b):
    return lax.dot_general(a, b, (((1,), (0,)), ((), ())), preferred_element_type=F32)


def nt(a, b):
    return lax.dot_general(a, b, (((1,), (1,)), ((), ())), preferred_element_type=F32)


def tn(a, b):
    return lax.dot_general(a, b, (((0,), (0,)), ((), ())), preferred_element_type=F32)


def inverse_rms(x):
    return lax.rsqrt(jnp.mean(x * x, axis=-1, keepdims=True) + EPS)


def norm_back(x, gain, up):
    r = inverse_rms(x)
    scaled = up * gain
    inner = jnp.mean(scaled * x, axis=-1, keepdims=True)
    return r * (scaled - x * (r * r * inner)), up * (x * r)


def stack_heads(rows):
    head = lax.broadcasted_iota(jnp.int32, rows.shape, 1) // HD
    return jnp.concatenate([jnp.where(head == h, rows, jnp.zeros_like(rows)) for h in range(4)], 0)


def unstack_heads(stacked):
    head = lax.broadcasted_iota(jnp.int32, (HD, GROUP), 1) // HD
    out = stacked[0:HD]
    for h in range(1, 4):
        out = jnp.where(head == h, stacked[h * HD : (h + 1) * HD], out)
    return out


def softmax_columns(scores):
    top = functools.reduce(jnp.maximum, [jnp.max(s, axis=0, keepdims=True) for s in scores])
    parts = [jnp.exp(s - top) for s in scores]
    inverse = 1.0 / sum(jnp.sum(p, axis=0, keepdims=True) for p in parts)
    return [(p * inverse).astype(BF) for p in parts]


def encode_lower(patch, low, w_qkv, gains, pn, q, bn, k, v):
    x = patch[...].astype(F32)
    normed = (x * inverse_rms(x) * gains[0:1]).astype(BF)
    pn[...] = normed
    q[...] = nn(normed, w_qkv.block(0)[...]).astype(BF)
    for i in range(2):
        at = pl.ds(i * 256, 256)
        b = low[at, :].astype(F32)
        normed = (b * inverse_rms(b) * gains[1:2]).astype(BF)
        bn[at, :] = normed
        k[at, :] = nn(normed, w_qkv.block(1)[...]).astype(BF)
        v[at, :] = nn(normed, w_qkv.block(2)[...]).astype(BF)


def encode_rest(m, patch, up, w_qkv, w_out, gains, bounds, q, k_lo, v_lo, hb, o1, weights, bn, k, v):
    b = up[...].astype(F32)
    normed = (b * inverse_rms(b) * gains[1:2]).astype(BF)
    bn[...] = normed
    k[...] = nn(normed, w_qkv.block(1)[...]).astype(BF)
    v[...] = nn(normed, w_qkv.block(2)[...]).astype(BF)
    spot = lax.broadcasted_iota(jnp.int32, (256, GROUP), 0)
    start = bounds[m, 0:1, :]
    end = bounds[m, 1:2, :]
    inside = [(spot + h * 256 >= start) & (spot + h * 256 < end) for h in range(2)]
    low_at = slice(m * 256, (m + 1) * 256)
    rows = slice(m * HD, (m + 1) * HD)
    for g in range(4):
        lanes = slice(g * GROUP, (g + 1) * GROUP)
        stacked = stack_heads(q[rows, lanes] * BF(SCALE))
        scores = [
            jnp.where(inside[h], nt(keys, stacked), NEG)
            for h, keys in enumerate((k_lo[low_at, lanes], k[:, lanes]))
        ]
        w = softmax_columns(scores)
        weights[g * 2] = w[0]
        weights[g * 2 + 1] = w[1]
        mixed = tn(w[0], v_lo[low_at, lanes]) + tn(w[1], v[:, lanes])
        o1[:, lanes] = unstack_heads(mixed).astype(BF)
    hb[...] = (patch[rows, :].astype(F32) + nn(o1[...], w_out[...])).astype(BF)


def latent_layer(
    ids, hb_a, hb_b, cot, allowed, w_qkv, w_out, gains, w_ff, d_hidden,
    latents, dhb, gain_grad, norms, grads, packed,
    qkv, weights, o2, ff_buf, acc_out, acc_norm, dqkv, sems,
):
    core = ids[0]
    units = w_ff.shape[1]
    step = 256
    parts = 4
    part = units // parts

    fetches = []
    for i in range(parts):
        at = slice(i * part, (i + 1) * part)
        fetches.append(pltpu.make_async_copy(w_ff.at[:, at, :], ff_buf.at[:, at, :], sems.at[i]))
        fetches[-1].start()
    x = jnp.concatenate([hb_a[...], hb_b[...]], 0).astype(F32)
    normed = (x * inverse_rms(x) * gains[0:1]).astype(BF)
    packed[PACK_LEFT : PACK_LEFT + D, :] = normed.T
    for j in range(3):
        qkv[:, j * D : (j + 1) * D] = nn(normed, w_qkv.block(j)[...]).astype(BF)
    for m in range(2):
        rows = slice(m * HD, (m + 1) * HD)
        for g in range(4):
            lanes = slice(g * GROUP, (g + 1) * GROUP)
            k_lanes = slice(D + g * GROUP, D + (g + 1) * GROUP)
            v_lanes = slice(2 * D + g * GROUP, 2 * D + (g + 1) * GROUP)
            stacked = stack_heads(qkv[rows, lanes] * BF(SCALE))
            scores = jnp.where(allowed[m] > 0.5, nt(qkv[rows, k_lanes], stacked), NEG)
            (w,) = softmax_columns([scores])
            weights[m * 4 + g] = w
            o2[rows, lanes] = unstack_heads(tn(w, qkv[rows, v_lanes])).astype(BF)
    packed[PACK_LEFT + D : PACK_LEFT + 2 * D, :] = o2[...].T
    after = x + nn(o2[...], w_out[...])
    yn = (after * inverse_rms(after) * gains[1:2]).astype(BF)
    c = cot[...]
    for h in range(2):

        @pl.when(core == h)
        def _(h=h):
            norms[0:128, :] = yn[:, h * HALF : (h + 1) * HALF]
            norms[128:256, :] = c[:, h * HALF : (h + 1) * HALF]

        @pl.when(core != h)
        def _(h=h):
            for b in range(4):
                lanes = slice(h * HALF + b * 128, h * HALF + (b + 1) * 128)
                packed[PACK_NORMS + b * 256 : PACK_NORMS + b * 256 + 128, :] = yn[:, lanes]
                packed[PACK_NORMS + b * 256 + 128 : PACK_NORMS + (b + 1) * 256, :] = c[:, lanes]

    for copy in fetches:
        copy.wait()
    acc_out[...] = after
    for i in range(units // step):
        at = slice(i * step, (i + 1) * step)
        gate = nt(yn, ff_buf[0, at, :])
        upward = nt(yn, ff_buf[1, at, :])
        du = d_hidden[:, at]
        sig = 1.0 / (1.0 + jnp.exp(-gate))
        active = gate * sig
        hidden = (active * upward).astype(BF)
        d_gate = (du * upward * (sig * (1.0 + gate * (1.0 - sig)))).astype(BF)
        d_up = (du * active).astype(BF)
        for j, value in enumerate((d_gate, d_up, hidden)):
            packed[i * step + j * units : (i + 1) * step + j * units, :] = value.T
        acc_out[...] += nn(hidden, ff_buf[2, at, :])
        back = nn(d_gate, ff_buf[0, at, :]) + nn(d_up, ff_buf[1, at, :])
        if i == 0:
            acc_norm[...] = back
        else:
            acc_norm[...] += back
    latents[...] = acc_out[...]
    back, gain_rows = norm_back(after, gains[1:2], acc_norm[...])
    gain_grad[1:2, :] = jnp.sum(gain_rows, axis=0, keepdims=True)
    d_after = c.astype(F32) + back
    da = d_after.astype(BF)
    d_mixed = nt(da, w_out[...]).astype(BF)
    for m in range(2):
        rows = slice(m * HD, (m + 1) * HD)
        for g in range(4):
            lanes = slice(g * GROUP, (g + 1) * GROUP)
            k_lanes = slice(D + g * GROUP, D + (g + 1) * GROUP)
            v_lanes = slice(2 * D + g * GROUP, 2 * D + (g + 1) * GROUP)
            q_stacked = stack_heads(qkv[rows, lanes] * BF(SCALE))
            o_stacked = stack_heads(d_mixed[rows, lanes])
            w_low = weights[m * 4 + g]
            w = w_low.astype(F32)
            dw = nt(qkv[rows, v_lanes], o_stacked)
            inner = jnp.sum(dw * w, axis=0, keepdims=True)
            ds = (w * (dw - inner)).astype(BF)
            dqkv[rows, lanes] = (unstack_heads(tn(ds, qkv[rows, k_lanes])) * SCALE).astype(BF)
            dqkv[rows, k_lanes] = nn(ds, q_stacked).astype(BF)
            dqkv[rows, v_lanes] = nn(w_low, o_stacked).astype(BF)
    d_normed = sum(nt(dqkv[:, j * D : (j + 1) * D], w_qkv.block(j)[...]) for j in range(3))
    back, gain_rows = norm_back(x, gains[0:1], d_normed)
    gain_grad[0:1, :] = jnp.sum(gain_rows, axis=0, keepdims=True)
    dhb[...] = (d_after + back).astype(BF)
    for h in range(2):
        pieces = (
            dqkv[:, h * HALF : (h + 1) * HALF],
            da[:, h * HALF : (h + 1) * HALF],
            dqkv[:, D + h * HALF : D + (h + 1) * HALF],
            dqkv[:, 2 * D + h * HALF : 2 * D + (h + 1) * HALF],
        )

        @pl.when(core == h)
        def _(pieces=pieces):
            for i, value in enumerate(pieces):
                grads[i * 128 : (i + 1) * 128, :] = value

        @pl.when(core != h)
        def _(pieces=pieces):
            for i, value in enumerate(pieces):
                for b in range(4):
                    first = PACK_GRADS + b * 512 + i * 128
                    packed[first : first + 128, :] = value[:, b * 128 : (b + 1) * 128]


def hidden_back(cot, w_ff, d_hidden, buffer, sems):
    parts = 4
    part = w_ff.shape[1] // parts
    copies = []
    for i in range(parts):
        at = slice(i * part, (i + 1) * part)
        copies.append(pltpu.make_async_copy(w_ff.at[2, at, :], buffer.at[at, :], sems.at[i]))
        copies[-1].start()
    for copy in copies:
        copy.wait()
    for i in range(w_ff.shape[1] // 256):
        at = slice(i * 256, (i + 1) * 256)
        d_hidden[:, at] = nt(cot[...], buffer[at, :])


def encoder_attention_back(
    ids, dhb, w_out, q, k_lo, v_lo, k_a, k_b, v_a, v_b, w_a, w_b, mine, other, both, sems
):
    d_mixed = nt(dhb[...], w_out[...]).astype(BF)
    for g in range(4):
        lanes = slice(g * GROUP, (g + 1) * GROUP)
        out_lanes = slice((g % 2) * GROUP, (g % 2 + 1) * GROUP)
        half = jnp.where(ids[0] == g // 2, 0, 1)

        def put(at, value, half=half, out_lanes=out_lanes):
            both[half, at, out_lanes] = value

        put(slice(128, 256), dhb[:, lanes])
        for m, (k_up, v_up, weights) in enumerate(((k_a, v_a, w_a), (k_b, v_b, w_b))):
            rows = slice(m * HD, (m + 1) * HD)
            low_at = slice(m * 256, (m + 1) * 256)
            q_stacked = stack_heads(q[rows, lanes] * BF(SCALE))
            o_stacked = stack_heads(d_mixed[rows, lanes])
            low = [weights[g * 2 + h] for h in range(2)]
            w = [piece.astype(F32) for piece in low]
            dw = [nt(values, o_stacked) for values in (v_lo[low_at, lanes], v_up[:, lanes])]
            inner = sum(jnp.sum(a * b, axis=0, keepdims=True) for a, b in zip(dw, w))
            ds = [(b * (a - inner)).astype(BF) for a, b in zip(dw, w)]
            dq = tn(ds[0], k_lo[low_at, lanes]) + tn(ds[1], k_up[:, lanes])
            put(rows, (unstack_heads(dq) * SCALE).astype(BF))
            for h in range(2):
                base = h * HALF + m * 256
                put(slice(256 + base, 512 + base), nn(ds[h], q_stacked).astype(BF))
                put(slice(1280 + base, 1536 + base), nn(low[h], o_stacked).astype(BF))
    copies = [pltpu.make_async_copy(both.at[i], out, sems.at[i]) for i, out in enumerate((mine, other))]
    for copy in copies:
        copy.start()
    for copy in copies:
        copy.wait()


def both_columns(core, block, w_qkv):
    return [
        w_qkv.block(block)[:, pl.ds(pl.multiple_of(which * HALF, HALF), HALF)] for which in (core, 1 - core)
    ]


def bytes_back(core, h, source, w_qkv, gains, grads):
    d_norm = sum(
        nt(ref[1024 * block - 768 + h * HALF : 1024 * block - 256 + h * HALF, :], columns)
        for block in (1, 2)
        for ref, columns in zip(grads, both_columns(core, block, w_qkv))
    )
    back, gain_rows = norm_back(source.astype(F32), gains[1:2], d_norm)
    return back.astype(BF), jnp.sum(gain_rows, axis=0, keepdims=True)


def encoder_upper_back(ids, up_a, up_b, w_qkv, gains, mine, other, up_grad, gain_grad):
    source = jnp.concatenate([up_a[...], up_b[...]], 0)
    back, rows = bytes_back(ids[0], 1, source, w_qkv, gains, (mine, other))
    up_grad[...] = back
    gain_grad[...] = rows


def encoder_lower_back(
    ids, dhb, patch, low, w_qkv, gains, mine, other, after, patch_grad, low_grad, gain_grad
):
    core = ids[0]
    up_norm = sum(nt(ref[0:128, :], columns) for ref, columns in zip((mine, other), both_columns(core, 0, w_qkv)))
    back, gain_rows = norm_back(patch[...].astype(F32), gains[0:1], up_norm)
    gain_grad[0:1, :] = jnp.sum(gain_rows, axis=0, keepdims=True)
    patch_grad[...] = dhb[...].astype(F32) + back
    back, rows = bytes_back(core, 0, low[...], w_qkv, gains, (mine, other))
    low_grad[...] = back
    gain_grad[1:2, :] = rows


def turn_encoder(pn, o_a, o_b, bn_lo, bn_a, bn_b, packed):
    for b, rows in enumerate([bn_lo[i * 128 : (i + 1) * 128, :] for i in range(4)]
                             + [ref[i * 128 : (i + 1) * 128, :] for ref in (bn_a, bn_b) for i in range(2)]):
        packed[b * D : (b + 1) * D, :] = rows.T
    packed[PACK_LEFT : PACK_LEFT + D, :] = pn[...].T
    packed[PACK_LEFT + D : PACK_LEFT + 2 * D, :] = jnp.concatenate([o_a[...], o_b[...]], 0).T


def rows_of_both(left, left_far, at):
    return jnp.concatenate([left[at, :], left_far[at, :]], 1)


def below(near, far, rows):
    return jnp.concatenate([near[rows, :], far[rows, :]], 0)


def encoder_weights(ids, packed, packed_far, near, far, after, *blocks):
    u = ids[1]
    queries = below(near, far, slice(0, 128))
    outputs = below(near, far, slice(128, 256))
    for k in range(4):
        first = lax.rem(u + k, 4) * 256

        def at(base, first=first):
            return pl.ds(pl.multiple_of(first + base, 256), 256)

        blocks[k][0] = nn(rows_of_both(packed, packed_far, at(PACK_LEFT)), queries).astype(BF)
        blocks[k][3] = nn(rows_of_both(packed, packed_far, at(PACK_LEFT + D)), outputs).astype(BF)
        lefts = [jnp.concatenate([ref[at(b * D), :] for b in range(8)], 1) for ref in (packed, packed_far)]
        for block in (1, 2):
            rows = slice(1024 * block - 768, 1024 * block + 256)
            blocks[k][block] = (nn(lefts[0], near[rows, :]) + nn(lefts[1], far[rows, :])).astype(BF)


def unpack(packed, first, rows):
    return jnp.concatenate([packed[first + b * rows : first + (b + 1) * rows, :] for b in range(4)], 1)


def latent_weights(ids, packed, packed_far, near, *blocks):
    u = ids[1]
    far = unpack(packed_far, PACK_GRADS, 512)
    rights = [jnp.concatenate([near[i * 128 : (i + 1) * 128, :], far[i * 128 : (i + 1) * 128, :]], 0) for i in range(4)]
    for k in range(4):
        first = PACK_LEFT + lax.rem(u + k, 4) * 256
        at = pl.ds(pl.multiple_of(first, 256), 256)
        low_at = pl.ds(pl.multiple_of(first + D, 256), 256)
        for block, (source, i) in enumerate(((at, 0), (at, 2), (at, 3), (low_at, 1))):
            blocks[k][block] = nn(rows_of_both(packed, packed_far, source), rights[i]).astype(BF)


def ff_weights_grad(ids, packed, packed_far, norms, own, right, left, far_a, far_b):
    core, u = ids[0], ids[1]
    share = UNITS // 16
    far = unpack(packed_far, PACK_NORMS, 256)
    normed = jnp.concatenate([norms[0:128, :], far[0:128, :]], 0)
    cot = jnp.concatenate([norms[128:256, :], far[128:256, :]], 0)
    for k in range(4):
        there = lax.rem(u + k, 4)
        for j in range(3):
            parts = []
            for v in range(4):
                chunk = jnp.where(core == 0, there * 4 + v, v * 4 + there)
                at = pl.ds(pl.multiple_of(j * UNITS + chunk * share, 16), share)
                parts.append(rows_of_both(packed, packed_far, at))
            value = nn(jnp.concatenate(parts, 0), normed if j < 2 else cot).astype(BF)
            rows = slice(j * share, (j + 1) * share)
            for v in range(4):
                piece = value[v * share : (v + 1) * share, :]
                if k == 2:
                    far_a[v, rows, :] = piece[:, :GROUP]
                    far_b[v, rows, :] = piece[:, GROUP:]
                else:
                    (own, right, None, left)[k][v, rows, :] = piece


def ff_add(right, left, from_left, from_right, after, new_right, new_left):
    new_right[:, :, 0:GROUP] = (right[:, :, 0:GROUP].astype(F32) + from_left[...].astype(F32)).astype(BF)
    new_right[:, :, GROUP:] = right[:, :, GROUP:]
    new_left[:, :, 0:GROUP] = left[:, :, 0:GROUP]
    new_left[:, :, GROUP:] = (left[:, :, GROUP:].astype(F32) + from_right[...].astype(F32)).astype(BF)


def sum_four(own, a, b, c):
    return own.astype(F32) + a.astype(F32) + b.astype(F32) + c.astype(F32)


def pack_gain(value):
    high = value.astype(BF)
    low = (value - high.astype(F32)).astype(BF)
    return jnp.concatenate(
        [high.astype(F32), low.astype(F32), jnp.zeros((8, HALF), F32)], 0
    ).astype(BF)


def unpack_gain(rows):
    rows = rows.astype(F32)
    return rows[0:4] + rows[4:8]


GAIN_AT = slice(256, 272)


def attn_sum_first(ids, own, a, b, c, *outs):
    v = ids[2]
    for k in range(4):
        at = pl.ds(pl.multiple_of(lax.rem(v + k, 4) * HD, HD), HD)
        for block in range(4):
            outs[k][block * HD : (block + 1) * HD, :] = sum_four(
                own[block, at, :], a[block, at, :], b[block, at, :], c[block, at, :]
            ).astype(BF)


def attn_sum_first_gain(ids, own, a, b, c, enc_gain, up_gain, lat_gain, *outs):
    attn_sum_first(ids, own, a, b, c, *outs)
    first = ids[4] == 0
    gain = jnp.where(
        first, jnp.concatenate([enc_gain[0:1, :], enc_gain[1:2, :] + up_gain[...]], 0), lat_gain[...]
    )
    halves = [gain[i : i + 1, h * HALF : (h + 1) * HALF] for i in range(2) for h in range(2)]
    packed = pack_gain(jnp.concatenate(halves, 0))
    for out in outs:
        out[GAIN_AT, :] = packed


def sum_all(*refs):
    refs, out = refs[:-1], refs[-1]
    out[0:256, :] = sum(ref[0:256, :].astype(F32) for ref in refs).astype(BF)
    out[GAIN_AT, :] = pack_gain(sum(unpack_gain(ref[GAIN_AT, :]) for ref in refs))


def stack_rows(*refs):
    refs, out = refs[:-1], refs[-1]
    for j, ref in enumerate(refs):
        out[j * 256 : (j + 1) * 256, :] = ref[0:256, :]
    out[1024:1040, :] = refs[0][GAIN_AT, :]


def ff_sum_first(ids, own, a, b, *outs):
    v = ids[2]
    for k in range(4):
        at = lax.rem(v + k, 4)
        outs[k][...] = (own[at].astype(F32) + a[at].astype(F32) + b[at].astype(F32)).astype(BF)


def ff_sum_second(own, a, b, c, out):
    out[...] = sum_four(own[...], a[...], b[...], c[...]).astype(BF)


def final_attn(ids, *refs):
    pieces, (qkv, out, gain) = refs[:8], refs[8:]
    step = pl.program_id(0)
    for side in range(2):
        core = ids[0] if side == 0 else 1 - ids[0]
        u = ids[1] if side == 0 else ids[2]
        v = ids[2] if side == 0 else ids[1]
        for k in range(4):
            piece = pieces[side * 4 + k]

            @pl.when(lax.rem(u + k, 4) == step)
            def _(piece=piece, v=v, core=core):
                for j in range(4):
                    at = pl.ds(pl.multiple_of(lax.rem(v + j, 4) * HD, HD), HD)
                    for block in range(4):
                        target, column = (qkv, block * D) if block < 3 else (out, 0)
                        lanes = pl.ds(pl.multiple_of(core * HALF + column, HALF), HALF)
                        first = j * 256 + block * HD
                        target[at, lanes] = piece[first : first + HD, :].astype(F32)

    mine = sum(unpack_gain(piece[1024:1040, :]) for piece in pieces[:4])
    other = sum(unpack_gain(piece[1024:1040, :]) for piece in pieces[4:])
    total = mine + other
    for i in range(2):
        for h in range(2):
            gain[i : i + 1, h * HALF : (h + 1) * HALF] = total[2 * i + h : 2 * i + h + 1, :]


SMEM = pltpu.MemorySpace.SMEM
VMEM = pltpu.MemorySpace.VMEM


def size(shape, dtype):
    return math.prod(shape) * jnp.dtype(dtype).itemsize


class Arriving:
    def __init__(self, copy, buffer):
        self.copy, self.buffer, self.here = copy, buffer, False

    def ready(self):
        if not self.here:
            self.copy.wait()
            self.here = True
        return self.buffer

    def __getitem__(self, index):
        return self.ready()[index]


class ArrivingBlocks:
    def __init__(self, blocks):
        self.blocks = blocks

    def block(self, j):
        return self.blocks[j]


def fetching(kernel, n_args, n_outs, plan):
    def wrapped(*refs):
        args, outs, rest = list(refs[:n_args]), refs[n_args : n_args + n_outs], refs[n_args + n_outs :]
        scratch, buffers, sems = rest[: len(rest) - len(plan) - 1], rest[len(rest) - len(plan) - 1 : -1], rest[-1]
        arriving = []
        blocks = {}
        for i, (a, j) in enumerate(plan):
            source = refs[a] if j is None else refs[a].at[:, j * D : (j + 1) * D]
            copy = pltpu.make_async_copy(source, buffers[i], sems.at[i])
            copy.start()
            arriving.append(Arriving(copy, buffers[i]))
            if j is None:
                args[a] = arriving[-1]
            else:
                blocks.setdefault(a, {})[j] = arriving[-1]
        for a, found in blocks.items():
            args[a] = ArrivingBlocks(found)
        kernel(*args, *outs, *scratch)
        for value in arriving:
            value.ready()

    return wrapped


def call(kernel, args, outs, scratch=(), spaces=None, spare=6, fetch=(), far_outs=False):
    spaces = dict(spaces or {})
    scratch = list(scratch)
    plan = [f if isinstance(f, tuple) else (f, None) for f in fetch]
    if plan:
        for a, j in plan:
            spaces[a] = pl.ANY
            shape = args[a].shape if j is None else (args[a].shape[0], D)
            scratch.append(pltpu.VMEM(shape, args[a].dtype))
        scratch.append(pltpu.SemaphoreType.DMA((len(plan),)))
        kernel = fetching(kernel, len(args), len(outs), plan)
    vmem = sum(size(a.shape, a.dtype) for i, a in enumerate(args) if i not in spaces)
    vmem += 0 if far_outs else sum(size(*o) for o in outs)
    vmem += sum(size(s.shape, s.dtype) for s in scratch if hasattr(s, "shape") and s.memory_space == VMEM)
    specs = [pl.BlockSpec(memory_space=spaces.get(i, VMEM)) for i in range(len(args))]
    return pl.pallas_call(
        kernel,
        out_shape=[jax.ShapeDtypeStruct(s, t) for s, t in outs],
        in_specs=specs,
        out_specs=[pl.BlockSpec(memory_space=pl.ANY if far_outs else VMEM) for _ in outs],
        scratch_shapes=scratch,
        compiler_params=pltpu.CompilerParams(vmem_limit_bytes=vmem + spare * 1024 * 1024),
    )(*args)


def nothing(outs):
    def kernel(*refs):
        pass

    return pl.pallas_call(
        kernel,
        out_shape=[jax.ShapeDtypeStruct(s, t) for s, t in outs],
        out_specs=[pl.BlockSpec(memory_space=pl.ANY) for _ in outs],
    )()


def on_section(flag, kernel, args, outs, **rest):
    return lax.cond(
        flag, lambda: call(kernel, args, outs, **rest), lambda: nothing(outs)
    )


def along(value, by):
    return lax.ppermute(value, "s", [(0, 1)] if by > 0 else [(1, 0)])


def swap(value, axis, sections=(0, 1)):
    pairs = [(s * 2 + i, s * 2 + 1 - i) for s in sections for i in range(2)]
    return lax.ppermute(value, ("s", axis), pairs)


def plane_shift(value, which, by, sections=(0, 1)):
    pairs = []
    for s in sections:
        for y in range(4):
            for x in range(4):
                for core in range(2):
                    ty, tx = ((y + by) % 4, x) if core == which else (y, (x + by) % 4)
                    pairs.append((((s * 4 + y) * 4 + x) * 2 + core, ((s * 4 + ty) * 4 + tx) * 2 + core))
    return lax.ppermute(value, ("s", "y", "x", "core"), pairs)


def exchange(blocks, which, sections=(0, 1)):
    return [plane_shift(blocks[k], which, k, sections) for k in (1, 2, 3)]


def collect(block, which):
    return [block] + [plane_shift(block, which, -k) for k in (1, 2, 3)]


def pick(stack, index, dim):
    return lax.dynamic_index_in_dim(stack, index, dim, keepdims=False)


def shards(patch_io, byte_states, patch_lengths, patch_live, attn_qkv, attn_out, gains, ff_weights):
    section = lax.axis_index("s")
    core = lax.axis_index("core")
    zh = lax.axis_index("zh")
    y, x = lax.axis_index("y"), lax.axis_index("x")
    first = section == 0
    second = section == 1
    ids = jnp.stack([core, jnp.where(core == 0, y, x), jnp.where(core == 0, x, y), zh, section])
    ids = ids.astype(jnp.int32)
    w_qkv = attn_qkv[0]
    w_out = attn_out[0]
    gain_pair = gains[0]
    micro, seq = patch_io.shape[1], patch_io.shape[3]
    half_bytes = byte_states.shape[2]
    units = ff_weights.shape[0]
    rows = micro * seq
    own_rows = patch_io.reshape(rows, D)
    up_a = along(byte_states[0, 0], -1)
    up_b = along(byte_states[1, 0], -1)
    lower = byte_states.reshape(micro * half_bytes, D)
    w_ff = jnp.swapaxes(ff_weights, 0, 1)
    lengths = patch_lengths[:, 0]
    live = patch_live[:, 0]
    ends = jnp.cumsum(lengths, axis=1)
    bounds = jnp.tile(jnp.stack([ends - lengths, ends], 1), (1, 1, 4))
    places = lax.iota(jnp.int32, seq)
    causal = places[:, None] <= places[None, :]
    diagonal = places[:, None] == places[None, :]
    allowed = causal[None] & ((live[:, :, None] == 1) | diagonal[None])
    allowed = lax.optimization_barrier(jnp.tile(allowed.astype(F32), (1, 1, 4)))

    wide = ((rows, D), BF)
    short = ((seq, D), BF)
    tall = ((micro * half_bytes, D), BF)
    piece = ((half_bytes, D), BF)
    (d_hidden,) = on_section(
        second,
        hidden_back,
        (own_rows, w_ff),
        [((rows, units), F32)],
        spaces={1: pl.ANY},
        scratch=[pltpu.VMEM((units, D), BF), pltpu.SemaphoreType.DMA((4,))],
    )
    pn, q, bn_lo, k_lo, v_lo = on_section(
        first,
        encode_lower,
        (own_rows, lower, w_qkv, gain_pair),
        [wide, wide, tall, tall, tall],
        fetch=((2, 0), 1, (2, 1), (2, 2)),
    )
    rest = []
    for m, up in enumerate((up_a, up_b)):
        rest.append(
            on_section(
                first,
                functools.partial(encode_rest, m),
                (own_rows, up, w_qkv, w_out, gain_pair, bounds, q, k_lo, v_lo),
                [short, short, ((8, 256, GROUP), BF), piece, piece, piece],
                fetch=((2, 1), (2, 2), 7, 8, 3),
            )
        )
    (hb_a, o_a, w_a, bn_a, k_a, v_a), (hb_b, o_b, w_b, bn_b, k_b, v_b) = rest
    arrived = [along(hb_a, 1), along(hb_b, 1)]

    latent_outs = [
        ((rows, D), F32), wide, ((2, D), F32), ((256, HALF), BF), ((512, HALF), BF), ((PACK_ROWS, rows), BF),
    ]

    def latent():
        return call(
            latent_layer,
            (ids, *arrived, own_rows, allowed, w_qkv, w_out, gain_pair, w_ff, d_hidden),
            latent_outs,
            spaces={0: SMEM, 8: pl.ANY},
            fetch=((5, 0), (5, 1), (5, 2), 6),
            scratch=[
                pltpu.VMEM((rows, 3 * D), BF),
                pltpu.VMEM((8, HD, GROUP), BF),
                pltpu.VMEM((rows, D), BF),
                pltpu.VMEM((3, units, D), BF),
                pltpu.VMEM((rows, D), F32),
                pltpu.VMEM((rows, D), F32),
                pltpu.VMEM((rows, 3 * D), BF),
                pltpu.SemaphoreType.DMA((4,)),
            ],
        )

    def turn():
        return nothing(latent_outs[:5]) + call(
            turn_encoder, (pn, o_a, o_b, bn_lo, bn_a, bn_b), latent_outs[5:]
        )

    latents, dhb, latent_gain, norms, lat_grads, packed = lax.cond(second, latent, turn)
    returned = along(dhb, -1)

    packed_far = swap(packed, "core")

    share = units // 16
    ff_block = ((4, 3 * share, HALF), BF)
    ff_half = ((4, 3 * share, GROUP), BF)
    ff_own, ff_right, ff_left, ff_far_a, ff_far_b = on_section(
        second,
        ff_weights_grad,
        (ids, packed, packed_far, norms),
        [ff_block, ff_block, ff_block, ff_half, ff_half],
        spaces={0: SMEM},
    )

    grads_long = ((2304, HALF), BF)
    enc_grads, enc_other = on_section(
        first,
        encoder_attention_back,
        (ids, returned, w_out, q, k_lo, v_lo, k_a, k_b, v_a, v_b, w_a, w_b),
        [grads_long, grads_long],
        spaces={0: SMEM},
        scratch=[pltpu.VMEM((2, 2304, HALF), BF), pltpu.SemaphoreType.DMA((2,))],
        fetch=(2, 5, 8, 10, 4, 6, 9, 11, 7),
        far_outs=True,
    )
    enc_far = swap(enc_other, "core", (0,))
    up_grad, up_gain = on_section(
        first,
        encoder_upper_back,
        (ids, up_a, up_b, w_qkv, gain_pair, enc_grads, enc_other),
        [tall, ((1, D), F32)],
        spaces={0: SMEM},
        fetch=(5, (3, 1), 6, (3, 2), 1, 2),
    )
    up_arrived = along(up_grad, 1)
    ff_far_a, ff_far_b, up_gain = lax.optimization_barrier((ff_far_a, ff_far_b, up_gain))
    from_left = plane_shift(ff_far_a, 0, 1)
    from_right = plane_shift(ff_far_b, 0, -1)
    outs = [((4, 256, HALF), BF)] * 4
    blocks = lax.cond(
        first,
        lambda: call(
            encoder_weights,
            (ids, packed, packed_far, enc_grads, enc_far, up_gain),
            outs,
            spaces={0: SMEM, 5: pl.ANY},
            fetch=(3, 4, 1, 2),
        ),
        lambda: call(latent_weights, (ids, packed, packed_far, lat_grads), outs, spaces={0: SMEM}),
    )
    last, from_left, from_right = lax.optimization_barrier((blocks[3], from_left, from_right))
    blocks = [*blocks[:3], last]
    got, up_arrived = lax.optimization_barrier((exchange(blocks, 0), up_arrived))
    low_outs = [((rows, D), F32), tall, ((2, D), F32)]

    def lower_grads():
        parts = call(
            encoder_lower_back,
            (ids, returned, own_rows, lower, w_qkv, gain_pair, enc_grads, enc_other, blocks[0]),
            low_outs,
            spaces={0: SMEM, 8: pl.ANY},
            fetch=(6, 7, (4, 0), (4, 1), (4, 2), 3),
        )
        return (*parts, *nothing([ff_block, ff_block]))

    def ff_middle():
        added = call(
            ff_add, (ff_right, ff_left, from_left, from_right, blocks[0]), [ff_block, ff_block], spaces={4: pl.ANY}
        )
        return (*nothing(low_outs), *added)

    patch_grad, low_grad, encoder_gain, ff_right_sum, ff_left_sum = lax.cond(first, lower_grads, ff_middle)
    line = [((272, HALF), BF)]
    blocks = call(
        attn_sum_first_gain,
        (ids, blocks[0], *got, encoder_gain, up_gain, latent_gain),
        line * 4,
        spaces={0: SMEM},
    )
    ff_right_sum, ff_left_sum, _ = lax.optimization_barrier((ff_right_sum, ff_left_sum, blocks))
    from_left = plane_shift(ff_right_sum, 0, 1, (1,))
    from_right = plane_shift(ff_left_sum, 0, -1, (1,))
    (block,) = call(sum_all, (blocks[0], *exchange(blocks, 1)), line)
    byte_grad = jnp.where(first, low_grad, up_arrived)
    patch_out = jnp.where(first, patch_grad, latents)
    from_left, from_right, block, byte_grad, patch_out = lax.optimization_barrier(
        (from_left, from_right, block, byte_grad, patch_out)
    )
    ff_line = ((3 * share, HALF), BF)
    ff_blocks = on_section(
        second, ff_sum_first, (ids, ff_own, from_left, from_right), [ff_line] * 4, spaces={0: SMEM}
    )
    ff_got = exchange(ff_blocks, 1)
    across, ff_got = lax.optimization_barrier((swap(block, "zh"), ff_got))
    (block,) = call(sum_all, (block, across), line)
    (block,) = call(stack_rows, collect(block, 1), [((1040, HALF), BF)])
    block, _ = lax.optimization_barrier((block, swap(block[0:16], "core")))
    pieces = collect(block, 0)
    own_far = swap(block, "core")
    (ff_sum,) = on_section(second, ff_sum_second, (ff_blocks[0], *ff_got), [ff_line])
    ff_sum = ff_sum.reshape(3, 2, share // 2, HALF)
    ff_far = swap(pick(ff_sum, 1 - zh, 1), "zh")
    ff_sum = (pick(ff_sum, zh, 1).astype(F32) + ff_far.astype(F32)).astype(BF).reshape(3, 2, share // 4, HALF)
    ff_mine = pick(ff_sum, core, 1)
    ff_far = swap(pick(ff_sum, 1 - core, 1), "core")

    def ff_result():
        low, high = jnp.where(core == 0, ff_mine, ff_far), jnp.where(core == 0, ff_far, ff_mine)
        return jnp.swapaxes(jnp.concatenate([low, high], 2), 0, 1).astype(F32)

    ff_grad = lax.cond(second, ff_result, lambda: jnp.zeros((share // 4, 3, D), F32))
    ff_grad, *pieces = lax.optimization_barrier((ff_grad, *pieces))
    pieces = pieces + [own_far] + [swap(p, "core") for p in pieces[1:]]
    whole = lambda p: pl.BlockSpec(p.shape, lambda i, n=p.ndim: (0,) * n)
    total_qkv, total_out, total_gain = pl.pallas_call(
        final_attn,
        grid=(4,),
        out_shape=[
            jax.ShapeDtypeStruct((D, 3 * D), F32),
            jax.ShapeDtypeStruct((D, D), F32),
            jax.ShapeDtypeStruct((2, D), F32),
        ],
        in_specs=[pl.BlockSpec(memory_space=SMEM)] + [whole(p) for p in pieces],
        out_specs=[
            pl.BlockSpec((256, 3 * D), lambda i: (i, 0)),
            pl.BlockSpec((256, D), lambda i: (i, 0)),
            pl.BlockSpec((2, D), lambda i: (0, 0)),
        ],
        compiler_params=pltpu.CompilerParams(vmem_limit_bytes=FINAL_VMEM),
    )(ids, *pieces)
    return (
        patch_out.reshape(1, micro, 1, seq, D),
        byte_grad.reshape(micro, 1, half_bytes, D),
        total_qkv[None],
        total_out[None],
        total_gain[None],
        ff_grad[None],
    )


def solution(mesh):
    fine = Mesh(mesh.devices.reshape(2, 4, 4, 2, 2), ("s",) + BATCH)
    in_specs = (
        P("s", None, BATCH, None, None),
        P(None, BATCH, "s", None),
        P(None, BATCH, None),
        P(None, BATCH, None),
        P("s", None, None),
        P("s", None, None),
        P("s", None, None),
        P(),
    )
    out_specs = (
        P("s", None, BATCH, None, None),
        P(None, BATCH, "s", None),
        P("s", None, None),
        P("s", None, None),
        P("s", None, None),
        P("s", BATCH, None, None),
    )
    return jax.shard_map(shards, mesh=fine, in_specs=in_specs, out_specs=out_specs, check_vma=False)
```

```python
import functools
import math

import jax
import jax.numpy as jnp
from jax import lax
from jax.experimental import pallas as pl
from jax.experimental.pallas import tpu as pltpu
from jax.sharding import Mesh
from jax.sharding import PartitionSpec as P

HD = 64
SCALE = HD**-0.5
EPS = 1e-05
NEG = -1e30
BATCH = ("y", "x", "zh", "core")
BF = jnp.bfloat16
F32 = jnp.float32
D = 1024
HALF = 512
GROUP = 256
FINAL_VMEM = 32 * 1024 * 1024


UNITS = 2816
PACK_NORMS = 3 * UNITS
PACK_LEFT = PACK_NORMS + 4 * 256
PACK_GRADS = PACK_LEFT + 2 * D
PACK_ROWS = PACK_GRADS + 4 * 512


def nn(a, b):
    return lax.dot_general(a, b, (((1,), (0,)), ((), ())), preferred_element_type=F32)


def nt(a, b):
    return lax.dot_general(a, b, (((1,), (1,)), ((), ())), preferred_element_type=F32)


def tn(a, b):
    return lax.dot_general(a, b, (((0,), (0,)), ((), ())), preferred_element_type=F32)


def inverse_rms(x):
    return lax.rsqrt(jnp.mean(x * x, axis=-1, keepdims=True) + EPS)


def norm_back(x, gain, up):
    r = inverse_rms(x)
    scaled = up * gain
    inner = jnp.mean(scaled * x, axis=-1, keepdims=True)
    return r * (scaled - x * (r * r * inner)), up * (x * r)


def stack_heads(rows):
    head = lax.broadcasted_iota(jnp.int32, rows.shape, 1) // HD
    return jnp.concatenate([jnp.where(head == h, rows, jnp.zeros_like(rows)) for h in range(4)], 0)


def unstack_heads(stacked):
    head = lax.broadcasted_iota(jnp.int32, (HD, GROUP), 1) // HD
    out = stacked[0:HD]
    for h in range(1, 4):
        out = jnp.where(head == h, stacked[h * HD : (h + 1) * HD], out)
    return out


def softmax_columns(scores):
    top = functools.reduce(jnp.maximum, [jnp.max(s, axis=0, keepdims=True) for s in scores])
    parts = [jnp.exp(s - top) for s in scores]
    inverse = 1.0 / sum(jnp.sum(p, axis=0, keepdims=True) for p in parts)
    return [(p * inverse).astype(BF) for p in parts]


def encode_lower(patch, low, w_qkv, gains, pn, q, bn, k, v):
    x = patch[...].astype(F32)
    normed = (x * inverse_rms(x) * gains[0:1]).astype(BF)
    pn[...] = normed
    q[...] = nn(normed, w_qkv.block(0)[...]).astype(BF)
    for i in range(2):
        at = pl.ds(i * 256, 256)
        b = low[at, :].astype(F32)
        normed = (b * inverse_rms(b) * gains[1:2]).astype(BF)
        bn[at, :] = normed
        k[at, :] = nn(normed, w_qkv.block(1)[...]).astype(BF)
        v[at, :] = nn(normed, w_qkv.block(2)[...]).astype(BF)


def encode_rest(m, patch, up, w_qkv, w_out, gains, bounds, q, k_lo, v_lo, hb, o1, weights, bn, k, v):
    b = up[...].astype(F32)
    normed = (b * inverse_rms(b) * gains[1:2]).astype(BF)
    bn[...] = normed
    k[...] = nn(normed, w_qkv.block(1)[...]).astype(BF)
    v[...] = nn(normed, w_qkv.block(2)[...]).astype(BF)
    spot = lax.broadcasted_iota(jnp.int32, (256, GROUP), 0)
    start = bounds[m, 0:1, :]
    end = bounds[m, 1:2, :]
    inside = [(spot + h * 256 >= start) & (spot + h * 256 < end) for h in range(2)]
    low_at = slice(m * 256, (m + 1) * 256)
    rows = slice(m * HD, (m + 1) * HD)
    for g in range(4):
        lanes = slice(g * GROUP, (g + 1) * GROUP)
        stacked = stack_heads(q[rows, lanes] * BF(SCALE))
        scores = [
            jnp.where(inside[h], nt(keys, stacked), NEG)
            for h, keys in enumerate((k_lo[low_at, lanes], k[:, lanes]))
        ]
        w = softmax_columns(scores)
        weights[g * 2] = w[0]
        weights[g * 2 + 1] = w[1]
        mixed = tn(w[0], v_lo[low_at, lanes]) + tn(w[1], v[:, lanes])
        o1[:, lanes] = unstack_heads(mixed).astype(BF)
    hb[...] = (patch[rows, :].astype(F32) + nn(o1[...], w_out[...])).astype(BF)


def latent_layer(
    ids, hb_a, hb_b, cot, allowed, w_qkv, w_out, gains, w_ff, d_hidden,
    latents, dhb, gain_grad, norms, grads, packed,
    qkv, weights, o2, ff_buf, acc_out, acc_norm, dqkv, sems,
):
    core = ids[0]
    units = w_ff.shape[1]
    step = 256
    parts = 4
    part = units // parts

    fetches = []
    for i in range(parts):
        at = slice(i * part, (i + 1) * part)
        fetches.append(pltpu.make_async_copy(w_ff.at[:, at, :], ff_buf.at[:, at, :], sems.at[i]))
        fetches[-1].start()
    x = jnp.concatenate([hb_a[...], hb_b[...]], 0).astype(F32)
    normed = (x * inverse_rms(x) * gains[0:1]).astype(BF)
    packed[PACK_LEFT : PACK_LEFT + D, :] = normed.T
    for j in range(3):
        qkv[:, j * D : (j + 1) * D] = nn(normed, w_qkv.block(j)[...]).astype(BF)
    for m in range(2):
        rows = slice(m * HD, (m + 1) * HD)
        for g in range(4):
            lanes = slice(g * GROUP, (g + 1) * GROUP)
            k_lanes = slice(D + g * GROUP, D + (g + 1) * GROUP)
            v_lanes = slice(2 * D + g * GROUP, 2 * D + (g + 1) * GROUP)
            stacked = stack_heads(qkv[rows, lanes] * BF(SCALE))
            scores = jnp.where(allowed[m] > 0.5, nt(qkv[rows, k_lanes], stacked), NEG)
            (w,) = softmax_columns([scores])
            weights[m * 4 + g] = w
            o2[rows, lanes] = unstack_heads(tn(w, qkv[rows, v_lanes])).astype(BF)
    packed[PACK_LEFT + D : PACK_LEFT + 2 * D, :] = o2[...].T
    after = x + nn(o2[...], w_out[...])
    yn = (after * inverse_rms(after) * gains[1:2]).astype(BF)
    c = cot[...]
    for h in range(2):

        @pl.when(core == h)
        def _(h=h):
            norms[0:128, :] = yn[:, h * HALF : (h + 1) * HALF]
            norms[128:256, :] = c[:, h * HALF : (h + 1) * HALF]

        @pl.when(core != h)
        def _(h=h):
            for b in range(4):
                lanes = slice(h * HALF + b * 128, h * HALF + (b + 1) * 128)
                packed[PACK_NORMS + b * 256 : PACK_NORMS + b * 256 + 128, :] = yn[:, lanes]
                packed[PACK_NORMS + b * 256 + 128 : PACK_NORMS + (b + 1) * 256, :] = c[:, lanes]

    for copy in fetches:
        copy.wait()
    acc_out[...] = after
    for i in range(units // step):
        at = slice(i * step, (i + 1) * step)
        gate = nt(yn, ff_buf[0, at, :])
        upward = nt(yn, ff_buf[1, at, :])
        du = d_hidden[:, at]
        sig = 1.0 / (1.0 + jnp.exp(-gate))
        active = gate * sig
        hidden = (active * upward).astype(BF)
        d_gate = (du * upward * (sig * (1.0 + gate * (1.0 - sig)))).astype(BF)
        d_up = (du * active).astype(BF)
        for j, value in enumerate((d_gate, d_up, hidden)):
            packed[i * step + j * units : (i + 1) * step + j * units, :] = value.T
        acc_out[...] += nn(hidden, ff_buf[2, at, :])
        back = nn(d_gate, ff_buf[0, at, :]) + nn(d_up, ff_buf[1, at, :])
        if i == 0:
            acc_norm[...] = back
        else:
            acc_norm[...] += back
    latents[...] = acc_out[...]
    back, gain_rows = norm_back(after, gains[1:2], acc_norm[...])
    gain_grad[1:2, :] = jnp.sum(gain_rows, axis=0, keepdims=True)
    d_after = c.astype(F32) + back
    da = d_after.astype(BF)
    d_mixed = nt(da, w_out[...]).astype(BF)
    for m in range(2):
        rows = slice(m * HD, (m + 1) * HD)
        for g in range(4):
            lanes = slice(g * GROUP, (g + 1) * GROUP)
            k_lanes = slice(D + g * GROUP, D + (g + 1) * GROUP)
            v_lanes = slice(2 * D + g * GROUP, 2 * D + (g + 1) * GROUP)
            q_stacked = stack_heads(qkv[rows, lanes] * BF(SCALE))
            o_stacked = stack_heads(d_mixed[rows, lanes])
            w_low = weights[m * 4 + g]
            w = w_low.astype(F32)
            dw = nt(qkv[rows, v_lanes], o_stacked)
            inner = jnp.sum(dw * w, axis=0, keepdims=True)
            ds = (w * (dw - inner)).astype(BF)
            dqkv[rows, lanes] = (unstack_heads(tn(ds, qkv[rows, k_lanes])) * SCALE).astype(BF)
            dqkv[rows, k_lanes] = nn(ds, q_stacked).astype(BF)
            dqkv[rows, v_lanes] = nn(w_low, o_stacked).astype(BF)
    d_normed = sum(nt(dqkv[:, j * D : (j + 1) * D], w_qkv.block(j)[...]) for j in range(3))
    back, gain_rows = norm_back(x, gains[0:1], d_normed)
    gain_grad[0:1, :] = jnp.sum(gain_rows, axis=0, keepdims=True)
    dhb[...] = (d_after + back).astype(BF)
    for h in range(2):
        pieces = (
            dqkv[:, h * HALF : (h + 1) * HALF],
            da[:, h * HALF : (h + 1) * HALF],
            dqkv[:, D + h * HALF : D + (h + 1) * HALF],
            dqkv[:, 2 * D + h * HALF : 2 * D + (h + 1) * HALF],
        )

        @pl.when(core == h)
        def _(pieces=pieces):
            for i, value in enumerate(pieces):
                grads[i * 128 : (i + 1) * 128, :] = value

        @pl.when(core != h)
        def _(pieces=pieces):
            for i, value in enumerate(pieces):
                for b in range(4):
                    first = PACK_GRADS + b * 512 + i * 128
                    packed[first : first + 128, :] = value[:, b * 128 : (b + 1) * 128]


def hidden_back(cot, w_ff, d_hidden, buffer, sems):
    parts = 4
    part = w_ff.shape[1] // parts
    copies = []
    for i in range(parts):
        at = slice(i * part, (i + 1) * part)
        copies.append(pltpu.make_async_copy(w_ff.at[2, at, :], buffer.at[at, :], sems.at[i]))
        copies[-1].start()
    for copy in copies:
        copy.wait()
    for i in range(w_ff.shape[1] // 256):
        at = slice(i * 256, (i + 1) * 256)
        d_hidden[:, at] = nt(cot[...], buffer[at, :])


def encoder_attention_back(
    ids, dhb, w_out, q, k_lo, v_lo, k_a, k_b, v_a, v_b, w_a, w_b, mine, other, both, sems
):
    d_mixed = nt(dhb[...], w_out[...]).astype(BF)
    for g in range(4):
        lanes = slice(g * GROUP, (g + 1) * GROUP)
        out_lanes = slice((g % 2) * GROUP, (g % 2 + 1) * GROUP)
        half = jnp.where(ids[0] == g // 2, 0, 1)

        def put(at, value, half=half, out_lanes=out_lanes):
            both[half, at, out_lanes] = value

        put(slice(128, 256), dhb[:, lanes])
        for m, (k_up, v_up, weights) in enumerate(((k_a, v_a, w_a), (k_b, v_b, w_b))):
            rows = slice(m * HD, (m + 1) * HD)
            low_at = slice(m * 256, (m + 1) * 256)
            q_stacked = stack_heads(q[rows, lanes] * BF(SCALE))
            o_stacked = stack_heads(d_mixed[rows, lanes])
            low = [weights[g * 2 + h] for h in range(2)]
            w = [piece.astype(F32) for piece in low]
            dw = [nt(values, o_stacked) for values in (v_lo[low_at, lanes], v_up[:, lanes])]
            inner = sum(jnp.sum(a * b, axis=0, keepdims=True) for a, b in zip(dw, w))
            ds = [(b * (a - inner)).astype(BF) for a, b in zip(dw, w)]
            dq = tn(ds[0], k_lo[low_at, lanes]) + tn(ds[1], k_up[:, lanes])
            put(rows, (unstack_heads(dq) * SCALE).astype(BF))
            for h in range(2):
                base = h * HALF + m * 256
                put(slice(256 + base, 512 + base), nn(ds[h], q_stacked).astype(BF))
                put(slice(1280 + base, 1536 + base), nn(low[h], o_stacked).astype(BF))
    copies = [pltpu.make_async_copy(both.at[i], out, sems.at[i]) for i, out in enumerate((mine, other))]
    for copy in copies:
        copy.start()
    for copy in copies:
        copy.wait()


def both_columns(core, block, w_qkv):
    return [
        w_qkv.block(block)[:, pl.ds(pl.multiple_of(which * HALF, HALF), HALF)] for which in (core, 1 - core)
    ]


def bytes_back(core, h, source, w_qkv, gains, grads):
    d_norm = sum(
        nt(ref[1024 * block - 768 + h * HALF : 1024 * block - 256 + h * HALF, :], columns)
        for block in (1, 2)
        for ref, columns in zip(grads, both_columns(core, block, w_qkv))
    )
    back, gain_rows = norm_back(source.astype(F32), gains[1:2], d_norm)
    return back.astype(BF), jnp.sum(gain_rows, axis=0, keepdims=True)


def encoder_upper_back(ids, up_a, up_b, w_qkv, gains, mine, other, up_grad, gain_grad):
    source = jnp.concatenate([up_a[...], up_b[...]], 0)
    back, rows = bytes_back(ids[0], 1, source, w_qkv, gains, (mine, other))
    up_grad[...] = back
    gain_grad[...] = rows


def encoder_lower_back(
    ids, dhb, patch, low, w_qkv, gains, mine, other, after, patch_grad, low_grad, gain_grad
):
    core = ids[0]
    up_norm = sum(nt(ref[0:128, :], columns) for ref, columns in zip((mine, other), both_columns(core, 0, w_qkv)))
    back, gain_rows = norm_back(patch[...].astype(F32), gains[0:1], up_norm)
    gain_grad[0:1, :] = jnp.sum(gain_rows, axis=0, keepdims=True)
    patch_grad[...] = dhb[...].astype(F32) + back
    back, rows = bytes_back(core, 0, low[...], w_qkv, gains, (mine, other))
    low_grad[...] = back
    gain_grad[1:2, :] = rows


def turn_encoder(pn, o_a, o_b, bn_lo, bn_a, bn_b, packed):
    for b, rows in enumerate([bn_lo[i * 128 : (i + 1) * 128, :] for i in range(4)]
                             + [ref[i * 128 : (i + 1) * 128, :] for ref in (bn_a, bn_b) for i in range(2)]):
        packed[b * D : (b + 1) * D, :] = rows.T
    packed[PACK_LEFT : PACK_LEFT + D, :] = pn[...].T
    packed[PACK_LEFT + D : PACK_LEFT + 2 * D, :] = jnp.concatenate([o_a[...], o_b[...]], 0).T


def rows_of_both(left, left_far, at):
    return jnp.concatenate([left[at, :], left_far[at, :]], 1)


def below(near, far, rows):
    return jnp.concatenate([near[rows, :], far[rows, :]], 0)


def encoder_weights(ids, packed, packed_far, near, far, after, *blocks):
    u = ids[1]
    queries = below(near, far, slice(0, 128))
    outputs = below(near, far, slice(128, 256))
    for k in range(4):
        first = lax.rem(u + k, 4) * 256

        def at(base, first=first):
            return pl.ds(pl.multiple_of(first + base, 256), 256)

        blocks[k][0] = nn(rows_of_both(packed, packed_far, at(PACK_LEFT)), queries).astype(BF)
        blocks[k][3] = nn(rows_of_both(packed, packed_far, at(PACK_LEFT + D)), outputs).astype(BF)
        lefts = [jnp.concatenate([ref[at(b * D), :] for b in range(8)], 1) for ref in (packed, packed_far)]
        for block in (1, 2):
            rows = slice(1024 * block - 768, 1024 * block + 256)
            blocks[k][block] = (nn(lefts[0], near[rows, :]) + nn(lefts[1], far[rows, :])).astype(BF)


def unpack(packed, first, rows):
    return jnp.concatenate([packed[first + b * rows : first + (b + 1) * rows, :] for b in range(4)], 1)


def latent_weights(ids, packed, packed_far, near, *blocks):
    u = ids[1]
    far = unpack(packed_far, PACK_GRADS, 512)
    rights = [jnp.concatenate([near[i * 128 : (i + 1) * 128, :], far[i * 128 : (i + 1) * 128, :]], 0) for i in range(4)]
    for k in range(4):
        first = PACK_LEFT + lax.rem(u + k, 4) * 256
        at = pl.ds(pl.multiple_of(first, 256), 256)
        low_at = pl.ds(pl.multiple_of(first + D, 256), 256)
        for block, (source, i) in enumerate(((at, 0), (at, 2), (at, 3), (low_at, 1))):
            blocks[k][block] = nn(rows_of_both(packed, packed_far, source), rights[i]).astype(BF)


def ff_weights_grad(ids, packed, packed_far, norms, own, right, left, far_a, far_b):
    core, u = ids[0], ids[1]
    share = UNITS // 16
    far = unpack(packed_far, PACK_NORMS, 256)
    normed = jnp.concatenate([norms[0:128, :], far[0:128, :]], 0)
    cot = jnp.concatenate([norms[128:256, :], far[128:256, :]], 0)
    for k in range(4):
        there = lax.rem(u + k, 4)
        for j in range(3):
            parts = []
            for v in range(4):
                chunk = jnp.where(core == 0, there * 4 + v, v * 4 + there)
                at = pl.ds(pl.multiple_of(j * UNITS + chunk * share, 16), share)
                parts.append(rows_of_both(packed, packed_far, at))
            value = nn(jnp.concatenate(parts, 0), normed if j < 2 else cot).astype(BF)
            rows = slice(j * share, (j + 1) * share)
            for v in range(4):
                piece = value[v * share : (v + 1) * share, :]
                if k == 2:
                    far_a[v, rows, :] = piece[:, :GROUP]
                    far_b[v, rows, :] = piece[:, GROUP:]
                else:
                    (own, right, None, left)[k][v, rows, :] = piece


def ff_add(right, left, from_left, from_right, after, new_right, new_left):
    new_right[:, :, 0:GROUP] = (right[:, :, 0:GROUP].astype(F32) + from_left[...].astype(F32)).astype(BF)
    new_right[:, :, GROUP:] = right[:, :, GROUP:]
    new_left[:, :, 0:GROUP] = left[:, :, 0:GROUP]
    new_left[:, :, GROUP:] = (left[:, :, GROUP:].astype(F32) + from_right[...].astype(F32)).astype(BF)


def sum_four(own, a, b, c):
    return own.astype(F32) + a.astype(F32) + b.astype(F32) + c.astype(F32)


def pack_gain(value):
    high = value.astype(BF)
    low = (value - high.astype(F32)).astype(BF)
    return jnp.concatenate(
        [high.astype(F32), low.astype(F32), jnp.zeros((8, HALF), F32)], 0
    ).astype(BF)


def unpack_gain(rows):
    rows = rows.astype(F32)
    return rows[0:4] + rows[4:8]


GAIN_AT = slice(256, 272)


def attn_sum_first(ids, own, a, b, c, *outs):
    v = ids[2]
    for k in range(4):
        at = pl.ds(pl.multiple_of(lax.rem(v + k, 4) * HD, HD), HD)
        for block in range(4):
            outs[k][block * HD : (block + 1) * HD, :] = sum_four(
                own[block, at, :], a[block, at, :], b[block, at, :], c[block, at, :]
            ).astype(BF)


def attn_sum_first_gain(ids, own, a, b, c, enc_gain, up_gain, lat_gain, *outs):
    attn_sum_first(ids, own, a, b, c, *outs)
    first = ids[4] == 0
    gain = jnp.where(
        first, jnp.concatenate([enc_gain[0:1, :], enc_gain[1:2, :] + up_gain[...]], 0), lat_gain[...]
    )
    halves = [gain[i : i + 1, h * HALF : (h + 1) * HALF] for i in range(2) for h in range(2)]
    packed = pack_gain(jnp.concatenate(halves, 0))
    for out in outs:
        out[GAIN_AT, :] = packed


def sum_all(*refs):
    refs, out = refs[:-1], refs[-1]
    out[0:256, :] = sum(ref[0:256, :].astype(F32) for ref in refs).astype(BF)
    out[GAIN_AT, :] = pack_gain(sum(unpack_gain(ref[GAIN_AT, :]) for ref in refs))


def stack_rows(*refs):
    refs, out = refs[:-2], refs[-1]
    for j, ref in enumerate(refs):
        out[j * 256 : (j + 1) * 256, :] = ref[0:256, :]
    out[1024:1040, :] = refs[0][GAIN_AT, :]


def ff_sum_first(ids, own, a, b, *outs):
    v = ids[2]
    for k in range(4):
        at = lax.rem(v + k, 4)
        outs[k][...] = (own[at].astype(F32) + a[at].astype(F32) + b[at].astype(F32)).astype(BF)


def ff_sum_second(own, a, b, c, out):
    out[...] = sum_four(own[...], a[...], b[...], c[...]).astype(BF)


def final_attn(ids, *refs):
    pieces, (qkv, out, gain) = refs[:8], refs[8:]
    step = pl.program_id(0)
    for side in range(2):
        core = ids[0] if side == 0 else 1 - ids[0]
        u = ids[1] if side == 0 else ids[2]
        v = ids[2] if side == 0 else ids[1]
        for k in range(4):
            piece = pieces[side * 4 + k]

            @pl.when(lax.rem(u + k, 4) == step)
            def _(piece=piece, v=v, core=core):
                for j in range(4):
                    at = pl.ds(pl.multiple_of(lax.rem(v + j, 4) * HD, HD), HD)
                    for block in range(4):
                        target, column = (qkv, block * D) if block < 3 else (out, 0)
                        lanes = pl.ds(pl.multiple_of(core * HALF + column, HALF), HALF)
                        first = j * 256 + block * HD
                        target[at, lanes] = piece[first : first + HD, :].astype(F32)

    mine = sum(unpack_gain(piece[1024:1040, :]) for piece in pieces[:4])
    other = sum(unpack_gain(piece[1024:1040, :]) for piece in pieces[4:])
    total = mine + other
    for i in range(2):
        for h in range(2):
            gain[i : i + 1, h * HALF : (h + 1) * HALF] = total[2 * i + h : 2 * i + h + 1, :]


SMEM = pltpu.MemorySpace.SMEM
VMEM = pltpu.MemorySpace.VMEM


def size(shape, dtype):
    return math.prod(shape) * jnp.dtype(dtype).itemsize


class Arriving:
    def __init__(self, copy, buffer):
        self.copy, self.buffer, self.here = copy, buffer, False

    def ready(self):
        if not self.here:
            self.copy.wait()
            self.here = True
        return self.buffer

    def __getitem__(self, index):
        return self.ready()[index]


class ArrivingBlocks:
    def __init__(self, blocks):
        self.blocks = blocks

    def block(self, j):
        return self.blocks[j]


def fetching(kernel, n_args, n_outs, plan):
    def wrapped(*refs):
        args, outs, rest = list(refs[:n_args]), refs[n_args : n_args + n_outs], refs[n_args + n_outs :]
        scratch, buffers, sems = rest[: len(rest) - len(plan) - 1], rest[len(rest) - len(plan) - 1 : -1], rest[-1]
        arriving = []
        blocks = {}
        for i, (a, j) in enumerate(plan):
            source = refs[a] if j is None else refs[a].at[:, j * D : (j + 1) * D]
            copy = pltpu.make_async_copy(source, buffers[i], sems.at[i])
            copy.start()
            arriving.append(Arriving(copy, buffers[i]))
            if j is None:
                args[a] = arriving[-1]
            else:
                blocks.setdefault(a, {})[j] = arriving[-1]
        for a, found in blocks.items():
            args[a] = ArrivingBlocks(found)
        kernel(*args, *outs, *scratch)
        for value in arriving:
            value.ready()

    return wrapped


def call(kernel, args, outs, scratch=(), spaces=None, spare=6, fetch=(), far_outs=False):
    spaces = dict(spaces or {})
    scratch = list(scratch)
    plan = [f if isinstance(f, tuple) else (f, None) for f in fetch]
    if plan:
        for a, j in plan:
            spaces[a] = pl.ANY
            shape = args[a].shape if j is None else (args[a].shape[0], D)
            scratch.append(pltpu.VMEM(shape, args[a].dtype))
        scratch.append(pltpu.SemaphoreType.DMA((len(plan),)))
        kernel = fetching(kernel, len(args), len(outs), plan)
    vmem = sum(size(a.shape, a.dtype) for i, a in enumerate(args) if i not in spaces)
    vmem += 0 if far_outs else sum(size(*o) for o in outs)
    vmem += sum(size(s.shape, s.dtype) for s in scratch if hasattr(s, "shape") and s.memory_space == VMEM)
    specs = [pl.BlockSpec(memory_space=spaces.get(i, VMEM)) for i in range(len(args))]
    return pl.pallas_call(
        kernel,
        out_shape=[jax.ShapeDtypeStruct(s, t) for s, t in outs],
        in_specs=specs,
        out_specs=[pl.BlockSpec(memory_space=pl.ANY if far_outs else VMEM) for _ in outs],
        scratch_shapes=scratch,
        compiler_params=pltpu.CompilerParams(vmem_limit_bytes=vmem + spare * 1024 * 1024),
    )(*args)


def nothing(outs):
    def kernel(*refs):
        pass

    return pl.pallas_call(
        kernel,
        out_shape=[jax.ShapeDtypeStruct(s, t) for s, t in outs],
        out_specs=[pl.BlockSpec(memory_space=pl.ANY) for _ in outs],
    )()


def on_section(flag, kernel, args, outs, **rest):
    return lax.cond(
        flag, lambda: call(kernel, args, outs, **rest), lambda: nothing(outs)
    )


def along(value, by):
    return lax.ppermute(value, "s", [(0, 1)] if by > 0 else [(1, 0)])


def swap(value, axis, sections=(0, 1)):
    pairs = [(s * 2 + i, s * 2 + 1 - i) for s in sections for i in range(2)]
    return lax.ppermute(value, ("s", axis), pairs)


def plane_shift(value, which, by, sections=(0, 1)):
    pairs = []
    for s in sections:
        for y in range(4):
            for x in range(4):
                for core in range(2):
                    ty, tx = ((y + by) % 4, x) if core == which else (y, (x + by) % 4)
                    pairs.append((((s * 4 + y) * 4 + x) * 2 + core, ((s * 4 + ty) * 4 + tx) * 2 + core))
    return lax.ppermute(value, ("s", "y", "x", "core"), pairs)


def exchange(blocks, which, sections=(0, 1)):
    return [plane_shift(blocks[k], which, k, sections) for k in (1, 2, 3)]


def collect(block, which):
    return [block] + [plane_shift(block, which, -k) for k in (1, 2, 3)]


def pick(stack, index, dim):
    return lax.dynamic_index_in_dim(stack, index, dim, keepdims=False)


def shards(patch_io, byte_states, patch_lengths, patch_live, attn_qkv, attn_out, gains, ff_weights):
    section = lax.axis_index("s")
    core = lax.axis_index("core")
    zh = lax.axis_index("zh")
    y, x = lax.axis_index("y"), lax.axis_index("x")
    first = section == 0
    second = section == 1
    ids = jnp.stack([core, jnp.where(core == 0, y, x), jnp.where(core == 0, x, y), zh, section])
    ids = ids.astype(jnp.int32)
    w_qkv = attn_qkv[0]
    w_out = attn_out[0]
    gain_pair = gains[0]
    micro, seq = patch_io.shape[1], patch_io.shape[3]
    half_bytes = byte_states.shape[2]
    units = ff_weights.shape[0]
    rows = micro * seq
    own_rows = patch_io.reshape(rows, D)
    up_a = along(byte_states[0, 0], -1)
    up_b = along(byte_states[1, 0], -1)
    lower = byte_states.reshape(micro * half_bytes, D)
    w_ff = jnp.swapaxes(ff_weights, 0, 1)
    lengths = patch_lengths[:, 0]
    live = patch_live[:, 0]
    ends = jnp.cumsum(lengths, axis=1)
    bounds = jnp.tile(jnp.stack([ends - lengths, ends], 1), (1, 1, 4))
    places = lax.iota(jnp.int32, seq)
    causal = places[:, None] <= places[None, :]
    diagonal = places[:, None] == places[None, :]
    allowed = causal[None] & ((live[:, :, None] == 1) | diagonal[None])
    allowed = lax.optimization_barrier(jnp.tile(allowed.astype(F32), (1, 1, 4)))

    wide = ((rows, D), BF)
    short = ((seq, D), BF)
    tall = ((micro * half_bytes, D), BF)
    piece = ((half_bytes, D), BF)
    (d_hidden,) = on_section(
        second,
        hidden_back,
        (own_rows, w_ff),
        [((rows, units), F32)],
        spaces={1: pl.ANY},
        scratch=[pltpu.VMEM((units, D), BF), pltpu.SemaphoreType.DMA((4,))],
    )
    pn, q, bn_lo, k_lo, v_lo = on_section(
        first,
        encode_lower,
        (own_rows, lower, w_qkv, gain_pair),
        [wide, wide, tall, tall, tall],
        fetch=((2, 0), 1, (2, 1), (2, 2)),
    )
    rest = []
    for m, up in enumerate((up_a, up_b)):
        rest.append(
            on_section(
                first,
                functools.partial(encode_rest, m),
                (own_rows, up, w_qkv, w_out, gain_pair, bounds, q, k_lo, v_lo),
                [short, short, ((8, 256, GROUP), BF), piece, piece, piece],
                fetch=((2, 1), (2, 2), 7, 8, 3),
            )
        )
    (hb_a, o_a, w_a, bn_a, k_a, v_a), (hb_b, o_b, w_b, bn_b, k_b, v_b) = rest
    arrived = [along(hb_a, 1), along(hb_b, 1)]

    latent_outs = [
        ((rows, D), F32), wide, ((2, D), F32), ((256, HALF), BF), ((512, HALF), BF), ((PACK_ROWS, rows), BF),
    ]

    def latent():
        return call(
            latent_layer,
            (ids, *arrived, own_rows, allowed, w_qkv, w_out, gain_pair, w_ff, d_hidden),
            latent_outs,
            spaces={0: SMEM, 8: pl.ANY},
            fetch=((5, 0), (5, 1), (5, 2), 6),
            scratch=[
                pltpu.VMEM((rows, 3 * D), BF),
                pltpu.VMEM((8, HD, GROUP), BF),
                pltpu.VMEM((rows, D), BF),
                pltpu.VMEM((3, units, D), BF),
                pltpu.VMEM((rows, D), F32),
                pltpu.VMEM((rows, D), F32),
                pltpu.VMEM((rows, 3 * D), BF),
                pltpu.SemaphoreType.DMA((4,)),
            ],
        )

    def turn():
        return nothing(latent_outs[:5]) + call(
            turn_encoder, (pn, o_a, o_b, bn_lo, bn_a, bn_b), latent_outs[5:]
        )

    latents, dhb, latent_gain, norms, lat_grads, packed = lax.cond(second, latent, turn)
    returned = along(dhb, -1)

    packed_far = swap(packed, "core")

    share = units // 16
    ff_block = ((4, 3 * share, HALF), BF)
    ff_half = ((4, 3 * share, GROUP), BF)
    ff_own, ff_right, ff_left, ff_far_a, ff_far_b = on_section(
        second,
        ff_weights_grad,
        (ids, packed, packed_far, norms),
        [ff_block, ff_block, ff_block, ff_half, ff_half],
        spaces={0: SMEM},
    )

    grads_long = ((2304, HALF), BF)
    enc_grads, enc_other = on_section(
        first,
        encoder_attention_back,
        (ids, returned, w_out, q, k_lo, v_lo, k_a, k_b, v_a, v_b, w_a, w_b),
        [grads_long, grads_long],
        spaces={0: SMEM},
        scratch=[pltpu.VMEM((2, 2304, HALF), BF), pltpu.SemaphoreType.DMA((2,))],
        fetch=(2, 5, 8, 10, 4, 6, 9, 11, 7),
        far_outs=True,
    )
    enc_far = swap(enc_other, "core", (0,))
    up_grad, up_gain = on_section(
        first,
        encoder_upper_back,
        (ids, up_a, up_b, w_qkv, gain_pair, enc_grads, enc_other),
        [tall, ((1, D), F32)],
        spaces={0: SMEM},
        fetch=(5, (3, 1), 6, (3, 2), 1, 2),
    )
    up_arrived = along(up_grad, 1)
    ff_far_a, ff_far_b, up_gain = lax.optimization_barrier((ff_far_a, ff_far_b, up_gain))
    from_left = plane_shift(ff_far_a, 0, 1)
    from_right = plane_shift(ff_far_b, 0, -1)
    outs = [((4, 256, HALF), BF)] * 4
    blocks = lax.cond(
        first,
        lambda: call(
            encoder_weights,
            (ids, packed, packed_far, enc_grads, enc_far, up_gain),
            outs,
            spaces={0: SMEM, 5: pl.ANY},
            fetch=(3, 4, 1, 2),
        ),
        lambda: call(latent_weights, (ids, packed, packed_far, lat_grads), outs, spaces={0: SMEM}),
    )
    last, from_left, from_right = lax.optimization_barrier((blocks[3], from_left, from_right))
    blocks = [*blocks[:3], last]
    got, up_arrived = lax.optimization_barrier((exchange(blocks, 0), up_arrived))
    low_outs = [((rows, D), F32), tall, ((2, D), F32)]

    def lower_grads():
        parts = call(
            encoder_lower_back,
            (ids, returned, own_rows, lower, w_qkv, gain_pair, enc_grads, enc_other, blocks[0]),
            low_outs,
            spaces={0: SMEM, 8: pl.ANY},
            fetch=(6, 7, (4, 0), (4, 1), (4, 2), 3),
        )
        return (*parts, *nothing([ff_block, ff_block]))

    def ff_middle():
        added = call(
            ff_add, (ff_right, ff_left, from_left, from_right, blocks[0]), [ff_block, ff_block], spaces={4: pl.ANY}
        )
        return (*nothing(low_outs), *added)

    patch_grad, low_grad, encoder_gain, ff_right_sum, ff_left_sum = lax.cond(first, lower_grads, ff_middle)
    line = [((272, HALF), BF)]
    blocks = call(
        attn_sum_first_gain,
        (ids, blocks[0], *got, encoder_gain, up_gain, latent_gain),
        line * 4,
        spaces={0: SMEM},
    )
    ff_right_sum, ff_left_sum, _ = lax.optimization_barrier((ff_right_sum, ff_left_sum, blocks))
    from_left = plane_shift(ff_right_sum, 0, 1, (1,))
    from_right = plane_shift(ff_left_sum, 0, -1, (1,))
    (block,) = call(sum_all, (blocks[0], *exchange(blocks, 1)), line)
    byte_grad = jnp.where(first, low_grad, up_arrived)
    patch_out = jnp.where(first, patch_grad, latents)
    from_left, from_right, block, byte_grad, patch_out = lax.optimization_barrier(
        (from_left, from_right, block, byte_grad, patch_out)
    )
    ff_line = ((3 * share, HALF), BF)
    ff_blocks = on_section(
        second, ff_sum_first, (ids, ff_own, from_left, from_right), [ff_line] * 4, spaces={0: SMEM}
    )
    ff_got = exchange(ff_blocks, 1)
    across, ff_got = lax.optimization_barrier((swap(block, "zh"), ff_got))
    (block,) = call(sum_all, (block, across), line)
    lines = collect(block, 1)
    step_in = swap(lines[3][0:16], "core")
    (block,) = call(stack_rows, (*lines, step_in), [((1040, HALF), BF)], spaces={4: pl.ANY})
    pieces = collect(block, 0)
    own_far = swap(block, "core")
    (ff_sum,) = on_section(second, ff_sum_second, (ff_blocks[0], *ff_got), [ff_line])
    ff_sum = ff_sum.reshape(3, 2, share // 2, HALF)
    ff_far = swap(pick(ff_sum, 1 - zh, 1), "zh")
    ff_sum = (pick(ff_sum, zh, 1).astype(F32) + ff_far.astype(F32)).astype(BF).reshape(3, 2, share // 4, HALF)
    ff_mine = pick(ff_sum, core, 1)
    ff_far = swap(pick(ff_sum, 1 - core, 1), "core")

    def ff_result():
        low, high = jnp.where(core == 0, ff_mine, ff_far), jnp.where(core == 0, ff_far, ff_mine)
        return jnp.swapaxes(jnp.concatenate([low, high], 2), 0, 1).astype(F32)

    ff_grad = lax.cond(second, ff_result, lambda: jnp.zeros((share // 4, 3, D), F32))
    ff_grad, *pieces = lax.optimization_barrier((ff_grad, *pieces))
    pieces = pieces + [own_far] + [swap(p, "core") for p in pieces[1:]]
    whole = lambda p: pl.BlockSpec(p.shape, lambda i, n=p.ndim: (0,) * n)
    total_qkv, total_out, total_gain = pl.pallas_call(
        final_attn,
        grid=(4,),
        out_shape=[
            jax.ShapeDtypeStruct((D, 3 * D), F32),
            jax.ShapeDtypeStruct((D, D), F32),
            jax.ShapeDtypeStruct((2, D), F32),
        ],
        in_specs=[pl.BlockSpec(memory_space=SMEM)] + [whole(p) for p in pieces],
        out_specs=[
            pl.BlockSpec((256, 3 * D), lambda i: (i, 0)),
            pl.BlockSpec((256, D), lambda i: (i, 0)),
            pl.BlockSpec((2, D), lambda i: (0, 0)),
        ],
        compiler_params=pltpu.CompilerParams(vmem_limit_bytes=FINAL_VMEM),
    )(ids, *pieces)
    return (
        patch_out.reshape(1, micro, 1, seq, D),
        byte_grad.reshape(micro, 1, half_bytes, D),
        total_qkv[None],
        total_out[None],
        total_gain[None],
        ff_grad[None],
    )


def solution(mesh):
    fine = Mesh(mesh.devices.reshape(2, 4, 4, 2, 2), ("s",) + BATCH)
    in_specs = (
        P("s", None, BATCH, None, None),
        P(None, BATCH, "s", None),
        P(None, BATCH, None),
        P(None, BATCH, None),
        P("s", None, None),
        P("s", None, None),
        P("s", None, None),
        P(),
    )
    out_specs = (
        P("s", None, BATCH, None, None),
        P(None, BATCH, "s", None),
        P("s", None, None),
        P("s", None, None),
        P("s", None, None),
        P("s", BATCH, None, None),
    )
    return jax.shard_map(shards, mesh=fine, in_specs=in_specs, out_specs=out_specs, check_vma=False)
```

```python
import functools
import math

import jax
import jax.numpy as jnp
from jax import lax
from jax.experimental import pallas as pl
from jax.experimental.pallas import tpu as pltpu
from jax.sharding import Mesh
from jax.sharding import PartitionSpec as P

HD = 64
SCALE = HD**-0.5
EPS = 1e-05
NEG = -1e30
BATCH = ("y", "x", "zh", "core")
BF = jnp.bfloat16
F32 = jnp.float32
D = 1024
HALF = 512
GROUP = 256
FINAL_VMEM = 32 * 1024 * 1024


UNITS = 2816
PACK_NORMS = 3 * UNITS
PACK_LEFT = PACK_NORMS + 4 * 256
PACK_GRADS = PACK_LEFT + 2 * D
PACK_ROWS = PACK_GRADS + 4 * 512


def nn(a, b):
    return lax.dot_general(a, b, (((1,), (0,)), ((), ())), preferred_element_type=F32)


def nt(a, b):
    return lax.dot_general(a, b, (((1,), (1,)), ((), ())), preferred_element_type=F32)


def tn(a, b):
    return lax.dot_general(a, b, (((0,), (0,)), ((), ())), preferred_element_type=F32)


def inverse_rms(x):
    return lax.rsqrt(jnp.mean(x * x, axis=-1, keepdims=True) + EPS)


def norm_back(x, gain, up):
    r = inverse_rms(x)
    scaled = up * gain
    inner = jnp.mean(scaled * x, axis=-1, keepdims=True)
    return r * (scaled - x * (r * r * inner)), up * (x * r)


def stack_heads(rows):
    head = lax.broadcasted_iota(jnp.int32, rows.shape, 1) // HD
    return jnp.concatenate([jnp.where(head == h, rows, jnp.zeros_like(rows)) for h in range(4)], 0)


def unstack_heads(stacked):
    head = lax.broadcasted_iota(jnp.int32, (HD, GROUP), 1) // HD
    out = stacked[0:HD]
    for h in range(1, 4):
        out = jnp.where(head == h, stacked[h * HD : (h + 1) * HD], out)
    return out


def softmax_columns(scores):
    top = functools.reduce(jnp.maximum, [jnp.max(s, axis=0, keepdims=True) for s in scores])
    parts = [jnp.exp(s - top) for s in scores]
    inverse = 1.0 / sum(jnp.sum(p, axis=0, keepdims=True) for p in parts)
    return [(p * inverse).astype(BF) for p in parts]


def encode_lower(patch, low, w_qkv, gains, pn, q, bn, k, v):
    x = patch[...].astype(F32)
    normed = (x * inverse_rms(x) * gains[0:1]).astype(BF)
    pn[...] = normed
    q[...] = nn(normed, w_qkv.block(0)[...]).astype(BF)
    for i in range(2):
        at = pl.ds(i * 256, 256)
        b = low[at, :].astype(F32)
        normed = (b * inverse_rms(b) * gains[1:2]).astype(BF)
        bn[at, :] = normed
        k[at, :] = nn(normed, w_qkv.block(1)[...]).astype(BF)
        v[at, :] = nn(normed, w_qkv.block(2)[...]).astype(BF)


def encode_rest(m, patch, up, w_qkv, w_out, gains, bounds, q, k_lo, v_lo, hb, o1, weights, bn, k, v):
    b = up[...].astype(F32)
    normed = (b * inverse_rms(b) * gains[1:2]).astype(BF)
    bn[...] = normed
    k[...] = nn(normed, w_qkv.block(1)[...]).astype(BF)
    v[...] = nn(normed, w_qkv.block(2)[...]).astype(BF)
    spot = lax.broadcasted_iota(jnp.int32, (256, GROUP), 0)
    start = bounds[m, 0:1, :]
    end = bounds[m, 1:2, :]
    inside = [(spot + h * 256 >= start) & (spot + h * 256 < end) for h in range(2)]
    low_at = slice(m * 256, (m + 1) * 256)
    rows = slice(m * HD, (m + 1) * HD)
    for g in range(4):
        lanes = slice(g * GROUP, (g + 1) * GROUP)
        stacked = stack_heads(q[rows, lanes] * BF(SCALE))
        scores = [
            jnp.where(inside[h], nt(keys, stacked), NEG)
            for h, keys in enumerate((k_lo[low_at, lanes], k[:, lanes]))
        ]
        w = softmax_columns(scores)
        weights[g * 2] = w[0]
        weights[g * 2 + 1] = w[1]
        mixed = tn(w[0], v_lo[low_at, lanes]) + tn(w[1], v[:, lanes])
        o1[:, lanes] = unstack_heads(mixed).astype(BF)
    hb[...] = (patch[rows, :].astype(F32) + nn(o1[...], w_out[...])).astype(BF)


def latent_layer(
    ids, hb_a, hb_b, cot, allowed, w_qkv, w_out, gains, w_ff, d_hidden,
    latents, dhb, gain_grad, norms, grads, packed,
    qkv, weights, o2, ff_buf, acc_out, acc_norm, dqkv, sems,
):
    core = ids[0]
    units = w_ff.shape[1]
    step = 256
    parts = 4
    part = units // parts

    fetches = []
    for i in range(parts):
        at = slice(i * part, (i + 1) * part)
        fetches.append(pltpu.make_async_copy(w_ff.at[:, at, :], ff_buf.at[:, at, :], sems.at[i]))
        fetches[-1].start()
    x = jnp.concatenate([hb_a[...], hb_b[...]], 0).astype(F32)
    normed = (x * inverse_rms(x) * gains[0:1]).astype(BF)
    packed[PACK_LEFT : PACK_LEFT + D, :] = normed.T
    for j in range(3):
        qkv[:, j * D : (j + 1) * D] = nn(normed, w_qkv.block(j)[...]).astype(BF)
    for m in range(2):
        rows = slice(m * HD, (m + 1) * HD)
        for g in range(4):
            lanes = slice(g * GROUP, (g + 1) * GROUP)
            k_lanes = slice(D + g * GROUP, D + (g + 1) * GROUP)
            v_lanes = slice(2 * D + g * GROUP, 2 * D + (g + 1) * GROUP)
            stacked = stack_heads(qkv[rows, lanes] * BF(SCALE))
            scores = jnp.where(allowed[m] > 0.5, nt(qkv[rows, k_lanes], stacked), NEG)
            (w,) = softmax_columns([scores])
            weights[m * 4 + g] = w
            o2[rows, lanes] = unstack_heads(tn(w, qkv[rows, v_lanes])).astype(BF)
    packed[PACK_LEFT + D : PACK_LEFT + 2 * D, :] = o2[...].T
    after = x + nn(o2[...], w_out[...])
    yn = (after * inverse_rms(after) * gains[1:2]).astype(BF)
    c = cot[...]
    for h in range(2):

        @pl.when(core == h)
        def _(h=h):
            norms[0:128, :] = yn[:, h * HALF : (h + 1) * HALF]
            norms[128:256, :] = c[:, h * HALF : (h + 1) * HALF]

        @pl.when(core != h)
        def _(h=h):
            for b in range(4):
                lanes = slice(h * HALF + b * 128, h * HALF + (b + 1) * 128)
                packed[PACK_NORMS + b * 256 : PACK_NORMS + b * 256 + 128, :] = yn[:, lanes]
                packed[PACK_NORMS + b * 256 + 128 : PACK_NORMS + (b + 1) * 256, :] = c[:, lanes]

    for copy in fetches:
        copy.wait()
    acc_out[...] = after
    for i in range(units // step):
        at = slice(i * step, (i + 1) * step)
        gate = nt(yn, ff_buf[0, at, :])
        upward = nt(yn, ff_buf[1, at, :])
        du = d_hidden[:, at]
        sig = 1.0 / (1.0 + jnp.exp(-gate))
        active = gate * sig
        hidden = (active * upward).astype(BF)
        d_gate = (du * upward * (sig * (1.0 + gate * (1.0 - sig)))).astype(BF)
        d_up = (du * active).astype(BF)
        for j, value in enumerate((d_gate, d_up, hidden)):
            packed[i * step + j * units : (i + 1) * step + j * units, :] = value.T
        acc_out[...] += nn(hidden, ff_buf[2, at, :])
        back = nn(d_gate, ff_buf[0, at, :]) + nn(d_up, ff_buf[1, at, :])
        if i == 0:
            acc_norm[...] = back
        else:
            acc_norm[...] += back
    latents[...] = acc_out[...]
    back, gain_rows = norm_back(after, gains[1:2], acc_norm[...])
    gain_grad[1:2, :] = jnp.sum(gain_rows, axis=0, keepdims=True)
    d_after = c.astype(F32) + back
    da = d_after.astype(BF)
    d_mixed = nt(da, w_out[...]).astype(BF)
    for m in range(2):
        rows = slice(m * HD, (m + 1) * HD)
        for g in range(4):
            lanes = slice(g * GROUP, (g + 1) * GROUP)
            k_lanes = slice(D + g * GROUP, D + (g + 1) * GROUP)
            v_lanes = slice(2 * D + g * GROUP, 2 * D + (g + 1) * GROUP)
            q_stacked = stack_heads(qkv[rows, lanes] * BF(SCALE))
            o_stacked = stack_heads(d_mixed[rows, lanes])
            w_low = weights[m * 4 + g]
            w = w_low.astype(F32)
            dw = nt(qkv[rows, v_lanes], o_stacked)
            inner = jnp.sum(dw * w, axis=0, keepdims=True)
            ds = (w * (dw - inner)).astype(BF)
            dqkv[rows, lanes] = (unstack_heads(tn(ds, qkv[rows, k_lanes])) * SCALE).astype(BF)
            dqkv[rows, k_lanes] = nn(ds, q_stacked).astype(BF)
            dqkv[rows, v_lanes] = nn(w_low, o_stacked).astype(BF)
    d_normed = sum(nt(dqkv[:, j * D : (j + 1) * D], w_qkv.block(j)[...]) for j in range(3))
    back, gain_rows = norm_back(x, gains[0:1], d_normed)
    gain_grad[0:1, :] = jnp.sum(gain_rows, axis=0, keepdims=True)
    dhb[...] = (d_after + back).astype(BF)
    for h in range(2):
        pieces = (
            dqkv[:, h * HALF : (h + 1) * HALF],
            da[:, h * HALF : (h + 1) * HALF],
            dqkv[:, D + h * HALF : D + (h + 1) * HALF],
            dqkv[:, 2 * D + h * HALF : 2 * D + (h + 1) * HALF],
        )

        @pl.when(core == h)
        def _(pieces=pieces):
            for i, value in enumerate(pieces):
                grads[i * 128 : (i + 1) * 128, :] = value

        @pl.when(core != h)
        def _(pieces=pieces):
            for i, value in enumerate(pieces):
                for b in range(4):
                    first = PACK_GRADS + b * 512 + i * 128
                    packed[first : first + 128, :] = value[:, b * 128 : (b + 1) * 128]


def hidden_back(cot, w_ff, d_hidden, buffer, sems):
    parts = 4
    part = w_ff.shape[1] // parts
    copies = []
    for i in range(parts):
        at = slice(i * part, (i + 1) * part)
        copies.append(pltpu.make_async_copy(w_ff.at[2, at, :], buffer.at[at, :], sems.at[i]))
        copies[-1].start()
    for copy in copies:
        copy.wait()
    for i in range(w_ff.shape[1] // 256):
        at = slice(i * 256, (i + 1) * 256)
        d_hidden[:, at] = nt(cot[...], buffer[at, :])


def encoder_attention_back(
    ids, dhb, w_out, q, k_lo, v_lo, k_a, k_b, v_a, v_b, w_a, w_b, mine, other, both, sems
):
    d_mixed = nt(dhb[...], w_out[...]).astype(BF)
    for g in range(4):
        lanes = slice(g * GROUP, (g + 1) * GROUP)
        out_lanes = slice((g % 2) * GROUP, (g % 2 + 1) * GROUP)
        half = jnp.where(ids[0] == g // 2, 0, 1)

        def put(at, value, half=half, out_lanes=out_lanes):
            both[half, at, out_lanes] = value

        put(slice(128, 256), dhb[:, lanes])
        for m, (k_up, v_up, weights) in enumerate(((k_a, v_a, w_a), (k_b, v_b, w_b))):
            rows = slice(m * HD, (m + 1) * HD)
            low_at = slice(m * 256, (m + 1) * 256)
            q_stacked = stack_heads(q[rows, lanes] * BF(SCALE))
            o_stacked = stack_heads(d_mixed[rows, lanes])
            low = [weights[g * 2 + h] for h in range(2)]
            w = [piece.astype(F32) for piece in low]
            dw = [nt(values, o_stacked) for values in (v_lo[low_at, lanes], v_up[:, lanes])]
            inner = sum(jnp.sum(a * b, axis=0, keepdims=True) for a, b in zip(dw, w))
            ds = [(b * (a - inner)).astype(BF) for a, b in zip(dw, w)]
            dq = tn(ds[0], k_lo[low_at, lanes]) + tn(ds[1], k_up[:, lanes])
            put(rows, (unstack_heads(dq) * SCALE).astype(BF))
            for h in range(2):
                base = h * HALF + m * 256
                put(slice(256 + base, 512 + base), nn(ds[h], q_stacked).astype(BF))
                put(slice(1280 + base, 1536 + base), nn(low[h], o_stacked).astype(BF))
    copies = [pltpu.make_async_copy(both.at[i], out, sems.at[i]) for i, out in enumerate((mine, other))]
    for copy in copies:
        copy.start()
    for copy in copies:
        copy.wait()


def both_columns(core, block, w_qkv):
    return [
        w_qkv.block(block)[:, pl.ds(pl.multiple_of(which * HALF, HALF), HALF)] for which in (core, 1 - core)
    ]


def bytes_back(core, h, source, w_qkv, gains, grads):
    d_norm = sum(
        nt(ref[1024 * block - 768 + h * HALF : 1024 * block - 256 + h * HALF, :], columns)
        for block in (1, 2)
        for ref, columns in zip(grads, both_columns(core, block, w_qkv))
    )
    back, gain_rows = norm_back(source.astype(F32), gains[1:2], d_norm)
    return back.astype(BF), jnp.sum(gain_rows, axis=0, keepdims=True)


def encoder_upper_back(ids, up_a, up_b, w_qkv, gains, mine, other, up_grad, gain_grad):
    source = jnp.concatenate([up_a[...], up_b[...]], 0)
    back, rows = bytes_back(ids[0], 1, source, w_qkv, gains, (mine, other))
    up_grad[...] = back
    gain_grad[...] = rows


def encoder_lower_back(
    ids, dhb, patch, low, w_qkv, gains, mine, other, after, patch_grad, low_grad, gain_grad
):
    core = ids[0]
    up_norm = sum(nt(ref[0:128, :], columns) for ref, columns in zip((mine, other), both_columns(core, 0, w_qkv)))
    back, gain_rows = norm_back(patch[...].astype(F32), gains[0:1], up_norm)
    gain_grad[0:1, :] = jnp.sum(gain_rows, axis=0, keepdims=True)
    patch_grad[...] = dhb[...].astype(F32) + back
    back, rows = bytes_back(core, 0, low[...], w_qkv, gains, (mine, other))
    low_grad[...] = back
    gain_grad[1:2, :] = rows


def turn_encoder(pn, o_a, o_b, bn_lo, bn_a, bn_b, packed):
    for b, rows in enumerate([bn_lo[i * 128 : (i + 1) * 128, :] for i in range(4)]
                             + [ref[i * 128 : (i + 1) * 128, :] for ref in (bn_a, bn_b) for i in range(2)]):
        packed[b * D : (b + 1) * D, :] = rows.T
    packed[PACK_LEFT : PACK_LEFT + D, :] = pn[...].T
    packed[PACK_LEFT + D : PACK_LEFT + 2 * D, :] = jnp.concatenate([o_a[...], o_b[...]], 0).T


def rows_of_both(left, left_far, at):
    return jnp.concatenate([left[at, :], left_far[at, :]], 1)


def below(near, far, rows):
    return jnp.concatenate([near[rows, :], far[rows, :]], 0)


def encoder_weights(ids, packed, packed_far, near, far, after, *blocks):
    u = ids[1]
    queries = below(near, far, slice(0, 128))
    outputs = below(near, far, slice(128, 256))
    for k in range(4):
        first = lax.rem(u + k, 4) * 256

        def at(base, first=first):
            return pl.ds(pl.multiple_of(first + base, 256), 256)

        blocks[k][0] = nn(rows_of_both(packed, packed_far, at(PACK_LEFT)), queries).astype(BF)
        blocks[k][3] = nn(rows_of_both(packed, packed_far, at(PACK_LEFT + D)), outputs).astype(BF)
        lefts = [jnp.concatenate([ref[at(b * D), :] for b in range(8)], 1) for ref in (packed, packed_far)]
        for block in (1, 2):
            rows = slice(1024 * block - 768, 1024 * block + 256)
            blocks[k][block] = (nn(lefts[0], near[rows, :]) + nn(lefts[1], far[rows, :])).astype(BF)


def unpack(packed, first, rows):
    return jnp.concatenate([packed[first + b * rows : first + (b + 1) * rows, :] for b in range(4)], 1)


def latent_weights(ids, packed, packed_far, near, *blocks):
    u = ids[1]
    far = unpack(packed_far, PACK_GRADS, 512)
    rights = [jnp.concatenate([near[i * 128 : (i + 1) * 128, :], far[i * 128 : (i + 1) * 128, :]], 0) for i in range(4)]
    for k in range(4):
        first = PACK_LEFT + lax.rem(u + k, 4) * 256
        at = pl.ds(pl.multiple_of(first, 256), 256)
        low_at = pl.ds(pl.multiple_of(first + D, 256), 256)
        for block, (source, i) in enumerate(((at, 0), (at, 2), (at, 3), (low_at, 1))):
            blocks[k][block] = nn(rows_of_both(packed, packed_far, source), rights[i]).astype(BF)


def ff_weights_grad(ids, packed, packed_far, norms, own, right, left, far_a, far_b):
    core, u = ids[0], ids[1]
    share = UNITS // 16
    far = unpack(packed_far, PACK_NORMS, 256)
    normed = jnp.concatenate([norms[0:128, :], far[0:128, :]], 0)
    cot = jnp.concatenate([norms[128:256, :], far[128:256, :]], 0)
    for k in range(4):
        there = lax.rem(u + k, 4)
        for j in range(3):
            parts = []
            for v in range(4):
                chunk = jnp.where(core == 0, there * 4 + v, v * 4 + there)
                at = pl.ds(pl.multiple_of(j * UNITS + chunk * share, 16), share)
                parts.append(rows_of_both(packed, packed_far, at))
            value = nn(jnp.concatenate(parts, 0), normed if j < 2 else cot).astype(BF)
            rows = slice(j * share, (j + 1) * share)
            for v in range(4):
                piece = value[v * share : (v + 1) * share, :]
                if k == 2:
                    far_a[v, rows, :] = piece[:, :GROUP]
                    far_b[v, rows, :] = piece[:, GROUP:]
                else:
                    (own, right, None, left)[k][v, rows, :] = piece


def ff_add(right, left, from_left, from_right, after, new_right, new_left):
    new_right[:, :, 0:GROUP] = (right[:, :, 0:GROUP].astype(F32) + from_left[...].astype(F32)).astype(BF)
    new_right[:, :, GROUP:] = right[:, :, GROUP:]
    new_left[:, :, 0:GROUP] = left[:, :, 0:GROUP]
    new_left[:, :, GROUP:] = (left[:, :, GROUP:].astype(F32) + from_right[...].astype(F32)).astype(BF)


def sum_four(own, a, b, c):
    return own.astype(F32) + a.astype(F32) + b.astype(F32) + c.astype(F32)


def pack_gain(value):
    high = value.astype(BF)
    low = (value - high.astype(F32)).astype(BF)
    return jnp.concatenate(
        [high.astype(F32), low.astype(F32), jnp.zeros((8, HALF), F32)], 0
    ).astype(BF)


def unpack_gain(rows):
    rows = rows.astype(F32)
    return rows[0:4] + rows[4:8]


GAIN_AT = slice(256, 272)


def attn_sum_first(ids, own, a, b, c, *outs):
    v = ids[2]
    for k in range(4):
        at = pl.ds(pl.multiple_of(lax.rem(v + k, 4) * HD, HD), HD)
        for block in range(4):
            outs[k][block * HD : (block + 1) * HD, :] = sum_four(
                own[block, at, :], a[block, at, :], b[block, at, :], c[block, at, :]
            ).astype(BF)


def attn_sum_first_gain(ids, own, a, b, c, enc_gain, up_gain, lat_gain, *outs):
    attn_sum_first(ids, own, a, b, c, *outs)
    first = ids[4] == 0
    gain = jnp.where(
        first, jnp.concatenate([enc_gain[0:1, :], enc_gain[1:2, :] + up_gain[...]], 0), lat_gain[...]
    )
    halves = [gain[i : i + 1, h * HALF : (h + 1) * HALF] for i in range(2) for h in range(2)]
    packed = pack_gain(jnp.concatenate(halves, 0))
    for out in outs:
        out[GAIN_AT, :] = packed


def sum_all(*refs):
    refs, out = refs[:-1], refs[-1]
    out[0:256, :] = sum(ref[0:256, :].astype(F32) for ref in refs).astype(BF)
    out[GAIN_AT, :] = pack_gain(sum(unpack_gain(ref[GAIN_AT, :]) for ref in refs))


def stack_rows(*refs):
    refs, out = refs[:-2], refs[-1]
    for j, ref in enumerate(refs):
        out[j * 256 : (j + 1) * 256, :] = ref[0:256, :]
    out[1024:1040, :] = refs[0][GAIN_AT, :]


def ff_sum_first(ids, own, a, b, *outs):
    v = ids[2]
    for k in range(4):
        at = lax.rem(v + k, 4)
        outs[k][...] = (own[at].astype(F32) + a[at].astype(F32) + b[at].astype(F32)).astype(BF)


def ff_sum_second(own, a, b, c, out):
    out[...] = sum_four(own[...], a[...], b[...], c[...]).astype(BF)


def final_attn(ids, *refs):
    pieces, (qkv, out, gain) = refs[:8], refs[8:]
    step = pl.program_id(0)
    for side in range(2):
        core = ids[0] if side == 0 else 1 - ids[0]
        u = ids[1] if side == 0 else ids[2]
        v = ids[2] if side == 0 else ids[1]
        for k in range(4):
            piece = pieces[side * 4 + k]

            @pl.when(lax.rem(u + k, 4) == step)
            def _(piece=piece, v=v, core=core):
                for j in range(4):
                    at = pl.ds(pl.multiple_of(lax.rem(v + j, 4) * HD, HD), HD)
                    for block in range(4):
                        target, column = (qkv, block * D) if block < 3 else (out, 0)
                        lanes = pl.ds(pl.multiple_of(core * HALF + column, HALF), HALF)
                        first = j * 256 + block * HD
                        target[at, lanes] = piece[first : first + HD, :].astype(F32)

    mine = sum(unpack_gain(piece[1024:1040, :]) for piece in pieces[:4])
    other = sum(unpack_gain(piece[1024:1040, :]) for piece in pieces[4:])
    total = mine + other
    for i in range(2):
        for h in range(2):
            gain[i : i + 1, h * HALF : (h + 1) * HALF] = total[2 * i + h : 2 * i + h + 1, :]


SMEM = pltpu.MemorySpace.SMEM
VMEM = pltpu.MemorySpace.VMEM


def size(shape, dtype):
    return math.prod(shape) * jnp.dtype(dtype).itemsize


class Arriving:
    def __init__(self, copy, buffer):
        self.copy, self.buffer, self.here = copy, buffer, False

    def ready(self):
        if not self.here:
            self.copy.wait()
            self.here = True
        return self.buffer

    def __getitem__(self, index):
        return self.ready()[index]


class ArrivingBlocks:
    def __init__(self, blocks):
        self.blocks = blocks

    def block(self, j):
        return self.blocks[j]


def fetching(kernel, n_args, n_outs, plan):
    def wrapped(*refs):
        args, outs, rest = list(refs[:n_args]), refs[n_args : n_args + n_outs], refs[n_args + n_outs :]
        scratch, buffers, sems = rest[: len(rest) - len(plan) - 1], rest[len(rest) - len(plan) - 1 : -1], rest[-1]
        arriving = []
        blocks = {}
        for i, (a, j) in enumerate(plan):
            source = refs[a] if j is None else refs[a].at[:, j * D : (j + 1) * D]
            copy = pltpu.make_async_copy(source, buffers[i], sems.at[i])
            copy.start()
            arriving.append(Arriving(copy, buffers[i]))
            if j is None:
                args[a] = arriving[-1]
            else:
                blocks.setdefault(a, {})[j] = arriving[-1]
        for a, found in blocks.items():
            args[a] = ArrivingBlocks(found)
        kernel(*args, *outs, *scratch)
        for value in arriving:
            value.ready()

    return wrapped


def call(kernel, args, outs, scratch=(), spaces=None, spare=6, fetch=(), far_outs=False):
    spaces = dict(spaces or {})
    scratch = list(scratch)
    plan = [f if isinstance(f, tuple) else (f, None) for f in fetch]
    if plan:
        for a, j in plan:
            spaces[a] = pl.ANY
            shape = args[a].shape if j is None else (args[a].shape[0], D)
            scratch.append(pltpu.VMEM(shape, args[a].dtype))
        scratch.append(pltpu.SemaphoreType.DMA((len(plan),)))
        kernel = fetching(kernel, len(args), len(outs), plan)
    vmem = sum(size(a.shape, a.dtype) for i, a in enumerate(args) if i not in spaces)
    vmem += 0 if far_outs else sum(size(*o) for o in outs)
    vmem += sum(size(s.shape, s.dtype) for s in scratch if hasattr(s, "shape") and s.memory_space == VMEM)
    specs = [pl.BlockSpec(memory_space=spaces.get(i, VMEM)) for i in range(len(args))]
    return pl.pallas_call(
        kernel,
        out_shape=[jax.ShapeDtypeStruct(s, t) for s, t in outs],
        in_specs=specs,
        out_specs=[pl.BlockSpec(memory_space=pl.ANY if far_outs else VMEM) for _ in outs],
        scratch_shapes=scratch,
        compiler_params=pltpu.CompilerParams(vmem_limit_bytes=vmem + spare * 1024 * 1024),
    )(*args)


def nothing(outs):
    def kernel(*refs):
        pass

    return pl.pallas_call(
        kernel,
        out_shape=[jax.ShapeDtypeStruct(s, t) for s, t in outs],
        out_specs=[pl.BlockSpec(memory_space=pl.ANY) for _ in outs],
    )()


def on_section(flag, kernel, args, outs, **rest):
    return lax.cond(
        flag, lambda: call(kernel, args, outs, **rest), lambda: nothing(outs)
    )


def along(value, by):
    return lax.ppermute(value, "s", [(0, 1)] if by > 0 else [(1, 0)])


def swap(value, axis, sections=(0, 1)):
    pairs = [(s * 2 + i, s * 2 + 1 - i) for s in sections for i in range(2)]
    return lax.ppermute(value, ("s", axis), pairs)


def plane_shift(value, which, by, sections=(0, 1)):
    pairs = []
    for s in sections:
        for y in range(4):
            for x in range(4):
                for core in range(2):
                    ty, tx = ((y + by) % 4, x) if core == which else (y, (x + by) % 4)
                    pairs.append((((s * 4 + y) * 4 + x) * 2 + core, ((s * 4 + ty) * 4 + tx) * 2 + core))
    return lax.ppermute(value, ("s", "y", "x", "core"), pairs)


def exchange(blocks, which, sections=(0, 1)):
    return [plane_shift(blocks[k], which, k, sections) for k in (1, 2, 3)]


def collect(block, which):
    return [block] + [plane_shift(block, which, -k) for k in (1, 2, 3)]


def pick(stack, index, dim):
    return lax.dynamic_index_in_dim(stack, index, dim, keepdims=False)


def shards(patch_io, byte_states, patch_lengths, patch_live, attn_qkv, attn_out, gains, ff_weights):
    section = lax.axis_index("s")
    core = lax.axis_index("core")
    zh = lax.axis_index("zh")
    y, x = lax.axis_index("y"), lax.axis_index("x")
    first = section == 0
    second = section == 1
    ids = jnp.stack([core, jnp.where(core == 0, y, x), jnp.where(core == 0, x, y), zh, section])
    ids = ids.astype(jnp.int32)
    w_qkv = attn_qkv[0]
    w_out = attn_out[0]
    gain_pair = gains[0]
    micro, seq = patch_io.shape[1], patch_io.shape[3]
    half_bytes = byte_states.shape[2]
    units = ff_weights.shape[0]
    rows = micro * seq
    own_rows = patch_io.reshape(rows, D)
    up_a = along(byte_states[0, 0], -1)
    up_b = along(byte_states[1, 0], -1)
    lower = byte_states.reshape(micro * half_bytes, D)
    w_ff = jnp.swapaxes(ff_weights, 0, 1)
    lengths = patch_lengths[:, 0]
    live = patch_live[:, 0]
    ends = jnp.cumsum(lengths, axis=1)
    bounds = jnp.tile(jnp.stack([ends - lengths, ends], 1), (1, 1, 4))
    places = lax.iota(jnp.int32, seq)
    causal = places[:, None] <= places[None, :]
    diagonal = places[:, None] == places[None, :]
    allowed = causal[None] & ((live[:, :, None] == 1) | diagonal[None])
    allowed = lax.optimization_barrier(jnp.tile(allowed.astype(F32), (1, 1, 4)))

    wide = ((rows, D), BF)
    short = ((seq, D), BF)
    tall = ((micro * half_bytes, D), BF)
    piece = ((half_bytes, D), BF)
    (d_hidden,) = on_section(
        second,
        hidden_back,
        (own_rows, w_ff),
        [((rows, units), F32)],
        spaces={1: pl.ANY},
        scratch=[pltpu.VMEM((units, D), BF), pltpu.SemaphoreType.DMA((4,))],
    )
    pn, q, bn_lo, k_lo, v_lo = on_section(
        first,
        encode_lower,
        (own_rows, lower, w_qkv, gain_pair),
        [wide, wide, tall, tall, tall],
        fetch=((2, 0), 1, (2, 1), (2, 2)),
    )
    rest = []
    for m, up in enumerate((up_a, up_b)):
        rest.append(
            on_section(
                first,
                functools.partial(encode_rest, m),
                (own_rows, up, w_qkv, w_out, gain_pair, bounds, q, k_lo, v_lo),
                [short, short, ((8, 256, GROUP), BF), piece, piece, piece],
                fetch=((2, 1), (2, 2), 7, 8, 3),
            )
        )
    (hb_a, o_a, w_a, bn_a, k_a, v_a), (hb_b, o_b, w_b, bn_b, k_b, v_b) = rest
    arrived = [along(hb_a, 1), along(hb_b, 1)]

    latent_outs = [
        ((rows, D), F32), wide, ((2, D), F32), ((256, HALF), BF), ((512, HALF), BF), ((PACK_ROWS, rows), BF),
    ]

    def latent():
        return call(
            latent_layer,
            (ids, *arrived, own_rows, allowed, w_qkv, w_out, gain_pair, w_ff, d_hidden),
            latent_outs,
            spaces={0: SMEM, 8: pl.ANY},
            fetch=((5, 0), (5, 1), (5, 2), 6),
            scratch=[
                pltpu.VMEM((rows, 3 * D), BF),
                pltpu.VMEM((8, HD, GROUP), BF),
                pltpu.VMEM((rows, D), BF),
                pltpu.VMEM((3, units, D), BF),
                pltpu.VMEM((rows, D), F32),
                pltpu.VMEM((rows, D), F32),
                pltpu.VMEM((rows, 3 * D), BF),
                pltpu.SemaphoreType.DMA((4,)),
            ],
        )

    def turn():
        return nothing(latent_outs[:5]) + call(
            turn_encoder, (pn, o_a, o_b, bn_lo, bn_a, bn_b), latent_outs[5:]
        )

    latents, dhb, latent_gain, norms, lat_grads, packed = lax.cond(second, latent, turn)
    returned = along(dhb, -1)

    packed_far = swap(packed, "core")

    share = units // 16
    ff_block = ((4, 3 * share, HALF), BF)
    ff_half = ((4, 3 * share, GROUP), BF)
    ff_own, ff_right, ff_left, ff_far_a, ff_far_b = on_section(
        second,
        ff_weights_grad,
        (ids, packed, packed_far, norms),
        [ff_block, ff_block, ff_block, ff_half, ff_half],
        spaces={0: SMEM},
    )

    grads_long = ((2304, HALF), BF)
    enc_grads, enc_other = on_section(
        first,
        encoder_attention_back,
        (ids, returned, w_out, q, k_lo, v_lo, k_a, k_b, v_a, v_b, w_a, w_b),
        [grads_long, grads_long],
        spaces={0: SMEM},
        scratch=[pltpu.VMEM((2, 2304, HALF), BF), pltpu.SemaphoreType.DMA((2,))],
        fetch=(2, 5, 8, 10, 4, 6, 9, 11, 7),
        far_outs=True,
    )
    enc_far = swap(enc_other, "core", (0,))
    up_grad, up_gain = on_section(
        first,
        encoder_upper_back,
        (ids, up_a, up_b, w_qkv, gain_pair, enc_grads, enc_other),
        [tall, ((1, D), F32)],
        spaces={0: SMEM},
        fetch=(5, (3, 1), 6, (3, 2), 1, 2),
    )
    up_arrived = along(up_grad, 1)
    ff_far_a, ff_far_b, up_gain = lax.optimization_barrier((ff_far_a, ff_far_b, up_gain))
    from_left = plane_shift(ff_far_a, 0, 1)
    from_right = plane_shift(ff_far_b, 0, -1)
    outs = [((4, 256, HALF), BF)] * 4
    blocks = lax.cond(
        first,
        lambda: call(
            encoder_weights,
            (ids, packed, packed_far, enc_grads, enc_far, up_gain),
            outs,
            spaces={0: SMEM, 5: pl.ANY},
            fetch=(3, 4, 1, 2),
        ),
        lambda: call(latent_weights, (ids, packed, packed_far, lat_grads), outs, spaces={0: SMEM}),
    )
    last, from_left, from_right = lax.optimization_barrier((blocks[3], from_left, from_right))
    blocks = [*blocks[:3], last]
    got, up_arrived = lax.optimization_barrier((exchange(blocks, 0), up_arrived))
    low_outs = [((rows, D), F32), tall, ((2, D), F32)]

    def lower_grads():
        parts = call(
            encoder_lower_back,
            (ids, returned, own_rows, lower, w_qkv, gain_pair, enc_grads, enc_other, blocks[0]),
            low_outs,
            spaces={0: SMEM, 8: pl.ANY},
            fetch=(6, 7, (4, 0), (4, 1), (4, 2), 3),
        )
        return (*parts, *nothing([ff_block, ff_block]))

    def ff_middle():
        added = call(
            ff_add, (ff_right, ff_left, from_left, from_right, blocks[0]), [ff_block, ff_block], spaces={4: pl.ANY}
        )
        return (*nothing(low_outs), *added)

    patch_grad, low_grad, encoder_gain, ff_right_sum, ff_left_sum = lax.cond(first, lower_grads, ff_middle)
    line = [((272, HALF), BF)]
    blocks = call(
        attn_sum_first_gain,
        (ids, blocks[0], *got, encoder_gain, up_gain, latent_gain),
        line * 4,
        spaces={0: SMEM},
    )
    ff_right_sum, ff_left_sum, _ = lax.optimization_barrier((ff_right_sum, ff_left_sum, blocks))
    from_left = plane_shift(ff_right_sum, 0, 1, (1,))
    from_right = plane_shift(ff_left_sum, 0, -1, (1,))
    (block,) = call(sum_all, (blocks[0], *exchange(blocks, 1)), line)
    byte_grad = jnp.where(first, low_grad, up_arrived)
    patch_out = jnp.where(first, patch_grad, latents)
    from_left, from_right, block, byte_grad, patch_out = lax.optimization_barrier(
        (from_left, from_right, block, byte_grad, patch_out)
    )
    ff_line = ((3 * share, HALF), BF)
    ff_blocks = on_section(
        second, ff_sum_first, (ids, ff_own, from_left, from_right), [ff_line] * 4, spaces={0: SMEM}
    )
    across, ff_blocks = lax.optimization_barrier((swap(block, "zh"), list(ff_blocks)))
    (block,) = call(sum_all, (block, across), line)
    ff_got = exchange(ff_blocks, 1)
    lines = collect(block, 1)
    step_in = swap(lines[3][0:16], "core")
    (block,) = call(stack_rows, (*lines, step_in), [((1040, HALF), BF)], spaces={4: pl.ANY})
    pieces = collect(block, 0)
    own_far = swap(block, "core")
    (ff_sum,) = on_section(second, ff_sum_second, (ff_blocks[0], *ff_got), [ff_line])
    ff_sum = ff_sum.reshape(3, 2, share // 2, HALF)
    ff_far = swap(pick(ff_sum, 1 - zh, 1), "zh")
    ff_sum = (pick(ff_sum, zh, 1).astype(F32) + ff_far.astype(F32)).astype(BF).reshape(3, 2, share // 4, HALF)
    ff_mine = pick(ff_sum, core, 1)
    ff_far = swap(pick(ff_sum, 1 - core, 1), "core")

    def ff_result():
        low, high = jnp.where(core == 0, ff_mine, ff_far), jnp.where(core == 0, ff_far, ff_mine)
        return jnp.swapaxes(jnp.concatenate([low, high], 2), 0, 1).astype(F32)

    ff_grad = lax.cond(second, ff_result, lambda: jnp.zeros((share // 4, 3, D), F32))
    ff_grad, *pieces = lax.optimization_barrier((ff_grad, *pieces))
    pieces = pieces + [own_far] + [swap(p, "core") for p in pieces[1:]]
    whole = lambda p: pl.BlockSpec(p.shape, lambda i, n=p.ndim: (0,) * n)
    total_qkv, total_out, total_gain = pl.pallas_call(
        final_attn,
        grid=(4,),
        out_shape=[
            jax.ShapeDtypeStruct((D, 3 * D), F32),
            jax.ShapeDtypeStruct((D, D), F32),
            jax.ShapeDtypeStruct((2, D), F32),
        ],
        in_specs=[pl.BlockSpec(memory_space=SMEM)] + [whole(p) for p in pieces],
        out_specs=[
            pl.BlockSpec((256, 3 * D), lambda i: (i, 0)),
            pl.BlockSpec((256, D), lambda i: (i, 0)),
            pl.BlockSpec((2, D), lambda i: (0, 0)),
        ],
        compiler_params=pltpu.CompilerParams(vmem_limit_bytes=FINAL_VMEM),
    )(ids, *pieces)
    return (
        patch_out.reshape(1, micro, 1, seq, D),
        byte_grad.reshape(micro, 1, half_bytes, D),
        total_qkv[None],
        total_out[None],
        total_gain[None],
        ff_grad[None],
    )


def solution(mesh):
    fine = Mesh(mesh.devices.reshape(2, 4, 4, 2, 2), ("s",) + BATCH)
    in_specs = (
        P("s", None, BATCH, None, None),
        P(None, BATCH, "s", None),
        P(None, BATCH, None),
        P(None, BATCH, None),
        P("s", None, None),
        P("s", None, None),
        P("s", None, None),
        P(),
    )
    out_specs = (
        P("s", None, BATCH, None, None),
        P(None, BATCH, "s", None),
        P("s", None, None),
        P("s", None, None),
        P("s", None, None),
        P("s", BATCH, None, None),
    )
    return jax.shard_map(shards, mesh=fine, in_specs=in_specs, out_specs=out_specs, check_vma=False)
```

```python
import functools
import math

import jax
import jax.numpy as jnp
from jax import lax
from jax.experimental import pallas as pl
from jax.experimental.pallas import tpu as pltpu
from jax.sharding import Mesh
from jax.sharding import PartitionSpec as P

HD = 64
SCALE = HD**-0.5
EPS = 1e-05
NEG = -1e30
BATCH = ("y", "x", "zh", "core")
BF = jnp.bfloat16
F32 = jnp.float32
D = 1024
HALF = 512
GROUP = 256
FINAL_VMEM = 32 * 1024 * 1024


UNITS = 2816
PACK_NORMS = 3 * UNITS
PACK_LEFT = PACK_NORMS + 4 * 256
PACK_GRADS = PACK_LEFT + 2 * D
PACK_ROWS = PACK_GRADS + 4 * 512


def nn(a, b):
    return lax.dot_general(a, b, (((1,), (0,)), ((), ())), preferred_element_type=F32)


def nt(a, b):
    return lax.dot_general(a, b, (((1,), (1,)), ((), ())), preferred_element_type=F32)


def tn(a, b):
    return lax.dot_general(a, b, (((0,), (0,)), ((), ())), preferred_element_type=F32)


def inverse_rms(x):
    return lax.rsqrt(jnp.mean(x * x, axis=-1, keepdims=True) + EPS)


def norm_back(x, gain, up):
    r = inverse_rms(x)
    scaled = up * gain
    inner = jnp.mean(scaled * x, axis=-1, keepdims=True)
    return r * (scaled - x * (r * r * inner)), up * (x * r)


def stack_heads(rows):
    head = lax.broadcasted_iota(jnp.int32, rows.shape, 1) // HD
    return jnp.concatenate([jnp.where(head == h, rows, jnp.zeros_like(rows)) for h in range(4)], 0)


def unstack_heads(stacked):
    head = lax.broadcasted_iota(jnp.int32, (HD, GROUP), 1) // HD
    out = stacked[0:HD]
    for h in range(1, 4):
        out = jnp.where(head == h, stacked[h * HD : (h + 1) * HD], out)
    return out


def softmax_columns(scores):
    top = functools.reduce(jnp.maximum, [jnp.max(s, axis=0, keepdims=True) for s in scores])
    parts = [jnp.exp(s - top) for s in scores]
    inverse = 1.0 / sum(jnp.sum(p, axis=0, keepdims=True) for p in parts)
    return [(p * inverse).astype(BF) for p in parts]


def encode_lower(patch, low, w_qkv, gains, pn, q, bn, k, v):
    x = patch[...].astype(F32)
    normed = (x * inverse_rms(x) * gains[0:1]).astype(BF)
    pn[...] = normed
    q[...] = nn(normed, w_qkv.block(0)[...]).astype(BF)
    for i in range(2):
        at = pl.ds(i * 256, 256)
        b = low[at, :].astype(F32)
        normed = (b * inverse_rms(b) * gains[1:2]).astype(BF)
        bn[at, :] = normed
        k[at, :] = nn(normed, w_qkv.block(1)[...]).astype(BF)
        v[at, :] = nn(normed, w_qkv.block(2)[...]).astype(BF)


def encode_rest(m, patch, up, w_qkv, w_out, gains, bounds, q, k_lo, v_lo, hb, o1, weights, bn, k, v):
    b = up[...].astype(F32)
    normed = (b * inverse_rms(b) * gains[1:2]).astype(BF)
    bn[...] = normed
    k[...] = nn(normed, w_qkv.block(1)[...]).astype(BF)
    v[...] = nn(normed, w_qkv.block(2)[...]).astype(BF)
    spot = lax.broadcasted_iota(jnp.int32, (256, GROUP), 0)
    start = bounds[m, 0:1, :]
    end = bounds[m, 1:2, :]
    inside = [(spot + h * 256 >= start) & (spot + h * 256 < end) for h in range(2)]
    low_at = slice(m * 256, (m + 1) * 256)
    rows = slice(m * HD, (m + 1) * HD)
    for g in range(4):
        lanes = slice(g * GROUP, (g + 1) * GROUP)
        stacked = stack_heads(q[rows, lanes] * BF(SCALE))
        scores = [
            jnp.where(inside[h], nt(keys, stacked), NEG)
            for h, keys in enumerate((k_lo[low_at, lanes], k[:, lanes]))
        ]
        w = softmax_columns(scores)
        weights[g * 2] = w[0]
        weights[g * 2 + 1] = w[1]
        mixed = tn(w[0], v_lo[low_at, lanes]) + tn(w[1], v[:, lanes])
        o1[:, lanes] = unstack_heads(mixed).astype(BF)
    hb[...] = (patch[rows, :].astype(F32) + nn(o1[...], w_out[...])).astype(BF)


def latent_layer(
    ids, hb_a, hb_b, cot, allowed, w_qkv, w_out, gains, w_ff, d_hidden,
    latents, dhb, gain_grad, norms, grads, packed,
    qkv, weights, o2, ff_buf, acc_out, acc_norm, dqkv, sems,
):
    core = ids[0]
    units = w_ff.shape[1]
    step = 256
    parts = 4
    part = units // parts

    fetches = []
    for i in range(parts):
        at = slice(i * part, (i + 1) * part)
        fetches.append(pltpu.make_async_copy(w_ff.at[:, at, :], ff_buf.at[:, at, :], sems.at[i]))
        fetches[-1].start()
    x = jnp.concatenate([hb_a[...], hb_b[...]], 0).astype(F32)
    normed = (x * inverse_rms(x) * gains[0:1]).astype(BF)
    packed[PACK_LEFT : PACK_LEFT + D, :] = normed.T
    for j in range(3):
        qkv[:, j * D : (j + 1) * D] = nn(normed, w_qkv.block(j)[...]).astype(BF)
    for m in range(2):
        rows = slice(m * HD, (m + 1) * HD)
        for g in range(4):
            lanes = slice(g * GROUP, (g + 1) * GROUP)
            k_lanes = slice(D + g * GROUP, D + (g + 1) * GROUP)
            v_lanes = slice(2 * D + g * GROUP, 2 * D + (g + 1) * GROUP)
            stacked = stack_heads(qkv[rows, lanes] * BF(SCALE))
            scores = jnp.where(allowed[m] > 0.5, nt(qkv[rows, k_lanes], stacked), NEG)
            (w,) = softmax_columns([scores])
            weights[m * 4 + g] = w
            o2[rows, lanes] = unstack_heads(tn(w, qkv[rows, v_lanes])).astype(BF)
    packed[PACK_LEFT + D : PACK_LEFT + 2 * D, :] = o2[...].T
    after = x + nn(o2[...], w_out[...])
    yn = (after * inverse_rms(after) * gains[1:2]).astype(BF)
    c = cot[...]
    for h in range(2):

        @pl.when(core == h)
        def _(h=h):
            norms[0:128, :] = yn[:, h * HALF : (h + 1) * HALF]
            norms[128:256, :] = c[:, h * HALF : (h + 1) * HALF]

        @pl.when(core != h)
        def _(h=h):
            for b in range(4):
                lanes = slice(h * HALF + b * 128, h * HALF + (b + 1) * 128)
                packed[PACK_NORMS + b * 256 : PACK_NORMS + b * 256 + 128, :] = yn[:, lanes]
                packed[PACK_NORMS + b * 256 + 128 : PACK_NORMS + (b + 1) * 256, :] = c[:, lanes]

    for copy in fetches:
        copy.wait()
    acc_out[...] = after
    for i in range(units // step):
        at = slice(i * step, (i + 1) * step)
        gate = nt(yn, ff_buf[0, at, :])
        upward = nt(yn, ff_buf[1, at, :])
        du = d_hidden[:, at]
        sig = 1.0 / (1.0 + jnp.exp(-gate))
        active = gate * sig
        hidden = (active * upward).astype(BF)
        d_gate = (du * upward * (sig * (1.0 + gate * (1.0 - sig)))).astype(BF)
        d_up = (du * active).astype(BF)
        for j, value in enumerate((d_gate, d_up, hidden)):
            packed[i * step + j * units : (i + 1) * step + j * units, :] = value.T
        acc_out[...] += nn(hidden, ff_buf[2, at, :])
        back = nn(d_gate, ff_buf[0, at, :]) + nn(d_up, ff_buf[1, at, :])
        if i == 0:
            acc_norm[...] = back
        else:
            acc_norm[...] += back
    latents[...] = acc_out[...]
    back, gain_rows = norm_back(after, gains[1:2], acc_norm[...])
    gain_grad[1:2, :] = jnp.sum(gain_rows, axis=0, keepdims=True)
    d_after = c.astype(F32) + back
    da = d_after.astype(BF)
    d_mixed = nt(da, w_out[...]).astype(BF)
    for m in range(2):
        rows = slice(m * HD, (m + 1) * HD)
        for g in range(4):
            lanes = slice(g * GROUP, (g + 1) * GROUP)
            k_lanes = slice(D + g * GROUP, D + (g + 1) * GROUP)
            v_lanes = slice(2 * D + g * GROUP, 2 * D + (g + 1) * GROUP)
            q_stacked = stack_heads(qkv[rows, lanes] * BF(SCALE))
            o_stacked = stack_heads(d_mixed[rows, lanes])
            w_low = weights[m * 4 + g]
            w = w_low.astype(F32)
            dw = nt(qkv[rows, v_lanes], o_stacked)
            inner = jnp.sum(dw * w, axis=0, keepdims=True)
            ds = (w * (dw - inner)).astype(BF)
            dqkv[rows, lanes] = (unstack_heads(tn(ds, qkv[rows, k_lanes])) * SCALE).astype(BF)
            dqkv[rows, k_lanes] = nn(ds, q_stacked).astype(BF)
            dqkv[rows, v_lanes] = nn(w_low, o_stacked).astype(BF)
    d_normed = sum(nt(dqkv[:, j * D : (j + 1) * D], w_qkv.block(j)[...]) for j in range(3))
    back, gain_rows = norm_back(x, gains[0:1], d_normed)
    gain_grad[0:1, :] = jnp.sum(gain_rows, axis=0, keepdims=True)
    dhb[...] = (d_after + back).astype(BF)
    for h in range(2):
        pieces = (
            dqkv[:, h * HALF : (h + 1) * HALF],
            da[:, h * HALF : (h + 1) * HALF],
            dqkv[:, D + h * HALF : D + (h + 1) * HALF],
            dqkv[:, 2 * D + h * HALF : 2 * D + (h + 1) * HALF],
        )

        @pl.when(core == h)
        def _(pieces=pieces):
            for i, value in enumerate(pieces):
                grads[i * 128 : (i + 1) * 128, :] = value

        @pl.when(core != h)
        def _(pieces=pieces):
            for i, value in enumerate(pieces):
                for b in range(4):
                    first = PACK_GRADS + b * 512 + i * 128
                    packed[first : first + 128, :] = value[:, b * 128 : (b + 1) * 128]


def hidden_back(cot, w_ff, d_hidden, buffer, sems):
    parts = 4
    part = w_ff.shape[1] // parts
    copies = []
    for i in range(parts):
        at = slice(i * part, (i + 1) * part)
        copies.append(pltpu.make_async_copy(w_ff.at[2, at, :], buffer.at[at, :], sems.at[i]))
        copies[-1].start()
    for copy in copies:
        copy.wait()
    for i in range(w_ff.shape[1] // 256):
        at = slice(i * 256, (i + 1) * 256)
        d_hidden[:, at] = nt(cot[...], buffer[at, :])


def encoder_attention_back(
    ids, dhb, w_out, q, k_lo, v_lo, k_a, k_b, v_a, v_b, w_a, w_b, mine, other, both, sems
):
    d_mixed = nt(dhb[...], w_out[...]).astype(BF)
    for g in range(4):
        lanes = slice(g * GROUP, (g + 1) * GROUP)
        out_lanes = slice((g % 2) * GROUP, (g % 2 + 1) * GROUP)
        half = jnp.where(ids[0] == g // 2, 0, 1)

        def put(at, value, half=half, out_lanes=out_lanes):
            both[half, at, out_lanes] = value

        put(slice(128, 256), dhb[:, lanes])
        for m, (k_up, v_up, weights) in enumerate(((k_a, v_a, w_a), (k_b, v_b, w_b))):
            rows = slice(m * HD, (m + 1) * HD)
            low_at = slice(m * 256, (m + 1) * 256)
            q_stacked = stack_heads(q[rows, lanes] * BF(SCALE))
            o_stacked = stack_heads(d_mixed[rows, lanes])
            low = [weights[g * 2 + h] for h in range(2)]
            w = [piece.astype(F32) for piece in low]
            dw = [nt(values, o_stacked) for values in (v_lo[low_at, lanes], v_up[:, lanes])]
            inner = sum(jnp.sum(a * b, axis=0, keepdims=True) for a, b in zip(dw, w))
            ds = [(b * (a - inner)).astype(BF) for a, b in zip(dw, w)]
            dq = tn(ds[0], k_lo[low_at, lanes]) + tn(ds[1], k_up[:, lanes])
            put(rows, (unstack_heads(dq) * SCALE).astype(BF))
            for h in range(2):
                base = h * HALF + m * 256
                put(slice(256 + base, 512 + base), nn(ds[h], q_stacked).astype(BF))
                put(slice(1280 + base, 1536 + base), nn(low[h], o_stacked).astype(BF))
    copies = [pltpu.make_async_copy(both.at[i], out, sems.at[i]) for i, out in enumerate((mine, other))]
    for copy in copies:
        copy.start()
    for copy in copies:
        copy.wait()


def both_columns(core, block, w_qkv):
    return [
        w_qkv.block(block)[:, pl.ds(pl.multiple_of(which * HALF, HALF), HALF)] for which in (core, 1 - core)
    ]


def bytes_back(core, h, source, w_qkv, gains, grads):
    d_norm = sum(
        nt(ref[1024 * block - 768 + h * HALF : 1024 * block - 256 + h * HALF, :], columns)
        for block in (1, 2)
        for ref, columns in zip(grads, both_columns(core, block, w_qkv))
    )
    back, gain_rows = norm_back(source.astype(F32), gains[1:2], d_norm)
    return back.astype(BF), jnp.sum(gain_rows, axis=0, keepdims=True)


def encoder_upper_back(ids, up_a, up_b, w_qkv, gains, mine, other, up_grad, gain_grad):
    source = jnp.concatenate([up_a[...], up_b[...]], 0)
    back, rows = bytes_back(ids[0], 1, source, w_qkv, gains, (mine, other))
    up_grad[...] = back
    gain_grad[...] = rows


def encoder_lower_back(
    ids, dhb, patch, low, w_qkv, gains, mine, other, after, patch_grad, low_grad, gain_grad
):
    core = ids[0]
    up_norm = sum(nt(ref[0:128, :], columns) for ref, columns in zip((mine, other), both_columns(core, 0, w_qkv)))
    back, gain_rows = norm_back(patch[...].astype(F32), gains[0:1], up_norm)
    gain_grad[0:1, :] = jnp.sum(gain_rows, axis=0, keepdims=True)
    patch_grad[...] = dhb[...].astype(F32) + back
    back, rows = bytes_back(core, 0, low[...], w_qkv, gains, (mine, other))
    low_grad[...] = back
    gain_grad[1:2, :] = rows


def turn_encoder(pn, o_a, o_b, bn_lo, bn_a, bn_b, packed):
    for b, rows in enumerate([bn_lo[i * 128 : (i + 1) * 128, :] for i in range(4)]
                             + [ref[i * 128 : (i + 1) * 128, :] for ref in (bn_a, bn_b) for i in range(2)]):
        packed[b * D : (b + 1) * D, :] = rows.T
    packed[PACK_LEFT : PACK_LEFT + D, :] = pn[...].T
    packed[PACK_LEFT + D : PACK_LEFT + 2 * D, :] = jnp.concatenate([o_a[...], o_b[...]], 0).T


def rows_of_both(left, left_far, at):
    return jnp.concatenate([left[at, :], left_far[at, :]], 1)


def below(near, far, rows):
    return jnp.concatenate([near[rows, :], far[rows, :]], 0)


def encoder_weights(ids, packed, packed_far, near, far, after, *blocks):
    u = ids[1]
    queries = below(near, far, slice(0, 128))
    outputs = below(near, far, slice(128, 256))
    for k in range(4):
        first = lax.rem(u + k, 4) * 256

        def at(base, first=first):
            return pl.ds(pl.multiple_of(first + base, 256), 256)

        blocks[k][0] = nn(rows_of_both(packed, packed_far, at(PACK_LEFT)), queries).astype(BF)
        blocks[k][3] = nn(rows_of_both(packed, packed_far, at(PACK_LEFT + D)), outputs).astype(BF)
        lefts = [jnp.concatenate([ref[at(b * D), :] for b in range(8)], 1) for ref in (packed, packed_far)]
        for block in (1, 2):
            rows = slice(1024 * block - 768, 1024 * block + 256)
            blocks[k][block] = (nn(lefts[0], near[rows, :]) + nn(lefts[1], far[rows, :])).astype(BF)


def unpack(packed, first, rows):
    return jnp.concatenate([packed[first + b * rows : first + (b + 1) * rows, :] for b in range(4)], 1)


def latent_weights(ids, packed, packed_far, near, *blocks):
    u = ids[1]
    far = unpack(packed_far, PACK_GRADS, 512)
    rights = [jnp.concatenate([near[i * 128 : (i + 1) * 128, :], far[i * 128 : (i + 1) * 128, :]], 0) for i in range(4)]
    for k in range(4):
        first = PACK_LEFT + lax.rem(u + k, 4) * 256
        at = pl.ds(pl.multiple_of(first, 256), 256)
        low_at = pl.ds(pl.multiple_of(first + D, 256), 256)
        for block, (source, i) in enumerate(((at, 0), (at, 2), (at, 3), (low_at, 1))):
            blocks[k][block] = nn(rows_of_both(packed, packed_far, source), rights[i]).astype(BF)


def ff_weights_grad(ids, packed, packed_far, norms, own, right, left, far_a, far_b):
    core, u = ids[0], ids[1]
    share = UNITS // 16
    far = unpack(packed_far, PACK_NORMS, 256)
    normed = jnp.concatenate([norms[0:128, :], far[0:128, :]], 0)
    cot = jnp.concatenate([norms[128:256, :], far[128:256, :]], 0)
    for k in range(4):
        there = lax.rem(u + k, 4)
        for j in range(3):
            parts = []
            for v in range(4):
                chunk = jnp.where(core == 0, there * 4 + v, v * 4 + there)
                at = pl.ds(pl.multiple_of(j * UNITS + chunk * share, 16), share)
                parts.append(rows_of_both(packed, packed_far, at))
            value = nn(jnp.concatenate(parts, 0), normed if j < 2 else cot).astype(BF)
            rows = slice(j * share, (j + 1) * share)
            for v in range(4):
                piece = value[v * share : (v + 1) * share, :]
                if k == 2:
                    far_a[v, rows, :] = piece[:, :GROUP]
                    far_b[v, rows, :] = piece[:, GROUP:]
                else:
                    (own, right, None, left)[k][v, rows, :] = piece


def ff_add(right, left, from_left, from_right, after, new_right, new_left):
    new_right[:, :, 0:GROUP] = (right[:, :, 0:GROUP].astype(F32) + from_left[...].astype(F32)).astype(BF)
    new_right[:, :, GROUP:] = right[:, :, GROUP:]
    new_left[:, :, 0:GROUP] = left[:, :, 0:GROUP]
    new_left[:, :, GROUP:] = (left[:, :, GROUP:].astype(F32) + from_right[...].astype(F32)).astype(BF)


def sum_four(own, a, b, c):
    return own.astype(F32) + a.astype(F32) + b.astype(F32) + c.astype(F32)


def pack_gain(value):
    high = value.astype(BF)
    low = (value - high.astype(F32)).astype(BF)
    return jnp.concatenate(
        [high.astype(F32), low.astype(F32), jnp.zeros((8, HALF), F32)], 0
    ).astype(BF)


def unpack_gain(rows):
    rows = rows.astype(F32)
    return rows[0:4] + rows[4:8]


GAIN_AT = slice(256, 272)


def attn_sum_first(ids, own, a, b, c, *outs):
    v = ids[2]
    for k in range(4):
        at = pl.ds(pl.multiple_of(lax.rem(v + k, 4) * HD, HD), HD)
        for block in range(4):
            outs[k][block * HD : (block + 1) * HD, :] = sum_four(
                own[block, at, :], a[block, at, :], b[block, at, :], c[block, at, :]
            ).astype(BF)


def attn_sum_first_gain(ids, own, a, b, c, enc_gain, up_gain, lat_gain, *outs):
    attn_sum_first(ids, own, a, b, c, *outs)
    first = ids[4] == 0
    gain = jnp.where(
        first, jnp.concatenate([enc_gain[0:1, :], enc_gain[1:2, :] + up_gain[...]], 0), lat_gain[...]
    )
    halves = [gain[i : i + 1, h * HALF : (h + 1) * HALF] for i in range(2) for h in range(2)]
    packed = pack_gain(jnp.concatenate(halves, 0))
    for out in outs:
        out[GAIN_AT, :] = packed


def sum_all(*refs):
    refs, out = refs[:-1], refs[-1]
    out[0:256, :] = sum(ref[0:256, :].astype(F32) for ref in refs).astype(BF)
    out[GAIN_AT, :] = pack_gain(sum(unpack_gain(ref[GAIN_AT, :]) for ref in refs))


def stack_rows(*refs):
    refs, out = refs[:-2], refs[-1]
    for j, ref in enumerate(refs):
        out[j * 256 : (j + 1) * 256, :] = ref[0:256, :]
    out[1024:1040, :] = refs[0][GAIN_AT, :]


def ff_sum_first(ids, own, a, b, *outs):
    v = ids[2]
    for k in range(4):
        at = lax.rem(v + k, 4)
        outs[k][...] = (own[at].astype(F32) + a[at].astype(F32) + b[at].astype(F32)).astype(BF)


def ff_sum_second(own, a, b, c, out):
    out[...] = sum_four(own[...], a[...], b[...], c[...]).astype(BF)


def final_attn(ids, *refs):
    pieces, (qkv, out, gain) = refs[:8], refs[8:]
    step = pl.program_id(0)
    for side in range(2):
        core = ids[0] if side == 0 else 1 - ids[0]
        u = ids[1] if side == 0 else ids[2]
        v = ids[2] if side == 0 else ids[1]
        for k in range(4):
            piece = pieces[side * 4 + k]

            @pl.when(lax.rem(u + k, 4) == step)
            def _(piece=piece, v=v, core=core):
                for j in range(4):
                    at = pl.ds(pl.multiple_of(lax.rem(v + j, 4) * HD, HD), HD)
                    for block in range(4):
                        target, column = (qkv, block * D) if block < 3 else (out, 0)
                        lanes = pl.ds(pl.multiple_of(core * HALF + column, HALF), HALF)
                        first = j * 256 + block * HD
                        target[at, lanes] = piece[first : first + HD, :].astype(F32)

    mine = sum(unpack_gain(piece[1024:1040, :]) for piece in pieces[:4])
    other = sum(unpack_gain(piece[1024:1040, :]) for piece in pieces[4:])
    total = mine + other
    for i in range(2):
        for h in range(2):
            gain[i : i + 1, h * HALF : (h + 1) * HALF] = total[2 * i + h : 2 * i + h + 1, :]


SMEM = pltpu.MemorySpace.SMEM
VMEM = pltpu.MemorySpace.VMEM


def size(shape, dtype):
    return math.prod(shape) * jnp.dtype(dtype).itemsize


class Arriving:
    def __init__(self, copy, buffer):
        self.copy, self.buffer, self.here = copy, buffer, False

    def ready(self):
        if not self.here:
            self.copy.wait()
            self.here = True
        return self.buffer

    def __getitem__(self, index):
        return self.ready()[index]


class ArrivingBlocks:
    def __init__(self, blocks):
        self.blocks = blocks

    def block(self, j):
        return self.blocks[j]


def fetching(kernel, n_args, n_outs, plan):
    def wrapped(*refs):
        args, outs, rest = list(refs[:n_args]), refs[n_args : n_args + n_outs], refs[n_args + n_outs :]
        scratch, buffers, sems = rest[: len(rest) - len(plan) - 1], rest[len(rest) - len(plan) - 1 : -1], rest[-1]
        arriving = []
        blocks = {}
        for i, (a, j) in enumerate(plan):
            source = refs[a] if j is None else refs[a].at[:, j * D : (j + 1) * D]
            copy = pltpu.make_async_copy(source, buffers[i], sems.at[i])
            copy.start()
            arriving.append(Arriving(copy, buffers[i]))
            if j is None:
                args[a] = arriving[-1]
            else:
                blocks.setdefault(a, {})[j] = arriving[-1]
        for a, found in blocks.items():
            args[a] = ArrivingBlocks(found)
        kernel(*args, *outs, *scratch)
        for value in arriving:
            value.ready()

    return wrapped


def call(kernel, args, outs, scratch=(), spaces=None, spare=6, fetch=(), far_outs=False):
    spaces = dict(spaces or {})
    scratch = list(scratch)
    plan = [f if isinstance(f, tuple) else (f, None) for f in fetch]
    if plan:
        for a, j in plan:
            spaces[a] = pl.ANY
            shape = args[a].shape if j is None else (args[a].shape[0], D)
            scratch.append(pltpu.VMEM(shape, args[a].dtype))
        scratch.append(pltpu.SemaphoreType.DMA((len(plan),)))
        kernel = fetching(kernel, len(args), len(outs), plan)
    vmem = sum(size(a.shape, a.dtype) for i, a in enumerate(args) if i not in spaces)
    vmem += 0 if far_outs else sum(size(*o) for o in outs)
    vmem += sum(size(s.shape, s.dtype) for s in scratch if hasattr(s, "shape") and s.memory_space == VMEM)
    specs = [pl.BlockSpec(memory_space=spaces.get(i, VMEM)) for i in range(len(args))]
    return pl.pallas_call(
        kernel,
        out_shape=[jax.ShapeDtypeStruct(s, t) for s, t in outs],
        in_specs=specs,
        out_specs=[pl.BlockSpec(memory_space=pl.ANY if far_outs else VMEM) for _ in outs],
        scratch_shapes=scratch,
        compiler_params=pltpu.CompilerParams(vmem_limit_bytes=vmem + spare * 1024 * 1024),
    )(*args)


def nothing(outs):
    def kernel(*refs):
        pass

    return pl.pallas_call(
        kernel,
        out_shape=[jax.ShapeDtypeStruct(s, t) for s, t in outs],
        out_specs=[pl.BlockSpec(memory_space=pl.ANY) for _ in outs],
    )()


def on_section(flag, kernel, args, outs, **rest):
    return lax.cond(
        flag, lambda: call(kernel, args, outs, **rest), lambda: nothing(outs)
    )


def along(value, by):
    return lax.ppermute(value, "s", [(0, 1)] if by > 0 else [(1, 0)])


def swap(value, axis, sections=(0, 1)):
    pairs = [(s * 2 + i, s * 2 + 1 - i) for s in sections for i in range(2)]
    return lax.ppermute(value, ("s", axis), pairs)


def plane_shift(value, which, by, sections=(0, 1)):
    pairs = []
    for s in sections:
        for y in range(4):
            for x in range(4):
                for core in range(2):
                    ty, tx = ((y + by) % 4, x) if core == which else (y, (x + by) % 4)
                    pairs.append((((s * 4 + y) * 4 + x) * 2 + core, ((s * 4 + ty) * 4 + tx) * 2 + core))
    return lax.ppermute(value, ("s", "y", "x", "core"), pairs)


def exchange(blocks, which, sections=(0, 1)):
    return [plane_shift(blocks[k], which, k, sections) for k in (1, 2, 3)]


def collect(block, which):
    return [block] + [plane_shift(block, which, -k) for k in (1, 2, 3)]


def pick(stack, index, dim):
    return lax.dynamic_index_in_dim(stack, index, dim, keepdims=False)


def shards(patch_io, byte_states, patch_lengths, patch_live, attn_qkv, attn_out, gains, ff_weights):
    section = lax.axis_index("s")
    core = lax.axis_index("core")
    zh = lax.axis_index("zh")
    y, x = lax.axis_index("y"), lax.axis_index("x")
    first = section == 0
    second = section == 1
    ids = jnp.stack([core, jnp.where(core == 0, y, x), jnp.where(core == 0, x, y), zh, section])
    ids = ids.astype(jnp.int32)
    w_qkv = attn_qkv[0]
    w_out = attn_out[0]
    gain_pair = gains[0]
    micro, seq = patch_io.shape[1], patch_io.shape[3]
    half_bytes = byte_states.shape[2]
    units = ff_weights.shape[0]
    rows = micro * seq
    own_rows = patch_io.reshape(rows, D)
    up_a = along(byte_states[0, 0], -1)
    up_b = along(byte_states[1, 0], -1)
    lower = byte_states.reshape(micro * half_bytes, D)
    w_ff = jnp.swapaxes(ff_weights, 0, 1)
    lengths = patch_lengths[:, 0]
    live = patch_live[:, 0]
    ends = jnp.cumsum(lengths, axis=1)
    bounds = jnp.tile(jnp.stack([ends - lengths, ends], 1), (1, 1, 4))
    places = lax.iota(jnp.int32, seq)
    causal = places[:, None] <= places[None, :]
    diagonal = places[:, None] == places[None, :]
    allowed = causal[None] & ((live[:, :, None] == 1) | diagonal[None])
    allowed = lax.optimization_barrier(jnp.tile(allowed.astype(F32), (1, 1, 4)))

    wide = ((rows, D), BF)
    short = ((seq, D), BF)
    tall = ((micro * half_bytes, D), BF)
    piece = ((half_bytes, D), BF)
    (d_hidden,) = on_section(
        second,
        hidden_back,
        (own_rows, w_ff),
        [((rows, units), F32)],
        spaces={1: pl.ANY},
        scratch=[pltpu.VMEM((units, D), BF), pltpu.SemaphoreType.DMA((4,))],
    )
    pn, q, bn_lo, k_lo, v_lo = on_section(
        first,
        encode_lower,
        (own_rows, lower, w_qkv, gain_pair),
        [wide, wide, tall, tall, tall],
        fetch=((2, 0), 1, (2, 1), (2, 2)),
    )
    rest = []
    for m, up in enumerate((up_a, up_b)):
        rest.append(
            on_section(
                first,
                functools.partial(encode_rest, m),
                (own_rows, up, w_qkv, w_out, gain_pair, bounds, q, k_lo, v_lo),
                [short, short, ((8, 256, GROUP), BF), piece, piece, piece],
                fetch=((2, 1), (2, 2), 7, 8, 3),
            )
        )
    (hb_a, o_a, w_a, bn_a, k_a, v_a), (hb_b, o_b, w_b, bn_b, k_b, v_b) = rest
    arrived = [along(hb_a, 1), along(hb_b, 1)]

    latent_outs = [
        ((rows, D), F32), wide, ((2, D), F32), ((256, HALF), BF), ((512, HALF), BF), ((PACK_ROWS, rows), BF),
    ]

    def latent():
        return call(
            latent_layer,
            (ids, *arrived, own_rows, allowed, w_qkv, w_out, gain_pair, w_ff, d_hidden),
            latent_outs,
            spaces={0: SMEM, 8: pl.ANY},
            fetch=((5, 0), (5, 1), (5, 2), 6),
            scratch=[
                pltpu.VMEM((rows, 3 * D), BF),
                pltpu.VMEM((8, HD, GROUP), BF),
                pltpu.VMEM((rows, D), BF),
                pltpu.VMEM((3, units, D), BF),
                pltpu.VMEM((rows, D), F32),
                pltpu.VMEM((rows, D), F32),
                pltpu.VMEM((rows, 3 * D), BF),
                pltpu.SemaphoreType.DMA((4,)),
            ],
        )

    def turn():
        return nothing(latent_outs[:5]) + call(
            turn_encoder, (pn, o_a, o_b, bn_lo, bn_a, bn_b), latent_outs[5:]
        )

    latents, dhb, latent_gain, norms, lat_grads, packed = lax.cond(second, latent, turn)
    returned = along(dhb, -1)

    packed_far = swap(packed, "core")

    share = units // 16
    ff_block = ((4, 3 * share, HALF), BF)
    ff_half = ((4, 3 * share, GROUP), BF)
    ff_own, ff_right, ff_left, ff_far_a, ff_far_b = on_section(
        second,
        ff_weights_grad,
        (ids, packed, packed_far, norms),
        [ff_block, ff_block, ff_block, ff_half, ff_half],
        spaces={0: SMEM},
    )

    grads_long = ((2304, HALF), BF)
    enc_grads, enc_other = on_section(
        first,
        encoder_attention_back,
        (ids, returned, w_out, q, k_lo, v_lo, k_a, k_b, v_a, v_b, w_a, w_b),
        [grads_long, grads_long],
        spaces={0: SMEM},
        scratch=[pltpu.VMEM((2, 2304, HALF), BF), pltpu.SemaphoreType.DMA((2,))],
        fetch=(2, 5, 8, 10, 4, 6, 9, 11, 7),
        far_outs=True,
    )
    enc_far = swap(enc_other, "core", (0,))
    up_grad, up_gain = on_section(
        first,
        encoder_upper_back,
        (ids, up_a, up_b, w_qkv, gain_pair, enc_grads, enc_other),
        [tall, ((1, D), F32)],
        spaces={0: SMEM},
        fetch=(5, (3, 1), 6, (3, 2), 1, 2),
    )
    up_arrived = along(up_grad, 1)
    ff_far_a, ff_far_b, up_gain = lax.optimization_barrier((ff_far_a, ff_far_b, up_gain))
    from_left = plane_shift(ff_far_a, 0, 1)
    from_right = plane_shift(ff_far_b, 0, -1)
    outs = [((4, 256, HALF), BF)] * 4
    blocks = lax.cond(
        first,
        lambda: call(
            encoder_weights,
            (ids, packed, packed_far, enc_grads, enc_far, up_gain),
            outs,
            spaces={0: SMEM, 5: pl.ANY},
            fetch=(3, 4, 1, 2),
        ),
        lambda: call(latent_weights, (ids, packed, packed_far, lat_grads), outs, spaces={0: SMEM}),
    )
    last, from_left, from_right = lax.optimization_barrier((blocks[3], from_left, from_right))
    blocks = [*blocks[:3], last]
    got, up_arrived = lax.optimization_barrier((exchange(blocks, 0), up_arrived))
    low_outs = [((rows, D), F32), tall, ((2, D), F32)]

    def lower_grads():
        parts = call(
            encoder_lower_back,
            (ids, returned, own_rows, lower, w_qkv, gain_pair, enc_grads, enc_other, blocks[0]),
            low_outs,
            spaces={0: SMEM, 8: pl.ANY},
            fetch=(6, 7, (4, 0), (4, 1), (4, 2), 3),
        )
        return (*parts, *nothing([ff_block, ff_block]))

    def ff_middle():
        added = call(
            ff_add, (ff_right, ff_left, from_left, from_right, blocks[0]), [ff_block, ff_block], spaces={4: pl.ANY}
        )
        return (*nothing(low_outs), *added)

    patch_grad, low_grad, encoder_gain, ff_right_sum, ff_left_sum = lax.cond(first, lower_grads, ff_middle)
    line = [((272, HALF), BF)]
    blocks = call(
        attn_sum_first_gain,
        (ids, blocks[0], *got, encoder_gain, up_gain, latent_gain),
        line * 4,
        spaces={0: SMEM},
    )
    ff_right_sum, ff_left_sum, _ = lax.optimization_barrier((ff_right_sum, ff_left_sum, got))
    from_left = plane_shift(ff_right_sum, 0, 1, (1,))
    from_right = plane_shift(ff_left_sum, 0, -1, (1,))
    (block,) = call(sum_all, (blocks[0], *exchange(blocks, 1)), line)
    byte_grad = jnp.where(first, low_grad, up_arrived)
    patch_out = jnp.where(first, patch_grad, latents)
    from_left, from_right, block, byte_grad, patch_out = lax.optimization_barrier(
        (from_left, from_right, block, byte_grad, patch_out)
    )
    ff_line = ((3 * share, HALF), BF)
    ff_blocks = on_section(
        second, ff_sum_first, (ids, ff_own, from_left, from_right), [ff_line] * 4, spaces={0: SMEM}
    )
    ff_got = exchange(ff_blocks, 1)
    across, ff_got = lax.optimization_barrier((swap(block, "zh"), ff_got))
    (block,) = call(sum_all, (block, across), line)
    lines = collect(block, 1)
    step_in = swap(lines[3][0:16], "core")
    (block,) = call(stack_rows, (*lines, step_in), [((1040, HALF), BF)], spaces={4: pl.ANY})
    pieces = collect(block, 0)
    own_far = swap(block, "core")
    (ff_sum,) = on_section(second, ff_sum_second, (ff_blocks[0], *ff_got), [ff_line])
    ff_sum = ff_sum.reshape(3, 2, share // 2, HALF)
    ff_far = swap(pick(ff_sum, 1 - zh, 1), "zh")
    ff_sum = (pick(ff_sum, zh, 1).astype(F32) + ff_far.astype(F32)).astype(BF).reshape(3, 2, share // 4, HALF)
    ff_mine = pick(ff_sum, core, 1)
    ff_far = swap(pick(ff_sum, 1 - core, 1), "core")

    def ff_result():
        low, high = jnp.where(core == 0, ff_mine, ff_far), jnp.where(core == 0, ff_far, ff_mine)
        return jnp.swapaxes(jnp.concatenate([low, high], 2), 0, 1).astype(F32)

    ff_grad = lax.cond(second, ff_result, lambda: jnp.zeros((share // 4, 3, D), F32))
    ff_grad, *pieces = lax.optimization_barrier((ff_grad, *pieces))
    pieces = pieces + [own_far] + [swap(p, "core") for p in pieces[1:]]
    whole = lambda p: pl.BlockSpec(p.shape, lambda i, n=p.ndim: (0,) * n)
    total_qkv, total_out, total_gain = pl.pallas_call(
        final_attn,
        grid=(4,),
        out_shape=[
            jax.ShapeDtypeStruct((D, 3 * D), F32),
            jax.ShapeDtypeStruct((D, D), F32),
            jax.ShapeDtypeStruct((2, D), F32),
        ],
        in_specs=[pl.BlockSpec(memory_space=SMEM)] + [whole(p) for p in pieces],
        out_specs=[
            pl.BlockSpec((256, 3 * D), lambda i: (i, 0)),
            pl.BlockSpec((256, D), lambda i: (i, 0)),
            pl.BlockSpec((2, D), lambda i: (0, 0)),
        ],
        compiler_params=pltpu.CompilerParams(vmem_limit_bytes=FINAL_VMEM),
    )(ids, *pieces)
    return (
        patch_out.reshape(1, micro, 1, seq, D),
        byte_grad.reshape(micro, 1, half_bytes, D),
        total_qkv[None],
        total_out[None],
        total_gain[None],
        ff_grad[None],
    )


def solution(mesh):
    fine = Mesh(mesh.devices.reshape(2, 4, 4, 2, 2), ("s",) + BATCH)
    in_specs = (
        P("s", None, BATCH, None, None),
        P(None, BATCH, "s", None),
        P(None, BATCH, None),
        P(None, BATCH, None),
        P("s", None, None),
        P("s", None, None),
        P("s", None, None),
        P(),
    )
    out_specs = (
        P("s", None, BATCH, None, None),
        P(None, BATCH, "s", None),
        P("s", None, None),
        P("s", None, None),
        P("s", None, None),
        P("s", BATCH, None, None),
    )
    return jax.shard_map(shards, mesh=fine, in_specs=in_specs, out_specs=out_specs, check_vma=False)
```

```python
import functools
import math

import jax
import jax.numpy as jnp
from jax import lax
from jax.experimental import pallas as pl
from jax.experimental.pallas import tpu as pltpu
from jax.sharding import Mesh
from jax.sharding import PartitionSpec as P

HD = 64
SCALE = HD**-0.5
EPS = 1e-05
NEG = -1e30
BATCH = ("y", "x", "zh", "core")
BF = jnp.bfloat16
F32 = jnp.float32
D = 1024
HALF = 512
GROUP = 256
FINAL_VMEM = 32 * 1024 * 1024


UNITS = 2816
PACK_NORMS = 3 * UNITS
PACK_LEFT = PACK_NORMS + 4 * 256
PACK_GRADS = PACK_LEFT + 2 * D
PACK_ROWS = PACK_GRADS + 4 * 512


def nn(a, b):
    return lax.dot_general(a, b, (((1,), (0,)), ((), ())), preferred_element_type=F32)


def nt(a, b):
    return lax.dot_general(a, b, (((1,), (1,)), ((), ())), preferred_element_type=F32)


def tn(a, b):
    return lax.dot_general(a, b, (((0,), (0,)), ((), ())), preferred_element_type=F32)


def inverse_rms(x):
    return lax.rsqrt(jnp.mean(x * x, axis=-1, keepdims=True) + EPS)


def norm_back(x, gain, up):
    r = inverse_rms(x)
    scaled = up * gain
    inner = jnp.mean(scaled * x, axis=-1, keepdims=True)
    return r * (scaled - x * (r * r * inner)), up * (x * r)


def stack_heads(rows):
    head = lax.broadcasted_iota(jnp.int32, rows.shape, 1) // HD
    return jnp.concatenate([jnp.where(head == h, rows, jnp.zeros_like(rows)) for h in range(4)], 0)


def unstack_heads(stacked):
    head = lax.broadcasted_iota(jnp.int32, (HD, GROUP), 1) // HD
    out = stacked[0:HD]
    for h in range(1, 4):
        out = jnp.where(head == h, stacked[h * HD : (h + 1) * HD], out)
    return out


def softmax_columns(scores):
    top = functools.reduce(jnp.maximum, [jnp.max(s, axis=0, keepdims=True) for s in scores])
    parts = [jnp.exp(s - top) for s in scores]
    inverse = 1.0 / sum(jnp.sum(p, axis=0, keepdims=True) for p in parts)
    return [(p * inverse).astype(BF) for p in parts]


def encode_lower(patch, low, w_qkv, gains, pn, q, bn, k, v):
    x = patch[...].astype(F32)
    normed = (x * inverse_rms(x) * gains[0:1]).astype(BF)
    pn[...] = normed
    q[...] = nn(normed, w_qkv.block(0)[...]).astype(BF)
    for i in range(2):
        at = pl.ds(i * 256, 256)
        b = low[at, :].astype(F32)
        normed = (b * inverse_rms(b) * gains[1:2]).astype(BF)
        bn[at, :] = normed
        k[at, :] = nn(normed, w_qkv.block(1)[...]).astype(BF)
        v[at, :] = nn(normed, w_qkv.block(2)[...]).astype(BF)


def encode_rest(m, patch, up, w_qkv, w_out, gains, bounds, q, k_lo, v_lo, hb, o1, weights, bn, k, v):
    b = up[...].astype(F32)
    normed = (b * inverse_rms(b) * gains[1:2]).astype(BF)
    bn[...] = normed
    k[...] = nn(normed, w_qkv.block(1)[...]).astype(BF)
    v[...] = nn(normed, w_qkv.block(2)[...]).astype(BF)
    spot = lax.broadcasted_iota(jnp.int32, (256, GROUP), 0)
    start = bounds[m, 0:1, :]
    end = bounds[m, 1:2, :]
    inside = [(spot + h * 256 >= start) & (spot + h * 256 < end) for h in range(2)]
    low_at = slice(m * 256, (m + 1) * 256)
    rows = slice(m * HD, (m + 1) * HD)
    for g in range(4):
        lanes = slice(g * GROUP, (g + 1) * GROUP)
        stacked = stack_heads(q[rows, lanes] * BF(SCALE))
        scores = [
            jnp.where(inside[h], nt(keys, stacked), NEG)
            for h, keys in enumerate((k_lo[low_at, lanes], k[:, lanes]))
        ]
        w = softmax_columns(scores)
        weights[g * 2] = w[0]
        weights[g * 2 + 1] = w[1]
        mixed = tn(w[0], v_lo[low_at, lanes]) + tn(w[1], v[:, lanes])
        o1[:, lanes] = unstack_heads(mixed).astype(BF)
    hb[...] = (patch[rows, :].astype(F32) + nn(o1[...], w_out[...])).astype(BF)


def latent_layer(
    ids, hb_a, hb_b, cot, allowed, w_qkv, w_out, gains, w_ff, d_hidden,
    latents, dhb, gain_grad, norms, grads, packed,
    qkv, weights, o2, ff_buf, acc_out, acc_norm, dqkv, sems,
):
    core = ids[0]
    units = w_ff.shape[1]
    step = 256
    parts = 4
    part = units // parts

    fetches = []
    for i in range(parts):
        at = slice(i * part, (i + 1) * part)
        fetches.append(pltpu.make_async_copy(w_ff.at[:, at, :], ff_buf.at[:, at, :], sems.at[i]))
        fetches[-1].start()
    x = jnp.concatenate([hb_a[...], hb_b[...]], 0).astype(F32)
    normed = (x * inverse_rms(x) * gains[0:1]).astype(BF)
    packed[PACK_LEFT : PACK_LEFT + D, :] = normed.T
    for j in range(3):
        qkv[:, j * D : (j + 1) * D] = nn(normed, w_qkv.block(j)[...]).astype(BF)
    for m in range(2):
        rows = slice(m * HD, (m + 1) * HD)
        for g in range(4):
            lanes = slice(g * GROUP, (g + 1) * GROUP)
            k_lanes = slice(D + g * GROUP, D + (g + 1) * GROUP)
            v_lanes = slice(2 * D + g * GROUP, 2 * D + (g + 1) * GROUP)
            stacked = stack_heads(qkv[rows, lanes] * BF(SCALE))
            scores = jnp.where(allowed[m] > 0.5, nt(qkv[rows, k_lanes], stacked), NEG)
            (w,) = softmax_columns([scores])
            weights[m * 4 + g] = w
            o2[rows, lanes] = unstack_heads(tn(w, qkv[rows, v_lanes])).astype(BF)
    packed[PACK_LEFT + D : PACK_LEFT + 2 * D, :] = o2[...].T
    after = x + nn(o2[...], w_out[...])
    yn = (after * inverse_rms(after) * gains[1:2]).astype(BF)
    c = cot[...]
    for h in range(2):

        @pl.when(core == h)
        def _(h=h):
            norms[0:128, :] = yn[:, h * HALF : (h + 1) * HALF]
            norms[128:256, :] = c[:, h * HALF : (h + 1) * HALF]

        @pl.when(core != h)
        def _(h=h):
            for b in range(4):
                lanes = slice(h * HALF + b * 128, h * HALF + (b + 1) * 128)
                packed[PACK_NORMS + b * 256 : PACK_NORMS + b * 256 + 128, :] = yn[:, lanes]
                packed[PACK_NORMS + b * 256 + 128 : PACK_NORMS + (b + 1) * 256, :] = c[:, lanes]

    for copy in fetches:
        copy.wait()
    acc_out[...] = after
    for i in range(units // step):
        at = slice(i * step, (i + 1) * step)
        gate = nt(yn, ff_buf[0, at, :])
        upward = nt(yn, ff_buf[1, at, :])
        du = d_hidden[:, at]
        sig = 1.0 / (1.0 + jnp.exp(-gate))
        active = gate * sig
        hidden = (active * upward).astype(BF)
        d_gate = (du * upward * (sig * (1.0 + gate * (1.0 - sig)))).astype(BF)
        d_up = (du * active).astype(BF)
        for j, value in enumerate((d_gate, d_up, hidden)):
            packed[i * step + j * units : (i + 1) * step + j * units, :] = value.T
        acc_out[...] += nn(hidden, ff_buf[2, at, :])
        back = nn(d_gate, ff_buf[0, at, :]) + nn(d_up, ff_buf[1, at, :])
        if i == 0:
            acc_norm[...] = back
        else:
            acc_norm[...] += back
    latents[...] = acc_out[...]
    back, gain_rows = norm_back(after, gains[1:2], acc_norm[...])
    gain_grad[1:2, :] = jnp.sum(gain_rows, axis=0, keepdims=True)
    d_after = c.astype(F32) + back
    da = d_after.astype(BF)
    d_mixed = nt(da, w_out[...]).astype(BF)
    for m in range(2):
        rows = slice(m * HD, (m + 1) * HD)
        for g in range(4):
            lanes = slice(g * GROUP, (g + 1) * GROUP)
            k_lanes = slice(D + g * GROUP, D + (g + 1) * GROUP)
            v_lanes = slice(2 * D + g * GROUP, 2 * D + (g + 1) * GROUP)
            q_stacked = stack_heads(qkv[rows, lanes] * BF(SCALE))
            o_stacked = stack_heads(d_mixed[rows, lanes])
            w_low = weights[m * 4 + g]
            w = w_low.astype(F32)
            dw = nt(qkv[rows, v_lanes], o_stacked)
            inner = jnp.sum(dw * w, axis=0, keepdims=True)
            ds = (w * (dw - inner)).astype(BF)
            dqkv[rows, lanes] = (unstack_heads(tn(ds, qkv[rows, k_lanes])) * SCALE).astype(BF)
            dqkv[rows, k_lanes] = nn(ds, q_stacked).astype(BF)
            dqkv[rows, v_lanes] = nn(w_low, o_stacked).astype(BF)
    d_normed = sum(nt(dqkv[:, j * D : (j + 1) * D], w_qkv.block(j)[...]) for j in range(3))
    back, gain_rows = norm_back(x, gains[0:1], d_normed)
    gain_grad[0:1, :] = jnp.sum(gain_rows, axis=0, keepdims=True)
    dhb[...] = (d_after + back).astype(BF)
    for h in range(2):
        pieces = (
            dqkv[:, h * HALF : (h + 1) * HALF],
            da[:, h * HALF : (h + 1) * HALF],
            dqkv[:, D + h * HALF : D + (h + 1) * HALF],
            dqkv[:, 2 * D + h * HALF : 2 * D + (h + 1) * HALF],
        )

        @pl.when(core == h)
        def _(pieces=pieces):
            for i, value in enumerate(pieces):
                grads[i * 128 : (i + 1) * 128, :] = value

        @pl.when(core != h)
        def _(pieces=pieces):
            for i, value in enumerate(pieces):
                for b in range(4):
                    first = PACK_GRADS + b * 512 + i * 128
                    packed[first : first + 128, :] = value[:, b * 128 : (b + 1) * 128]


def hidden_back(cot, w_ff, d_hidden, buffer, sems):
    parts = 4
    part = w_ff.shape[1] // parts
    copies = []
    for i in range(parts):
        at = slice(i * part, (i + 1) * part)
        copies.append(pltpu.make_async_copy(w_ff.at[2, at, :], buffer.at[at, :], sems.at[i]))
        copies[-1].start()
    for copy in copies:
        copy.wait()
    for i in range(w_ff.shape[1] // 256):
        at = slice(i * 256, (i + 1) * 256)
        d_hidden[:, at] = nt(cot[...], buffer[at, :])


def encoder_attention_back(
    ids, dhb, w_out, q, k_lo, v_lo, k_a, k_b, v_a, v_b, w_a, w_b, mine, other, both, sems
):
    d_mixed = nt(dhb[...], w_out[...]).astype(BF)
    for g in range(4):
        lanes = slice(g * GROUP, (g + 1) * GROUP)
        out_lanes = slice((g % 2) * GROUP, (g % 2 + 1) * GROUP)
        half = jnp.where(ids[0] == g // 2, 0, 1)

        def put(at, value, half=half, out_lanes=out_lanes):
            both[half, at, out_lanes] = value

        put(slice(128, 256), dhb[:, lanes])
        for m, (k_up, v_up, weights) in enumerate(((k_a, v_a, w_a), (k_b, v_b, w_b))):
            rows = slice(m * HD, (m + 1) * HD)
            low_at = slice(m * 256, (m + 1) * 256)
            q_stacked = stack_heads(q[rows, lanes] * BF(SCALE))
            o_stacked = stack_heads(d_mixed[rows, lanes])
            low = [weights[g * 2 + h] for h in range(2)]
            w = [piece.astype(F32) for piece in low]
            dw = [nt(values, o_stacked) for values in (v_lo[low_at, lanes], v_up[:, lanes])]
            inner = sum(jnp.sum(a * b, axis=0, keepdims=True) for a, b in zip(dw, w))
            ds = [(b * (a - inner)).astype(BF) for a, b in zip(dw, w)]
            dq = tn(ds[0], k_lo[low_at, lanes]) + tn(ds[1], k_up[:, lanes])
            put(rows, (unstack_heads(dq) * SCALE).astype(BF))
            for h in range(2):
                base = h * HALF + m * 256
                put(slice(256 + base, 512 + base), nn(ds[h], q_stacked).astype(BF))
                put(slice(1280 + base, 1536 + base), nn(low[h], o_stacked).astype(BF))
    copies = [pltpu.make_async_copy(both.at[i], out, sems.at[i]) for i, out in enumerate((mine, other))]
    for copy in copies:
        copy.start()
    for copy in copies:
        copy.wait()


def both_columns(core, block, w_qkv):
    return [
        w_qkv.block(block)[:, pl.ds(pl.multiple_of(which * HALF, HALF), HALF)] for which in (core, 1 - core)
    ]


def bytes_back(core, h, source, w_qkv, gains, grads):
    d_norm = sum(
        nt(ref[1024 * block - 768 + h * HALF : 1024 * block - 256 + h * HALF, :], columns)
        for block in (1, 2)
        for ref, columns in zip(grads, both_columns(core, block, w_qkv))
    )
    back, gain_rows = norm_back(source.astype(F32), gains[1:2], d_norm)
    return back.astype(BF), jnp.sum(gain_rows, axis=0, keepdims=True)


def encoder_upper_back(ids, up_a, up_b, w_qkv, gains, mine, other, up_grad, gain_grad):
    source = jnp.concatenate([up_a[...], up_b[...]], 0)
    back, rows = bytes_back(ids[0], 1, source, w_qkv, gains, (mine, other))
    up_grad[...] = back
    gain_grad[...] = rows


def encoder_lower_back(
    ids, dhb, patch, low, w_qkv, gains, mine, other, after, patch_grad, low_grad, gain_grad
):
    core = ids[0]
    up_norm = sum(nt(ref[0:128, :], columns) for ref, columns in zip((mine, other), both_columns(core, 0, w_qkv)))
    back, gain_rows = norm_back(patch[...].astype(F32), gains[0:1], up_norm)
    gain_grad[0:1, :] = jnp.sum(gain_rows, axis=0, keepdims=True)
    patch_grad[...] = dhb[...].astype(F32) + back
    back, rows = bytes_back(core, 0, low[...], w_qkv, gains, (mine, other))
    low_grad[...] = back
    gain_grad[1:2, :] = rows


def turn_encoder(pn, o_a, o_b, bn_lo, bn_a, bn_b, packed):
    for b, rows in enumerate([bn_lo[i * 128 : (i + 1) * 128, :] for i in range(4)]
                             + [ref[i * 128 : (i + 1) * 128, :] for ref in (bn_a, bn_b) for i in range(2)]):
        packed[b * D : (b + 1) * D, :] = rows.T
    packed[PACK_LEFT : PACK_LEFT + D, :] = pn[...].T
    packed[PACK_LEFT + D : PACK_LEFT + 2 * D, :] = jnp.concatenate([o_a[...], o_b[...]], 0).T


def rows_of_both(left, left_far, at):
    return jnp.concatenate([left[at, :], left_far[at, :]], 1)


def below(near, far, rows):
    return jnp.concatenate([near[rows, :], far[rows, :]], 0)


def encoder_weights(ids, packed, packed_far, near, far, after, *blocks):
    u = ids[1]
    queries = below(near, far, slice(0, 128))
    outputs = below(near, far, slice(128, 256))
    for k in range(4):
        first = lax.rem(u + k, 4) * 256

        def at(base, first=first):
            return pl.ds(pl.multiple_of(first + base, 256), 256)

        blocks[k][0] = nn(rows_of_both(packed, packed_far, at(PACK_LEFT)), queries).astype(BF)
        blocks[k][3] = nn(rows_of_both(packed, packed_far, at(PACK_LEFT + D)), outputs).astype(BF)
        lefts = [jnp.concatenate([ref[at(b * D), :] for b in range(8)], 1) for ref in (packed, packed_far)]
        for block in (1, 2):
            rows = slice(1024 * block - 768, 1024 * block + 256)
            blocks[k][block] = (nn(lefts[0], near[rows, :]) + nn(lefts[1], far[rows, :])).astype(BF)


def unpack(packed, first, rows):
    return jnp.concatenate([packed[first + b * rows : first + (b + 1) * rows, :] for b in range(4)], 1)


def latent_weights(ids, packed, packed_far, near, *blocks):
    u = ids[1]
    far = unpack(packed_far, PACK_GRADS, 512)
    rights = [jnp.concatenate([near[i * 128 : (i + 1) * 128, :], far[i * 128 : (i + 1) * 128, :]], 0) for i in range(4)]
    for k in range(4):
        first = PACK_LEFT + lax.rem(u + k, 4) * 256
        at = pl.ds(pl.multiple_of(first, 256), 256)
        low_at = pl.ds(pl.multiple_of(first + D, 256), 256)
        for block, (source, i) in enumerate(((at, 0), (at, 2), (at, 3), (low_at, 1))):
            blocks[k][block] = nn(rows_of_both(packed, packed_far, source), rights[i]).astype(BF)


def ff_weights_grad(ids, packed, packed_far, norms, own, right, left, far_a, far_b):
    core, u = ids[0], ids[1]
    share = UNITS // 16
    far = unpack(packed_far, PACK_NORMS, 256)
    normed = jnp.concatenate([norms[0:128, :], far[0:128, :]], 0)
    cot = jnp.concatenate([norms[128:256, :], far[128:256, :]], 0)
    for k in range(4):
        there = lax.rem(u + k, 4)
        for j in range(3):
            parts = []
            for v in range(4):
                chunk = jnp.where(core == 0, there * 4 + v, v * 4 + there)
                at = pl.ds(pl.multiple_of(j * UNITS + chunk * share, 16), share)
                parts.append(rows_of_both(packed, packed_far, at))
            value = nn(jnp.concatenate(parts, 0), normed if j < 2 else cot).astype(BF)
            rows = slice(j * share, (j + 1) * share)
            for v in range(4):
                piece = value[v * share : (v + 1) * share, :]
                if k == 2:
                    far_a[v, rows, :] = piece[:, :GROUP]
                    far_b[v, rows, :] = piece[:, GROUP:]
                else:
                    (own, right, None, left)[k][v, rows, :] = piece


def ff_add(right, left, from_left, from_right, after, new_right, new_left):
    new_right[:, :, 0:GROUP] = (right[:, :, 0:GROUP].astype(F32) + from_left[...].astype(F32)).astype(BF)
    new_right[:, :, GROUP:] = right[:, :, GROUP:]
    new_left[:, :, 0:GROUP] = left[:, :, 0:GROUP]
    new_left[:, :, GROUP:] = (left[:, :, GROUP:].astype(F32) + from_right[...].astype(F32)).astype(BF)


def sum_four(own, a, b, c):
    return own.astype(F32) + a.astype(F32) + b.astype(F32) + c.astype(F32)


def pack_gain(value):
    high = value.astype(BF)
    low = (value - high.astype(F32)).astype(BF)
    return jnp.concatenate(
        [high.astype(F32), low.astype(F32), jnp.zeros((8, HALF), F32)], 0
    ).astype(BF)


def unpack_gain(rows):
    rows = rows.astype(F32)
    return rows[0:4] + rows[4:8]


GAIN_AT = slice(256, 272)


def attn_sum_first(ids, own, a, b, c, *outs):
    v = ids[2]
    for k in range(4):
        at = pl.ds(pl.multiple_of(lax.rem(v + k, 4) * HD, HD), HD)
        for block in range(4):
            outs[k][block * HD : (block + 1) * HD, :] = sum_four(
                own[block, at, :], a[block, at, :], b[block, at, :], c[block, at, :]
            ).astype(BF)


def attn_sum_first_gain(ids, own, a, b, c, enc_gain, up_gain, lat_gain, *outs):
    attn_sum_first(ids, own, a, b, c, *outs)
    first = ids[4] == 0
    gain = jnp.where(
        first, jnp.concatenate([enc_gain[0:1, :], enc_gain[1:2, :] + up_gain[...]], 0), lat_gain[...]
    )
    halves = [gain[i : i + 1, h * HALF : (h + 1) * HALF] for i in range(2) for h in range(2)]
    packed = pack_gain(jnp.concatenate(halves, 0))
    for out in outs:
        out[GAIN_AT, :] = packed


def sum_all(*refs):
    refs, out = refs[:-1], refs[-1]
    out[0:256, :] = sum(ref[0:256, :].astype(F32) for ref in refs).astype(BF)
    out[GAIN_AT, :] = pack_gain(sum(unpack_gain(ref[GAIN_AT, :]) for ref in refs))


def stack_rows(*refs):
    refs, out = refs[:-2], refs[-1]
    for j, ref in enumerate(refs):
        out[j * 256 : (j + 1) * 256, :] = ref[0:256, :]
    out[1024:1040, :] = refs[0][GAIN_AT, :]


def ff_sum_first(ids, own, a, b, *outs):
    v = ids[2]
    for k in range(4):
        at = lax.rem(v + k, 4)
        outs[k][...] = (own[at].astype(F32) + a[at].astype(F32) + b[at].astype(F32)).astype(BF)


def ff_sum_second(own, a, b, c, out):
    out[...] = sum_four(own[...], a[...], b[...], c[...]).astype(BF)


def final_attn(ids, *refs):
    pieces, (qkv, out, gain) = refs[:8], refs[8:]
    step = pl.program_id(0)
    for side in range(2):
        core = ids[0] if side == 0 else 1 - ids[0]
        u = ids[1] if side == 0 else ids[2]
        v = ids[2] if side == 0 else ids[1]
        for k in range(4):
            piece = pieces[side * 4 + k]

            @pl.when(lax.rem(u + k, 4) == step)
            def _(piece=piece, v=v, core=core):
                for j in range(4):
                    at = pl.ds(pl.multiple_of(lax.rem(v + j, 4) * HD, HD), HD)
                    for block in range(4):
                        target, column = (qkv, block * D) if block < 3 else (out, 0)
                        lanes = pl.ds(pl.multiple_of(core * HALF + column, HALF), HALF)
                        first = j * 256 + block * HD
                        target[at, lanes] = piece[first : first + HD, :].astype(F32)

    mine = sum(unpack_gain(piece[1024:1040, :]) for piece in pieces[:4])
    other = sum(unpack_gain(piece[1024:1040, :]) for piece in pieces[4:])
    total = mine + other
    for i in range(2):
        for h in range(2):
            gain[i : i + 1, h * HALF : (h + 1) * HALF] = total[2 * i + h : 2 * i + h + 1, :]


SMEM = pltpu.MemorySpace.SMEM
VMEM = pltpu.MemorySpace.VMEM


def size(shape, dtype):
    return math.prod(shape) * jnp.dtype(dtype).itemsize


class Arriving:
    def __init__(self, copy, buffer):
        self.copy, self.buffer, self.here = copy, buffer, False

    def ready(self):
        if not self.here:
            self.copy.wait()
            self.here = True
        return self.buffer

    def __getitem__(self, index):
        return self.ready()[index]


class ArrivingBlocks:
    def __init__(self, blocks):
        self.blocks = blocks

    def block(self, j):
        return self.blocks[j]


def fetching(kernel, n_args, n_outs, plan):
    def wrapped(*refs):
        args, outs, rest = list(refs[:n_args]), refs[n_args : n_args + n_outs], refs[n_args + n_outs :]
        scratch, buffers, sems = rest[: len(rest) - len(plan) - 1], rest[len(rest) - len(plan) - 1 : -1], rest[-1]
        arriving = []
        blocks = {}
        for i, (a, j) in enumerate(plan):
            source = refs[a] if j is None else refs[a].at[:, j * D : (j + 1) * D]
            copy = pltpu.make_async_copy(source, buffers[i], sems.at[i])
            copy.start()
            arriving.append(Arriving(copy, buffers[i]))
            if j is None:
                args[a] = arriving[-1]
            else:
                blocks.setdefault(a, {})[j] = arriving[-1]
        for a, found in blocks.items():
            args[a] = ArrivingBlocks(found)
        kernel(*args, *outs, *scratch)
        for value in arriving:
            value.ready()

    return wrapped


def call(kernel, args, outs, scratch=(), spaces=None, spare=6, fetch=(), far_outs=False):
    spaces = dict(spaces or {})
    scratch = list(scratch)
    plan = [f if isinstance(f, tuple) else (f, None) for f in fetch]
    if plan:
        for a, j in plan:
            spaces[a] = pl.ANY
            shape = args[a].shape if j is None else (args[a].shape[0], D)
            scratch.append(pltpu.VMEM(shape, args[a].dtype))
        scratch.append(pltpu.SemaphoreType.DMA((len(plan),)))
        kernel = fetching(kernel, len(args), len(outs), plan)
    vmem = sum(size(a.shape, a.dtype) for i, a in enumerate(args) if i not in spaces)
    vmem += 0 if far_outs else sum(size(*o) for o in outs)
    vmem += sum(size(s.shape, s.dtype) for s in scratch if hasattr(s, "shape") and s.memory_space == VMEM)
    specs = [pl.BlockSpec(memory_space=spaces.get(i, VMEM)) for i in range(len(args))]
    return pl.pallas_call(
        kernel,
        out_shape=[jax.ShapeDtypeStruct(s, t) for s, t in outs],
        in_specs=specs,
        out_specs=[pl.BlockSpec(memory_space=pl.ANY if far_outs else VMEM) for _ in outs],
        scratch_shapes=scratch,
        compiler_params=pltpu.CompilerParams(vmem_limit_bytes=vmem + spare * 1024 * 1024),
    )(*args)


def nothing(outs):
    def kernel(*refs):
        pass

    return pl.pallas_call(
        kernel,
        out_shape=[jax.ShapeDtypeStruct(s, t) for s, t in outs],
        out_specs=[pl.BlockSpec(memory_space=pl.ANY) for _ in outs],
    )()


def on_section(flag, kernel, args, outs, **rest):
    return lax.cond(
        flag, lambda: call(kernel, args, outs, **rest), lambda: nothing(outs)
    )


def along(value, by):
    return lax.ppermute(value, "s", [(0, 1)] if by > 0 else [(1, 0)])


def swap(value, axis, sections=(0, 1)):
    pairs = [(s * 2 + i, s * 2 + 1 - i) for s in sections for i in range(2)]
    return lax.ppermute(value, ("s", axis), pairs)


def plane_shift(value, which, by, sections=(0, 1)):
    pairs = []
    for s in sections:
        for y in range(4):
            for x in range(4):
                for core in range(2):
                    ty, tx = ((y + by) % 4, x) if core == which else (y, (x + by) % 4)
                    pairs.append((((s * 4 + y) * 4 + x) * 2 + core, ((s * 4 + ty) * 4 + tx) * 2 + core))
    return lax.ppermute(value, ("s", "y", "x", "core"), pairs)


def exchange(blocks, which, sections=(0, 1)):
    return [plane_shift(blocks[k], which, k, sections) for k in (1, 2, 3)]


def collect(block, which):
    return [block] + [plane_shift(block, which, -k) for k in (1, 2, 3)]


def pick(stack, index, dim):
    return lax.dynamic_index_in_dim(stack, index, dim, keepdims=False)


def shards(patch_io, byte_states, patch_lengths, patch_live, attn_qkv, attn_out, gains, ff_weights):
    section = lax.axis_index("s")
    core = lax.axis_index("core")
    zh = lax.axis_index("zh")
    y, x = lax.axis_index("y"), lax.axis_index("x")
    first = section == 0
    second = section == 1
    ids = jnp.stack([core, jnp.where(core == 0, y, x), jnp.where(core == 0, x, y), zh, section])
    ids = ids.astype(jnp.int32)
    w_qkv = attn_qkv[0]
    w_out = attn_out[0]
    gain_pair = gains[0]
    micro, seq = patch_io.shape[1], patch_io.shape[3]
    half_bytes = byte_states.shape[2]
    units = ff_weights.shape[0]
    rows = micro * seq
    own_rows = patch_io.reshape(rows, D)
    up_a = along(byte_states[0, 0], -1)
    up_b = along(byte_states[1, 0], -1)
    lower = byte_states.reshape(micro * half_bytes, D)
    w_ff = jnp.swapaxes(ff_weights, 0, 1)
    lengths = patch_lengths[:, 0]
    live = patch_live[:, 0]
    ends = jnp.cumsum(lengths, axis=1)
    bounds = jnp.tile(jnp.stack([ends - lengths, ends], 1), (1, 1, 4))
    places = lax.iota(jnp.int32, seq)
    causal = places[:, None] <= places[None, :]
    diagonal = places[:, None] == places[None, :]
    allowed = causal[None] & ((live[:, :, None] == 1) | diagonal[None])
    allowed = lax.optimization_barrier(jnp.tile(allowed.astype(F32), (1, 1, 4)))

    wide = ((rows, D), BF)
    short = ((seq, D), BF)
    tall = ((micro * half_bytes, D), BF)
    piece = ((half_bytes, D), BF)
    (d_hidden,) = on_section(
        second,
        hidden_back,
        (own_rows, w_ff),
        [((rows, units), F32)],
        spaces={1: pl.ANY},
        scratch=[pltpu.VMEM((units, D), BF), pltpu.SemaphoreType.DMA((4,))],
    )
    pn, q, bn_lo, k_lo, v_lo = on_section(
        first,
        encode_lower,
        (own_rows, lower, w_qkv, gain_pair),
        [wide, wide, tall, tall, tall],
        fetch=((2, 0), 1, (2, 1), (2, 2)),
    )
    rest = []
    for m, up in enumerate((up_a, up_b)):
        rest.append(
            on_section(
                first,
                functools.partial(encode_rest, m),
                (own_rows, up, w_qkv, w_out, gain_pair, bounds, q, k_lo, v_lo),
                [short, short, ((8, 256, GROUP), BF), piece, piece, piece],
                fetch=((2, 1), (2, 2), 7, 8, 3),
            )
        )
    (hb_a, o_a, w_a, bn_a, k_a, v_a), (hb_b, o_b, w_b, bn_b, k_b, v_b) = rest
    arrived = [along(hb_a, 1), along(hb_b, 1)]

    latent_outs = [
        ((rows, D), F32), wide, ((2, D), F32), ((256, HALF), BF), ((512, HALF), BF), ((PACK_ROWS, rows), BF),
    ]

    def latent():
        return call(
            latent_layer,
            (ids, *arrived, own_rows, allowed, w_qkv, w_out, gain_pair, w_ff, d_hidden),
            latent_outs,
            spaces={0: SMEM, 8: pl.ANY},
            fetch=((5, 0), (5, 1), (5, 2), 6),
            scratch=[
                pltpu.VMEM((rows, 3 * D), BF),
                pltpu.VMEM((8, HD, GROUP), BF),
                pltpu.VMEM((rows, D), BF),
                pltpu.VMEM((3, units, D), BF),
                pltpu.VMEM((rows, D), F32),
                pltpu.VMEM((rows, D), F32),
                pltpu.VMEM((rows, 3 * D), BF),
                pltpu.SemaphoreType.DMA((4,)),
            ],
        )

    def turn():
        return nothing(latent_outs[:5]) + call(
            turn_encoder, (pn, o_a, o_b, bn_lo, bn_a, bn_b), latent_outs[5:]
        )

    latents, dhb, latent_gain, norms, lat_grads, packed = lax.cond(second, latent, turn)
    returned = along(dhb, -1)

    packed_far = swap(packed, "core")

    share = units // 16
    ff_block = ((4, 3 * share, HALF), BF)
    ff_half = ((4, 3 * share, GROUP), BF)
    ff_own, ff_right, ff_left, ff_far_a, ff_far_b = on_section(
        second,
        ff_weights_grad,
        (ids, packed, packed_far, norms),
        [ff_block, ff_block, ff_block, ff_half, ff_half],
        spaces={0: SMEM},
    )

    grads_long = ((2304, HALF), BF)
    enc_grads, enc_other = on_section(
        first,
        encoder_attention_back,
        (ids, returned, w_out, q, k_lo, v_lo, k_a, k_b, v_a, v_b, w_a, w_b),
        [grads_long, grads_long],
        spaces={0: SMEM},
        scratch=[pltpu.VMEM((2, 2304, HALF), BF), pltpu.SemaphoreType.DMA((2,))],
        fetch=(2, 5, 8, 10, 4, 6, 9, 11, 7),
        far_outs=True,
    )
    enc_far = swap(enc_other, "core", (0,))
    up_grad, up_gain = on_section(
        first,
        encoder_upper_back,
        (ids, up_a, up_b, w_qkv, gain_pair, enc_grads, enc_other),
        [tall, ((1, D), F32)],
        spaces={0: SMEM},
        fetch=(5, (3, 1), 6, (3, 2), 1, 2),
    )
    up_arrived = along(up_grad, 1)
    ff_far_a, ff_far_b, up_gain = lax.optimization_barrier((ff_far_a, ff_far_b, up_gain))
    from_left = plane_shift(ff_far_a, 0, 1)
    from_right = plane_shift(ff_far_b, 0, -1)
    outs = [((4, 256, HALF), BF)] * 4
    blocks = lax.cond(
        first,
        lambda: call(
            encoder_weights,
            (ids, packed, packed_far, enc_grads, enc_far, up_gain),
            outs,
            spaces={0: SMEM, 5: pl.ANY},
            fetch=(3, 4, 1, 2),
        ),
        lambda: call(latent_weights, (ids, packed, packed_far, lat_grads), outs, spaces={0: SMEM}),
    )
    last, from_left, from_right = lax.optimization_barrier((blocks[3], from_left, from_right))
    blocks = [*blocks[:3], last]
    got, up_arrived = lax.optimization_barrier((exchange(blocks, 0), up_arrived))
    low_outs = [((rows, D), F32), tall, ((2, D), F32)]

    def lower_grads():
        parts = call(
            encoder_lower_back,
            (ids, returned, own_rows, lower, w_qkv, gain_pair, enc_grads, enc_other, blocks[0]),
            low_outs,
            spaces={0: SMEM, 8: pl.ANY},
            fetch=(6, 7, (4, 0), (4, 1), (4, 2), 3),
        )
        return (*parts, *nothing([ff_block, ff_block]))

    def ff_middle():
        added = call(
            ff_add, (ff_right, ff_left, from_left, from_right, blocks[0]), [ff_block, ff_block], spaces={4: pl.ANY}
        )
        return (*nothing(low_outs), *added)

    patch_grad, low_grad, encoder_gain, ff_right_sum, ff_left_sum = lax.cond(first, lower_grads, ff_middle)
    line = [((272, HALF), BF)]
    blocks = call(
        attn_sum_first_gain,
        (ids, blocks[0], *got, encoder_gain, up_gain, latent_gain),
        line * 4,
        spaces={0: SMEM},
    )
    ff_right_sum, ff_left_sum, _ = lax.optimization_barrier((ff_right_sum, ff_left_sum, got))
    from_left = plane_shift(ff_right_sum, 0, 1, (1,))
    from_right = plane_shift(ff_left_sum, 0, -1, (1,))
    (block,) = call(sum_all, (blocks[0], *exchange(blocks, 1)), line)
    byte_grad = jnp.where(first, low_grad, up_arrived)
    from_left, from_right, block, byte_grad = lax.optimization_barrier((from_left, from_right, block, byte_grad))
    ff_line = ((3 * share, HALF), BF)
    ff_blocks = on_section(
        second, ff_sum_first, (ids, ff_own, from_left, from_right), [ff_line] * 4, spaces={0: SMEM}
    )
    ff_got = exchange(ff_blocks, 1)
    across, ff_got = lax.optimization_barrier((swap(block, "zh"), ff_got))
    (block,) = call(sum_all, (block, across), line)
    lines = collect(block, 1)
    step_in = swap(lines[3][0:16], "core")
    (block,) = call(stack_rows, (*lines, step_in), [((1040, HALF), BF)], spaces={4: pl.ANY})
    pieces = collect(block, 0)
    own_far = swap(block, "core")
    (ff_sum,) = on_section(second, ff_sum_second, (ff_blocks[0], *ff_got), [ff_line])
    ff_sum = ff_sum.reshape(3, 2, share // 2, HALF)
    ff_far = swap(pick(ff_sum, 1 - zh, 1), "zh")
    ff_sum = (pick(ff_sum, zh, 1).astype(F32) + ff_far.astype(F32)).astype(BF).reshape(3, 2, share // 4, HALF)
    ff_mine = pick(ff_sum, core, 1)
    ff_far = swap(pick(ff_sum, 1 - core, 1), "core")

    def ff_result():
        low, high = jnp.where(core == 0, ff_mine, ff_far), jnp.where(core == 0, ff_far, ff_mine)
        return jnp.swapaxes(jnp.concatenate([low, high], 2), 0, 1).astype(F32)

    ff_grad = lax.cond(second, ff_result, lambda: jnp.zeros((share // 4, 3, D), F32))
    patch_out = jnp.where(first, patch_grad, latents)
    patch_out, ff_grad, *pieces = lax.optimization_barrier((patch_out, ff_grad, *pieces))
    pieces = pieces + [own_far] + [swap(p, "core") for p in pieces[1:]]
    whole = lambda p: pl.BlockSpec(p.shape, lambda i, n=p.ndim: (0,) * n)
    total_qkv, total_out, total_gain = pl.pallas_call(
        final_attn,
        grid=(4,),
        out_shape=[
            jax.ShapeDtypeStruct((D, 3 * D), F32),
            jax.ShapeDtypeStruct((D, D), F32),
            jax.ShapeDtypeStruct((2, D), F32),
        ],
        in_specs=[pl.BlockSpec(memory_space=SMEM)] + [whole(p) for p in pieces],
        out_specs=[
            pl.BlockSpec((256, 3 * D), lambda i: (i, 0)),
            pl.BlockSpec((256, D), lambda i: (i, 0)),
            pl.BlockSpec((2, D), lambda i: (0, 0)),
        ],
        compiler_params=pltpu.CompilerParams(vmem_limit_bytes=FINAL_VMEM),
    )(ids, *pieces)
    return (
        patch_out.reshape(1, micro, 1, seq, D),
        byte_grad.reshape(micro, 1, half_bytes, D),
        total_qkv[None],
        total_out[None],
        total_gain[None],
        ff_grad[None],
    )


def solution(mesh):
    fine = Mesh(mesh.devices.reshape(2, 4, 4, 2, 2), ("s",) + BATCH)
    in_specs = (
        P("s", None, BATCH, None, None),
        P(None, BATCH, "s", None),
        P(None, BATCH, None),
        P(None, BATCH, None),
        P("s", None, None),
        P("s", None, None),
        P("s", None, None),
        P(),
    )
    out_specs = (
        P("s", None, BATCH, None, None),
        P(None, BATCH, "s", None),
        P("s", None, None),
        P("s", None, None),
        P("s", None, None),
        P("s", BATCH, None, None),
    )
    return jax.shard_map(shards, mesh=fine, in_specs=in_specs, out_specs=out_specs, check_vma=False)
```
